32 devices in a mesh: task: 4 (over y, x), batch: 8 (over z, core).
Axes of the slice: x: 2, y: 2, z: 4, core: 2. Of those that a mesh axis runs over, the one named last changes fastest.
Arguments:
- images: bfloat16 [32, 18, 24, 512], P(('task', 'batch')), may hold values from -6 to 6
- image_small: int32 [32], P(('task', 'batch')), may hold values from 0 to 1, as said below
- pool_index: int32 [32, 9, 12], P(('task', 'batch')), may hold values from 0 to 3
- row_slot: int32 [9216], replicated, may hold values from 0 to 9215, each once
- trunk_weight: float32 [9216, 512], P('batch'), may hold values from -0.09375 to 0.09375
- trunk_mean_grad: float32 [9216, 512], P('batch'), may hold values from -5.173322 to 5.173322
- trunk_mean_square: float32 [9216, 512], P('batch'), may hold values from 7.32672 to 116.1216
- trunk_statistic: float32 [2, 512, 512], replicated, as said below
- trunk_basis: float32 [2, 512, 512], replicated, as said below
- head_weight: float32 [4, 5632, 512], P('task', 'batch'), may hold values from -0.15625 to 0.15625
- head_mean_grad: float32 [4, 5632, 512], P('task', 'batch'), may hold values from -5.173322 to 5.173322
- head_mean_square: float32 [4, 5632, 512], P('task', 'batch'), may hold values from 7.32672 to 116.1216
- head_statistic: float32 [4, 3, 512, 512], P('task'), as said below
- head_basis: float32 [4, 3, 512, 512], P('task'), as said below
- trunk_gain: float32 [2, 512], replicated, may hold values from 0.5 to 1.5
- trunk_offset: float32 [2, 512], replicated, may hold values from -1.2 to 1.2
- trunk_norm_mean_grad: float32 [2, 2, 512], replicated, may hold values from -5.173322 to 5.173322
- trunk_norm_mean_square: float32 [2, 2, 512], replicated, may hold values from 7.32672 to 116.1216
- head_gain: float32 [4, 3, 512], P('task'), may hold values from 0.5 to 1.5
- head_offset: float32 [4, 3, 512], P('task'), may hold values from -1.2 to 1.2
- head_norm_mean_grad: float32 [4, 3, 2, 512], P('task'), may hold values from -5.173322 to 5.173322
- head_norm_mean_square: float32 [4, 3, 2, 512], P('task'), may hold values from 7.32672 to 116.1216
- cotangent: bfloat16 [4, 4, 8, 9, 12, 512], P('task', None, 'batch'), may hold values from -6 to 6
Outputs:
- task_features: bfloat16 [4, 4, 8, 9, 12, 512], P('task', None, 'batch')
- input_grad: float32 [32, 18, 24, 512], P(('task', 'batch'))
- trunk_weight_new: float32 [9216, 512], P('batch')
- trunk_mean_grad_new: float32 [9216, 512], P('batch')
- trunk_mean_square_new: float32 [9216, 512], P('batch')
- trunk_statistic_new: float32 [2, 512, 512], replicated
- trunk_basis_new: float32 [2, 512, 512], replicated
- head_weight_new: float32 [4, 5632, 512], P('task', 'batch')
- head_mean_grad_new: float32 [4, 5632, 512], P('task', 'batch')
- head_mean_square_new: float32 [4, 5632, 512], P('task', 'batch')
- head_statistic_new: float32 [4, 3, 512, 512], P('task')
- head_basis_new: float32 [4, 3, 512, 512], P('task')
- trunk_norm_new: float32 [2, 2, 512], replicated
- trunk_norm_mean_grad_new: float32 [2, 2, 512], replicated
- trunk_norm_mean_square_new: float32 [2, 2, 512], replicated
- head_norm_new: float32 [4, 3, 2, 512], P('task')
- head_norm_mean_grad_new: float32 [4, 3, 2, 512], P('task')
- head_norm_mean_square_new: float32 [4, 3, 2, 512], P('task')
The draws below stay inside these ranges and needn't reach their ends.
Inputs may be any that keep to these rules, and one draw needn't show every extreme that they name: `image_small`: 1 marks a 144x192 image whose valid region is its first 9 rows and 12 columns; 0 marks a 288x384 image, valid everywhere. `pool_index`: which cell of a 2x2 window receives the value: 2 times the row offset plus the column offset. A permutation: row r of the stacked trunk kernels is held at row row_slot[r] of the slot-ordered arrays. `trunk_statistic`: each matrix is symmetric with a dominant positive diagonal. `head_statistic`: each matrix is symmetric with a dominant positive diagonal. `trunk_basis`: each matrix is orthogonal. `head_basis`: each matrix is orthogonal.
All inputs are finite; a program needn't handle non-finite values.
Results may differ from the reference program's by a relative error of at most 0.023.
Values may be sent and summed in bfloat16 or wider, within the bound.
A program may use at most 320 MiB of HBM per device.

```python
import math
import jax
import jax.numpy as jnp
from jax import lax

C = 512
H = 18
W = 24
IMG_DEV = 1
STEP = 10
TASKS = 4
IMAGES = 32
HP = 9
WP = 12
TROWS = 9216
HROWS = 5632
N_TASK = 4


def statistic_blocks(key, row_counts):
    scale_base = 0.00105 * IMAGES * H * W
    scales = jnp.array([row_total * scale_base for row_total in row_counts], jnp.float32)
    matrix_total = len(row_counts)
    diag_key, rough_key = jax.random.split(key)
    diagonal = jnp.exp(jax.random.uniform(diag_key, (matrix_total, C), jnp.float32, 0.0, math.log(4.0))) * scales[:, None]
    rough_part = jax.random.uniform(rough_key, (matrix_total, C, C), jnp.float32, -1.0, 1.0)
    symmetric = 0.5 * (rough_part + jnp.swapaxes(rough_part, 1, 2))
    identity = jnp.eye(C, dtype=jnp.float32)
    return symmetric * (1.0 - identity) * (0.4 / C) * scales[:, None, None] + identity * diagonal[:, None, :]


def orthogonal_blocks(key, matrix_total):
    angle_key, order_key = jax.random.split(key)
    half_size = C // 2
    angles = jax.random.uniform(angle_key, (matrix_total, half_size), jnp.float32, -math.pi, math.pi)
    identity = jnp.eye(half_size, dtype=jnp.float32)
    cosine = jnp.cos(angles)[:, :, None] * identity
    sine_part = jnp.sin(angles)[:, :, None] * identity
    upper = jnp.concatenate([cosine, -sine_part], axis=2)
    lower = jnp.concatenate([sine_part, cosine], axis=2)
    rotation = jnp.concatenate([upper, lower], axis=1)
    orders = jax.vmap(lambda order_seed: jax.random.permutation(order_seed, C))(jax.random.split(order_key, matrix_total))
    indices = jnp.broadcast_to(orders[:, None, :].astype(jnp.int32), rotation.shape)
    return jnp.take_along_axis(rotation, indices, axis=2)


def draw_trunk_statistic(key, part):
    key = jax.random.fold_in(key, 21)
    return statistic_blocks(key, [9 * C, 9 * C])


def draw_head_statistic(key, part):
    key = jax.random.fold_in(key, 22)
    return statistic_blocks(key, [C, C, 9 * C] * TASKS).reshape(TASKS, 3, C, C)


def draw_trunk_basis(key, part):
    key = jax.random.fold_in(key, 23)
    return orthogonal_blocks(key, 2)


def draw_head_basis(key, part):
    key = jax.random.fold_in(key, 24)
    return orthogonal_blocks(key, 3 * TASKS).reshape(TASKS, 3, C, C)


def draw_image_small(key, part):
    key = jax.random.fold_in(key, 25)
    devices_all = IMAGES // IMG_DEV
    per_task = devices_all // TASKS
    device_index = jnp.arange(IMAGES, dtype=jnp.int32) // IMG_DEV
    task_index = device_index // per_task
    batch_index = device_index % per_task
    drawn = jax.random.randint(key, (IMAGES,), 0, per_task * 4 * TASKS, dtype=jnp.int32)
    large = drawn < (batch_index + 1) * (TASKS + 3 * (task_index + 1))
    return jnp.where(large, 0, 1).astype(jnp.int32)


def set_ends(entries, rng, smallest, top_value):
    spot = [jax.random.randint(jax.random.fold_in(rng, axis), (), 0, length) for axis, length in enumerate(entries.shape)]
    main_axis = entries.shape.index(max(entries.shape))
    neighbour = spot[:main_axis] + [(spot[main_axis] + 1) % entries.shape[main_axis]] + spot[main_axis + 1:]
    return entries.at[tuple(spot)].set(smallest).at[tuple(neighbour)].set(top_value)


def levels(own_key, shape, cuts, smallest, top_value):
    gain = 1.0
    for dim, parts in cuts:
        steps = jax.random.uniform(jax.random.fold_in(jax.random.fold_in(own_key, 6), dim), (parts,), jnp.float32, smallest / len(cuts), top_value / len(cuts))
        gain = gain * jnp.repeat(jnp.exp(steps), shape[dim] // parts).reshape((-1,) + (1,) * (len(shape) - 1 - dim))
    return gain


def normal_values(key, shape, width, limit, cuts=(), kind=jnp.bfloat16):
    entries = width * jax.random.normal(key, shape, jnp.float32)
    if cuts:
        entries = entries * levels(key, shape, cuts, -0.22, 0.18)
    return jnp.clip(entries, -limit, limit).astype(kind)


def setup_inputs(seed: int = 0) -> dict:
    splits = jax.random.split(jax.random.key(seed), 24)
    images = normal_values(splits[0], (IMAGES, H, W, C), 1.0, 6.0, ((0, 32),))
    image_small = draw_image_small(jax.random.fold_in(splits[23], 71), 0)
    pool_index = set_ends(jax.random.randint(splits[2], (IMAGES, HP, WP), 0, 4), jax.random.fold_in(splits[2], 1), 0, 3).astype(jnp.int32)
    row_slot = jax.random.permutation(splits[3], TROWS).astype(jnp.int32)
    trunk_weight = normal_values(splits[4], (TROWS, C), (9 * C) ** -0.5, 0.09375, ((0, 8),), jnp.float32)
    trunk_mean_grad = normal_values(splits[5], (TROWS, C), (0.0074 * (IMAGES * H * W) ** 0.5), 5.173322, ((0, 8),), jnp.float32)
    trunk_mean_square = jnp.clip(jnp.exp(math.log(116.1216) - 2.76311 * jax.random.uniform(splits[6], (TROWS, C), jnp.float32) ** levels(splits[6], (TROWS, C), ((0, 8),), -0.2, 0.2)), 7.32672, 116.1216)
    trunk_statistic = draw_trunk_statistic(jax.random.fold_in(splits[23], 71), 0)
    trunk_basis = draw_trunk_basis(jax.random.fold_in(splits[23], 71), 0)
    head_weight = normal_values(splits[9], (TASKS, HROWS, C), (3 * C) ** -0.5, 0.15625, ((0, 4), (1, 8)), jnp.float32)
    head_mean_grad = normal_values(splits[10], (TASKS, HROWS, C), (0.0074 * (IMAGES * H * W) ** 0.5), 5.173322, ((0, 4), (1, 8)), jnp.float32)
    head_mean_square = jnp.clip(jnp.exp(math.log(116.1216) - 2.76311 * jax.random.uniform(splits[11], (TASKS, HROWS, C), jnp.float32) ** levels(splits[11], (TASKS, HROWS, C), ((0, 4), (1, 8)), -0.2, 0.2)), 7.32672, 116.1216)
    head_statistic = draw_head_statistic(jax.random.fold_in(splits[23], 71), 0)
    head_basis = draw_head_basis(jax.random.fold_in(splits[23], 71), 0)
    trunk_gain = jnp.clip(1.0 + 0.1 * jax.random.normal(splits[14], (2, C), jnp.float32), 0.5, 1.5)
    trunk_offset = normal_values(splits[15], (2, C), 0.3, 1.2, (), jnp.float32)
    trunk_norm_mean_grad = normal_values(splits[16], (2, 2, C), (0.0074 * (IMAGES * H * W) ** 0.5), 5.173322, (), jnp.float32)
    trunk_norm_mean_square = jnp.clip(jnp.exp(jax.random.uniform(splits[17], (2, 2, C), jnp.float32, math.log(7.32672), math.log(116.1216))), 7.32672, 116.1216)
    head_gain = jnp.clip(1.0 + 0.1 * jax.random.normal(splits[18], (TASKS, 3, C), jnp.float32), 0.5, 1.5)
    head_offset = normal_values(splits[19], (TASKS, 3, C), 0.3, 1.2, ((0, 4),), jnp.float32)
    head_norm_mean_grad = normal_values(splits[20], (TASKS, 3, 2, C), (0.0074 * (IMAGES * H * W) ** 0.5), 5.173322, ((0, 4),), jnp.float32)
    head_norm_mean_square = jnp.clip(jnp.exp(math.log(116.1216) - 2.76311 * jax.random.uniform(splits[21], (TASKS, 3, 2, C), jnp.float32) ** levels(splits[21], (TASKS, 3, 2, C), ((0, 4),), -0.2, 0.2)), 7.32672, 116.1216)
    cotangent = normal_values(splits[22], (TASKS, N_TASK, IMAGES // N_TASK, HP, WP, C), 1.0, 6.0, ((0, 4), (2, 8)))
    return dict(images=images, image_small=image_small, pool_index=pool_index, row_slot=row_slot, trunk_weight=trunk_weight, trunk_mean_grad=trunk_mean_grad, trunk_mean_square=trunk_mean_square, trunk_statistic=trunk_statistic, trunk_basis=trunk_basis, head_weight=head_weight, head_mean_grad=head_mean_grad, head_mean_square=head_mean_square, head_statistic=head_statistic, head_basis=head_basis, trunk_gain=trunk_gain, trunk_offset=trunk_offset, trunk_norm_mean_grad=trunk_norm_mean_grad, trunk_norm_mean_square=trunk_norm_mean_square, head_gain=head_gain, head_offset=head_offset, head_norm_mean_grad=head_norm_mean_grad, head_norm_mean_square=head_norm_mean_square, cotangent=cotangent)


EPS = 1e-05
ADAM_EPS = 1e-08
BETA_ONE = 0.95
BETA_TWO = 0.95
STAT_DECAY = 0.95
LEARN_MATRIX = 0.02
LEARN_NORM = 0.5
DECAY_MATRIX = 0.01
HIGHEST = lax.Precision.HIGHEST

@jax.custom_vjp
def low(v):
    return lax.optimization_barrier(v.astype(jnp.bfloat16)).astype(jnp.float32)

@jax.custom_vjp
def low_back(v):
    return v

def low_keep(v):
    return (low(v), None)

def low_pass(kept, grad):
    return (grad,)

def back_keep(v):
    return (v, None)

def back_low(kept, grad):
    return (low(grad),)
low.defvjp(low_keep, low_pass)
low_back.defvjp(back_keep, back_low)

def make_validity(small_flags, height, breadth):
    shrunk = small_flags > 0
    row_limit = jnp.where(shrunk, height // 2, height)
    col_limit = jnp.where(shrunk, breadth // 2, breadth)
    row_index = lax.broadcasted_iota(jnp.int32, (1, height, breadth, 1), 1)
    col_index = lax.broadcasted_iota(jnp.int32, (1, height, breadth, 1), 2)
    inside = (row_index < row_limit[:, None, None, None]) & (col_index < col_limit[:, None, None, None])
    return inside.astype(jnp.float32)

def conv_three(inputs, kernel):
    height, breadth = (inputs.shape[1], inputs.shape[2])
    padded = jnp.pad(inputs, ((0, 0), (1, 1), (1, 1), (0, 0)))
    summed = jnp.zeros(inputs.shape[:3] + (kernel.shape[2],), jnp.float32)
    for position in range(9):
        window = padded[:, position // 3:position // 3 + height, position % 3:position % 3 + breadth, :]
        summed = summed + jnp.einsum('nhwc,cd->nhwd', window, kernel[position], precision=HIGHEST)
    return summed

def batch_norm(values, validity, gain_row, offset_row):
    sum_valid = jnp.sum(validity)
    center = lax.optimization_barrier(jnp.sum(values * validity, axis=(0, 1, 2))) / sum_valid
    square = lax.optimization_barrier(jnp.sum(values * values * validity, axis=(0, 1, 2))) / sum_valid
    return (values - center) * lax.rsqrt(square - center * center + EPS) * gain_row + offset_row

def pool_mean(values):
    number, height, breadth, channels = values.shape
    return lax.optimization_barrier(jnp.mean(values.reshape(number, height // 2, 2, breadth // 2, 2, channels), axis=(2, 4)))

def unpool_cells(pooled, places):
    number, height, breadth, channels = pooled.shape
    choose = (places[..., None] == jnp.arange(4, dtype=jnp.int32)).astype(jnp.float32)
    placed = pooled[:, :, :, None, :] * choose[..., None]
    placed = placed.reshape(number, height, breadth, 2, 2, channels).transpose(0, 1, 3, 2, 4, 5)
    return placed.reshape(number, 2 * height, 2 * breadth, channels)

def adam_step(gradient, moment_one, moment_two):
    new_one = BETA_ONE * moment_one + (1.0 - BETA_ONE) * gradient
    new_two = BETA_TWO * moment_two + (1.0 - BETA_TWO) * gradient * gradient
    direction = new_one / (1.0 - BETA_ONE ** STEP) / (jnp.sqrt(new_two / (1.0 - BETA_TWO ** STEP)) + ADAM_EPS)
    return (new_one, new_two, direction)

def rotate_rows(rows_grad, owners, basis_set):
    turned = jnp.einsum('rc,mcd->rmd', rows_grad, basis_set, precision=HIGHEST)
    return jnp.einsum('rm,rmd->rd', owners, turned, precision=HIGHEST)

def rotate_back(rows_step, owners, basis_set):
    turned = jnp.einsum('rd,mcd->rmc', rows_step, basis_set, precision=HIGHEST)
    return jnp.einsum('rm,rmc->rc', owners, turned, precision=HIGHEST)

def owner_grams(rows_grad, owners):
    spread_rows = owners[:, :, None] * rows_grad[:, None, :]
    return jnp.einsum('rmc,rd->mcd', spread_rows, rows_grad, precision=HIGHEST)

def renew_basis(statistic, basis_set, grams):
    new_stat = STAT_DECAY * statistic + (1.0 - STAT_DECAY) * grams
    product = jnp.einsum('mcd,mde->mce', new_stat, basis_set, precision=HIGHEST)
    inner_gram = jnp.einsum('mcd,mce->mde', product, product, precision=HIGHEST)
    factor = jnp.linalg.cholesky(inner_gram)
    return (new_stat, lax.linalg.triangular_solve(factor, product, left_side=False, lower=True, transpose_a=True))

def soap_update(rows_grad, owners, weight_rows, mean_grad, mean_square, statistic, basis_set):
    rotated = rotate_rows(rows_grad, owners, basis_set)
    new_one, new_two, direction = adam_step(rotated, mean_grad, mean_square)
    stepped = rotate_back(direction, owners, basis_set)
    new_weight = weight_rows - LEARN_MATRIX * (stepped + DECAY_MATRIX * weight_rows)
    new_stat, new_basis = renew_basis(statistic, basis_set, owner_grams(rows_grad, owners))
    return (new_weight, new_one, new_two, new_stat, new_basis)

def reference(images, image_small, pool_index, row_slot, trunk_weight, trunk_mean_grad, trunk_mean_square, trunk_statistic, trunk_basis, head_weight, head_mean_grad, head_mean_square, head_statistic, head_basis, trunk_gain, trunk_offset, trunk_norm_mean_grad, trunk_norm_mean_square, head_gain, head_offset, head_norm_mean_grad, head_norm_mean_square, cotangent):
    tap_rows = 9 * C
    validity = make_validity(image_small, H, W)
    natural = jnp.take(trunk_weight, row_slot, axis=0)
    encoder = natural[:tap_rows].reshape(9, C, C)
    decoder = natural[tap_rows:].reshape(9, C, C)
    attend_first = head_weight[:, :C]
    attend_second = head_weight[:, C:2 * C]
    head_kernel = head_weight[:, 2 * C:].reshape(TASKS, 9, C, C)

    def forward(image_values, enc_kernel, dec_kernel, gain_rows, offset_rows, first_set, second_set, kernel_set, head_gain_rows, head_offset_rows):
        enc_pre = low_back(conv_three(image_values * validity, low(enc_kernel)))
        enc_act = jax.nn.silu(batch_norm(enc_pre, validity, gain_rows[0], offset_rows[0])) * validity
        spread = low(unpool_cells(pool_mean(enc_act), pool_index) * validity)
        dec_pre = low_back(conv_three(spread, low(dec_kernel)))
        features = low(jax.nn.silu(batch_norm(dec_pre, validity, gain_rows[1], offset_rows[1])) * validity)

        def one_task(weights):
            attend_one, attend_two, kernel_one, gain_one, offset_one = weights
            first_pre = low_back(jnp.einsum('nhwc,cd->nhwd', features, low(attend_one), precision=HIGHEST))
            hidden = low(jax.nn.silu(batch_norm(first_pre, validity, gain_one[0], offset_one[0])) * validity)
            second_pre = low_back(jnp.einsum('nhwc,cd->nhwd', hidden, low(attend_two), precision=HIGHEST))
            gate_value = jax.nn.sigmoid(batch_norm(second_pre, validity, gain_one[1], offset_one[1]))
            gated = low(gate_value * features)
            third_pre = low_back(conv_three(gated, low(kernel_one)))
            return pool_mean(jax.nn.silu(batch_norm(third_pre, validity, gain_one[2], offset_one[2])) * validity)
        return lax.map(jax.checkpoint(one_task), (first_set, second_set, kernel_set, head_gain_rows, head_offset_rows))
    outputs, pullback = jax.vjp(forward, images.astype(jnp.float32), encoder, decoder, trunk_gain, trunk_offset, attend_first, attend_second, head_kernel, head_gain, head_offset)
    grads = pullback(cotangent.astype(jnp.float32).reshape(TASKS, IMAGES, H // 2, W // 2, C))
    task_features = outputs.reshape(TASKS, N_TASK, IMAGES // N_TASK, H // 2, W // 2, C).astype(jnp.bfloat16)
    input_grad = grads[0]
    trunk_grads = jnp.concatenate([grads[1].reshape(tap_rows, C), grads[2].reshape(tap_rows, C)], axis=0)
    inverse_slot = jnp.argsort(row_slot).astype(jnp.int32)
    owned_rows = jnp.take(trunk_grads, inverse_slot, axis=0)
    trunk_owner = inverse_slot // tap_rows
    trunk_onehot = (trunk_owner[:, None] == jnp.arange(2, dtype=jnp.int32)).astype(jnp.float32)
    trunk_new = soap_update(owned_rows, trunk_onehot, trunk_weight, trunk_mean_grad, trunk_mean_square, trunk_statistic, trunk_basis)
    head_owner = jnp.minimum(jnp.arange(HROWS, dtype=jnp.int32) // C, 2)
    head_onehot = (head_owner[:, None] == jnp.arange(3, dtype=jnp.int32)).astype(jnp.float32)
    head_parts = []
    for task_number in range(TASKS):
        rows_grad = jnp.concatenate([grads[5][task_number], grads[6][task_number], grads[7][task_number].reshape(tap_rows, C)], axis=0)
        head_parts.append(soap_update(rows_grad, head_onehot, head_weight[task_number], head_mean_grad[task_number], head_mean_square[task_number], head_statistic[task_number], head_basis[task_number]))
    head_new = [jnp.stack([piece[field] for piece in head_parts]) for field in range(5)]
    trunk_norm = jnp.stack([trunk_gain, trunk_offset], axis=1)
    trunk_norm_grad = jnp.stack([grads[3], grads[4]], axis=1)
    trunk_norm_one, trunk_norm_two, trunk_direction = adam_step(trunk_norm_grad, trunk_norm_mean_grad, trunk_norm_mean_square)
    head_norm = jnp.stack([head_gain, head_offset], axis=2)
    head_norm_grad = jnp.stack([grads[8], grads[9]], axis=2)
    head_norm_one, head_norm_two, head_direction = adam_step(head_norm_grad, head_norm_mean_grad, head_norm_mean_square)
    return (task_features, input_grad, trunk_new[0], trunk_new[1], trunk_new[2], trunk_new[3], trunk_new[4], head_new[0], head_new[1], head_new[2], head_new[3], head_new[4], trunk_norm - LEARN_NORM * trunk_direction, trunk_norm_one, trunk_norm_two, head_norm - LEARN_NORM * head_direction, head_norm_one, head_norm_two)
```

```python
import functools

import jax
import jax.numpy as jnp
from jax import lax
from jax.experimental import pallas as pl
from jax.experimental.pallas import tpu as pltpu
from jax.sharding import PartitionSpec as P

STEP = 10


EPS = 1e-05
ADAM_EPS = 1e-08
BETA_ONE = 0.95
BETA_TWO = 0.95
STAT_DECAY = 0.95
LEARN_MATRIX = 0.02
LEARN_NORM = 0.5
DECAY_MATRIX = 0.01
BF = jnp.bfloat16
F32 = jnp.float32
MESH = pl.DeviceIdType.MESH
MIB = 1 << 20

VMEM_SPEC = pl.BlockSpec(memory_space=pltpu.VMEM)
SMEM_SPEC = pl.BlockSpec(memory_space=pltpu.SMEM)


def run(body, outs, specs, args, scratch=(), vmem=40, flops=0):
    size = sum(o.size * o.dtype.itemsize for o in outs) + sum(a.size * a.dtype.itemsize for a in args)
    return pl.pallas_call(
        body,
        out_shape=tuple(outs),
        in_specs=[SMEM_SPEC if s == "s" else VMEM_SPEC for s in specs],
        out_specs=tuple(VMEM_SPEC for _ in outs),
        scratch_shapes=list(scratch),
        compiler_params=pltpu.CompilerParams(vmem_limit_bytes=vmem * MIB),
        cost_estimate=pl.CostEstimate(flops=flops, bytes_accessed=size, transcendentals=0),
    )(*args)


def shape(dims, kind):
    return jax.ShapeDtypeStruct(tuple(dims), kind)


def dot(a, b):
    return jnp.dot(a, b, preferred_element_type=F32)


def dot_nt(a, b):
    return lax.dot_general(a, b, (((1,), (1,)), ((), ())), preferred_element_type=F32)


def dot_tn(a, b):
    return lax.dot_general(a, b, (((0,), (0,)), ((), ())), preferred_element_type=F32)


def split(a):
    high = a.astype(BF)
    return high, (a - high.astype(F32)).astype(BF)


def dot3(kind, a, b):
    a_high, a_low = split(a)
    b_high, b_low = split(b)
    return kind(a_high, b_high) + (kind(a_high, b_low) + kind(a_low, b_high))


def places(height, breadth):
    index = lax.broadcasted_iota(jnp.int32, (height * breadth, 1), 0)
    row = lax.div(index, breadth)
    return row, index - row * breadth


def valid_rows(small, height, breadth):
    row, col = places(height, breadth)
    row_limit = jnp.where(small > 0, height // 2, height)
    col_limit = jnp.where(small > 0, breadth // 2, breadth)
    return jnp.where((row < row_limit) & (col < col_limit), 1.0, 0.0).astype(F32)


def move(values, rows):
    gap = jnp.zeros((abs(rows),) + values.shape[1:], values.dtype)
    if rows > 0:
        return jnp.concatenate([gap, values[:-rows]], axis=0)
    return jnp.concatenate([values[-rows:], gap], axis=0)


def from_left(values, col):
    return jnp.where(col > 0, pltpu.roll(values, 1, 0), 0.0)


def from_right(values, col, breadth):
    return jnp.where(col < breadth - 1, pltpu.roll(values, values.shape[0] - 1, 0), 0.0)


def gather_taps(tap, breadth, col):
    lines = [move(tap(b), breadth) + tap(3 + b) + move(tap(6 + b), -breadth) for b in range(3)]
    return lines[1] + from_left(lines[0], col) + from_right(lines[2], col, breadth)


def spread_taps(values, breadth, col):
    lines = [from_right(values, col, breadth), values, from_left(values, col)]
    return [
        move(lines[b], breadth * (a - 1)) if a != 1 else lines[b] for a in range(3) for b in range(3)
    ]


def window_sum(values, row, col, breadth):
    count = values.shape[0]
    pair = values + jnp.where(
        col % 2 == 0, pltpu.roll(values, count - 1, 0), pltpu.roll(values, 1, 0)
    )
    return pair + jnp.where(row % 2 == 0, move(pair, -breadth), move(pair, breadth))


def norm_of(values, totals, scale):
    count = totals[2:3]
    center = totals[0:1] / count
    inverse = lax.rsqrt(totals[1:2] / count - center * center + EPS)
    normal = (values - center) * inverse
    return normal, inverse, normal * scale[0:1] + scale[1:2]


def silu_back(scaled):
    sig = jax.nn.sigmoid(scaled)
    return sig * (1.0 + scaled * (1.0 - sig))


def norm_back(upstream, normal, inverse, totals, sums, scale, valid):
    count = totals[2:3]
    return (
        scale[0:1] * inverse * (upstream - sums[0:1] / count - normal * sums[1:2] / count) * valid
    )


def col_sum(values):
    return jnp.sum(values, axis=0, keepdims=True)


def put_sums(ref, rows):
    width = ref.shape[1]
    rows = list(rows) + [jnp.zeros((1, width), F32)] * (8 - len(rows))
    ref[...] = jnp.concatenate(rows, axis=0)


def each_image(geometry, body, start):
    number, height, breadth = geometry
    pixels = height * breadth

    def step(image, carry):
        return body(image, pl.ds(pl.multiple_of(image * pixels, 16), pixels), carry)

    return lax.fori_loop(0, number, step, start)


def zero_rows(count, width):
    return (jnp.zeros((1, width), F32),) * count


def trunk_conv_body(geometry, small, x, taps, pre, stats, work):
    number, height, breadth = geometry
    width = pre.shape[1]
    _, col = places(height, breadth)

    def image(i, rows, carry):
        valid = valid_rows(small[i], height, breadth)
        work[...] = dot(x[rows, :], taps[...])
        out = gather_taps(lambda p: work[:, p * width : (p + 1) * width], breadth, col)
        pre[rows, :] = out
        kept = out * valid
        return (
            carry[0] + col_sum(kept),
            carry[1] + col_sum(kept * out),
            carry[2] + jnp.broadcast_to(col_sum(valid), (1, width)),
        )

    put_sums(stats, each_image(geometry, image, zero_rows(3, width)))


def trunk_conv(geometry, small, x, taps):
    pixels = geometry[1] * geometry[2]
    width = taps.shape[1] // 9
    return run(
        functools.partial(trunk_conv_body, geometry),
        [shape((x.shape[0], width), F32), shape((8, width), F32)],
        "svv",
        (small, x, taps),
        [pltpu.VMEM((pixels, 9 * width), F32)],
        flops=2 * x.size * taps.shape[1],
    )


def enc_act_body(geometry, small, pre, totals, scale, choose, spread):
    number, height, breadth = geometry
    row, col = places(height, breadth)

    def image(i, rows, carry):
        valid = valid_rows(small[i], height, breadth)
        _, _, scaled = norm_of(pre[rows, :], totals[...], scale[...])
        act = scaled * jax.nn.sigmoid(scaled) * valid
        pooled = window_sum(act, row, col, breadth) * 0.25
        spread[rows, :] = (pooled * choose[rows, :]).astype(BF)
        return carry

    each_image(geometry, image, 0)


def enc_act(geometry, small, pre, totals, scale, choose):
    return run(
        functools.partial(enc_act_body, geometry),
        [shape(pre.shape, BF)],
        "svvvv",
        (small, pre, totals, scale, choose),
    )[0]


def dec_act_body(geometry, small, pre, totals, scale, features):
    number, height, breadth = geometry

    def image(i, rows, carry):
        valid = valid_rows(small[i], height, breadth)
        _, _, scaled = norm_of(pre[rows, :], totals[...], scale[...])
        features[rows, :] = (scaled * jax.nn.sigmoid(scaled) * valid).astype(BF)
        return carry

    each_image(geometry, image, 0)


def dec_act(geometry, small, pre, totals, scale):
    return run(
        functools.partial(dec_act_body, geometry),
        [shape(pre.shape, BF)],
        "svvv",
        (small, pre, totals, scale),
    )[0]


def trunk_upstream(rows, geometry, valid, upstream, choose, pool):
    if not pool:
        return upstream * valid
    row, col = places(geometry[1], geometry[2])
    return window_sum(upstream * choose, row, col, geometry[2]) * 0.25 * valid


def trunk_sums_body(geometry, pool, small, upstream, pre, totals, scale, choose, sums):
    number, height, breadth = geometry
    width = pre.shape[1]

    def image(i, rows, carry):
        valid = valid_rows(small[i], height, breadth)
        normal, _, scaled = norm_of(pre[rows, :], totals[...], scale[...])
        dy = silu_back(scaled) * trunk_upstream(
            rows, geometry, valid, upstream[rows, :], choose[rows, :], pool
        )
        return carry[0] + col_sum(dy), carry[1] + col_sum(dy * normal)

    put_sums(sums, each_image(geometry, image, zero_rows(2, width)))


def trunk_sums(geometry, pool, small, upstream, pre, totals, scale, choose):
    return run(
        functools.partial(trunk_sums_body, geometry, pool),
        [shape((8, pre.shape[1]), F32)],
        "svvvvv",
        (small, upstream, pre, totals, scale, choose),
    )[0]


def trunk_back_body(
    geometry, pool, small, upstream, pre, totals, sums, scale, choose, x, taps, grad, lower, nine
):
    number, height, breadth = geometry
    width = pre.shape[1]
    _, col = places(height, breadth)

    def image(i, rows, carry):
        valid = valid_rows(small[i], height, breadth)
        normal, inverse, scaled = norm_of(pre[rows, :], totals[...], scale[...])
        dy = silu_back(scaled) * trunk_upstream(
            rows, geometry, valid, upstream[rows, :], choose[rows, :], pool
        )
        dz = norm_back(dy, normal, inverse, totals[...], sums[...], scale[...], valid)
        for p, moved in enumerate(spread_taps(dz, breadth, col)):
            nine[rows, p * width : (p + 1) * width] = moved.astype(BF)
        lower[rows, :] = (dot_nt(nine[rows, :], taps[...]) * valid).astype(BF)
        return carry

    each_image(geometry, image, 0)
    grad[...] = dot_tn(x[...], nine[...])


def trunk_back(geometry, pool, small, upstream, pre, totals, sums, scale, choose, x, taps):
    return run(
        functools.partial(trunk_back_body, geometry, pool),
        [shape(taps.shape, F32), shape(x.shape, BF)],
        "svvvvvvvv",
        (small, upstream, pre, totals, sums, scale, choose, x, taps),
        [pltpu.VMEM((x.shape[0], taps.shape[1]), BF)],
        flops=4 * x.size * taps.shape[1],
    )


def put_stats(pre, out, rows, valid, carry):
    pre[rows, :] = out
    kept = out * valid
    width = out.shape[1]
    return (
        carry[0] + col_sum(kept),
        carry[1] + col_sum(kept * out),
        carry[2] + jnp.broadcast_to(col_sum(valid), (1, width)),
    )


def head_first_body(geometry, small, features, weight, pre, stats):
    number, height, breadth = geometry

    def image(i, rows, carry):
        valid = valid_rows(small[i], height, breadth)
        return put_stats(pre, dot(features[rows, :], weight[...]), rows, valid, carry)

    put_sums(stats, each_image(geometry, image, zero_rows(3, pre.shape[1])))


def head_first(geometry, small, features, weight):
    return run(
        functools.partial(head_first_body, geometry),
        [shape(features.shape, F32), shape((8, weight.shape[1]), F32)],
        "svv",
        (small, features, weight),
        flops=2 * features.size * weight.shape[1],
    )


def head_second_body(geometry, small, pre_one, totals, scale, weight, hidden, pre, stats):
    number, height, breadth = geometry

    def image(i, rows, carry):
        valid = valid_rows(small[i], height, breadth)
        _, _, scaled = norm_of(pre_one[rows, :], totals[...], scale[...])
        low = (scaled * jax.nn.sigmoid(scaled) * valid).astype(BF)
        hidden[rows, :] = low
        return put_stats(pre, dot(low, weight[...]), rows, valid, carry)

    put_sums(stats, each_image(geometry, image, zero_rows(3, pre.shape[1])))


def head_second(geometry, small, pre_one, totals, scale, weight):
    return run(
        functools.partial(head_second_body, geometry),
        [shape(pre_one.shape, BF), shape(pre_one.shape, F32), shape((8, weight.shape[1]), F32)],
        "svvvv",
        (small, pre_one, totals, scale, weight),
        flops=2 * pre_one.size * weight.shape[1],
    )


def head_third_body(
    geometry, small, pre_two, totals, scale, features, kernel, gated, pre, stats, work
):
    number, height, breadth = geometry
    width = pre.shape[1]
    half = work.shape[2]
    channels = features.shape[1]
    _, col = places(height, breadth)

    def image(i, rows, carry):
        valid = valid_rows(small[i], height, breadth)
        _, _, scaled = norm_of(pre_two[rows, :], totals[...], scale[...])
        low = (jax.nn.sigmoid(scaled) * features[rows, :].astype(F32)).astype(BF)
        gated[rows, :] = low
        parts = []
        for j in range(width // half):
            cut = slice(j * half, (j + 1) * half)
            for p in range(9):
                work[p] = dot(low, kernel[p * channels : (p + 1) * channels, cut])
            parts.append(gather_taps(lambda p: work[p], breadth, col))
        return put_stats(pre, jnp.concatenate(parts, axis=1), rows, valid, carry)

    put_sums(stats, each_image(geometry, image, zero_rows(3, width)))


def head_third(geometry, small, pre_two, totals, scale, features, kernel):
    pixels = geometry[1] * geometry[2]
    return run(
        functools.partial(head_third_body, geometry),
        [shape(pre_two.shape, BF), shape(pre_two.shape, F32), shape((8, kernel.shape[1]), F32)],
        "svvvvv",
        (small, pre_two, totals, scale, features, kernel),
        [pltpu.VMEM((9, pixels, 256), F32)],
        flops=2 * pre_two.size * kernel.shape[0],
    )


def pool_choice(height, breadth, flipped):
    pixels, windows = height * breadth, height * breadth // 4
    dims = (windows, pixels) if flipped else (pixels, windows)
    pixel = lax.broadcasted_iota(jnp.int32, dims, 1 if flipped else 0)
    window = lax.broadcasted_iota(jnp.int32, dims, 0 if flipped else 1)
    row = lax.div(pixel, breadth)
    col = pixel - row * breadth
    home = lax.div(row, 2) * (breadth // 2) + lax.div(col, 2)
    return jnp.where(home == window, 1.0, 0.0).astype(BF)


def head_out_body(geometry, small, pre, totals, scale, cotangent, pooled, sums):
    number, height, breadth = geometry
    widen = pool_choice(height, breadth, False)
    narrow = pool_choice(height, breadth, True)

    def image(i, rows, carry):
        valid = valid_rows(small[i], height, breadth)
        normal, _, scaled = norm_of(pre[rows, :], totals[...], scale[...])
        high, low = split(scaled * jax.nn.sigmoid(scaled) * valid)
        pooled[i] = ((dot(narrow, high) + dot(narrow, low)) * 0.25).astype(BF)
        dy = silu_back(scaled) * dot(widen, cotangent[i]) * 0.25 * valid
        return carry[0] + col_sum(dy), carry[1] + col_sum(dy * normal)

    put_sums(sums, each_image(geometry, image, zero_rows(2, pre.shape[1])))


def head_out(geometry, small, pre, totals, scale, cotangent):
    return run(
        functools.partial(head_out_body, geometry),
        [shape(cotangent.shape, BF), shape((8, pre.shape[1]), F32)],
        "svvvv",
        (small, pre, totals, scale, cotangent),
    )


def head_third_grad_body(
    geometry, small, pre, totals, sums, scale, cotangent, gated, kernel, grad, lower, nine
):
    number, height, breadth = geometry
    width = pre.shape[1]
    channels = gated.shape[1]
    _, col = places(height, breadth)
    widen = pool_choice(height, breadth, False)

    def image(i, rows, carry):
        valid = valid_rows(small[i], height, breadth)
        normal, inverse, scaled = norm_of(pre[rows, :], totals[...], scale[...])
        dy = silu_back(scaled) * dot(widen, cotangent[i]) * 0.25 * valid
        dz = norm_back(dy, normal, inverse, totals[...], sums[...], scale[...], valid)
        for p, moved in enumerate(spread_taps(dz, breadth, col)):
            nine[p, rows, :] = moved.astype(BF)
        total = None
        for p in range(9):
            part = dot_nt(nine[p, rows, :], kernel[p * channels : (p + 1) * channels, :])
            total = part if total is None else total + part
        lower[rows, :] = total
        return carry

    each_image(geometry, image, 0)

    def tap(p, carry):
        rows = pl.ds(pl.multiple_of(p * channels, channels), channels)
        grad[rows, :] = dot_tn(gated[...], nine[p]).astype(grad.dtype)
        return carry

    lax.fori_loop(0, 9, tap, 0)


def head_third_grad(geometry, small, pre, totals, sums, scale, cotangent, gated, kernel):
    return run(
        functools.partial(head_third_grad_body, geometry),
        [shape(kernel.shape, BF), shape(gated.shape, F32)],
        "svvvvvvv",
        (small, pre, totals, sums, scale, cotangent, gated, kernel),
        [pltpu.VMEM((9,) + pre.shape, BF)],
        vmem=56,
        flops=4 * pre.size * kernel.shape[0],
    )


def head_gate_body(geometry, small, lower, pre, totals, scale, features, sums):
    number, height, breadth = geometry

    def image(i, rows, carry):
        valid = valid_rows(small[i], height, breadth)
        normal, _, scaled = norm_of(pre[rows, :], totals[...], scale[...])
        gate = jax.nn.sigmoid(scaled)
        dy = lower[rows, :] * features[rows, :].astype(F32) * gate * (1.0 - gate) * valid
        return carry[0] + col_sum(dy), carry[1] + col_sum(dy * normal)

    put_sums(sums, each_image(geometry, image, zero_rows(2, pre.shape[1])))


def head_gate(geometry, small, lower, pre, totals, scale, features):
    return run(
        functools.partial(head_gate_body, geometry),
        [shape((8, pre.shape[1]), F32)],
        "svvvvv",
        (small, lower, pre, totals, scale, features),
    )[0]


def head_second_grad_body(
    geometry, small, lower, pre, totals, sums, scale, features, weight, hidden,
    pre_one, totals_one, scale_one, grad, upstream, sums_one, low,
):
    number, height, breadth = geometry

    def image(i, rows, carry):
        valid = valid_rows(small[i], height, breadth)
        normal, inverse, scaled = norm_of(pre[rows, :], totals[...], scale[...])
        gate = jax.nn.sigmoid(scaled)
        dy = lower[rows, :] * features[rows, :].astype(F32) * gate * (1.0 - gate) * valid
        dz = norm_back(dy, normal, inverse, totals[...], sums[...], scale[...], valid).astype(BF)
        low[rows, :] = dz
        normal, _, scaled = norm_of(pre_one[rows, :], totals_one[...], scale_one[...])
        dy = silu_back(scaled) * dot_nt(dz, weight[...]) * valid
        upstream[rows, :] = dy
        return carry[0] + col_sum(dy), carry[1] + col_sum(dy * normal)

    put_sums(sums_one, each_image(geometry, image, zero_rows(2, pre.shape[1])))
    grad[...] = dot_tn(hidden[...], low[...]).astype(grad.dtype)


def head_second_grad(
    geometry, small, lower, pre, totals, sums, scale, features, weight, hidden,
    pre_one, totals_one, scale_one,
):
    return run(
        functools.partial(head_second_grad_body, geometry),
        [shape(weight.shape, BF), shape(pre.shape, F32), shape((8, pre.shape[1]), F32)],
        "svvvvvvvvvvv",
        (small, lower, pre, totals, sums, scale, features, weight, hidden, pre_one, totals_one, scale_one),
        [pltpu.VMEM(pre.shape, BF)],
        flops=4 * pre.size * weight.shape[0],
    )


def head_first_grad_body(
    geometry, small, upstream, pre, totals, sums, scale, features, weight,
    lower, pre_two, totals_two, scale_two, grad, out, low,
):
    number, height, breadth = geometry

    def image(i, rows, carry):
        valid = valid_rows(small[i], height, breadth)
        normal, inverse, _ = norm_of(pre[rows, :], totals[...], scale[...])
        dz = norm_back(
            upstream[rows, :], normal, inverse, totals[...], sums[...], scale[...], valid
        ).astype(BF)
        low[rows, :] = dz
        _, _, scaled = norm_of(pre_two[rows, :], totals_two[...], scale_two[...])
        total = lower[rows, :] * jax.nn.sigmoid(scaled) + dot_nt(dz, weight[...])
        out[rows, :] = (total * valid).astype(BF)
        return carry

    each_image(geometry, image, 0)
    grad[...] = dot_tn(features[...], low[...]).astype(grad.dtype)


def head_first_grad(
    geometry, small, upstream, pre, totals, sums, scale, features, weight,
    lower, pre_two, totals_two, scale_two,
):
    return run(
        functools.partial(head_first_grad_body, geometry),
        [shape(weight.shape, BF), shape(pre.shape, BF)],
        "svvvvvvvvvvv",
        (small, upstream, pre, totals, sums, scale, features, weight, lower, pre_two, totals_two, scale_two),
        [pltpu.VMEM(pre.shape, BF)],
        flops=4 * pre.size * weight.shape[0],
    )


def to_taps_body(index, slots, enc, dec, wide, tap):
    count = slots.shape[0]
    channels = enc.shape[0]
    width = slots.shape[1]
    step = 1024

    def widen(i, carry):
        rows = pl.ds(pl.multiple_of(i * step, step), step)
        wide[rows, :] = slots[rows, :].astype(F32)
        return carry

    lax.fori_loop(0, count // step, widen, 0)
    group = 32
    for p in range(18):

        def fetch(i, carry):
            base = i * group
            for u in range(group):
                tap[pl.ds(base + u, 1), :] = wide[pl.ds(index[p * channels + base + u], 1), :]
            return carry

        lax.fori_loop(0, channels // group, fetch, 0)
        out = enc if p < 9 else dec
        q = p % 9
        out[:, q * width : (q + 1) * width] = tap[...].astype(BF)


def to_taps(index, slots, channels):
    width = slots.shape[1]
    return run(
        to_taps_body,
        [shape((channels, 9 * width), BF)] * 2,
        "sv",
        (index, slots),
        [pltpu.VMEM(slots.shape, F32), pltpu.VMEM((channels, width), F32)],
    )


def to_slots_body(index, enc, dec, slots, wide):
    count = slots.shape[0]
    channels = enc.shape[0]
    width = slots.shape[1]
    step = 1024
    group = 32
    for p in range(18):
        source = enc if p < 9 else dec
        q = p % 9

        def place(i, carry):
            base = pl.multiple_of(i * group, group)
            values = source[pl.ds(base, group), q * width : (q + 1) * width]
            for u in range(group):
                wide[pl.ds(index[p * channels + base + u], 1), :] = values[u : u + 1, :]
            return carry

        lax.fori_loop(0, channels // group, place, 0)

    def narrow(i, carry):
        rows = pl.ds(pl.multiple_of(i * step, step), step)
        slots[rows, :] = wide[rows, :].astype(BF)
        return carry

    lax.fori_loop(0, count // step, narrow, 0)


def to_slots(index, enc, dec):
    width = enc.shape[1] // 9
    dims = (index.shape[0], width)
    return run(
        to_slots_body, [shape(dims, BF)], "svv", (index, enc, dec), [pltpu.VMEM(dims, F32)]
    )[0]


def adam(gradient, moment_one, moment_two):
    new_one = BETA_ONE * moment_one + (1.0 - BETA_ONE) * gradient
    new_two = BETA_TWO * moment_two + (1.0 - BETA_TWO) * gradient * gradient
    direction = (
        new_one / (1.0 - BETA_ONE**STEP) / (jnp.sqrt(new_two / (1.0 - BETA_TWO**STEP)) + ADAM_EPS)
    )
    return new_one, new_two, direction


def soap_body(
    cuts, grad, owners, weight, one, two, basis, weight_new, one_new, two_new, low
):
    count = basis.shape[0]
    total = grad.shape[0]
    for m in range(count):
        low[m] = basis[m].astype(BF)

    def chunk(i, carry):
        rows = pl.ds(pl.multiple_of(i * (total // cuts), 8), total // cuts)
        values = grad[rows, :].astype(F32)
        rotated = None
        for m in range(count):
            part = dot((values * owners[rows, m : m + 1]).astype(BF), low[m])
            rotated = part if rotated is None else rotated + part
        new_one, new_two, direction = adam(rotated, one[rows, :], two[rows, :])
        one_new[rows, :] = new_one
        two_new[rows, :] = new_two
        stepped = None
        for m in range(count):
            part = dot_nt((direction * owners[rows, m : m + 1]).astype(BF), low[m])
            stepped = part if stepped is None else stepped + part
        old = weight[rows, :]
        weight_new[rows, :] = old - LEARN_MATRIX * (stepped + DECAY_MATRIX * old)
        return carry

    lax.fori_loop(0, cuts, chunk, 0)


def soap(grad, owners, weight, one, two, basis):
    total = grad.shape[0]
    cuts = 4 if total % 64 == 0 else 1
    return run(
        functools.partial(soap_body, cuts),
        [shape(weight.shape, F32)] * 3,
        "vvvvvv",
        (grad, owners, weight, one, two, basis),
        [pltpu.VMEM(basis.shape, BF)],
        flops=4 * weight.size * weight.shape[1] * basis.shape[0],
    )


def grams_body(grad, part, owners, grams):
    for m in range(grams.shape[0]):
        held = (grad[...].astype(F32) * owners[:, m : m + 1]).astype(BF)
        grams[m] = dot_tn(held, part[...])


def owner_grams(grad, part, owners):
    dims = (owners.shape[1], grad.shape[1], part.shape[1])
    return run(
        grams_body,
        [shape(dims, F32)],
        "vvv",
        (grad, part, owners),
        flops=2 * grad.size * part.shape[1] * owners.shape[1],
    )[0]


def factor_rows(values, identity, turn):
    width = values.shape[1]
    sub = lax.broadcasted_iota(jnp.int32, (8, width), 0)
    rolled = pltpu.roll(values, turn, 1)
    columns = [jnp.broadcast_to(rolled[:, j : j + 1], (8, width)) for j in range(8)]
    scale = jnp.zeros((8, width), F32)
    for j in range(8):
        root = lax.rsqrt(columns[j][j : j + 1, :])
        scale = jnp.where(sub == j, root, scale)
        lower = jnp.where(sub > j, columns[j] * root, 0.0)
        values = values - lower * (values[j : j + 1, :] * root)
        identity = identity - lower * (identity[j : j + 1, :] * root)
        for i in range(j + 1, 8):
            columns[i] = columns[i] - lower * (columns[i][j : j + 1, :] * root)
    return values * scale, identity * scale


def renew_body(stat, basis, gram, stat_new, basis_new, product, *work):
    count, size = stat.shape[0], stat.shape[1]
    panel = 128
    matrices = range(count)
    tables, inverses = work[:count], work[count:]
    row = lax.broadcasted_iota(jnp.int32, (panel, panel), 0)
    col = lax.broadcasted_iota(jnp.int32, (panel, panel), 1)
    unit = jnp.where(row == col, 1.0, 0.0).astype(F32)
    for m in matrices:
        stat_new[m] = STAT_DECAY * stat[m] + (1.0 - STAT_DECAY) * gram[m]
        product[m] = dot3(dot, stat_new[m], basis[m])
    for k in range(size // panel):
        here = slice(k * panel, (k + 1) * panel)
        for m in matrices:
            tables[m][:, :panel] = dot3(dot_tn, product[m, :, here], product[m, :, here])
            tables[m][:, panel:] = unit

        def group(q, carry):
            rows = pl.ds(pl.multiple_of(q * 8, 8), 8)
            turn = lax.rem(panel - q * 8, panel)
            done = [
                factor_rows(tables[m][rows, :panel], tables[m][rows, panel:], turn)
                for m in matrices
            ]
            for m in matrices:
                upper, inverse = done[m]
                inverses[m][rows, :] = inverse
                both = jnp.concatenate([upper, inverse], axis=1)
                tables[m][...] = tables[m][...] - dot3(dot_tn, upper, both)
            return carry

        lax.fori_loop(0, panel // 8, group, 0)
        for m in matrices:
            basis_new[m, :, here] = dot3(dot_nt, product[m, :, here], inverses[m][...])
            if k < size // panel - 1:
                rest = slice((k + 1) * panel, size)
                turned = basis_new[m, :, here]
                product[m, :, rest] = product[m, :, rest] - dot3(
                    dot, turned, dot3(dot_tn, turned, product[m, :, rest])
                )


def renew_basis(stat, basis, gram):
    count = stat.shape[0]
    return run(
        renew_body,
        [shape(stat.shape, F32)] * 2,
        "vvv",
        (stat, basis, gram),
        [pltpu.VMEM(stat.shape, F32)]
        + [pltpu.VMEM((128, 256), F32)] * count
        + [pltpu.VMEM((128, 128), F32)] * count,
        flops=12 * stat.size * stat.shape[1],
    )


def greet(axis, size):
    me = lax.axis_index(axis)
    barrier = pltpu.get_barrier_semaphore()
    for step in range(1, size):
        pl.semaphore_signal(
            barrier, inc=1, device_id={axis: lax.rem(me + step, size)}, device_id_type=MESH
        )
    pl.semaphore_wait(barrier, size - 1)
    return me


def remote(source, target, sends, receives, peer, axis):
    return pltpu.make_async_remote_copy(
        src_ref=source,
        dst_ref=target,
        send_sem=sends,
        recv_sem=receives,
        device_id={axis: peer},
        device_id_type=MESH,
    )


def exchange(body, outs, args, scratch, identity, vmem=32):
    size = sum(o.size * o.dtype.itemsize for o in outs) + sum(a.size * a.dtype.itemsize for a in args)
    return pl.pallas_call(
        body,
        out_shape=tuple(outs),
        in_specs=[VMEM_SPEC] * len(args),
        out_specs=tuple(VMEM_SPEC for _ in outs),
        scratch_shapes=list(scratch),
        compiler_params=pltpu.CompilerParams(
            vmem_limit_bytes=vmem * MIB, collective_id=identity, has_side_effects=True
        ),
        cost_estimate=pl.CostEstimate(flops=0, bytes_accessed=size, transcendentals=0),
    )(*args)


def total_body(axis, size, x, out, slots, sends, receives):
    me = greet(axis, size)
    copies = []
    for step in range(1, size):
        peer = lax.rem(me + step, size)
        copy = remote(x, slots.at[me], sends.at[step], receives.at[me], peer, axis)
        copy.start()
        copies.append(copy)
    slots[me] = x[...]
    for step in range(1, size):
        peer = lax.rem(me + size - step, size)
        remote(x, slots.at[peer], sends.at[step], receives.at[peer], peer, axis).wait_recv()
    total = slots[0]
    for peer in range(1, size):
        total = total + slots[peer]
    out[...] = total
    for copy in copies:
        copy.wait_send()


def total_over(axis, size, x, identity):
    return exchange(
        functools.partial(total_body, axis, size),
        [shape(x.shape, F32)],
        (x,),
        [
            pltpu.VMEM((size,) + x.shape, F32),
            pltpu.SemaphoreType.DMA((size,)),
            pltpu.SemaphoreType.DMA((size,)),
        ],
        identity,
    )[0]


def block_of(ref, place, size, dim):
    length = ref.shape[dim] // size
    start = place * length
    if dim == 0:
        return ref.at[pl.ds(pl.multiple_of(start, 8), length), :]
    return ref.at[:, pl.ds(pl.multiple_of(start, 128), length)]


def gather_body(axis, size, dims, *refs):
    count = len(dims)
    sources, targets = refs[:count], refs[count : 2 * count]
    sends, receives, own = refs[2 * count :]
    me = greet(axis, size)
    copies = []
    for k in range(count):
        mine = block_of(targets[k], me, size, dims[k])
        for step in range(1, size):
            peer = lax.rem(me + step, size)
            copy = remote(sources[k], mine, sends.at[k, step], receives.at[k, me], peer, axis)
            copy.start()
            copies.append(copy)
    locals_ = []
    for k in range(count):
        mine = block_of(targets[k], me, size, dims[k])
        copy = pltpu.make_async_copy(sources[k], mine, own.at[k])
        copy.start()
        locals_.append(copy)
    for copy in locals_:
        copy.wait()
    for k in range(count):
        for step in range(1, size):
            peer = lax.rem(me + size - step, size)
            theirs = block_of(targets[k], peer, size, dims[k])
            remote(
                sources[k], theirs, sends.at[k, step], receives.at[k, peer], peer, axis
            ).wait_recv()
    for copy in copies:
        copy.wait_send()


def gather_over(axis, size, arrays, dims, identity):
    outs = []
    for x, dim in zip(arrays, dims):
        full = list(x.shape)
        full[dim] *= size
        outs.append(shape(full, x.dtype))
    count = len(arrays)
    return exchange(
        functools.partial(gather_body, axis, size, tuple(dims)),
        outs,
        arrays,
        [
            pltpu.SemaphoreType.DMA((count, size)),
            pltpu.SemaphoreType.DMA((count, size)),
            pltpu.SemaphoreType.DMA((count,)),
        ],
        identity,
    )


def scatter_body(axis, size, dim, x, out, slots, sends, receives):
    me = greet(axis, size)
    copies = []
    for step in range(1, size):
        peer = lax.rem(me + step, size)
        copy = remote(
            block_of(x, peer, size, dim), slots.at[me], sends.at[step], receives.at[me], peer, axis
        )
        copy.start()
        copies.append(copy)
    out[...] = block_of(x, me, size, dim)[...].astype(F32)
    for step in range(1, size):
        peer = lax.rem(me + size - step, size)
        remote(
            block_of(x, peer, size, dim), slots.at[peer], sends.at[step], receives.at[peer], peer, axis
        ).wait_recv()
        out[...] = out[...] + slots[peer].astype(F32)
    for copy in copies:
        copy.wait_send()


def scatter_over(axis, size, x, dim, identity):
    part = list(x.shape)
    part[dim] //= size
    return exchange(
        functools.partial(scatter_body, axis, size, dim),
        [shape(part, F32)],
        (x,),
        [
            pltpu.VMEM((size,) + tuple(part), x.dtype),
            pltpu.SemaphoreType.DMA((size,)),
            pltpu.SemaphoreType.DMA((size,)),
        ],
        identity,
    )[0]


def local(
    tasks,
    batches,
    images,
    image_small,
    pool_index,
    row_slot,
    trunk_weight,
    trunk_mean_grad,
    trunk_mean_square,
    trunk_statistic,
    trunk_basis,
    head_weight,
    head_mean_grad,
    head_mean_square,
    head_statistic,
    head_basis,
    trunk_gain,
    trunk_offset,
    trunk_norm_mean_grad,
    trunk_norm_mean_square,
    head_gain,
    head_offset,
    head_norm_mean_grad,
    head_norm_mean_square,
    cotangent,
):
    number, height, breadth, channels = images.shape
    pixels = height * breadth
    tap_rows = 9 * channels
    shown = tasks * number
    geometry = (shown, height, breadth)
    task = lax.axis_index("task")
    batch = lax.axis_index("batch")
    width = channels // tasks

    def quarter(values):
        return lax.dynamic_slice_in_dim(values, task * width, width, values.ndim - 1)

    slots = lax.all_gather(quarter(trunk_weight).astype(BF), "batch", axis=0, tiled=True)
    head_rows = lax.all_gather(head_weight.astype(BF), "batch", axis=1, tiled=True)[0]
    kinds = jnp.concatenate([image_small, pool_index.reshape(-1)])
    kinds = lax.all_gather(kinds, "task", axis=0, tiled=True).reshape(tasks, -1)
    small = kinds[:, :number].reshape(-1)
    cells = kinds[:, number:].reshape(shown, height // 2, 1, breadth // 2, 1)
    cell = 2 * jnp.arange(2, dtype=jnp.int32)[:, None, None] + jnp.arange(2, dtype=jnp.int32)
    choose = (cells == cell).reshape(shown, height, breadth)
    row_limit = jnp.where(small > 0, height // 2, height)[:, None, None]
    col_limit = jnp.where(small > 0, breadth // 2, breadth)[:, None, None]
    inside = (jnp.arange(height, dtype=jnp.int32)[None, :, None] < row_limit) & (
        jnp.arange(breadth, dtype=jnp.int32)[None, None, :] < col_limit
    )
    choose = (choose & inside).astype(F32).reshape(shown * pixels, 1)
    inverse_slot = jnp.argsort(row_slot)
    own_valid = (
        (jnp.arange(height, dtype=jnp.int32)[None, :, None] < jnp.where(image_small > 0, height // 2, height)[:, None, None])
        & (jnp.arange(breadth, dtype=jnp.int32)[None, None, :] < jnp.where(image_small > 0, breadth // 2, breadth)[:, None, None])
    )[..., None]
    masked = (images * own_valid.astype(BF)).reshape(number * pixels, channels)
    x = gather_over("task", tasks, (masked,), (0,), 1)[0]
    enc_taps, dec_taps = to_taps(row_slot, slots, channels)

    scales = quarter(jnp.stack([trunk_gain, trunk_offset], axis=1))
    enc_pre, stats = trunk_conv(geometry, small, x, enc_taps)
    enc_totals = total_over("batch", batches, stats, 2)
    spread = enc_act(geometry, small, enc_pre, enc_totals, scales[0], choose)
    spread = gather_over("task", tasks, (spread,), (1,), 3)[0]
    dec_pre, stats = trunk_conv(geometry, small, spread, dec_taps)
    dec_totals = total_over("batch", batches, stats, 2)
    features = dec_act(geometry, small, dec_pre, dec_totals, scales[1])
    features = gather_over("task", tasks, (features,), (1,), 3)[0]

    first = head_rows[:channels]
    second = head_rows[channels : 2 * channels]
    kernel = head_rows[2 * channels :]
    head_scales = jnp.stack([head_gain[0], head_offset[0]], axis=1)
    cot = cotangent.reshape(shown, pixels // 4, channels)
    pre_one, stats = head_first(geometry, small, features, first)
    totals_one = total_over("batch", batches, stats, 4)
    hidden, pre_two, stats = head_second(
        geometry, small, pre_one, totals_one, head_scales[0], second
    )
    totals_two = total_over("batch", batches, stats, 4)
    gated, pre_three, stats = head_third(
        geometry, small, pre_two, totals_two, head_scales[1], features, kernel
    )
    totals_three = total_over("batch", batches, stats, 4)
    pooled, sums = head_out(geometry, small, pre_three, totals_three, head_scales[2], cot)
    task_features = pooled.reshape(cotangent.shape)

    sums_three = total_over("batch", batches, sums, 4)
    kernel_grad, lower = head_third_grad(
        geometry, small, pre_three, totals_three, sums_three, head_scales[2], cot, gated, kernel
    )
    sums = head_gate(geometry, small, lower, pre_two, totals_two, head_scales[1], features)
    sums_two = total_over("batch", batches, sums, 4)
    second_grad, upstream, sums = head_second_grad(
        geometry, small, lower, pre_two, totals_two, sums_two, head_scales[1], features, second,
        hidden, pre_one, totals_one, head_scales[0],
    )
    sums_one = total_over("batch", batches, sums, 4)
    first_grad, feature_grad = head_first_grad(
        geometry, small, upstream, pre_one, totals_one, sums_one, head_scales[0], features, first,
        lower, pre_two, totals_two, head_scales[1],
    )
    head_grads = jnp.concatenate([first_grad, second_grad, kernel_grad], axis=0)
    head_owned = lax.psum_scatter(head_grads, "batch", scatter_dimension=0, tiled=True)

    upstream = scatter_over("task", tasks, feature_grad, 1, 5)
    sums = trunk_sums(geometry, False, small, upstream, dec_pre, dec_totals, scales[1], choose)
    dec_sums = total_over("batch", batches, sums, 2)
    dec_grad, lower = trunk_back(
        geometry, False, small, upstream, dec_pre, dec_totals, dec_sums, scales[1], choose, spread,
        dec_taps,
    )
    upstream = scatter_over("task", tasks, lower, 1, 5)
    sums = trunk_sums(geometry, True, small, upstream, enc_pre, enc_totals, scales[0], choose)
    enc_sums = total_over("batch", batches, sums, 2)
    enc_grad, lower = trunk_back(
        geometry, True, small, upstream, enc_pre, enc_totals, enc_sums, scales[0], choose, x,
        enc_taps,
    )
    trunk_part = lax.psum_scatter(
        to_slots(row_slot, enc_grad, dec_grad), "batch", scatter_dimension=0, tiled=True
    )
    input_grad = scatter_over("task", tasks, lower, 0, 6).reshape(images.shape)

    head_local = head_weight.shape[1]
    head_ids = batch * head_local + jnp.arange(head_local, dtype=jnp.int32)
    head_owner = jnp.minimum(head_ids // channels, 2)
    head_onehot = (head_owner[:, None] == jnp.arange(3, dtype=jnp.int32)).astype(F32)
    head_grams = lax.psum(owner_grams(head_owned, head_owned, head_onehot).astype(BF), "batch")
    head_weight_new, head_one_new, head_two_new = soap(
        head_owned, head_onehot, head_weight[0], head_mean_grad[0], head_mean_square[0],
        head_basis[0],
    )
    head_stat_new, head_basis_new = renew_basis(head_statistic[0], head_basis[0], head_grams.astype(F32))

    norm_part = jnp.concatenate([enc_sums[:2], dec_sums[:2], jnp.zeros((4, width), F32)], axis=0)
    trunk_owned, norm_sums = gather_over("task", tasks, (trunk_part, norm_part), (1, 1), 7)
    local_rows = trunk_weight.shape[0]
    slot_ids = batch * local_rows + jnp.arange(local_rows, dtype=jnp.int32)
    trunk_owner = jnp.take(inverse_slot, slot_ids) // tap_rows
    trunk_onehot = (trunk_owner[:, None] == jnp.arange(2, dtype=jnp.int32)).astype(F32)
    trunk_grams = lax.psum(owner_grams(trunk_owned, trunk_part, trunk_onehot), "batch").astype(BF)
    trunk_grams = gather_over(
        "task", tasks, (trunk_grams.reshape(2 * channels, width),), (1,), 8
    )[0].reshape(2, channels, channels)
    trunk_weight_new, trunk_one_new, trunk_two_new = soap(
        trunk_owned, trunk_onehot, trunk_weight, trunk_mean_grad, trunk_mean_square, trunk_basis
    )
    trunk_stat_new, trunk_basis_new = renew_basis(trunk_statistic, trunk_basis, trunk_grams.astype(F32))

    trunk_norm = jnp.stack([trunk_gain, trunk_offset], axis=1)
    trunk_norm_grad = norm_sums[:4].reshape(2, 2, channels)[:, ::-1]
    trunk_norm_one, trunk_norm_two, trunk_direction = adam(
        trunk_norm_grad, trunk_norm_mean_grad, trunk_norm_mean_square
    )
    head_norm = jnp.stack([head_gain, head_offset], axis=2)
    head_norm_grad = jnp.stack([sums_one[:2], sums_two[:2], sums_three[:2]])[None, :, ::-1]
    head_norm_one, head_norm_two, head_direction = adam(
        head_norm_grad, head_norm_mean_grad, head_norm_mean_square
    )
    return (
        task_features,
        input_grad,
        trunk_weight_new,
        trunk_one_new,
        trunk_two_new,
        trunk_stat_new,
        trunk_basis_new,
        head_weight_new[None],
        head_one_new[None],
        head_two_new[None],
        head_stat_new[None],
        head_basis_new[None],
        trunk_norm - LEARN_NORM * trunk_direction,
        trunk_norm_one,
        trunk_norm_two,
        head_norm - LEARN_NORM * head_direction,
        head_norm_one,
        head_norm_two,
    )


def solution(mesh):
    placed = (
        P(("task", "batch"), None, None, None),
        P(("task", "batch")),
        P(("task", "batch"), None, None),
        P(),
        P("batch", None),
        P("batch", None),
        P("batch", None),
        P(),
        P(),
        P("task", "batch", None),
        P("task", "batch", None),
        P("task", "batch", None),
        P("task", None, None, None),
        P("task", None, None, None),
        P(),
        P(),
        P(),
        P(),
        P("task", None, None),
        P("task", None, None),
        P("task", None, None, None),
        P("task", None, None, None),
        P("task", None, "batch", None, None, None),
    )
    return jax.shard_map(
        functools.partial(local, mesh.shape["task"], mesh.shape["batch"]),
        mesh=mesh,
        in_specs=placed,
        out_specs=(
            P("task", None, "batch", None, None, None),
            P(("task", "batch"), None, None, None),
            P("batch", None),
            P("batch", None),
            P("batch", None),
            P(),
            P(),
            P("task", "batch", None),
            P("task", "batch", None),
            P("task", "batch", None),
            P("task", None, None, None),
            P("task", None, None, None),
            P(),
            P(),
            P(),
            P("task", None, None, None),
            P("task", None, None, None),
            P("task", None, None, None),
        ),
        check_vma=False,
    )
```

```python
import functools

import jax
import jax.numpy as jnp
from jax import lax
from jax.experimental import pallas as pl
from jax.experimental.pallas import tpu as pltpu
from jax.sharding import PartitionSpec as P

STEP = 10


EPS = 1e-05
ADAM_EPS = 1e-08
BETA_ONE = 0.95
BETA_TWO = 0.95
STAT_DECAY = 0.95
LEARN_MATRIX = 0.02
LEARN_NORM = 0.5
DECAY_MATRIX = 0.01
BF = jnp.bfloat16
F32 = jnp.float32
MESH = pl.DeviceIdType.MESH
MIB = 1 << 20

VMEM_SPEC = pl.BlockSpec(memory_space=pltpu.VMEM)
SMEM_SPEC = pl.BlockSpec(memory_space=pltpu.SMEM)


def run(body, outs, specs, args, scratch=(), vmem=40, flops=0):
    size = sum(o.size * o.dtype.itemsize for o in outs) + sum(a.size * a.dtype.itemsize for a in args)
    return pl.pallas_call(
        body,
        out_shape=tuple(outs),
        in_specs=[SMEM_SPEC if s == "s" else VMEM_SPEC for s in specs],
        out_specs=tuple(VMEM_SPEC for _ in outs),
        scratch_shapes=list(scratch),
        compiler_params=pltpu.CompilerParams(vmem_limit_bytes=vmem * MIB),
        cost_estimate=pl.CostEstimate(flops=flops, bytes_accessed=size, transcendentals=0),
    )(*args)


def shape(dims, kind):
    return jax.ShapeDtypeStruct(tuple(dims), kind)


def dot(a, b):
    return jnp.dot(a, b, preferred_element_type=F32)


def dot_nt(a, b):
    return lax.dot_general(a, b, (((1,), (1,)), ((), ())), preferred_element_type=F32)


def dot_tn(a, b):
    return lax.dot_general(a, b, (((0,), (0,)), ((), ())), preferred_element_type=F32)


def split(a):
    high = a.astype(BF)
    return high, (a - high.astype(F32)).astype(BF)


def dot3(kind, a, b):
    a_high, a_low = split(a)
    b_high, b_low = split(b)
    return kind(a_high, b_high) + (kind(a_high, b_low) + kind(a_low, b_high))


def places(height, breadth):
    index = lax.broadcasted_iota(jnp.int32, (height * breadth, 1), 0)
    row = lax.div(index, breadth)
    return row, index - row * breadth


def valid_rows(small, height, breadth):
    row, col = places(height, breadth)
    row_limit = jnp.where(small > 0, height // 2, height)
    col_limit = jnp.where(small > 0, breadth // 2, breadth)
    return jnp.where((row < row_limit) & (col < col_limit), 1.0, 0.0).astype(F32)


def move(values, rows):
    gap = jnp.zeros((abs(rows),) + values.shape[1:], values.dtype)
    if rows > 0:
        return jnp.concatenate([gap, values[:-rows]], axis=0)
    return jnp.concatenate([values[-rows:], gap], axis=0)


def from_left(values, col):
    return jnp.where(col > 0, pltpu.roll(values, 1, 0), 0.0)


def from_right(values, col, breadth):
    return jnp.where(col < breadth - 1, pltpu.roll(values, values.shape[0] - 1, 0), 0.0)


def gather_taps(tap, breadth, col):
    lines = [move(tap(b), breadth) + tap(3 + b) + move(tap(6 + b), -breadth) for b in range(3)]
    return lines[1] + from_left(lines[0], col) + from_right(lines[2], col, breadth)


def spread_taps(values, breadth, col):
    lines = [from_right(values, col, breadth), values, from_left(values, col)]
    return [
        move(lines[b], breadth * (a - 1)) if a != 1 else lines[b] for a in range(3) for b in range(3)
    ]


def window_sum(values, row, col, breadth):
    count = values.shape[0]
    pair = values + jnp.where(
        col % 2 == 0, pltpu.roll(values, count - 1, 0), pltpu.roll(values, 1, 0)
    )
    return pair + jnp.where(row % 2 == 0, move(pair, -breadth), move(pair, breadth))


def silu_back(scaled):
    sig = jax.nn.sigmoid(scaled)
    return sig * (1.0 + scaled * (1.0 - sig))


def col_sum(values):
    return jnp.sum(values, axis=0, keepdims=True)


def put_sums(ref, rows):
    width = ref.shape[1]
    rows = list(rows) + [jnp.zeros((1, width), F32)] * (8 - len(rows))
    ref[...] = jnp.concatenate(rows, axis=0)


def each_image(geometry, body, start):
    number, height, breadth = geometry
    pixels = height * breadth

    def step(image, carry):
        return body(image, pl.ds(pl.multiple_of(image * pixels, 16), pixels), carry)

    return lax.fori_loop(0, number, step, start)


def zero_rows(count, width):
    return (jnp.zeros((1, width), F32),) * count


def greet(axes):
    barrier = pltpu.get_barrier_semaphore()
    for axis, size in axes:
        me = lax.axis_index(axis)
        for step in range(1, size):
            pl.semaphore_signal(
                barrier, inc=1, device_id={axis: lax.rem(me + step, size)}, device_id_type=MESH
            )
    pl.semaphore_wait(barrier, sum(size - 1 for _, size in axes))


def remote(source, target, sends, receives, peer, axis):
    return pltpu.make_async_remote_copy(
        src_ref=source,
        dst_ref=target,
        send_sem=sends,
        recv_sem=receives,
        device_id={axis: peer},
        device_id_type=MESH,
    )


def pack(rows):
    parts = [row[:, i : i + 128] for row in rows for i in range(0, row.shape[1], 128)]
    parts += [jnp.zeros((1, 128), F32)] * (8 - len(parts))
    return jnp.concatenate(parts, axis=0)


def unpack(tile, count, width):
    per = width // 128
    return [
        jnp.concatenate([tile[k * per + i : k * per + i + 1, :] for i in range(per)], axis=1)
        for k in range(count)
    ]


def total_rows(k, axis, size, rows, mine, slots, sends, receives):
    me = lax.axis_index(axis)
    tile = pack(rows)
    mine[k] = tile
    slots[k, me] = tile
    for step in range(1, size):
        peer = lax.rem(me + step, size)
        remote(mine.at[k], slots.at[k, me], sends.at[k, step], receives.at[k, me], peer, axis).start()
    for step in range(1, size):
        peer = lax.rem(me + size - step, size)
        remote(
            mine.at[k], slots.at[k, peer], sends.at[k, step], receives.at[k, peer], peer, axis
        ).wait_recv()
    total = slots[k, 0]
    for peer in range(1, size):
        total = total + slots[k, peer]
    for step in range(1, size):
        peer = lax.rem(me + step, size)
        remote(
            mine.at[k], slots.at[k, me], sends.at[k, step], receives.at[k, me], peer, axis
        ).wait_send()
    return unpack(total, len(rows), rows[0].shape[1])


def total_scratch(count, size):
    return [
        pltpu.VMEM((count, 8, 128), F32),
        pltpu.VMEM((count, size, 8, 128), F32),
        pltpu.SemaphoreType.DMA((count, size)),
        pltpu.SemaphoreType.DMA((count, size)),
    ]


def columns_of(place, width):
    return pl.ds(pl.multiple_of(place * width, 128), width)


def exchange_kernel(body, outs, specs, args, scratch, identity, vmem, flops=0):
    size = sum(o.size * o.dtype.itemsize for o in outs) + sum(a.size * a.dtype.itemsize for a in args)
    return pl.pallas_call(
        body,
        out_shape=tuple(outs),
        in_specs=[SMEM_SPEC if s == "s" else VMEM_SPEC for s in specs],
        out_specs=tuple(VMEM_SPEC for _ in outs),
        scratch_shapes=list(scratch),
        compiler_params=pltpu.CompilerParams(
            vmem_limit_bytes=vmem * MIB, collective_id=identity, has_side_effects=True
        ),
        cost_estimate=pl.CostEstimate(flops=flops, bytes_accessed=size, transcendentals=0),
    )(*args)


def norm_with(values, totals, scale):
    total, squares, count = totals
    center = total / count
    inverse = lax.rsqrt(squares / count - center * center + EPS)
    normal = (values - center) * inverse
    return normal, inverse, normal * scale[0] + scale[1]


def norm_back_with(upstream, normal, inverse, count, sums, scale, valid):
    return scale[0] * inverse * (upstream - sums[0] / count - normal * (sums[1] / count)) * valid


def silu(values):
    return values * jax.nn.sigmoid(values)


def window_count(height, breadth):
    return -(-(height * breadth // 4) // 16) * 16


def pool_choice(height, breadth, windows, flipped):
    pixels = height * breadth
    dims = (windows, pixels) if flipped else (pixels, windows)
    pixel = lax.broadcasted_iota(jnp.int32, dims, 1 if flipped else 0)
    window = lax.broadcasted_iota(jnp.int32, dims, 0 if flipped else 1)
    row = lax.div(pixel, breadth)
    col = pixel - row * breadth
    home = lax.div(row, 2) * (breadth // 2) + lax.div(col, 2)
    return jnp.where(home == window, 1.0, 0.0).astype(F32)


def rows_of(ref, first, count):
    return [ref[first + k : first + k + 1, :] for k in range(count)]


def window_rows(i, windows):
    return pl.ds(pl.multiple_of(i * windows, 16), windows)


def trunk_forward_body(
    geometry, tasks, batches,
    small, x, enc_taps, dec_taps, scales, choose,
    enc_pre, enc_totals, spread, dec_pre, dec_totals, features,
    work, pooled, pooled_all, part, pool_sends, pool_receives, sends, receives,
    mine, slots, total_sends, total_receives,
):
    number, height, breadth = geometry
    width = enc_pre.shape[1]
    windows = window_count(height, breadth)
    task = lax.axis_index("task")
    _, col = places(height, breadth)
    widen = pool_choice(height, breadth, windows, False).astype(BF)
    narrow = pool_choice(height, breadth, windows, True).astype(BF)

    def conv(x, taps, pre):
        def image(i, rows, carry):
            valid = valid_rows(small[i], height, breadth)
            work[...] = dot(x[rows, :], taps[...])
            out = gather_taps(lambda p: work[:, p * width : (p + 1) * width], breadth, col)
            pre[rows, :] = out
            kept = out * valid
            return (
                carry[0] + col_sum(kept),
                carry[1] + col_sum(kept * out),
                carry[2] + jnp.broadcast_to(col_sum(valid), (1, width)),
            )

        return each_image(geometry, image, zero_rows(3, width))

    def total(k, rows):
        return total_rows(
            k, "batch", batches, list(rows), mine, slots, total_sends, total_receives
        )

    sums = conv(x, enc_taps, enc_pre)
    greet((("task", tasks), ("batch", batches)))
    totals = total(0, sums)
    put_sums(enc_totals, totals)
    scale = rows_of(scales, 0, 2)

    def peer_of(step, incoming):
        return lax.rem(task + (tasks - step if incoming else step), tasks)

    def pool_copy(i, step, incoming=False):
        rows = window_rows(i, windows)
        peer = peer_of(step, incoming)
        target = pooled_all.at[rows, columns_of(peer if incoming else task, width)]
        return remote(
            pooled.at[rows, :], target, pool_sends.at[i, step], pool_receives.at[i, step], peer, "task"
        )

    def pool(i, rows, carry):
        valid = valid_rows(small[i], height, breadth)
        _, _, scaled = norm_with(enc_pre[rows, :], totals, scale)
        high, low = split(silu(scaled) * valid)
        mean = ((dot(narrow, high) + dot(narrow, low)) * 0.25).astype(BF)
        here = window_rows(i, windows)
        pooled[here, :] = mean
        pooled_all[here, columns_of(task, width)] = mean
        for step in range(1, tasks):
            pool_copy(i, step).start()
        return carry

    each_image(geometry, pool, 0)

    def unpool(i, rows, carry):
        for step in range(1, tasks):
            pool_copy(i, step, True).wait_recv()
        wide = dot(widen, pooled_all[window_rows(i, windows), :])
        spread[rows, :] = (wide * choose[rows, :]).astype(BF)
        return carry

    each_image(geometry, unpool, 0)
    sums = conv(spread, dec_taps, dec_pre)
    totals = total(1, sums)
    put_sums(dec_totals, totals)
    scale = rows_of(scales, 2, 2)

    def feature_copy(i, rows, step, incoming=False):
        peer = peer_of(step, incoming)
        target = features.at[rows, columns_of(peer if incoming else task, width)]
        return remote(
            part.at[rows, :], target, sends.at[i, step], receives.at[i, step], peer, "task"
        )

    def finish(i, rows, carry):
        valid = valid_rows(small[i], height, breadth)
        _, _, scaled = norm_with(dec_pre[rows, :], totals, scale)
        low = (silu(scaled) * valid).astype(BF)
        part[rows, :] = low
        features[rows, columns_of(task, width)] = low
        for step in range(1, tasks):
            feature_copy(i, rows, step).start()
        return carry

    each_image(geometry, finish, 0)

    def settle(i, rows, carry):
        for step in range(1, tasks):
            feature_copy(i, rows, step, True).wait_recv()
            feature_copy(i, rows, step).wait_send()
            pool_copy(i, step).wait_send()
        return carry

    each_image(geometry, settle, 0)


def trunk_forward(geometry, tasks, batches, small, x, enc_taps, dec_taps, scales, choose):
    number, height, breadth = geometry
    pixels = height * breadth
    channels = x.shape[1]
    width = channels // tasks
    windows = window_count(height, breadth)
    return exchange_kernel(
        functools.partial(trunk_forward_body, geometry, tasks, batches),
        [
            shape((x.shape[0], width), F32),
            shape((8, width), F32),
            shape(x.shape, BF),
            shape((x.shape[0], width), F32),
            shape((8, width), F32),
            shape(x.shape, BF),
        ],
        "svvvvv",
        (small, x, enc_taps, dec_taps, scales, choose),
        [
            pltpu.VMEM((pixels, 9 * width), F32),
            pltpu.VMEM((number * windows, width), BF),
            pltpu.VMEM((number * windows, channels), BF),
            pltpu.VMEM((x.shape[0], width), BF),
        ]
        + [pltpu.SemaphoreType.DMA((number, tasks))] * 4
        + total_scratch(2, batches),
        1,
        32,
        flops=4 * x.size * enc_taps.shape[1],
    )


def head_body(
    geometry, tasks, batches,
    small, features, rows_in, cotangent, scales, counts,
    task_out, grads, upstream, norm_sums,
    pre_one, pre_two, pre_three, hidden, gated, nine, work, lower, out, arrived, sends, receives,
    mine, slots, total_sends, total_receives,
):
    number, height, breadth = geometry
    channels = features.shape[1]
    width = channels // tasks
    windows = task_out.shape[1]
    task = lax.axis_index("task")
    half = work.shape[2]
    _, col = places(height, breadth)
    widen = pool_choice(height, breadth, windows, False).astype(BF)
    narrow = pool_choice(height, breadth, windows, True).astype(BF)
    count = jnp.broadcast_to(counts[2:3, 0:1], (1, channels))
    first = rows_in.at[pl.ds(0, channels), :]
    second = rows_in.at[pl.ds(channels, channels), :]

    def kernel_rows(p):
        return pl.ds((2 + p) * channels, channels)

    def total(k, rows):
        return total_rows(
            k, "batch", batches, list(rows), mine, slots, total_sends, total_receives
        )

    def put_stats(pre, rows, value, valid, carry):
        pre[rows, :] = value
        kept = value * valid
        return carry[0] + col_sum(kept), carry[1] + col_sum(kept * value)

    nothing = zero_rows(2, channels)
    scale_one, scale_two, scale_three = (rows_of(scales, 2 * k, 2) for k in range(3))

    def first_step(i, rows, carry):
        valid = valid_rows(small[i], height, breadth)
        return put_stats(pre_one, rows, dot(features[rows, :], first[...]), valid, carry)

    sums = each_image(geometry, first_step, nothing)
    greet((("task", tasks), ("batch", batches)))
    totals_one = total(0, sums) + [count]

    def second_step(i, rows, carry):
        valid = valid_rows(small[i], height, breadth)
        _, _, scaled = norm_with(pre_one[rows, :], totals_one, scale_one)
        low = (silu(scaled) * valid).astype(BF)
        hidden[rows, :] = low
        return put_stats(pre_two, rows, dot(low, second[...]), valid, carry)

    sums = each_image(geometry, second_step, nothing)
    totals_two = total(1, sums) + [count]

    def third_step(i, rows, carry):
        valid = valid_rows(small[i], height, breadth)
        _, _, scaled = norm_with(pre_two[rows, :], totals_two, scale_two)
        low = (jax.nn.sigmoid(scaled) * features[rows, :].astype(F32)).astype(BF)
        gated[rows, :] = low
        parts = []
        for j in range(channels // half):
            cut = slice(j * half, (j + 1) * half)
            for p in range(9):
                work[p] = dot(low, rows_in[kernel_rows(p), cut])
            parts.append(gather_taps(lambda p: work[p], breadth, col))
        return put_stats(pre_three, rows, jnp.concatenate(parts, axis=1), valid, carry)

    sums = each_image(geometry, third_step, nothing)
    totals_three = total(2, sums) + [count]

    def out_step(i, rows, carry):
        valid = valid_rows(small[i], height, breadth)
        normal, _, scaled = norm_with(pre_three[rows, :], totals_three, scale_three)
        high, low = split(silu(scaled) * valid)
        mean = (dot(narrow, high) + dot(narrow, low)) * 0.25
        task_out[i] = mean.astype(BF)
        dy = silu_back(scaled) * dot(widen, cotangent[i]) * 0.25 * valid
        lower[rows, :] = dy
        return carry[0] + col_sum(dy), carry[1] + col_sum(dy * normal)

    sums = each_image(geometry, out_step, nothing)
    sums_three = total(3, sums)

    def third_back(i, rows, carry):
        valid = valid_rows(small[i], height, breadth)
        normal, inverse, _ = norm_with(pre_three[rows, :], totals_three, scale_three)
        dz = norm_back_with(lower[rows, :], normal, inverse, count, sums_three, scale_three, valid)
        for p, moved in enumerate(spread_taps(dz, breadth, col)):
            nine[p, rows, :] = moved.astype(BF)
        flow = None
        for p in range(9):
            piece = dot_nt(nine[p, rows, :], rows_in[kernel_rows(p), :])
            flow = piece if flow is None else flow + piece
        lower[rows, :] = flow
        normal, _, scaled = norm_with(pre_two[rows, :], totals_two, scale_two)
        gate = jax.nn.sigmoid(scaled)
        dy = flow * features[rows, :].astype(F32) * gate * (1.0 - gate) * valid
        pre_three[rows, :] = dy
        return carry[0] + col_sum(dy), carry[1] + col_sum(dy * normal)

    sums = each_image(geometry, third_back, nothing)
    sums_two = total(4, sums)

    def second_back(i, rows, carry):
        valid = valid_rows(small[i], height, breadth)
        normal, inverse, scaled = norm_with(pre_two[rows, :], totals_two, scale_two)
        dz = norm_back_with(
            pre_three[rows, :], normal, inverse, count, sums_two, scale_two, valid
        ).astype(BF)
        out[rows, :] = dz
        lower[rows, :] = lower[rows, :] * jax.nn.sigmoid(scaled)
        normal, _, scaled = norm_with(pre_one[rows, :], totals_one, scale_one)
        dy = silu_back(scaled) * dot_nt(dz, second[...]) * valid
        pre_three[rows, :] = dy
        return carry[0] + col_sum(dy), carry[1] + col_sum(dy * normal)

    sums = each_image(geometry, second_back, nothing)
    sums_one = total(5, sums)
    grads[pl.ds(channels, channels), :] = dot_tn(hidden[...], out[...]).astype(BF)

    def flow_copy(i, rows, step, incoming=False):
        peer = lax.rem(task + (tasks - step if incoming else step), tasks)
        return remote(
            out.at[rows, columns_of(peer, width)], arrived.at[step - 1, rows, :],
            sends.at[i, step], receives.at[i, step], peer, "task",
        )

    def first_back(i, rows, carry):
        valid = valid_rows(small[i], height, breadth)
        normal, inverse, _ = norm_with(pre_one[rows, :], totals_one, scale_one)
        dz = norm_back_with(
            pre_three[rows, :], normal, inverse, count, sums_one, scale_one, valid
        ).astype(BF)
        hidden[rows, :] = dz
        flow = (lower[rows, :] + dot_nt(dz, first[...])) * valid
        out[rows, :] = flow.astype(BF)
        for step in range(1, tasks):
            flow_copy(i, rows, step).start()
        return carry

    each_image(geometry, first_back, 0)
    grads[pl.ds(0, channels), :] = dot_tn(features[...], hidden[...]).astype(BF)

    def tap(p, carry):
        rows = pl.ds(pl.multiple_of((2 + p) * channels, channels), channels)
        grads[rows, :] = dot_tn(gated[...], nine[p]).astype(BF)
        return carry

    lax.fori_loop(0, 9, tap, 0)
    put_sums(norm_sums, sums_one + sums_two + sums_three)

    def settle(i, rows, carry):
        for step in range(1, tasks):
            flow_copy(i, rows, step, True).wait_recv()
        flow = out[rows, columns_of(task, width)].astype(F32)
        for step in range(1, tasks):
            flow = flow + arrived[step - 1, rows, :].astype(F32)
        upstream[rows, :] = flow
        for step in range(1, tasks):
            flow_copy(i, rows, step).wait_send()
        return carry

    each_image(geometry, settle, 0)


def head(geometry, tasks, batches, small, features, rows_in, cotangent, scales, counts):
    number, height, breadth = geometry
    pixels = height * breadth
    total, channels = features.shape
    width = channels // tasks
    return exchange_kernel(
        functools.partial(head_body, geometry, tasks, batches),
        [
            shape((number, pixels // 4, channels), BF),
            shape(rows_in.shape, BF),
            shape((total, width), F32),
            shape((8, channels), F32),
        ],
        "svvvvv",
        (small, features, rows_in, cotangent, scales, counts),
        [
            pltpu.VMEM(features.shape, F32),
            pltpu.VMEM(features.shape, F32),
            pltpu.VMEM(features.shape, F32),
            pltpu.VMEM(features.shape, BF),
            pltpu.VMEM(features.shape, BF),
            pltpu.VMEM((9,) + features.shape, BF),
            pltpu.VMEM((9, pixels, min(channels, 256)), F32),
            pltpu.VMEM(features.shape, F32),
            pltpu.VMEM(features.shape, BF),
            pltpu.VMEM((tasks - 1, total, width), BF),
        ]
        + [pltpu.SemaphoreType.DMA((number, tasks))] * 2
        + total_scratch(6, batches),
        2,
        60,
        flops=6 * total * channels * rows_in.shape[0],
    )


def trunk_backward_body(
    geometry, tasks, batches,
    small, upstream, enc_pre, enc_totals, dec_pre, dec_totals, scales, choose, choose_row,
    x, spread, enc_taps, dec_taps,
    enc_grad, dec_grad, flow_out, norm_sums,
    nine, change, packed, arrived, pooled, sends, receives,
    mine, slots, total_sends, total_receives,
):
    number, height, breadth = geometry
    channels = x.shape[1]
    width = enc_pre.shape[1]
    windows = window_count(height, breadth)
    task = lax.axis_index("task")
    _, col = places(height, breadth)
    widen = pool_choice(height, breadth, windows, False).astype(BF)
    narrow = pool_choice(height, breadth, windows, True)
    nothing = zero_rows(2, width)

    def total(k, rows):
        return total_rows(
            k, "batch", batches, list(rows), mine, slots, total_sends, total_receives
        )

    def change_of(pre, totals, scale, flow):
        def image(i, rows, carry):
            valid = valid_rows(small[i], height, breadth)
            normal, _, scaled = norm_with(pre[rows, :], totals, scale)
            dy = silu_back(scaled) * flow(i, rows) * valid
            change[rows, :] = dy
            return carry[0] + col_sum(dy), carry[1] + col_sum(dy * normal)

        return each_image(geometry, image, nothing)

    def back(pre, totals, scale, sums, taps, put):
        def image(i, rows, carry):
            valid = valid_rows(small[i], height, breadth)
            normal, inverse, _ = norm_with(pre[rows, :], totals, scale)
            dz = norm_back_with(change[rows, :], normal, inverse, totals[2], sums, scale, valid)
            for p, moved in enumerate(spread_taps(dz, breadth, col)):
                nine[rows, p * width : (p + 1) * width] = moved.astype(BF)
            put(i, rows, dot_nt(nine[rows, :], taps[...]) * valid)
            return carry

        each_image(geometry, image, 0)

    totals = rows_of(dec_totals, 0, 3)
    scale = rows_of(scales, 2, 2)
    sums = change_of(dec_pre, totals, scale, lambda i, rows: upstream[rows, :])
    greet((("task", tasks), ("batch", batches)))
    dec_sums = total(0, sums)

    def copy_of(i, step, incoming=False):
        rows = window_rows(i, windows)
        peer = lax.rem(task + (tasks - step if incoming else step), tasks)
        return remote(
            packed.at[rows, columns_of(peer, width)], arrived.at[step - 1, rows, :],
            sends.at[i, step], receives.at[i, step], peer, "task",
        )

    def put_packed(i, rows, flow):
        chosen = (narrow * choose_row[i]).astype(BF)
        packed[window_rows(i, windows), :] = dot(chosen, flow.astype(BF)).astype(BF)
        for step in range(1, tasks):
            copy_of(i, step).start()

    back(dec_pre, totals, scale, dec_sums, dec_taps, put_packed)
    dec_grad[...] = dot_tn(spread[...], nine[...])

    def collect(i, carry):
        for step in range(1, tasks):
            copy_of(i, step, True).wait_recv()
        rows = window_rows(i, windows)
        flow = packed[rows, columns_of(task, width)].astype(F32)
        for step in range(1, tasks):
            flow = flow + arrived[step - 1, rows, :].astype(F32)
        pooled[rows, :] = flow
        for step in range(1, tasks):
            copy_of(i, step).wait_send()
        return carry

    lax.fori_loop(0, number, collect, 0)

    def widened(i, rows):
        high, low = split(pooled[window_rows(i, windows), :])
        return (dot(widen, high) + dot(widen, low)) * 0.25

    totals = rows_of(enc_totals, 0, 3)
    scale = rows_of(scales, 0, 2)
    sums = change_of(enc_pre, totals, scale, widened)
    enc_sums = total(1, sums)

    def put_flow(i, rows, flow):
        flow_out[rows, :] = flow.astype(BF)

    back(enc_pre, totals, scale, enc_sums, enc_taps, put_flow)
    enc_grad[...] = dot_tn(x[...], nine[...])
    put_sums(norm_sums, enc_sums + dec_sums)


def trunk_backward(
    geometry, tasks, batches, small, upstream, enc_pre, enc_totals, dec_pre, dec_totals, scales,
    choose, choose_row, x, spread, enc_taps, dec_taps,
):
    number, height, breadth = geometry
    total, channels = x.shape
    width = channels // tasks
    windows = window_count(height, breadth)
    return exchange_kernel(
        functools.partial(trunk_backward_body, geometry, tasks, batches),
        [
            shape(enc_taps.shape, F32),
            shape(dec_taps.shape, F32),
            shape(x.shape, BF),
            shape((8, width), F32),
        ],
        "svvvvvvvvvvvv",
        (small, upstream, enc_pre, enc_totals, dec_pre, dec_totals, scales, choose, choose_row, x,
         spread, enc_taps, dec_taps),
        [
            pltpu.VMEM((total, 9 * width), BF),
            pltpu.VMEM((total, width), F32),
            pltpu.VMEM((number * windows, channels), BF),
            pltpu.VMEM((tasks - 1, number * windows, width), BF),
            pltpu.VMEM((number * windows, width), F32),
        ]
        + [pltpu.SemaphoreType.DMA((number, tasks))] * 2
        + total_scratch(2, batches),
        3,
        40,
        flops=8 * x.size * enc_taps.shape[1],
    )


def exchange(body, outs, args, scratch, identity, vmem=32):
    size = sum(o.size * o.dtype.itemsize for o in outs) + sum(a.size * a.dtype.itemsize for a in args)
    return pl.pallas_call(
        body,
        out_shape=tuple(outs),
        in_specs=[VMEM_SPEC] * len(args),
        out_specs=tuple(VMEM_SPEC for _ in outs),
        scratch_shapes=list(scratch),
        compiler_params=pltpu.CompilerParams(
            vmem_limit_bytes=vmem * MIB, collective_id=identity, has_side_effects=True
        ),
        cost_estimate=pl.CostEstimate(flops=0, bytes_accessed=size, transcendentals=0),
    )(*args)


def block_of(ref, place, size, dim):
    length = ref.shape[dim] // size
    start = place * length
    if dim == 0:
        return ref.at[pl.ds(pl.multiple_of(start, 8), length), :]
    return ref.at[:, pl.ds(pl.multiple_of(start, 128), length)]


def gather_body(axis, size, dims, *refs):
    count = len(dims)
    sources, targets = refs[:count], refs[count : 2 * count]
    sends, receives, own = refs[2 * count :]
    greet(((axis, size),))
    me = lax.axis_index(axis)
    copies = []
    for k in range(count):
        mine = block_of(targets[k], me, size, dims[k])
        for step in range(1, size):
            peer = lax.rem(me + step, size)
            copy = remote(sources[k], mine, sends.at[k, step], receives.at[k, me], peer, axis)
            copy.start()
            copies.append(copy)
    locals_ = []
    for k in range(count):
        mine = block_of(targets[k], me, size, dims[k])
        copy = pltpu.make_async_copy(sources[k], mine, own.at[k])
        copy.start()
        locals_.append(copy)
    for copy in locals_:
        copy.wait()
    for k in range(count):
        for step in range(1, size):
            peer = lax.rem(me + size - step, size)
            theirs = block_of(targets[k], peer, size, dims[k])
            remote(
                sources[k], theirs, sends.at[k, step], receives.at[k, peer], peer, axis
            ).wait_recv()
    for copy in copies:
        copy.wait_send()


def gather_over(axis, size, arrays, dims, identity):
    outs = []
    for x, dim in zip(arrays, dims):
        full = list(x.shape)
        full[dim] *= size
        outs.append(shape(full, x.dtype))
    count = len(arrays)
    return exchange(
        functools.partial(gather_body, axis, size, tuple(dims)),
        outs,
        arrays,
        [
            pltpu.SemaphoreType.DMA((count, size)),
            pltpu.SemaphoreType.DMA((count, size)),
            pltpu.SemaphoreType.DMA((count,)),
        ],
        identity,
    )


def to_taps_body(index, slots, enc, dec, wide, tap):
    count = slots.shape[0]
    channels = enc.shape[0]
    width = slots.shape[1]
    step = 1024

    def widen(i, carry):
        rows = pl.ds(pl.multiple_of(i * step, step), step)
        wide[rows, :] = slots[rows, :].astype(F32)
        return carry

    lax.fori_loop(0, count // step, widen, 0)
    group = 32
    for p in range(18):

        def fetch(i, carry):
            base = i * group
            for u in range(group):
                tap[pl.ds(base + u, 1), :] = wide[pl.ds(index[p * channels + base + u], 1), :]
            return carry

        lax.fori_loop(0, channels // group, fetch, 0)
        out = enc if p < 9 else dec
        q = p % 9
        out[:, q * width : (q + 1) * width] = tap[...].astype(BF)


def to_taps(index, slots, channels):
    width = slots.shape[1]
    return run(
        to_taps_body,
        [shape((channels, 9 * width), BF)] * 2,
        "sv",
        (index, slots),
        [pltpu.VMEM(slots.shape, F32), pltpu.VMEM((channels, width), F32)],
    )


def to_slots_body(index, enc, dec, slots, wide):
    count = slots.shape[0]
    channels = enc.shape[0]
    width = slots.shape[1]
    step = 1024
    group = 32
    for p in range(18):
        source = enc if p < 9 else dec
        q = p % 9

        def place(i, carry):
            base = pl.multiple_of(i * group, group)
            values = source[pl.ds(base, group), q * width : (q + 1) * width]
            for u in range(group):
                wide[pl.ds(index[p * channels + base + u], 1), :] = values[u : u + 1, :]
            return carry

        lax.fori_loop(0, channels // group, place, 0)

    def narrow(i, carry):
        rows = pl.ds(pl.multiple_of(i * step, step), step)
        slots[rows, :] = wide[rows, :].astype(BF)
        return carry

    lax.fori_loop(0, count // step, narrow, 0)


def to_slots(index, enc, dec):
    width = enc.shape[1] // 9
    dims = (index.shape[0], width)
    return run(
        to_slots_body, [shape(dims, BF)], "svv", (index, enc, dec), [pltpu.VMEM(dims, F32)]
    )[0]


def adam(gradient, moment_one, moment_two):
    new_one = BETA_ONE * moment_one + (1.0 - BETA_ONE) * gradient
    new_two = BETA_TWO * moment_two + (1.0 - BETA_TWO) * gradient * gradient
    direction = (
        new_one / (1.0 - BETA_ONE**STEP) / (jnp.sqrt(new_two / (1.0 - BETA_TWO**STEP)) + ADAM_EPS)
    )
    return new_one, new_two, direction


def soap_body(
    cuts, grad, owners, weight, one, two, basis, weight_new, one_new, two_new, low
):
    count = basis.shape[0]
    total = grad.shape[0]
    for m in range(count):
        low[m] = basis[m].astype(BF)

    def chunk(i, carry):
        rows = pl.ds(pl.multiple_of(i * (total // cuts), 8), total // cuts)
        values = grad[rows, :].astype(F32)
        rotated = None
        for m in range(count):
            part = dot((values * owners[rows, m : m + 1]).astype(BF), low[m])
            rotated = part if rotated is None else rotated + part
        new_one, new_two, direction = adam(rotated, one[rows, :], two[rows, :])
        one_new[rows, :] = new_one
        two_new[rows, :] = new_two
        stepped = None
        for m in range(count):
            part = dot_nt((direction * owners[rows, m : m + 1]).astype(BF), low[m])
            stepped = part if stepped is None else stepped + part
        old = weight[rows, :]
        weight_new[rows, :] = old - LEARN_MATRIX * (stepped + DECAY_MATRIX * old)
        return carry

    lax.fori_loop(0, cuts, chunk, 0)


def soap(grad, owners, weight, one, two, basis):
    total = grad.shape[0]
    cuts = 4 if total % 64 == 0 else 1
    return run(
        functools.partial(soap_body, cuts),
        [shape(weight.shape, F32)] * 3,
        "vvvvvv",
        (grad, owners, weight, one, two, basis),
        [pltpu.VMEM(basis.shape, BF)],
        flops=4 * weight.size * weight.shape[1] * basis.shape[0],
    )


def grams_body(grad, part, owners, grams):
    for m in range(grams.shape[0]):
        held = (grad[...].astype(F32) * owners[:, m : m + 1]).astype(BF)
        grams[m] = dot_tn(held, part[...])


def owner_grams(grad, part, owners):
    dims = (owners.shape[1], grad.shape[1], part.shape[1])
    return run(
        grams_body,
        [shape(dims, F32)],
        "vvv",
        (grad, part, owners),
        flops=2 * grad.size * part.shape[1] * owners.shape[1],
    )[0]


def factor_rows(values, identity, turn):
    width = values.shape[1]
    sub = lax.broadcasted_iota(jnp.int32, (8, width), 0)
    rolled = pltpu.roll(values, turn, 1)
    columns = [jnp.broadcast_to(rolled[:, j : j + 1], (8, width)) for j in range(8)]
    scale = jnp.zeros((8, width), F32)
    for j in range(8):
        root = lax.rsqrt(columns[j][j : j + 1, :])
        scale = jnp.where(sub == j, root, scale)
        lower = jnp.where(sub > j, columns[j] * root, 0.0)
        values = values - lower * (values[j : j + 1, :] * root)
        identity = identity - lower * (identity[j : j + 1, :] * root)
        for i in range(j + 1, 8):
            columns[i] = columns[i] - lower * (columns[i][j : j + 1, :] * root)
    return values * scale, identity * scale


def renew_body(counts, *refs):
    groups = len(counts)
    stats, bases, grams = (refs[k * groups : (k + 1) * groups] for k in range(3))
    stats_new, bases_new = (refs[k * groups : (k + 1) * groups] for k in (3, 4))
    count = sum(counts)
    product = refs[5 * groups]
    tables = refs[5 * groups + 1 : 5 * groups + 1 + count]
    inverses = refs[5 * groups + 1 + count :]
    homes = [(g, m) for g in range(groups) for m in range(counts[g])]
    size = stats[0].shape[1]
    panel = 128
    matrices = range(count)
    row = lax.broadcasted_iota(jnp.int32, (panel, panel), 0)
    col = lax.broadcasted_iota(jnp.int32, (panel, panel), 1)
    unit = jnp.where(row == col, 1.0, 0.0).astype(F32)
    for n, (g, m) in enumerate(homes):
        new = STAT_DECAY * stats[g][m] + (1.0 - STAT_DECAY) * grams[g][m].astype(F32)
        stats_new[g][m] = new
        product[n] = dot3(dot, new, bases[g][m])
    for k in range(size // panel):
        here = slice(k * panel, (k + 1) * panel)
        for n in matrices:
            tables[n][:, :panel] = dot3(dot_tn, product[n, :, here], product[n, :, here])
            tables[n][:, panel:] = unit

        def group(q, carry):
            rows = pl.ds(pl.multiple_of(q * 8, 8), 8)
            turn = lax.rem(panel - q * 8, panel)
            done = [
                factor_rows(tables[n][rows, :panel], tables[n][rows, panel:], turn)
                for n in matrices
            ]
            for n in matrices:
                upper, inverse = done[n]
                inverses[n][rows, :] = inverse
                both = jnp.concatenate([upper, inverse], axis=1)
                tables[n][...] = tables[n][...] - dot3(dot_tn, upper, both)
            return carry

        lax.fori_loop(0, panel // 8, group, 0)
        for n, (g, m) in enumerate(homes):
            turned = dot3(dot_nt, product[n, :, here], inverses[n][...])
            bases_new[g][m, :, here] = turned
            if k < size // panel - 1:
                rest = slice((k + 1) * panel, size)
                product[n, :, rest] = product[n, :, rest] - dot3(
                    dot, turned, dot3(dot_tn, turned, product[n, :, rest])
                )


def renew_bases(stats, bases, grams):
    counts = tuple(s.shape[0] for s in stats)
    count = sum(counts)
    size = stats[0].shape[1]
    return run(
        functools.partial(renew_body, counts),
        [shape(s.shape, F32) for s in stats] * 2,
        "v" * (3 * len(stats)),
        (*stats, *bases, *grams),
        [pltpu.VMEM((count, size, size), F32)]
        + [pltpu.VMEM((128, 256), F32)] * count
        + [pltpu.VMEM((128, 128), F32)] * count,
        flops=60 * MIB * MIB // 1024,
    )


def local(
    tasks,
    batches,
    images,
    image_small,
    pool_index,
    row_slot,
    trunk_weight,
    trunk_mean_grad,
    trunk_mean_square,
    trunk_statistic,
    trunk_basis,
    head_weight,
    head_mean_grad,
    head_mean_square,
    head_statistic,
    head_basis,
    trunk_gain,
    trunk_offset,
    trunk_norm_mean_grad,
    trunk_norm_mean_square,
    head_gain,
    head_offset,
    head_norm_mean_grad,
    head_norm_mean_square,
    cotangent,
):
    number, height, breadth, channels = images.shape
    pixels = height * breadth
    tap_rows = 9 * channels
    shown = tasks * number
    geometry = (shown, height, breadth)
    task = lax.axis_index("task")
    batch = lax.axis_index("batch")
    width = channels // tasks

    def quarter(values):
        return lax.dynamic_slice_in_dim(values, task * width, width, values.ndim - 1)

    def inside(flags):
        row_limit = jnp.where(flags > 0, height // 2, height)[:, None, None]
        col_limit = jnp.where(flags > 0, breadth // 2, breadth)[:, None, None]
        return (jnp.arange(height, dtype=jnp.int32)[None, :, None] < row_limit) & (
            jnp.arange(breadth, dtype=jnp.int32)[None, None, :] < col_limit
        )

    slots = lax.all_gather(quarter(trunk_weight).astype(BF), "batch", axis=0, tiled=True)
    head_rows = lax.all_gather(head_weight.astype(BF), "batch", axis=1, tiled=True)[0]
    kinds = jnp.concatenate([image_small, pool_index.reshape(-1)])
    kinds = lax.all_gather(kinds, "task", axis=0, tiled=True).reshape(tasks, -1)
    small = kinds[:, :number].reshape(-1)
    cells = kinds[:, number:].reshape(shown, height // 2, 1, breadth // 2, 1)
    cell = 2 * jnp.arange(2, dtype=jnp.int32)[:, None, None] + jnp.arange(2, dtype=jnp.int32)
    choose = (cells == cell).reshape(shown, height, breadth) & inside(small)
    choose = choose.astype(F32)
    choose_row = choose.reshape(shown, 1, pixels)
    choose = choose.reshape(shown * pixels, 1)
    masked = (images * inside(image_small)[..., None].astype(BF)).reshape(number * pixels, channels)
    x = gather_over("task", tasks, (masked,), (0,), 4)[0]
    enc_taps, dec_taps = to_taps(row_slot, slots, channels)

    scales = quarter(jnp.stack([trunk_gain, trunk_offset], axis=1)).reshape(4, width)
    enc_pre, enc_totals, spread, dec_pre, dec_totals, features = trunk_forward(
        geometry, tasks, batches, small, x, enc_taps, dec_taps, scales, choose
    )
    head_scales = jnp.stack([head_gain[0], head_offset[0]], axis=1).reshape(6, channels)
    pooled, head_grads, upstream, head_sums = head(
        geometry, tasks, batches, small, features, head_rows,
        cotangent.reshape(shown, pixels // 4, channels), head_scales, enc_totals,
    )
    task_features = pooled.reshape(cotangent.shape)
    head_owned = lax.psum_scatter(head_grads, "batch", scatter_dimension=0, tiled=True)
    enc_grad, dec_grad, flow, trunk_sums = trunk_backward(
        geometry, tasks, batches, small, upstream, enc_pre, enc_totals, dec_pre, dec_totals,
        scales, choose, choose_row, x, spread, enc_taps, dec_taps,
    )
    trunk_part = lax.psum_scatter(
        to_slots(row_slot, enc_grad, dec_grad), "batch", scatter_dimension=0, tiled=True
    )
    input_grad = lax.psum_scatter(flow, "task", scatter_dimension=0, tiled=True)
    input_grad = input_grad.astype(F32).reshape(images.shape)

    head_local = head_weight.shape[1]
    head_ids = batch * head_local + jnp.arange(head_local, dtype=jnp.int32)
    head_owner = jnp.minimum(head_ids // channels, 2)
    head_onehot = (head_owner[:, None] == jnp.arange(3, dtype=jnp.int32)).astype(F32)
    head_grams = lax.psum(owner_grams(head_owned, head_owned, head_onehot).astype(BF), "batch")
    head_weight_new, head_one_new, head_two_new = soap(
        head_owned, head_onehot, head_weight[0], head_mean_grad[0], head_mean_square[0],
        head_basis[0],
    )

    trunk_owned, norm_sums = gather_over("task", tasks, (trunk_part, trunk_sums), (1, 1), 5)
    local_rows = trunk_weight.shape[0]
    slot_ids = batch * local_rows + jnp.arange(local_rows, dtype=jnp.int32)
    trunk_owner = jnp.take(jnp.argsort(row_slot), slot_ids) // tap_rows
    trunk_onehot = (trunk_owner[:, None] == jnp.arange(2, dtype=jnp.int32)).astype(F32)
    trunk_grams = lax.psum(owner_grams(trunk_owned, trunk_part, trunk_onehot), "batch").astype(BF)
    trunk_grams = gather_over(
        "task", tasks, (trunk_grams.reshape(2 * channels, width),), (1,), 6
    )[0].reshape(2, channels, channels)
    trunk_weight_new, trunk_one_new, trunk_two_new = soap(
        trunk_owned, trunk_onehot, trunk_weight, trunk_mean_grad, trunk_mean_square, trunk_basis
    )
    trunk_stat_new, head_stat_new, trunk_basis_new, head_basis_new = renew_bases(
        (trunk_statistic, head_statistic[0]),
        (trunk_basis, head_basis[0]),
        (trunk_grams, head_grams),
    )

    trunk_norm = jnp.stack([trunk_gain, trunk_offset], axis=1)
    trunk_norm_grad = norm_sums[:4].reshape(2, 2, channels)[:, ::-1]
    trunk_norm_one, trunk_norm_two, trunk_direction = adam(
        trunk_norm_grad, trunk_norm_mean_grad, trunk_norm_mean_square
    )
    head_norm = jnp.stack([head_gain, head_offset], axis=2)
    head_norm_grad = head_sums[:6].reshape(1, 3, 2, channels)[:, :, ::-1]
    head_norm_one, head_norm_two, head_direction = adam(
        head_norm_grad, head_norm_mean_grad, head_norm_mean_square
    )
    return (
        task_features,
        input_grad,
        trunk_weight_new,
        trunk_one_new,
        trunk_two_new,
        trunk_stat_new,
        trunk_basis_new,
        head_weight_new[None],
        head_one_new[None],
        head_two_new[None],
        head_stat_new[None],
        head_basis_new[None],
        trunk_norm - LEARN_NORM * trunk_direction,
        trunk_norm_one,
        trunk_norm_two,
        head_norm - LEARN_NORM * head_direction,
        head_norm_one,
        head_norm_two,
    )


def solution(mesh):
    placed = (
        P(("task", "batch"), None, None, None),
        P(("task", "batch")),
        P(("task", "batch"), None, None),
        P(),
        P("batch", None),
        P("batch", None),
        P("batch", None),
        P(),
        P(),
        P("task", "batch", None),
        P("task", "batch", None),
        P("task", "batch", None),
        P("task", None, None, None),
        P("task", None, None, None),
        P(),
        P(),
        P(),
        P(),
        P("task", None, None),
        P("task", None, None),
        P("task", None, None, None),
        P("task", None, None, None),
        P("task", None, "batch", None, None, None),
    )
    return jax.shard_map(
        functools.partial(local, mesh.shape["task"], mesh.shape["batch"]),
        mesh=mesh,
        in_specs=placed,
        out_specs=(
            P("task", None, "batch", None, None, None),
            P(("task", "batch"), None, None, None),
            P("batch", None),
            P("batch", None),
            P("batch", None),
            P(),
            P(),
            P("task", "batch", None),
            P("task", "batch", None),
            P("task", "batch", None),
            P("task", None, None, None),
            P("task", None, None, None),
            P(),
            P(),
            P(),
            P("task", None, None, None),
            P("task", None, None, None),
            P("task", None, None, None),
        ),
        check_vma=False,
    )
```

```python
import functools

import jax
import jax.numpy as jnp
from jax import lax
from jax.experimental import pallas as pl
from jax.experimental.pallas import tpu as pltpu
from jax.sharding import PartitionSpec as P

STEP = 10


EPS = 1e-05
ADAM_EPS = 1e-08
BETA_ONE = 0.95
BETA_TWO = 0.95
STAT_DECAY = 0.95
LEARN_MATRIX = 0.02
LEARN_NORM = 0.5
DECAY_MATRIX = 0.01
BF = jnp.bfloat16
F32 = jnp.float32
MESH = pl.DeviceIdType.MESH
MIB = 1 << 20

VMEM_SPEC = pl.BlockSpec(memory_space=pltpu.VMEM)
SMEM_SPEC = pl.BlockSpec(memory_space=pltpu.SMEM)


def run(body, outs, specs, args, scratch=(), vmem=40, flops=0):
    size = sum(o.size * o.dtype.itemsize for o in outs) + sum(a.size * a.dtype.itemsize for a in args)
    return pl.pallas_call(
        body,
        out_shape=tuple(outs),
        in_specs=[SMEM_SPEC if s == "s" else VMEM_SPEC for s in specs],
        out_specs=tuple(VMEM_SPEC for _ in outs),
        scratch_shapes=list(scratch),
        compiler_params=pltpu.CompilerParams(vmem_limit_bytes=vmem * MIB),
        cost_estimate=pl.CostEstimate(flops=flops, bytes_accessed=size, transcendentals=0),
    )(*args)


def shape(dims, kind):
    return jax.ShapeDtypeStruct(tuple(dims), kind)


def dot(a, b):
    return jnp.dot(a, b, preferred_element_type=F32)


def dot_nt(a, b):
    return lax.dot_general(a, b, (((1,), (1,)), ((), ())), preferred_element_type=F32)


def dot_tn(a, b):
    return lax.dot_general(a, b, (((0,), (0,)), ((), ())), preferred_element_type=F32)


def split(a):
    high = a.astype(BF)
    return high, (a - high.astype(F32)).astype(BF)


def dot3(kind, a, b):
    a_high, a_low = split(a)
    b_high, b_low = split(b)
    return kind(a_high, b_high) + (kind(a_high, b_low) + kind(a_low, b_high))


def places(height, breadth):
    index = lax.broadcasted_iota(jnp.int32, (height * breadth, 1), 0)
    row = lax.div(index, breadth)
    return row, index - row * breadth


def valid_rows(small, height, breadth):
    row, col = places(height, breadth)
    row_limit = jnp.where(small > 0, height // 2, height)
    col_limit = jnp.where(small > 0, breadth // 2, breadth)
    return jnp.where((row < row_limit) & (col < col_limit), 1.0, 0.0).astype(F32)


def move(values, rows):
    gap = jnp.zeros((abs(rows),) + values.shape[1:], values.dtype)
    if rows > 0:
        return jnp.concatenate([gap, values[:-rows]], axis=0)
    return jnp.concatenate([values[-rows:], gap], axis=0)


def from_left(values, col):
    return jnp.where(col > 0, pltpu.roll(values, 1, 0), 0.0)


def from_right(values, col, breadth):
    return jnp.where(col < breadth - 1, pltpu.roll(values, values.shape[0] - 1, 0), 0.0)


def gather_taps(tap, breadth, col):
    lines = [move(tap(b), breadth) + tap(3 + b) + move(tap(6 + b), -breadth) for b in range(3)]
    return lines[1] + from_left(lines[0], col) + from_right(lines[2], col, breadth)


def spread_taps(values, breadth, col):
    lines = [from_right(values, col, breadth), values, from_left(values, col)]
    return [
        move(lines[b], breadth * (a - 1)) if a != 1 else lines[b] for a in range(3) for b in range(3)
    ]


def window_sum(values, row, col, breadth):
    count = values.shape[0]
    pair = values + jnp.where(
        col % 2 == 0, pltpu.roll(values, count - 1, 0), pltpu.roll(values, 1, 0)
    )
    return pair + jnp.where(row % 2 == 0, move(pair, -breadth), move(pair, breadth))


def silu_back(scaled):
    sig = jax.nn.sigmoid(scaled)
    return sig * (1.0 + scaled * (1.0 - sig))


def col_sum(values):
    return jnp.sum(values, axis=0, keepdims=True)


def put_sums(ref, rows):
    width = ref.shape[1]
    rows = list(rows) + [jnp.zeros((1, width), F32)] * (8 - len(rows))
    ref[...] = jnp.concatenate(rows, axis=0)


def each_image(geometry, body, start):
    number, height, breadth = geometry
    pixels = height * breadth

    def step(image, carry):
        return body(image, pl.ds(pl.multiple_of(image * pixels, 16), pixels), carry)

    return lax.fori_loop(0, number, step, start)


def zero_rows(count, width):
    return (jnp.zeros((1, width), F32),) * count


def greet(axes):
    barrier = pltpu.get_barrier_semaphore()
    for axis, size in axes:
        me = lax.axis_index(axis)
        for step in range(1, size):
            pl.semaphore_signal(
                barrier, inc=1, device_id={axis: lax.rem(me + step, size)}, device_id_type=MESH
            )
    pl.semaphore_wait(barrier, sum(size - 1 for _, size in axes))


def remote(source, target, sends, receives, peer, axis):
    return pltpu.make_async_remote_copy(
        src_ref=source,
        dst_ref=target,
        send_sem=sends,
        recv_sem=receives,
        device_id={axis: peer},
        device_id_type=MESH,
    )


def pack(rows):
    parts = [row[:, i : i + 128] for row in rows for i in range(0, row.shape[1], 128)]
    parts += [jnp.zeros((1, 128), F32)] * (8 - len(parts))
    return jnp.concatenate(parts, axis=0)


def unpack(tile, count, width):
    per = width // 128
    return [
        jnp.concatenate([tile[k * per + i : k * per + i + 1, :] for i in range(per)], axis=1)
        for k in range(count)
    ]


def total_rows(k, axis, size, rows, mine, slots, sends, receives):
    me = lax.axis_index(axis)
    tile = pack(rows)
    mine[k] = tile
    slots[k, me] = tile
    for step in range(1, size):
        peer = lax.rem(me + step, size)
        remote(mine.at[k], slots.at[k, me], sends.at[k, step], receives.at[k, me], peer, axis).start()
    for step in range(1, size):
        peer = lax.rem(me + size - step, size)
        remote(
            mine.at[k], slots.at[k, peer], sends.at[k, step], receives.at[k, peer], peer, axis
        ).wait_recv()
    total = slots[k, 0]
    for peer in range(1, size):
        total = total + slots[k, peer]
    for step in range(1, size):
        peer = lax.rem(me + step, size)
        remote(
            mine.at[k], slots.at[k, me], sends.at[k, step], receives.at[k, me], peer, axis
        ).wait_send()
    return unpack(total, len(rows), rows[0].shape[1])


def total_scratch(count, size):
    return [
        pltpu.VMEM((count, 8, 128), F32),
        pltpu.VMEM((count, size, 8, 128), F32),
        pltpu.SemaphoreType.DMA((count, size)),
        pltpu.SemaphoreType.DMA((count, size)),
    ]


def columns_of(place, width):
    return pl.ds(pl.multiple_of(place * width, 128), width)


def exchange_kernel(body, outs, specs, args, scratch, identity, vmem, flops=0):
    size = sum(o.size * o.dtype.itemsize for o in outs) + sum(a.size * a.dtype.itemsize for a in args)
    return pl.pallas_call(
        body,
        out_shape=tuple(outs),
        in_specs=[SMEM_SPEC if s == "s" else VMEM_SPEC for s in specs],
        out_specs=tuple(VMEM_SPEC for _ in outs),
        scratch_shapes=list(scratch),
        compiler_params=pltpu.CompilerParams(
            vmem_limit_bytes=vmem * MIB, collective_id=identity, has_side_effects=True
        ),
        cost_estimate=pl.CostEstimate(flops=flops, bytes_accessed=size, transcendentals=0),
    )(*args)


def norm_with(values, totals, scale):
    total, squares, count = totals
    center = total / count
    inverse = lax.rsqrt(squares / count - center * center + EPS)
    normal = (values - center) * inverse
    return normal, inverse, normal * scale[0] + scale[1]


def norm_back_with(upstream, normal, inverse, count, sums, scale, valid):
    return scale[0] * inverse * (upstream - sums[0] / count - normal * (sums[1] / count)) * valid


def silu(values):
    return values * jax.nn.sigmoid(values)


def window_count(height, breadth):
    return -(-(height * breadth // 4) // 16) * 16


def pool_choice(height, breadth, windows, flipped):
    pixels = height * breadth
    dims = (windows, pixels) if flipped else (pixels, windows)
    pixel = lax.broadcasted_iota(jnp.int32, dims, 1 if flipped else 0)
    window = lax.broadcasted_iota(jnp.int32, dims, 0 if flipped else 1)
    row = lax.div(pixel, breadth)
    col = pixel - row * breadth
    home = lax.div(row, 2) * (breadth // 2) + lax.div(col, 2)
    return jnp.where(home == window, 1.0, 0.0).astype(F32)


def rows_of(ref, first, count):
    return [ref[first + k : first + k + 1, :] for k in range(count)]


def window_rows(i, windows):
    return pl.ds(pl.multiple_of(i * windows, 16), windows)


def trunk_forward_body(
    geometry, tasks, batches,
    small, x, enc_taps, dec_taps, scales, choose,
    enc_pre, enc_totals, spread, dec_pre, dec_totals, features,
    work, pooled, pooled_all, part, pool_sends, pool_receives, sends, receives,
    mine, slots, total_sends, total_receives,
):
    number, height, breadth = geometry
    width = enc_pre.shape[1]
    windows = window_count(height, breadth)
    task = lax.axis_index("task")
    _, col = places(height, breadth)
    widen = pool_choice(height, breadth, windows, False).astype(BF)
    narrow = pool_choice(height, breadth, windows, True).astype(BF)

    def conv(x, taps, pre):
        def image(i, rows, carry):
            valid = valid_rows(small[i], height, breadth)
            work[...] = dot(x[rows, :], taps[...])
            out = gather_taps(lambda p: work[:, p * width : (p + 1) * width], breadth, col)
            pre[rows, :] = out
            kept = out * valid
            return (
                carry[0] + col_sum(kept),
                carry[1] + col_sum(kept * out),
                carry[2] + jnp.broadcast_to(col_sum(valid), (1, width)),
            )

        return each_image(geometry, image, zero_rows(3, width))

    def total(k, rows):
        return total_rows(
            k, "batch", batches, list(rows), mine, slots, total_sends, total_receives
        )

    sums = conv(x, enc_taps, enc_pre)
    greet((("task", tasks), ("batch", batches)))
    totals = total(0, sums)
    put_sums(enc_totals, totals)
    scale = rows_of(scales, 0, 2)

    def peer_of(step, incoming):
        return lax.rem(task + (tasks - step if incoming else step), tasks)

    def pool_copy(i, step, incoming=False):
        rows = window_rows(i, windows)
        peer = peer_of(step, incoming)
        target = pooled_all.at[rows, columns_of(peer if incoming else task, width)]
        return remote(
            pooled.at[rows, :], target, pool_sends.at[i, step], pool_receives.at[i, step], peer, "task"
        )

    def pool(i, rows, carry):
        valid = valid_rows(small[i], height, breadth)
        _, _, scaled = norm_with(enc_pre[rows, :], totals, scale)
        high, low = split(silu(scaled) * valid)
        mean = ((dot(narrow, high) + dot(narrow, low)) * 0.25).astype(BF)
        here = window_rows(i, windows)
        pooled[here, :] = mean
        pooled_all[here, columns_of(task, width)] = mean
        for step in range(1, tasks):
            pool_copy(i, step).start()
        return carry

    each_image(geometry, pool, 0)

    def unpool(i, rows, carry):
        for step in range(1, tasks):
            pool_copy(i, step, True).wait_recv()
        wide = dot(widen, pooled_all[window_rows(i, windows), :])
        spread[rows, :] = (wide * choose[rows, :]).astype(BF)
        return carry

    each_image(geometry, unpool, 0)
    sums = conv(spread, dec_taps, dec_pre)
    totals = total(1, sums)
    put_sums(dec_totals, totals)
    scale = rows_of(scales, 2, 2)

    def feature_copy(i, rows, step, incoming=False):
        peer = peer_of(step, incoming)
        target = features.at[rows, columns_of(peer if incoming else task, width)]
        return remote(
            part.at[rows, :], target, sends.at[i, step], receives.at[i, step], peer, "task"
        )

    def finish(i, rows, carry):
        valid = valid_rows(small[i], height, breadth)
        _, _, scaled = norm_with(dec_pre[rows, :], totals, scale)
        low = (silu(scaled) * valid).astype(BF)
        part[rows, :] = low
        features[rows, columns_of(task, width)] = low
        for step in range(1, tasks):
            feature_copy(i, rows, step).start()
        return carry

    each_image(geometry, finish, 0)

    def settle(i, rows, carry):
        for step in range(1, tasks):
            feature_copy(i, rows, step, True).wait_recv()
            feature_copy(i, rows, step).wait_send()
            pool_copy(i, step).wait_send()
        return carry

    each_image(geometry, settle, 0)


def trunk_forward(geometry, tasks, batches, small, x, enc_taps, dec_taps, scales, choose):
    number, height, breadth = geometry
    pixels = height * breadth
    channels = x.shape[1]
    width = channels // tasks
    windows = window_count(height, breadth)
    return exchange_kernel(
        functools.partial(trunk_forward_body, geometry, tasks, batches),
        [
            shape((x.shape[0], width), F32),
            shape((8, width), F32),
            shape(x.shape, BF),
            shape((x.shape[0], width), F32),
            shape((8, width), F32),
            shape(x.shape, BF),
        ],
        "svvvvv",
        (small, x, enc_taps, dec_taps, scales, choose),
        [
            pltpu.VMEM((pixels, 9 * width), F32),
            pltpu.VMEM((number * windows, width), BF),
            pltpu.VMEM((number * windows, channels), BF),
            pltpu.VMEM((x.shape[0], width), BF),
        ]
        + [pltpu.SemaphoreType.DMA((number, tasks))] * 4
        + total_scratch(2, batches),
        1,
        32,
        flops=4 * x.size * enc_taps.shape[1],
    )


def head_body(
    geometry, tasks, batches,
    small, features, rows_in, cotangent, scales, counts,
    task_out, grads, upstream, norm_sums,
    pre_one, pre_two, pre_three, hidden, gated, nine, work, lower, out, arrived, sends, receives,
    mine, slots, total_sends, total_receives,
):
    number, height, breadth = geometry
    channels = features.shape[1]
    width = channels // tasks
    windows = task_out.shape[1]
    task = lax.axis_index("task")
    half = work.shape[2]
    _, col = places(height, breadth)
    widen = pool_choice(height, breadth, windows, False).astype(BF)
    narrow = pool_choice(height, breadth, windows, True).astype(BF)
    count = jnp.broadcast_to(counts[2:3, 0:1], (1, channels))
    first = rows_in.at[pl.ds(0, channels), :]
    second = rows_in.at[pl.ds(channels, channels), :]

    def kernel_rows(p):
        return pl.ds((2 + p) * channels, channels)

    def total(k, rows):
        return total_rows(
            k, "batch", batches, list(rows), mine, slots, total_sends, total_receives
        )

    def put_stats(pre, rows, value, valid, carry):
        pre[rows, :] = value
        kept = value * valid
        return carry[0] + col_sum(kept), carry[1] + col_sum(kept * value)

    nothing = zero_rows(2, channels)
    scale_one, scale_two, scale_three = (rows_of(scales, 2 * k, 2) for k in range(3))

    def first_step(i, rows, carry):
        valid = valid_rows(small[i], height, breadth)
        return put_stats(pre_one, rows, dot(features[rows, :], first[...]), valid, carry)

    sums = each_image(geometry, first_step, nothing)
    greet((("task", tasks), ("batch", batches)))
    totals_one = total(0, sums) + [count]

    def second_step(i, rows, carry):
        valid = valid_rows(small[i], height, breadth)
        _, _, scaled = norm_with(pre_one[rows, :], totals_one, scale_one)
        low = (silu(scaled) * valid).astype(BF)
        hidden[rows, :] = low
        return put_stats(pre_two, rows, dot(low, second[...]), valid, carry)

    sums = each_image(geometry, second_step, nothing)
    totals_two = total(1, sums) + [count]

    def third_step(i, rows, carry):
        valid = valid_rows(small[i], height, breadth)
        _, _, scaled = norm_with(pre_two[rows, :], totals_two, scale_two)
        low = (jax.nn.sigmoid(scaled) * features[rows, :].astype(F32)).astype(BF)
        gated[rows, :] = low
        parts = []
        for j in range(channels // half):
            cut = slice(j * half, (j + 1) * half)
            for p in range(9):
                work[p] = dot(low, rows_in[kernel_rows(p), cut])
            parts.append(gather_taps(lambda p: work[p], breadth, col))
        return put_stats(pre_three, rows, jnp.concatenate(parts, axis=1), valid, carry)

    sums = each_image(geometry, third_step, nothing)
    totals_three = total(2, sums) + [count]

    def out_step(i, rows, carry):
        valid = valid_rows(small[i], height, breadth)
        normal, _, scaled = norm_with(pre_three[rows, :], totals_three, scale_three)
        high, low = split(silu(scaled) * valid)
        mean = (dot(narrow, high) + dot(narrow, low)) * 0.25
        task_out[i] = mean.astype(BF)
        dy = silu_back(scaled) * dot(widen, cotangent[i]) * 0.25 * valid
        lower[rows, :] = dy
        return carry[0] + col_sum(dy), carry[1] + col_sum(dy * normal)

    sums = each_image(geometry, out_step, nothing)
    sums_three = total(3, sums)

    def third_back(i, rows, carry):
        valid = valid_rows(small[i], height, breadth)
        normal, inverse, _ = norm_with(pre_three[rows, :], totals_three, scale_three)
        dz = norm_back_with(lower[rows, :], normal, inverse, count, sums_three, scale_three, valid)
        for p, moved in enumerate(spread_taps(dz, breadth, col)):
            nine[p, rows, :] = moved.astype(BF)
        flow = None
        for p in range(9):
            piece = dot_nt(nine[p, rows, :], rows_in[kernel_rows(p), :])
            flow = piece if flow is None else flow + piece
        lower[rows, :] = flow
        normal, _, scaled = norm_with(pre_two[rows, :], totals_two, scale_two)
        gate = jax.nn.sigmoid(scaled)
        dy = flow * features[rows, :].astype(F32) * gate * (1.0 - gate) * valid
        pre_three[rows, :] = dy
        return carry[0] + col_sum(dy), carry[1] + col_sum(dy * normal)

    sums = each_image(geometry, third_back, nothing)
    sums_two = total(4, sums)

    def second_back(i, rows, carry):
        valid = valid_rows(small[i], height, breadth)
        normal, inverse, scaled = norm_with(pre_two[rows, :], totals_two, scale_two)
        dz = norm_back_with(
            pre_three[rows, :], normal, inverse, count, sums_two, scale_two, valid
        ).astype(BF)
        out[rows, :] = dz
        lower[rows, :] = lower[rows, :] * jax.nn.sigmoid(scaled)
        normal, _, scaled = norm_with(pre_one[rows, :], totals_one, scale_one)
        dy = silu_back(scaled) * dot_nt(dz, second[...]) * valid
        pre_three[rows, :] = dy
        return carry[0] + col_sum(dy), carry[1] + col_sum(dy * normal)

    sums = each_image(geometry, second_back, nothing)
    sums_one = total(5, sums)
    grads[pl.ds(channels, channels), :] = dot_tn(hidden[...], out[...]).astype(BF)

    def flow_copy(i, rows, step, incoming=False):
        peer = lax.rem(task + (tasks - step if incoming else step), tasks)
        return remote(
            out.at[rows, columns_of(peer, width)], arrived.at[step - 1, rows, :],
            sends.at[i, step], receives.at[i, step], peer, "task",
        )

    def first_back(i, rows, carry):
        valid = valid_rows(small[i], height, breadth)
        normal, inverse, _ = norm_with(pre_one[rows, :], totals_one, scale_one)
        dz = norm_back_with(
            pre_three[rows, :], normal, inverse, count, sums_one, scale_one, valid
        ).astype(BF)
        hidden[rows, :] = dz
        flow = (lower[rows, :] + dot_nt(dz, first[...])) * valid
        out[rows, :] = flow.astype(BF)
        for step in range(1, tasks):
            flow_copy(i, rows, step).start()
        return carry

    each_image(geometry, first_back, 0)
    grads[pl.ds(0, channels), :] = dot_tn(features[...], hidden[...]).astype(BF)

    def tap(p, carry):
        rows = pl.ds(pl.multiple_of((2 + p) * channels, channels), channels)
        grads[rows, :] = dot_tn(gated[...], nine[p]).astype(BF)
        return carry

    lax.fori_loop(0, 9, tap, 0)
    put_sums(norm_sums, sums_one + sums_two + sums_three)

    def settle(i, rows, carry):
        for step in range(1, tasks):
            flow_copy(i, rows, step, True).wait_recv()
        flow = out[rows, columns_of(task, width)].astype(F32)
        for step in range(1, tasks):
            flow = flow + arrived[step - 1, rows, :].astype(F32)
        upstream[rows, :] = flow
        for step in range(1, tasks):
            flow_copy(i, rows, step).wait_send()
        return carry

    each_image(geometry, settle, 0)


def head(geometry, tasks, batches, small, features, rows_in, cotangent, scales, counts):
    number, height, breadth = geometry
    pixels = height * breadth
    total, channels = features.shape
    width = channels // tasks
    return exchange_kernel(
        functools.partial(head_body, geometry, tasks, batches),
        [
            shape((number, pixels // 4, channels), BF),
            shape(rows_in.shape, BF),
            shape((total, width), F32),
            shape((8, channels), F32),
        ],
        "svvvvv",
        (small, features, rows_in, cotangent, scales, counts),
        [
            pltpu.VMEM(features.shape, F32),
            pltpu.VMEM(features.shape, F32),
            pltpu.VMEM(features.shape, F32),
            pltpu.VMEM(features.shape, BF),
            pltpu.VMEM(features.shape, BF),
            pltpu.VMEM((9,) + features.shape, BF),
            pltpu.VMEM((9, pixels, min(channels, 256)), F32),
            pltpu.VMEM(features.shape, F32),
            pltpu.VMEM(features.shape, BF),
            pltpu.VMEM((tasks - 1, total, width), BF),
        ]
        + [pltpu.SemaphoreType.DMA((number, tasks))] * 2
        + total_scratch(6, batches),
        2,
        60,
        flops=6 * total * channels * rows_in.shape[0],
    )


def trunk_backward_body(
    geometry, tasks, batches,
    small, upstream, enc_pre, enc_totals, dec_pre, dec_totals, scales, choose, choose_row,
    x, spread, enc_taps, dec_taps,
    enc_grad, dec_grad, flow_out, norm_sums,
    nine, change, packed, arrived, pooled, sends, receives,
    mine, slots, total_sends, total_receives,
):
    number, height, breadth = geometry
    channels = x.shape[1]
    width = enc_pre.shape[1]
    windows = window_count(height, breadth)
    task = lax.axis_index("task")
    _, col = places(height, breadth)
    widen = pool_choice(height, breadth, windows, False).astype(BF)
    narrow = pool_choice(height, breadth, windows, True)
    nothing = zero_rows(2, width)

    def total(k, rows):
        return total_rows(
            k, "batch", batches, list(rows), mine, slots, total_sends, total_receives
        )

    def change_of(pre, totals, scale, flow):
        def image(i, rows, carry):
            valid = valid_rows(small[i], height, breadth)
            normal, _, scaled = norm_with(pre[rows, :], totals, scale)
            dy = silu_back(scaled) * flow(i, rows) * valid
            change[rows, :] = dy
            return carry[0] + col_sum(dy), carry[1] + col_sum(dy * normal)

        return each_image(geometry, image, nothing)

    def back(pre, totals, scale, sums, taps, put):
        def image(i, rows, carry):
            valid = valid_rows(small[i], height, breadth)
            normal, inverse, _ = norm_with(pre[rows, :], totals, scale)
            dz = norm_back_with(change[rows, :], normal, inverse, totals[2], sums, scale, valid)
            for p, moved in enumerate(spread_taps(dz, breadth, col)):
                nine[rows, p * width : (p + 1) * width] = moved.astype(BF)
            put(i, rows, dot_nt(nine[rows, :], taps[...]) * valid)
            return carry

        each_image(geometry, image, 0)

    totals = rows_of(dec_totals, 0, 3)
    scale = rows_of(scales, 2, 2)
    sums = change_of(dec_pre, totals, scale, lambda i, rows: upstream[rows, :])
    greet((("task", tasks), ("batch", batches)))
    dec_sums = total(0, sums)

    def copy_of(i, step, incoming=False):
        rows = window_rows(i, windows)
        peer = lax.rem(task + (tasks - step if incoming else step), tasks)
        return remote(
            packed.at[rows, columns_of(peer, width)], arrived.at[step - 1, rows, :],
            sends.at[i, step], receives.at[i, step], peer, "task",
        )

    def put_packed(i, rows, flow):
        chosen = (narrow * choose_row[i]).astype(BF)
        packed[window_rows(i, windows), :] = dot(chosen, flow.astype(BF)).astype(BF)
        for step in range(1, tasks):
            copy_of(i, step).start()

    back(dec_pre, totals, scale, dec_sums, dec_taps, put_packed)
    dec_grad[...] = dot_tn(spread[...], nine[...])

    def collect(i, carry):
        for step in range(1, tasks):
            copy_of(i, step, True).wait_recv()
        rows = window_rows(i, windows)
        flow = packed[rows, columns_of(task, width)].astype(F32)
        for step in range(1, tasks):
            flow = flow + arrived[step - 1, rows, :].astype(F32)
        pooled[rows, :] = flow
        for step in range(1, tasks):
            copy_of(i, step).wait_send()
        return carry

    lax.fori_loop(0, number, collect, 0)

    def widened(i, rows):
        high, low = split(pooled[window_rows(i, windows), :])
        return (dot(widen, high) + dot(widen, low)) * 0.25

    totals = rows_of(enc_totals, 0, 3)
    scale = rows_of(scales, 0, 2)
    sums = change_of(enc_pre, totals, scale, widened)
    enc_sums = total(1, sums)

    def put_flow(i, rows, flow):
        flow_out[rows, :] = flow.astype(BF)

    back(enc_pre, totals, scale, enc_sums, enc_taps, put_flow)
    enc_grad[...] = dot_tn(x[...], nine[...])
    put_sums(norm_sums, enc_sums + dec_sums)


def trunk_backward(
    geometry, tasks, batches, small, upstream, enc_pre, enc_totals, dec_pre, dec_totals, scales,
    choose, choose_row, x, spread, enc_taps, dec_taps,
):
    number, height, breadth = geometry
    total, channels = x.shape
    width = channels // tasks
    windows = window_count(height, breadth)
    return exchange_kernel(
        functools.partial(trunk_backward_body, geometry, tasks, batches),
        [
            shape(enc_taps.shape, F32),
            shape(dec_taps.shape, F32),
            shape(x.shape, BF),
            shape((8, width), F32),
        ],
        "svvvvvvvvvvvv",
        (small, upstream, enc_pre, enc_totals, dec_pre, dec_totals, scales, choose, choose_row, x,
         spread, enc_taps, dec_taps),
        [
            pltpu.VMEM((total, 9 * width), BF),
            pltpu.VMEM((total, width), F32),
            pltpu.VMEM((number * windows, channels), BF),
            pltpu.VMEM((tasks - 1, number * windows, width), BF),
            pltpu.VMEM((number * windows, width), F32),
        ]
        + [pltpu.SemaphoreType.DMA((number, tasks))] * 2
        + total_scratch(2, batches),
        3,
        40,
        flops=8 * x.size * enc_taps.shape[1],
    )


def pair_place(batches):
    me = lax.axis_index("batch")
    place = lax.div(me, 2)
    return place, me - 2 * place, batches // 2


def greet_pairs(tasks, batches):
    place, core, chips = pair_place(batches)
    task = lax.axis_index("task")
    barrier = pltpu.get_barrier_semaphore()

    def signal(device):
        pl.semaphore_signal(barrier, inc=1, device_id=device, device_id_type=MESH)

    for step in range(1, tasks):
        signal({"task": lax.rem(task + step, tasks)})
    signal({"batch": 2 * place + 1 - core})
    for step in range(1, chips):
        signal({"batch": 2 * lax.rem(place + step, chips) + core})
    pl.semaphore_wait(barrier, tasks - 1 + chips)


def block_rows(ref, index, count):
    return ref.at[pl.ds(pl.multiple_of(index * count, 8), count), :]


def far_first(chips):
    return sorted(range(chips), key=lambda step: -min(step, chips - step))


def pair_sum(batches, source, near, paired, far, sems):
    place, core, chips = pair_place(batches)
    count = near.shape[1]
    near_send, near_receive, far_send, far_receive = sems
    other = 2 * place + 1 - core

    def near_copy(step):
        chip = lax.rem(place + step, chips)
        return remote(block_rows(source, 2 * chip + 1 - core, count), near.at[step],
                      near_send.at[step], near_receive.at[step], other, "batch")

    def far_copy(step, incoming=False):
        chip = lax.rem(place + (chips - step if incoming else step), chips)
        return remote(paired.at[step], far.at[step], far_send.at[step], far_receive.at[step],
                      2 * chip + core, "batch")

    for step in far_first(chips):
        near_copy(step).start()

    def middle():
        for step in far_first(chips):
            chip = lax.rem(place + step, chips)
            near_copy(step).wait_recv()
            if step:
                total = block_rows(source, 2 * chip + core, count)[...].astype(F32)
                paired[step] = (total + near[step].astype(F32)).astype(paired.dtype)
                far_copy(step).start()

    def end():
        total = block_rows(source, 2 * place + core, count)[...].astype(F32)
        total = total + near[0].astype(F32)
        for step in range(1, chips):
            far_copy(step, True).wait_recv()
            total = total + far[step].astype(F32)
        for step in range(chips):
            near_copy(step).wait_send()
            if step:
                far_copy(step).wait_send()
        return total

    return middle, end


def pair_scratch(batches, rows, width, kind):
    chips = batches // 2
    return [pltpu.VMEM((chips, rows // batches, width), kind)] * 3 + [
        pltpu.SemaphoreType.DMA((chips,))
    ] * 4


def collect_body(
    tasks, batches,
    slots, flow, sums,
    input_grad, owned, part, norm_sums,
    near, paired, far, near_send, near_receive, far_send, far_receive,
    flow_in, flow_send, flow_receive, send, receive, sum_send, sum_receive,
):
    task = lax.axis_index("task")
    width = part.shape[1]
    pixels = input_grad.shape[0]

    def peer_of(step, incoming):
        return lax.rem(task + (tasks - step if incoming else step), tasks)

    def flow_copy(step, incoming=False):
        peer = peer_of(step, incoming)
        return remote(block_rows(flow, peer, pixels), flow_in.at[step - 1], flow_send.at[step],
                      flow_receive.at[step], peer, "task")

    def sum_copy(step, incoming=False):
        peer = peer_of(step, incoming)
        home = peer if incoming else task
        return remote(sums, norm_sums.at[:, columns_of(home, width)], sum_send.at[step],
                      sum_receive.at[step], peer, "task")

    def part_copy(step, incoming=False):
        peer = peer_of(step, incoming)
        home = peer if incoming else task
        return remote(part, owned.at[:, columns_of(home, width)], send.at[step], receive.at[step],
                      peer, "task")

    greet_pairs(tasks, batches)
    middle, end = pair_sum(
        batches, slots, near, paired, far, (near_send, near_receive, far_send, far_receive)
    )
    for step in range(1, tasks):
        sum_copy(step).start()
        flow_copy(step).start()
    norm_sums[:, columns_of(task, width)] = sums[...]
    middle()
    total = end().astype(BF)
    part[...] = total
    for step in range(1, tasks):
        part_copy(step).start()
    owned[:, columns_of(task, width)] = total
    total = block_rows(flow, task, pixels)[...].astype(F32)
    for step in range(1, tasks):
        flow_copy(step, True).wait_recv()
        total = total + flow_in[step - 1].astype(F32)
    input_grad[...] = total
    for step in range(1, tasks):
        sum_copy(step, True).wait_recv()
        part_copy(step, True).wait_recv()
        sum_copy(step).wait_send()
        part_copy(step).wait_send()
        flow_copy(step).wait_send()


def collect(tasks, batches, slots, flow, sums):
    count, width = slots.shape
    rows = count // batches
    pixels, channels = flow.shape[0] // tasks, flow.shape[1]
    return exchange_kernel(
        functools.partial(collect_body, tasks, batches),
        [
            shape((pixels, channels), F32),
            shape((rows, channels), BF),
            shape((rows, width), BF),
            shape((8, channels), F32),
        ],
        "vvv",
        (slots, flow, sums),
        pair_scratch(batches, count, width, BF)
        + [pltpu.VMEM((tasks - 1, pixels, channels), BF)]
        + [pltpu.SemaphoreType.DMA((tasks,))] * 6,
        5,
        24,
        flops=20000 * MIB,
    )


def grams_body(
    tasks, batches,
    grad, part, owners, head_grad, head_owners,
    grams, head_grams,
    mine, head_mine,
    near, paired, far, near_send, near_receive, far_send, far_receive,
    head_near, head_paired, head_far, *rest,
):
    head_sems = rest[:4]
    chip_send, chip_receive, task_send, task_receive, pair_send, pair_receive = rest[4:]
    task = lax.axis_index("task")
    place, core, chips = pair_place(batches)
    width = part.shape[1]
    channels = grad.shape[1]
    count, head_count = near.shape[1], head_near.shape[1]
    for m in range(head_owners.shape[1]):
        held = (head_grad[...].astype(F32) * head_owners[:, m : m + 1]).astype(BF)
        head_mine[m * channels : (m + 1) * channels, :] = dot_tn(held, head_grad[...]).astype(
            head_mine.dtype
        )
    greet_pairs(tasks, batches)
    head_middle, head_end = pair_sum(
        batches, head_mine, head_near, head_paired, head_far, head_sems
    )
    for m in range(owners.shape[1]):
        held = (grad[...].astype(F32) * owners[:, m : m + 1]).astype(BF)
        mine[m * channels : (m + 1) * channels, :] = dot_tn(held, part[...]).astype(mine.dtype)
    middle, end = pair_sum(
        batches, mine, near, paired, far, (near_send, near_receive, far_send, far_receive)
    )
    head_middle()
    middle()

    def trunk_block(chip, home, which):
        rows = pl.ds(pl.multiple_of((2 * chip + which) * count, 8), count)
        return grams.at[rows, columns_of(home, width)]

    def head_block(chip, which):
        return block_rows(head_grams, 2 * chip + which, head_count)

    def chip_copy(kind, step, incoming=False):
        peer = lax.rem(place + (chips - step if incoming else step), chips)
        home = peer if incoming else place
        block = head_block(home, core) if kind else trunk_block(home, task, core)
        return remote(block, block, chip_send.at[kind, step], chip_receive.at[kind, step],
                      2 * peer + core, "batch")

    def task_copy(step, hop, incoming=False):
        peer = lax.rem(task + (tasks - step if incoming else step), tasks)
        chip = lax.rem(place + chips - hop, chips)
        block = trunk_block(chip, peer if incoming else task, core)
        return remote(block, block, task_send.at[step, hop], task_receive.at[step, hop], peer, "task")

    def pair_copy(kind, hop, incoming=False):
        chip = lax.rem(place + chips - hop, chips)
        which = 1 - core if incoming else core
        home = lax.rem(task + tasks - kind, tasks)
        block = head_block(chip, which) if kind == tasks else trunk_block(chip, home, which)
        return remote(block, block, pair_send.at[kind, hop], pair_receive.at[kind, hop],
                      2 * place + 1 - core, "batch")

    total = end().astype(grams.dtype)
    trunk_block(place, task, core)[...] = total
    for step in range(1, chips):
        chip_copy(0, step).start()
    for step in range(1, tasks):
        task_copy(step, 0).start()
    pair_copy(0, 0).start()
    total = head_end().astype(head_grams.dtype)
    head_block(place, core)[...] = total
    for step in range(1, chips):
        chip_copy(1, step).start()
    pair_copy(tasks, 0).start()
    for hop in range(1, chips):
        chip_copy(0, hop, True).wait_recv()
        for step in range(1, tasks):
            task_copy(step, hop).start()
        pair_copy(0, hop).start()
    for hop in range(chips):
        for step in range(1, tasks):
            task_copy(step, hop, True).wait_recv()
            pair_copy(step, hop).start()
    for hop in range(1, chips):
        chip_copy(1, hop, True).wait_recv()
        pair_copy(tasks, hop).start()
    for hop in range(chips):
        for kind in range(tasks + 1):
            pair_copy(kind, hop, True).wait_recv()
    for hop in range(chips):
        for kind in range(tasks + 1):
            pair_copy(kind, hop).wait_send()
        for step in range(1, tasks):
            task_copy(step, hop).wait_send()
        if hop:
            chip_copy(0, hop).wait_send()
            chip_copy(1, hop).wait_send()


def all_grams(tasks, batches, grad, part, owners, head_grad, head_owners):
    channels, width = grad.shape[1], part.shape[1]
    rows, head_rows = owners.shape[1] * channels, head_owners.shape[1] * channels
    chips = batches // 2
    kind = BF if rows % (16 * batches) == 0 else F32
    head_kind = BF if head_rows % (16 * batches) == 0 else F32
    return exchange_kernel(
        functools.partial(grams_body, tasks, batches),
        [shape((rows, channels), kind), shape((head_rows, channels), head_kind)],
        "vvvvv",
        (grad, part, owners, head_grad, head_owners),
        [pltpu.VMEM((rows, width), kind), pltpu.VMEM((head_rows, channels), head_kind)]
        + pair_scratch(batches, rows, width, kind)
        + pair_scratch(batches, head_rows, channels, head_kind)
        + [pltpu.SemaphoreType.DMA((2, chips))] * 2
        + [pltpu.SemaphoreType.DMA((tasks, chips))] * 2
        + [pltpu.SemaphoreType.DMA((tasks + 1, chips))] * 2,
        6,
        32,
        flops=20000 * MIB,
    )


def exchange(body, outs, args, scratch, identity, vmem=32):
    size = sum(o.size * o.dtype.itemsize for o in outs) + sum(a.size * a.dtype.itemsize for a in args)
    return pl.pallas_call(
        body,
        out_shape=tuple(outs),
        in_specs=[VMEM_SPEC] * len(args),
        out_specs=tuple(VMEM_SPEC for _ in outs),
        scratch_shapes=list(scratch),
        compiler_params=pltpu.CompilerParams(
            vmem_limit_bytes=vmem * MIB, collective_id=identity, has_side_effects=True
        ),
        cost_estimate=pl.CostEstimate(flops=0, bytes_accessed=size, transcendentals=0),
    )(*args)


def block_of(ref, place, size, dim):
    length = ref.shape[dim] // size
    start = place * length
    if dim == 0:
        return ref.at[pl.ds(pl.multiple_of(start, 8), length), :]
    return ref.at[:, pl.ds(pl.multiple_of(start, 128), length)]


def gather_body(axis, size, dims, *refs):
    count = len(dims)
    sources, targets = refs[:count], refs[count : 2 * count]
    sends, receives, own = refs[2 * count :]
    greet(((axis, size),))
    me = lax.axis_index(axis)
    copies = []
    for k in range(count):
        mine = block_of(targets[k], me, size, dims[k])
        for step in range(1, size):
            peer = lax.rem(me + step, size)
            copy = remote(sources[k], mine, sends.at[k, step], receives.at[k, me], peer, axis)
            copy.start()
            copies.append(copy)
    locals_ = []
    for k in range(count):
        mine = block_of(targets[k], me, size, dims[k])
        copy = pltpu.make_async_copy(sources[k], mine, own.at[k])
        copy.start()
        locals_.append(copy)
    for copy in locals_:
        copy.wait()
    for k in range(count):
        for step in range(1, size):
            peer = lax.rem(me + size - step, size)
            theirs = block_of(targets[k], peer, size, dims[k])
            remote(
                sources[k], theirs, sends.at[k, step], receives.at[k, peer], peer, axis
            ).wait_recv()
    for copy in copies:
        copy.wait_send()


def gather_over(axis, size, arrays, dims, identity):
    outs = []
    for x, dim in zip(arrays, dims):
        full = list(x.shape)
        full[dim] *= size
        outs.append(shape(full, x.dtype))
    count = len(arrays)
    return exchange(
        functools.partial(gather_body, axis, size, tuple(dims)),
        outs,
        arrays,
        [
            pltpu.SemaphoreType.DMA((count, size)),
            pltpu.SemaphoreType.DMA((count, size)),
            pltpu.SemaphoreType.DMA((count,)),
        ],
        identity,
    )


def to_taps_body(index, slots, enc, dec, wide, tap):
    count = slots.shape[0]
    channels = enc.shape[0]
    width = slots.shape[1]
    step = 1024

    def widen(i, carry):
        rows = pl.ds(pl.multiple_of(i * step, step), step)
        wide[rows, :] = slots[rows, :].astype(F32)
        return carry

    lax.fori_loop(0, count // step, widen, 0)
    group = 32
    for p in range(18):

        def fetch(i, carry):
            base = i * group
            for u in range(group):
                tap[pl.ds(base + u, 1), :] = wide[pl.ds(index[p * channels + base + u], 1), :]
            return carry

        lax.fori_loop(0, channels // group, fetch, 0)
        out = enc if p < 9 else dec
        q = p % 9
        out[:, q * width : (q + 1) * width] = tap[...].astype(BF)


def to_taps(index, slots, channels):
    width = slots.shape[1]
    return run(
        to_taps_body,
        [shape((channels, 9 * width), BF)] * 2,
        "sv",
        (index, slots),
        [pltpu.VMEM(slots.shape, F32), pltpu.VMEM((channels, width), F32)],
    )


def to_slots_body(index, enc, dec, slots, wide):
    count = slots.shape[0]
    channels = enc.shape[0]
    width = slots.shape[1]
    step = 1024
    group = 32
    for p in range(18):
        source = enc if p < 9 else dec
        q = p % 9

        def place(i, carry):
            base = pl.multiple_of(i * group, group)
            values = source[pl.ds(base, group), q * width : (q + 1) * width]
            for u in range(group):
                wide[pl.ds(index[p * channels + base + u], 1), :] = values[u : u + 1, :]
            return carry

        lax.fori_loop(0, channels // group, place, 0)

    def narrow(i, carry):
        rows = pl.ds(pl.multiple_of(i * step, step), step)
        slots[rows, :] = wide[rows, :].astype(BF)
        return carry

    lax.fori_loop(0, count // step, narrow, 0)


def to_slots(index, enc, dec):
    width = enc.shape[1] // 9
    dims = (index.shape[0], width)
    return run(
        to_slots_body, [shape(dims, BF)], "svv", (index, enc, dec), [pltpu.VMEM(dims, F32)]
    )[0]


def adam(gradient, moment_one, moment_two):
    new_one = BETA_ONE * moment_one + (1.0 - BETA_ONE) * gradient
    new_two = BETA_TWO * moment_two + (1.0 - BETA_TWO) * gradient * gradient
    direction = (
        new_one / (1.0 - BETA_ONE**STEP) / (jnp.sqrt(new_two / (1.0 - BETA_TWO**STEP)) + ADAM_EPS)
    )
    return new_one, new_two, direction


def soap_body(
    cuts, grad, owners, weight, one, two, basis, weight_new, one_new, two_new, low
):
    count = basis.shape[0]
    total = grad.shape[0]
    for m in range(count):
        low[m] = basis[m].astype(BF)

    def chunk(i, carry):
        rows = pl.ds(pl.multiple_of(i * (total // cuts), 8), total // cuts)
        values = grad[rows, :].astype(F32)
        rotated = None
        for m in range(count):
            part = dot((values * owners[rows, m : m + 1]).astype(BF), low[m])
            rotated = part if rotated is None else rotated + part
        new_one, new_two, direction = adam(rotated, one[rows, :], two[rows, :])
        one_new[rows, :] = new_one
        two_new[rows, :] = new_two
        stepped = None
        for m in range(count):
            part = dot_nt((direction * owners[rows, m : m + 1]).astype(BF), low[m])
            stepped = part if stepped is None else stepped + part
        old = weight[rows, :]
        weight_new[rows, :] = old - LEARN_MATRIX * (stepped + DECAY_MATRIX * old)
        return carry

    lax.fori_loop(0, cuts, chunk, 0)


def soap(grad, owners, weight, one, two, basis):
    total = grad.shape[0]
    cuts = 4 if total % 64 == 0 else 1
    return run(
        functools.partial(soap_body, cuts),
        [shape(weight.shape, F32)] * 3,
        "vvvvvv",
        (grad, owners, weight, one, two, basis),
        [pltpu.VMEM(basis.shape, BF)],
        flops=4 * weight.size * weight.shape[1] * basis.shape[0],
    )


def factor_rows(values, identity, turn):
    width = values.shape[1]
    sub = lax.broadcasted_iota(jnp.int32, (8, width), 0)
    rolled = pltpu.roll(values, turn, 1)
    columns = [jnp.broadcast_to(rolled[:, j : j + 1], (8, width)) for j in range(8)]
    scale = jnp.zeros((8, width), F32)
    for j in range(8):
        root = lax.rsqrt(columns[j][j : j + 1, :])
        scale = jnp.where(sub == j, root, scale)
        lower = jnp.where(sub > j, columns[j] * root, 0.0)
        values = values - lower * (values[j : j + 1, :] * root)
        identity = identity - lower * (identity[j : j + 1, :] * root)
        for i in range(j + 1, 8):
            columns[i] = columns[i] - lower * (columns[i][j : j + 1, :] * root)
    return values * scale, identity * scale


def renew_body(counts, *refs):
    groups = len(counts)
    stats, bases, grams = (refs[k * groups : (k + 1) * groups] for k in range(3))
    stats_new, bases_new = (refs[k * groups : (k + 1) * groups] for k in (3, 4))
    count = sum(counts)
    product = refs[5 * groups]
    tables = refs[5 * groups + 1 : 5 * groups + 1 + count]
    inverses = refs[5 * groups + 1 + count :]
    homes = [(g, m) for g in range(groups) for m in range(counts[g])]
    size = stats[0].shape[1]
    panel = 128
    matrices = range(count)
    row = lax.broadcasted_iota(jnp.int32, (panel, panel), 0)
    col = lax.broadcasted_iota(jnp.int32, (panel, panel), 1)
    unit = jnp.where(row == col, 1.0, 0.0).astype(F32)
    for n, (g, m) in enumerate(homes):
        new = STAT_DECAY * stats[g][m] + (1.0 - STAT_DECAY) * grams[g][m].astype(F32)
        stats_new[g][m] = new
        product[n] = dot3(dot, new, bases[g][m])
    for k in range(size // panel):
        here = slice(k * panel, (k + 1) * panel)
        for n in matrices:
            tables[n][:, :panel] = dot3(dot_tn, product[n, :, here], product[n, :, here])
            tables[n][:, panel:] = unit

        def group(q, carry):
            rows = pl.ds(pl.multiple_of(q * 8, 8), 8)
            turn = lax.rem(panel - q * 8, panel)
            done = [
                factor_rows(tables[n][rows, :panel], tables[n][rows, panel:], turn)
                for n in matrices
            ]
            for n in matrices:
                upper, inverse = done[n]
                inverses[n][rows, :] = inverse
                both = jnp.concatenate([upper, inverse], axis=1)
                tables[n][...] = tables[n][...] - dot3(dot_tn, upper, both)
            return carry

        lax.fori_loop(0, panel // 8, group, 0)
        for n, (g, m) in enumerate(homes):
            turned = dot3(dot_nt, product[n, :, here], inverses[n][...])
            bases_new[g][m, :, here] = turned
            if k < size // panel - 1:
                rest = slice((k + 1) * panel, size)
                product[n, :, rest] = product[n, :, rest] - dot3(
                    dot, turned, dot3(dot_tn, turned, product[n, :, rest])
                )


def renew_bases(stats, bases, grams):
    counts = tuple(s.shape[0] for s in stats)
    count = sum(counts)
    size = stats[0].shape[1]
    return run(
        functools.partial(renew_body, counts),
        [shape(s.shape, F32) for s in stats] * 2,
        "v" * (3 * len(stats)),
        (*stats, *bases, *grams),
        [pltpu.VMEM((count, size, size), F32)]
        + [pltpu.VMEM((128, 256), F32)] * count
        + [pltpu.VMEM((128, 128), F32)] * count,
        flops=60 * MIB * MIB // 1024,
    )


def local(
    tasks,
    batches,
    images,
    image_small,
    pool_index,
    row_slot,
    trunk_weight,
    trunk_mean_grad,
    trunk_mean_square,
    trunk_statistic,
    trunk_basis,
    head_weight,
    head_mean_grad,
    head_mean_square,
    head_statistic,
    head_basis,
    trunk_gain,
    trunk_offset,
    trunk_norm_mean_grad,
    trunk_norm_mean_square,
    head_gain,
    head_offset,
    head_norm_mean_grad,
    head_norm_mean_square,
    cotangent,
):
    number, height, breadth, channels = images.shape
    pixels = height * breadth
    tap_rows = 9 * channels
    shown = tasks * number
    geometry = (shown, height, breadth)
    task = lax.axis_index("task")
    batch = lax.axis_index("batch")
    width = channels // tasks

    def quarter(values):
        return lax.dynamic_slice_in_dim(values, task * width, width, values.ndim - 1)

    def inside(flags):
        row_limit = jnp.where(flags > 0, height // 2, height)[:, None, None]
        col_limit = jnp.where(flags > 0, breadth // 2, breadth)[:, None, None]
        return (jnp.arange(height, dtype=jnp.int32)[None, :, None] < row_limit) & (
            jnp.arange(breadth, dtype=jnp.int32)[None, None, :] < col_limit
        )

    slots = lax.all_gather(quarter(trunk_weight).astype(BF), "batch", axis=0, tiled=True)
    head_rows = lax.all_gather(head_weight.astype(BF), "batch", axis=1, tiled=True)[0]
    kinds = jnp.concatenate([image_small, pool_index.reshape(-1)])
    kinds = lax.all_gather(kinds, "task", axis=0, tiled=True).reshape(tasks, -1)
    small = kinds[:, :number].reshape(-1)
    cells = kinds[:, number:].reshape(shown, height // 2, 1, breadth // 2, 1)
    cell = 2 * jnp.arange(2, dtype=jnp.int32)[:, None, None] + jnp.arange(2, dtype=jnp.int32)
    choose = (cells == cell).reshape(shown, height, breadth) & inside(small)
    choose = choose.astype(F32)
    choose_row = choose.reshape(shown, 1, pixels)
    choose = choose.reshape(shown * pixels, 1)
    masked = (images * inside(image_small)[..., None].astype(BF)).reshape(number * pixels, channels)
    x = gather_over("task", tasks, (masked,), (0,), 4)[0]
    enc_taps, dec_taps = to_taps(row_slot, slots, channels)

    scales = quarter(jnp.stack([trunk_gain, trunk_offset], axis=1)).reshape(4, width)
    enc_pre, enc_totals, spread, dec_pre, dec_totals, features = trunk_forward(
        geometry, tasks, batches, small, x, enc_taps, dec_taps, scales, choose
    )
    head_scales = jnp.stack([head_gain[0], head_offset[0]], axis=1).reshape(6, channels)
    pooled, head_grads, upstream, head_sums = head(
        geometry, tasks, batches, small, features, head_rows,
        cotangent.reshape(shown, pixels // 4, channels), head_scales, enc_totals,
    )
    task_features = pooled.reshape(cotangent.shape)
    head_owned = lax.psum_scatter(head_grads, "batch", scatter_dimension=0, tiled=True)
    enc_grad, dec_grad, flow, trunk_sums = trunk_backward(
        geometry, tasks, batches, small, upstream, enc_pre, enc_totals, dec_pre, dec_totals,
        scales, choose, choose_row, x, spread, enc_taps, dec_taps,
    )
    input_grad, trunk_owned, trunk_part, norm_sums = collect(
        tasks, batches, to_slots(row_slot, enc_grad, dec_grad), flow, trunk_sums
    )
    input_grad = input_grad.reshape(images.shape)

    head_local = head_weight.shape[1]
    head_ids = batch * head_local + jnp.arange(head_local, dtype=jnp.int32)
    head_owner = jnp.minimum(head_ids // channels, 2)
    head_onehot = (head_owner[:, None] == jnp.arange(3, dtype=jnp.int32)).astype(F32)
    head_weight_new, head_one_new, head_two_new = soap(
        head_owned, head_onehot, head_weight[0], head_mean_grad[0], head_mean_square[0],
        head_basis[0],
    )

    local_rows = trunk_weight.shape[0]
    slot_ids = batch * local_rows + jnp.arange(local_rows, dtype=jnp.int32)
    trunk_owner = jnp.take(jnp.argsort(row_slot), slot_ids) // tap_rows
    trunk_onehot = (trunk_owner[:, None] == jnp.arange(2, dtype=jnp.int32)).astype(F32)
    trunk_grams, head_grams = all_grams(
        tasks, batches, trunk_owned, trunk_part, trunk_onehot, head_owned, head_onehot
    )
    trunk_weight_new, trunk_one_new, trunk_two_new = soap(
        trunk_owned, trunk_onehot, trunk_weight, trunk_mean_grad, trunk_mean_square, trunk_basis
    )
    trunk_stat_new, head_stat_new, trunk_basis_new, head_basis_new = renew_bases(
        (trunk_statistic, head_statistic[0]),
        (trunk_basis, head_basis[0]),
        (trunk_grams.reshape(trunk_basis.shape), head_grams.reshape(head_basis.shape[1:])),
    )

    trunk_norm = jnp.stack([trunk_gain, trunk_offset], axis=1)
    trunk_norm_grad = norm_sums[:4].reshape(2, 2, channels)[:, ::-1]
    trunk_norm_one, trunk_norm_two, trunk_direction = adam(
        trunk_norm_grad, trunk_norm_mean_grad, trunk_norm_mean_square
    )
    head_norm = jnp.stack([head_gain, head_offset], axis=2)
    head_norm_grad = head_sums[:6].reshape(1, 3, 2, channels)[:, :, ::-1]
    head_norm_one, head_norm_two, head_direction = adam(
        head_norm_grad, head_norm_mean_grad, head_norm_mean_square
    )
    return (
        task_features,
        input_grad,
        trunk_weight_new,
        trunk_one_new,
        trunk_two_new,
        trunk_stat_new,
        trunk_basis_new,
        head_weight_new[None],
        head_one_new[None],
        head_two_new[None],
        head_stat_new[None],
        head_basis_new[None],
        trunk_norm - LEARN_NORM * trunk_direction,
        trunk_norm_one,
        trunk_norm_two,
        head_norm - LEARN_NORM * head_direction,
        head_norm_one,
        head_norm_two,
    )


def solution(mesh):
    placed = (
        P(("task", "batch"), None, None, None),
        P(("task", "batch")),
        P(("task", "batch"), None, None),
        P(),
        P("batch", None),
        P("batch", None),
        P("batch", None),
        P(),
        P(),
        P("task", "batch", None),
        P("task", "batch", None),
        P("task", "batch", None),
        P("task", None, None, None),
        P("task", None, None, None),
        P(),
        P(),
        P(),
        P(),
        P("task", None, None),
        P("task", None, None),
        P("task", None, None, None),
        P("task", None, None, None),
        P("task", None, "batch", None, None, None),
    )
    return jax.shard_map(
        functools.partial(local, mesh.shape["task"], mesh.shape["batch"]),
        mesh=mesh,
        in_specs=placed,
        out_specs=(
            P("task", None, "batch", None, None, None),
            P(("task", "batch"), None, None, None),
            P("batch", None),
            P("batch", None),
            P("batch", None),
            P(),
            P(),
            P("task", "batch", None),
            P("task", "batch", None),
            P("task", "batch", None),
            P("task", None, None, None),
            P("task", None, None, None),
            P(),
            P(),
            P(),
            P("task", None, None, None),
            P("task", None, None, None),
            P("task", None, None, None),
        ),
        check_vma=False,
    )
```

```python
import functools

import jax
import jax.numpy as jnp
from jax import lax
from jax.experimental import pallas as pl
from jax.experimental.pallas import tpu as pltpu
from jax.sharding import PartitionSpec as P

STEP = 10


EPS = 1e-05
ADAM_EPS = 1e-08
BETA_ONE = 0.95
BETA_TWO = 0.95
STAT_DECAY = 0.95
LEARN_MATRIX = 0.02
LEARN_NORM = 0.5
DECAY_MATRIX = 0.01
BF = jnp.bfloat16
F32 = jnp.float32
MESH = pl.DeviceIdType.MESH
MIB = 1 << 20

VMEM_SPEC = pl.BlockSpec(memory_space=pltpu.VMEM)
SMEM_SPEC = pl.BlockSpec(memory_space=pltpu.SMEM)


def run(body, outs, specs, args, scratch=(), vmem=40, flops=0):
    size = sum(o.size * o.dtype.itemsize for o in outs) + sum(a.size * a.dtype.itemsize for a in args)
    return pl.pallas_call(
        body,
        out_shape=tuple(outs),
        in_specs=[SMEM_SPEC if s == "s" else VMEM_SPEC for s in specs],
        out_specs=tuple(VMEM_SPEC for _ in outs),
        scratch_shapes=list(scratch),
        compiler_params=pltpu.CompilerParams(vmem_limit_bytes=vmem * MIB),
        cost_estimate=pl.CostEstimate(flops=flops, bytes_accessed=size, transcendentals=0),
    )(*args)


def shape(dims, kind):
    return jax.ShapeDtypeStruct(tuple(dims), kind)


def dot(a, b):
    return jnp.dot(a, b, preferred_element_type=F32)


def dot_nt(a, b):
    return lax.dot_general(a, b, (((1,), (1,)), ((), ())), preferred_element_type=F32)


def dot_tn(a, b):
    return lax.dot_general(a, b, (((0,), (0,)), ((), ())), preferred_element_type=F32)


def split(a):
    high = a.astype(BF)
    return high, (a - high.astype(F32)).astype(BF)


def dot3(kind, a, b):
    a_high, a_low = split(a)
    b_high, b_low = split(b)
    return kind(a_high, b_high) + (kind(a_high, b_low) + kind(a_low, b_high))


def places(height, breadth):
    index = lax.broadcasted_iota(jnp.int32, (height * breadth, 1), 0)
    row = lax.div(index, breadth)
    return row, index - row * breadth


def valid_rows(small, height, breadth):
    row, col = places(height, breadth)
    row_limit = jnp.where(small > 0, height // 2, height)
    col_limit = jnp.where(small > 0, breadth // 2, breadth)
    return jnp.where((row < row_limit) & (col < col_limit), 1.0, 0.0).astype(F32)


def move(values, rows):
    gap = jnp.zeros((abs(rows),) + values.shape[1:], values.dtype)
    if rows > 0:
        return jnp.concatenate([gap, values[:-rows]], axis=0)
    return jnp.concatenate([values[-rows:], gap], axis=0)


def from_left(values, col):
    return jnp.where(col > 0, pltpu.roll(values, 1, 0), 0.0)


def from_right(values, col, breadth):
    return jnp.where(col < breadth - 1, pltpu.roll(values, values.shape[0] - 1, 0), 0.0)


def gather_taps(tap, breadth, col):
    lines = [move(tap(b), breadth) + tap(3 + b) + move(tap(6 + b), -breadth) for b in range(3)]
    return lines[1] + from_left(lines[0], col) + from_right(lines[2], col, breadth)


def spread_taps(values, breadth, col):
    lines = [from_right(values, col, breadth), values, from_left(values, col)]
    return [
        move(lines[b], breadth * (a - 1)) if a != 1 else lines[b] for a in range(3) for b in range(3)
    ]


def window_sum(values, row, col, breadth):
    count = values.shape[0]
    pair = values + jnp.where(
        col % 2 == 0, pltpu.roll(values, count - 1, 0), pltpu.roll(values, 1, 0)
    )
    return pair + jnp.where(row % 2 == 0, move(pair, -breadth), move(pair, breadth))


def silu_back(scaled):
    sig = jax.nn.sigmoid(scaled)
    return sig * (1.0 + scaled * (1.0 - sig))


def col_sum(values):
    return jnp.sum(values, axis=0, keepdims=True)


def put_sums(ref, rows):
    width = ref.shape[1]
    rows = list(rows) + [jnp.zeros((1, width), F32)] * (8 - len(rows))
    ref[...] = jnp.concatenate(rows, axis=0)


def each_image(geometry, body, start):
    number, height, breadth = geometry
    pixels = height * breadth

    def step(image, carry):
        return body(image, pl.ds(pl.multiple_of(image * pixels, 16), pixels), carry)

    return lax.fori_loop(0, number, step, start)


def zero_rows(count, width):
    return (jnp.zeros((1, width), F32),) * count


def greet(axes):
    barrier = pltpu.get_barrier_semaphore()
    for axis, size in axes:
        me = lax.axis_index(axis)
        for step in range(1, size):
            pl.semaphore_signal(
                barrier, inc=1, device_id={axis: lax.rem(me + step, size)}, device_id_type=MESH
            )
    pl.semaphore_wait(barrier, sum(size - 1 for _, size in axes))


def remote(source, target, sends, receives, peer, axis):
    return pltpu.make_async_remote_copy(
        src_ref=source,
        dst_ref=target,
        send_sem=sends,
        recv_sem=receives,
        device_id={axis: peer},
        device_id_type=MESH,
    )


def pack(rows):
    parts = [row[:, i : i + 128] for row in rows for i in range(0, row.shape[1], 128)]
    parts += [jnp.zeros((1, 128), F32)] * (8 - len(parts))
    return jnp.concatenate(parts, axis=0)


def unpack(tile, count, width):
    per = width // 128
    return [
        jnp.concatenate([tile[k * per + i : k * per + i + 1, :] for i in range(per)], axis=1)
        for k in range(count)
    ]


def total_rows(k, axis, size, rows, mine, slots, sends, receives):
    me = lax.axis_index(axis)
    tile = pack(rows)
    mine[k] = tile
    slots[k, me] = tile
    for step in range(1, size):
        peer = lax.rem(me + step, size)
        remote(mine.at[k], slots.at[k, me], sends.at[k, step], receives.at[k, me], peer, axis).start()
    for step in range(1, size):
        peer = lax.rem(me + size - step, size)
        remote(
            mine.at[k], slots.at[k, peer], sends.at[k, step], receives.at[k, peer], peer, axis
        ).wait_recv()
    total = slots[k, 0]
    for peer in range(1, size):
        total = total + slots[k, peer]
    for step in range(1, size):
        peer = lax.rem(me + step, size)
        remote(
            mine.at[k], slots.at[k, me], sends.at[k, step], receives.at[k, me], peer, axis
        ).wait_send()
    return unpack(total, len(rows), rows[0].shape[1])


def total_scratch(count, size):
    return [
        pltpu.VMEM((count, 8, 128), F32),
        pltpu.VMEM((count, size, 8, 128), F32),
        pltpu.SemaphoreType.DMA((count, size)),
        pltpu.SemaphoreType.DMA((count, size)),
    ]


def columns_of(place, width):
    return pl.ds(pl.multiple_of(place * width, 128), width)


SPECS = {"s": SMEM_SPEC, "v": VMEM_SPEC, "h": pl.BlockSpec(memory_space=pltpu.HBM)}


def exchange_kernel(body, outs, specs, args, scratch, identity, vmem, flops=0, places_out=None):
    size = sum(o.size * o.dtype.itemsize for o in outs) + sum(a.size * a.dtype.itemsize for a in args)
    return pl.pallas_call(
        body,
        out_shape=tuple(outs),
        in_specs=[SPECS[s] for s in specs],
        out_specs=tuple(SPECS[s] for s in places_out or "v" * len(outs)),
        scratch_shapes=list(scratch),
        compiler_params=pltpu.CompilerParams(
            vmem_limit_bytes=vmem * MIB, collective_id=identity, has_side_effects=True
        ),
        cost_estimate=pl.CostEstimate(flops=flops, bytes_accessed=size, transcendentals=0),
    )(*args)


def norm_with(values, totals, scale):
    total, squares, count = totals
    center = total / count
    inverse = lax.rsqrt(squares / count - center * center + EPS)
    normal = (values - center) * inverse
    return normal, inverse, normal * scale[0] + scale[1]


def norm_back_with(upstream, normal, inverse, count, sums, scale, valid):
    return scale[0] * inverse * (upstream - sums[0] / count - normal * (sums[1] / count)) * valid


def silu(values):
    return values * jax.nn.sigmoid(values)


def window_count(height, breadth):
    return -(-(height * breadth // 4) // 16) * 16


def pool_choice(height, breadth, windows, flipped):
    pixels = height * breadth
    dims = (windows, pixels) if flipped else (pixels, windows)
    pixel = lax.broadcasted_iota(jnp.int32, dims, 1 if flipped else 0)
    window = lax.broadcasted_iota(jnp.int32, dims, 0 if flipped else 1)
    row = lax.div(pixel, breadth)
    col = pixel - row * breadth
    home = lax.div(row, 2) * (breadth // 2) + lax.div(col, 2)
    return jnp.where(home == window, 1.0, 0.0).astype(F32)


def rows_of(ref, first, count):
    return [ref[first + k : first + k + 1, :] for k in range(count)]


def window_rows(i, windows):
    return pl.ds(pl.multiple_of(i * windows, 16), windows)


def trunk_forward_body(
    geometry, tasks, batches,
    small, x, enc_taps, dec_taps, scales, choose,
    enc_totals, dec_totals, features, *rest,
):
    kept, (enc_pre, dec_pre, spread), rest = rest[:6], rest[6:9], rest[9:]
    (
        work, pooled, pooled_all, part, pool_sends, pool_receives, sends, receives,
    mine, slots, total_sends, total_receives, saved,
    ) = rest
    number, height, breadth = geometry
    width = enc_pre.shape[1]
    windows = window_count(height, breadth)
    task = lax.axis_index("task")
    _, col = places(height, breadth)
    widen = pool_choice(height, breadth, windows, False).astype(BF)
    narrow = pool_choice(height, breadth, windows, True).astype(BF)

    sources = (x, enc_taps, dec_taps, enc_pre, dec_pre, spread)
    saves = [pltpu.make_async_copy(a, b, saved.at[k]) for k, (a, b) in enumerate(zip(sources, kept))]
    for copy in saves[:3]:
        copy.start()

    def conv(x, taps, pre):
        def image(i, rows, carry):
            valid = valid_rows(small[i], height, breadth)
            work[...] = dot(x[rows, :], taps[...])
            out = gather_taps(lambda p: work[:, p * width : (p + 1) * width], breadth, col)
            pre[rows, :] = out
            kept = out * valid
            return (
                carry[0] + col_sum(kept),
                carry[1] + col_sum(kept * out),
                carry[2] + jnp.broadcast_to(col_sum(valid), (1, width)),
            )

        return each_image(geometry, image, zero_rows(3, width))

    def total(k, rows):
        return total_rows(
            k, "batch", batches, list(rows), mine, slots, total_sends, total_receives
        )

    sums = conv(x, enc_taps, enc_pre)
    saves[3].start()
    greet((("task", tasks), ("batch", batches)))
    totals = total(0, sums)
    put_sums(enc_totals, totals)
    scale = rows_of(scales, 0, 2)

    def peer_of(step, incoming):
        return lax.rem(task + (tasks - step if incoming else step), tasks)

    def pool_copy(i, step, incoming=False):
        rows = window_rows(i, windows)
        peer = peer_of(step, incoming)
        target = pooled_all.at[rows, columns_of(peer if incoming else task, width)]
        return remote(
            pooled.at[rows, :], target, pool_sends.at[i, step], pool_receives.at[i, step], peer, "task"
        )

    def pool(i, rows, carry):
        valid = valid_rows(small[i], height, breadth)
        _, _, scaled = norm_with(enc_pre[rows, :], totals, scale)
        high, low = split(silu(scaled) * valid)
        mean = ((dot(narrow, high) + dot(narrow, low)) * 0.25).astype(BF)
        here = window_rows(i, windows)
        pooled[here, :] = mean
        pooled_all[here, columns_of(task, width)] = mean
        for step in range(1, tasks):
            pool_copy(i, step).start()
        return carry

    each_image(geometry, pool, 0)

    def unpool(i, rows, carry):
        for step in range(1, tasks):
            pool_copy(i, step, True).wait_recv()
        wide = dot(widen, pooled_all[window_rows(i, windows), :])
        spread[rows, :] = (wide * choose[rows, :]).astype(BF)
        return carry

    each_image(geometry, unpool, 0)
    saves[5].start()
    sums = conv(spread, dec_taps, dec_pre)
    saves[4].start()
    totals = total(1, sums)
    put_sums(dec_totals, totals)
    scale = rows_of(scales, 2, 2)

    def feature_copy(i, rows, step, incoming=False):
        peer = peer_of(step, incoming)
        target = features.at[rows, columns_of(peer if incoming else task, width)]
        return remote(
            part.at[rows, :], target, sends.at[i, step], receives.at[i, step], peer, "task"
        )

    def finish(i, rows, carry):
        valid = valid_rows(small[i], height, breadth)
        _, _, scaled = norm_with(dec_pre[rows, :], totals, scale)
        low = (silu(scaled) * valid).astype(BF)
        part[rows, :] = low
        features[rows, columns_of(task, width)] = low
        for step in range(1, tasks):
            feature_copy(i, rows, step).start()
        return carry

    each_image(geometry, finish, 0)

    def settle(i, rows, carry):
        for step in range(1, tasks):
            feature_copy(i, rows, step, True).wait_recv()
            feature_copy(i, rows, step).wait_send()
            pool_copy(i, step).wait_send()
        return carry

    each_image(geometry, settle, 0)
    for copy in saves:
        copy.wait()


def trunk_forward(geometry, tasks, batches, small, x, enc_taps, dec_taps, scales, choose):
    number, height, breadth = geometry
    pixels = height * breadth
    channels = x.shape[1]
    width = channels // tasks
    windows = window_count(height, breadth)
    tall = shape((x.shape[0], width), F32)
    outs = [
        shape((8, width), F32), shape((8, width), F32), shape(x.shape, BF),
        shape(x.shape, BF), shape(enc_taps.shape, BF), shape(dec_taps.shape, BF),
        tall, tall, shape(x.shape, BF),
    ]
    return exchange_kernel(
        functools.partial(trunk_forward_body, geometry, tasks, batches),
        outs,
        "svvvvv",
        (small, x, enc_taps, dec_taps, scales, choose),
        [
            pltpu.VMEM(tall.shape, F32),
            pltpu.VMEM(tall.shape, F32),
            pltpu.VMEM(x.shape, BF),
            pltpu.VMEM((pixels, 9 * width), F32),
            pltpu.VMEM((number * windows, width), BF),
            pltpu.VMEM((number * windows, channels), BF),
            pltpu.VMEM((x.shape[0], width), BF),
        ]
        + [pltpu.SemaphoreType.DMA((number, tasks))] * 4
        + total_scratch(2, batches)
        + [pltpu.SemaphoreType.DMA((6,))],
        1,
        32,
        flops=4 * x.size * enc_taps.shape[1],
        places_out="vvvhhhhhh",
    )


def head_body(
    geometry, tasks, batches,
    small, features, rows_in, cotangent, scales, counts,
    task_out, grads, upstream, norm_sums,
    pre_one, pre_two, pre_three, hidden, gated, nine, work, lower, out, arrived, sends, receives,
    mine, slots, total_sends, total_receives,
):
    number, height, breadth = geometry
    channels = features.shape[1]
    width = channels // tasks
    windows = task_out.shape[1]
    task = lax.axis_index("task")
    half = work.shape[2]
    _, col = places(height, breadth)
    widen = pool_choice(height, breadth, windows, False).astype(BF)
    narrow = pool_choice(height, breadth, windows, True).astype(BF)
    count = jnp.broadcast_to(counts[2:3, 0:1], (1, channels))
    first = rows_in.at[pl.ds(0, channels), :]
    second = rows_in.at[pl.ds(channels, channels), :]

    def kernel_rows(p):
        return pl.ds((2 + p) * channels, channels)

    def total(k, rows):
        return total_rows(
            k, "batch", batches, list(rows), mine, slots, total_sends, total_receives
        )

    def put_stats(pre, rows, value, valid, carry):
        pre[rows, :] = value
        kept = value * valid
        return carry[0] + col_sum(kept), carry[1] + col_sum(kept * value)

    nothing = zero_rows(2, channels)
    scale_one, scale_two, scale_three = (rows_of(scales, 2 * k, 2) for k in range(3))

    def first_step(i, rows, carry):
        valid = valid_rows(small[i], height, breadth)
        return put_stats(pre_one, rows, dot(features[rows, :], first[...]), valid, carry)

    sums = each_image(geometry, first_step, nothing)
    greet((("task", tasks), ("batch", batches)))
    totals_one = total(0, sums) + [count]

    def second_step(i, rows, carry):
        valid = valid_rows(small[i], height, breadth)
        _, _, scaled = norm_with(pre_one[rows, :], totals_one, scale_one)
        low = (silu(scaled) * valid).astype(BF)
        hidden[rows, :] = low
        return put_stats(pre_two, rows, dot(low, second[...]), valid, carry)

    sums = each_image(geometry, second_step, nothing)
    totals_two = total(1, sums) + [count]

    def third_step(i, rows, carry):
        valid = valid_rows(small[i], height, breadth)
        _, _, scaled = norm_with(pre_two[rows, :], totals_two, scale_two)
        low = (jax.nn.sigmoid(scaled) * features[rows, :].astype(F32)).astype(BF)
        gated[rows, :] = low
        parts = []
        for j in range(channels // half):
            cut = slice(j * half, (j + 1) * half)
            for p in range(9):
                work[p] = dot(low, rows_in[kernel_rows(p), cut])
            parts.append(gather_taps(lambda p: work[p], breadth, col))
        return put_stats(pre_three, rows, jnp.concatenate(parts, axis=1), valid, carry)

    sums = each_image(geometry, third_step, nothing)
    totals_three = total(2, sums) + [count]

    def out_step(i, rows, carry):
        valid = valid_rows(small[i], height, breadth)
        normal, _, scaled = norm_with(pre_three[rows, :], totals_three, scale_three)
        high, low = split(silu(scaled) * valid)
        mean = (dot(narrow, high) + dot(narrow, low)) * 0.25
        task_out[i] = mean.astype(BF)
        dy = silu_back(scaled) * dot(widen, cotangent[i]) * 0.25 * valid
        lower[rows, :] = dy
        return carry[0] + col_sum(dy), carry[1] + col_sum(dy * normal)

    sums = each_image(geometry, out_step, nothing)
    sums_three = total(3, sums)

    def third_back(i, rows, carry):
        valid = valid_rows(small[i], height, breadth)
        normal, inverse, _ = norm_with(pre_three[rows, :], totals_three, scale_three)
        dz = norm_back_with(lower[rows, :], normal, inverse, count, sums_three, scale_three, valid)
        for p, moved in enumerate(spread_taps(dz, breadth, col)):
            nine[p, rows, :] = moved.astype(BF)
        flow = None
        for p in range(9):
            piece = dot_nt(nine[p, rows, :], rows_in[kernel_rows(p), :])
            flow = piece if flow is None else flow + piece
        lower[rows, :] = flow
        normal, _, scaled = norm_with(pre_two[rows, :], totals_two, scale_two)
        gate = jax.nn.sigmoid(scaled)
        dy = flow * features[rows, :].astype(F32) * gate * (1.0 - gate) * valid
        pre_three[rows, :] = dy
        return carry[0] + col_sum(dy), carry[1] + col_sum(dy * normal)

    sums = each_image(geometry, third_back, nothing)
    sums_two = total(4, sums)

    def second_back(i, rows, carry):
        valid = valid_rows(small[i], height, breadth)
        normal, inverse, scaled = norm_with(pre_two[rows, :], totals_two, scale_two)
        dz = norm_back_with(
            pre_three[rows, :], normal, inverse, count, sums_two, scale_two, valid
        ).astype(BF)
        out[rows, :] = dz
        lower[rows, :] = lower[rows, :] * jax.nn.sigmoid(scaled)
        normal, _, scaled = norm_with(pre_one[rows, :], totals_one, scale_one)
        dy = silu_back(scaled) * dot_nt(dz, second[...]) * valid
        pre_three[rows, :] = dy
        return carry[0] + col_sum(dy), carry[1] + col_sum(dy * normal)

    sums = each_image(geometry, second_back, nothing)
    sums_one = total(5, sums)
    grads[pl.ds(channels, channels), :] = dot_tn(hidden[...], out[...]).astype(BF)

    def flow_copy(i, rows, step, incoming=False):
        peer = lax.rem(task + (tasks - step if incoming else step), tasks)
        return remote(
            out.at[rows, columns_of(peer, width)], arrived.at[step - 1, rows, :],
            sends.at[i, step], receives.at[i, step], peer, "task",
        )

    def first_back(i, rows, carry):
        valid = valid_rows(small[i], height, breadth)
        normal, inverse, _ = norm_with(pre_one[rows, :], totals_one, scale_one)
        dz = norm_back_with(
            pre_three[rows, :], normal, inverse, count, sums_one, scale_one, valid
        ).astype(BF)
        hidden[rows, :] = dz
        flow = (lower[rows, :] + dot_nt(dz, first[...])) * valid
        out[rows, :] = flow.astype(BF)
        for step in range(1, tasks):
            flow_copy(i, rows, step).start()
        return carry

    each_image(geometry, first_back, 0)
    grads[pl.ds(0, channels), :] = dot_tn(features[...], hidden[...]).astype(BF)

    def tap(p, carry):
        rows = pl.ds(pl.multiple_of((2 + p) * channels, channels), channels)
        grads[rows, :] = dot_tn(gated[...], nine[p]).astype(BF)
        return carry

    lax.fori_loop(0, 9, tap, 0)
    put_sums(norm_sums, sums_one + sums_two + sums_three)

    def settle(i, rows, carry):
        for step in range(1, tasks):
            flow_copy(i, rows, step, True).wait_recv()
        flow = out[rows, columns_of(task, width)].astype(F32)
        for step in range(1, tasks):
            flow = flow + arrived[step - 1, rows, :].astype(F32)
        upstream[rows, :] = flow
        for step in range(1, tasks):
            flow_copy(i, rows, step).wait_send()
        return carry

    each_image(geometry, settle, 0)


def head(geometry, tasks, batches, small, features, rows_in, cotangent, scales, counts):
    number, height, breadth = geometry
    pixels = height * breadth
    total, channels = features.shape
    width = channels // tasks
    return exchange_kernel(
        functools.partial(head_body, geometry, tasks, batches),
        [
            shape((number, pixels // 4, channels), BF),
            shape(rows_in.shape, BF),
            shape((total, width), F32),
            shape((8, channels), F32),
        ],
        "svvvvv",
        (small, features, rows_in, cotangent, scales, counts),
        [
            pltpu.VMEM(features.shape, F32),
            pltpu.VMEM(features.shape, F32),
            pltpu.VMEM(features.shape, F32),
            pltpu.VMEM(features.shape, BF),
            pltpu.VMEM(features.shape, BF),
            pltpu.VMEM((9,) + features.shape, BF),
            pltpu.VMEM((9, pixels, min(channels, 256)), F32),
            pltpu.VMEM(features.shape, F32),
            pltpu.VMEM(features.shape, BF),
            pltpu.VMEM((tasks - 1, total, width), BF),
        ]
        + [pltpu.SemaphoreType.DMA((number, tasks))] * 2
        + total_scratch(6, batches),
        2,
        60,
        flops=6 * total * channels * rows_in.shape[0],
    )


def trunk_backward_body(
    geometry, tasks, batches,
    small, upstream, enc_totals, dec_totals, scales, choose_row, *rest,
):
    kept, (enc_grad, dec_grad, flow_out, norm_sums), rest = rest[:6], rest[6:10], rest[10:]
    (x, enc_taps, dec_taps, enc_pre, dec_pre, spread), rest = rest[:6], rest[6:]
    (
        nine, change, packed, arrived, pooled, sends, receives,
        mine, slots, total_sends, total_receives, loaded,
    ) = rest
    targets = (x, enc_taps, dec_taps, enc_pre, dec_pre, spread)
    loads = [pltpu.make_async_copy(a, b, loaded.at[k]) for k, (a, b) in enumerate(zip(kept, targets))]
    for k in (4, 2, 5, 3, 1, 0):
        loads[k].start()
    number, height, breadth = geometry
    channels = x.shape[1]
    width = enc_pre.shape[1]
    windows = window_count(height, breadth)
    task = lax.axis_index("task")
    _, col = places(height, breadth)
    widen = pool_choice(height, breadth, windows, False).astype(BF)
    narrow = pool_choice(height, breadth, windows, True)
    nothing = zero_rows(2, width)

    def total(k, rows):
        return total_rows(
            k, "batch", batches, list(rows), mine, slots, total_sends, total_receives
        )

    def change_of(pre, totals, scale, flow):
        def image(i, rows, carry):
            valid = valid_rows(small[i], height, breadth)
            normal, _, scaled = norm_with(pre[rows, :], totals, scale)
            dy = silu_back(scaled) * flow(i, rows) * valid
            change[rows, :] = dy
            return carry[0] + col_sum(dy), carry[1] + col_sum(dy * normal)

        return each_image(geometry, image, nothing)

    def back(pre, totals, scale, sums, taps, put):
        def image(i, rows, carry):
            valid = valid_rows(small[i], height, breadth)
            normal, inverse, _ = norm_with(pre[rows, :], totals, scale)
            dz = norm_back_with(change[rows, :], normal, inverse, totals[2], sums, scale, valid)
            for p, moved in enumerate(spread_taps(dz, breadth, col)):
                nine[rows, p * width : (p + 1) * width] = moved.astype(BF)
            put(i, rows, dot_nt(nine[rows, :], taps[...]) * valid)
            return carry

        each_image(geometry, image, 0)

    totals = rows_of(dec_totals, 0, 3)
    scale = rows_of(scales, 2, 2)
    loads[4].wait()
    sums = change_of(dec_pre, totals, scale, lambda i, rows: upstream[rows, :])
    greet((("task", tasks), ("batch", batches)))
    dec_sums = total(0, sums)

    def copy_of(i, step, incoming=False):
        rows = window_rows(i, windows)
        peer = lax.rem(task + (tasks - step if incoming else step), tasks)
        return remote(
            packed.at[rows, columns_of(peer, width)], arrived.at[step - 1, rows, :],
            sends.at[i, step], receives.at[i, step], peer, "task",
        )

    def put_packed(i, rows, flow):
        chosen = (narrow * choose_row[i]).astype(BF)
        packed[window_rows(i, windows), :] = dot(chosen, flow.astype(BF)).astype(BF)
        for step in range(1, tasks):
            copy_of(i, step).start()

    loads[2].wait()
    back(dec_pre, totals, scale, dec_sums, dec_taps, put_packed)
    loads[5].wait()
    dec_grad[...] = dot_tn(spread[...], nine[...])

    def collect(i, carry):
        for step in range(1, tasks):
            copy_of(i, step, True).wait_recv()
        rows = window_rows(i, windows)
        flow = packed[rows, columns_of(task, width)].astype(F32)
        for step in range(1, tasks):
            flow = flow + arrived[step - 1, rows, :].astype(F32)
        pooled[rows, :] = flow
        for step in range(1, tasks):
            copy_of(i, step).wait_send()
        return carry

    lax.fori_loop(0, number, collect, 0)

    def widened(i, rows):
        high, low = split(pooled[window_rows(i, windows), :])
        return (dot(widen, high) + dot(widen, low)) * 0.25

    totals = rows_of(enc_totals, 0, 3)
    scale = rows_of(scales, 0, 2)
    loads[3].wait()
    sums = change_of(enc_pre, totals, scale, widened)
    enc_sums = total(1, sums)

    def put_flow(i, rows, flow):
        flow_out[rows, :] = flow.astype(BF)

    loads[1].wait()
    back(enc_pre, totals, scale, enc_sums, enc_taps, put_flow)
    loads[0].wait()
    enc_grad[...] = dot_tn(x[...], nine[...])
    put_sums(norm_sums, enc_sums + dec_sums)


def trunk_backward(
    geometry, tasks, batches, small, upstream, enc_totals, dec_totals, scales, choose_row, kept
):
    number, height, breadth = geometry
    x, enc_taps, dec_taps = kept[:3]
    total, channels = x.shape
    width = channels // tasks
    windows = window_count(height, breadth)
    return exchange_kernel(
        functools.partial(trunk_backward_body, geometry, tasks, batches),
        [
            shape(enc_taps.shape, F32),
            shape(dec_taps.shape, F32),
            shape(x.shape, BF),
            shape((8, width), F32),
        ],
        "svvvvvhhhhhh",
        (small, upstream, enc_totals, dec_totals, scales, choose_row, *kept),
        [pltpu.VMEM(a.shape, a.dtype) for a in kept]
        + [
            pltpu.VMEM((total, 9 * width), BF),
            pltpu.VMEM((total, width), F32),
            pltpu.VMEM((number * windows, channels), BF),
            pltpu.VMEM((tasks - 1, number * windows, width), BF),
            pltpu.VMEM((number * windows, width), F32),
        ]
        + [pltpu.SemaphoreType.DMA((number, tasks))] * 2
        + total_scratch(2, batches)
        + [pltpu.SemaphoreType.DMA((6,))],
        3,
        40,
        flops=8 * x.size * enc_taps.shape[1],
    )


def exchange(body, outs, args, scratch, identity, vmem=32):
    size = sum(o.size * o.dtype.itemsize for o in outs) + sum(a.size * a.dtype.itemsize for a in args)
    return pl.pallas_call(
        body,
        out_shape=tuple(outs),
        in_specs=[VMEM_SPEC] * len(args),
        out_specs=tuple(VMEM_SPEC for _ in outs),
        scratch_shapes=list(scratch),
        compiler_params=pltpu.CompilerParams(
            vmem_limit_bytes=vmem * MIB, collective_id=identity, has_side_effects=True
        ),
        cost_estimate=pl.CostEstimate(flops=0, bytes_accessed=size, transcendentals=0),
    )(*args)


def block_of(ref, place, size, dim):
    length = ref.shape[dim] // size
    start = place * length
    if dim == 0:
        return ref.at[pl.ds(pl.multiple_of(start, 8), length), :]
    return ref.at[:, pl.ds(pl.multiple_of(start, 128), length)]


def gather_body(axis, size, dims, *refs):
    count = len(dims)
    sources, targets = refs[:count], refs[count : 2 * count]
    sends, receives, own = refs[2 * count :]
    greet(((axis, size),))
    me = lax.axis_index(axis)
    copies = []
    for k in range(count):
        mine = block_of(targets[k], me, size, dims[k])
        for step in range(1, size):
            peer = lax.rem(me + step, size)
            copy = remote(sources[k], mine, sends.at[k, step], receives.at[k, me], peer, axis)
            copy.start()
            copies.append(copy)
    locals_ = []
    for k in range(count):
        mine = block_of(targets[k], me, size, dims[k])
        copy = pltpu.make_async_copy(sources[k], mine, own.at[k])
        copy.start()
        locals_.append(copy)
    for copy in locals_:
        copy.wait()
    for k in range(count):
        for step in range(1, size):
            peer = lax.rem(me + size - step, size)
            theirs = block_of(targets[k], peer, size, dims[k])
            remote(
                sources[k], theirs, sends.at[k, step], receives.at[k, peer], peer, axis
            ).wait_recv()
    for copy in copies:
        copy.wait_send()


def gather_over(axis, size, arrays, dims, identity):
    outs = []
    for x, dim in zip(arrays, dims):
        full = list(x.shape)
        full[dim] *= size
        outs.append(shape(full, x.dtype))
    count = len(arrays)
    return exchange(
        functools.partial(gather_body, axis, size, tuple(dims)),
        outs,
        arrays,
        [
            pltpu.SemaphoreType.DMA((count, size)),
            pltpu.SemaphoreType.DMA((count, size)),
            pltpu.SemaphoreType.DMA((count,)),
        ],
        identity,
    )


def to_taps_body(index, slots, enc, dec, owner, wide, tap):
    count = slots.shape[0]
    channels = enc.shape[0]
    width = slots.shape[1]
    step = 1024

    def widen(i, carry):
        rows = pl.ds(pl.multiple_of(i * step, step), step)
        wide[rows, :] = slots[rows, :].astype(F32)
        return carry

    lax.fori_loop(0, count // step, widen, 0)
    group = 32
    for p in range(18):

        def fetch(i, carry):
            base = i * group
            for u in range(group):
                slot = index[p * channels + base + u]
                tap[pl.ds(base + u, 1), :] = wide[pl.ds(slot, 1), :]
                owner[slot] = p // 9
            return carry

        lax.fori_loop(0, channels // group, fetch, 0)
        out = enc if p < 9 else dec
        q = p % 9
        out[:, q * width : (q + 1) * width] = tap[...].astype(BF)


def to_taps(index, slots, channels):
    width = slots.shape[1]
    taps = shape((channels, 9 * width), BF)
    return pl.pallas_call(
        to_taps_body,
        out_shape=(taps, taps, shape(index.shape, jnp.int32)),
        in_specs=[SMEM_SPEC, VMEM_SPEC],
        out_specs=(VMEM_SPEC, VMEM_SPEC, SMEM_SPEC),
        scratch_shapes=[pltpu.VMEM(slots.shape, F32), pltpu.VMEM((channels, width), F32)],
        compiler_params=pltpu.CompilerParams(vmem_limit_bytes=24 * MIB),
        cost_estimate=pl.CostEstimate(flops=10000 * MIB, bytes_accessed=8 * MIB, transcendentals=0),
    )(index, slots)


def to_slots_body(index, enc, dec, slots, wide):
    count = slots.shape[0]
    channels = enc.shape[0]
    width = slots.shape[1]
    step = 1024
    group = 32
    for p in range(18):
        source = enc if p < 9 else dec
        q = p % 9

        def place(i, carry):
            base = pl.multiple_of(i * group, group)
            values = source[pl.ds(base, group), q * width : (q + 1) * width]
            for u in range(group):
                wide[pl.ds(index[p * channels + base + u], 1), :] = values[u : u + 1, :]
            return carry

        lax.fori_loop(0, channels // group, place, 0)

    def narrow(i, carry):
        rows = pl.ds(pl.multiple_of(i * step, step), step)
        slots[rows, :] = wide[rows, :].astype(BF)
        return carry

    lax.fori_loop(0, count // step, narrow, 0)


def to_slots(index, enc, dec):
    width = enc.shape[1] // 9
    dims = (index.shape[0], width)
    return run(
        to_slots_body, [shape(dims, BF)], "svv", (index, enc, dec), [pltpu.VMEM(dims, F32)], vmem=24
    )[0]


def adam(gradient, moment_one, moment_two):
    new_one = BETA_ONE * moment_one + (1.0 - BETA_ONE) * gradient
    new_two = BETA_TWO * moment_two + (1.0 - BETA_TWO) * gradient * gradient
    direction = (
        new_one / (1.0 - BETA_ONE**STEP) / (jnp.sqrt(new_two / (1.0 - BETA_TWO**STEP)) + ADAM_EPS)
    )
    return new_one, new_two, direction


def pair_place(batches):
    me = lax.axis_index("batch")
    place = lax.div(me, 2)
    return place, me - 2 * place, batches // 2


def greet_pairs(tasks, batches):
    place, core, chips = pair_place(batches)
    task = lax.axis_index("task")
    barrier = pltpu.get_barrier_semaphore()

    def signal(device):
        pl.semaphore_signal(barrier, inc=1, device_id=device, device_id_type=MESH)

    for step in range(1, tasks):
        signal({"task": lax.rem(task + step, tasks)})
    signal({"batch": 2 * place + 1 - core})
    for step in range(1, chips):
        signal({"batch": 2 * lax.rem(place + step, chips) + core})
    pl.semaphore_wait(barrier, tasks - 1 + chips)


def block_rows(ref, index, count):
    return ref.at[pl.ds(pl.multiple_of(index * count, 8), count), :]


def far_first(chips):
    return sorted(range(chips), key=lambda step: -min(step, chips - step))


def pair_sum(batches, source, near, paired, far, sems):
    place, core, chips = pair_place(batches)
    count = near.shape[1]
    near_send, near_receive, far_send, far_receive = sems
    other = 2 * place + 1 - core

    def near_copy(step):
        chip = lax.rem(place + step, chips)
        return remote(block_rows(source, 2 * chip + 1 - core, count), near.at[step],
                      near_send.at[step], near_receive.at[step], other, "batch")

    def far_copy(step, incoming=False):
        chip = lax.rem(place + (chips - step if incoming else step), chips)
        return remote(paired.at[step], far.at[step], far_send.at[step], far_receive.at[step],
                      2 * chip + core, "batch")

    for step in far_first(chips):
        near_copy(step).start()

    def middle():
        for step in far_first(chips):
            chip = lax.rem(place + step, chips)
            near_copy(step).wait_recv()
            if step:
                total = block_rows(source, 2 * chip + core, count)[...].astype(F32)
                paired[step] = (total + near[step].astype(F32)).astype(paired.dtype)
                far_copy(step).start()

    def end():
        total = block_rows(source, 2 * place + core, count)[...].astype(F32)
        total = total + near[0].astype(F32)
        for step in range(1, chips):
            far_copy(step, True).wait_recv()
            total = total + far[step].astype(F32)
        for step in range(chips):
            near_copy(step).wait_send()
            if step:
                far_copy(step).wait_send()
        return total

    return middle, end


def pair_scratch(batches, rows, width, kind):
    chips = batches // 2
    return [pltpu.VMEM((chips, rows // batches, width), kind)] * 3 + [
        pltpu.SemaphoreType.DMA((chips,))
    ] * 4


def collect_body(
    tasks, batches,
    slots, flow, sums,
    input_grad, owned, part, norm_sums,
    near, paired, far, near_send, near_receive, far_send, far_receive,
    flow_in, flow_send, flow_receive, send, receive, sum_send, sum_receive,
):
    task = lax.axis_index("task")
    width = part.shape[1]
    pixels = input_grad.shape[0]

    def peer_of(step, incoming):
        return lax.rem(task + (tasks - step if incoming else step), tasks)

    def flow_copy(step, incoming=False):
        peer = peer_of(step, incoming)
        return remote(block_rows(flow, peer, pixels), flow_in.at[step - 1], flow_send.at[step],
                      flow_receive.at[step], peer, "task")

    def sum_copy(step, incoming=False):
        peer = peer_of(step, incoming)
        home = peer if incoming else task
        return remote(sums, norm_sums.at[:, columns_of(home, width)], sum_send.at[step],
                      sum_receive.at[step], peer, "task")

    def part_copy(step, incoming=False):
        peer = peer_of(step, incoming)
        home = peer if incoming else task
        return remote(part, owned.at[:, columns_of(home, width)], send.at[step], receive.at[step],
                      peer, "task")

    greet_pairs(tasks, batches)
    middle, end = pair_sum(
        batches, slots, near, paired, far, (near_send, near_receive, far_send, far_receive)
    )
    for step in range(1, tasks):
        sum_copy(step).start()
        flow_copy(step).start()
    norm_sums[:, columns_of(task, width)] = sums[...]
    middle()
    total = end().astype(BF)
    part[...] = total
    for step in range(1, tasks):
        part_copy(step).start()
    owned[:, columns_of(task, width)] = total
    total = block_rows(flow, task, pixels)[...].astype(F32)
    for step in range(1, tasks):
        flow_copy(step, True).wait_recv()
        total = total + flow_in[step - 1].astype(F32)
    input_grad[...] = total
    for step in range(1, tasks):
        sum_copy(step, True).wait_recv()
        part_copy(step, True).wait_recv()
        sum_copy(step).wait_send()
        part_copy(step).wait_send()
        flow_copy(step).wait_send()


def collect(tasks, batches, slots, flow, sums):
    count, width = slots.shape
    rows = count // batches
    pixels, channels = flow.shape[0] // tasks, flow.shape[1]
    return exchange_kernel(
        functools.partial(collect_body, tasks, batches),
        [
            shape((pixels, channels), F32),
            shape((rows, channels), BF),
            shape((rows, width), BF),
            shape((8, channels), F32),
        ],
        "vvv",
        (slots, flow, sums),
        pair_scratch(batches, count, width, BF)
        + [pltpu.VMEM((tasks - 1, pixels, channels), BF)]
        + [pltpu.SemaphoreType.DMA((tasks,))] * 6,
        5,
        24,
        flops=20000 * MIB,
    )


def soap_rows(cuts, grad, owners, state, low, first):
    count = owners.shape[1]
    total = grad.shape[0]

    def chunk(i, carry):
        rows = pl.ds(pl.multiple_of(i * (total // cuts), 8), total // cuts)
        values = grad[rows, :].astype(F32)
        rotated = None
        for m in range(count):
            part = dot((values * owners[rows, m : m + 1]).astype(BF), low[first + m])
            rotated = part if rotated is None else rotated + part
        new_one, new_two, direction = adam(rotated, state[1, rows, :], state[2, rows, :])
        state[1, rows, :] = new_one
        state[2, rows, :] = new_two
        stepped = None
        for m in range(count):
            part = dot_nt((direction * owners[rows, m : m + 1]).astype(BF), low[first + m])
            stepped = part if stepped is None else stepped + part
        old = state[0, rows, :]
        state[0, rows, :] = old - LEARN_MATRIX * (stepped + DECAY_MATRIX * old)
        return carry

    lax.fori_loop(0, cuts, chunk, 0)


def factor_rows(values, identity, turn):
    size, width = values.shape
    sub = lax.broadcasted_iota(jnp.int32, (size, width), 0)
    rolled = pltpu.roll(values, turn, 1)
    columns = [jnp.broadcast_to(rolled[:, j : j + 1], (size, width)) for j in range(size)]
    scale = jnp.zeros((size, width), F32)
    for j in range(size):
        root = lax.rsqrt(columns[j][j : j + 1, :])
        scale = jnp.where(sub == j, root, scale)
        lower = jnp.where(sub > j, columns[j] * root, 0.0)
        values = values - lower * (values[j : j + 1, :] * root)
        identity = identity - lower * (identity[j : j + 1, :] * root)
        for i in range(j + 1, size):
            columns[i] = columns[i] - lower * (columns[i][j : j + 1, :] * root)
    return values * scale, identity * scale


GROUP = 16
PANEL = 128


def renew_panel(k, product, made, tables, inverses):
    count, size = product.shape[0], product.shape[1]
    here = slice(k * PANEL, (k + 1) * PANEL)
    row = lax.broadcasted_iota(jnp.int32, (PANEL, PANEL), 0)
    col = lax.broadcasted_iota(jnp.int32, (PANEL, PANEL), 1)
    unit = jnp.where(row == col, 1.0, 0.0).astype(F32)
    for n in range(count):
        tables[n][:, :PANEL] = dot3(dot_tn, product[n, :, here], product[n, :, here])
        tables[n][:, PANEL:] = unit

    def group(q, carry):
        rows = pl.ds(pl.multiple_of(q * GROUP, GROUP), GROUP)
        turn = lax.rem(PANEL - q * GROUP, PANEL)
        done = [
            factor_rows(tables[n][rows, :PANEL], tables[n][rows, PANEL:], turn)
            for n in range(count)
        ]
        for n in range(count):
            upper, inverse = done[n]
            inverses[n][rows, :] = inverse
            both = jnp.concatenate([upper, inverse], axis=1)
            tables[n][...] = tables[n][...] - dot3(dot_tn, upper, both)
        return carry

    lax.fori_loop(0, PANEL // GROUP, group, 0)
    for n in range(count):
        turned = dot3(dot_nt, product[n, :, here], inverses[n][...])
        made[n, :, here] = turned
        if k < size // PANEL - 1:
            rest = slice((k + 1) * PANEL, size)
            product[n, :, rest] = product[n, :, rest] - dot3(
                dot, turned, dot3(dot_tn, turned, product[n, :, rest])
            )


def finish_body(
    tasks, batches, cuts,
    grad, part, owners, head_grad, head_owners,
    weight, one, two, head_weight, head_one, head_two, stat, head_stat, basis, head_basis,
    weight_new, one_new, two_new, head_weight_new, head_one_new, head_two_new,
    stat_new, head_stat_new, basis_new, head_basis_new,
    grams, head_grams, mine, head_mine,
    state, head_state, stats, bases, low, product, made, theirs,
    table_one, table_two, table_three, inverse_one, inverse_two, inverse_three,
    near, paired, far, near_send, near_receive, far_send, far_receive,
    head_near, head_paired, head_far, *rest,
):
    head_sems = rest[:4]
    chip_send, chip_receive, task_send, task_receive, pair_send, pair_receive = rest[4:10]
    panel_send, panel_receive, load, save = rest[10:]
    task = lax.axis_index("task")
    place, core, chips = pair_place(batches)
    width = part.shape[1]
    channels = grad.shape[1]
    count, head_count = near.shape[1], head_near.shape[1]
    trunk_total, head_total = owners.shape[1], head_owners.shape[1]

    moves = [
        (basis, bases.at[pl.ds(0, trunk_total)]),
        (head_basis, bases.at[pl.ds(trunk_total, head_total)]),
        (weight, state.at[0]),
        (one, state.at[1]),
        (two, state.at[2]),
        (head_weight, head_state.at[0]),
        (head_one, head_state.at[1]),
        (head_two, head_state.at[2]),
        (stat, stats.at[pl.ds(0, trunk_total)]),
        (head_stat, stats.at[pl.ds(trunk_total, head_total)]),
    ]
    loads = [pltpu.make_async_copy(a, b, load.at[k]) for k, (a, b) in enumerate(moves)]
    for copy in loads:
        copy.start()
    for m in range(head_total):
        held = (head_grad[...].astype(F32) * head_owners[:, m : m + 1]).astype(BF)
        head_mine[m * channels : (m + 1) * channels, :] = dot_tn(held, head_grad[...]).astype(
            head_mine.dtype
        )
    greet_pairs(tasks, batches)
    head_middle, head_end = pair_sum(
        batches, head_mine, head_near, head_paired, head_far, head_sems
    )
    for m in range(trunk_total):
        held = (grad[...].astype(F32) * owners[:, m : m + 1]).astype(BF)
        mine[m * channels : (m + 1) * channels, :] = dot_tn(held, part[...]).astype(mine.dtype)
    middle, end = pair_sum(
        batches, mine, near, paired, far, (near_send, near_receive, far_send, far_receive)
    )
    head_middle()
    middle()

    def trunk_block(chip, home, which):
        rows = pl.ds(pl.multiple_of((2 * chip + which) * count, 8), count)
        return grams.at[rows, columns_of(home, width)]

    def head_block(chip, which):
        return block_rows(head_grams, 2 * chip + which, head_count)

    def chip_copy(kind, step, incoming=False):
        peer = lax.rem(place + (chips - step if incoming else step), chips)
        home = peer if incoming else place
        block = head_block(home, core) if kind else trunk_block(home, task, core)
        return remote(block, block, chip_send.at[kind, step], chip_receive.at[kind, step],
                      2 * peer + core, "batch")

    def task_copy(step, hop, incoming=False):
        peer = lax.rem(task + (tasks - step if incoming else step), tasks)
        chip = lax.rem(place + chips - hop, chips)
        block = trunk_block(chip, peer if incoming else task, core)
        return remote(block, block, task_send.at[step, hop], task_receive.at[step, hop], peer, "task")

    def pair_copy(kind, hop, incoming=False):
        chip = lax.rem(place + chips - hop, chips)
        which = 1 - core if incoming else core
        home = lax.rem(task + tasks - kind, tasks)
        block = head_block(chip, which) if kind == tasks else trunk_block(chip, home, which)
        return remote(block, block, pair_send.at[kind, hop], pair_receive.at[kind, hop],
                      2 * place + 1 - core, "batch")

    for copy in loads[:5]:
        copy.wait()
    for m in range(trunk_total + head_total):
        low[m] = bases[m].astype(BF)
    total = end().astype(grams.dtype)
    trunk_block(place, task, core)[...] = total
    for step in range(1, chips):
        chip_copy(0, step).start()
    for step in range(1, tasks):
        task_copy(step, 0).start()
    pair_copy(0, 0).start()
    soap_rows(cuts, grad, owners, state, low, 0)
    saves = [
        pltpu.make_async_copy(state.at[k], out, save.at[k])
        for k, out in enumerate((weight_new, one_new, two_new))
    ]
    for copy in saves:
        copy.start()
    total = head_end().astype(head_grams.dtype)
    head_block(place, core)[...] = total
    for step in range(1, chips):
        chip_copy(1, step).start()
    pair_copy(tasks, 0).start()
    for hop in range(1, chips):
        chip_copy(0, hop, True).wait_recv()
        for step in range(1, tasks):
            task_copy(step, hop).start()
        pair_copy(0, hop).start()
    for copy in loads[5:]:
        copy.wait()
    soap_rows(cuts, head_grad, head_owners, head_state, low, trunk_total)
    for k, out in enumerate((head_weight_new, head_one_new, head_two_new)):
        copy = pltpu.make_async_copy(head_state.at[k], out, save.at[3 + k])
        copy.start()
        saves.append(copy)
    for hop in range(chips):
        for step in range(1, tasks):
            task_copy(step, hop, True).wait_recv()
            pair_copy(step, hop).start()
    for hop in range(1, chips):
        chip_copy(1, hop, True).wait_recv()
        pair_copy(tasks, hop).start()
    for hop in range(chips):
        for kind in range(tasks + 1):
            pair_copy(kind, hop, True).wait_recv()

    for m in range(trunk_total + head_total):
        first = m < trunk_total
        start = (m if first else m - trunk_total) * channels
        gram = (grams if first else head_grams)[start : start + channels, :]
        stats[m] = STAT_DECAY * stats[m] + (1.0 - STAT_DECAY) * gram.astype(F32)
    for k, (out, begin, size) in enumerate(
        ((stat_new, 0, trunk_total), (head_stat_new, trunk_total, head_total))
    ):
        copy = pltpu.make_async_copy(stats.at[pl.ds(begin, size)], out, save.at[6 + k])
        copy.start()
        saves.append(copy)
    for n in range(head_total):
        chosen = trunk_total * core + n
        product[n] = dot3(dot, stats[chosen], bases[chosen])
    panels = channels // PANEL

    def panel_copy(k):
        cut = pl.ds(k * PANEL, PANEL)
        return remote(made.at[:, :, cut], theirs.at[:, :, cut], panel_send.at[k],
                      panel_receive.at[k], 2 * place + 1 - core, "batch")

    for k in range(panels):
        renew_panel(
            k, product, made, (table_one, table_two, table_three),
            (inverse_one, inverse_two, inverse_three),
        )
        panel_copy(k).start()
    for k in range(panels):
        panel_copy(k).wait_recv()

    def put_bases(trunk_from, head_from):
        copies = [
            pltpu.make_async_copy(trunk_from.at[pl.ds(0, trunk_total)], basis_new, save.at[8]),
            pltpu.make_async_copy(head_from.at[pl.ds(0, head_total)], head_basis_new, save.at[9]),
        ]
        for copy in copies:
            copy.start()
        for copy in copies:
            copy.wait()

    @pl.when(core == 0)
    def _():
        put_bases(made, theirs)

    @pl.when(core == 1)
    def _():
        put_bases(theirs, made)

    for copy in saves:
        copy.wait()
    for k in range(panels):
        panel_copy(k).wait_send()
    for hop in range(chips):
        for kind in range(tasks + 1):
            pair_copy(kind, hop).wait_send()
        for step in range(1, tasks):
            task_copy(step, hop).wait_send()
        if hop:
            chip_copy(0, hop).wait_send()
            chip_copy(1, hop).wait_send()


def finish(tasks, batches, local_grads, rows, matrices):
    grad, part, owners, head_grad, head_owners = local_grads
    channels, width = grad.shape[1], part.shape[1]
    trunk_total, head_total = owners.shape[1], head_owners.shape[1]
    gram_rows, head_rows = trunk_total * channels, head_total * channels
    chips = batches // 2
    kind = BF if gram_rows % (16 * batches) == 0 else F32
    head_kind = BF if head_rows % (16 * batches) == 0 else F32
    cuts = 4 if grad.shape[0] % 64 == 0 and head_grad.shape[0] % 64 == 0 else 1
    square = (trunk_total + head_total, channels, channels)
    outs = [shape(a.shape, F32) for a in (*rows, *matrices)]
    hbm = pl.BlockSpec(memory_space=pltpu.HBM)
    args = (*local_grads, *rows, *matrices)
    return pl.pallas_call(
        functools.partial(finish_body, tasks, batches, cuts),
        out_shape=tuple(outs),
        in_specs=[VMEM_SPEC] * 5 + [hbm] * 10,
        out_specs=tuple(hbm for _ in outs),
        scratch_shapes=[
            pltpu.VMEM((gram_rows, channels), kind),
            pltpu.VMEM((head_rows, channels), head_kind),
            pltpu.VMEM((gram_rows, width), kind),
            pltpu.VMEM((head_rows, channels), head_kind),
            pltpu.VMEM((3,) + grad.shape, F32),
            pltpu.VMEM((3,) + head_grad.shape, F32),
            pltpu.VMEM(square, F32),
            pltpu.VMEM(square, F32),
            pltpu.VMEM(square, BF),
        ]
        + [pltpu.VMEM((head_total,) + square[1:], F32)] * 3
        + [pltpu.VMEM((PANEL, 2 * PANEL), F32)] * head_total
        + [pltpu.VMEM((PANEL, PANEL), F32)] * head_total
        + pair_scratch(batches, gram_rows, width, kind)
        + pair_scratch(batches, head_rows, channels, head_kind)
        + [pltpu.SemaphoreType.DMA((2, chips))] * 2
        + [pltpu.SemaphoreType.DMA((tasks, chips))] * 2
        + [pltpu.SemaphoreType.DMA((tasks + 1, chips))] * 2
        + [pltpu.SemaphoreType.DMA((channels // PANEL,))] * 2
        + [pltpu.SemaphoreType.DMA((10,))] * 2,
        compiler_params=pltpu.CompilerParams(
            vmem_limit_bytes=52 * MIB, collective_id=6, has_side_effects=True
        ),
        cost_estimate=pl.CostEstimate(
            flops=100000 * MIB, bytes_accessed=sum(4 * o.size for o in outs), transcendentals=0
        ),
    )(*args)


def local(
    tasks,
    batches,
    images,
    image_small,
    pool_index,
    row_slot,
    trunk_weight,
    trunk_mean_grad,
    trunk_mean_square,
    trunk_statistic,
    trunk_basis,
    head_weight,
    head_mean_grad,
    head_mean_square,
    head_statistic,
    head_basis,
    trunk_gain,
    trunk_offset,
    trunk_norm_mean_grad,
    trunk_norm_mean_square,
    head_gain,
    head_offset,
    head_norm_mean_grad,
    head_norm_mean_square,
    cotangent,
):
    number, height, breadth, channels = images.shape
    pixels = height * breadth
    tap_rows = 9 * channels
    shown = tasks * number
    geometry = (shown, height, breadth)
    task = lax.axis_index("task")
    batch = lax.axis_index("batch")
    width = channels // tasks

    def quarter(values):
        return lax.dynamic_slice_in_dim(values, task * width, width, values.ndim - 1)

    def inside(flags):
        row_limit = jnp.where(flags > 0, height // 2, height)[:, None, None]
        col_limit = jnp.where(flags > 0, breadth // 2, breadth)[:, None, None]
        return (jnp.arange(height, dtype=jnp.int32)[None, :, None] < row_limit) & (
            jnp.arange(breadth, dtype=jnp.int32)[None, None, :] < col_limit
        )

    slots = lax.all_gather(quarter(trunk_weight).astype(BF), "batch", axis=0, tiled=True)
    head_rows = lax.all_gather(head_weight.astype(BF), "batch", axis=1, tiled=True)[0]
    kinds = jnp.concatenate([image_small, pool_index.reshape(-1)])
    kinds = lax.all_gather(kinds, "task", axis=0, tiled=True).reshape(tasks, -1)
    small = kinds[:, :number].reshape(-1)
    cells = kinds[:, number:].reshape(shown, height // 2, 1, breadth // 2, 1)
    cell = 2 * jnp.arange(2, dtype=jnp.int32)[:, None, None] + jnp.arange(2, dtype=jnp.int32)
    choose = (cells == cell).reshape(shown, height, breadth) & inside(small)
    choose = choose.astype(F32)
    choose_row = choose.reshape(shown, 1, pixels)
    choose = choose.reshape(shown * pixels, 1)
    masked = (images * inside(image_small)[..., None].astype(BF)).reshape(number * pixels, channels)
    x = gather_over("task", tasks, (masked,), (0,), 4)[0]
    enc_taps, dec_taps, slot_owner = to_taps(row_slot, slots, channels)

    scales = quarter(jnp.stack([trunk_gain, trunk_offset], axis=1)).reshape(4, width)
    enc_totals, dec_totals, features, *kept = trunk_forward(
        geometry, tasks, batches, small, x, enc_taps, dec_taps, scales, choose
    )
    head_scales = jnp.stack([head_gain[0], head_offset[0]], axis=1).reshape(6, channels)
    pooled, head_grads, upstream, head_sums = head(
        geometry, tasks, batches, small, features, head_rows,
        cotangent.reshape(shown, pixels // 4, channels), head_scales, enc_totals,
    )
    task_features = pooled.reshape(cotangent.shape)
    head_owned = lax.psum_scatter(head_grads, "batch", scatter_dimension=0, tiled=True)
    enc_grad, dec_grad, flow, trunk_sums = trunk_backward(
        geometry, tasks, batches, small, upstream, enc_totals, dec_totals, scales, choose_row, kept
    )
    input_grad, trunk_owned, trunk_part, norm_sums = collect(
        tasks, batches, to_slots(row_slot, enc_grad, dec_grad), flow, trunk_sums
    )
    input_grad = input_grad.reshape(images.shape)

    head_local = head_weight.shape[1]
    head_ids = batch * head_local + jnp.arange(head_local, dtype=jnp.int32)
    head_owner = jnp.minimum(head_ids // channels, 2)
    head_onehot = (head_owner[:, None] == jnp.arange(3, dtype=jnp.int32)).astype(F32)
    local_rows = trunk_weight.shape[0]
    trunk_owner = lax.dynamic_slice_in_dim(slot_owner, batch * local_rows, local_rows)
    trunk_onehot = (trunk_owner[:, None] == jnp.arange(2, dtype=jnp.int32)).astype(F32)
    (
        trunk_weight_new, trunk_one_new, trunk_two_new,
        head_weight_new, head_one_new, head_two_new,
        trunk_stat_new, head_stat_new, trunk_basis_new, head_basis_new,
    ) = finish(
        tasks, batches,
        (trunk_owned, trunk_part, trunk_onehot, head_owned, head_onehot),
        (trunk_weight, trunk_mean_grad, trunk_mean_square,
         head_weight[0], head_mean_grad[0], head_mean_square[0]),
        (trunk_statistic, head_statistic[0], trunk_basis, head_basis[0]),
    )

    trunk_norm = jnp.stack([trunk_gain, trunk_offset], axis=1)
    trunk_norm_grad = norm_sums[:4].reshape(2, 2, channels)[:, ::-1]
    trunk_norm_one, trunk_norm_two, trunk_direction = adam(
        trunk_norm_grad, trunk_norm_mean_grad, trunk_norm_mean_square
    )
    head_norm = jnp.stack([head_gain, head_offset], axis=2)
    head_norm_grad = head_sums[:6].reshape(1, 3, 2, channels)[:, :, ::-1]
    head_norm_one, head_norm_two, head_direction = adam(
        head_norm_grad, head_norm_mean_grad, head_norm_mean_square
    )
    return (
        task_features,
        input_grad,
        trunk_weight_new,
        trunk_one_new,
        trunk_two_new,
        trunk_stat_new,
        trunk_basis_new,
        head_weight_new[None],
        head_one_new[None],
        head_two_new[None],
        head_stat_new[None],
        head_basis_new[None],
        trunk_norm - LEARN_NORM * trunk_direction,
        trunk_norm_one,
        trunk_norm_two,
        head_norm - LEARN_NORM * head_direction,
        head_norm_one,
        head_norm_two,
    )


def solution(mesh):
    placed = (
        P(("task", "batch"), None, None, None),
        P(("task", "batch")),
        P(("task", "batch"), None, None),
        P(),
        P("batch", None),
        P("batch", None),
        P("batch", None),
        P(),
        P(),
        P("task", "batch", None),
        P("task", "batch", None),
        P("task", "batch", None),
        P("task", None, None, None),
        P("task", None, None, None),
        P(),
        P(),
        P(),
        P(),
        P("task", None, None),
        P("task", None, None),
        P("task", None, None, None),
        P("task", None, None, None),
        P("task", None, "batch", None, None, None),
    )
    return jax.shard_map(
        functools.partial(local, mesh.shape["task"], mesh.shape["batch"]),
        mesh=mesh,
        in_specs=placed,
        out_specs=(
            P("task", None, "batch", None, None, None),
            P(("task", "batch"), None, None, None),
            P("batch", None),
            P("batch", None),
            P("batch", None),
            P(),
            P(),
            P("task", "batch", None),
            P("task", "batch", None),
            P("task", "batch", None),
            P("task", None, None, None),
            P("task", None, None, None),
            P(),
            P(),
            P(),
            P("task", None, None, None),
            P("task", None, None, None),
            P("task", None, None, None),
        ),
        check_vma=False,
    )
```

```python
import functools

import jax
import jax.numpy as jnp
from jax import lax
from jax.experimental import pallas as pl
from jax.experimental.pallas import tpu as pltpu
from jax.sharding import PartitionSpec as P

STEP = 10


EPS = 1e-05
ADAM_EPS = 1e-08
BETA_ONE = 0.95
BETA_TWO = 0.95
STAT_DECAY = 0.95
LEARN_MATRIX = 0.02
LEARN_NORM = 0.5
DECAY_MATRIX = 0.01
BF = jnp.bfloat16
F32 = jnp.float32
MESH = pl.DeviceIdType.MESH
MIB = 1 << 20

VMEM_SPEC = pl.BlockSpec(memory_space=pltpu.VMEM)
SMEM_SPEC = pl.BlockSpec(memory_space=pltpu.SMEM)


def run(body, outs, specs, args, scratch=(), vmem=40, flops=0):
    size = sum(o.size * o.dtype.itemsize for o in outs) + sum(a.size * a.dtype.itemsize for a in args)
    return pl.pallas_call(
        body,
        out_shape=tuple(outs),
        in_specs=[SMEM_SPEC if s == "s" else VMEM_SPEC for s in specs],
        out_specs=tuple(VMEM_SPEC for _ in outs),
        scratch_shapes=list(scratch),
        compiler_params=pltpu.CompilerParams(vmem_limit_bytes=vmem * MIB),
        cost_estimate=pl.CostEstimate(flops=flops, bytes_accessed=size, transcendentals=0),
    )(*args)


def shape(dims, kind):
    return jax.ShapeDtypeStruct(tuple(dims), kind)


def dot(a, b):
    return jnp.dot(a, b, preferred_element_type=F32)


def dot_nt(a, b):
    return lax.dot_general(a, b, (((1,), (1,)), ((), ())), preferred_element_type=F32)


def dot_tn(a, b):
    return lax.dot_general(a, b, (((0,), (0,)), ((), ())), preferred_element_type=F32)


def split(a):
    high = a.astype(BF)
    return high, (a - high.astype(F32)).astype(BF)


def dot3(kind, a, b):
    dims = {dot: (1, 0), dot_nt: (1, 1), dot_tn: (0, 0)}[kind]
    a_high, a_low = split(a)
    b_high, b_low = split(b)
    return kind(
        jnp.concatenate([a_high, a_high, a_low], axis=dims[0]),
        jnp.concatenate([b_high, b_low, b_high], axis=dims[1]),
    )


def places(height, breadth):
    index = lax.broadcasted_iota(jnp.int32, (height * breadth, 1), 0)
    row = lax.div(index, breadth)
    return row, index - row * breadth


def valid_rows(small, height, breadth):
    row, col = places(height, breadth)
    row_limit = jnp.where(small > 0, height // 2, height)
    col_limit = jnp.where(small > 0, breadth // 2, breadth)
    return jnp.where((row < row_limit) & (col < col_limit), 1.0, 0.0).astype(F32)


def move(values, rows):
    gap = jnp.zeros((abs(rows),) + values.shape[1:], values.dtype)
    if rows > 0:
        return jnp.concatenate([gap, values[:-rows]], axis=0)
    return jnp.concatenate([values[-rows:], gap], axis=0)


def from_left(values, col):
    return jnp.where(col > 0, pltpu.roll(values, 1, 0), 0.0)


def from_right(values, col, breadth):
    return jnp.where(col < breadth - 1, pltpu.roll(values, values.shape[0] - 1, 0), 0.0)


def gather_taps(tap, breadth, col):
    lines = [move(tap(b), breadth) + tap(3 + b) + move(tap(6 + b), -breadth) for b in range(3)]
    return lines[1] + from_left(lines[0], col) + from_right(lines[2], col, breadth)


def spread_taps(values, breadth, col):
    lines = [from_right(values, col, breadth), values, from_left(values, col)]
    return [
        move(lines[b], breadth * (a - 1)) if a != 1 else lines[b] for a in range(3) for b in range(3)
    ]


def window_sum(values, row, col, breadth):
    count = values.shape[0]
    pair = values + jnp.where(
        col % 2 == 0, pltpu.roll(values, count - 1, 0), pltpu.roll(values, 1, 0)
    )
    return pair + jnp.where(row % 2 == 0, move(pair, -breadth), move(pair, breadth))


def silu_back(scaled):
    sig = jax.nn.sigmoid(scaled)
    return sig * (1.0 + scaled * (1.0 - sig))


def col_sum(values):
    return jnp.sum(values, axis=0, keepdims=True)


def put_sums(ref, rows):
    width = ref.shape[1]
    rows = list(rows) + [jnp.zeros((1, width), F32)] * (8 - len(rows))
    ref[...] = jnp.concatenate(rows, axis=0)


def each_image(geometry, body, start):
    number, height, breadth = geometry
    pixels = height * breadth

    def step(image, carry):
        return body(image, pl.ds(pl.multiple_of(image * pixels, 16), pixels), carry)

    return lax.fori_loop(0, number, step, start)


def zero_rows(count, width):
    return (jnp.zeros((1, width), F32),) * count


def greet(axes):
    barrier = pltpu.get_barrier_semaphore()
    for axis, size in axes:
        me = lax.axis_index(axis)
        for step in range(1, size):
            pl.semaphore_signal(
                barrier, inc=1, device_id={axis: lax.rem(me + step, size)}, device_id_type=MESH
            )
    pl.semaphore_wait(barrier, sum(size - 1 for _, size in axes))


def remote(source, target, sends, receives, peer, axis):
    return pltpu.make_async_remote_copy(
        src_ref=source,
        dst_ref=target,
        send_sem=sends,
        recv_sem=receives,
        device_id={axis: peer},
        device_id_type=MESH,
    )


def pack(rows):
    parts = [row[:, i : i + 128] for row in rows for i in range(0, row.shape[1], 128)]
    parts += [jnp.zeros((1, 128), F32)] * (8 - len(parts))
    return jnp.concatenate(parts, axis=0)


def unpack(tile, count, width):
    per = width // 128
    return [
        jnp.concatenate([tile[k * per + i : k * per + i + 1, :] for i in range(per)], axis=1)
        for k in range(count)
    ]


def total_rows(k, axis, size, rows, mine, slots, sends, receives):
    me = lax.axis_index(axis)
    tile = pack(rows)
    mine[k] = tile
    slots[k, me] = tile
    for step in range(1, size):
        peer = lax.rem(me + step, size)
        remote(mine.at[k], slots.at[k, me], sends.at[k, step], receives.at[k, me], peer, axis).start()
    for step in range(1, size):
        peer = lax.rem(me + size - step, size)
        remote(
            mine.at[k], slots.at[k, peer], sends.at[k, step], receives.at[k, peer], peer, axis
        ).wait_recv()
    total = slots[k, 0]
    for peer in range(1, size):
        total = total + slots[k, peer]
    for step in range(1, size):
        peer = lax.rem(me + step, size)
        remote(
            mine.at[k], slots.at[k, me], sends.at[k, step], receives.at[k, me], peer, axis
        ).wait_send()
    return unpack(total, len(rows), rows[0].shape[1])


def total_scratch(count, size):
    return [
        pltpu.VMEM((count, 8, 128), F32),
        pltpu.VMEM((count, size, 8, 128), F32),
        pltpu.SemaphoreType.DMA((count, size)),
        pltpu.SemaphoreType.DMA((count, size)),
    ]


def columns_of(place, width):
    return pl.ds(pl.multiple_of(place * width, 128), width)


SPECS = {"s": SMEM_SPEC, "v": VMEM_SPEC, "h": pl.BlockSpec(memory_space=pltpu.HBM)}


def exchange_kernel(body, outs, specs, args, scratch, identity, vmem, flops=0, places_out=None):
    size = sum(o.size * o.dtype.itemsize for o in outs) + sum(a.size * a.dtype.itemsize for a in args)
    return pl.pallas_call(
        body,
        out_shape=tuple(outs),
        in_specs=[SPECS[s] for s in specs],
        out_specs=tuple(SPECS[s] for s in places_out or "v" * len(outs)),
        scratch_shapes=list(scratch),
        compiler_params=pltpu.CompilerParams(
            vmem_limit_bytes=vmem * MIB, collective_id=identity, has_side_effects=True
        ),
        cost_estimate=pl.CostEstimate(flops=flops, bytes_accessed=size, transcendentals=0),
    )(*args)


def norm_with(values, totals, scale):
    total, squares, count = totals
    center = total / count
    inverse = lax.rsqrt(squares / count - center * center + EPS)
    normal = (values - center) * inverse
    return normal, inverse, normal * scale[0] + scale[1]


def norm_back_with(upstream, normal, inverse, count, sums, scale, valid):
    return scale[0] * inverse * (upstream - sums[0] / count - normal * (sums[1] / count)) * valid


def silu(values):
    return values * jax.nn.sigmoid(values)


def window_count(height, breadth):
    return -(-(height * breadth // 4) // 16) * 16


def pool_choice(height, breadth, windows, flipped):
    pixels = height * breadth
    dims = (windows, pixels) if flipped else (pixels, windows)
    pixel = lax.broadcasted_iota(jnp.int32, dims, 1 if flipped else 0)
    window = lax.broadcasted_iota(jnp.int32, dims, 0 if flipped else 1)
    row = lax.div(pixel, breadth)
    col = pixel - row * breadth
    home = lax.div(row, 2) * (breadth // 2) + lax.div(col, 2)
    return jnp.where(home == window, 1.0, 0.0).astype(F32)


def rows_of(ref, first, count):
    return [ref[first + k : first + k + 1, :] for k in range(count)]


def window_rows(i, windows):
    return pl.ds(pl.multiple_of(i * windows, 16), windows)


def trunk_forward_body(
    geometry, tasks, batches,
    small, x, enc_taps, dec_taps, scales, choose,
    enc_totals, dec_totals, features, *rest,
):
    kept, (enc_pre, dec_pre, spread), rest = rest[:6], rest[6:9], rest[9:]
    (
        work, pooled, pooled_all, part, pool_sends, pool_receives, sends, receives,
    mine, slots, total_sends, total_receives, saved,
    ) = rest
    number, height, breadth = geometry
    width = enc_pre.shape[1]
    windows = window_count(height, breadth)
    task = lax.axis_index("task")
    _, col = places(height, breadth)
    widen = pool_choice(height, breadth, windows, False).astype(BF)
    narrow = pool_choice(height, breadth, windows, True).astype(BF)

    sources = (x, enc_taps, dec_taps, enc_pre, dec_pre, spread)
    saves = [pltpu.make_async_copy(a, b, saved.at[k]) for k, (a, b) in enumerate(zip(sources, kept))]
    for copy in saves[:3]:
        copy.start()

    def conv(x, taps, pre):
        def image(i, rows, carry):
            valid = valid_rows(small[i], height, breadth)
            work[...] = dot(x[rows, :], taps[...])
            out = gather_taps(lambda p: work[:, p * width : (p + 1) * width], breadth, col)
            pre[rows, :] = out
            kept = out * valid
            return (
                carry[0] + col_sum(kept),
                carry[1] + col_sum(kept * out),
                carry[2] + jnp.broadcast_to(col_sum(valid), (1, width)),
            )

        return each_image(geometry, image, zero_rows(3, width))

    def total(k, rows):
        return total_rows(
            k, "batch", batches, list(rows), mine, slots, total_sends, total_receives
        )

    sums = conv(x, enc_taps, enc_pre)
    saves[3].start()
    greet((("task", tasks), ("batch", batches)))
    totals = total(0, sums)
    put_sums(enc_totals, totals)
    scale = rows_of(scales, 0, 2)

    def peer_of(step, incoming):
        return lax.rem(task + (tasks - step if incoming else step), tasks)

    def pool_copy(i, step, incoming=False):
        rows = window_rows(i, windows)
        peer = peer_of(step, incoming)
        target = pooled_all.at[rows, columns_of(peer if incoming else task, width)]
        return remote(
            pooled.at[rows, :], target, pool_sends.at[i, step], pool_receives.at[i, step], peer, "task"
        )

    def pool(i, rows, carry):
        valid = valid_rows(small[i], height, breadth)
        _, _, scaled = norm_with(enc_pre[rows, :], totals, scale)
        high, low = split(silu(scaled) * valid)
        mean = ((dot(narrow, high) + dot(narrow, low)) * 0.25).astype(BF)
        here = window_rows(i, windows)
        pooled[here, :] = mean
        pooled_all[here, columns_of(task, width)] = mean
        for step in range(1, tasks):
            pool_copy(i, step).start()
        return carry

    each_image(geometry, pool, 0)

    def unpool(i, rows, carry):
        for step in range(1, tasks):
            pool_copy(i, step, True).wait_recv()
        wide = dot(widen, pooled_all[window_rows(i, windows), :])
        spread[rows, :] = (wide * choose[rows, :]).astype(BF)
        return carry

    each_image(geometry, unpool, 0)
    saves[5].start()
    sums = conv(spread, dec_taps, dec_pre)
    saves[4].start()
    totals = total(1, sums)
    put_sums(dec_totals, totals)
    scale = rows_of(scales, 2, 2)

    def feature_copy(i, rows, step, incoming=False):
        peer = peer_of(step, incoming)
        target = features.at[rows, columns_of(peer if incoming else task, width)]
        return remote(
            part.at[rows, :], target, sends.at[i, step], receives.at[i, step], peer, "task"
        )

    def finish(i, rows, carry):
        valid = valid_rows(small[i], height, breadth)
        _, _, scaled = norm_with(dec_pre[rows, :], totals, scale)
        low = (silu(scaled) * valid).astype(BF)
        part[rows, :] = low
        features[rows, columns_of(task, width)] = low
        for step in range(1, tasks):
            feature_copy(i, rows, step).start()
        return carry

    each_image(geometry, finish, 0)

    def settle(i, rows, carry):
        for step in range(1, tasks):
            feature_copy(i, rows, step, True).wait_recv()
            feature_copy(i, rows, step).wait_send()
            pool_copy(i, step).wait_send()
        return carry

    each_image(geometry, settle, 0)
    for copy in saves:
        copy.wait()


def trunk_forward(geometry, tasks, batches, small, x, enc_taps, dec_taps, scales, choose):
    number, height, breadth = geometry
    pixels = height * breadth
    channels = x.shape[1]
    width = channels // tasks
    windows = window_count(height, breadth)
    tall = shape((x.shape[0], width), F32)
    outs = [
        shape((8, width), F32), shape((8, width), F32), shape(x.shape, BF),
        shape(x.shape, BF), shape(enc_taps.shape, BF), shape(dec_taps.shape, BF),
        tall, tall, shape(x.shape, BF),
    ]
    return exchange_kernel(
        functools.partial(trunk_forward_body, geometry, tasks, batches),
        outs,
        "svvvvv",
        (small, x, enc_taps, dec_taps, scales, choose),
        [
            pltpu.VMEM(tall.shape, F32),
            pltpu.VMEM(tall.shape, F32),
            pltpu.VMEM(x.shape, BF),
            pltpu.VMEM((pixels, 9 * width), F32),
            pltpu.VMEM((number * windows, width), BF),
            pltpu.VMEM((number * windows, channels), BF),
            pltpu.VMEM((x.shape[0], width), BF),
        ]
        + [pltpu.SemaphoreType.DMA((number, tasks))] * 4
        + total_scratch(2, batches)
        + [pltpu.SemaphoreType.DMA((6,))],
        1,
        60,
        flops=4 * x.size * enc_taps.shape[1],
        places_out="vvvhhhhhh",
    )


def head_body(
    geometry, tasks, batches,
    small, features, rows_in, cotangent, scales, counts,
    task_out, grads, upstream, norm_sums,
    pre_one, pre_two, pre_three, hidden, gated, nine, work, lower, out, arrived, sends, receives,
    mine, slots, total_sends, total_receives,
):
    number, height, breadth = geometry
    channels = features.shape[1]
    width = channels // tasks
    windows = task_out.shape[1]
    task = lax.axis_index("task")
    half = work.shape[2]
    _, col = places(height, breadth)
    widen = pool_choice(height, breadth, windows, False).astype(BF)
    narrow = pool_choice(height, breadth, windows, True).astype(BF)
    count = jnp.broadcast_to(counts[2:3, 0:1], (1, channels))
    first = rows_in.at[pl.ds(0, channels), :]
    second = rows_in.at[pl.ds(channels, channels), :]

    def kernel_rows(p):
        return pl.ds((2 + p) * channels, channels)

    def total(k, rows):
        return total_rows(
            k, "batch", batches, list(rows), mine, slots, total_sends, total_receives
        )

    def put_stats(pre, rows, value, valid, carry):
        pre[rows, :] = value
        kept = value * valid
        return carry[0] + col_sum(kept), carry[1] + col_sum(kept * value)

    nothing = zero_rows(2, channels)
    scale_one, scale_two, scale_three = (rows_of(scales, 2 * k, 2) for k in range(3))

    def first_step(i, rows, carry):
        valid = valid_rows(small[i], height, breadth)
        return put_stats(pre_one, rows, dot(features[rows, :], first[...]), valid, carry)

    sums = each_image(geometry, first_step, nothing)
    greet((("task", tasks), ("batch", batches)))
    totals_one = total(0, sums) + [count]

    def second_step(i, rows, carry):
        valid = valid_rows(small[i], height, breadth)
        _, _, scaled = norm_with(pre_one[rows, :], totals_one, scale_one)
        low = (silu(scaled) * valid).astype(BF)
        hidden[rows, :] = low
        return put_stats(pre_two, rows, dot(low, second[...]), valid, carry)

    sums = each_image(geometry, second_step, nothing)
    totals_two = total(1, sums) + [count]

    def third_step(i, rows, carry):
        valid = valid_rows(small[i], height, breadth)
        _, _, scaled = norm_with(pre_two[rows, :], totals_two, scale_two)
        low = (jax.nn.sigmoid(scaled) * features[rows, :].astype(F32)).astype(BF)
        gated[rows, :] = low
        parts = []
        for j in range(channels // half):
            cut = slice(j * half, (j + 1) * half)
            for p in range(9):
                work[p] = dot(low, rows_in[kernel_rows(p), cut])
            parts.append(gather_taps(lambda p: work[p], breadth, col))
        return put_stats(pre_three, rows, jnp.concatenate(parts, axis=1), valid, carry)

    sums = each_image(geometry, third_step, nothing)
    totals_three = total(2, sums) + [count]

    def out_step(i, rows, carry):
        valid = valid_rows(small[i], height, breadth)
        normal, _, scaled = norm_with(pre_three[rows, :], totals_three, scale_three)
        high, low = split(silu(scaled) * valid)
        mean = (dot(narrow, high) + dot(narrow, low)) * 0.25
        task_out[i] = mean.astype(BF)
        dy = silu_back(scaled) * dot(widen, cotangent[i]) * 0.25 * valid
        lower[rows, :] = dy
        return carry[0] + col_sum(dy), carry[1] + col_sum(dy * normal)

    sums = each_image(geometry, out_step, nothing)
    sums_three = total(3, sums)

    def third_back(i, rows, carry):
        valid = valid_rows(small[i], height, breadth)
        normal, inverse, _ = norm_with(pre_three[rows, :], totals_three, scale_three)
        dz = norm_back_with(lower[rows, :], normal, inverse, count, sums_three, scale_three, valid)
        for p, moved in enumerate(spread_taps(dz, breadth, col)):
            nine[p, rows, :] = moved.astype(BF)
        flow = None
        for p in range(9):
            piece = dot_nt(nine[p, rows, :], rows_in[kernel_rows(p), :])
            flow = piece if flow is None else flow + piece
        lower[rows, :] = flow
        normal, _, scaled = norm_with(pre_two[rows, :], totals_two, scale_two)
        gate = jax.nn.sigmoid(scaled)
        dy = flow * features[rows, :].astype(F32) * gate * (1.0 - gate) * valid
        pre_three[rows, :] = dy
        return carry[0] + col_sum(dy), carry[1] + col_sum(dy * normal)

    sums = each_image(geometry, third_back, nothing)
    sums_two = total(4, sums)

    def second_back(i, rows, carry):
        valid = valid_rows(small[i], height, breadth)
        normal, inverse, scaled = norm_with(pre_two[rows, :], totals_two, scale_two)
        dz = norm_back_with(
            pre_three[rows, :], normal, inverse, count, sums_two, scale_two, valid
        ).astype(BF)
        out[rows, :] = dz
        lower[rows, :] = lower[rows, :] * jax.nn.sigmoid(scaled)
        normal, _, scaled = norm_with(pre_one[rows, :], totals_one, scale_one)
        dy = silu_back(scaled) * dot_nt(dz, second[...]) * valid
        pre_three[rows, :] = dy
        return carry[0] + col_sum(dy), carry[1] + col_sum(dy * normal)

    sums = each_image(geometry, second_back, nothing)
    sums_one = total(5, sums)
    grads[pl.ds(channels, channels), :] = dot_tn(hidden[...], out[...]).astype(grads.dtype)

    def flow_copy(i, rows, step, incoming=False):
        peer = lax.rem(task + (tasks - step if incoming else step), tasks)
        return remote(
            out.at[rows, columns_of(peer, width)], arrived.at[step - 1, rows, :],
            sends.at[i, step], receives.at[i, step], peer, "task",
        )

    def first_back(i, rows, carry):
        valid = valid_rows(small[i], height, breadth)
        normal, inverse, _ = norm_with(pre_one[rows, :], totals_one, scale_one)
        dz = norm_back_with(
            pre_three[rows, :], normal, inverse, count, sums_one, scale_one, valid
        ).astype(BF)
        hidden[rows, :] = dz
        flow = (lower[rows, :] + dot_nt(dz, first[...])) * valid
        out[rows, :] = flow.astype(BF)
        for step in range(1, tasks):
            flow_copy(i, rows, step).start()
        return carry

    each_image(geometry, first_back, 0)
    grads[pl.ds(0, channels), :] = dot_tn(features[...], hidden[...]).astype(grads.dtype)

    def tap(p, carry):
        rows = pl.ds(pl.multiple_of((2 + p) * channels, channels), channels)
        grads[rows, :] = dot_tn(gated[...], nine[p]).astype(grads.dtype)
        return carry

    lax.fori_loop(0, 9, tap, 0)
    put_sums(norm_sums, sums_one + sums_two + sums_three)

    def settle(i, rows, carry):
        for step in range(1, tasks):
            flow_copy(i, rows, step, True).wait_recv()
        flow = out[rows, columns_of(task, width)].astype(F32)
        for step in range(1, tasks):
            flow = flow + arrived[step - 1, rows, :].astype(F32)
        upstream[rows, :] = flow
        for step in range(1, tasks):
            flow_copy(i, rows, step).wait_send()
        return carry

    each_image(geometry, settle, 0)


def head(geometry, tasks, batches, small, features, rows_in, cotangent, scales, counts):
    number, height, breadth = geometry
    pixels = height * breadth
    total, channels = features.shape
    width = channels // tasks
    return exchange_kernel(
        functools.partial(head_body, geometry, tasks, batches),
        [
            shape((number, pixels // 4, channels), BF),
            shape(rows_in.shape, BF),
            shape((total, width), F32),
            shape((8, channels), F32),
        ],
        "svvvvv",
        (small, features, rows_in, cotangent, scales, counts),
        [
            pltpu.VMEM(features.shape, F32),
            pltpu.VMEM(features.shape, F32),
            pltpu.VMEM(features.shape, F32),
            pltpu.VMEM(features.shape, BF),
            pltpu.VMEM(features.shape, BF),
            pltpu.VMEM((9,) + features.shape, BF),
            pltpu.VMEM((9, pixels, min(channels, 256)), F32),
            pltpu.VMEM(features.shape, F32),
            pltpu.VMEM(features.shape, BF),
            pltpu.VMEM((tasks - 1, total, width), BF),
        ]
        + [pltpu.SemaphoreType.DMA((number, tasks))] * 2
        + total_scratch(6, batches),
        2,
        60,
        flops=6 * total * channels * rows_in.shape[0],
    )


def trunk_backward_body(
    geometry, tasks, batches, summing,
    small, upstream, enc_totals, dec_totals, scales, choose_row, *rest,
):
    kept, rest = rest[:6], rest[6:]
    if summing:
        head_grads, rest = rest[0], rest[1:]
    (enc_grad, dec_grad, flow_out, norm_sums), rest = rest[:4], rest[4:]
    if summing:
        head_owned, rest = rest[0], rest[1:]
    (x, enc_taps, dec_taps, enc_pre, dec_pre, spread), rest = rest[:6], rest[6:]
    (
        nine, change, packed, arrived, pooled, sends, receives,
        mine, slots, total_sends, total_receives, loaded,
    ) = rest[:12]
    head_stages = [lambda: None] * 3
    if summing:
        near, paired, far, near_send, near_receive, far_send, far_receive, own, own_loaded = rest[12:]
        place, core, chips = pair_place(batches)
        count = near.shape[1]

        def own_load(step):
            chip = lax.rem(place + step, chips)
            source = block_rows(head_grads, 2 * chip + core, count)
            return pltpu.make_async_copy(source, own.at[step], own_loaded.at[step])

        for step in range(chips):
            own_load(step).start()
        *head_stages, head_end = pair_sum(
            batches, lambda index: block_rows(head_grads, index, count),
            lambda step: own[step].astype(F32), near, paired, far,
            (near_send, near_receive, far_send, far_receive),
        )
    head_start, head_middle, head_relay = head_stages
    targets = (x, enc_taps, dec_taps, enc_pre, dec_pre, spread)
    loads = [pltpu.make_async_copy(a, b, loaded.at[k]) for k, (a, b) in enumerate(zip(kept, targets))]
    for k in (4, 2, 5, 3, 1, 0):
        loads[k].start()
    number, height, breadth = geometry
    channels = x.shape[1]
    width = enc_pre.shape[1]
    windows = window_count(height, breadth)
    task = lax.axis_index("task")
    _, col = places(height, breadth)
    widen = pool_choice(height, breadth, windows, False).astype(BF)
    narrow = pool_choice(height, breadth, windows, True)
    nothing = zero_rows(2, width)

    def total(k, rows):
        return total_rows(
            k, "batch", batches, list(rows), mine, slots, total_sends, total_receives
        )

    def change_of(pre, totals, scale, flow):
        def image(i, rows, carry):
            valid = valid_rows(small[i], height, breadth)
            normal, _, scaled = norm_with(pre[rows, :], totals, scale)
            dy = silu_back(scaled) * flow(i, rows) * valid
            change[rows, :] = dy
            return carry[0] + col_sum(dy), carry[1] + col_sum(dy * normal)

        return each_image(geometry, image, nothing)

    def back(pre, totals, scale, sums, taps, put):
        def image(i, rows, carry):
            valid = valid_rows(small[i], height, breadth)
            normal, inverse, _ = norm_with(pre[rows, :], totals, scale)
            dz = norm_back_with(change[rows, :], normal, inverse, totals[2], sums, scale, valid)
            for p, moved in enumerate(spread_taps(dz, breadth, col)):
                nine[rows, p * width : (p + 1) * width] = moved.astype(BF)
            put(i, rows, dot_nt(nine[rows, :], taps[...]) * valid)
            return carry

        each_image(geometry, image, 0)

    totals = rows_of(dec_totals, 0, 3)
    scale = rows_of(scales, 2, 2)
    loads[4].wait()
    sums = change_of(dec_pre, totals, scale, lambda i, rows: upstream[rows, :])
    greet((("task", tasks), ("batch", batches)))
    head_start()
    dec_sums = total(0, sums)
    if summing:
        for step in range(chips):
            own_load(step).wait()

    def copy_of(i, step, incoming=False):
        rows = window_rows(i, windows)
        peer = lax.rem(task + (tasks - step if incoming else step), tasks)
        return remote(
            packed.at[rows, columns_of(peer, width)], arrived.at[step - 1, rows, :],
            sends.at[i, step], receives.at[i, step], peer, "task",
        )

    def put_packed(i, rows, flow):
        chosen = (narrow * choose_row[i]).astype(BF)
        packed[window_rows(i, windows), :] = dot(chosen, flow.astype(BF)).astype(BF)
        for step in range(1, tasks):
            copy_of(i, step).start()

    loads[2].wait()
    back(dec_pre, totals, scale, dec_sums, dec_taps, put_packed)
    loads[5].wait()
    head_middle()
    dec_grad[...] = dot_tn(spread[...], nine[...])

    def collect(i, carry):
        for step in range(1, tasks):
            copy_of(i, step, True).wait_recv()
        rows = window_rows(i, windows)
        flow = packed[rows, columns_of(task, width)].astype(F32)
        for step in range(1, tasks):
            flow = flow + arrived[step - 1, rows, :].astype(F32)
        pooled[rows, :] = flow
        for step in range(1, tasks):
            copy_of(i, step).wait_send()
        return carry

    lax.fori_loop(0, number, collect, 0)

    def widened(i, rows):
        high, low = split(pooled[window_rows(i, windows), :])
        return (dot(widen, high) + dot(widen, low)) * 0.25

    totals = rows_of(enc_totals, 0, 3)
    scale = rows_of(scales, 0, 2)
    loads[3].wait()
    sums = change_of(enc_pre, totals, scale, widened)
    enc_sums = total(1, sums)
    head_relay()

    def put_flow(i, rows, flow):
        flow_out[rows, :] = flow.astype(BF)

    loads[1].wait()
    back(enc_pre, totals, scale, enc_sums, enc_taps, put_flow)
    loads[0].wait()
    enc_grad[...] = dot_tn(x[...], nine[...])
    put_sums(norm_sums, enc_sums + dec_sums)
    if summing:
        head_owned[...] = head_end().astype(BF)


def trunk_backward(
    geometry, tasks, batches, small, upstream, enc_totals, dec_totals, scales, choose_row,
    head_grads, kept,
):
    number, height, breadth = geometry
    x, enc_taps, dec_taps = kept[:3]
    total, channels = x.shape
    width = channels // tasks
    windows = window_count(height, breadth)
    head_rows = head_grads.shape[0]
    summing = head_rows % (16 * batches) == 0
    outs = [
        shape(enc_taps.shape, F32),
        shape(dec_taps.shape, F32),
        shape(x.shape, BF),
        shape((8, width), F32),
    ]
    specs = "svvvvvhhhhhh"
    args = (small, upstream, enc_totals, dec_totals, scales, choose_row, *kept)
    scratch = []
    if summing:
        outs.append(shape((head_rows // batches, channels), BF))
        specs += "h"
        args += (head_grads,)
        scratch = pair_scratch(batches, head_rows, channels, BF) + [
            pltpu.VMEM((batches // 2, head_rows // batches, channels), BF),
            pltpu.SemaphoreType.DMA((batches // 2,)),
        ]
    made = exchange_kernel(
        functools.partial(trunk_backward_body, geometry, tasks, batches, summing),
        outs,
        specs,
        args,
        [pltpu.VMEM(a.shape, a.dtype) for a in kept]
        + [
            pltpu.VMEM((total, 9 * width), BF),
            pltpu.VMEM((total, width), F32),
            pltpu.VMEM((number * windows, channels), BF),
            pltpu.VMEM((tasks - 1, number * windows, width), BF),
            pltpu.VMEM((number * windows, width), F32),
        ]
        + [pltpu.SemaphoreType.DMA((number, tasks))] * 2
        + total_scratch(2, batches)
        + [pltpu.SemaphoreType.DMA((6,))]
        + scratch,
        3,
        60,
        flops=8 * x.size * enc_taps.shape[1],
    )
    if summing:
        return made
    return *made, lax.psum_scatter(head_grads, "batch", scatter_dimension=0, tiled=True)


def exchange(body, outs, args, scratch, identity, vmem=60):
    size = sum(o.size * o.dtype.itemsize for o in outs) + sum(a.size * a.dtype.itemsize for a in args)
    return pl.pallas_call(
        body,
        out_shape=tuple(outs),
        in_specs=[VMEM_SPEC] * len(args),
        out_specs=tuple(VMEM_SPEC for _ in outs),
        scratch_shapes=list(scratch),
        compiler_params=pltpu.CompilerParams(
            vmem_limit_bytes=vmem * MIB, collective_id=identity, has_side_effects=True
        ),
        cost_estimate=pl.CostEstimate(flops=0, bytes_accessed=size, transcendentals=0),
    )(*args)


def block_of(ref, place, size, dim):
    length = ref.shape[dim] // size
    start = place * length
    if dim == 0:
        return ref.at[pl.ds(pl.multiple_of(start, 8), length), :]
    return ref.at[:, pl.ds(pl.multiple_of(start, 128), length)]


def gather_body(axis, size, dims, *refs):
    count = len(dims)
    sources, targets = refs[:count], refs[count : 2 * count]
    sends, receives, own = refs[2 * count :]
    greet(((axis, size),))
    me = lax.axis_index(axis)
    copies = []
    for k in range(count):
        mine = block_of(targets[k], me, size, dims[k])
        for step in range(1, size):
            peer = lax.rem(me + step, size)
            copy = remote(sources[k], mine, sends.at[k, step], receives.at[k, me], peer, axis)
            copy.start()
            copies.append(copy)
    locals_ = []
    for k in range(count):
        mine = block_of(targets[k], me, size, dims[k])
        copy = pltpu.make_async_copy(sources[k], mine, own.at[k])
        copy.start()
        locals_.append(copy)
    for copy in locals_:
        copy.wait()
    for k in range(count):
        for step in range(1, size):
            peer = lax.rem(me + size - step, size)
            theirs = block_of(targets[k], peer, size, dims[k])
            remote(
                sources[k], theirs, sends.at[k, step], receives.at[k, peer], peer, axis
            ).wait_recv()
    for copy in copies:
        copy.wait_send()


def gather_over(axis, size, arrays, dims, identity):
    outs = []
    for x, dim in zip(arrays, dims):
        full = list(x.shape)
        full[dim] *= size
        outs.append(shape(full, x.dtype))
    count = len(arrays)
    return exchange(
        functools.partial(gather_body, axis, size, tuple(dims)),
        outs,
        arrays,
        [
            pltpu.SemaphoreType.DMA((count, size)),
            pltpu.SemaphoreType.DMA((count, size)),
            pltpu.SemaphoreType.DMA((count,)),
        ],
        identity,
    )


def to_taps_body(index, slots, enc, dec, wide, tap):
    count = slots.shape[0]
    channels = enc.shape[0]
    width = slots.shape[1]
    step = 1024

    def widen(i, carry):
        rows = pl.ds(pl.multiple_of(i * step, step), step)
        wide[rows, :] = slots[rows, :].astype(F32)
        return carry

    lax.fori_loop(0, count // step, widen, 0)
    group = 32
    for p in range(18):

        def fetch(i, carry):
            base = i * group
            for u in range(group):
                tap[pl.ds(base + u, 1), :] = wide[pl.ds(index[p * channels + base + u], 1), :]
            return carry

        lax.fori_loop(0, channels // group, fetch, 0)
        out = enc if p < 9 else dec
        q = p % 9
        out[:, q * width : (q + 1) * width] = tap[...].astype(BF)


def to_taps(index, slots, channels):
    width = slots.shape[1]
    return run(
        to_taps_body,
        [shape((channels, 9 * width), BF)] * 2,
        "sv",
        (index, slots),
        [pltpu.VMEM(slots.shape, F32), pltpu.VMEM((channels, width), F32)],
        vmem=60,
        flops=10000 * MIB,
    )


def to_slots_body(index, enc, dec, slots, wide):
    count = slots.shape[0]
    channels = enc.shape[0]
    width = slots.shape[1]
    step = 1024
    group = 32
    for p in range(18):
        source = enc if p < 9 else dec
        q = p % 9

        def place(i, carry):
            base = pl.multiple_of(i * group, group)
            values = source[pl.ds(base, group), q * width : (q + 1) * width]
            for u in range(group):
                wide[pl.ds(index[p * channels + base + u], 1), :] = values[u : u + 1, :]
            return carry

        lax.fori_loop(0, channels // group, place, 0)

    def narrow(i, carry):
        rows = pl.ds(pl.multiple_of(i * step, step), step)
        slots[rows, :] = wide[rows, :].astype(BF)
        return carry

    lax.fori_loop(0, count // step, narrow, 0)


def to_slots(index, enc, dec):
    width = enc.shape[1] // 9
    dims = (index.shape[0], width)
    return run(
        to_slots_body, [shape(dims, BF)], "svv", (index, enc, dec), [pltpu.VMEM(dims, F32)], vmem=60
    )[0]


def adam(gradient, moment_one, moment_two):
    new_one = BETA_ONE * moment_one + (1.0 - BETA_ONE) * gradient
    new_two = BETA_TWO * moment_two + (1.0 - BETA_TWO) * gradient * gradient
    direction = (
        new_one / (1.0 - BETA_ONE**STEP) / (jnp.sqrt(new_two / (1.0 - BETA_TWO**STEP)) + ADAM_EPS)
    )
    return new_one, new_two, direction


def pair_place(batches):
    me = lax.axis_index("batch")
    place = lax.div(me, 2)
    return place, me - 2 * place, batches // 2


def greet_pairs(tasks, batches):
    place, core, chips = pair_place(batches)
    task = lax.axis_index("task")
    barrier = pltpu.get_barrier_semaphore()

    def signal(device):
        pl.semaphore_signal(barrier, inc=1, device_id=device, device_id_type=MESH)

    for step in range(1, tasks):
        signal({"task": lax.rem(task + step, tasks)})
    signal({"batch": 2 * place + 1 - core})
    for step in range(1, chips):
        signal({"batch": 2 * lax.rem(place + step, chips) + core})
    pl.semaphore_wait(barrier, tasks - 1 + chips)


def block_rows(ref, index, count):
    return ref.at[pl.ds(pl.multiple_of(index * count, 8), count), :]


def far_first(chips):
    return sorted(range(chips), key=lambda step: -min(step, chips - step))


def pair_sum(batches, rows_of_block, own_block, near, paired, far, sems):
    place, core, chips = pair_place(batches)
    count = near.shape[1]
    near_send, near_receive, far_send, far_receive = sems
    other = 2 * place + 1 - core
    ring = chips == 4 and count % 32 == 0
    half = count // 2
    halves = (pl.ds(0, half), pl.ds(half, half))

    def near_copy(step):
        chip = lax.rem(place + step, chips)
        return remote(rows_of_block(2 * chip + 1 - core), near.at[step],
                      near_send.at[step], near_receive.at[step], other, "batch")

    def far_copy(step, incoming=False):
        chip = lax.rem(place + (chips - step if incoming else step), chips)
        return remote(paired.at[step], far.at[step], far_send.at[step], far_receive.at[step],
                      2 * chip + core, "batch")

    def ring_copy(which, way):
        chip = lax.rem(place + (1 if way == 0 else chips - 1), chips)
        if which == 0:
            source, target = paired.at[2, halves[way], :], far.at[2 + way, halves[0], :]
        else:
            cut = halves[way] if which == 2 else halves[1 - way]
            source, target = paired.at[1 if way == 0 else 3, cut, :], far.at[way, cut, :]
        k = 2 * which + way
        return remote(source, target, far_send.at[k], far_receive.at[k], 2 * chip + core, "batch")

    def start():
        for step in far_first(chips):
            near_copy(step).start()

    def middle():
        for step in far_first(chips):
            near_copy(step).wait_recv()
            if step:
                paired[step] = (own_block(step) + near[step].astype(F32)).astype(paired.dtype)
                if not ring:
                    far_copy(step).start()
                elif step == 2:
                    ring_copy(0, 0).start()
                    ring_copy(0, 1).start()
                else:
                    ring_copy(1, 0 if step == 1 else 1).start()

    def relay():
        if not ring:
            return
        for way in range(2):
            ring_copy(0, way).wait_recv()
            step = 1 if way == 0 else 3
            total = paired[step, halves[way], :].astype(F32) + far[2 + way, halves[0], :].astype(F32)
            paired[step, halves[way], :] = total.astype(paired.dtype)
            ring_copy(2, way).start()

    def end():
        total = own_block(0) + near[0].astype(F32)
        if ring:
            for way in range(2):
                ring_copy(1, way).wait_recv()
                ring_copy(2, way).wait_recv()
                total = total + far[way].astype(F32)
            for k in range(3):
                for way in range(2):
                    ring_copy(k, way).wait_send()
        else:
            for step in range(1, chips):
                far_copy(step, True).wait_recv()
                total = total + far[step].astype(F32)
            for step in range(1, chips):
                far_copy(step).wait_send()
        for step in range(chips):
            near_copy(step).wait_send()
        return total

    return start, middle, relay, end


def blocks_in(source, batches, count):
    place, core, chips = pair_place(batches)

    def own(step):
        chip = lax.rem(place + step, chips)
        return block_rows(source, 2 * chip + core, count)[...].astype(F32)

    return (lambda index: block_rows(source, index, count)), own


def pair_scratch(batches, rows, width, kind):
    chips = batches // 2
    return [pltpu.VMEM((chips, rows // batches, width), kind)] * 3 + [
        pltpu.SemaphoreType.DMA((max(chips, 6),))
    ] * 4


def chip_spread(batches, block, sends, receives):
    place, core, chips = pair_place(batches)
    count = block(place).shape[0]
    ring = chips == 4 and count % 32 == 0
    half = count // 2

    def copy(step, incoming=False):
        peer = lax.rem(place + (chips - step if incoming else step), chips)
        ref = block(peer if incoming else place)
        return remote(ref, ref, sends.at[step], receives.at[step], 2 * peer + core, "batch")

    def pass_on(way, incoming=False):
        step = 1 if way == 0 else chips - 1
        peer = lax.rem(place + (chips - step if incoming else step), chips)
        home = lax.rem(place + (2 if incoming else chips - step), chips)
        ref = block(home).at[pl.ds(way * half, half), :]
        k = 2 if way == 0 else 0
        return remote(ref, ref, sends.at[k], receives.at[k], 2 * peer + core, "batch")

    steps = (1, chips - 1) if ring else tuple(range(1, chips))

    def start():
        for step in steps:
            copy(step).start()

    def relay():
        if ring:
            for way, step in enumerate(steps):
                copy(step, True).wait_recv()
                pass_on(way).start()

    def settle():
        if ring:
            for way in range(2):
                pass_on(way, True).wait_recv()
        else:
            for step in steps:
                copy(step, True).wait_recv()

    def drain():
        for step in steps:
            copy(step).wait_send()
        if ring:
            for way in range(2):
                pass_on(way).wait_send()

    return start, relay, settle, drain


def collect_body(
    tasks, batches,
    slots, flow, sums,
    input_grad, owned, part, norm_sums,
    near, paired, far, near_send, near_receive, far_send, far_receive,
    flow_in, flow_send, flow_receive, send, receive, sum_send, sum_receive,
):
    task = lax.axis_index("task")
    width = part.shape[1]
    pixels = input_grad.shape[0]

    def peer_of(step, incoming):
        return lax.rem(task + (tasks - step if incoming else step), tasks)

    def flow_copy(step, incoming=False):
        peer = peer_of(step, incoming)
        return remote(block_rows(flow, peer, pixels), flow_in.at[step - 1], flow_send.at[step],
                      flow_receive.at[step], peer, "task")

    def sum_copy(step, incoming=False):
        peer = peer_of(step, incoming)
        home = peer if incoming else task
        return remote(sums, norm_sums.at[:, columns_of(home, width)], sum_send.at[step],
                      sum_receive.at[step], peer, "task")

    def part_copy(step, incoming=False):
        peer = peer_of(step, incoming)
        home = peer if incoming else task
        return remote(part, owned.at[:, columns_of(home, width)], send.at[step], receive.at[step],
                      peer, "task")

    greet_pairs(tasks, batches)
    start, middle, relay, end = pair_sum(
        batches, *blocks_in(slots, batches, near.shape[1]), near, paired, far,
        (near_send, near_receive, far_send, far_receive),
    )
    start()
    for step in range(1, tasks):
        sum_copy(step).start()
        flow_copy(step).start()
    norm_sums[:, columns_of(task, width)] = sums[...]
    middle()
    relay()
    total = end().astype(BF)
    part[...] = total
    for step in range(1, tasks):
        part_copy(step).start()
    owned[:, columns_of(task, width)] = total
    total = block_rows(flow, task, pixels)[...].astype(F32)
    for step in range(1, tasks):
        flow_copy(step, True).wait_recv()
        total = total + flow_in[step - 1].astype(F32)
    input_grad[...] = total
    for step in range(1, tasks):
        sum_copy(step, True).wait_recv()
        part_copy(step, True).wait_recv()
        sum_copy(step).wait_send()
        part_copy(step).wait_send()
        flow_copy(step).wait_send()


def collect(tasks, batches, slots, flow, sums):
    count, width = slots.shape
    rows = count // batches
    pixels, channels = flow.shape[0] // tasks, flow.shape[1]
    return exchange_kernel(
        functools.partial(collect_body, tasks, batches),
        [
            shape((pixels, channels), F32),
            shape((rows, channels), BF),
            shape((rows, width), BF),
            shape((8, channels), F32),
        ],
        "vvv",
        (slots, flow, sums),
        pair_scratch(batches, count, width, BF)
        + [pltpu.VMEM((tasks - 1, pixels, channels), BF)]
        + [pltpu.SemaphoreType.DMA((tasks,))] * 6,
        5,
        60,
        flops=20000 * MIB,
    )


def soap_rows(cuts, grad, owners, state, low, first):
    count = owners.shape[1]
    total = grad.shape[0]

    def chunk(i, carry):
        rows = pl.ds(pl.multiple_of(i * (total // cuts), 8), total // cuts)
        values = grad[rows, :].astype(F32)
        rotated = None
        for m in range(count):
            part = dot((values * owners[rows, m : m + 1]).astype(BF), low[first + m])
            rotated = part if rotated is None else rotated + part
        new_one, new_two, direction = adam(rotated, state[1, rows, :], state[2, rows, :])
        state[1, rows, :] = new_one
        state[2, rows, :] = new_two
        stepped = None
        for m in range(count):
            part = dot_nt((direction * owners[rows, m : m + 1]).astype(BF), low[first + m])
            stepped = part if stepped is None else stepped + part
        old = state[0, rows, :]
        state[0, rows, :] = old - LEARN_MATRIX * (stepped + DECAY_MATRIX * old)
        return carry

    lax.fori_loop(0, cuts, chunk, 0)


def factor_rows(values, identity, turn):
    size, width = values.shape
    sub = lax.broadcasted_iota(jnp.int32, (size, width), 0)
    rolled = pltpu.roll(values, turn, 1)
    columns = [jnp.broadcast_to(rolled[:, j : j + 1], (size, width)) for j in range(size)]
    scale = jnp.zeros((size, width), F32)
    for j in range(size):
        root = lax.rsqrt(columns[j][j : j + 1, :])
        scale = jnp.where(sub == j, root, scale)
        lower = jnp.where(sub > j, columns[j] * root, 0.0)
        values = values - lower * (values[j : j + 1, :] * root)
        identity = identity - lower * (identity[j : j + 1, :] * root)
        for i in range(j + 1, size):
            columns[i] = columns[i] - lower * (columns[i][j : j + 1, :] * root)
    return values * scale, identity * scale


GROUP = 16
PANEL = 128


def renew_panel(k, product, made, tables, inverses):
    count, size = product.shape[0], product.shape[1]
    here = slice(k * PANEL, (k + 1) * PANEL)
    row = lax.broadcasted_iota(jnp.int32, (PANEL, PANEL), 0)
    col = lax.broadcasted_iota(jnp.int32, (PANEL, PANEL), 1)
    unit = jnp.where(row == col, 1.0, 0.0).astype(F32)
    for n in range(count):
        tables[n][:, :PANEL] = dot3(dot_tn, product[n, :, here], product[n, :, here])
        tables[n][:, PANEL:] = unit

    def group(q, carry):
        rows = pl.ds(pl.multiple_of(q * GROUP, GROUP), GROUP)
        turn = lax.rem(PANEL - q * GROUP, PANEL)
        done = [
            factor_rows(tables[n][rows, :PANEL], tables[n][rows, PANEL:], turn)
            for n in range(count)
        ]
        for n in range(count):
            upper, inverse = done[n]
            inverses[n][rows, :] = inverse
            both = jnp.concatenate([upper, inverse], axis=1)
            tables[n][...] = tables[n][...] - dot3(dot_tn, upper, both)
        return carry

    lax.fori_loop(0, PANEL // GROUP, group, 0)
    for n in range(count):
        turned = dot3(dot_nt, product[n, :, here], inverses[n][...])
        made[n, :, here] = turned
        if k < size // PANEL - 1:
            rest = slice((k + 1) * PANEL, size)
            product[n, :, rest] = product[n, :, rest] - dot3(
                dot, turned, dot3(dot_tn, turned, product[n, :, rest])
            )


def rows_body(
    tasks, batches, cuts,
    grad, part, owners, head_grad, head_owners,
    weight, one, two, head_weight, head_one, head_two, basis, head_basis,
    state_new, head_state_new, grams, head_grams,
    state, head_state, mine, head_mine, bases, low,
    near, paired, far, near_send, near_receive, far_send, far_receive,
    head_near, head_paired, head_far, *rest,
):
    head_sems = rest[:4]
    chip_send, chip_receive, task_send, task_receive, pair_send, pair_receive, load, save = rest[4:]
    task = lax.axis_index("task")
    place, core, chips = pair_place(batches)
    width = part.shape[1]
    channels = grad.shape[1]
    count, head_count = near.shape[1], head_near.shape[1]
    trunk_total, head_total = owners.shape[1], head_owners.shape[1]

    moves = [
        (basis, bases.at[pl.ds(0, trunk_total)]),
        (head_basis, bases.at[pl.ds(trunk_total, head_total)]),
        (weight, state.at[0]),
        (one, state.at[1]),
        (two, state.at[2]),
        (head_weight, head_state.at[0]),
        (head_one, head_state.at[1]),
        (head_two, head_state.at[2]),
    ]
    loads = [pltpu.make_async_copy(a, b, load.at[k]) for k, (a, b) in enumerate(moves)]
    for copy in loads:
        copy.start()
    for m in range(head_total):
        held = (head_grad[...].astype(F32) * head_owners[:, m : m + 1]).astype(BF)
        head_mine[m * channels : (m + 1) * channels, :] = dot_tn(held, head_grad[...]).astype(
            head_mine.dtype
        )
    greet_pairs(tasks, batches)
    head_start, head_middle, head_relay, head_end = pair_sum(
        batches, *blocks_in(head_mine, batches, head_count), head_near, head_paired, head_far,
        head_sems,
    )
    head_start()
    for m in range(trunk_total):
        held = (grad[...].astype(F32) * owners[:, m : m + 1]).astype(BF)
        mine[m * channels : (m + 1) * channels, :] = dot_tn(held, part[...]).astype(mine.dtype)
    start, middle, relay, end = pair_sum(
        batches, *blocks_in(mine, batches, count), near, paired, far,
        (near_send, near_receive, far_send, far_receive),
    )
    start()
    head_middle()
    middle()
    head_relay()
    relay()

    def trunk_block(chip, home, which):
        rows = pl.ds(pl.multiple_of((2 * chip + which) * count, 8), count)
        return grams.at[rows, columns_of(home, width)]

    def head_block(chip, which):
        return block_rows(head_grams, 2 * chip + which, head_count)

    trunk_spread = chip_spread(
        batches, lambda chip: trunk_block(chip, task, core), chip_send.at[0], chip_receive.at[0]
    )
    head_spread = chip_spread(
        batches, lambda chip: head_block(chip, core), chip_send.at[1], chip_receive.at[1]
    )

    def task_copy(step, hop, incoming=False):
        peer = lax.rem(task + (tasks - step if incoming else step), tasks)
        chip = lax.rem(place + chips - hop, chips)
        block = trunk_block(chip, peer if incoming else task, core)
        return remote(block, block, task_send.at[step, hop], task_receive.at[step, hop], peer, "task")

    def pair_copy(kind, hop, incoming=False):
        chip = lax.rem(place + chips - hop, chips)
        which = 1 - core if incoming else core
        home = lax.rem(task + tasks - kind, tasks)
        block = head_block(chip, which) if kind == tasks else trunk_block(chip, home, which)
        return remote(block, block, pair_send.at[kind, hop], pair_receive.at[kind, hop],
                      2 * place + 1 - core, "batch")

    for copy in loads[:5]:
        copy.wait()
    for m in range(trunk_total + head_total):
        low[m] = bases[m].astype(BF)
    total = end().astype(grams.dtype)
    trunk_block(place, task, core)[...] = total
    trunk_spread[0]()
    for step in range(1, tasks):
        task_copy(step, 0).start()
    pair_copy(0, 0).start()
    soap_rows(cuts, grad, owners, state, low, 0)
    saves = [
        pltpu.make_async_copy(state, state_new, save.at[0]),
        pltpu.make_async_copy(head_state, head_state_new, save.at[1]),
    ]
    saves[0].start()
    total = head_end().astype(head_grams.dtype)
    head_block(place, core)[...] = total
    head_spread[0]()
    pair_copy(tasks, 0).start()
    trunk_spread[1]()
    trunk_spread[2]()
    for hop in range(1, chips):
        for step in range(1, tasks):
            task_copy(step, hop).start()
        pair_copy(0, hop).start()
    head_spread[1]()
    for copy in loads[5:]:
        copy.wait()
    soap_rows(cuts, head_grad, head_owners, head_state, low, trunk_total)
    saves[1].start()
    for hop in range(chips):
        for step in range(1, tasks):
            task_copy(step, hop, True).wait_recv()
            pair_copy(step, hop).start()
    head_spread[2]()
    for hop in range(1, chips):
        pair_copy(tasks, hop).start()
    for hop in range(chips):
        for kind in range(tasks + 1):
            pair_copy(kind, hop, True).wait_recv()
    for copy in saves:
        copy.wait()
    for hop in range(chips):
        for kind in range(tasks + 1):
            pair_copy(kind, hop).wait_send()
        for step in range(1, tasks):
            task_copy(step, hop).wait_send()
    trunk_spread[3]()
    head_spread[3]()


def renew_body(
    state, head_state, grams, head_grams, stat, head_stat, basis, head_basis,
    weight_new, one_new, two_new, head_weight_new, head_one_new, head_two_new,
    stat_new, head_stat_new, basis_new, head_basis_new,
    stats, product, made, save, *work,
):
    trunk_total, head_total = stat.shape[0], head_stat.shape[0]
    channels = stat.shape[1]
    count = trunk_total + head_total
    tables, inverses = work[:count], work[count:]
    sources = [state.at[k] for k in range(3)] + [head_state.at[k] for k in range(3)]
    targets = [weight_new, one_new, two_new, head_weight_new, head_one_new, head_two_new]
    saves = [pltpu.make_async_copy(a, b, save.at[k]) for k, (a, b) in enumerate(zip(sources, targets))]
    for copy in saves:
        copy.start()
    for m in range(count):
        first = m < trunk_total
        place = m if first else m - trunk_total
        gram = (grams if first else head_grams)[place * channels : (place + 1) * channels, :]
        old = (stat if first else head_stat)[place]
        stats[m] = STAT_DECAY * old + (1.0 - STAT_DECAY) * gram.astype(F32)
        product[m] = dot3(dot, stats[m], (basis if first else head_basis)[place])
    groups = ((0, trunk_total, stat_new, basis_new), (trunk_total, head_total, head_stat_new, head_basis_new))
    for begin, size, out, _ in groups:
        copy = pltpu.make_async_copy(stats.at[pl.ds(begin, size)], out, save.at[len(saves)])
        copy.start()
        saves.append(copy)
    for k in range(channels // PANEL):
        renew_panel(k, product, made, tables, inverses)
        cut = pl.ds(k * PANEL, PANEL)
        for begin, size, _, out in groups:
            copy = pltpu.make_async_copy(
                made.at[pl.ds(begin, size), :, cut], out.at[:, :, cut], save.at[len(saves)]
            )
            copy.start()
            saves.append(copy)
    for copy in saves:
        copy.wait()


def finish(tasks, batches, local_grads, rows, matrices):
    grad, part, owners, head_grad, head_owners = local_grads
    stat, head_stat, basis, head_basis = matrices
    channels, width = grad.shape[1], part.shape[1]
    trunk_total, head_total = owners.shape[1], head_owners.shape[1]
    gram_rows, head_rows = trunk_total * channels, head_total * channels
    chips = batches // 2
    kind = BF if gram_rows % (16 * batches) == 0 else F32
    head_kind = BF if head_rows % (16 * batches) == 0 else F32
    cuts = 4 if grad.shape[0] % 64 == 0 and head_grad.shape[0] % 64 == 0 else 1
    square = (trunk_total + head_total, channels, channels)
    made = exchange_kernel(
        functools.partial(rows_body, tasks, batches, cuts),
        [
            shape((3,) + grad.shape, F32),
            shape((3,) + head_grad.shape, F32),
            shape((gram_rows, channels), kind),
            shape((head_rows, channels), head_kind),
        ],
        "vvvvvhhhhhhhh",
        (*local_grads, *rows, basis, head_basis),
        [
            pltpu.VMEM((3,) + grad.shape, F32),
            pltpu.VMEM((3,) + head_grad.shape, F32),
            pltpu.VMEM((gram_rows, width), kind),
            pltpu.VMEM((head_rows, channels), head_kind),
            pltpu.VMEM(square, F32),
            pltpu.VMEM(square, BF),
        ]
        + pair_scratch(batches, gram_rows, width, kind)
        + pair_scratch(batches, head_rows, channels, head_kind)
        + [pltpu.SemaphoreType.DMA((2, max(chips, 4)))] * 2
        + [pltpu.SemaphoreType.DMA((tasks, chips))] * 2
        + [pltpu.SemaphoreType.DMA((tasks + 1, chips))] * 2
        + [pltpu.SemaphoreType.DMA((8,)), pltpu.SemaphoreType.DMA((2,))],
        6,
        60,
        flops=50000 * MIB,
        places_out="hhvv",
    )
    outs = [shape(a.shape, F32) for a in (*rows, *matrices)]
    hbm = pl.BlockSpec(memory_space=pltpu.HBM)
    count = trunk_total + head_total
    return pl.pallas_call(
        renew_body,
        out_shape=tuple(outs),
        in_specs=[hbm] * 2 + [VMEM_SPEC] * 6,
        out_specs=tuple(hbm for _ in outs),
        scratch_shapes=[pltpu.VMEM(square, F32)] * 3
        + [pltpu.SemaphoreType.DMA((8 + 2 * (channels // PANEL),))]
        + [pltpu.VMEM((PANEL, 2 * PANEL), F32)] * count
        + [pltpu.VMEM((PANEL, PANEL), F32)] * count,
        compiler_params=pltpu.CompilerParams(vmem_limit_bytes=60 * MIB),
        cost_estimate=pl.CostEstimate(
            flops=60000 * MIB, bytes_accessed=64 * MIB, transcendentals=0
        ),
    )(*made, *matrices)


def local(
    tasks,
    batches,
    images,
    image_small,
    pool_index,
    row_slot,
    trunk_weight,
    trunk_mean_grad,
    trunk_mean_square,
    trunk_statistic,
    trunk_basis,
    head_weight,
    head_mean_grad,
    head_mean_square,
    head_statistic,
    head_basis,
    trunk_gain,
    trunk_offset,
    trunk_norm_mean_grad,
    trunk_norm_mean_square,
    head_gain,
    head_offset,
    head_norm_mean_grad,
    head_norm_mean_square,
    cotangent,
):
    number, height, breadth, channels = images.shape
    pixels = height * breadth
    tap_rows = 9 * channels
    shown = tasks * number
    geometry = (shown, height, breadth)
    task = lax.axis_index("task")
    batch = lax.axis_index("batch")
    width = channels // tasks

    def quarter(values):
        return lax.dynamic_slice_in_dim(values, task * width, width, values.ndim - 1)

    def inside(flags):
        row_limit = jnp.where(flags > 0, height // 2, height)[:, None, None]
        col_limit = jnp.where(flags > 0, breadth // 2, breadth)[:, None, None]
        return (jnp.arange(height, dtype=jnp.int32)[None, :, None] < row_limit) & (
            jnp.arange(breadth, dtype=jnp.int32)[None, None, :] < col_limit
        )

    slots = lax.all_gather(quarter(trunk_weight).astype(BF), "batch", axis=0, tiled=True)
    head_rows = lax.all_gather(head_weight.astype(BF), "batch", axis=1, tiled=True)[0]
    kinds = jnp.concatenate([image_small, pool_index.reshape(-1)])
    kinds = lax.all_gather(kinds, "task", axis=0, tiled=True).reshape(tasks, -1)
    small = kinds[:, :number].reshape(-1)
    cells = kinds[:, number:].reshape(shown, height // 2, 1, breadth // 2, 1)
    cell = 2 * jnp.arange(2, dtype=jnp.int32)[:, None, None] + jnp.arange(2, dtype=jnp.int32)
    choose = (cells == cell).reshape(shown, height, breadth) & inside(small)
    choose = choose.astype(F32)
    choose_row = choose.reshape(shown, 1, pixels)
    choose = choose.reshape(shown * pixels, 1)
    masked = (images * inside(image_small)[..., None].astype(BF)).reshape(number * pixels, channels)
    x = gather_over("task", tasks, (masked,), (0,), 4)[0]
    enc_taps, dec_taps = to_taps(row_slot, slots, channels)

    local_rows = trunk_weight.shape[0]
    slot_ids = batch * local_rows + jnp.arange(local_rows, dtype=jnp.int32)
    decoded = jnp.any(row_slot[tap_rows:][None, :] == slot_ids[:, None], axis=1)
    trunk_onehot = jnp.stack([~decoded, decoded], axis=1).astype(F32)
    x, trunk_onehot = lax.optimization_barrier((x, trunk_onehot))

    scales = quarter(jnp.stack([trunk_gain, trunk_offset], axis=1)).reshape(4, width)
    enc_totals, dec_totals, features, *kept = trunk_forward(
        geometry, tasks, batches, small, x, enc_taps, dec_taps, scales, choose
    )
    head_scales = jnp.stack([head_gain[0], head_offset[0]], axis=1).reshape(6, channels)
    pooled, head_grads, upstream, head_sums = head(
        geometry, tasks, batches, small, features, head_rows,
        cotangent.reshape(shown, pixels // 4, channels), head_scales, enc_totals,
    )
    task_features = pooled.reshape(cotangent.shape)
    enc_grad, dec_grad, flow, trunk_sums, head_owned = trunk_backward(
        geometry, tasks, batches, small, upstream, enc_totals, dec_totals, scales, choose_row,
        head_grads, kept,
    )
    input_grad, trunk_owned, trunk_part, norm_sums = collect(
        tasks, batches, to_slots(row_slot, enc_grad, dec_grad), flow, trunk_sums
    )
    input_grad = input_grad.reshape(images.shape)

    head_local = head_weight.shape[1]
    head_ids = batch * head_local + jnp.arange(head_local, dtype=jnp.int32)
    head_owner = jnp.minimum(head_ids // channels, 2)
    head_onehot = (head_owner[:, None] == jnp.arange(3, dtype=jnp.int32)).astype(F32)
    (
        trunk_weight_new, trunk_one_new, trunk_two_new,
        head_weight_new, head_one_new, head_two_new,
        trunk_stat_new, head_stat_new, trunk_basis_new, head_basis_new,
    ) = finish(
        tasks, batches,
        (trunk_owned, trunk_part, trunk_onehot, head_owned, head_onehot),
        (trunk_weight, trunk_mean_grad, trunk_mean_square,
         head_weight[0], head_mean_grad[0], head_mean_square[0]),
        (trunk_statistic, head_statistic[0], trunk_basis, head_basis[0]),
    )

    trunk_norm = jnp.stack([trunk_gain, trunk_offset], axis=1)
    trunk_norm_grad = norm_sums[:4].reshape(2, 2, channels)[:, ::-1]
    trunk_norm_one, trunk_norm_two, trunk_direction = adam(
        trunk_norm_grad, trunk_norm_mean_grad, trunk_norm_mean_square
    )
    head_norm = jnp.stack([head_gain, head_offset], axis=2)
    head_norm_grad = head_sums[:6].reshape(1, 3, 2, channels)[:, :, ::-1]
    head_norm_one, head_norm_two, head_direction = adam(
        head_norm_grad, head_norm_mean_grad, head_norm_mean_square
    )
    return (
        task_features,
        input_grad,
        trunk_weight_new,
        trunk_one_new,
        trunk_two_new,
        trunk_stat_new,
        trunk_basis_new,
        head_weight_new[None],
        head_one_new[None],
        head_two_new[None],
        head_stat_new[None],
        head_basis_new[None],
        trunk_norm - LEARN_NORM * trunk_direction,
        trunk_norm_one,
        trunk_norm_two,
        head_norm - LEARN_NORM * head_direction,
        head_norm_one,
        head_norm_two,
    )


def solution(mesh):
    placed = (
        P(("task", "batch"), None, None, None),
        P(("task", "batch")),
        P(("task", "batch"), None, None),
        P(),
        P("batch", None),
        P("batch", None),
        P("batch", None),
        P(),
        P(),
        P("task", "batch", None),
        P("task", "batch", None),
        P("task", "batch", None),
        P("task", None, None, None),
        P("task", None, None, None),
        P(),
        P(),
        P(),
        P(),
        P("task", None, None),
        P("task", None, None),
        P("task", None, None, None),
        P("task", None, None, None),
        P("task", None, "batch", None, None, None),
    )
    return jax.shard_map(
        functools.partial(local, mesh.shape["task"], mesh.shape["batch"]),
        mesh=mesh,
        in_specs=placed,
        out_specs=(
            P("task", None, "batch", None, None, None),
            P(("task", "batch"), None, None, None),
            P("batch", None),
            P("batch", None),
            P("batch", None),
            P(),
            P(),
            P("task", "batch", None),
            P("task", "batch", None),
            P("task", "batch", None),
            P("task", None, None, None),
            P("task", None, None, None),
            P(),
            P(),
            P(),
            P("task", None, None, None),
            P("task", None, None, None),
            P("task", None, None, None),
        ),
        check_vma=False,
    )
```

```python
import functools

import jax
import jax.numpy as jnp
from jax import lax
from jax.experimental import pallas as pl
from jax.experimental.pallas import tpu as pltpu
from jax.sharding import PartitionSpec as P

STEP = 10


EPS = 1e-05
ADAM_EPS = 1e-08
BETA_ONE = 0.95
BETA_TWO = 0.95
STAT_DECAY = 0.95
LEARN_MATRIX = 0.02
LEARN_NORM = 0.5
DECAY_MATRIX = 0.01
BF = jnp.bfloat16
F32 = jnp.float32
MESH = pl.DeviceIdType.MESH
MIB = 1 << 20

VMEM_SPEC = pl.BlockSpec(memory_space=pltpu.VMEM)
SMEM_SPEC = pl.BlockSpec(memory_space=pltpu.SMEM)


def run(body, outs, specs, args, scratch=(), vmem=40, flops=0):
    size = sum(o.size * o.dtype.itemsize for o in outs) + sum(a.size * a.dtype.itemsize for a in args)
    return pl.pallas_call(
        body,
        out_shape=tuple(outs),
        in_specs=[SMEM_SPEC if s == "s" else VMEM_SPEC for s in specs],
        out_specs=tuple(VMEM_SPEC for _ in outs),
        scratch_shapes=list(scratch),
        compiler_params=pltpu.CompilerParams(vmem_limit_bytes=vmem * MIB),
        cost_estimate=pl.CostEstimate(flops=flops, bytes_accessed=size, transcendentals=0),
    )(*args)


def shape(dims, kind):
    return jax.ShapeDtypeStruct(tuple(dims), kind)


def dot(a, b):
    return jnp.dot(a, b, preferred_element_type=F32)


def dot_nt(a, b):
    return lax.dot_general(a, b, (((1,), (1,)), ((), ())), preferred_element_type=F32)


def dot_tn(a, b):
    return lax.dot_general(a, b, (((0,), (0,)), ((), ())), preferred_element_type=F32)


def split(a):
    high = a.astype(BF)
    return high, (a - high.astype(F32)).astype(BF)


def dot3(kind, a, b):
    dims = {dot: (1, 0), dot_nt: (1, 1), dot_tn: (0, 0)}[kind]
    a_high, a_low = split(a)
    b_high, b_low = split(b)
    return kind(
        jnp.concatenate([a_high, a_high, a_low], axis=dims[0]),
        jnp.concatenate([b_high, b_low, b_high], axis=dims[1]),
    )


def places(height, breadth):
    index = lax.broadcasted_iota(jnp.int32, (height * breadth, 1), 0)
    row = lax.div(index, breadth)
    return row, index - row * breadth


def valid_rows(small, height, breadth):
    row, col = places(height, breadth)
    row_limit = jnp.where(small > 0, height // 2, height)
    col_limit = jnp.where(small > 0, breadth // 2, breadth)
    return jnp.where((row < row_limit) & (col < col_limit), 1.0, 0.0).astype(F32)


def move(values, rows):
    gap = jnp.zeros((abs(rows),) + values.shape[1:], values.dtype)
    if rows > 0:
        return jnp.concatenate([gap, values[:-rows]], axis=0)
    return jnp.concatenate([values[-rows:], gap], axis=0)


def from_left(values, col):
    return jnp.where(col > 0, pltpu.roll(values, 1, 0), 0.0)


def from_right(values, col, breadth):
    return jnp.where(col < breadth - 1, pltpu.roll(values, values.shape[0] - 1, 0), 0.0)


def gather_taps(tap, breadth, col):
    lines = [move(tap(b), breadth) + tap(3 + b) + move(tap(6 + b), -breadth) for b in range(3)]
    return lines[1] + from_left(lines[0], col) + from_right(lines[2], col, breadth)


def spread_taps(values, breadth, col):
    lines = [from_right(values, col, breadth), values, from_left(values, col)]
    return [
        move(lines[b], breadth * (a - 1)) if a != 1 else lines[b] for a in range(3) for b in range(3)
    ]


def window_sum(values, row, col, breadth):
    count = values.shape[0]
    pair = values + jnp.where(
        col % 2 == 0, pltpu.roll(values, count - 1, 0), pltpu.roll(values, 1, 0)
    )
    return pair + jnp.where(row % 2 == 0, move(pair, -breadth), move(pair, breadth))


def silu_back(scaled):
    sig = jax.nn.sigmoid(scaled)
    return sig * (1.0 + scaled * (1.0 - sig))


def col_sum(values):
    return jnp.sum(values, axis=0, keepdims=True)


def put_sums(ref, rows):
    width = ref.shape[1]
    rows = list(rows) + [jnp.zeros((1, width), F32)] * (8 - len(rows))
    ref[...] = jnp.concatenate(rows, axis=0)


def each_image(geometry, body, start):
    number, height, breadth = geometry
    pixels = height * breadth

    def step(image, carry):
        return body(image, pl.ds(pl.multiple_of(image * pixels, 16), pixels), carry)

    return lax.fori_loop(0, number, step, start)


def zero_rows(count, width):
    return (jnp.zeros((1, width), F32),) * count


def greet(axes):
    barrier = pltpu.get_barrier_semaphore()
    for axis, size in axes:
        me = lax.axis_index(axis)
        for step in range(1, size):
            pl.semaphore_signal(
                barrier, inc=1, device_id={axis: lax.rem(me + step, size)}, device_id_type=MESH
            )
    pl.semaphore_wait(barrier, sum(size - 1 for _, size in axes))


def remote(source, target, sends, receives, peer, axis):
    return pltpu.make_async_remote_copy(
        src_ref=source,
        dst_ref=target,
        send_sem=sends,
        recv_sem=receives,
        device_id={axis: peer},
        device_id_type=MESH,
    )


def pack(rows):
    parts = [row[:, i : i + 128] for row in rows for i in range(0, row.shape[1], 128)]
    parts += [jnp.zeros((1, 128), F32)] * (8 - len(parts))
    return jnp.concatenate(parts, axis=0)


def unpack(tile, count, width):
    per = width // 128
    return [
        jnp.concatenate([tile[k * per + i : k * per + i + 1, :] for i in range(per)], axis=1)
        for k in range(count)
    ]


def total_rows(k, axis, size, rows, mine, slots, sends, receives):
    me = lax.axis_index(axis)
    tile = pack(rows)
    mine[k] = tile
    slots[k, me] = tile
    for step in range(1, size):
        peer = lax.rem(me + step, size)
        remote(mine.at[k], slots.at[k, me], sends.at[k, step], receives.at[k, me], peer, axis).start()
    for step in range(1, size):
        peer = lax.rem(me + size - step, size)
        remote(
            mine.at[k], slots.at[k, peer], sends.at[k, step], receives.at[k, peer], peer, axis
        ).wait_recv()
    total = slots[k, 0]
    for peer in range(1, size):
        total = total + slots[k, peer]
    for step in range(1, size):
        peer = lax.rem(me + step, size)
        remote(
            mine.at[k], slots.at[k, me], sends.at[k, step], receives.at[k, me], peer, axis
        ).wait_send()
    return unpack(total, len(rows), rows[0].shape[1])


def total_scratch(count, size):
    return [
        pltpu.VMEM((count, 8, 128), F32),
        pltpu.VMEM((count, size, 8, 128), F32),
        pltpu.SemaphoreType.DMA((count, size)),
        pltpu.SemaphoreType.DMA((count, size)),
    ]


def columns_of(place, width):
    return pl.ds(pl.multiple_of(place * width, 128), width)


SPECS = {"s": SMEM_SPEC, "v": VMEM_SPEC, "h": pl.BlockSpec(memory_space=pltpu.HBM)}


def exchange_kernel(body, outs, specs, args, scratch, identity, vmem, flops=0, places_out=None):
    size = sum(o.size * o.dtype.itemsize for o in outs) + sum(a.size * a.dtype.itemsize for a in args)
    return pl.pallas_call(
        body,
        out_shape=tuple(outs),
        in_specs=[SPECS[s] for s in specs],
        out_specs=tuple(SPECS[s] for s in places_out or "v" * len(outs)),
        scratch_shapes=list(scratch),
        compiler_params=pltpu.CompilerParams(
            vmem_limit_bytes=vmem * MIB, collective_id=identity, has_side_effects=True
        ),
        cost_estimate=pl.CostEstimate(flops=flops, bytes_accessed=size, transcendentals=0),
    )(*args)


def norm_with(values, totals, scale):
    total, squares, count = totals
    center = total / count
    inverse = lax.rsqrt(squares / count - center * center + EPS)
    normal = (values - center) * inverse
    return normal, inverse, normal * scale[0] + scale[1]


def norm_back_with(upstream, normal, inverse, count, sums, scale, valid):
    return scale[0] * inverse * (upstream - sums[0] / count - normal * (sums[1] / count)) * valid


def silu(values):
    return values * jax.nn.sigmoid(values)


def window_count(height, breadth):
    return -(-(height * breadth // 4) // 16) * 16


def pool_choice(height, breadth, windows, flipped):
    pixels = height * breadth
    dims = (windows, pixels) if flipped else (pixels, windows)
    pixel = lax.broadcasted_iota(jnp.int32, dims, 1 if flipped else 0)
    window = lax.broadcasted_iota(jnp.int32, dims, 0 if flipped else 1)
    row = lax.div(pixel, breadth)
    col = pixel - row * breadth
    home = lax.div(row, 2) * (breadth // 2) + lax.div(col, 2)
    return jnp.where(home == window, 1.0, 0.0).astype(F32)


def rows_of(ref, first, count):
    return [ref[first + k : first + k + 1, :] for k in range(count)]


def window_rows(i, windows):
    return pl.ds(pl.multiple_of(i * windows, 16), windows)


def trunk_forward_body(
    geometry, tasks, batches,
    small, x, enc_taps, dec_taps, scales, choose,
    enc_totals, dec_totals, features, *rest,
):
    kept, (enc_pre, dec_pre, spread), rest = rest[:6], rest[6:9], rest[9:]
    (
        work, pooled, pooled_all, part, pool_sends, pool_receives, sends, receives,
    mine, slots, total_sends, total_receives, saved,
    ) = rest
    number, height, breadth = geometry
    width = enc_pre.shape[1]
    windows = window_count(height, breadth)
    task = lax.axis_index("task")
    _, col = places(height, breadth)
    widen = pool_choice(height, breadth, windows, False).astype(BF)
    narrow = pool_choice(height, breadth, windows, True).astype(BF)

    sources = (x, enc_taps, dec_taps, enc_pre, dec_pre, spread)
    saves = [pltpu.make_async_copy(a, b, saved.at[k]) for k, (a, b) in enumerate(zip(sources, kept))]
    for copy in saves[:3]:
        copy.start()

    def conv(x, taps, pre):
        def image(i, rows, carry):
            valid = valid_rows(small[i], height, breadth)
            work[...] = dot(x[rows, :], taps[...])
            out = gather_taps(lambda p: work[:, p * width : (p + 1) * width], breadth, col)
            pre[rows, :] = out
            kept = out * valid
            return (
                carry[0] + col_sum(kept),
                carry[1] + col_sum(kept * out),
                carry[2] + jnp.broadcast_to(col_sum(valid), (1, width)),
            )

        return each_image(geometry, image, zero_rows(3, width))

    def total(k, rows):
        return total_rows(
            k, "batch", batches, list(rows), mine, slots, total_sends, total_receives
        )

    sums = conv(x, enc_taps, enc_pre)
    saves[3].start()
    greet((("task", tasks), ("batch", batches)))
    totals = total(0, sums)
    put_sums(enc_totals, totals)
    scale = rows_of(scales, 0, 2)

    def peer_of(step, incoming):
        return lax.rem(task + (tasks - step if incoming else step), tasks)

    def pool_copy(i, step, incoming=False):
        rows = window_rows(i, windows)
        peer = peer_of(step, incoming)
        target = pooled_all.at[rows, columns_of(peer if incoming else task, width)]
        return remote(
            pooled.at[rows, :], target, pool_sends.at[i, step], pool_receives.at[i, step], peer, "task"
        )

    def pool(i, rows, carry):
        valid = valid_rows(small[i], height, breadth)
        _, _, scaled = norm_with(enc_pre[rows, :], totals, scale)
        high, low = split(silu(scaled) * valid)
        mean = ((dot(narrow, high) + dot(narrow, low)) * 0.25).astype(BF)
        here = window_rows(i, windows)
        pooled[here, :] = mean
        pooled_all[here, columns_of(task, width)] = mean
        for step in range(1, tasks):
            pool_copy(i, step).start()
        return carry

    each_image(geometry, pool, 0)

    def unpool(i, rows, carry):
        for step in range(1, tasks):
            pool_copy(i, step, True).wait_recv()
        wide = dot(widen, pooled_all[window_rows(i, windows), :])
        spread[rows, :] = (wide * choose[rows, :]).astype(BF)
        return carry

    each_image(geometry, unpool, 0)
    saves[5].start()
    sums = conv(spread, dec_taps, dec_pre)
    saves[4].start()
    totals = total(1, sums)
    put_sums(dec_totals, totals)
    scale = rows_of(scales, 2, 2)

    def feature_copy(i, rows, step, incoming=False):
        peer = peer_of(step, incoming)
        target = features.at[rows, columns_of(peer if incoming else task, width)]
        return remote(
            part.at[rows, :], target, sends.at[i, step], receives.at[i, step], peer, "task"
        )

    def finish(i, rows, carry):
        valid = valid_rows(small[i], height, breadth)
        _, _, scaled = norm_with(dec_pre[rows, :], totals, scale)
        low = (silu(scaled) * valid).astype(BF)
        part[rows, :] = low
        features[rows, columns_of(task, width)] = low
        for step in range(1, tasks):
            feature_copy(i, rows, step).start()
        return carry

    each_image(geometry, finish, 0)

    def settle(i, rows, carry):
        for step in range(1, tasks):
            feature_copy(i, rows, step, True).wait_recv()
            feature_copy(i, rows, step).wait_send()
            pool_copy(i, step).wait_send()
        return carry

    each_image(geometry, settle, 0)
    for copy in saves:
        copy.wait()


def trunk_forward(geometry, tasks, batches, small, x, enc_taps, dec_taps, scales, choose):
    number, height, breadth = geometry
    pixels = height * breadth
    channels = x.shape[1]
    width = channels // tasks
    windows = window_count(height, breadth)
    tall = shape((x.shape[0], width), F32)
    outs = [
        shape((8, width), F32), shape((8, width), F32), shape(x.shape, BF),
        shape(x.shape, BF), shape(enc_taps.shape, BF), shape(dec_taps.shape, BF),
        tall, tall, shape(x.shape, BF),
    ]
    return exchange_kernel(
        functools.partial(trunk_forward_body, geometry, tasks, batches),
        outs,
        "svvvvv",
        (small, x, enc_taps, dec_taps, scales, choose),
        [
            pltpu.VMEM(tall.shape, F32),
            pltpu.VMEM(tall.shape, F32),
            pltpu.VMEM(x.shape, BF),
            pltpu.VMEM((pixels, 9 * width), F32),
            pltpu.VMEM((number * windows, width), BF),
            pltpu.VMEM((number * windows, channels), BF),
            pltpu.VMEM((x.shape[0], width), BF),
        ]
        + [pltpu.SemaphoreType.DMA((number, tasks))] * 4
        + total_scratch(2, batches)
        + [pltpu.SemaphoreType.DMA((6,))],
        1,
        60,
        flops=4 * x.size * enc_taps.shape[1],
        places_out="vvvhhhhhh",
    )


def head_body(
    geometry, tasks, batches,
    small, features, rows_in, cotangent, scales, counts,
    task_out, grads, upstream, norm_sums,
    pre_one, pre_two, pre_three, hidden, gated, nine, work, lower, out, arrived, sends, receives,
    mine, slots, total_sends, total_receives,
):
    number, height, breadth = geometry
    channels = features.shape[1]
    width = channels // tasks
    windows = task_out.shape[1]
    task = lax.axis_index("task")
    half = work.shape[2]
    _, col = places(height, breadth)
    widen = pool_choice(height, breadth, windows, False).astype(BF)
    narrow = pool_choice(height, breadth, windows, True).astype(BF)
    count = jnp.broadcast_to(counts[2:3, 0:1], (1, channels))
    first = rows_in.at[pl.ds(0, channels), :]
    second = rows_in.at[pl.ds(channels, channels), :]

    def kernel_rows(p):
        return pl.ds((2 + p) * channels, channels)

    def total(k, rows):
        return total_rows(
            k, "batch", batches, list(rows), mine, slots, total_sends, total_receives
        )

    def put_stats(pre, rows, value, valid, carry):
        pre[rows, :] = value
        kept = value * valid
        return carry[0] + col_sum(kept), carry[1] + col_sum(kept * value)

    nothing = zero_rows(2, channels)
    scale_one, scale_two, scale_three = (rows_of(scales, 2 * k, 2) for k in range(3))

    def first_step(i, rows, carry):
        valid = valid_rows(small[i], height, breadth)
        return put_stats(pre_one, rows, dot(features[rows, :], first[...]), valid, carry)

    sums = each_image(geometry, first_step, nothing)
    greet((("task", tasks), ("batch", batches)))
    totals_one = total(0, sums) + [count]

    def second_step(i, rows, carry):
        valid = valid_rows(small[i], height, breadth)
        _, _, scaled = norm_with(pre_one[rows, :], totals_one, scale_one)
        low = (silu(scaled) * valid).astype(BF)
        hidden[rows, :] = low
        return put_stats(pre_two, rows, dot(low, second[...]), valid, carry)

    sums = each_image(geometry, second_step, nothing)
    totals_two = total(1, sums) + [count]

    def third_step(i, rows, carry):
        valid = valid_rows(small[i], height, breadth)
        _, _, scaled = norm_with(pre_two[rows, :], totals_two, scale_two)
        low = (jax.nn.sigmoid(scaled) * features[rows, :].astype(F32)).astype(BF)
        gated[rows, :] = low
        parts = []
        for j in range(channels // half):
            cut = slice(j * half, (j + 1) * half)
            for p in range(9):
                work[p] = dot(low, rows_in[kernel_rows(p), cut])
            parts.append(gather_taps(lambda p: work[p], breadth, col))
        return put_stats(pre_three, rows, jnp.concatenate(parts, axis=1), valid, carry)

    sums = each_image(geometry, third_step, nothing)
    totals_three = total(2, sums) + [count]

    def out_step(i, rows, carry):
        valid = valid_rows(small[i], height, breadth)
        normal, _, scaled = norm_with(pre_three[rows, :], totals_three, scale_three)
        high, low = split(silu(scaled) * valid)
        mean = (dot(narrow, high) + dot(narrow, low)) * 0.25
        task_out[i] = mean.astype(BF)
        dy = silu_back(scaled) * dot(widen, cotangent[i]) * 0.25 * valid
        lower[rows, :] = dy
        return carry[0] + col_sum(dy), carry[1] + col_sum(dy * normal)

    sums = each_image(geometry, out_step, nothing)
    sums_three = total(3, sums)

    def third_back(i, rows, carry):
        valid = valid_rows(small[i], height, breadth)
        normal, inverse, _ = norm_with(pre_three[rows, :], totals_three, scale_three)
        dz = norm_back_with(lower[rows, :], normal, inverse, count, sums_three, scale_three, valid)
        for p, moved in enumerate(spread_taps(dz, breadth, col)):
            nine[p, rows, :] = moved.astype(BF)
        flow = None
        for p in range(9):
            piece = dot_nt(nine[p, rows, :], rows_in[kernel_rows(p), :])
            flow = piece if flow is None else flow + piece
        lower[rows, :] = flow
        normal, _, scaled = norm_with(pre_two[rows, :], totals_two, scale_two)
        gate = jax.nn.sigmoid(scaled)
        dy = flow * features[rows, :].astype(F32) * gate * (1.0 - gate) * valid
        pre_three[rows, :] = dy
        return carry[0] + col_sum(dy), carry[1] + col_sum(dy * normal)

    sums = each_image(geometry, third_back, nothing)
    sums_two = total(4, sums)

    def second_back(i, rows, carry):
        valid = valid_rows(small[i], height, breadth)
        normal, inverse, scaled = norm_with(pre_two[rows, :], totals_two, scale_two)
        dz = norm_back_with(
            pre_three[rows, :], normal, inverse, count, sums_two, scale_two, valid
        ).astype(BF)
        out[rows, :] = dz
        lower[rows, :] = lower[rows, :] * jax.nn.sigmoid(scaled)
        normal, _, scaled = norm_with(pre_one[rows, :], totals_one, scale_one)
        dy = silu_back(scaled) * dot_nt(dz, second[...]) * valid
        pre_three[rows, :] = dy
        return carry[0] + col_sum(dy), carry[1] + col_sum(dy * normal)

    sums = each_image(geometry, second_back, nothing)
    sums_one = total(5, sums)
    grads[pl.ds(channels, channels), :] = dot_tn(hidden[...], out[...]).astype(grads.dtype)

    def flow_copy(i, rows, step, incoming=False):
        peer = lax.rem(task + (tasks - step if incoming else step), tasks)
        return remote(
            out.at[rows, columns_of(peer, width)], arrived.at[step - 1, rows, :],
            sends.at[i, step], receives.at[i, step], peer, "task",
        )

    def first_back(i, rows, carry):
        valid = valid_rows(small[i], height, breadth)
        normal, inverse, _ = norm_with(pre_one[rows, :], totals_one, scale_one)
        dz = norm_back_with(
            pre_three[rows, :], normal, inverse, count, sums_one, scale_one, valid
        ).astype(BF)
        hidden[rows, :] = dz
        flow = (lower[rows, :] + dot_nt(dz, first[...])) * valid
        out[rows, :] = flow.astype(BF)
        for step in range(1, tasks):
            flow_copy(i, rows, step).start()
        return carry

    each_image(geometry, first_back, 0)
    grads[pl.ds(0, channels), :] = dot_tn(features[...], hidden[...]).astype(grads.dtype)

    def tap(p, carry):
        rows = pl.ds(pl.multiple_of((2 + p) * channels, channels), channels)
        grads[rows, :] = dot_tn(gated[...], nine[p]).astype(grads.dtype)
        return carry

    lax.fori_loop(0, 9, tap, 0)
    put_sums(norm_sums, sums_one + sums_two + sums_three)

    def settle(i, rows, carry):
        for step in range(1, tasks):
            flow_copy(i, rows, step, True).wait_recv()
        flow = out[rows, columns_of(task, width)].astype(F32)
        for step in range(1, tasks):
            flow = flow + arrived[step - 1, rows, :].astype(F32)
        upstream[rows, :] = flow
        for step in range(1, tasks):
            flow_copy(i, rows, step).wait_send()
        return carry

    each_image(geometry, settle, 0)


def head(geometry, tasks, batches, small, features, rows_in, cotangent, scales, counts):
    number, height, breadth = geometry
    pixels = height * breadth
    total, channels = features.shape
    width = channels // tasks
    return exchange_kernel(
        functools.partial(head_body, geometry, tasks, batches),
        [
            shape((number, pixels // 4, channels), BF),
            shape(rows_in.shape, BF),
            shape((total, width), F32),
            shape((8, channels), F32),
        ],
        "svvvvv",
        (small, features, rows_in, cotangent, scales, counts),
        [
            pltpu.VMEM(features.shape, F32),
            pltpu.VMEM(features.shape, F32),
            pltpu.VMEM(features.shape, F32),
            pltpu.VMEM(features.shape, BF),
            pltpu.VMEM(features.shape, BF),
            pltpu.VMEM((9,) + features.shape, BF),
            pltpu.VMEM((9, pixels, min(channels, 256)), F32),
            pltpu.VMEM(features.shape, F32),
            pltpu.VMEM(features.shape, BF),
            pltpu.VMEM((tasks - 1, total, width), BF),
        ]
        + [pltpu.SemaphoreType.DMA((number, tasks))] * 2
        + total_scratch(6, batches),
        2,
        60,
        flops=6 * total * channels * rows_in.shape[0],
    )


SUM_IN_KERNEL = False


def trunk_backward_body(
    geometry, tasks, batches, summing,
    small, upstream, enc_totals, dec_totals, scales, choose_row, *rest,
):
    kept, rest = rest[:6], rest[6:]
    if summing:
        head_grads, rest = rest[0], rest[1:]
    (enc_grad, dec_grad, flow_out, norm_sums), rest = rest[:4], rest[4:]
    if summing:
        head_owned, rest = rest[0], rest[1:]
    (x, enc_taps, dec_taps, enc_pre, dec_pre, spread), rest = rest[:6], rest[6:]
    (
        nine, change, packed, arrived, pooled, sends, receives,
        mine, slots, total_sends, total_receives, loaded,
    ) = rest[:12]
    head_stages = [lambda: None] * 3
    if summing:
        near, paired, far, near_send, near_receive, far_send, far_receive, own, own_loaded = rest[12:]
        place, core, chips = pair_place(batches)
        count = near.shape[1]

        def own_load(step):
            chip = lax.rem(place + step, chips)
            source = block_rows(head_grads, 2 * chip + core, count)
            return pltpu.make_async_copy(source, own.at[step], own_loaded.at[step])

        for step in range(chips):
            own_load(step).start()
        *head_stages, head_end = pair_sum(
            batches, lambda index: block_rows(head_grads, index, count),
            lambda step: own[step].astype(F32), near, paired, far,
            (near_send, near_receive, far_send, far_receive),
        )
    head_start, head_middle, head_relay = head_stages
    targets = (x, enc_taps, dec_taps, enc_pre, dec_pre, spread)
    loads = [pltpu.make_async_copy(a, b, loaded.at[k]) for k, (a, b) in enumerate(zip(kept, targets))]
    for k in (4, 2, 5, 3, 1, 0):
        loads[k].start()
    number, height, breadth = geometry
    channels = x.shape[1]
    width = enc_pre.shape[1]
    windows = window_count(height, breadth)
    task = lax.axis_index("task")
    _, col = places(height, breadth)
    widen = pool_choice(height, breadth, windows, False).astype(BF)
    narrow = pool_choice(height, breadth, windows, True)
    nothing = zero_rows(2, width)

    def total(k, rows):
        return total_rows(
            k, "batch", batches, list(rows), mine, slots, total_sends, total_receives
        )

    def change_of(pre, totals, scale, flow):
        def image(i, rows, carry):
            valid = valid_rows(small[i], height, breadth)
            normal, _, scaled = norm_with(pre[rows, :], totals, scale)
            dy = silu_back(scaled) * flow(i, rows) * valid
            change[rows, :] = dy
            return carry[0] + col_sum(dy), carry[1] + col_sum(dy * normal)

        return each_image(geometry, image, nothing)

    def back(pre, totals, scale, sums, taps, put):
        def image(i, rows, carry):
            valid = valid_rows(small[i], height, breadth)
            normal, inverse, _ = norm_with(pre[rows, :], totals, scale)
            dz = norm_back_with(change[rows, :], normal, inverse, totals[2], sums, scale, valid)
            for p, moved in enumerate(spread_taps(dz, breadth, col)):
                nine[rows, p * width : (p + 1) * width] = moved.astype(BF)
            put(i, rows, dot_nt(nine[rows, :], taps[...]) * valid)
            return carry

        each_image(geometry, image, 0)

    totals = rows_of(dec_totals, 0, 3)
    scale = rows_of(scales, 2, 2)
    loads[4].wait()
    sums = change_of(dec_pre, totals, scale, lambda i, rows: upstream[rows, :])
    greet((("task", tasks), ("batch", batches)))
    head_start()
    dec_sums = total(0, sums)
    if summing:
        for step in range(chips):
            own_load(step).wait()

    def copy_of(i, step, incoming=False):
        rows = window_rows(i, windows)
        peer = lax.rem(task + (tasks - step if incoming else step), tasks)
        return remote(
            packed.at[rows, columns_of(peer, width)], arrived.at[step - 1, rows, :],
            sends.at[i, step], receives.at[i, step], peer, "task",
        )

    def put_packed(i, rows, flow):
        chosen = (narrow * choose_row[i]).astype(BF)
        packed[window_rows(i, windows), :] = dot(chosen, flow.astype(BF)).astype(BF)
        for step in range(1, tasks):
            copy_of(i, step).start()

    loads[2].wait()
    back(dec_pre, totals, scale, dec_sums, dec_taps, put_packed)
    loads[5].wait()
    head_middle()
    dec_grad[...] = dot_tn(spread[...], nine[...])

    def collect(i, carry):
        for step in range(1, tasks):
            copy_of(i, step, True).wait_recv()
        rows = window_rows(i, windows)
        flow = packed[rows, columns_of(task, width)].astype(F32)
        for step in range(1, tasks):
            flow = flow + arrived[step - 1, rows, :].astype(F32)
        pooled[rows, :] = flow
        for step in range(1, tasks):
            copy_of(i, step).wait_send()
        return carry

    lax.fori_loop(0, number, collect, 0)

    def widened(i, rows):
        high, low = split(pooled[window_rows(i, windows), :])
        return (dot(widen, high) + dot(widen, low)) * 0.25

    totals = rows_of(enc_totals, 0, 3)
    scale = rows_of(scales, 0, 2)
    loads[3].wait()
    sums = change_of(enc_pre, totals, scale, widened)
    enc_sums = total(1, sums)
    head_relay()

    def put_flow(i, rows, flow):
        flow_out[rows, :] = flow.astype(BF)

    loads[1].wait()
    back(enc_pre, totals, scale, enc_sums, enc_taps, put_flow)
    loads[0].wait()
    enc_grad[...] = dot_tn(x[...], nine[...])
    put_sums(norm_sums, enc_sums + dec_sums)
    if summing:
        head_owned[...] = head_end().astype(BF)


def trunk_backward(
    geometry, tasks, batches, small, upstream, enc_totals, dec_totals, scales, choose_row,
    head_grads, kept,
):
    number, height, breadth = geometry
    x, enc_taps, dec_taps = kept[:3]
    total, channels = x.shape
    width = channels // tasks
    windows = window_count(height, breadth)
    head_rows = head_grads.shape[0]
    summing = SUM_IN_KERNEL and head_rows % (16 * batches) == 0
    outs = [
        shape(enc_taps.shape, F32),
        shape(dec_taps.shape, F32),
        shape(x.shape, BF),
        shape((8, width), F32),
    ]
    specs = "svvvvvhhhhhh"
    args = (small, upstream, enc_totals, dec_totals, scales, choose_row, *kept)
    scratch = []
    if summing:
        outs.append(shape((head_rows // batches, channels), BF))
        specs += "h"
        args += (head_grads,)
        scratch = pair_scratch(batches, head_rows, channels, BF) + [
            pltpu.VMEM((batches // 2, head_rows // batches, channels), BF),
            pltpu.SemaphoreType.DMA((batches // 2,)),
        ]
    made = exchange_kernel(
        functools.partial(trunk_backward_body, geometry, tasks, batches, summing),
        outs,
        specs,
        args,
        [pltpu.VMEM(a.shape, a.dtype) for a in kept]
        + [
            pltpu.VMEM((total, 9 * width), BF),
            pltpu.VMEM((total, width), F32),
            pltpu.VMEM((number * windows, channels), BF),
            pltpu.VMEM((tasks - 1, number * windows, width), BF),
            pltpu.VMEM((number * windows, width), F32),
        ]
        + [pltpu.SemaphoreType.DMA((number, tasks))] * 2
        + total_scratch(2, batches)
        + [pltpu.SemaphoreType.DMA((6,))]
        + scratch,
        3,
        60,
        flops=8 * x.size * enc_taps.shape[1],
    )
    if summing:
        return made
    return *made, lax.psum_scatter(head_grads, "batch", scatter_dimension=0, tiled=True)


def to_taps_body(index, slots, enc, dec, wide, tap):
    count = slots.shape[0]
    channels = enc.shape[0]
    width = slots.shape[1]
    step = 1024

    def widen(i, carry):
        rows = pl.ds(pl.multiple_of(i * step, step), step)
        wide[rows, :] = slots[rows, :].astype(F32)
        return carry

    lax.fori_loop(0, count // step, widen, 0)
    group = 32
    for p in range(18):

        def fetch(i, carry):
            base = i * group
            for u in range(group):
                tap[pl.ds(base + u, 1), :] = wide[pl.ds(index[p * channels + base + u], 1), :]
            return carry

        lax.fori_loop(0, channels // group, fetch, 0)
        out = enc if p < 9 else dec
        q = p % 9
        out[:, q * width : (q + 1) * width] = tap[...].astype(BF)


def to_taps(index, slots, channels):
    width = slots.shape[1]
    return run(
        to_taps_body,
        [shape((channels, 9 * width), BF)] * 2,
        "sv",
        (index, slots),
        [pltpu.VMEM(slots.shape, F32), pltpu.VMEM((channels, width), F32)],
        vmem=60,
        flops=10000 * MIB,
    )


def to_slots_body(index, enc, dec, slots, wide):
    count = slots.shape[0]
    channels = enc.shape[0]
    width = slots.shape[1]
    step = 1024
    group = 32
    for p in range(18):
        source = enc if p < 9 else dec
        q = p % 9

        def place(i, carry):
            base = pl.multiple_of(i * group, group)
            values = source[pl.ds(base, group), q * width : (q + 1) * width]
            for u in range(group):
                wide[pl.ds(index[p * channels + base + u], 1), :] = values[u : u + 1, :]
            return carry

        lax.fori_loop(0, channels // group, place, 0)

    def narrow(i, carry):
        rows = pl.ds(pl.multiple_of(i * step, step), step)
        slots[rows, :] = wide[rows, :].astype(BF)
        return carry

    lax.fori_loop(0, count // step, narrow, 0)


def to_slots(index, enc, dec):
    width = enc.shape[1] // 9
    dims = (index.shape[0], width)
    return run(
        to_slots_body, [shape(dims, BF)], "svv", (index, enc, dec), [pltpu.VMEM(dims, F32)], vmem=60
    )[0]


def adam(gradient, moment_one, moment_two):
    new_one = BETA_ONE * moment_one + (1.0 - BETA_ONE) * gradient
    new_two = BETA_TWO * moment_two + (1.0 - BETA_TWO) * gradient * gradient
    direction = (
        new_one / (1.0 - BETA_ONE**STEP) / (jnp.sqrt(new_two / (1.0 - BETA_TWO**STEP)) + ADAM_EPS)
    )
    return new_one, new_two, direction


def pair_place(batches):
    me = lax.axis_index("batch")
    place = lax.div(me, 2)
    return place, me - 2 * place, batches // 2


def greet_pairs(tasks, batches):
    place, core, chips = pair_place(batches)
    task = lax.axis_index("task")
    barrier = pltpu.get_barrier_semaphore()

    def signal(device):
        pl.semaphore_signal(barrier, inc=1, device_id=device, device_id_type=MESH)

    for step in range(1, tasks):
        signal({"task": lax.rem(task + step, tasks)})
    signal({"batch": 2 * place + 1 - core})
    for step in range(1, chips):
        signal({"batch": 2 * lax.rem(place + step, chips) + core})
    pl.semaphore_wait(barrier, tasks - 1 + chips)


def block_rows(ref, index, count):
    return ref.at[pl.ds(pl.multiple_of(index * count, 8), count), :]


def far_first(chips):
    return sorted(range(chips), key=lambda step: -min(step, chips - step))


def pair_sum(batches, rows_of_block, own_block, near, paired, far, sems):
    place, core, chips = pair_place(batches)
    count = near.shape[1]
    near_send, near_receive, far_send, far_receive = sems
    other = 2 * place + 1 - core
    ring = chips == 4 and count % 32 == 0
    half = count // 2
    halves = (pl.ds(0, half), pl.ds(half, half))

    def near_copy(step):
        chip = lax.rem(place + step, chips)
        return remote(rows_of_block(2 * chip + 1 - core), near.at[step],
                      near_send.at[step], near_receive.at[step], other, "batch")

    def far_copy(step, incoming=False):
        chip = lax.rem(place + (chips - step if incoming else step), chips)
        return remote(paired.at[step], far.at[step], far_send.at[step], far_receive.at[step],
                      2 * chip + core, "batch")

    def ring_copy(which, way):
        chip = lax.rem(place + (1 if way == 0 else chips - 1), chips)
        if which == 0:
            source, target = paired.at[2, halves[way], :], far.at[2 + way, halves[0], :]
        else:
            cut = halves[way] if which == 2 else halves[1 - way]
            source, target = paired.at[1 if way == 0 else 3, cut, :], far.at[way, cut, :]
        k = 2 * which + way
        return remote(source, target, far_send.at[k], far_receive.at[k], 2 * chip + core, "batch")

    def start():
        for step in far_first(chips):
            near_copy(step).start()

    def middle():
        for step in far_first(chips):
            near_copy(step).wait_recv()
            if step:
                paired[step] = (own_block(step) + near[step].astype(F32)).astype(paired.dtype)
                if not ring:
                    far_copy(step).start()
                elif step == 2:
                    ring_copy(0, 0).start()
                    ring_copy(0, 1).start()
                else:
                    ring_copy(1, 0 if step == 1 else 1).start()

    def relay():
        if not ring:
            return
        for way in range(2):
            ring_copy(0, way).wait_recv()
            step = 1 if way == 0 else 3
            total = paired[step, halves[way], :].astype(F32) + far[2 + way, halves[0], :].astype(F32)
            paired[step, halves[way], :] = total.astype(paired.dtype)
            ring_copy(2, way).start()

    def end():
        total = own_block(0) + near[0].astype(F32)
        if ring:
            for way in range(2):
                ring_copy(1, way).wait_recv()
                ring_copy(2, way).wait_recv()
                total = total + far[way].astype(F32)
            for k in range(3):
                for way in range(2):
                    ring_copy(k, way).wait_send()
        else:
            for step in range(1, chips):
                far_copy(step, True).wait_recv()
                total = total + far[step].astype(F32)
            for step in range(1, chips):
                far_copy(step).wait_send()
        for step in range(chips):
            near_copy(step).wait_send()
        return total

    return start, middle, relay, end


def blocks_in(source, batches, count):
    place, core, chips = pair_place(batches)

    def own(step):
        chip = lax.rem(place + step, chips)
        return block_rows(source, 2 * chip + core, count)[...].astype(F32)

    return (lambda index: block_rows(source, index, count)), own


def pair_scratch(batches, rows, width, kind):
    chips = batches // 2
    return [pltpu.VMEM((chips, rows // batches, width), kind)] * 3 + [
        pltpu.SemaphoreType.DMA((max(chips, 6),))
    ] * 4


def chip_spread(batches, block, sends, receives):
    place, core, chips = pair_place(batches)
    count = block(place).shape[0]
    ring = chips == 4 and count % 32 == 0
    half = count // 2

    def copy(step, incoming=False):
        peer = lax.rem(place + (chips - step if incoming else step), chips)
        ref = block(peer if incoming else place)
        return remote(ref, ref, sends.at[step], receives.at[step], 2 * peer + core, "batch")

    def pass_on(way, incoming=False):
        step = 1 if way == 0 else chips - 1
        peer = lax.rem(place + (chips - step if incoming else step), chips)
        home = lax.rem(place + (2 if incoming else chips - step), chips)
        ref = block(home).at[pl.ds(way * half, half), :]
        k = 2 if way == 0 else 0
        return remote(ref, ref, sends.at[k], receives.at[k], 2 * peer + core, "batch")

    steps = (1, chips - 1) if ring else tuple(range(1, chips))

    def start():
        for step in steps:
            copy(step).start()

    def relay():
        if ring:
            for way, step in enumerate(steps):
                copy(step, True).wait_recv()
                pass_on(way).start()

    def settle():
        if ring:
            for way in range(2):
                pass_on(way, True).wait_recv()
        else:
            for step in steps:
                copy(step, True).wait_recv()

    def drain():
        for step in steps:
            copy(step).wait_send()
        if ring:
            for way in range(2):
                pass_on(way).wait_send()

    return start, relay, settle, drain


def arrive_body(
    tasks, batches,
    image, info, weight,
    slots, x, infos,
    raw, raw_loaded, x_send, x_receive, info_send, info_receive,
    chip_send, chip_receive, pair_send, pair_receive, own,
):
    task = lax.axis_index("task")
    place, core, chips = pair_place(batches)
    count, width = raw.shape
    load = pltpu.make_async_copy(weight.at[:, columns_of(task, width)], raw, raw_loaded)
    load.start()
    greet_pairs(tasks, batches)

    def task_copy(source, target, sends, receives, step, incoming=False):
        peer = lax.rem(task + (tasks - step if incoming else step), tasks)
        home = peer if incoming else task
        return remote(source, block_rows(target, home, source.shape[0]), sends.at[step],
                      receives.at[step], peer, "task")

    def moves(step, incoming=False):
        return (
            task_copy(info, infos, info_send, info_receive, step, incoming),
            task_copy(image, x, x_send, x_receive, step, incoming),
        )

    def block(chip):
        return block_rows(slots, 2 * chip + core, count)

    def pair_copy(hop, incoming=False):
        chip = lax.rem(place + chips - hop, chips)
        ref = block_rows(slots, 2 * chip + (1 - core if incoming else core), count)
        return remote(ref, ref, pair_send.at[hop], pair_receive.at[hop], 2 * place + 1 - core, "batch")

    start, relay, settle, drain = chip_spread(batches, block, chip_send, chip_receive)
    load.wait()
    block(place)[...] = raw[...].astype(BF)
    start()
    pair_copy(0).start()
    for step in range(1, tasks):
        for copy in moves(step):
            copy.start()
    locals_ = [
        pltpu.make_async_copy(image, block_rows(x, task, image.shape[0]), own.at[0]),
        pltpu.make_async_copy(info, block_rows(infos, task, info.shape[0]), own.at[1]),
    ]
    for copy in locals_:
        copy.start()
    relay()
    if chips == 4 and count % 32 == 0:
        pair_copy(1).start()
        pair_copy(3).start()
        settle()
        pair_copy(2).start()
    else:
        settle()
        for hop in range(1, chips):
            pair_copy(hop).start()
    for copy in locals_:
        copy.wait()
    for step in range(1, tasks):
        for copy in moves(step, True):
            copy.wait_recv()
    for hop in range(chips):
        pair_copy(hop, True).wait_recv()
    for step in range(1, tasks):
        for copy in moves(step):
            copy.wait_send()
    for hop in range(chips):
        pair_copy(hop).wait_send()
    drain()


def arrive(tasks, batches, image, info, weight):
    count, channels = weight.shape
    width = channels // tasks
    chips = batches // 2
    return exchange_kernel(
        functools.partial(arrive_body, tasks, batches),
        [
            shape((count * batches, width), BF),
            shape((image.shape[0] * tasks, channels), BF),
            shape((info.shape[0] * tasks, info.shape[1]), F32),
        ],
        "vvh",
        (image, info, weight),
        [pltpu.VMEM((count, width), F32), pltpu.SemaphoreType.DMA]
        + [pltpu.SemaphoreType.DMA((tasks,))] * 4
        + [pltpu.SemaphoreType.DMA((max(chips, 4),))] * 4
        + [pltpu.SemaphoreType.DMA((2,))],
        4,
        60,
        flops=20000 * MIB,
    )


def collect_body(
    tasks, batches,
    slots, flow, sums,
    input_grad, owned, part, norm_sums,
    near, paired, far, near_send, near_receive, far_send, far_receive,
    flow_in, flow_send, flow_receive, send, receive, sum_send, sum_receive,
):
    task = lax.axis_index("task")
    width = part.shape[1]
    pixels = input_grad.shape[0]

    def peer_of(step, incoming):
        return lax.rem(task + (tasks - step if incoming else step), tasks)

    def flow_copy(step, incoming=False):
        peer = peer_of(step, incoming)
        return remote(block_rows(flow, peer, pixels), flow_in.at[step - 1], flow_send.at[step],
                      flow_receive.at[step], peer, "task")

    def sum_copy(step, incoming=False):
        peer = peer_of(step, incoming)
        home = peer if incoming else task
        return remote(sums, norm_sums.at[:, columns_of(home, width)], sum_send.at[step],
                      sum_receive.at[step], peer, "task")

    def part_copy(step, incoming=False):
        peer = peer_of(step, incoming)
        home = peer if incoming else task
        return remote(part, owned.at[:, columns_of(home, width)], send.at[step], receive.at[step],
                      peer, "task")

    greet_pairs(tasks, batches)
    start, middle, relay, end = pair_sum(
        batches, *blocks_in(slots, batches, near.shape[1]), near, paired, far,
        (near_send, near_receive, far_send, far_receive),
    )
    start()
    for step in range(1, tasks):
        sum_copy(step).start()
        flow_copy(step).start()
    norm_sums[:, columns_of(task, width)] = sums[...]
    middle()
    relay()
    total = end().astype(BF)
    part[...] = total
    for step in range(1, tasks):
        part_copy(step).start()
    owned[:, columns_of(task, width)] = total
    total = block_rows(flow, task, pixels)[...].astype(F32)
    for step in range(1, tasks):
        flow_copy(step, True).wait_recv()
        total = total + flow_in[step - 1].astype(F32)
    input_grad[...] = total
    for step in range(1, tasks):
        sum_copy(step, True).wait_recv()
        part_copy(step, True).wait_recv()
        sum_copy(step).wait_send()
        part_copy(step).wait_send()
        flow_copy(step).wait_send()


def collect(tasks, batches, slots, flow, sums):
    count, width = slots.shape
    rows = count // batches
    pixels, channels = flow.shape[0] // tasks, flow.shape[1]
    return exchange_kernel(
        functools.partial(collect_body, tasks, batches),
        [
            shape((pixels, channels), F32),
            shape((rows, channels), BF),
            shape((rows, width), BF),
            shape((8, channels), F32),
        ],
        "vvv",
        (slots, flow, sums),
        pair_scratch(batches, count, width, BF)
        + [pltpu.VMEM((tasks - 1, pixels, channels), BF)]
        + [pltpu.SemaphoreType.DMA((tasks,))] * 6,
        5,
        60,
        flops=20000 * MIB,
    )


def soap_rows(cuts, grad, owners, state, low, first):
    count = owners.shape[1]
    total = grad.shape[0]

    def chunk(i, carry):
        rows = pl.ds(pl.multiple_of(i * (total // cuts), 8), total // cuts)
        values = grad[rows, :].astype(F32)
        rotated = None
        for m in range(count):
            part = dot((values * owners[rows, m : m + 1]).astype(BF), low[first + m])
            rotated = part if rotated is None else rotated + part
        new_one, new_two, direction = adam(rotated, state[1, rows, :], state[2, rows, :])
        state[1, rows, :] = new_one
        state[2, rows, :] = new_two
        stepped = None
        for m in range(count):
            part = dot_nt((direction * owners[rows, m : m + 1]).astype(BF), low[first + m])
            stepped = part if stepped is None else stepped + part
        old = state[0, rows, :]
        state[0, rows, :] = old - LEARN_MATRIX * (stepped + DECAY_MATRIX * old)
        return carry

    lax.fori_loop(0, cuts, chunk, 0)


def factor_rows(values, identity, turn):
    size, width = values.shape
    sub = lax.broadcasted_iota(jnp.int32, (size, width), 0)
    rolled = pltpu.roll(values, turn, 1)
    columns = [jnp.broadcast_to(rolled[:, j : j + 1], (size, width)) for j in range(size)]
    scale = jnp.zeros((size, width), F32)
    for j in range(size):
        root = lax.rsqrt(columns[j][j : j + 1, :])
        scale = jnp.where(sub == j, root, scale)
        lower = jnp.where(sub > j, columns[j] * root, 0.0)
        values = values - lower * (values[j : j + 1, :] * root)
        identity = identity - lower * (identity[j : j + 1, :] * root)
        for i in range(j + 1, size):
            columns[i] = columns[i] - lower * (columns[i][j : j + 1, :] * root)
    return values * scale, identity * scale


GROUP = 16
PANEL = 128


def renew_panel(k, product, made, tables, inverses):
    count, size = product.shape[0], product.shape[1]
    here = slice(k * PANEL, (k + 1) * PANEL)
    row = lax.broadcasted_iota(jnp.int32, (PANEL, PANEL), 0)
    col = lax.broadcasted_iota(jnp.int32, (PANEL, PANEL), 1)
    unit = jnp.where(row == col, 1.0, 0.0).astype(F32)
    for n in range(count):
        tables[n][:, :PANEL] = dot3(dot_tn, product[n, :, here], product[n, :, here])
        tables[n][:, PANEL:] = unit

    def group(q, carry):
        rows = pl.ds(pl.multiple_of(q * GROUP, GROUP), GROUP)
        turn = lax.rem(PANEL - q * GROUP, PANEL)
        done = [
            factor_rows(tables[n][rows, :PANEL], tables[n][rows, PANEL:], turn)
            for n in range(count)
        ]
        for n in range(count):
            upper, inverse = done[n]
            inverses[n][rows, :] = inverse
            both = jnp.concatenate([upper, inverse], axis=1)
            tables[n][...] = tables[n][...] - dot3(dot_tn, upper, both)
        return carry

    lax.fori_loop(0, PANEL // GROUP, group, 0)
    for n in range(count):
        turned = dot3(dot_nt, product[n, :, here], inverses[n][...])
        made[n, :, here] = turned
        if k < size // PANEL - 1:
            rest = slice((k + 1) * PANEL, size)
            product[n, :, rest] = product[n, :, rest] - dot3(
                dot, turned, dot3(dot_tn, turned, product[n, :, rest])
            )


def rows_body(
    tasks, batches, cuts,
    grad, part, owners, head_grad, head_owners,
    weight, one, two, head_weight, head_one, head_two, basis, head_basis,
    state_new, head_state_new, grams, head_grams,
    state, head_state, mine, head_mine, bases, low,
    near, paired, far, near_send, near_receive, far_send, far_receive,
    head_near, head_paired, head_far, *rest,
):
    head_sems = rest[:4]
    chip_send, chip_receive, task_send, task_receive, pair_send, pair_receive, load, save = rest[4:]
    task = lax.axis_index("task")
    place, core, chips = pair_place(batches)
    width = part.shape[1]
    channels = grad.shape[1]
    count, head_count = near.shape[1], head_near.shape[1]
    trunk_total, head_total = owners.shape[1], head_owners.shape[1]

    moves = [
        (basis, bases.at[pl.ds(0, trunk_total)]),
        (head_basis, bases.at[pl.ds(trunk_total, head_total)]),
        (weight, state.at[0]),
        (one, state.at[1]),
        (two, state.at[2]),
        (head_weight, head_state.at[0]),
        (head_one, head_state.at[1]),
        (head_two, head_state.at[2]),
    ]
    loads = [pltpu.make_async_copy(a, b, load.at[k]) for k, (a, b) in enumerate(moves)]
    for copy in loads:
        copy.start()
    for m in range(head_total):
        held = (head_grad[...].astype(F32) * head_owners[:, m : m + 1]).astype(BF)
        head_mine[m * channels : (m + 1) * channels, :] = dot_tn(held, head_grad[...]).astype(
            head_mine.dtype
        )
    greet_pairs(tasks, batches)
    head_start, head_middle, head_relay, head_end = pair_sum(
        batches, *blocks_in(head_mine, batches, head_count), head_near, head_paired, head_far,
        head_sems,
    )
    head_start()
    for m in range(trunk_total):
        held = (grad[...].astype(F32) * owners[:, m : m + 1]).astype(BF)
        mine[m * channels : (m + 1) * channels, :] = dot_tn(held, part[...]).astype(mine.dtype)
    start, middle, relay, end = pair_sum(
        batches, *blocks_in(mine, batches, count), near, paired, far,
        (near_send, near_receive, far_send, far_receive),
    )
    start()
    head_middle()
    middle()
    head_relay()
    relay()

    def trunk_block(chip, home, which):
        rows = pl.ds(pl.multiple_of((2 * chip + which) * count, 8), count)
        return grams.at[rows, columns_of(home, width)]

    def head_block(chip, which):
        return block_rows(head_grams, 2 * chip + which, head_count)

    trunk_spread = chip_spread(
        batches, lambda chip: trunk_block(chip, task, core), chip_send.at[0], chip_receive.at[0]
    )
    head_spread = chip_spread(
        batches, lambda chip: head_block(chip, core), chip_send.at[1], chip_receive.at[1]
    )

    def task_copy(step, hop, incoming=False):
        peer = lax.rem(task + (tasks - step if incoming else step), tasks)
        chip = lax.rem(place + chips - hop, chips)
        block = trunk_block(chip, peer if incoming else task, core)
        return remote(block, block, task_send.at[step, hop], task_receive.at[step, hop], peer, "task")

    def pair_copy(kind, hop, incoming=False):
        chip = lax.rem(place + chips - hop, chips)
        which = 1 - core if incoming else core
        home = lax.rem(task + tasks - kind, tasks)
        block = head_block(chip, which) if kind == tasks else trunk_block(chip, home, which)
        return remote(block, block, pair_send.at[kind, hop], pair_receive.at[kind, hop],
                      2 * place + 1 - core, "batch")

    for copy in loads[:5]:
        copy.wait()
    for m in range(trunk_total + head_total):
        low[m] = bases[m].astype(BF)
    total = end().astype(grams.dtype)
    trunk_block(place, task, core)[...] = total
    trunk_spread[0]()
    for step in range(1, tasks):
        task_copy(step, 0).start()
    pair_copy(0, 0).start()
    soap_rows(cuts, grad, owners, state, low, 0)
    saves = [
        pltpu.make_async_copy(state, state_new, save.at[0]),
        pltpu.make_async_copy(head_state, head_state_new, save.at[1]),
    ]
    saves[0].start()
    total = head_end().astype(head_grams.dtype)
    head_block(place, core)[...] = total
    head_spread[0]()
    pair_copy(tasks, 0).start()
    trunk_spread[1]()
    trunk_spread[2]()
    for hop in range(1, chips):
        for step in range(1, tasks):
            task_copy(step, hop).start()
        pair_copy(0, hop).start()
    head_spread[1]()
    for copy in loads[5:]:
        copy.wait()
    soap_rows(cuts, head_grad, head_owners, head_state, low, trunk_total)
    saves[1].start()
    for hop in range(chips):
        for step in range(1, tasks):
            task_copy(step, hop, True).wait_recv()
            pair_copy(step, hop).start()
    head_spread[2]()
    for hop in range(1, chips):
        pair_copy(tasks, hop).start()
    for hop in range(chips):
        for kind in range(tasks + 1):
            pair_copy(kind, hop, True).wait_recv()
    for copy in saves:
        copy.wait()
    for hop in range(chips):
        for kind in range(tasks + 1):
            pair_copy(kind, hop).wait_send()
        for step in range(1, tasks):
            task_copy(step, hop).wait_send()
    trunk_spread[3]()
    head_spread[3]()


def renew_body(
    state, head_state, grams, head_grams, stat, head_stat, basis, head_basis,
    weight_new, one_new, two_new, head_weight_new, head_one_new, head_two_new,
    stat_new, head_stat_new, basis_new, head_basis_new,
    stats, product, made, held, head_held, load, save, *work,
):
    trunk_total, head_total = stat.shape[0], head_stat.shape[0]
    channels = stat.shape[1]
    count = trunk_total + head_total
    tables, inverses = work[:count], work[count:]
    loads = [
        pltpu.make_async_copy(state, held, load.at[0]),
        pltpu.make_async_copy(head_state, head_held, load.at[1]),
    ]
    for copy in loads:
        copy.start()
    sources = [held.at[k] for k in range(3)] + [head_held.at[k] for k in range(3)]
    targets = [weight_new, one_new, two_new, head_weight_new, head_one_new, head_two_new]
    saves = [pltpu.make_async_copy(a, b, save.at[k]) for k, (a, b) in enumerate(zip(sources, targets))]
    for m in range(count):
        first = m < trunk_total
        place = m if first else m - trunk_total
        gram = (grams if first else head_grams)[place * channels : (place + 1) * channels, :]
        old = (stat if first else head_stat)[place]
        stats[m] = STAT_DECAY * old + (1.0 - STAT_DECAY) * gram.astype(F32)
        product[m] = dot3(dot, stats[m], (basis if first else head_basis)[place])
    groups = ((0, trunk_total, stat_new, basis_new), (trunk_total, head_total, head_stat_new, head_basis_new))
    for begin, size, out, _ in groups:
        copy = pltpu.make_async_copy(stats.at[pl.ds(begin, size)], out, save.at[len(saves)])
        copy.start()
        saves.append(copy)
    for copy in loads:
        copy.wait()
    for copy in saves[:6]:
        copy.start()
    for k in range(channels // PANEL):
        renew_panel(k, product, made, tables, inverses)
        cut = pl.ds(k * PANEL, PANEL)
        for begin, size, _, out in groups:
            copy = pltpu.make_async_copy(
                made.at[pl.ds(begin, size), :, cut], out.at[:, :, cut], save.at[len(saves)]
            )
            copy.start()
            saves.append(copy)
    for copy in saves:
        copy.wait()


def finish(tasks, batches, local_grads, rows, matrices):
    grad, part, owners, head_grad, head_owners = local_grads
    stat, head_stat, basis, head_basis = matrices
    channels, width = grad.shape[1], part.shape[1]
    trunk_total, head_total = owners.shape[1], head_owners.shape[1]
    gram_rows, head_rows = trunk_total * channels, head_total * channels
    chips = batches // 2
    kind = BF if gram_rows % (16 * batches) == 0 else F32
    head_kind = BF if head_rows % (16 * batches) == 0 else F32
    cuts = 4 if grad.shape[0] % 64 == 0 and head_grad.shape[0] % 64 == 0 else 1
    square = (trunk_total + head_total, channels, channels)
    made = exchange_kernel(
        functools.partial(rows_body, tasks, batches, cuts),
        [
            shape((3,) + grad.shape, F32),
            shape((3,) + head_grad.shape, F32),
            shape((gram_rows, channels), kind),
            shape((head_rows, channels), head_kind),
        ],
        "vvvvvhhhhhhhh",
        (*local_grads, *rows, basis, head_basis),
        [
            pltpu.VMEM((3,) + grad.shape, F32),
            pltpu.VMEM((3,) + head_grad.shape, F32),
            pltpu.VMEM((gram_rows, width), kind),
            pltpu.VMEM((head_rows, channels), head_kind),
            pltpu.VMEM(square, F32),
            pltpu.VMEM(square, BF),
        ]
        + pair_scratch(batches, gram_rows, width, kind)
        + pair_scratch(batches, head_rows, channels, head_kind)
        + [pltpu.SemaphoreType.DMA((2, max(chips, 4)))] * 2
        + [pltpu.SemaphoreType.DMA((tasks, chips))] * 2
        + [pltpu.SemaphoreType.DMA((tasks + 1, chips))] * 2
        + [pltpu.SemaphoreType.DMA((8,)), pltpu.SemaphoreType.DMA((2,))],
        6,
        60,
        flops=50000 * MIB,
        places_out="hhvv",
    )
    outs = [shape(a.shape, F32) for a in (*rows, *matrices)]
    hbm = pl.BlockSpec(memory_space=pltpu.HBM)
    count = trunk_total + head_total
    return pl.pallas_call(
        renew_body,
        out_shape=tuple(outs),
        in_specs=[hbm] * 2 + [VMEM_SPEC] * 6,
        out_specs=tuple(hbm for _ in outs),
        scratch_shapes=[pltpu.VMEM(square, F32)] * 3
        + [pltpu.VMEM(made[0].shape, F32), pltpu.VMEM(made[1].shape, F32)]
        + [pltpu.SemaphoreType.DMA((2,))]
        + [pltpu.SemaphoreType.DMA((8 + 2 * (channels // PANEL),))]
        + [pltpu.VMEM((PANEL, 2 * PANEL), F32)] * count
        + [pltpu.VMEM((PANEL, PANEL), F32)] * count,
        compiler_params=pltpu.CompilerParams(vmem_limit_bytes=60 * MIB),
        cost_estimate=pl.CostEstimate(
            flops=60000 * MIB, bytes_accessed=64 * MIB, transcendentals=0
        ),
    )(*made, *matrices)


def local(
    tasks,
    batches,
    images,
    image_small,
    pool_index,
    row_slot,
    trunk_weight,
    trunk_mean_grad,
    trunk_mean_square,
    trunk_statistic,
    trunk_basis,
    head_weight,
    head_mean_grad,
    head_mean_square,
    head_statistic,
    head_basis,
    trunk_gain,
    trunk_offset,
    trunk_norm_mean_grad,
    trunk_norm_mean_square,
    head_gain,
    head_offset,
    head_norm_mean_grad,
    head_norm_mean_square,
    cotangent,
):
    number, height, breadth, channels = images.shape
    pixels = height * breadth
    tap_rows = 9 * channels
    shown = tasks * number
    geometry = (shown, height, breadth)
    task = lax.axis_index("task")
    batch = lax.axis_index("batch")
    width = channels // tasks

    def quarter(values):
        return lax.dynamic_slice_in_dim(values, task * width, width, values.ndim - 1)

    def inside(flags):
        row_limit = jnp.where(flags > 0, height // 2, height)[:, None, None]
        col_limit = jnp.where(flags > 0, breadth // 2, breadth)[:, None, None]
        return (jnp.arange(height, dtype=jnp.int32)[None, :, None] < row_limit) & (
            jnp.arange(breadth, dtype=jnp.int32)[None, None, :] < col_limit
        )

    cell = 2 * jnp.arange(2, dtype=jnp.int32)[:, None, None] + jnp.arange(2, dtype=jnp.int32)
    cells = pool_index.reshape(number, height // 2, 1, breadth // 2, 1)
    valid = inside(image_small)
    chosen = ((cells == cell).reshape(number, height, breadth) & valid).reshape(number, pixels)
    info = jnp.zeros((8 * number, channels), F32)
    info = info.at[::8, :pixels].set(chosen.astype(F32))
    info = info.at[1::8, 0].set(image_small.astype(F32))
    masked = (images * valid[..., None].astype(BF)).reshape(number * pixels, channels)
    slots, x, infos = arrive(tasks, batches, masked, info, trunk_weight)
    head_low = head_weight.astype(BF)
    slots, head_low = lax.optimization_barrier((slots, head_low))
    head_rows = lax.all_gather(head_low, "batch", axis=1, tiled=True)[0]
    infos = infos.reshape(shown, 8, channels)
    small = infos[:, 1, 0].astype(jnp.int32)
    choose_row = infos[:, :1, :pixels]
    choose = choose_row.reshape(shown * pixels, 1)
    enc_taps, dec_taps = to_taps(row_slot, slots, channels)

    local_rows = trunk_weight.shape[0]
    slot_ids = batch * local_rows + jnp.arange(local_rows, dtype=jnp.int32)
    decoded = jnp.any(row_slot[tap_rows:][None, :] == slot_ids[:, None], axis=1)
    trunk_onehot = jnp.stack([~decoded, decoded], axis=1).astype(F32)
    x, trunk_onehot = lax.optimization_barrier((x, trunk_onehot))

    scales = quarter(jnp.stack([trunk_gain, trunk_offset], axis=1)).reshape(4, width)
    enc_totals, dec_totals, features, *kept = trunk_forward(
        geometry, tasks, batches, small, x, enc_taps, dec_taps, scales, choose
    )
    head_scales = jnp.stack([head_gain[0], head_offset[0]], axis=1).reshape(6, channels)
    pooled, head_grads, upstream, head_sums = head(
        geometry, tasks, batches, small, features, head_rows,
        cotangent.reshape(shown, pixels // 4, channels), head_scales, enc_totals,
    )
    task_features = pooled.reshape(cotangent.shape)
    enc_grad, dec_grad, flow, trunk_sums, head_owned = trunk_backward(
        geometry, tasks, batches, small, upstream, enc_totals, dec_totals, scales, choose_row,
        head_grads, kept,
    )
    input_grad, trunk_owned, trunk_part, norm_sums = collect(
        tasks, batches, to_slots(row_slot, enc_grad, dec_grad), flow, trunk_sums
    )
    input_grad = input_grad.reshape(images.shape)

    head_local = head_weight.shape[1]
    head_ids = batch * head_local + jnp.arange(head_local, dtype=jnp.int32)
    head_owner = jnp.minimum(head_ids // channels, 2)
    head_onehot = (head_owner[:, None] == jnp.arange(3, dtype=jnp.int32)).astype(F32)
    (
        trunk_weight_new, trunk_one_new, trunk_two_new,
        head_weight_new, head_one_new, head_two_new,
        trunk_stat_new, head_stat_new, trunk_basis_new, head_basis_new,
    ) = finish(
        tasks, batches,
        (trunk_owned, trunk_part, trunk_onehot, head_owned, head_onehot),
        (trunk_weight, trunk_mean_grad, trunk_mean_square,
         head_weight[0], head_mean_grad[0], head_mean_square[0]),
        (trunk_statistic, head_statistic[0], trunk_basis, head_basis[0]),
    )

    trunk_norm = jnp.stack([trunk_gain, trunk_offset], axis=1)
    trunk_norm_grad = norm_sums[:4].reshape(2, 2, channels)[:, ::-1]
    trunk_norm_one, trunk_norm_two, trunk_direction = adam(
        trunk_norm_grad, trunk_norm_mean_grad, trunk_norm_mean_square
    )
    head_norm = jnp.stack([head_gain, head_offset], axis=2)
    head_norm_grad = head_sums[:6].reshape(1, 3, 2, channels)[:, :, ::-1]
    head_norm_one, head_norm_two, head_direction = adam(
        head_norm_grad, head_norm_mean_grad, head_norm_mean_square
    )
    return (
        task_features,
        input_grad,
        trunk_weight_new,
        trunk_one_new,
        trunk_two_new,
        trunk_stat_new,
        trunk_basis_new,
        head_weight_new[None],
        head_one_new[None],
        head_two_new[None],
        head_stat_new[None],
        head_basis_new[None],
        trunk_norm - LEARN_NORM * trunk_direction,
        trunk_norm_one,
        trunk_norm_two,
        head_norm - LEARN_NORM * head_direction,
        head_norm_one,
        head_norm_two,
    )


def solution(mesh):
    placed = (
        P(("task", "batch"), None, None, None),
        P(("task", "batch")),
        P(("task", "batch"), None, None),
        P(),
        P("batch", None),
        P("batch", None),
        P("batch", None),
        P(),
        P(),
        P("task", "batch", None),
        P("task", "batch", None),
        P("task", "batch", None),
        P("task", None, None, None),
        P("task", None, None, None),
        P(),
        P(),
        P(),
        P(),
        P("task", None, None),
        P("task", None, None),
        P("task", None, None, None),
        P("task", None, None, None),
        P("task", None, "batch", None, None, None),
    )
    return jax.shard_map(
        functools.partial(local, mesh.shape["task"], mesh.shape["batch"]),
        mesh=mesh,
        in_specs=placed,
        out_specs=(
            P("task", None, "batch", None, None, None),
            P(("task", "batch"), None, None, None),
            P("batch", None),
            P("batch", None),
            P("batch", None),
            P(),
            P(),
            P("task", "batch", None),
            P("task", "batch", None),
            P("task", "batch", None),
            P("task", None, None, None),
            P("task", None, None, None),
            P(),
            P(),
            P(),
            P("task", None, None, None),
            P("task", None, None, None),
            P("task", None, None, None),
        ),
        check_vma=False,
    )
```

```python
import functools

import jax
import jax.numpy as jnp
from jax import lax
from jax.experimental import pallas as pl
from jax.experimental.pallas import tpu as pltpu
from jax.sharding import PartitionSpec as P

STEP = 10


EPS = 1e-05
ADAM_EPS = 1e-08
BETA_ONE = 0.95
BETA_TWO = 0.95
STAT_DECAY = 0.95
LEARN_MATRIX = 0.02
LEARN_NORM = 0.5
DECAY_MATRIX = 0.01
BF = jnp.bfloat16
F32 = jnp.float32
MESH = pl.DeviceIdType.MESH
MIB = 1 << 20

VMEM_SPEC = pl.BlockSpec(memory_space=pltpu.VMEM)
SMEM_SPEC = pl.BlockSpec(memory_space=pltpu.SMEM)


def run(body, outs, specs, args, scratch=(), vmem=40, flops=0):
    size = sum(o.size * o.dtype.itemsize for o in outs) + sum(a.size * a.dtype.itemsize for a in args)
    return pl.pallas_call(
        body,
        out_shape=tuple(outs),
        in_specs=[SMEM_SPEC if s == "s" else VMEM_SPEC for s in specs],
        out_specs=tuple(VMEM_SPEC for _ in outs),
        scratch_shapes=list(scratch),
        compiler_params=pltpu.CompilerParams(vmem_limit_bytes=vmem * MIB),
        cost_estimate=pl.CostEstimate(flops=flops, bytes_accessed=size, transcendentals=0),
    )(*args)


def shape(dims, kind):
    return jax.ShapeDtypeStruct(tuple(dims), kind)


def dot(a, b):
    return jnp.dot(a, b, preferred_element_type=F32)


def dot_nt(a, b):
    return lax.dot_general(a, b, (((1,), (1,)), ((), ())), preferred_element_type=F32)


def dot_tn(a, b):
    return lax.dot_general(a, b, (((0,), (0,)), ((), ())), preferred_element_type=F32)


def split(a):
    high = a.astype(BF)
    return high, (a - high.astype(F32)).astype(BF)


def dot3(kind, a, b):
    dims = {dot: (1, 0), dot_nt: (1, 1), dot_tn: (0, 0)}[kind]
    a_high, a_low = split(a)
    b_high, b_low = split(b)
    return kind(
        jnp.concatenate([a_high, a_high, a_low], axis=dims[0]),
        jnp.concatenate([b_high, b_low, b_high], axis=dims[1]),
    )


def places(height, breadth):
    index = lax.broadcasted_iota(jnp.int32, (height * breadth, 1), 0)
    row = lax.div(index, breadth)
    return row, index - row * breadth


def valid_rows(kind, height, breadth):
    row, col = places(height, breadth)
    shrunk = kind > 0
    row_limit = jnp.where(shrunk, height // 2, height)
    col_limit = jnp.where(shrunk, breadth // 2, breadth)
    return jnp.where((row < row_limit) & (col < col_limit), 1.0, 0.0).astype(F32)


def move(values, rows):
    gap = jnp.zeros((abs(rows),) + values.shape[1:], values.dtype)
    if rows > 0:
        return jnp.concatenate([gap, values[:-rows]], axis=0)
    return jnp.concatenate([values[-rows:], gap], axis=0)


def from_left(values, col):
    return jnp.where(col > 0, pltpu.roll(values, 1, 0), 0.0)


def from_right(values, col, breadth):
    return jnp.where(col < breadth - 1, pltpu.roll(values, values.shape[0] - 1, 0), 0.0)


def gather_taps(tap, breadth, col):
    lines = [move(tap(b), breadth) + tap(3 + b) + move(tap(6 + b), -breadth) for b in range(3)]
    return lines[1] + from_left(lines[0], col) + from_right(lines[2], col, breadth)


def spread_taps(values, breadth, col):
    lines = [from_right(values, col, breadth), values, from_left(values, col)]
    return [
        move(lines[b], breadth * (a - 1)) if a != 1 else lines[b] for a in range(3) for b in range(3)
    ]


def window_sum(values, row, col, breadth):
    count = values.shape[0]
    pair = values + jnp.where(
        col % 2 == 0, pltpu.roll(values, count - 1, 0), pltpu.roll(values, 1, 0)
    )
    return pair + jnp.where(row % 2 == 0, move(pair, -breadth), move(pair, breadth))


def silu_back(scaled):
    sig = jax.nn.sigmoid(scaled)
    return sig * (1.0 + scaled * (1.0 - sig))


def col_sum(values):
    return jnp.sum(values, axis=0, keepdims=True)


def put_sums(ref, rows):
    width = ref.shape[1]
    rows = list(rows) + [jnp.zeros((1, width), F32)] * (8 - len(rows))
    ref[...] = jnp.concatenate(rows, axis=0)


def each_image(geometry, body, start):
    number, height, breadth = geometry
    pixels = height * breadth

    def step(image, carry):
        return body(image, pl.ds(pl.multiple_of(image * pixels, 16), pixels), carry)

    return lax.fori_loop(0, number, step, start)


def zero_rows(count, width):
    return (jnp.zeros((1, width), F32),) * count


def greet(axes):
    barrier = pltpu.get_barrier_semaphore()
    for axis, size in axes:
        me = lax.axis_index(axis)
        for step in range(1, size):
            pl.semaphore_signal(
                barrier, inc=1, device_id={axis: lax.rem(me + step, size)}, device_id_type=MESH
            )
    pl.semaphore_wait(barrier, sum(size - 1 for _, size in axes))


def remote(source, target, sends, receives, peer, axis):
    return pltpu.make_async_remote_copy(
        src_ref=source,
        dst_ref=target,
        send_sem=sends,
        recv_sem=receives,
        device_id={axis: peer},
        device_id_type=MESH,
    )


def pack(rows):
    parts = [row[:, i : i + 128] for row in rows for i in range(0, row.shape[1], 128)]
    parts += [jnp.zeros((1, 128), F32)] * (8 - len(parts))
    return jnp.concatenate(parts, axis=0)


def unpack(tile, count, width):
    per = width // 128
    return [
        jnp.concatenate([tile[k * per + i : k * per + i + 1, :] for i in range(per)], axis=1)
        for k in range(count)
    ]


def total_rows(k, axis, size, rows, mine, slots, sends, receives, meanwhile=None):
    me = lax.axis_index(axis)
    tile = pack(rows)
    mine[k] = tile
    slots[k, me] = tile
    for step in range(1, size):
        peer = lax.rem(me + step, size)
        remote(mine.at[k], slots.at[k, me], sends.at[k, step], receives.at[k, me], peer, axis).start()
    if meanwhile:
        meanwhile()
    for step in range(1, size):
        peer = lax.rem(me + size - step, size)
        remote(
            mine.at[k], slots.at[k, peer], sends.at[k, step], receives.at[k, peer], peer, axis
        ).wait_recv()
    total = slots[k, 0]
    for peer in range(1, size):
        total = total + slots[k, peer]
    for step in range(1, size):
        peer = lax.rem(me + step, size)
        remote(
            mine.at[k], slots.at[k, me], sends.at[k, step], receives.at[k, me], peer, axis
        ).wait_send()
    return unpack(total, len(rows), rows[0].shape[1])


def total_scratch(count, size):
    return [
        pltpu.VMEM((count, 8, 128), F32),
        pltpu.VMEM((count, size, 8, 128), F32),
        pltpu.SemaphoreType.DMA((count, size)),
        pltpu.SemaphoreType.DMA((count, size)),
    ]


def columns_of(place, width):
    return pl.ds(pl.multiple_of(place * width, 128), width)


SPECS = {"s": SMEM_SPEC, "v": VMEM_SPEC, "h": pl.BlockSpec(memory_space=pltpu.HBM)}


def exchange_kernel(body, outs, specs, args, scratch, identity, vmem, flops=0, places_out=None):
    size = sum(o.size * o.dtype.itemsize for o in outs) + sum(a.size * a.dtype.itemsize for a in args)
    return pl.pallas_call(
        body,
        out_shape=tuple(outs),
        in_specs=[SPECS[s] for s in specs],
        out_specs=tuple(SPECS[s] for s in places_out or "v" * len(outs)),
        scratch_shapes=list(scratch),
        compiler_params=pltpu.CompilerParams(
            vmem_limit_bytes=vmem * MIB, collective_id=identity, has_side_effects=True
        ),
        cost_estimate=pl.CostEstimate(flops=flops, bytes_accessed=size, transcendentals=0),
    )(*args)


def info_rows(infos, i):
    return infos[pl.ds(pl.multiple_of(i * 8, 8), 8), :]


def valid_of(infos, i, height, breadth):
    return valid_rows(info_rows(infos, i)[1:2, 0:1], height, breadth)


def chosen_cells(narrow, infos, i):
    return (narrow * info_rows(infos, i)[0:1, : narrow.shape[1]]).astype(BF)


def norm_with(values, totals, scale):
    total, squares, count = totals
    center = total / count
    inverse = lax.rsqrt(squares / count - center * center + EPS)
    normal = (values - center) * inverse
    return normal, inverse, normal * scale[0] + scale[1]


def norm_back_with(upstream, normal, inverse, count, sums, scale, valid):
    return scale[0] * inverse * (upstream - sums[0] / count - normal * (sums[1] / count)) * valid


def silu(values):
    return values * jax.nn.sigmoid(values)


def window_count(height, breadth):
    return -(-(height * breadth // 4) // 16) * 16


def pool_choice(height, breadth, windows, flipped):
    pixels = height * breadth
    dims = (windows, pixels) if flipped else (pixels, windows)
    pixel = lax.broadcasted_iota(jnp.int32, dims, 1 if flipped else 0)
    window = lax.broadcasted_iota(jnp.int32, dims, 0 if flipped else 1)
    row = lax.div(pixel, breadth)
    col = pixel - row * breadth
    home = lax.div(row, 2) * (breadth // 2) + lax.div(col, 2)
    return jnp.where(home == window, 1.0, 0.0).astype(F32)


def rows_of(ref, first, count):
    return [ref[first + k : first + k + 1, :] for k in range(count)]


def window_rows(i, windows):
    return pl.ds(pl.multiple_of(i * windows, 16), windows)


def trunk_forward_body(
    geometry, tasks, batches,
    infos, x, enc_taps, dec_taps, scales,
    enc_totals, dec_totals, features, *rest,
):
    kept, (enc_pre, dec_pre, spread), rest = rest[:6], rest[6:9], rest[9:]
    (
        work, pooled, pooled_all, part, pool_sends, pool_receives, sends, receives,
    mine, slots, total_sends, total_receives, saved,
    ) = rest
    number, height, breadth = geometry
    width = enc_pre.shape[1]
    windows = window_count(height, breadth)
    task = lax.axis_index("task")
    _, col = places(height, breadth)
    choice = pool_choice(height, breadth, windows, True)
    narrow = choice.astype(BF)

    sources = (x, enc_taps, dec_taps, enc_pre, dec_pre, spread)
    saves = [pltpu.make_async_copy(a, b, saved.at[k]) for k, (a, b) in enumerate(zip(sources, kept))]
    for copy in saves[:3]:
        copy.start()

    def conv(x, taps, pre):
        def image(i, rows, carry):
            valid = valid_of(infos, i, height, breadth)
            work[...] = dot(x[rows, :], taps[...])
            out = gather_taps(lambda p: work[:, p * width : (p + 1) * width], breadth, col)
            pre[rows, :] = out
            kept = out * valid
            return (
                carry[0] + col_sum(kept),
                carry[1] + col_sum(kept * out),
                carry[2] + jnp.broadcast_to(col_sum(valid), (1, width)),
            )

        return each_image(geometry, image, zero_rows(3, width))

    def total(k, rows):
        return total_rows(
            k, "batch", batches, list(rows), mine, slots, total_sends, total_receives
        )

    sums = conv(x, enc_taps, enc_pre)
    saves[3].start()
    greet((("task", tasks), ("batch", batches)))
    totals = total(0, sums)
    put_sums(enc_totals, totals)
    scale = rows_of(scales, 0, 2)

    def peer_of(step, incoming):
        return lax.rem(task + (tasks - step if incoming else step), tasks)

    def pool_copy(i, step, incoming=False):
        rows = window_rows(i, windows)
        peer = peer_of(step, incoming)
        target = pooled_all.at[rows, columns_of(peer if incoming else task, width)]
        return remote(
            pooled.at[rows, :], target, pool_sends.at[i, step], pool_receives.at[i, step], peer, "task"
        )

    def pool(i, rows, carry):
        valid = valid_of(infos, i, height, breadth)
        _, _, scaled = norm_with(enc_pre[rows, :], totals, scale)
        high, low = split(silu(scaled) * valid)
        mean = ((dot(narrow, high) + dot(narrow, low)) * 0.25).astype(BF)
        here = window_rows(i, windows)
        pooled[here, :] = mean
        pooled_all[here, columns_of(task, width)] = mean
        for step in range(1, tasks):
            pool_copy(i, step).start()
        return carry

    each_image(geometry, pool, 0)

    def unpool(i, rows, carry):
        for step in range(1, tasks):
            pool_copy(i, step, True).wait_recv()
        wide = dot_tn(chosen_cells(choice, infos, i), pooled_all[window_rows(i, windows), :])
        spread[rows, :] = wide.astype(BF)
        return carry

    each_image(geometry, unpool, 0)
    saves[5].start()
    sums = conv(spread, dec_taps, dec_pre)
    saves[4].start()
    totals = total(1, sums)
    put_sums(dec_totals, totals)
    scale = rows_of(scales, 2, 2)

    def feature_copy(i, rows, step, incoming=False):
        peer = peer_of(step, incoming)
        target = features.at[rows, columns_of(peer if incoming else task, width)]
        return remote(
            part.at[rows, :], target, sends.at[i, step], receives.at[i, step], peer, "task"
        )

    def finish(i, rows, carry):
        valid = valid_of(infos, i, height, breadth)
        _, _, scaled = norm_with(dec_pre[rows, :], totals, scale)
        low = (silu(scaled) * valid).astype(BF)
        part[rows, :] = low
        features[rows, columns_of(task, width)] = low
        for step in range(1, tasks):
            feature_copy(i, rows, step).start()
        return carry

    each_image(geometry, finish, 0)

    def settle(i, rows, carry):
        for step in range(1, tasks):
            feature_copy(i, rows, step, True).wait_recv()
            feature_copy(i, rows, step).wait_send()
            pool_copy(i, step).wait_send()
        return carry

    each_image(geometry, settle, 0)
    for copy in saves:
        copy.wait()


def trunk_forward(geometry, tasks, batches, infos, x, enc_taps, dec_taps, scales):
    number, height, breadth = geometry
    pixels = height * breadth
    channels = x.shape[1]
    width = channels // tasks
    windows = window_count(height, breadth)
    tall = shape((x.shape[0], width), F32)
    outs = [
        shape((8, width), F32), shape((8, width), F32), shape(x.shape, BF),
        shape(x.shape, BF), shape(enc_taps.shape, BF), shape(dec_taps.shape, BF),
        tall, tall, shape(x.shape, BF),
    ]
    return exchange_kernel(
        functools.partial(trunk_forward_body, geometry, tasks, batches),
        outs,
        "vvvvv",
        (infos, x, enc_taps, dec_taps, scales),
        [
            pltpu.VMEM(tall.shape, F32),
            pltpu.VMEM(tall.shape, F32),
            pltpu.VMEM(x.shape, BF),
            pltpu.VMEM((pixels, 9 * width), F32),
            pltpu.VMEM((number * windows, width), BF),
            pltpu.VMEM((number * windows, channels), BF),
            pltpu.VMEM((x.shape[0], width), BF),
        ]
        + [pltpu.SemaphoreType.DMA((number, tasks))] * 4
        + total_scratch(2, batches)
        + [pltpu.SemaphoreType.DMA((6,))],
        1,
        60,
        flops=4 * x.size * enc_taps.shape[1],
        places_out="vvvhhhhhh",
    )


def head_body(
    geometry, tasks, batches, summing,
    infos, features, weights, cotangent, scales, counts,
    task_out, upstream, norm_sums, *rest,
):
    if summing:
        (outward, inward), rest = rest[:2], rest[2:]
    else:
        grads_out, rest = rest[0], rest[1:]
    (
        grads, pre_one, pre_two, pre_three, hidden, gated, nine, work, lower, out, arrived,
        sends, receives, mine, slots, total_sends, total_receives, loaded,
    ) = rest[:18]
    number, height, breadth = geometry
    channels = features.shape[1]
    width = channels // tasks
    windows = task_out.shape[1]
    task = lax.axis_index("task")
    half = work.shape[2]
    _, col = places(height, breadth)
    widen = pool_choice(height, breadth, windows, False).astype(BF)
    narrow = pool_choice(height, breadth, windows, True).astype(BF)
    count = jnp.broadcast_to(counts[2:3, 0:1], (1, channels))
    cuts = (pl.ds(0, 2 * channels), pl.ds(2 * channels, 9 * channels))
    loads = [
        pltpu.make_async_copy(weights.at[cut, :], grads.at[cut, :], loaded.at[k])
        for k, cut in enumerate(cuts)
    ]
    for copy in loads:
        copy.start()
    first = grads.at[pl.ds(0, channels), :]
    second = grads.at[pl.ds(channels, channels), :]

    def kernel_rows(p):
        return pl.ds((2 + p) * channels, channels)

    def total(k, rows, meanwhile=None):
        return total_rows(
            k, "batch", batches, list(rows), mine, slots, total_sends, total_receives, meanwhile
        )

    if summing:
        near, paired, passed, near_sends, near_receives, pass_sends, pass_receives = rest[18:]
        place, core, chips = pair_place(batches)
        block = near.shape[1]
        part = block // 2

        def near_copy(chip):
            return remote(
                block_rows(grads, 2 * chip + 1 - core, block), near.at[chip],
                near_sends.at[chip], near_receives.at[chip], 2 * place + 1 - core, "batch",
            )

        def near_sum(chip):
            own = block_rows(grads, 2 * chip + core, block)[...].astype(F32)
            return own + near[chip].astype(F32)

        def pass_copy(way):
            chip = lax.rem(place + (1 if way == 0 else chips - 1), chips)
            far = lax.rem(place + 2, chips)
            return remote(
                paired.at[far, pl.ds(way * part, part), :], passed.at[way],
                pass_sends.at[way], pass_receives.at[way], 2 * chip + core, "batch",
            )

    def put_stats(pre, rows, value, valid, carry):
        pre[rows, :] = value
        kept = value * valid
        return carry[0] + col_sum(kept), carry[1] + col_sum(kept * value)

    nothing = zero_rows(2, channels)
    scale_one, scale_two, scale_three = (rows_of(scales, 2 * k, 2) for k in range(3))

    loads[0].wait()

    def first_step(i, rows, carry):
        valid = valid_of(infos, i, height, breadth)
        return put_stats(pre_one, rows, dot(features[rows, :], first[...]), valid, carry)

    sums = each_image(geometry, first_step, nothing)
    greet((("task", tasks), ("batch", batches)))
    totals_one = total(0, sums) + [count]

    def second_step(i, rows, carry):
        valid = valid_of(infos, i, height, breadth)
        _, _, scaled = norm_with(pre_one[rows, :], totals_one, scale_one)
        low = (silu(scaled) * valid).astype(BF)
        hidden[rows, :] = low
        return put_stats(pre_two, rows, dot(low, second[...]), valid, carry)

    sums = each_image(geometry, second_step, nothing)
    totals_two = total(1, sums) + [count]

    def third_step(i, rows, carry):
        valid = valid_of(infos, i, height, breadth)
        _, _, scaled = norm_with(pre_two[rows, :], totals_two, scale_two)
        low = (jax.nn.sigmoid(scaled) * features[rows, :].astype(F32)).astype(BF)
        gated[rows, :] = low
        parts = []
        for j in range(channels // half):
            cut = slice(j * half, (j + 1) * half)
            for p in range(9):
                work[p] = dot(low, grads[kernel_rows(p), cut])
            parts.append(gather_taps(lambda p: work[p], breadth, col))
        return put_stats(pre_three, rows, jnp.concatenate(parts, axis=1), valid, carry)

    loads[1].wait()
    sums = each_image(geometry, third_step, nothing)
    totals_three = total(2, sums) + [count]

    def out_step(i, rows, carry):
        valid = valid_of(infos, i, height, breadth)
        normal, _, scaled = norm_with(pre_three[rows, :], totals_three, scale_three)
        high, low = split(silu(scaled) * valid)
        mean = (dot(narrow, high) + dot(narrow, low)) * 0.25
        task_out[i] = mean.astype(BF)
        dy = silu_back(scaled) * dot(widen, cotangent[i]) * 0.25 * valid
        lower[rows, :] = dy
        return carry[0] + col_sum(dy), carry[1] + col_sum(dy * normal)

    sums = each_image(geometry, out_step, nothing)
    sums_three = total(3, sums)

    def third_back(i, rows, carry):
        valid = valid_of(infos, i, height, breadth)
        normal, inverse, _ = norm_with(pre_three[rows, :], totals_three, scale_three)
        dz = norm_back_with(lower[rows, :], normal, inverse, count, sums_three, scale_three, valid)
        for p, moved in enumerate(spread_taps(dz, breadth, col)):
            nine[p, rows, :] = moved.astype(BF)
        flow = None
        for p in range(9):
            piece = dot_nt(nine[p, rows, :], grads[kernel_rows(p), :])
            flow = piece if flow is None else flow + piece
        lower[rows, :] = flow
        normal, _, scaled = norm_with(pre_two[rows, :], totals_two, scale_two)
        gate = jax.nn.sigmoid(scaled)
        dy = flow * features[rows, :].astype(F32) * gate * (1.0 - gate) * valid
        pre_three[rows, :] = dy
        return carry[0] + col_sum(dy), carry[1] + col_sum(dy * normal)

    sums = each_image(geometry, third_back, nothing)

    def taps(begin, end):
        def tap(p, carry):
            rows = pl.ds(pl.multiple_of((2 + p) * channels, channels), channels)
            grads[rows, :] = dot_tn(gated[...], nine[p]).astype(BF)
            return carry

        lax.fori_loop(begin, end, tap, 0)

    sums_two = total(4, sums, lambda: taps(0, 4))

    def second_back(i, rows, carry):
        valid = valid_of(infos, i, height, breadth)
        normal, inverse, scaled = norm_with(pre_two[rows, :], totals_two, scale_two)
        dz = norm_back_with(
            pre_three[rows, :], normal, inverse, count, sums_two, scale_two, valid
        ).astype(BF)
        out[rows, :] = dz
        lower[rows, :] = lower[rows, :] * jax.nn.sigmoid(scaled)
        normal, _, scaled = norm_with(pre_one[rows, :], totals_one, scale_one)
        dy = silu_back(scaled) * dot_nt(dz, second[...]) * valid
        pre_three[rows, :] = dy
        return carry[0] + col_sum(dy), carry[1] + col_sum(dy * normal)

    sums = each_image(geometry, second_back, nothing)

    def weight_rows():
        grads[pl.ds(channels, channels), :] = dot_tn(hidden[...], out[...]).astype(BF)
        taps(4, 9)
        if summing:
            for chip in range(1, chips):
                near_copy(chip).start()

    sums_one = total(5, sums, weight_rows)

    def flow_copy(i, rows, step, incoming=False):
        peer = lax.rem(task + (tasks - step if incoming else step), tasks)
        return remote(
            out.at[rows, columns_of(peer, width)], arrived.at[step - 1, rows, :],
            sends.at[i, step], receives.at[i, step], peer, "task",
        )

    def first_back(i, rows, carry):
        valid = valid_of(infos, i, height, breadth)
        normal, inverse, _ = norm_with(pre_one[rows, :], totals_one, scale_one)
        dz = norm_back_with(
            pre_three[rows, :], normal, inverse, count, sums_one, scale_one, valid
        ).astype(BF)
        hidden[rows, :] = dz
        flow = (lower[rows, :] + dot_nt(dz, first[...])) * valid
        out[rows, :] = flow.astype(BF)
        for step in range(1, tasks):
            flow_copy(i, rows, step).start()
        return carry

    each_image(geometry, first_back, 0)
    grads[pl.ds(0, channels), :] = dot_tn(features[...], hidden[...]).astype(BF)
    if summing:
        near_copy(0).start()
        for chip in (1, 2, 3, 0):
            near_copy(chip).wait_recv()
        far = lax.rem(place + 2, chips)
        paired[far] = near_sum(far).astype(BF)
        for way in range(2):
            pass_copy(way).start()
        for way in range(2):
            chip = lax.rem(place + (1 if way == 0 else chips - 1), chips)
            paired[chip] = near_sum(chip).astype(BF)
        inward[...] = near_sum(place).astype(BF)
    else:
        grads_out[...] = grads[...]
    put_sums(norm_sums, sums_one + sums_two + sums_three)

    def settle(i, rows, carry):
        for step in range(1, tasks):
            flow_copy(i, rows, step, True).wait_recv()
        flow = out[rows, columns_of(task, width)].astype(F32)
        for step in range(1, tasks):
            flow = flow + arrived[step - 1, rows, :].astype(F32)
        upstream[rows, :] = flow
        for step in range(1, tasks):
            flow_copy(i, rows, step).wait_send()
        return carry

    each_image(geometry, settle, 0)
    if summing:
        for way in range(2):
            chip = lax.rem(place + (1 if way == 0 else chips - 1), chips)
            here, other = (pl.ds(k * part, part) for k in (way, 1 - way))
            pass_copy(way).wait_recv()
            total_part = paired[chip, here, :].astype(F32) + passed[way].astype(F32)
            outward[way, here, :] = total_part.astype(BF)
            outward[way, other, :] = paired[chip, other, :]
        for way in range(2):
            pass_copy(way).wait_send()
        for chip in range(chips):
            near_copy(chip).wait_send()


def head(geometry, tasks, batches, infos, features, weights, cotangent, scales, counts):
    number, height, breadth = geometry
    pixels = height * breadth
    total, channels = features.shape
    width = channels // tasks
    block = weights.shape[0] // batches
    summing = batches == 8 and block % 32 == 0
    outs = [
        shape((number, pixels // 4, channels), BF),
        shape((total, width), F32),
        shape((8, channels), F32),
    ]
    scratch = []
    if summing:
        outs += [shape((2, block, channels), BF), shape((block, channels), BF)]
        scratch = [
            pltpu.VMEM((batches // 2, block, channels), BF),
            pltpu.VMEM((batches // 2, block, channels), BF),
            pltpu.VMEM((2, block // 2, channels), BF),
        ]
        scratch += [pltpu.SemaphoreType.DMA((batches // 2,))] * 2 + [pltpu.SemaphoreType.DMA((2,))] * 2
    else:
        outs.append(shape(weights.shape, BF))
    pooled, upstream, sums, *grads = exchange_kernel(
        functools.partial(head_body, geometry, tasks, batches, summing),
        outs,
        "vvhvvv",
        (infos, features, weights, cotangent, scales, counts),
        [
            pltpu.VMEM(weights.shape, BF),
            pltpu.VMEM(features.shape, F32),
            pltpu.VMEM(features.shape, F32),
            pltpu.VMEM(features.shape, F32),
            pltpu.VMEM(features.shape, BF),
            pltpu.VMEM(features.shape, BF),
            pltpu.VMEM((9,) + features.shape, BF),
            pltpu.VMEM((9, pixels, min(channels, 256)), F32),
            pltpu.VMEM(features.shape, F32),
            pltpu.VMEM(features.shape, BF),
            pltpu.VMEM((tasks - 1, total, width), BF),
        ]
        + [pltpu.SemaphoreType.DMA((number, tasks))] * 2
        + total_scratch(6, batches)
        + [pltpu.SemaphoreType.DMA((2,))]
        + scratch,
        2,
        61,
        flops=6 * total * channels * weights.shape[0],
    )
    return pooled, upstream, sums, grads


def trunk_backward_body(
    geometry, tasks, batches, summing,
    infos, upstream, enc_totals, dec_totals, scales, *rest,
):
    kept, rest = rest[:6], rest[6:]
    if summing:
        (outward, inward), rest = rest[:2], rest[2:]
    (enc_grad, dec_grad, flow_out, norm_sums), rest = rest[:4], rest[4:]
    if summing:
        head_owned, rest = rest[0], rest[1:]
    (x, enc_taps, dec_taps, enc_pre, dec_pre, spread), rest = rest[:6], rest[6:]
    (
        nine, change, packed, arrived, pooled, sends, receives,
        mine, slots, total_sends, total_receives, loaded,
    ) = rest[:12]
    if summing:
        arrivals, head_sends, head_receives = rest[12:]
        place, core, chips = pair_place(batches)

        def head_copy(way):
            chip = lax.rem(place + (1 if way == 0 else chips - 1), chips)
            return remote(outward.at[way], arrivals.at[way], head_sends.at[way],
                          head_receives.at[way], 2 * chip + core, "batch")

    targets = (x, enc_taps, dec_taps, enc_pre, dec_pre, spread)
    loads = [pltpu.make_async_copy(a, b, loaded.at[k]) for k, (a, b) in enumerate(zip(kept, targets))]
    for k in (4, 2, 5, 3, 1, 0):
        loads[k].start()
    number, height, breadth = geometry
    channels = x.shape[1]
    width = enc_pre.shape[1]
    windows = window_count(height, breadth)
    task = lax.axis_index("task")
    _, col = places(height, breadth)
    widen = pool_choice(height, breadth, windows, False).astype(BF)
    narrow = pool_choice(height, breadth, windows, True)
    nothing = zero_rows(2, width)

    def total(k, rows):
        return total_rows(
            k, "batch", batches, list(rows), mine, slots, total_sends, total_receives
        )

    def change_of(pre, totals, scale, flow):
        def image(i, rows, carry):
            valid = valid_of(infos, i, height, breadth)
            normal, _, scaled = norm_with(pre[rows, :], totals, scale)
            dy = silu_back(scaled) * flow(i, rows) * valid
            change[rows, :] = dy
            return carry[0] + col_sum(dy), carry[1] + col_sum(dy * normal)

        return each_image(geometry, image, nothing)

    def back(pre, totals, scale, sums, taps, put):
        def image(i, rows, carry):
            valid = valid_of(infos, i, height, breadth)
            normal, inverse, _ = norm_with(pre[rows, :], totals, scale)
            dz = norm_back_with(change[rows, :], normal, inverse, totals[2], sums, scale, valid)
            for p, moved in enumerate(spread_taps(dz, breadth, col)):
                nine[rows, p * width : (p + 1) * width] = moved.astype(BF)
            put(i, rows, dot_nt(nine[rows, :], taps[...]) * valid)
            return carry

        each_image(geometry, image, 0)

    totals = rows_of(dec_totals, 0, 3)
    scale = rows_of(scales, 2, 2)
    loads[4].wait()
    sums = change_of(dec_pre, totals, scale, lambda i, rows: upstream[rows, :])
    greet((("task", tasks), ("batch", batches)))
    dec_sums = total(0, sums)
    if summing:
        for way in range(2):
            head_copy(way).start()

    def copy_of(i, step, incoming=False):
        rows = window_rows(i, windows)
        peer = lax.rem(task + (tasks - step if incoming else step), tasks)
        return remote(
            packed.at[rows, columns_of(peer, width)], arrived.at[step - 1, rows, :],
            sends.at[i, step], receives.at[i, step], peer, "task",
        )

    def put_packed(i, rows, flow):
        chosen = chosen_cells(narrow, infos, i)
        packed[window_rows(i, windows), :] = dot(chosen, flow.astype(BF)).astype(BF)
        for step in range(1, tasks):
            copy_of(i, step).start()

    loads[2].wait()
    back(dec_pre, totals, scale, dec_sums, dec_taps, put_packed)
    loads[5].wait()
    dec_grad[...] = dot_tn(spread[...], nine[...])

    def collect(i, carry):
        for step in range(1, tasks):
            copy_of(i, step, True).wait_recv()
        rows = window_rows(i, windows)
        flow = packed[rows, columns_of(task, width)].astype(F32)
        for step in range(1, tasks):
            flow = flow + arrived[step - 1, rows, :].astype(F32)
        pooled[rows, :] = flow
        for step in range(1, tasks):
            copy_of(i, step).wait_send()
        return carry

    lax.fori_loop(0, number, collect, 0)

    def widened(i, rows):
        high, low = split(pooled[window_rows(i, windows), :])
        return (dot(widen, high) + dot(widen, low)) * 0.25

    totals = rows_of(enc_totals, 0, 3)
    scale = rows_of(scales, 0, 2)
    loads[3].wait()
    sums = change_of(enc_pre, totals, scale, widened)
    enc_sums = total(1, sums)

    def put_flow(i, rows, flow):
        flow_out[rows, :] = flow.astype(BF)

    loads[1].wait()
    back(enc_pre, totals, scale, enc_sums, enc_taps, put_flow)
    loads[0].wait()
    enc_grad[...] = dot_tn(x[...], nine[...])
    put_sums(norm_sums, enc_sums + dec_sums)
    if summing:
        total_head = inward[...].astype(F32)
        for way in range(2):
            head_copy(way).wait_recv()
            total_head = total_head + arrivals[way].astype(F32)
        head_owned[...] = total_head.astype(BF)
        for way in range(2):
            head_copy(way).wait_send()


def trunk_backward(
    geometry, tasks, batches, infos, upstream, enc_totals, dec_totals, scales, head_grads, kept
):
    number, height, breadth = geometry
    x, enc_taps, dec_taps = kept[:3]
    total, channels = x.shape
    width = channels // tasks
    windows = window_count(height, breadth)
    summing = len(head_grads) == 2
    outs = [
        shape(enc_taps.shape, F32),
        shape(dec_taps.shape, F32),
        shape(x.shape, BF),
        shape((8, width), F32),
    ]
    specs = "vvvvvhhhhhh"
    args = (infos, upstream, enc_totals, dec_totals, scales, *kept)
    scratch = []
    if summing:
        outs.append(shape(head_grads[1].shape, BF))
        specs += "hv"
        args += tuple(head_grads)
        scratch = [pltpu.VMEM(head_grads[0].shape, BF)] + [pltpu.SemaphoreType.DMA((2,))] * 2
    made = exchange_kernel(
        functools.partial(trunk_backward_body, geometry, tasks, batches, summing),
        outs,
        specs,
        args,
        [pltpu.VMEM(a.shape, a.dtype) for a in kept]
        + [
            pltpu.VMEM((total, 9 * width), BF),
            pltpu.VMEM((total, width), F32),
            pltpu.VMEM((number * windows, channels), BF),
            pltpu.VMEM((tasks - 1, number * windows, width), BF),
            pltpu.VMEM((number * windows, width), F32),
        ]
        + [pltpu.SemaphoreType.DMA((number, tasks))] * 2
        + total_scratch(2, batches)
        + [pltpu.SemaphoreType.DMA((6,))]
        + scratch,
        3,
        60,
        flops=8 * x.size * enc_taps.shape[1],
    )
    if summing:
        return made
    return *made, lax.psum_scatter(head_grads[0], "batch", scatter_dimension=0, tiled=True)


def to_taps_body(index, slots, enc, dec, wide, tap):
    count = slots.shape[0]
    channels = enc.shape[0]
    width = slots.shape[1]
    step = 1024

    def widen(i, carry):
        rows = pl.ds(pl.multiple_of(i * step, step), step)
        wide[rows, :] = slots[rows, :].astype(F32)
        return carry

    lax.fori_loop(0, count // step, widen, 0)
    group = 32
    for p in range(18):

        def fetch(i, carry):
            base = i * group
            for u in range(group):
                tap[pl.ds(base + u, 1), :] = wide[pl.ds(index[p * channels + base + u], 1), :]
            return carry

        lax.fori_loop(0, channels // group, fetch, 0)
        out = enc if p < 9 else dec
        q = p % 9
        out[:, q * width : (q + 1) * width] = tap[...].astype(BF)


def to_taps(index, slots, channels):
    width = slots.shape[1]
    return run(
        to_taps_body,
        [shape((channels, 9 * width), BF)] * 2,
        "sv",
        (index, slots),
        [pltpu.VMEM(slots.shape, F32), pltpu.VMEM((channels, width), F32)],
        vmem=60,
        flops=10000 * MIB,
    )


def to_slots_body(index, enc, dec, slots, wide):
    count = slots.shape[0]
    channels = enc.shape[0]
    width = slots.shape[1]
    step = 1024
    group = 32
    for p in range(18):
        source = enc if p < 9 else dec
        q = p % 9

        def place(i, carry):
            base = pl.multiple_of(i * group, group)
            values = source[pl.ds(base, group), q * width : (q + 1) * width]
            for u in range(group):
                wide[pl.ds(index[p * channels + base + u], 1), :] = values[u : u + 1, :]
            return carry

        lax.fori_loop(0, channels // group, place, 0)

    def narrow(i, carry):
        rows = pl.ds(pl.multiple_of(i * step, step), step)
        slots[rows, :] = wide[rows, :].astype(BF)
        return carry

    lax.fori_loop(0, count // step, narrow, 0)


def to_slots(index, enc, dec):
    width = enc.shape[1] // 9
    dims = (index.shape[0], width)
    return run(
        to_slots_body, [shape(dims, BF)], "svv", (index, enc, dec), [pltpu.VMEM(dims, F32)], vmem=60
    )[0]


def adam(gradient, moment_one, moment_two):
    new_one = BETA_ONE * moment_one + (1.0 - BETA_ONE) * gradient
    new_two = BETA_TWO * moment_two + (1.0 - BETA_TWO) * gradient * gradient
    direction = (
        new_one / (1.0 - BETA_ONE**STEP) / (jnp.sqrt(new_two / (1.0 - BETA_TWO**STEP)) + ADAM_EPS)
    )
    return new_one, new_two, direction


def pair_place(batches):
    me = lax.axis_index("batch")
    place = lax.div(me, 2)
    return place, me - 2 * place, batches // 2


def greet_pairs(tasks, batches):
    place, core, chips = pair_place(batches)
    task = lax.axis_index("task")
    barrier = pltpu.get_barrier_semaphore()

    def signal(device):
        pl.semaphore_signal(barrier, inc=1, device_id=device, device_id_type=MESH)

    for step in range(1, tasks):
        signal({"task": lax.rem(task + step, tasks)})
    signal({"batch": 2 * place + 1 - core})
    for step in range(1, chips):
        signal({"batch": 2 * lax.rem(place + step, chips) + core})
    pl.semaphore_wait(barrier, tasks - 1 + chips)


def block_rows(ref, index, count):
    return ref.at[pl.ds(pl.multiple_of(index * count, 8), count), :]


def far_first(chips):
    return sorted(range(chips), key=lambda step: -min(step, chips - step))


def pair_sum(batches, rows_of_block, own_block, near, paired, far, sems):
    place, core, chips = pair_place(batches)
    count = near.shape[1]
    near_send, near_receive, far_send, far_receive = sems
    other = 2 * place + 1 - core
    ring = chips == 4 and count % 32 == 0
    half = count // 2
    halves = (pl.ds(0, half), pl.ds(half, half))

    def near_copy(step):
        chip = lax.rem(place + step, chips)
        return remote(rows_of_block(2 * chip + 1 - core), near.at[step],
                      near_send.at[step], near_receive.at[step], other, "batch")

    def far_copy(step, incoming=False):
        chip = lax.rem(place + (chips - step if incoming else step), chips)
        return remote(paired.at[step], far.at[step], far_send.at[step], far_receive.at[step],
                      2 * chip + core, "batch")

    def ring_copy(which, way):
        chip = lax.rem(place + (1 if way == 0 else chips - 1), chips)
        if which == 0:
            source, target = paired.at[2, halves[way], :], far.at[2 + way, halves[0], :]
        else:
            cut = halves[way] if which == 2 else halves[1 - way]
            source, target = paired.at[1 if way == 0 else 3, cut, :], far.at[way, cut, :]
        k = 2 * which + way
        return remote(source, target, far_send.at[k], far_receive.at[k], 2 * chip + core, "batch")

    def start():
        for step in far_first(chips):
            near_copy(step).start()

    def middle():
        for step in far_first(chips):
            near_copy(step).wait_recv()
            if step:
                paired[step] = (own_block(step) + near[step].astype(F32)).astype(paired.dtype)
                if not ring:
                    far_copy(step).start()
                elif step == 2:
                    ring_copy(0, 0).start()
                    ring_copy(0, 1).start()
                else:
                    ring_copy(1, 0 if step == 1 else 1).start()

    def relay():
        if not ring:
            return
        for way in range(2):
            ring_copy(0, way).wait_recv()
            step = 1 if way == 0 else 3
            total = paired[step, halves[way], :].astype(F32) + far[2 + way, halves[0], :].astype(F32)
            paired[step, halves[way], :] = total.astype(paired.dtype)
            ring_copy(2, way).start()

    def end():
        total = own_block(0) + near[0].astype(F32)
        if ring:
            for way in range(2):
                ring_copy(1, way).wait_recv()
                ring_copy(2, way).wait_recv()
                total = total + far[way].astype(F32)
            for k in range(3):
                for way in range(2):
                    ring_copy(k, way).wait_send()
        else:
            for step in range(1, chips):
                far_copy(step, True).wait_recv()
                total = total + far[step].astype(F32)
            for step in range(1, chips):
                far_copy(step).wait_send()
        for step in range(chips):
            near_copy(step).wait_send()
        return total

    return start, middle, relay, end


def blocks_in(source, batches, count):
    place, core, chips = pair_place(batches)

    def own(step):
        chip = lax.rem(place + step, chips)
        return block_rows(source, 2 * chip + core, count)[...].astype(F32)

    return (lambda index: block_rows(source, index, count)), own


def pair_scratch(batches, rows, width, kind):
    chips = batches // 2
    return [pltpu.VMEM((chips, rows // batches, width), kind)] * 3 + [
        pltpu.SemaphoreType.DMA((max(chips, 6),))
    ] * 4


def chip_spread(batches, block, sends, receives):
    place, core, chips = pair_place(batches)
    count = block(place).shape[0]
    ring = chips == 4 and count % 32 == 0
    half = count // 2

    def copy(step, incoming=False):
        peer = lax.rem(place + (chips - step if incoming else step), chips)
        ref = block(peer if incoming else place)
        return remote(ref, ref, sends.at[step], receives.at[step], 2 * peer + core, "batch")

    def pass_on(way, incoming=False):
        step = 1 if way == 0 else chips - 1
        peer = lax.rem(place + (chips - step if incoming else step), chips)
        home = lax.rem(place + (2 if incoming else chips - step), chips)
        ref = block(home).at[pl.ds(way * half, half), :]
        k = 2 if way == 0 else 0
        return remote(ref, ref, sends.at[k], receives.at[k], 2 * peer + core, "batch")

    steps = (1, chips - 1) if ring else tuple(range(1, chips))

    def start():
        for step in steps:
            copy(step).start()

    def relay():
        if ring:
            for way, step in enumerate(steps):
                copy(step, True).wait_recv()
                pass_on(way).start()

    def settle():
        if ring:
            for way in range(2):
                pass_on(way, True).wait_recv()
        else:
            for step in steps:
                copy(step, True).wait_recv()

    def drain():
        for step in steps:
            copy(step).wait_send()
        if ring:
            for way in range(2):
                pass_on(way).wait_send()

    return start, relay, settle, drain


def arrive_body(
    tasks, batches,
    image, info, index, weight,
    slots, x, infos, owners,
    raw, raw_loaded, x_send, x_receive, info_send, info_receive,
    chip_send, chip_receive, pair_send, pair_receive, own,
):
    task = lax.axis_index("task")
    place, core, chips = pair_place(batches)
    count, width = raw.shape
    load = pltpu.make_async_copy(weight.at[:, columns_of(task, width)], raw, raw_loaded)
    load.start()
    greet_pairs(tasks, batches)

    def task_copy(source, target, sends, receives, step, incoming=False):
        peer = lax.rem(task + (tasks - step if incoming else step), tasks)
        home = peer if incoming else task
        return remote(source, block_rows(target, home, source.shape[0]), sends.at[step],
                      receives.at[step], peer, "task")

    def moves(step, incoming=False):
        return (
            task_copy(info, infos, info_send, info_receive, step, incoming),
            task_copy(image, x, x_send, x_receive, step, incoming),
        )

    def block(chip):
        return block_rows(slots, 2 * chip + core, count)

    def pair_copy(hop, incoming=False):
        chip = lax.rem(place + chips - hop, chips)
        ref = block_rows(slots, 2 * chip + (1 - core if incoming else core), count)
        return remote(ref, ref, pair_send.at[hop], pair_receive.at[hop], 2 * place + 1 - core, "batch")

    start, relay, settle, drain = chip_spread(batches, block, chip_send, chip_receive)
    load.wait()
    block(place)[...] = raw[...].astype(BF)
    start()
    pair_copy(0).start()
    for step in range(1, tasks):
        for copy in moves(step):
            copy.start()
    locals_ = [
        pltpu.make_async_copy(image, block_rows(x, task, image.shape[0]), own.at[0]),
        pltpu.make_async_copy(info, block_rows(infos, task, info.shape[0]), own.at[1]),
    ]
    for copy in locals_:
        copy.start()
    mine = lax.broadcasted_iota(jnp.int32, (count, 1), 0) + lax.axis_index("batch") * count
    found = jnp.zeros((count, 128), F32)
    for k in range(index.shape[0] // 2, index.shape[0]):
        found = jnp.where(index[k : k + 1, :] == mine, 1.0, found)
    found = jnp.max(found, axis=1, keepdims=True)
    owners[:, 0:1] = 1.0 - found
    owners[:, 1:2] = found
    relay()
    if chips == 4 and count % 32 == 0:
        pair_copy(1).start()
        pair_copy(3).start()
        settle()
        pair_copy(2).start()
    else:
        settle()
        for hop in range(1, chips):
            pair_copy(hop).start()
    for copy in locals_:
        copy.wait()
    for step in range(1, tasks):
        for copy in moves(step, True):
            copy.wait_recv()
    for hop in range(chips):
        pair_copy(hop, True).wait_recv()
    for step in range(1, tasks):
        for copy in moves(step):
            copy.wait_send()
    for hop in range(chips):
        pair_copy(hop).wait_send()
    drain()


def arrive(tasks, batches, image, info, index, weight):
    count, channels = weight.shape
    width = channels // tasks
    chips = batches // 2
    return exchange_kernel(
        functools.partial(arrive_body, tasks, batches),
        [
            shape((count * batches, width), BF),
            shape((image.shape[0] * tasks, channels), BF),
            shape((info.shape[0] * tasks, info.shape[1]), F32),
            shape((count, 2), F32),
        ],
        "vvvh",
        (image, info, index.reshape(-1, 128), weight),
        [pltpu.VMEM((count, width), F32), pltpu.SemaphoreType.DMA]
        + [pltpu.SemaphoreType.DMA((tasks,))] * 4
        + [pltpu.SemaphoreType.DMA((max(chips, 4),))] * 4
        + [pltpu.SemaphoreType.DMA((2,))],
        4,
        60,
        flops=20000 * MIB,
    )


def soap_rows(cuts, grad, owners, state, low, first):
    total = grad.shape[0]

    def chunk(i, carry):
        rows = pl.ds(pl.multiple_of(i * (total // cuts), 8), total // cuts)
        values = grad[rows, :].astype(F32)
        marks = owners(i * (total // cuts), total // cuts)
        count = len(marks)
        rotated = None
        for m in range(count):
            part = dot((values * marks[m]).astype(BF), low[first + m])
            rotated = part if rotated is None else rotated + part
        new_one, new_two, direction = adam(rotated, state[1, rows, :], state[2, rows, :])
        state[1, rows, :] = new_one
        state[2, rows, :] = new_two
        stepped = None
        for m in range(count):
            part = dot_nt((direction * marks[m]).astype(BF), low[first + m])
            stepped = part if stepped is None else stepped + part
        old = state[0, rows, :]
        state[0, rows, :] = old - LEARN_MATRIX * (stepped + DECAY_MATRIX * old)
        return carry

    lax.fori_loop(0, cuts, chunk, 0)


def factor_rows(values, identity, turn):
    size, width = values.shape
    sub = lax.broadcasted_iota(jnp.int32, (size, width), 0)
    rolled = pltpu.roll(values, turn, 1)
    columns = [jnp.broadcast_to(rolled[:, j : j + 1], (size, width)) for j in range(size)]
    scale = jnp.zeros((size, width), F32)
    for j in range(size):
        root = lax.rsqrt(columns[j][j : j + 1, :])
        scale = jnp.where(sub == j, root, scale)
        lower = jnp.where(sub > j, columns[j] * root, 0.0)
        values = values - lower * (values[j : j + 1, :] * root)
        identity = identity - lower * (identity[j : j + 1, :] * root)
        for i in range(j + 1, size):
            columns[i] = columns[i] - lower * (columns[i][j : j + 1, :] * root)
    return values * scale, identity * scale


GROUP = 16
PANEL = 128


def renew_panel(k, product, made, tables, inverses):
    count, size = product.shape[0], product.shape[1]
    here = slice(k * PANEL, (k + 1) * PANEL)
    row = lax.broadcasted_iota(jnp.int32, (PANEL, PANEL), 0)
    col = lax.broadcasted_iota(jnp.int32, (PANEL, PANEL), 1)
    unit = jnp.where(row == col, 1.0, 0.0).astype(F32)
    for n in range(count):
        tables[n][:, :PANEL] = dot3(dot_tn, product[n, :, here], product[n, :, here])
        tables[n][:, PANEL:] = unit

    def group(q, carry):
        rows = pl.ds(pl.multiple_of(q * GROUP, GROUP), GROUP)
        turn = lax.rem(PANEL - q * GROUP, PANEL)
        done = [
            factor_rows(tables[n][rows, :PANEL], tables[n][rows, PANEL:], turn)
            for n in range(count)
        ]
        for n in range(count):
            upper, inverse = done[n]
            inverses[n][rows, :] = inverse
            both = jnp.concatenate([upper, inverse], axis=1)
            tables[n][...] = tables[n][...] - dot3(dot_tn, upper, both)
        return carry

    lax.fori_loop(0, PANEL // GROUP, group, 0)
    for n in range(count):
        turned = dot3(dot_nt, product[n, :, here], inverses[n][...])
        made[n, :, here] = turned
        if k < size // PANEL - 1:
            rest = slice((k + 1) * PANEL, size)
            product[n, :, rest] = product[n, :, rest] - dot3(
                dot, turned, dot3(dot_tn, turned, product[n, :, rest])
            )


def tail_body(
    tasks, batches, cuts,
    slots, flow, sums, owners, head_grad,
    weight, one, two, head_weight, head_one, head_two, basis, head_basis,
    input_grad, norm_sums, state_new, head_state_new, grams, head_grams,
    grad, part, state, head_state, mine, head_mine, bases, low,
    flow_in, flow_send, flow_receive, send, receive, sum_send, sum_receive,
    *rest,
):
    row_scratch, gram_scratch, head_scratch = rest[:7], rest[7:14], rest[14:21]
    chip_send, chip_receive, task_send, task_receive, pair_send, pair_receive, load, save = rest[21:]
    task = lax.axis_index("task")
    place, core, chips = pair_place(batches)
    width = part.shape[1]
    channels = grad.shape[1]
    pixels = input_grad.shape[0]
    trunk_total = basis.shape[0]
    head_total = head_basis.shape[0]
    count, head_count = mine.shape[0] // batches, head_mine.shape[0] // batches

    def trunk_marks(start, size):
        rows = pl.ds(pl.multiple_of(start, 8), size)
        return [owners[rows, m : m + 1] for m in range(trunk_total)]

    def head_marks(start, size):
        index = lax.broadcasted_iota(jnp.int32, (size, 1), 0) + start
        index = index + lax.axis_index("batch") * head_grad.shape[0]
        owner = jnp.minimum(lax.div(index, channels), head_total - 1)
        return [jnp.where(owner == m, 1.0, 0.0).astype(F32) for m in range(head_total)]

    def put_grams(target, rows, columns, marks):
        for m, mark in enumerate(marks):
            held = (rows[...].astype(F32) * mark).astype(BF)
            target[m * channels : (m + 1) * channels, :] = dot_tn(held, columns[...]).astype(
                target.dtype
            )

    def peer_of(step, incoming):
        return lax.rem(task + (tasks - step if incoming else step), tasks)

    def flow_copy(step, incoming=False):
        peer = peer_of(step, incoming)
        return remote(block_rows(flow, peer, pixels), flow_in.at[step - 1], flow_send.at[step],
                      flow_receive.at[step], peer, "task")

    def sum_copy(step, incoming=False):
        peer = peer_of(step, incoming)
        home = peer if incoming else task
        return remote(sums, norm_sums.at[:, columns_of(home, width)], sum_send.at[step],
                      sum_receive.at[step], peer, "task")

    def part_copy(step, incoming=False):
        peer = peer_of(step, incoming)
        home = peer if incoming else task
        return remote(part, grad.at[:, columns_of(home, width)], send.at[step], receive.at[step],
                      peer, "task")

    def trunk_block(chip, home, which):
        rows = pl.ds(pl.multiple_of((2 * chip + which) * count, 8), count)
        return grams.at[rows, columns_of(home, width)]

    def head_block(chip, which):
        return block_rows(head_grams, 2 * chip + which, head_count)

    def task_copy(step, hop, incoming=False):
        peer = peer_of(step, incoming)
        chip = lax.rem(place + chips - hop, chips)
        block = trunk_block(chip, peer if incoming else task, core)
        return remote(block, block, task_send.at[step, hop], task_receive.at[step, hop], peer, "task")

    def pair_copy(kind, hop, incoming=False):
        chip = lax.rem(place + chips - hop, chips)
        which = 1 - core if incoming else core
        home = lax.rem(task + tasks - kind, tasks)
        block = head_block(chip, which) if kind == tasks else trunk_block(chip, home, which)
        return remote(block, block, pair_send.at[kind, hop], pair_receive.at[kind, hop],
                      2 * place + 1 - core, "batch")

    def sum_of(source, scratch):
        near, paired, far, *sems = scratch
        return pair_sum(
            batches, *blocks_in(source, batches, near.shape[1]), near, paired, far, sems
        )

    moves = [
        (basis, bases.at[pl.ds(0, trunk_total)]),
        (head_basis, bases.at[pl.ds(trunk_total, head_total)]),
        (head_weight, head_state.at[0]),
        (head_one, head_state.at[1]),
        (head_two, head_state.at[2]),
        (weight, state.at[0]),
        (one, state.at[1]),
        (two, state.at[2]),
    ]
    loads = [pltpu.make_async_copy(a, b, load.at[k]) for k, (a, b) in enumerate(moves)]
    for copy in loads:
        copy.start()
    saves = [
        pltpu.make_async_copy(state, state_new, save.at[0]),
        pltpu.make_async_copy(head_state, head_state_new, save.at[1]),
    ]

    greet_pairs(tasks, batches)
    row_start, row_middle, row_relay, row_end = sum_of(slots, row_scratch)
    row_start()
    for step in range(1, tasks):
        sum_copy(step).start()
        flow_copy(step).start()
    norm_sums[:, columns_of(task, width)] = sums[...]
    row_middle()
    put_grams(head_mine, head_grad, head_grad, head_marks(0, head_grad.shape[0]))
    head_start, head_middle, head_relay, head_end = sum_of(head_mine, head_scratch)
    head_start()
    row_relay()
    head_middle()
    for copy in loads[:5]:
        copy.wait()
    for m in range(trunk_total + head_total):
        low[m] = bases[m].astype(BF)
    total = row_end().astype(BF)
    part[...] = total
    for step in range(1, tasks):
        part_copy(step).start()
    grad[:, columns_of(task, width)] = total
    head_relay()

    soap_rows(cuts, head_grad, head_marks, head_state, low, trunk_total)
    saves[1].start()
    total = block_rows(flow, task, pixels)[...].astype(F32)
    for step in range(1, tasks):
        flow_copy(step, True).wait_recv()
        total = total + flow_in[step - 1].astype(F32)
    input_grad[...] = total
    head_block(place, core)[...] = head_end().astype(head_grams.dtype)
    trunk_spread = chip_spread(
        batches, lambda chip: trunk_block(chip, task, core), chip_send.at[0], chip_receive.at[0]
    )
    head_spread = chip_spread(
        batches, lambda chip: head_block(chip, core), chip_send.at[1], chip_receive.at[1]
    )
    head_spread[0]()
    pair_copy(tasks, 0).start()
    for step in range(1, tasks):
        part_copy(step, True).wait_recv()

    put_grams(mine, grad, part, trunk_marks(0, grad.shape[0]))
    start, middle, relay, end = sum_of(mine, gram_scratch)
    start()
    middle()
    head_spread[1]()
    for copy in loads[5:]:
        copy.wait()
    relay()
    soap_rows(cuts, grad, trunk_marks, state, low, 0)
    saves[0].start()
    trunk_block(place, task, core)[...] = end().astype(grams.dtype)
    trunk_spread[0]()
    for step in range(1, tasks):
        task_copy(step, 0).start()
    pair_copy(0, 0).start()
    trunk_spread[1]()
    trunk_spread[2]()
    for hop in range(1, chips):
        for step in range(1, tasks):
            task_copy(step, hop).start()
        pair_copy(0, hop).start()
    head_spread[2]()
    for hop in range(1, chips):
        pair_copy(tasks, hop).start()
    for hop in range(chips):
        for step in range(1, tasks):
            task_copy(step, hop, True).wait_recv()
            pair_copy(step, hop).start()
    for hop in range(chips):
        for kind in range(tasks + 1):
            pair_copy(kind, hop, True).wait_recv()
    for step in range(1, tasks):
        sum_copy(step, True).wait_recv()

    for copy in saves:
        copy.wait()
    for step in range(1, tasks):
        sum_copy(step).wait_send()
        part_copy(step).wait_send()
        flow_copy(step).wait_send()
    for hop in range(chips):
        for kind in range(tasks + 1):
            pair_copy(kind, hop).wait_send()
        for step in range(1, tasks):
            task_copy(step, hop).wait_send()
    trunk_spread[3]()
    head_spread[3]()


def renew_body(
    state, head_state, grams, head_grams, stat, head_stat, basis, head_basis,
    weight_new, one_new, two_new, head_weight_new, head_one_new, head_two_new,
    stat_new, head_stat_new, basis_new, head_basis_new,
    stats, product, made, held, head_held, load, save, *work,
):
    trunk_total, head_total = stat.shape[0], head_stat.shape[0]
    channels = stat.shape[1]
    count = trunk_total + head_total
    tables, inverses = work[:count], work[count:]
    loads = [
        pltpu.make_async_copy(state, held, load.at[0]),
        pltpu.make_async_copy(head_state, head_held, load.at[1]),
    ]
    for copy in loads:
        copy.start()
    sources = [held.at[k] for k in range(3)] + [head_held.at[k] for k in range(3)]
    targets = [weight_new, one_new, two_new, head_weight_new, head_one_new, head_two_new]
    saves = [pltpu.make_async_copy(a, b, save.at[k]) for k, (a, b) in enumerate(zip(sources, targets))]
    for m in range(count):
        first = m < trunk_total
        place = m if first else m - trunk_total
        gram = (grams if first else head_grams)[place * channels : (place + 1) * channels, :]
        old = (stat if first else head_stat)[place]
        stats[m] = STAT_DECAY * old + (1.0 - STAT_DECAY) * gram.astype(F32)
        product[m] = dot3(dot, stats[m], (basis if first else head_basis)[place])
    groups = ((0, trunk_total, stat_new, basis_new), (trunk_total, head_total, head_stat_new, head_basis_new))
    for begin, size, out, _ in groups:
        copy = pltpu.make_async_copy(stats.at[pl.ds(begin, size)], out, save.at[len(saves)])
        copy.start()
        saves.append(copy)
    for copy in loads:
        copy.wait()
    for copy in saves[:6]:
        copy.start()
    for k in range(channels // PANEL):
        renew_panel(k, product, made, tables, inverses)
        cut = pl.ds(k * PANEL, PANEL)
        for begin, size, _, out in groups:
            copy = pltpu.make_async_copy(
                made.at[pl.ds(begin, size), :, cut], out.at[:, :, cut], save.at[len(saves)]
            )
            copy.start()
            saves.append(copy)
    for copy in saves:
        copy.wait()


def finish(tasks, batches, local_grads, rows, matrices):
    slots, flow, sums, owners, head_grad = local_grads
    stat, head_stat, basis, head_basis = matrices
    total, channels = rows[0].shape
    width = channels // tasks
    trunk_total, head_total = basis.shape[0], head_basis.shape[0]
    gram_rows, head_rows = trunk_total * channels, head_total * channels
    chips = batches // 2
    kind = BF if gram_rows % (16 * batches) == 0 else F32
    head_kind = BF if head_rows % (16 * batches) == 0 else F32
    cuts = 4 if total % 64 == 0 and head_grad.shape[0] % 64 == 0 else 1
    square = (trunk_total + head_total, channels, channels)
    pixels = flow.shape[0] // tasks
    input_grad, norm_sums, *made = exchange_kernel(
        functools.partial(tail_body, tasks, batches, cuts),
        [
            shape((pixels, channels), F32),
            shape((8, channels), F32),
            shape((3, total, channels), F32),
            shape((3,) + head_grad.shape, F32),
            shape((gram_rows, channels), kind),
            shape((head_rows, channels), head_kind),
        ],
        "vvvvvhhhhhhhh",
        (*local_grads, *rows, basis, head_basis),
        [
            pltpu.VMEM((total, channels), BF),
            pltpu.VMEM((total, width), BF),
            pltpu.VMEM((3, total, channels), F32),
            pltpu.VMEM((3,) + head_grad.shape, F32),
            pltpu.VMEM((gram_rows, width), kind),
            pltpu.VMEM((head_rows, channels), head_kind),
            pltpu.VMEM(square, F32),
            pltpu.VMEM(square, BF),
            pltpu.VMEM((tasks - 1, pixels, channels), BF),
        ]
        + [pltpu.SemaphoreType.DMA((tasks,))] * 6
        + pair_scratch(batches, slots.shape[0], width, BF)
        + pair_scratch(batches, gram_rows, width, kind)
        + pair_scratch(batches, head_rows, channels, head_kind)
        + [pltpu.SemaphoreType.DMA((2, max(chips, 4)))] * 2
        + [pltpu.SemaphoreType.DMA((tasks, chips))] * 2
        + [pltpu.SemaphoreType.DMA((tasks + 1, chips))] * 2
        + [pltpu.SemaphoreType.DMA((8,)), pltpu.SemaphoreType.DMA((2,))],
        5,
        60,
        flops=50000 * MIB,
        places_out="vvhhvv",
    )
    outs = [shape(a.shape, F32) for a in (*rows, *matrices)]
    hbm = pl.BlockSpec(memory_space=pltpu.HBM)
    count = trunk_total + head_total
    results = pl.pallas_call(
        renew_body,
        out_shape=tuple(outs),
        in_specs=[hbm] * 2 + [VMEM_SPEC] * 6,
        out_specs=tuple(hbm for _ in outs),
        scratch_shapes=[pltpu.VMEM(square, F32)] * 3
        + [pltpu.VMEM(made[0].shape, F32), pltpu.VMEM(made[1].shape, F32)]
        + [pltpu.SemaphoreType.DMA((2,))]
        + [pltpu.SemaphoreType.DMA((8 + 2 * (channels // PANEL),))]
        + [pltpu.VMEM((PANEL, 2 * PANEL), F32)] * count
        + [pltpu.VMEM((PANEL, PANEL), F32)] * count,
        compiler_params=pltpu.CompilerParams(vmem_limit_bytes=60 * MIB),
        cost_estimate=pl.CostEstimate(
            flops=60000 * MIB, bytes_accessed=64 * MIB, transcendentals=0
        ),
    )(*made, *matrices)
    return input_grad, norm_sums, results


def local(
    tasks,
    batches,
    images,
    image_small,
    pool_index,
    row_slot,
    trunk_weight,
    trunk_mean_grad,
    trunk_mean_square,
    trunk_statistic,
    trunk_basis,
    head_weight,
    head_mean_grad,
    head_mean_square,
    head_statistic,
    head_basis,
    trunk_gain,
    trunk_offset,
    trunk_norm_mean_grad,
    trunk_norm_mean_square,
    head_gain,
    head_offset,
    head_norm_mean_grad,
    head_norm_mean_square,
    cotangent,
):
    number, height, breadth, channels = images.shape
    pixels = height * breadth
    shown = tasks * number
    geometry = (shown, height, breadth)
    task = lax.axis_index("task")
    width = channels // tasks

    def quarter(values):
        return lax.dynamic_slice_in_dim(values, task * width, width, values.ndim - 1)

    def inside(flags):
        row_limit = jnp.where(flags > 0, height // 2, height)[:, None, None]
        col_limit = jnp.where(flags > 0, breadth // 2, breadth)[:, None, None]
        return (jnp.arange(height, dtype=jnp.int32)[None, :, None] < row_limit) & (
            jnp.arange(breadth, dtype=jnp.int32)[None, None, :] < col_limit
        )

    cell = 2 * jnp.arange(2, dtype=jnp.int32)[:, None, None] + jnp.arange(2, dtype=jnp.int32)
    cells = pool_index.reshape(number, height // 2, 1, breadth // 2, 1)
    valid = inside(image_small)
    chosen = ((cells == cell).reshape(number, height, breadth) & valid).reshape(number, pixels)
    info = jnp.zeros((8 * number, channels), F32)
    info = info.at[::8, :pixels].set(chosen.astype(F32))
    info = info.at[1::8, 0].set(image_small.astype(F32))
    masked = (images * valid[..., None].astype(BF)).reshape(number * pixels, channels)
    slots, x, infos, trunk_owners = arrive(
        tasks, batches, masked, info, row_slot, trunk_weight
    )
    head_low = head_weight.astype(BF)
    slots, head_low = lax.optimization_barrier((slots, head_low))
    head_rows = lax.all_gather(head_low, "batch", axis=1, tiled=True)[0]
    enc_taps, dec_taps = to_taps(row_slot, slots, channels)

    scales = quarter(jnp.stack([trunk_gain, trunk_offset], axis=1)).reshape(4, width)
    enc_totals, dec_totals, features, *kept = trunk_forward(
        geometry, tasks, batches, infos, x, enc_taps, dec_taps, scales
    )
    head_scales = jnp.stack([head_gain[0], head_offset[0]], axis=1).reshape(6, channels)
    pooled, upstream, head_sums, head_grads = head(
        geometry, tasks, batches, infos, features, head_rows,
        cotangent.reshape(shown, pixels // 4, channels), head_scales, enc_totals,
    )
    task_features = pooled.reshape(cotangent.shape)
    enc_grad, dec_grad, flow, trunk_sums, head_owned = trunk_backward(
        geometry, tasks, batches, infos, upstream, enc_totals, dec_totals, scales, head_grads, kept
    )
    input_grad, norm_sums, results = finish(
        tasks, batches,
        (to_slots(row_slot, enc_grad, dec_grad), flow, trunk_sums, trunk_owners, head_owned),
        (trunk_weight, trunk_mean_grad, trunk_mean_square,
         head_weight[0], head_mean_grad[0], head_mean_square[0]),
        (trunk_statistic, head_statistic[0], trunk_basis, head_basis[0]),
    )
    input_grad = input_grad.reshape(images.shape)
    (
        trunk_weight_new, trunk_one_new, trunk_two_new,
        head_weight_new, head_one_new, head_two_new,
        trunk_stat_new, head_stat_new, trunk_basis_new, head_basis_new,
    ) = results

    trunk_norm = jnp.stack([trunk_gain, trunk_offset], axis=1)
    trunk_norm_grad = norm_sums[:4].reshape(2, 2, channels)[:, ::-1]
    trunk_norm_one, trunk_norm_two, trunk_direction = adam(
        trunk_norm_grad, trunk_norm_mean_grad, trunk_norm_mean_square
    )
    head_norm = jnp.stack([head_gain, head_offset], axis=2)
    head_norm_grad = head_sums[:6].reshape(1, 3, 2, channels)[:, :, ::-1]
    head_norm_one, head_norm_two, head_direction = adam(
        head_norm_grad, head_norm_mean_grad, head_norm_mean_square
    )
    return (
        task_features,
        input_grad,
        trunk_weight_new,
        trunk_one_new,
        trunk_two_new,
        trunk_stat_new,
        trunk_basis_new,
        head_weight_new[None],
        head_one_new[None],
        head_two_new[None],
        head_stat_new[None],
        head_basis_new[None],
        trunk_norm - LEARN_NORM * trunk_direction,
        trunk_norm_one,
        trunk_norm_two,
        head_norm - LEARN_NORM * head_direction,
        head_norm_one,
        head_norm_two,
    )


def solution(mesh):
    placed = (
        P(("task", "batch"), None, None, None),
        P(("task", "batch")),
        P(("task", "batch"), None, None),
        P(),
        P("batch", None),
        P("batch", None),
        P("batch", None),
        P(),
        P(),
        P("task", "batch", None),
        P("task", "batch", None),
        P("task", "batch", None),
        P("task", None, None, None),
        P("task", None, None, None),
        P(),
        P(),
        P(),
        P(),
        P("task", None, None),
        P("task", None, None),
        P("task", None, None, None),
        P("task", None, None, None),
        P("task", None, "batch", None, None, None),
    )
    return jax.shard_map(
        functools.partial(local, mesh.shape["task"], mesh.shape["batch"]),
        mesh=mesh,
        in_specs=placed,
        out_specs=(
            P("task", None, "batch", None, None, None),
            P(("task", "batch"), None, None, None),
            P("batch", None),
            P("batch", None),
            P("batch", None),
            P(),
            P(),
            P("task", "batch", None),
            P("task", "batch", None),
            P("task", "batch", None),
            P("task", None, None, None),
            P("task", None, None, None),
            P(),
            P(),
            P(),
            P("task", None, None, None),
            P("task", None, None, None),
            P("task", None, None, None),
        ),
        check_vma=False,
    )
```

```python
import functools

import jax
import jax.numpy as jnp
from jax import lax
from jax.experimental import pallas as pl
from jax.experimental.pallas import tpu as pltpu
from jax.sharding import PartitionSpec as P

STEP = 10


EPS = 1e-05
ADAM_EPS = 1e-08
BETA_ONE = 0.95
BETA_TWO = 0.95
STAT_DECAY = 0.95
LEARN_MATRIX = 0.02
LEARN_NORM = 0.5
DECAY_MATRIX = 0.01
BF = jnp.bfloat16
F32 = jnp.float32
MESH = pl.DeviceIdType.MESH
MIB = 1 << 20

VMEM_SPEC = pl.BlockSpec(memory_space=pltpu.VMEM)
SMEM_SPEC = pl.BlockSpec(memory_space=pltpu.SMEM)


def run(body, outs, specs, args, scratch=(), vmem=40, flops=0):
    size = sum(o.size * o.dtype.itemsize for o in outs) + sum(a.size * a.dtype.itemsize for a in args)
    return pl.pallas_call(
        body,
        out_shape=tuple(outs),
        in_specs=[SMEM_SPEC if s == "s" else VMEM_SPEC for s in specs],
        out_specs=tuple(VMEM_SPEC for _ in outs),
        scratch_shapes=list(scratch),
        compiler_params=pltpu.CompilerParams(vmem_limit_bytes=vmem * MIB),
        cost_estimate=pl.CostEstimate(flops=flops, bytes_accessed=size, transcendentals=0),
    )(*args)


def shape(dims, kind):
    return jax.ShapeDtypeStruct(tuple(dims), kind)


def dot(a, b):
    return jnp.dot(a, b, preferred_element_type=F32)


def dot_nt(a, b):
    return lax.dot_general(a, b, (((1,), (1,)), ((), ())), preferred_element_type=F32)


def dot_tn(a, b):
    return lax.dot_general(a, b, (((0,), (0,)), ((), ())), preferred_element_type=F32)


def split(a):
    high = a.astype(BF)
    return high, (a - high.astype(F32)).astype(BF)


def dot3(kind, a, b):
    dims = {dot: (1, 0), dot_nt: (1, 1), dot_tn: (0, 0)}[kind]
    a_high, a_low = split(a)
    b_high, b_low = split(b)
    return kind(
        jnp.concatenate([a_high, a_high, a_low], axis=dims[0]),
        jnp.concatenate([b_high, b_low, b_high], axis=dims[1]),
    )


def places(height, breadth):
    index = lax.broadcasted_iota(jnp.int32, (height * breadth, 1), 0)
    row = lax.div(index, breadth)
    return row, index - row * breadth


def valid_rows(kind, height, breadth):
    row, col = places(height, breadth)
    shrunk = kind > 0
    row_limit = jnp.where(shrunk, height // 2, height)
    col_limit = jnp.where(shrunk, breadth // 2, breadth)
    return jnp.where((row < row_limit) & (col < col_limit), 1.0, 0.0).astype(F32)


def move(values, rows):
    gap = jnp.zeros((abs(rows),) + values.shape[1:], values.dtype)
    if rows > 0:
        return jnp.concatenate([gap, values[:-rows]], axis=0)
    return jnp.concatenate([values[-rows:], gap], axis=0)


def from_left(values, col):
    return jnp.where(col > 0, pltpu.roll(values, 1, 0), 0.0)


def from_right(values, col, breadth):
    return jnp.where(col < breadth - 1, pltpu.roll(values, values.shape[0] - 1, 0), 0.0)


def gather_taps(tap, breadth, col):
    lines = [move(tap(b), breadth) + tap(3 + b) + move(tap(6 + b), -breadth) for b in range(3)]
    return lines[1] + from_left(lines[0], col) + from_right(lines[2], col, breadth)


def spread_taps(values, breadth, col):
    lines = [from_right(values, col, breadth), values, from_left(values, col)]
    return [
        move(lines[b], breadth * (a - 1)) if a != 1 else lines[b] for a in range(3) for b in range(3)
    ]


def window_sum(values, row, col, breadth):
    count = values.shape[0]
    pair = values + jnp.where(
        col % 2 == 0, pltpu.roll(values, count - 1, 0), pltpu.roll(values, 1, 0)
    )
    return pair + jnp.where(row % 2 == 0, move(pair, -breadth), move(pair, breadth))


def silu_back(scaled):
    sig = jax.nn.sigmoid(scaled)
    return sig * (1.0 + scaled * (1.0 - sig))


def col_sum(values):
    return jnp.sum(values, axis=0, keepdims=True)


def put_sums(ref, rows):
    width = ref.shape[1]
    rows = list(rows) + [jnp.zeros((1, width), F32)] * (8 - len(rows))
    ref[...] = jnp.concatenate(rows, axis=0)


def each_image(geometry, body, start):
    number, height, breadth = geometry
    pixels = height * breadth

    def step(image, carry):
        return body(image, pl.ds(pl.multiple_of(image * pixels, 16), pixels), carry)

    return lax.fori_loop(0, number, step, start)


def zero_rows(count, width):
    return (jnp.zeros((1, width), F32),) * count


def greet(axes):
    barrier = pltpu.get_barrier_semaphore()
    for axis, size in axes:
        me = lax.axis_index(axis)
        for step in range(1, size):
            pl.semaphore_signal(
                barrier, inc=1, device_id={axis: lax.rem(me + step, size)}, device_id_type=MESH
            )
    pl.semaphore_wait(barrier, sum(size - 1 for _, size in axes))


def remote(source, target, sends, receives, peer, axis):
    return pltpu.make_async_remote_copy(
        src_ref=source,
        dst_ref=target,
        send_sem=sends,
        recv_sem=receives,
        device_id={axis: peer},
        device_id_type=MESH,
    )


def pack(rows):
    parts = [row[:, i : i + 128] for row in rows for i in range(0, row.shape[1], 128)]
    parts += [jnp.zeros((1, 128), F32)] * (8 - len(parts))
    return jnp.concatenate(parts, axis=0)


def unpack(tile, count, width):
    per = width // 128
    return [
        jnp.concatenate([tile[k * per + i : k * per + i + 1, :] for i in range(per)], axis=1)
        for k in range(count)
    ]


def total_rows(k, axis, size, rows, mine, slots, sends, receives, meanwhile=None):
    me = lax.axis_index(axis)
    tile = pack(rows)
    mine[k] = tile
    slots[k, me] = tile
    for step in range(1, size):
        peer = lax.rem(me + step, size)
        remote(mine.at[k], slots.at[k, me], sends.at[k, step], receives.at[k, me], peer, axis).start()
    if meanwhile:
        meanwhile()
    for step in range(1, size):
        peer = lax.rem(me + size - step, size)
        remote(
            mine.at[k], slots.at[k, peer], sends.at[k, step], receives.at[k, peer], peer, axis
        ).wait_recv()
    total = slots[k, 0]
    for peer in range(1, size):
        total = total + slots[k, peer]
    for step in range(1, size):
        peer = lax.rem(me + step, size)
        remote(
            mine.at[k], slots.at[k, me], sends.at[k, step], receives.at[k, me], peer, axis
        ).wait_send()
    return unpack(total, len(rows), rows[0].shape[1])


def total_scratch(count, size):
    return [
        pltpu.VMEM((count, 8, 128), F32),
        pltpu.VMEM((count, size, 8, 128), F32),
        pltpu.SemaphoreType.DMA((count, size)),
        pltpu.SemaphoreType.DMA((count, size)),
    ]


def columns_of(place, width):
    return pl.ds(pl.multiple_of(place * width, 128), width)


SPECS = {"s": SMEM_SPEC, "v": VMEM_SPEC, "h": pl.BlockSpec(memory_space=pltpu.HBM)}


def exchange_kernel(body, outs, specs, args, scratch, identity, vmem, flops=0, places_out=None):
    size = sum(o.size * o.dtype.itemsize for o in outs) + sum(a.size * a.dtype.itemsize for a in args)
    return pl.pallas_call(
        body,
        out_shape=tuple(outs),
        in_specs=[SPECS[s] for s in specs],
        out_specs=tuple(SPECS[s] for s in places_out or "v" * len(outs)),
        scratch_shapes=list(scratch),
        compiler_params=pltpu.CompilerParams(
            vmem_limit_bytes=vmem * MIB, collective_id=identity, has_side_effects=True
        ),
        cost_estimate=pl.CostEstimate(flops=flops, bytes_accessed=size, transcendentals=0),
    )(*args)


def info_rows(infos, i):
    return infos[pl.ds(pl.multiple_of(i * 8, 8), 8), :]


def valid_of(infos, i, height, breadth):
    return valid_rows(info_rows(infos, i)[1:2, 0:1], height, breadth)


def chosen_cells(narrow, infos, i):
    return (narrow * info_rows(infos, i)[0:1, : narrow.shape[1]]).astype(BF)


def norm_with(values, totals, scale):
    total, squares, count = totals
    center = total / count
    inverse = lax.rsqrt(squares / count - center * center + EPS)
    normal = (values - center) * inverse
    return normal, inverse, normal * scale[0] + scale[1]


def norm_back_with(upstream, normal, inverse, count, sums, scale, valid):
    return scale[0] * inverse * (upstream - sums[0] / count - normal * (sums[1] / count)) * valid


def silu(values):
    return values * jax.nn.sigmoid(values)


def window_count(height, breadth):
    return -(-(height * breadth // 4) // 16) * 16


def pool_choice(height, breadth, windows, flipped):
    pixels = height * breadth
    dims = (windows, pixels) if flipped else (pixels, windows)
    pixel = lax.broadcasted_iota(jnp.int32, dims, 1 if flipped else 0)
    window = lax.broadcasted_iota(jnp.int32, dims, 0 if flipped else 1)
    row = lax.div(pixel, breadth)
    col = pixel - row * breadth
    home = lax.div(row, 2) * (breadth // 2) + lax.div(col, 2)
    return jnp.where(home == window, 1.0, 0.0).astype(F32)


def rows_of(ref, first, count):
    return [ref[first + k : first + k + 1, :] for k in range(count)]


def window_rows(i, windows):
    return pl.ds(pl.multiple_of(i * windows, 16), windows)


def trunk_forward_body(
    geometry, tasks, batches,
    index, infos, x, kernel_slots, scales,
    enc_totals, dec_totals, features, *rest,
):
    kept, (enc_pre, dec_pre, spread), rest = rest[:6], rest[6:9], rest[9:]
    (
        enc_taps, dec_taps, wide, tap,
        work, pooled, pooled_all, part, pool_sends, pool_receives, sends, receives,
    mine, slots, total_sends, total_receives, saved,
    ) = rest
    number, height, breadth = geometry
    width = enc_pre.shape[1]
    windows = window_count(height, breadth)
    task = lax.axis_index("task")
    _, col = places(height, breadth)
    choice = pool_choice(height, breadth, windows, True)
    narrow = choice.astype(BF)

    sources = (x, enc_taps, dec_taps, enc_pre, dec_pre, spread)
    saves = [pltpu.make_async_copy(a, b, saved.at[k]) for k, (a, b) in enumerate(zip(sources, kept))]
    saves[0].start()
    channels = x.shape[1]

    def widen(i, carry):
        rows = pl.ds(pl.multiple_of(i * channels, 16), channels)
        wide[rows, :] = kernel_slots[rows, :].astype(F32)
        return carry

    def fetch(taps, first, begin, end):
        group = 32
        for p in range(begin, end):

            def some(i, carry):
                base = i * group
                for u in range(group):
                    slot = index[(first + p) * channels + base + u]
                    tap[pl.ds(base + u, 1), :] = wide[pl.ds(slot, 1), :]
                return carry

            lax.fori_loop(0, channels // group, some, 0)
            taps[:, p * width : (p + 1) * width] = tap[...].astype(BF)

    lax.fori_loop(0, wide.shape[0] // channels, widen, 0)
    fetch(enc_taps, 0, 0, 9)
    saves[1].start()

    def conv(x, taps, pre):
        def image(i, rows, carry):
            valid = valid_of(infos, i, height, breadth)
            work[...] = dot(x[rows, :], taps[...])
            out = gather_taps(lambda p: work[:, p * width : (p + 1) * width], breadth, col)
            pre[rows, :] = out
            kept = out * valid
            return (
                carry[0] + col_sum(kept),
                carry[1] + col_sum(kept * out),
                carry[2] + jnp.broadcast_to(col_sum(valid), (1, width)),
            )

        return each_image(geometry, image, zero_rows(3, width))

    def total(k, rows, meanwhile=None):
        return total_rows(
            k, "batch", batches, list(rows), mine, slots, total_sends, total_receives, meanwhile
        )

    sums = conv(x, enc_taps, enc_pre)
    saves[3].start()
    greet((("task", tasks), ("batch", batches)))
    totals = total(0, sums, lambda: fetch(dec_taps, 9, 0, 4))
    put_sums(enc_totals, totals)
    scale = rows_of(scales, 0, 2)

    def peer_of(step, incoming):
        return lax.rem(task + (tasks - step if incoming else step), tasks)

    def pool_copy(i, step, incoming=False):
        rows = window_rows(i, windows)
        peer = peer_of(step, incoming)
        target = pooled_all.at[rows, columns_of(peer if incoming else task, width)]
        return remote(
            pooled.at[rows, :], target, pool_sends.at[i, step], pool_receives.at[i, step], peer, "task"
        )

    def pool(i, rows, carry):
        valid = valid_of(infos, i, height, breadth)
        _, _, scaled = norm_with(enc_pre[rows, :], totals, scale)
        high, low = split(silu(scaled) * valid)
        mean = ((dot(narrow, high) + dot(narrow, low)) * 0.25).astype(BF)
        here = window_rows(i, windows)
        pooled[here, :] = mean
        pooled_all[here, columns_of(task, width)] = mean
        for step in range(1, tasks):
            pool_copy(i, step).start()
        return carry

    each_image(geometry, pool, 0)
    fetch(dec_taps, 9, 4, 9)
    saves[2].start()

    def unpool(i, rows, carry):
        for step in range(1, tasks):
            pool_copy(i, step, True).wait_recv()
        wide = dot_tn(chosen_cells(choice, infos, i), pooled_all[window_rows(i, windows), :])
        spread[rows, :] = wide.astype(BF)
        return carry

    each_image(geometry, unpool, 0)
    saves[5].start()
    sums = conv(spread, dec_taps, dec_pre)
    saves[4].start()
    totals = total(1, sums)
    put_sums(dec_totals, totals)
    scale = rows_of(scales, 2, 2)

    def feature_copy(i, rows, step, incoming=False):
        peer = peer_of(step, incoming)
        target = features.at[rows, columns_of(peer if incoming else task, width)]
        return remote(
            part.at[rows, :], target, sends.at[i, step], receives.at[i, step], peer, "task"
        )

    def finish(i, rows, carry):
        valid = valid_of(infos, i, height, breadth)
        _, _, scaled = norm_with(dec_pre[rows, :], totals, scale)
        low = (silu(scaled) * valid).astype(BF)
        part[rows, :] = low
        features[rows, columns_of(task, width)] = low
        for step in range(1, tasks):
            feature_copy(i, rows, step).start()
        return carry

    each_image(geometry, finish, 0)

    def settle(i, rows, carry):
        for step in range(1, tasks):
            feature_copy(i, rows, step, True).wait_recv()
            feature_copy(i, rows, step).wait_send()
            pool_copy(i, step).wait_send()
        return carry

    each_image(geometry, settle, 0)
    for copy in saves:
        copy.wait()


def trunk_forward(geometry, tasks, batches, index, infos, x, kernel_slots, scales):
    number, height, breadth = geometry
    pixels = height * breadth
    channels = x.shape[1]
    width = channels // tasks
    windows = window_count(height, breadth)
    tall = shape((x.shape[0], width), F32)
    taps = shape((channels, 9 * width), BF)
    outs = [
        shape((8, width), F32), shape((8, width), F32), shape(x.shape, BF),
        shape(x.shape, BF), taps, taps,
        tall, tall, shape(x.shape, BF),
    ]
    return exchange_kernel(
        functools.partial(trunk_forward_body, geometry, tasks, batches),
        outs,
        "svvvv",
        (index, infos, x, kernel_slots, scales),
        [
            pltpu.VMEM(tall.shape, F32),
            pltpu.VMEM(tall.shape, F32),
            pltpu.VMEM(x.shape, BF),
            pltpu.VMEM(taps.shape, BF),
            pltpu.VMEM(taps.shape, BF),
            pltpu.VMEM(kernel_slots.shape, F32),
            pltpu.VMEM((channels, width), F32),
            pltpu.VMEM((pixels, 9 * width), F32),
            pltpu.VMEM((number * windows, width), BF),
            pltpu.VMEM((number * windows, channels), BF),
            pltpu.VMEM((x.shape[0], width), BF),
        ]
        + [pltpu.SemaphoreType.DMA((number, tasks))] * 4
        + total_scratch(2, batches)
        + [pltpu.SemaphoreType.DMA((6,))],
        1,
        60,
        flops=4 * x.size * taps.shape[1],
        places_out="vvvhhhhhh",
    )


def head_body(
    geometry, tasks, batches, summing,
    infos, features, weights, cotangent, scales, counts,
    task_out, upstream, norm_sums, *rest,
):
    grads_out, rest = rest[0], rest[1:]
    (
        grads, pre_one, pre_two, pre_three, hidden, gated, nine, work, lower, out, arrived,
        sends, receives, mine, slots, total_sends, total_receives, loaded,
    ) = rest[:18]
    number, height, breadth = geometry
    channels = features.shape[1]
    width = channels // tasks
    windows = task_out.shape[1]
    task = lax.axis_index("task")
    half = work.shape[2]
    _, col = places(height, breadth)
    widen = pool_choice(height, breadth, windows, False).astype(BF)
    narrow = pool_choice(height, breadth, windows, True).astype(BF)
    count = jnp.broadcast_to(counts[2:3, 0:1], (1, channels))
    cuts = (pl.ds(0, 2 * channels), pl.ds(2 * channels, 9 * channels))
    loads = [
        pltpu.make_async_copy(weights.at[cut, :], grads.at[cut, :], loaded.at[k])
        for k, cut in enumerate(cuts)
    ]
    for copy in loads:
        copy.start()
    first = grads.at[pl.ds(0, channels), :]
    second = grads.at[pl.ds(channels, channels), :]

    def kernel_rows(p):
        return pl.ds((2 + p) * channels, channels)

    def total(k, rows, meanwhile=None):
        return total_rows(
            k, "batch", batches, list(rows), mine, slots, total_sends, total_receives, meanwhile
        )

    if summing:
        near, near_sends, near_receives = rest[18:]
        place, core, chips = pair_place(batches)
        block = near.shape[1]

        def near_copy(chip):
            return remote(
                block_rows(grads, 2 * chip + 1 - core, block), near.at[chip],
                near_sends.at[chip], near_receives.at[chip], 2 * place + 1 - core, "batch",
            )

    def put_stats(pre, rows, value, valid, carry):
        pre[rows, :] = value
        kept = value * valid
        return carry[0] + col_sum(kept), carry[1] + col_sum(kept * value)

    nothing = zero_rows(2, channels)
    scale_one, scale_two, scale_three = (rows_of(scales, 2 * k, 2) for k in range(3))

    loads[0].wait()

    def first_step(i, rows, carry):
        valid = valid_of(infos, i, height, breadth)
        return put_stats(pre_one, rows, dot(features[rows, :], first[...]), valid, carry)

    sums = each_image(geometry, first_step, nothing)
    greet((("task", tasks), ("batch", batches)))
    totals_one = total(0, sums) + [count]

    def second_step(i, rows, carry):
        valid = valid_of(infos, i, height, breadth)
        _, _, scaled = norm_with(pre_one[rows, :], totals_one, scale_one)
        low = (silu(scaled) * valid).astype(BF)
        hidden[rows, :] = low
        return put_stats(pre_two, rows, dot(low, second[...]), valid, carry)

    sums = each_image(geometry, second_step, nothing)
    totals_two = total(1, sums) + [count]

    def third_step(i, rows, carry):
        valid = valid_of(infos, i, height, breadth)
        _, _, scaled = norm_with(pre_two[rows, :], totals_two, scale_two)
        low = (jax.nn.sigmoid(scaled) * features[rows, :].astype(F32)).astype(BF)
        gated[rows, :] = low
        parts = []
        for j in range(channels // half):
            cut = slice(j * half, (j + 1) * half)
            for p in range(9):
                work[p] = dot(low, grads[kernel_rows(p), cut])
            parts.append(gather_taps(lambda p: work[p], breadth, col))
        return put_stats(pre_three, rows, jnp.concatenate(parts, axis=1), valid, carry)

    loads[1].wait()
    sums = each_image(geometry, third_step, nothing)
    totals_three = total(2, sums) + [count]

    def out_step(i, rows, carry):
        valid = valid_of(infos, i, height, breadth)
        normal, _, scaled = norm_with(pre_three[rows, :], totals_three, scale_three)
        high, low = split(silu(scaled) * valid)
        mean = (dot(narrow, high) + dot(narrow, low)) * 0.25
        task_out[i] = mean.astype(BF)
        dy = silu_back(scaled) * dot(widen, cotangent[i]) * 0.25 * valid
        lower[rows, :] = dy
        return carry[0] + col_sum(dy), carry[1] + col_sum(dy * normal)

    sums = each_image(geometry, out_step, nothing)
    sums_three = total(3, sums)

    def third_back(i, rows, carry):
        valid = valid_of(infos, i, height, breadth)
        normal, inverse, _ = norm_with(pre_three[rows, :], totals_three, scale_three)
        dz = norm_back_with(lower[rows, :], normal, inverse, count, sums_three, scale_three, valid)
        for p, moved in enumerate(spread_taps(dz, breadth, col)):
            nine[p, rows, :] = moved.astype(BF)
        flow = None
        for p in range(9):
            piece = dot_nt(nine[p, rows, :], grads[kernel_rows(p), :])
            flow = piece if flow is None else flow + piece
        lower[rows, :] = flow
        normal, _, scaled = norm_with(pre_two[rows, :], totals_two, scale_two)
        gate = jax.nn.sigmoid(scaled)
        dy = flow * features[rows, :].astype(F32) * gate * (1.0 - gate) * valid
        pre_three[rows, :] = dy
        return carry[0] + col_sum(dy), carry[1] + col_sum(dy * normal)

    sums = each_image(geometry, third_back, nothing)

    def taps(begin, end):
        def tap(p, carry):
            rows = pl.ds(pl.multiple_of((2 + p) * channels, channels), channels)
            grads[rows, :] = dot_tn(gated[...], nine[p]).astype(BF)
            return carry

        lax.fori_loop(begin, end, tap, 0)

    sums_two = total(4, sums, lambda: taps(0, 4))

    def second_back(i, rows, carry):
        valid = valid_of(infos, i, height, breadth)
        normal, inverse, scaled = norm_with(pre_two[rows, :], totals_two, scale_two)
        dz = norm_back_with(
            pre_three[rows, :], normal, inverse, count, sums_two, scale_two, valid
        ).astype(BF)
        out[rows, :] = dz
        lower[rows, :] = lower[rows, :] * jax.nn.sigmoid(scaled)
        normal, _, scaled = norm_with(pre_one[rows, :], totals_one, scale_one)
        dy = silu_back(scaled) * dot_nt(dz, second[...]) * valid
        pre_three[rows, :] = dy
        return carry[0] + col_sum(dy), carry[1] + col_sum(dy * normal)

    sums = each_image(geometry, second_back, nothing)

    def weight_rows():
        grads[pl.ds(channels, channels), :] = dot_tn(hidden[...], out[...]).astype(BF)
        taps(4, 9)
        if summing:
            for chip in range(1, chips):
                near_copy(chip).start()

    sums_one = total(5, sums, weight_rows)

    def flow_copy(i, rows, step, incoming=False):
        peer = lax.rem(task + (tasks - step if incoming else step), tasks)
        return remote(
            out.at[rows, columns_of(peer, width)], arrived.at[step - 1, rows, :],
            sends.at[i, step], receives.at[i, step], peer, "task",
        )

    def first_back(i, rows, carry):
        valid = valid_of(infos, i, height, breadth)
        normal, inverse, _ = norm_with(pre_one[rows, :], totals_one, scale_one)
        dz = norm_back_with(
            pre_three[rows, :], normal, inverse, count, sums_one, scale_one, valid
        ).astype(BF)
        hidden[rows, :] = dz
        flow = (lower[rows, :] + dot_nt(dz, first[...])) * valid
        out[rows, :] = flow.astype(BF)
        for step in range(1, tasks):
            flow_copy(i, rows, step).start()
        return carry

    each_image(geometry, first_back, 0)
    grads[pl.ds(0, channels), :] = dot_tn(features[...], hidden[...]).astype(BF)
    if summing:
        near_copy(0).start()
        for chip in (*range(1, chips), 0):
            near_copy(chip).wait_recv()
            own = block_rows(grads, 2 * chip + core, block)[...].astype(F32)
            grads_out[chip] = (own + near[chip].astype(F32)).astype(BF)
    else:
        grads_out[...] = grads[...]
    put_sums(norm_sums, sums_one + sums_two + sums_three)

    def settle(i, rows, carry):
        for step in range(1, tasks):
            flow_copy(i, rows, step, True).wait_recv()
        flow = out[rows, columns_of(task, width)].astype(F32)
        for step in range(1, tasks):
            flow = flow + arrived[step - 1, rows, :].astype(F32)
        upstream[rows, :] = flow
        for step in range(1, tasks):
            flow_copy(i, rows, step).wait_send()
        return carry

    each_image(geometry, settle, 0)
    if summing:
        for chip in range(chips):
            near_copy(chip).wait_send()


def head(geometry, tasks, batches, infos, features, weights, cotangent, scales, counts):
    number, height, breadth = geometry
    pixels = height * breadth
    total, channels = features.shape
    width = channels // tasks
    block = weights.shape[0] // batches
    chips = batches // 2
    summing = block % 16 == 0
    outs = [
        shape((number, pixels // 4, channels), BF),
        shape((total, width), F32),
        shape((8, channels), F32),
        shape((chips, block, channels) if summing else weights.shape, BF),
    ]
    scratch = []
    if summing:
        scratch = [pltpu.VMEM((chips, block, channels), BF)]
        scratch += [pltpu.SemaphoreType.DMA((chips,))] * 2
    pooled, upstream, sums, grads = exchange_kernel(
        functools.partial(head_body, geometry, tasks, batches, summing),
        outs,
        "vvhvvv",
        (infos, features, weights, cotangent, scales, counts),
        [
            pltpu.VMEM(weights.shape, BF),
            pltpu.VMEM(features.shape, F32),
            pltpu.VMEM(features.shape, F32),
            pltpu.VMEM(features.shape, F32),
            pltpu.VMEM(features.shape, BF),
            pltpu.VMEM(features.shape, BF),
            pltpu.VMEM((9,) + features.shape, BF),
            pltpu.VMEM((9, pixels, min(channels, 256)), F32),
            pltpu.VMEM(features.shape, F32),
            pltpu.VMEM(features.shape, BF),
            pltpu.VMEM((tasks - 1, total, width), BF),
        ]
        + [pltpu.SemaphoreType.DMA((number, tasks))] * 2
        + total_scratch(6, batches)
        + [pltpu.SemaphoreType.DMA((2,))]
        + scratch,
        2,
        61,
        flops=6 * total * channels * weights.shape[0],
    )
    if summing:
        owned = lax.psum_scatter(
            grads.reshape(chips * block, channels), "batch", scatter_dimension=0,
            axis_index_groups=[list(range(core, batches, 2)) for core in range(2)], tiled=True,
        )
    else:
        owned = lax.psum_scatter(grads, "batch", scatter_dimension=0, tiled=True)
    return pooled, upstream, sums, owned


def trunk_backward_body(
    geometry, tasks, batches,
    infos, upstream, enc_totals, dec_totals, scales, *rest,
):
    kept, rest = rest[:6], rest[6:]
    (enc_grad, dec_grad, flow_out, norm_sums), rest = rest[:4], rest[4:]
    (x, enc_taps, dec_taps, enc_pre, dec_pre, spread), rest = rest[:6], rest[6:]
    (
        nine, change, packed, arrived, pooled, sends, receives,
        mine, slots, total_sends, total_receives, loaded,
    ) = rest
    targets = (x, enc_taps, dec_taps, enc_pre, dec_pre, spread)
    loads = [pltpu.make_async_copy(a, b, loaded.at[k]) for k, (a, b) in enumerate(zip(kept, targets))]
    for k in (4, 2, 5, 3, 1, 0):
        loads[k].start()
    number, height, breadth = geometry
    channels = x.shape[1]
    width = enc_pre.shape[1]
    windows = window_count(height, breadth)
    task = lax.axis_index("task")
    _, col = places(height, breadth)
    widen = pool_choice(height, breadth, windows, False).astype(BF)
    narrow = pool_choice(height, breadth, windows, True)
    nothing = zero_rows(2, width)

    def total(k, rows):
        return total_rows(
            k, "batch", batches, list(rows), mine, slots, total_sends, total_receives
        )

    def change_of(pre, totals, scale, flow):
        def image(i, rows, carry):
            valid = valid_of(infos, i, height, breadth)
            normal, _, scaled = norm_with(pre[rows, :], totals, scale)
            dy = silu_back(scaled) * flow(i, rows) * valid
            change[rows, :] = dy
            return carry[0] + col_sum(dy), carry[1] + col_sum(dy * normal)

        return each_image(geometry, image, nothing)

    def back(pre, totals, scale, sums, taps, put):
        def image(i, rows, carry):
            valid = valid_of(infos, i, height, breadth)
            normal, inverse, _ = norm_with(pre[rows, :], totals, scale)
            dz = norm_back_with(change[rows, :], normal, inverse, totals[2], sums, scale, valid)
            for p, moved in enumerate(spread_taps(dz, breadth, col)):
                nine[rows, p * width : (p + 1) * width] = moved.astype(BF)
            put(i, rows, dot_nt(nine[rows, :], taps[...]) * valid)
            return carry

        each_image(geometry, image, 0)

    totals = rows_of(dec_totals, 0, 3)
    scale = rows_of(scales, 2, 2)
    loads[4].wait()
    sums = change_of(dec_pre, totals, scale, lambda i, rows: upstream[rows, :])
    greet((("task", tasks), ("batch", batches)))
    dec_sums = total(0, sums)

    def copy_of(i, step, incoming=False):
        rows = window_rows(i, windows)
        peer = lax.rem(task + (tasks - step if incoming else step), tasks)
        return remote(
            packed.at[rows, columns_of(peer, width)], arrived.at[step - 1, rows, :],
            sends.at[i, step], receives.at[i, step], peer, "task",
        )

    def put_packed(i, rows, flow):
        chosen = chosen_cells(narrow, infos, i)
        packed[window_rows(i, windows), :] = dot(chosen, flow.astype(BF)).astype(BF)
        for step in range(1, tasks):
            copy_of(i, step).start()

    loads[2].wait()
    back(dec_pre, totals, scale, dec_sums, dec_taps, put_packed)
    loads[5].wait()
    dec_grad[...] = dot_tn(spread[...], nine[...])

    def collect(i, carry):
        for step in range(1, tasks):
            copy_of(i, step, True).wait_recv()
        rows = window_rows(i, windows)
        flow = packed[rows, columns_of(task, width)].astype(F32)
        for step in range(1, tasks):
            flow = flow + arrived[step - 1, rows, :].astype(F32)
        pooled[rows, :] = flow
        for step in range(1, tasks):
            copy_of(i, step).wait_send()
        return carry

    lax.fori_loop(0, number, collect, 0)

    def widened(i, rows):
        high, low = split(pooled[window_rows(i, windows), :])
        return (dot(widen, high) + dot(widen, low)) * 0.25

    totals = rows_of(enc_totals, 0, 3)
    scale = rows_of(scales, 0, 2)
    loads[3].wait()
    sums = change_of(enc_pre, totals, scale, widened)
    enc_sums = total(1, sums)

    def put_flow(i, rows, flow):
        flow_out[rows, :] = flow.astype(BF)

    loads[1].wait()
    back(enc_pre, totals, scale, enc_sums, enc_taps, put_flow)
    loads[0].wait()
    enc_grad[...] = dot_tn(x[...], nine[...])
    put_sums(norm_sums, enc_sums + dec_sums)


def trunk_backward(
    geometry, tasks, batches, infos, upstream, enc_totals, dec_totals, scales, kept
):
    number, height, breadth = geometry
    x, enc_taps, dec_taps = kept[:3]
    total, channels = x.shape
    width = channels // tasks
    windows = window_count(height, breadth)
    outs = [
        shape(enc_taps.shape, F32),
        shape(dec_taps.shape, F32),
        shape(x.shape, BF),
        shape((8, width), F32),
    ]
    return exchange_kernel(
        functools.partial(trunk_backward_body, geometry, tasks, batches),
        outs,
        "vvvvvhhhhhh",
        (infos, upstream, enc_totals, dec_totals, scales, *kept),
        [pltpu.VMEM(a.shape, a.dtype) for a in kept]
        + [
            pltpu.VMEM((total, 9 * width), BF),
            pltpu.VMEM((total, width), F32),
            pltpu.VMEM((number * windows, channels), BF),
            pltpu.VMEM((tasks - 1, number * windows, width), BF),
            pltpu.VMEM((number * windows, width), F32),
        ]
        + [pltpu.SemaphoreType.DMA((number, tasks))] * 2
        + total_scratch(2, batches)
        + [pltpu.SemaphoreType.DMA((6,))],
        3,
        60,
        flops=8 * x.size * enc_taps.shape[1],
    )


def to_slots_body(index, enc, dec, slots, wide):
    count = slots.shape[0]
    channels = enc.shape[0]
    width = slots.shape[1]
    step = 1024
    group = 32
    for p in range(18):
        source = enc if p < 9 else dec
        q = p % 9

        def place(i, carry):
            base = pl.multiple_of(i * group, group)
            values = source[pl.ds(base, group), q * width : (q + 1) * width]
            for u in range(group):
                wide[pl.ds(index[p * channels + base + u], 1), :] = values[u : u + 1, :]
            return carry

        lax.fori_loop(0, channels // group, place, 0)

    def narrow(i, carry):
        rows = pl.ds(pl.multiple_of(i * step, step), step)
        slots[rows, :] = wide[rows, :].astype(BF)
        return carry

    lax.fori_loop(0, count // step, narrow, 0)


def to_slots(index, enc, dec):
    width = enc.shape[1] // 9
    dims = (index.shape[0], width)
    return run(
        to_slots_body, [shape(dims, BF)], "svv", (index, enc, dec), [pltpu.VMEM(dims, F32)], vmem=60
    )[0]


def adam(gradient, moment_one, moment_two):
    new_one = BETA_ONE * moment_one + (1.0 - BETA_ONE) * gradient
    new_two = BETA_TWO * moment_two + (1.0 - BETA_TWO) * gradient * gradient
    direction = (
        new_one / (1.0 - BETA_ONE**STEP) / (jnp.sqrt(new_two / (1.0 - BETA_TWO**STEP)) + ADAM_EPS)
    )
    return new_one, new_two, direction


def pair_place(batches):
    me = lax.axis_index("batch")
    place = lax.div(me, 2)
    return place, me - 2 * place, batches // 2


def greet_pairs(tasks, batches):
    place, core, chips = pair_place(batches)
    task = lax.axis_index("task")
    barrier = pltpu.get_barrier_semaphore()

    def signal(device):
        pl.semaphore_signal(barrier, inc=1, device_id=device, device_id_type=MESH)

    for step in range(1, tasks):
        signal({"task": lax.rem(task + step, tasks)})
    signal({"batch": 2 * place + 1 - core})
    for step in range(1, chips):
        signal({"batch": 2 * lax.rem(place + step, chips) + core})
    pl.semaphore_wait(barrier, tasks - 1 + chips)


def block_rows(ref, index, count):
    return ref.at[pl.ds(pl.multiple_of(index * count, 8), count), :]


SMALL = 128 * 128


def far_first(chips):
    return sorted(range(chips), key=lambda step: -min(step, chips - step))


def pair_sum(batches, rows_of_block, own_block, near, paired, far, sems):
    place, core, chips = pair_place(batches)
    count = near.shape[1]
    near_send, near_receive, far_send, far_receive = sems
    other = 2 * place + 1 - core
    ring = chips == 4 and count % 32 == 0 and near.shape[2] * count > SMALL
    half = count // 2
    halves = (pl.ds(0, half), pl.ds(half, half))

    def near_copy(step):
        chip = lax.rem(place + step, chips)
        return remote(rows_of_block(2 * chip + 1 - core), near.at[step],
                      near_send.at[step], near_receive.at[step], other, "batch")

    def far_copy(step, incoming=False):
        chip = lax.rem(place + (chips - step if incoming else step), chips)
        return remote(paired.at[step], far.at[step], far_send.at[step], far_receive.at[step],
                      2 * chip + core, "batch")

    def ring_copy(which, way):
        chip = lax.rem(place + (1 if way == 0 else chips - 1), chips)
        if which == 0:
            source, target = paired.at[2, halves[way], :], far.at[2 + way, halves[0], :]
        else:
            cut = halves[way] if which == 2 else halves[1 - way]
            source, target = paired.at[1 if way == 0 else 3, cut, :], far.at[way, cut, :]
        k = 2 * which + way
        return remote(source, target, far_send.at[k], far_receive.at[k], 2 * chip + core, "batch")

    def start():
        for step in far_first(chips):
            near_copy(step).start()

    def middle():
        for step in far_first(chips):
            near_copy(step).wait_recv()
            if step:
                paired[step] = (own_block(step) + near[step].astype(F32)).astype(paired.dtype)
                if not ring:
                    far_copy(step).start()
                elif step == 2:
                    ring_copy(0, 0).start()
                    ring_copy(0, 1).start()
                else:
                    ring_copy(1, 0 if step == 1 else 1).start()

    def relay():
        if not ring:
            return
        for way in range(2):
            ring_copy(0, way).wait_recv()
            step = 1 if way == 0 else 3
            total = paired[step, halves[way], :].astype(F32) + far[2 + way, halves[0], :].astype(F32)
            paired[step, halves[way], :] = total.astype(paired.dtype)
            ring_copy(2, way).start()

    def end():
        total = own_block(0) + near[0].astype(F32)
        if ring:
            for way in range(2):
                ring_copy(1, way).wait_recv()
                ring_copy(2, way).wait_recv()
                total = total + far[way].astype(F32)
            for k in range(3):
                for way in range(2):
                    ring_copy(k, way).wait_send()
        else:
            for step in range(1, chips):
                far_copy(step, True).wait_recv()
                total = total + far[step].astype(F32)
            for step in range(1, chips):
                far_copy(step).wait_send()
        for step in range(chips):
            near_copy(step).wait_send()
        return total

    return start, middle, relay, end


def blocks_in(source, batches, count):
    place, core, chips = pair_place(batches)

    def own(step):
        chip = lax.rem(place + step, chips)
        return block_rows(source, 2 * chip + core, count)[...].astype(F32)

    return (lambda index: block_rows(source, index, count)), own


def pair_scratch(batches, rows, width, kind):
    chips = batches // 2
    return [pltpu.VMEM((chips, rows // batches, width), kind)] * 3 + [
        pltpu.SemaphoreType.DMA((max(chips, 6),))
    ] * 4


def chip_spread(batches, block, sends, receives):
    place, core, chips = pair_place(batches)
    count, width = block(place).shape
    ring = chips == 4 and count % 32 == 0 and width * count > SMALL
    half = count // 2

    def copy(step, incoming=False):
        peer = lax.rem(place + (chips - step if incoming else step), chips)
        ref = block(peer if incoming else place)
        return remote(ref, ref, sends.at[step], receives.at[step], 2 * peer + core, "batch")

    def pass_on(way, incoming=False):
        step = 1 if way == 0 else chips - 1
        peer = lax.rem(place + (chips - step if incoming else step), chips)
        home = lax.rem(place + (2 if incoming else chips - step), chips)
        ref = block(home).at[pl.ds(way * half, half), :]
        k = 2 if way == 0 else 0
        return remote(ref, ref, sends.at[k], receives.at[k], 2 * peer + core, "batch")

    steps = (1, chips - 1) if ring else tuple(range(1, chips))

    def start():
        for step in steps:
            copy(step).start()

    def relay():
        if ring:
            for way, step in enumerate(steps):
                copy(step, True).wait_recv()
                pass_on(way).start()

    def settle():
        if ring:
            for way in range(2):
                pass_on(way, True).wait_recv()
        else:
            for step in steps:
                copy(step, True).wait_recv()

    def drain():
        for step in steps:
            copy(step).wait_send()
        if ring:
            for way in range(2):
                pass_on(way).wait_send()

    return start, relay, settle, drain


def arrive_body(
    tasks, batches, geometry,
    image_raw, info, index, weight, head_weight,
    slots, x, infos, owners, head_low,
    image, head_raw, head_loaded, raw, raw_loaded, x_send, x_receive, info_send, info_receive,
    chip_send, chip_receive, pair_send, pair_receive, own,
):
    task = lax.axis_index("task")
    place, core, chips = pair_place(batches)
    count, width = raw.shape
    load = pltpu.make_async_copy(weight.at[:, columns_of(task, width)], raw, raw_loaded)
    load.start()
    head_load = pltpu.make_async_copy(head_weight, head_raw, head_loaded)
    head_load.start()
    number, height, breadth = geometry
    pixels = height * breadth
    for n in range(number):
        valid = valid_rows(info[8 * n + 1 : 8 * n + 2, 0:1], height, breadth)
        rows = slice(n * pixels, (n + 1) * pixels)
        image[rows, :] = (image_raw[rows, :].astype(F32) * valid).astype(BF)
    greet_pairs(tasks, batches)

    def task_copy(source, target, sends, receives, step, incoming=False):
        peer = lax.rem(task + (tasks - step if incoming else step), tasks)
        home = peer if incoming else task
        return remote(source, block_rows(target, home, source.shape[0]), sends.at[step],
                      receives.at[step], peer, "task")

    def moves(step, incoming=False):
        return (
            task_copy(info, infos, info_send, info_receive, step, incoming),
            task_copy(image, x, x_send, x_receive, step, incoming),
        )

    def block(chip):
        return block_rows(slots, 2 * chip + core, count)

    def pair_copy(hop, incoming=False):
        chip = lax.rem(place + chips - hop, chips)
        ref = block_rows(slots, 2 * chip + (1 - core if incoming else core), count)
        return remote(ref, ref, pair_send.at[hop], pair_receive.at[hop], 2 * place + 1 - core, "batch")

    start, relay, settle, drain = chip_spread(batches, block, chip_send, chip_receive)
    ring = chips == 4 and count % 32 == 0 and width * count > SMALL
    load.wait()
    block(place)[...] = raw[...].astype(BF)
    start()
    pair_copy(0).start()
    for step in range(1, tasks):
        for copy in moves(step):
            copy.start()
    locals_ = [
        pltpu.make_async_copy(image, block_rows(x, task, image.shape[0]), own.at[0]),
        pltpu.make_async_copy(info, block_rows(infos, task, info.shape[0]), own.at[1]),
    ]
    for copy in locals_:
        copy.start()
    mine = lax.broadcasted_iota(jnp.int32, (count, 1), 0) + lax.axis_index("batch") * count
    found = jnp.zeros((count, 128), F32)
    for k in range(index.shape[0] // 2, index.shape[0]):
        found = jnp.where(index[k : k + 1, :] == mine, 1.0, found)
    found = jnp.max(found, axis=1, keepdims=True)
    owners[:, 0:1] = 1.0 - found
    owners[:, 1:2] = found
    head_load.wait()
    head_low[...] = head_raw[...].astype(BF)
    relay()
    if ring:
        pair_copy(1).start()
        pair_copy(3).start()
        settle()
        pair_copy(2).start()
    else:
        settle()
        for hop in range(1, chips):
            pair_copy(hop).start()
    for copy in locals_:
        copy.wait()
    for step in range(1, tasks):
        for copy in moves(step, True):
            copy.wait_recv()
    for hop in range(chips):
        pair_copy(hop, True).wait_recv()
    for step in range(1, tasks):
        for copy in moves(step):
            copy.wait_send()
    for hop in range(chips):
        pair_copy(hop).wait_send()
    drain()


def arrive(tasks, batches, geometry, image, info, index, weight, head_weight):
    count, channels = weight.shape
    width = channels // tasks
    chips = batches // 2
    return exchange_kernel(
        functools.partial(arrive_body, tasks, batches, geometry),
        [
            shape((count * batches, width), BF),
            shape((image.shape[0] * tasks, channels), BF),
            shape((info.shape[0] * tasks, info.shape[1]), F32),
            shape((count, 2), F32),
            shape(head_weight.shape, BF),
        ],
        "vvvhh",
        (image, info, index.reshape(-1, 128), weight, head_weight),
        [
            pltpu.VMEM(image.shape, BF),
            pltpu.VMEM(head_weight.shape, F32),
            pltpu.SemaphoreType.DMA,
            pltpu.VMEM((count, width), F32),
            pltpu.SemaphoreType.DMA,
        ]
        + [pltpu.SemaphoreType.DMA((tasks,))] * 4
        + [pltpu.SemaphoreType.DMA((max(chips, 4),))] * 4
        + [pltpu.SemaphoreType.DMA((2,))],
        4,
        60,
        flops=20000 * MIB,
    )


def soap_rows(cuts, grad, owners, state, low, first, begin=0, end=None):
    total = grad.shape[0]

    def chunk(i, carry):
        rows = pl.ds(pl.multiple_of(i * (total // cuts), 8), total // cuts)
        values = grad[rows, :].astype(F32)
        marks = owners(i * (total // cuts), total // cuts)
        count = len(marks)
        rotated = None
        for m in range(count):
            part = dot((values * marks[m]).astype(BF), low[first + m])
            rotated = part if rotated is None else rotated + part
        new_one, new_two, direction = adam(rotated, state[1, rows, :], state[2, rows, :])
        state[1, rows, :] = new_one
        state[2, rows, :] = new_two
        stepped = None
        for m in range(count):
            part = dot_nt((direction * marks[m]).astype(BF), low[first + m])
            stepped = part if stepped is None else stepped + part
        old = state[0, rows, :]
        state[0, rows, :] = old - LEARN_MATRIX * (stepped + DECAY_MATRIX * old)
        return carry

    lax.fori_loop(begin, cuts if end is None else end, chunk, 0)


def factor_rows(values, identity, turn):
    size, width = values.shape
    sub = lax.broadcasted_iota(jnp.int32, (size, width), 0)
    rolled = pltpu.roll(values, turn, 1)
    columns = [jnp.broadcast_to(rolled[:, j : j + 1], (size, width)) for j in range(size)]
    scale = jnp.zeros((size, width), F32)
    for j in range(size):
        root = lax.rsqrt(columns[j][j : j + 1, :])
        scale = jnp.where(sub == j, root, scale)
        lower = jnp.where(sub > j, columns[j] * root, 0.0)
        values = values - lower * (values[j : j + 1, :] * root)
        identity = identity - lower * (identity[j : j + 1, :] * root)
        for i in range(j + 1, size):
            columns[i] = columns[i] - lower * (columns[i][j : j + 1, :] * root)
    return values * scale, identity * scale


GROUP = 16
PANEL = 128


def renew_panel(k, product, made, tables, inverses):
    count, size = product.shape[0], product.shape[1]
    here = slice(k * PANEL, (k + 1) * PANEL)
    row = lax.broadcasted_iota(jnp.int32, (PANEL, PANEL), 0)
    col = lax.broadcasted_iota(jnp.int32, (PANEL, PANEL), 1)
    unit = jnp.where(row == col, 1.0, 0.0).astype(F32)
    for n in range(count):
        tables[n][:, :PANEL] = dot3(dot_tn, product[n, :, here], product[n, :, here])
        tables[n][:, PANEL:] = unit

    def group(q, carry):
        rows = pl.ds(pl.multiple_of(q * GROUP, GROUP), GROUP)
        turn = lax.rem(PANEL - q * GROUP, PANEL)
        done = [
            factor_rows(tables[n][rows, :PANEL], tables[n][rows, PANEL:], turn)
            for n in range(count)
        ]
        for n in range(count):
            upper, inverse = done[n]
            inverses[n][rows, :] = inverse
            both = jnp.concatenate([upper, inverse], axis=1)
            tables[n][...] = tables[n][...] - dot3(dot_tn, upper, both)
        return carry

    lax.fori_loop(0, PANEL // GROUP, group, 0)
    for n in range(count):
        turned = dot3(dot_nt, product[n, :, here], inverses[n][...])
        made[n, :, here] = turned
        if k < size // PANEL - 1:
            rest = slice((k + 1) * PANEL, size)
            product[n, :, rest] = product[n, :, rest] - dot3(
                dot, turned, dot3(dot_tn, turned, product[n, :, rest])
            )


def tail_body(
    tasks, batches, cuts,
    slots, flow, sums, owners, head_grad,
    weight, one, two, head_weight, head_one, head_two, basis, head_basis,
    input_grad, norm_sums, state_new, head_state_new, grams, head_grams,
    grad, part, state, head_state, mine, head_mine, bases, low,
    flow_in, flow_send, flow_receive, send, receive, sum_send, sum_receive,
    *rest,
):
    row_scratch, gram_scratch, head_scratch = rest[:7], rest[7:14], rest[14:21]
    chip_send, chip_receive, task_send, task_receive, pair_send, pair_receive, load, save = rest[21:]
    task = lax.axis_index("task")
    place, core, chips = pair_place(batches)
    width = part.shape[1]
    channels = grad.shape[1]
    pixels = input_grad.shape[0]
    trunk_total = basis.shape[0]
    head_total = head_basis.shape[0]
    count, head_count = mine.shape[0] // batches, head_mine.shape[0] // batches

    def trunk_marks(start, size):
        rows = pl.ds(pl.multiple_of(start, 8), size)
        return [owners[rows, m : m + 1] for m in range(trunk_total)]

    def head_marks(start, size):
        index = lax.broadcasted_iota(jnp.int32, (size, 1), 0) + start
        index = index + lax.axis_index("batch") * head_grad.shape[0]
        owner = jnp.minimum(lax.div(index, channels), head_total - 1)
        return [jnp.where(owner == m, 1.0, 0.0).astype(F32) for m in range(head_total)]

    def put_grams(target, rows, columns, marks):
        for m, mark in enumerate(marks):
            held = (rows[...].astype(F32) * mark).astype(BF)
            target[m * channels : (m + 1) * channels, :] = dot_tn(held, columns[...]).astype(
                target.dtype
            )

    def peer_of(step, incoming):
        return lax.rem(task + (tasks - step if incoming else step), tasks)

    def flow_copy(step, incoming=False):
        peer = peer_of(step, incoming)
        return remote(block_rows(flow, peer, pixels), flow_in.at[step - 1], flow_send.at[step],
                      flow_receive.at[step], peer, "task")

    def sum_copy(step, incoming=False):
        peer = peer_of(step, incoming)
        home = peer if incoming else task
        return remote(sums, norm_sums.at[:, columns_of(home, width)], sum_send.at[step],
                      sum_receive.at[step], peer, "task")

    def part_copy(step, incoming=False):
        peer = peer_of(step, incoming)
        home = peer if incoming else task
        return remote(part, grad.at[:, columns_of(home, width)], send.at[step], receive.at[step],
                      peer, "task")

    def trunk_block(chip, home, which):
        rows = pl.ds(pl.multiple_of((2 * chip + which) * count, 8), count)
        return grams.at[rows, columns_of(home, width)]

    def head_block(chip, which):
        return block_rows(head_grams, 2 * chip + which, head_count)

    def task_copy(step, hop, incoming=False):
        peer = peer_of(step, incoming)
        chip = lax.rem(place + chips - hop, chips)
        block = trunk_block(chip, peer if incoming else task, core)
        return remote(block, block, task_send.at[step, hop], task_receive.at[step, hop], peer, "task")

    def pair_copy(kind, hop, incoming=False):
        chip = lax.rem(place + chips - hop, chips)
        which = 1 - core if incoming else core
        home = lax.rem(task + tasks - kind, tasks)
        block = head_block(chip, which) if kind == tasks else trunk_block(chip, home, which)
        return remote(block, block, pair_send.at[kind, hop], pair_receive.at[kind, hop],
                      2 * place + 1 - core, "batch")

    def sum_of(source, scratch):
        near, paired, far, *sems = scratch
        return pair_sum(
            batches, *blocks_in(source, batches, near.shape[1]), near, paired, far, sems
        )

    moves = [
        (basis, bases.at[pl.ds(0, trunk_total)]),
        (head_basis, bases.at[pl.ds(trunk_total, head_total)]),
        (head_weight, head_state.at[0]),
        (head_one, head_state.at[1]),
        (head_two, head_state.at[2]),
        (weight, state.at[0]),
        (one, state.at[1]),
        (two, state.at[2]),
    ]
    loads = [pltpu.make_async_copy(a, b, load.at[k]) for k, (a, b) in enumerate(moves)]
    for copy in loads:
        copy.start()
    saves = [
        pltpu.make_async_copy(state, state_new, save.at[0]),
        pltpu.make_async_copy(head_state, head_state_new, save.at[1]),
    ]

    greet_pairs(tasks, batches)
    row_start, row_middle, row_relay, row_end = sum_of(slots, row_scratch)
    row_start()
    for step in range(1, tasks):
        sum_copy(step).start()
        flow_copy(step).start()
    norm_sums[:, columns_of(task, width)] = sums[...]
    row_middle()
    put_grams(head_mine, head_grad, head_grad, head_marks(0, head_grad.shape[0]))
    head_start, head_middle, head_relay, head_end = sum_of(head_mine, head_scratch)
    head_start()
    row_relay()
    head_middle()
    for copy in loads[:5]:
        copy.wait()
    for m in range(trunk_total + head_total):
        low[m] = bases[m].astype(BF)
    total = row_end().astype(BF)
    part[...] = total
    for step in range(1, tasks):
        part_copy(step).start()
    grad[:, columns_of(task, width)] = total
    head_relay()

    soap_rows(cuts, head_grad, head_marks, head_state, low, trunk_total)
    saves[1].start()
    total = block_rows(flow, task, pixels)[...].astype(F32)
    for step in range(1, tasks):
        flow_copy(step, True).wait_recv()
        total = total + flow_in[step - 1].astype(F32)
    input_grad[...] = total
    head_block(place, core)[...] = head_end().astype(head_grams.dtype)
    trunk_spread = chip_spread(
        batches, lambda chip: trunk_block(chip, task, core), chip_send.at[0], chip_receive.at[0]
    )
    head_spread = chip_spread(
        batches, lambda chip: head_block(chip, core), chip_send.at[1], chip_receive.at[1]
    )
    head_spread[0]()
    pair_copy(tasks, 0).start()
    for step in range(1, tasks):
        part_copy(step, True).wait_recv()

    put_grams(mine, grad, part, trunk_marks(0, grad.shape[0]))
    start, middle, relay, end = sum_of(mine, gram_scratch)
    start()
    middle()
    head_spread[1]()
    for copy in loads[5:]:
        copy.wait()
    relay()
    soap_rows(cuts, grad, trunk_marks, state, low, 0, 0, cuts // 2)
    trunk_block(place, task, core)[...] = end().astype(grams.dtype)
    trunk_spread[0]()
    for step in range(1, tasks):
        task_copy(step, 0).start()
    pair_copy(0, 0).start()
    soap_rows(cuts, grad, trunk_marks, state, low, 0, cuts // 2, cuts)
    saves[0].start()
    trunk_spread[1]()
    trunk_spread[2]()
    for hop in range(1, chips):
        for step in range(1, tasks):
            task_copy(step, hop).start()
        pair_copy(0, hop).start()
    head_spread[2]()
    for hop in range(1, chips):
        pair_copy(tasks, hop).start()
    for hop in range(chips):
        for step in range(1, tasks):
            task_copy(step, hop, True).wait_recv()
            pair_copy(step, hop).start()
    for hop in range(chips):
        for kind in range(tasks + 1):
            pair_copy(kind, hop, True).wait_recv()
    for step in range(1, tasks):
        sum_copy(step, True).wait_recv()

    for copy in saves:
        copy.wait()
    for step in range(1, tasks):
        sum_copy(step).wait_send()
        part_copy(step).wait_send()
        flow_copy(step).wait_send()
    for hop in range(chips):
        for kind in range(tasks + 1):
            pair_copy(kind, hop).wait_send()
        for step in range(1, tasks):
            task_copy(step, hop).wait_send()
    trunk_spread[3]()
    head_spread[3]()


def renew_body(
    state, head_state, grams, head_grams, stat, head_stat, basis, head_basis,
    weight_new, one_new, two_new, head_weight_new, head_one_new, head_two_new,
    stat_new, head_stat_new, basis_new, head_basis_new,
    stats, product, made, held, head_held, load, save, *work,
):
    trunk_total, head_total = stat.shape[0], head_stat.shape[0]
    channels = stat.shape[1]
    count = trunk_total + head_total
    tables, inverses = work[:count], work[count:]
    loads = [
        pltpu.make_async_copy(state, held, load.at[0]),
        pltpu.make_async_copy(head_state, head_held, load.at[1]),
    ]
    for copy in loads:
        copy.start()
    sources = [held.at[k] for k in range(3)] + [head_held.at[k] for k in range(3)]
    targets = [weight_new, one_new, two_new, head_weight_new, head_one_new, head_two_new]
    saves = [pltpu.make_async_copy(a, b, save.at[k]) for k, (a, b) in enumerate(zip(sources, targets))]
    for m in range(count):
        first = m < trunk_total
        place = m if first else m - trunk_total
        gram = (grams if first else head_grams)[place * channels : (place + 1) * channels, :]
        old = (stat if first else head_stat)[place]
        stats[m] = STAT_DECAY * old + (1.0 - STAT_DECAY) * gram.astype(F32)
        product[m] = dot3(dot, stats[m], (basis if first else head_basis)[place])
    groups = ((0, trunk_total, stat_new, basis_new), (trunk_total, head_total, head_stat_new, head_basis_new))
    for begin, size, out, _ in groups:
        copy = pltpu.make_async_copy(stats.at[pl.ds(begin, size)], out, save.at[len(saves)])
        copy.start()
        saves.append(copy)
    for copy in loads:
        copy.wait()
    for copy in saves[:6]:
        copy.start()
    for k in range(channels // PANEL):
        renew_panel(k, product, made, tables, inverses)
        cut = pl.ds(k * PANEL, PANEL)
        for begin, size, _, out in groups:
            copy = pltpu.make_async_copy(
                made.at[pl.ds(begin, size), :, cut], out.at[:, :, cut], save.at[len(saves)]
            )
            copy.start()
            saves.append(copy)
    for copy in saves:
        copy.wait()


def finish(tasks, batches, local_grads, rows, matrices):
    slots, flow, sums, owners, head_grad = local_grads
    stat, head_stat, basis, head_basis = matrices
    total, channels = rows[0].shape
    width = channels // tasks
    trunk_total, head_total = basis.shape[0], head_basis.shape[0]
    gram_rows, head_rows = trunk_total * channels, head_total * channels
    chips = batches // 2
    kind = BF if gram_rows % (16 * batches) == 0 else F32
    head_kind = BF if head_rows % (16 * batches) == 0 else F32
    cuts = 4 if total % 64 == 0 and head_grad.shape[0] % 64 == 0 else 1
    square = (trunk_total + head_total, channels, channels)
    pixels = flow.shape[0] // tasks
    input_grad, norm_sums, *made = exchange_kernel(
        functools.partial(tail_body, tasks, batches, cuts),
        [
            shape((pixels, channels), F32),
            shape((8, channels), F32),
            shape((3, total, channels), F32),
            shape((3,) + head_grad.shape, F32),
            shape((gram_rows, channels), kind),
            shape((head_rows, channels), head_kind),
        ],
        "vvvvvhhhhhhhh",
        (*local_grads, *rows, basis, head_basis),
        [
            pltpu.VMEM((total, channels), BF),
            pltpu.VMEM((total, width), BF),
            pltpu.VMEM((3, total, channels), F32),
            pltpu.VMEM((3,) + head_grad.shape, F32),
            pltpu.VMEM((gram_rows, width), kind),
            pltpu.VMEM((head_rows, channels), head_kind),
            pltpu.VMEM(square, F32),
            pltpu.VMEM(square, BF),
            pltpu.VMEM((tasks - 1, pixels, channels), BF),
        ]
        + [pltpu.SemaphoreType.DMA((tasks,))] * 6
        + pair_scratch(batches, slots.shape[0], width, BF)
        + pair_scratch(batches, gram_rows, width, kind)
        + pair_scratch(batches, head_rows, channels, head_kind)
        + [pltpu.SemaphoreType.DMA((2, max(chips, 4)))] * 2
        + [pltpu.SemaphoreType.DMA((tasks, chips))] * 2
        + [pltpu.SemaphoreType.DMA((tasks + 1, chips))] * 2
        + [pltpu.SemaphoreType.DMA((8,)), pltpu.SemaphoreType.DMA((2,))],
        5,
        60,
        flops=50000 * MIB,
        places_out="vvhhvv",
    )
    outs = [shape(a.shape, F32) for a in (*rows, *matrices)]
    hbm = pl.BlockSpec(memory_space=pltpu.HBM)
    count = trunk_total + head_total
    results = pl.pallas_call(
        renew_body,
        out_shape=tuple(outs),
        in_specs=[hbm] * 2 + [VMEM_SPEC] * 6,
        out_specs=tuple(hbm for _ in outs),
        scratch_shapes=[pltpu.VMEM(square, F32)] * 3
        + [pltpu.VMEM(made[0].shape, F32), pltpu.VMEM(made[1].shape, F32)]
        + [pltpu.SemaphoreType.DMA((2,))]
        + [pltpu.SemaphoreType.DMA((8 + 2 * (channels // PANEL),))]
        + [pltpu.VMEM((PANEL, 2 * PANEL), F32)] * count
        + [pltpu.VMEM((PANEL, PANEL), F32)] * count,
        compiler_params=pltpu.CompilerParams(vmem_limit_bytes=60 * MIB),
        cost_estimate=pl.CostEstimate(
            flops=60000 * MIB, bytes_accessed=64 * MIB, transcendentals=0
        ),
    )(*made, *matrices)
    return input_grad, norm_sums, results


def local(
    tasks,
    batches,
    images,
    image_small,
    pool_index,
    row_slot,
    trunk_weight,
    trunk_mean_grad,
    trunk_mean_square,
    trunk_statistic,
    trunk_basis,
    head_weight,
    head_mean_grad,
    head_mean_square,
    head_statistic,
    head_basis,
    trunk_gain,
    trunk_offset,
    trunk_norm_mean_grad,
    trunk_norm_mean_square,
    head_gain,
    head_offset,
    head_norm_mean_grad,
    head_norm_mean_square,
    cotangent,
):
    number, height, breadth, channels = images.shape
    pixels = height * breadth
    shown = tasks * number
    geometry = (shown, height, breadth)
    task = lax.axis_index("task")
    width = channels // tasks

    def quarter(values):
        return lax.dynamic_slice_in_dim(values, task * width, width, values.ndim - 1)

    def inside(flags):
        row_limit = jnp.where(flags > 0, height // 2, height)[:, None, None]
        col_limit = jnp.where(flags > 0, breadth // 2, breadth)[:, None, None]
        return (jnp.arange(height, dtype=jnp.int32)[None, :, None] < row_limit) & (
            jnp.arange(breadth, dtype=jnp.int32)[None, None, :] < col_limit
        )

    cell = 2 * jnp.arange(2, dtype=jnp.int32)[:, None, None] + jnp.arange(2, dtype=jnp.int32)
    cells = pool_index.reshape(number, height // 2, 1, breadth // 2, 1)
    valid = inside(image_small)
    chosen = ((cells == cell).reshape(number, height, breadth) & valid).reshape(number, pixels)
    info = jnp.zeros((8 * number, channels), F32)
    info = info.at[::8, :pixels].set(chosen.astype(F32))
    info = info.at[1::8, 0].set(image_small.astype(F32))
    slots, x, infos, trunk_owners, head_low = arrive(
        tasks, batches, (number, height, breadth), images.reshape(number * pixels, channels),
        info, row_slot, trunk_weight, head_weight[0],
    )
    head_rows = lax.all_gather(head_low, "batch", axis=0, tiled=True)

    scales = quarter(jnp.stack([trunk_gain, trunk_offset], axis=1)).reshape(4, width)
    enc_totals, dec_totals, features, *kept = trunk_forward(
        geometry, tasks, batches, row_slot, infos, x, slots, scales
    )
    head_scales = jnp.stack([head_gain[0], head_offset[0]], axis=1).reshape(6, channels)
    pooled, upstream, head_sums, head_owned = head(
        geometry, tasks, batches, infos, features, head_rows,
        cotangent.reshape(shown, pixels // 4, channels), head_scales, enc_totals,
    )
    task_features = pooled.reshape(cotangent.shape)
    enc_grad, dec_grad, flow, trunk_sums = trunk_backward(
        geometry, tasks, batches, infos, upstream, enc_totals, dec_totals, scales, kept
    )
    input_grad, norm_sums, results = finish(
        tasks, batches,
        (to_slots(row_slot, enc_grad, dec_grad), flow, trunk_sums, trunk_owners, head_owned),
        (trunk_weight, trunk_mean_grad, trunk_mean_square,
         head_weight[0], head_mean_grad[0], head_mean_square[0]),
        (trunk_statistic, head_statistic[0], trunk_basis, head_basis[0]),
    )
    input_grad = input_grad.reshape(images.shape)
    (
        trunk_weight_new, trunk_one_new, trunk_two_new,
        head_weight_new, head_one_new, head_two_new,
        trunk_stat_new, head_stat_new, trunk_basis_new, head_basis_new,
    ) = results

    trunk_norm = jnp.stack([trunk_gain, trunk_offset], axis=1)
    trunk_norm_grad = norm_sums[:4].reshape(2, 2, channels)[:, ::-1]
    trunk_norm_one, trunk_norm_two, trunk_direction = adam(
        trunk_norm_grad, trunk_norm_mean_grad, trunk_norm_mean_square
    )
    head_norm = jnp.stack([head_gain, head_offset], axis=2)
    head_norm_grad = head_sums[:6].reshape(1, 3, 2, channels)[:, :, ::-1]
    head_norm_one, head_norm_two, head_direction = adam(
        head_norm_grad, head_norm_mean_grad, head_norm_mean_square
    )
    return (
        task_features,
        input_grad,
        trunk_weight_new,
        trunk_one_new,
        trunk_two_new,
        trunk_stat_new,
        trunk_basis_new,
        head_weight_new[None],
        head_one_new[None],
        head_two_new[None],
        head_stat_new[None],
        head_basis_new[None],
        trunk_norm - LEARN_NORM * trunk_direction,
        trunk_norm_one,
        trunk_norm_two,
        head_norm - LEARN_NORM * head_direction,
        head_norm_one,
        head_norm_two,
    )


def solution(mesh):
    placed = (
        P(("task", "batch"), None, None, None),
        P(("task", "batch")),
        P(("task", "batch"), None, None),
        P(),
        P("batch", None),
        P("batch", None),
        P("batch", None),
        P(),
        P(),
        P("task", "batch", None),
        P("task", "batch", None),
        P("task", "batch", None),
        P("task", None, None, None),
        P("task", None, None, None),
        P(),
        P(),
        P(),
        P(),
        P("task", None, None),
        P("task", None, None),
        P("task", None, None, None),
        P("task", None, None, None),
        P("task", None, "batch", None, None, None),
    )
    return jax.shard_map(
        functools.partial(local, mesh.shape["task"], mesh.shape["batch"]),
        mesh=mesh,
        in_specs=placed,
        out_specs=(
            P("task", None, "batch", None, None, None),
            P(("task", "batch"), None, None, None),
            P("batch", None),
            P("batch", None),
            P("batch", None),
            P(),
            P(),
            P("task", "batch", None),
            P("task", "batch", None),
            P("task", "batch", None),
            P("task", None, None, None),
            P("task", None, None, None),
            P(),
            P(),
            P(),
            P("task", None, None, None),
            P("task", None, None, None),
            P("task", None, None, None),
        ),
        check_vma=False,
    )
```

```python
import functools

import jax
import jax.numpy as jnp
from jax import lax
from jax.experimental import pallas as pl
from jax.experimental.pallas import tpu as pltpu
from jax.sharding import PartitionSpec as P

STEP = 10


EPS = 1e-05
ADAM_EPS = 1e-08
BETA_ONE = 0.95
BETA_TWO = 0.95
STAT_DECAY = 0.95
LEARN_MATRIX = 0.02
LEARN_NORM = 0.5
DECAY_MATRIX = 0.01
BF = jnp.bfloat16
F32 = jnp.float32
MESH = pl.DeviceIdType.MESH
MIB = 1 << 20

VMEM_SPEC = pl.BlockSpec(memory_space=pltpu.VMEM)
SMEM_SPEC = pl.BlockSpec(memory_space=pltpu.SMEM)


def run(body, outs, specs, args, scratch=(), vmem=40, flops=0):
    size = sum(o.size * o.dtype.itemsize for o in outs) + sum(a.size * a.dtype.itemsize for a in args)
    return pl.pallas_call(
        body,
        out_shape=tuple(outs),
        in_specs=[SMEM_SPEC if s == "s" else VMEM_SPEC for s in specs],
        out_specs=tuple(VMEM_SPEC for _ in outs),
        scratch_shapes=list(scratch),
        compiler_params=pltpu.CompilerParams(vmem_limit_bytes=vmem * MIB),
        cost_estimate=pl.CostEstimate(flops=flops, bytes_accessed=size, transcendentals=0),
    )(*args)


def shape(dims, kind):
    return jax.ShapeDtypeStruct(tuple(dims), kind)


def dot(a, b):
    return jnp.dot(a, b, preferred_element_type=F32)


def dot_nt(a, b):
    return lax.dot_general(a, b, (((1,), (1,)), ((), ())), preferred_element_type=F32)


def dot_tn(a, b):
    return lax.dot_general(a, b, (((0,), (0,)), ((), ())), preferred_element_type=F32)


def split(a):
    high = a.astype(BF)
    return high, (a - high.astype(F32)).astype(BF)


def dot3(kind, a, b):
    dims = {dot: (1, 0), dot_nt: (1, 1), dot_tn: (0, 0)}[kind]
    a_high, a_low = split(a)
    b_high, b_low = split(b)
    return kind(
        jnp.concatenate([a_high, a_high, a_low], axis=dims[0]),
        jnp.concatenate([b_high, b_low, b_high], axis=dims[1]),
    )


def places(height, breadth):
    index = lax.broadcasted_iota(jnp.int32, (height * breadth, 1), 0)
    row = lax.div(index, breadth)
    return row, index - row * breadth


def valid_rows(kind, height, breadth):
    row, col = places(height, breadth)
    shrunk = kind > 0
    row_limit = jnp.where(shrunk, height // 2, height)
    col_limit = jnp.where(shrunk, breadth // 2, breadth)
    return jnp.where((row < row_limit) & (col < col_limit), 1.0, 0.0).astype(F32)


def move(values, rows):
    gap = jnp.zeros((abs(rows),) + values.shape[1:], values.dtype)
    if rows > 0:
        return jnp.concatenate([gap, values[:-rows]], axis=0)
    return jnp.concatenate([values[-rows:], gap], axis=0)


def from_left(values, col):
    return jnp.where(col > 0, pltpu.roll(values, 1, 0), 0.0)


def from_right(values, col, breadth):
    return jnp.where(col < breadth - 1, pltpu.roll(values, values.shape[0] - 1, 0), 0.0)


def gather_taps(tap, breadth, col):
    lines = [move(tap(b), breadth) + tap(3 + b) + move(tap(6 + b), -breadth) for b in range(3)]
    return lines[1] + from_left(lines[0], col) + from_right(lines[2], col, breadth)


def spread_taps(values, breadth, col):
    lines = [from_right(values, col, breadth), values, from_left(values, col)]
    return [
        move(lines[b], breadth * (a - 1)) if a != 1 else lines[b] for a in range(3) for b in range(3)
    ]


def window_sum(values, row, col, breadth):
    count = values.shape[0]
    pair = values + jnp.where(
        col % 2 == 0, pltpu.roll(values, count - 1, 0), pltpu.roll(values, 1, 0)
    )
    return pair + jnp.where(row % 2 == 0, move(pair, -breadth), move(pair, breadth))


def silu_back(scaled):
    sig = jax.nn.sigmoid(scaled)
    return sig * (1.0 + scaled * (1.0 - sig))


def col_sum(values):
    return jnp.sum(values, axis=0, keepdims=True)


def put_sums(ref, rows):
    width = ref.shape[1]
    rows = list(rows) + [jnp.zeros((1, width), F32)] * (8 - len(rows))
    ref[...] = jnp.concatenate(rows, axis=0)


def each_image(geometry, body, start):
    number, height, breadth = geometry
    pixels = height * breadth

    def step(image, carry):
        return body(image, pl.ds(pl.multiple_of(image * pixels, 16), pixels), carry)

    return lax.fori_loop(0, number, step, start)


def zero_rows(count, width):
    return (jnp.zeros((1, width), F32),) * count


def greet(axes):
    barrier = pltpu.get_barrier_semaphore()
    for axis, size in axes:
        me = lax.axis_index(axis)
        for step in range(1, size):
            pl.semaphore_signal(
                barrier, inc=1, device_id={axis: lax.rem(me + step, size)}, device_id_type=MESH
            )
    pl.semaphore_wait(barrier, sum(size - 1 for _, size in axes))


def remote(source, target, sends, receives, peer, axis):
    return pltpu.make_async_remote_copy(
        src_ref=source,
        dst_ref=target,
        send_sem=sends,
        recv_sem=receives,
        device_id={axis: peer},
        device_id_type=MESH,
    )


def pack(rows):
    parts = [row[:, i : i + 128] for row in rows for i in range(0, row.shape[1], 128)]
    parts += [jnp.zeros((1, 128), F32)] * (8 - len(parts))
    return jnp.concatenate(parts, axis=0)


def unpack(tile, count, width):
    per = width // 128
    return [
        jnp.concatenate([tile[k * per + i : k * per + i + 1, :] for i in range(per)], axis=1)
        for k in range(count)
    ]


def total_rows(k, axis, size, rows, mine, slots, sends, receives, meanwhile=None):
    me = lax.axis_index(axis)
    tile = pack(rows)
    mine[k] = tile
    slots[k, me] = tile
    for step in range(1, size):
        peer = lax.rem(me + step, size)
        remote(mine.at[k], slots.at[k, me], sends.at[k, step], receives.at[k, me], peer, axis).start()
    if meanwhile:
        meanwhile()
    for step in range(1, size):
        peer = lax.rem(me + size - step, size)
        remote(
            mine.at[k], slots.at[k, peer], sends.at[k, step], receives.at[k, peer], peer, axis
        ).wait_recv()
    total = slots[k, 0]
    for peer in range(1, size):
        total = total + slots[k, peer]
    for step in range(1, size):
        peer = lax.rem(me + step, size)
        remote(
            mine.at[k], slots.at[k, me], sends.at[k, step], receives.at[k, me], peer, axis
        ).wait_send()
    return unpack(total, len(rows), rows[0].shape[1])


def total_scratch(count, size):
    return [
        pltpu.VMEM((count, 8, 128), F32),
        pltpu.VMEM((count, size, 8, 128), F32),
        pltpu.SemaphoreType.DMA((count, size)),
        pltpu.SemaphoreType.DMA((count, size)),
    ]


def columns_of(place, width):
    return pl.ds(pl.multiple_of(place * width, 128), width)


SPECS = {"s": SMEM_SPEC, "v": VMEM_SPEC, "h": pl.BlockSpec(memory_space=pltpu.HBM)}


def exchange_kernel(body, outs, specs, args, scratch, identity, vmem, flops=0, places_out=None):
    size = sum(o.size * o.dtype.itemsize for o in outs) + sum(a.size * a.dtype.itemsize for a in args)
    return pl.pallas_call(
        body,
        out_shape=tuple(outs),
        in_specs=[SPECS[s] for s in specs],
        out_specs=tuple(SPECS[s] for s in places_out or "v" * len(outs)),
        scratch_shapes=list(scratch),
        compiler_params=pltpu.CompilerParams(
            vmem_limit_bytes=vmem * MIB, collective_id=identity, has_side_effects=True
        ),
        cost_estimate=pl.CostEstimate(flops=flops, bytes_accessed=size, transcendentals=0),
    )(*args)


def info_rows(infos, i):
    return infos[pl.ds(pl.multiple_of(i * 8, 8), 8), :]


def valid_of(infos, i, height, breadth):
    return valid_rows(info_rows(infos, i)[1:2, 0:1], height, breadth)


def chosen_cells(narrow, infos, i):
    return (narrow * info_rows(infos, i)[0:1, : narrow.shape[1]]).astype(BF)


def norm_with(values, totals, scale):
    total, squares, count = totals
    center = total / count
    inverse = lax.rsqrt(squares / count - center * center + EPS)
    normal = (values - center) * inverse
    return normal, inverse, normal * scale[0] + scale[1]


def norm_back_with(upstream, normal, inverse, count, sums, scale, valid):
    return scale[0] * inverse * (upstream - sums[0] / count - normal * (sums[1] / count)) * valid


def silu(values):
    return values * jax.nn.sigmoid(values)


def window_count(height, breadth):
    return -(-(height * breadth // 4) // 16) * 16


def pool_choice(height, breadth, windows, flipped):
    pixels = height * breadth
    dims = (windows, pixels) if flipped else (pixels, windows)
    pixel = lax.broadcasted_iota(jnp.int32, dims, 1 if flipped else 0)
    window = lax.broadcasted_iota(jnp.int32, dims, 0 if flipped else 1)
    row = lax.div(pixel, breadth)
    col = pixel - row * breadth
    home = lax.div(row, 2) * (breadth // 2) + lax.div(col, 2)
    return jnp.where(home == window, 1.0, 0.0).astype(F32)


def rows_of(ref, first, count):
    return [ref[first + k : first + k + 1, :] for k in range(count)]


def window_rows(i, windows):
    return pl.ds(pl.multiple_of(i * windows, 16), windows)


def trunk_forward_body(
    geometry, tasks, batches,
    index, infos, x, kernel_slots, scales,
    enc_totals, dec_totals, features, *rest,
):
    kept, (enc_pre, dec_pre, spread), rest = rest[:6], rest[6:9], rest[9:]
    (
        enc_taps, dec_taps, wide, tap,
        work, pooled, pooled_all, part, pool_sends, pool_receives, sends, receives,
    mine, slots, total_sends, total_receives, saved,
    ) = rest
    number, height, breadth = geometry
    width = enc_pre.shape[1]
    windows = window_count(height, breadth)
    task = lax.axis_index("task")
    _, col = places(height, breadth)
    choice = pool_choice(height, breadth, windows, True)
    narrow = choice.astype(BF)

    sources = (x, enc_taps, dec_taps, enc_pre, dec_pre, spread)
    saves = [pltpu.make_async_copy(a, b, saved.at[k]) for k, (a, b) in enumerate(zip(sources, kept))]
    saves[0].start()
    channels = x.shape[1]

    def widen(i, carry):
        rows = pl.ds(pl.multiple_of(i * channels, 16), channels)
        wide[rows, :] = kernel_slots[rows, :].astype(F32)
        return carry

    def fetch(taps, first, begin, end):
        group = 32
        for p in range(begin, end):

            def some(i, carry):
                base = i * group
                for u in range(group):
                    slot = index[(first + p) * channels + base + u]
                    tap[pl.ds(base + u, 1), :] = wide[pl.ds(slot, 1), :]
                return carry

            lax.fori_loop(0, channels // group, some, 0)
            taps[:, p * width : (p + 1) * width] = tap[...].astype(BF)

    lax.fori_loop(0, wide.shape[0] // channels, widen, 0)
    fetch(enc_taps, 0, 0, 9)
    saves[1].start()

    def conv(x, taps, pre):
        def image(i, rows, carry):
            valid = valid_of(infos, i, height, breadth)
            work[...] = dot(x[rows, :], taps[...])
            out = gather_taps(lambda p: work[:, p * width : (p + 1) * width], breadth, col)
            pre[rows, :] = out
            kept = out * valid
            return (
                carry[0] + col_sum(kept),
                carry[1] + col_sum(kept * out),
                carry[2] + jnp.broadcast_to(col_sum(valid), (1, width)),
            )

        return each_image(geometry, image, zero_rows(3, width))

    def total(k, rows, meanwhile=None):
        return total_rows(
            k, "batch", batches, list(rows), mine, slots, total_sends, total_receives, meanwhile
        )

    sums = conv(x, enc_taps, enc_pre)
    saves[3].start()
    greet((("task", tasks), ("batch", batches)))
    totals = total(0, sums, lambda: fetch(dec_taps, 9, 0, 4))
    put_sums(enc_totals, totals)
    scale = rows_of(scales, 0, 2)

    def peer_of(step, incoming):
        return lax.rem(task + (tasks - step if incoming else step), tasks)

    def pool_copy(i, step, incoming=False):
        rows = window_rows(i, windows)
        peer = peer_of(step, incoming)
        target = pooled_all.at[rows, columns_of(peer if incoming else task, width)]
        return remote(
            pooled.at[rows, :], target, pool_sends.at[i, step], pool_receives.at[i, step], peer, "task"
        )

    def pool(i, rows, carry):
        valid = valid_of(infos, i, height, breadth)
        _, _, scaled = norm_with(enc_pre[rows, :], totals, scale)
        high, low = split(silu(scaled) * valid)
        mean = ((dot(narrow, high) + dot(narrow, low)) * 0.25).astype(BF)
        here = window_rows(i, windows)
        pooled[here, :] = mean
        pooled_all[here, columns_of(task, width)] = mean
        for step in range(1, tasks):
            pool_copy(i, step).start()
        return carry

    each_image(geometry, pool, 0)
    fetch(dec_taps, 9, 4, 9)
    saves[2].start()

    def unpool(i, rows, carry):
        for step in range(1, tasks):
            pool_copy(i, step, True).wait_recv()
        wide = dot_tn(chosen_cells(choice, infos, i), pooled_all[window_rows(i, windows), :])
        spread[rows, :] = wide.astype(BF)
        return carry

    each_image(geometry, unpool, 0)
    saves[5].start()
    sums = conv(spread, dec_taps, dec_pre)
    saves[4].start()
    totals = total(1, sums)
    put_sums(dec_totals, totals)
    scale = rows_of(scales, 2, 2)

    def feature_copy(i, rows, step, incoming=False):
        peer = peer_of(step, incoming)
        target = features.at[rows, columns_of(peer if incoming else task, width)]
        return remote(
            part.at[rows, :], target, sends.at[i, step], receives.at[i, step], peer, "task"
        )

    def finish(i, rows, carry):
        valid = valid_of(infos, i, height, breadth)
        _, _, scaled = norm_with(dec_pre[rows, :], totals, scale)
        low = (silu(scaled) * valid).astype(BF)
        part[rows, :] = low
        features[rows, columns_of(task, width)] = low
        for step in range(1, tasks):
            feature_copy(i, rows, step).start()
        return carry

    each_image(geometry, finish, 0)

    def settle(i, rows, carry):
        for step in range(1, tasks):
            feature_copy(i, rows, step, True).wait_recv()
            feature_copy(i, rows, step).wait_send()
            pool_copy(i, step).wait_send()
        return carry

    each_image(geometry, settle, 0)
    for copy in saves:
        copy.wait()


def trunk_forward(geometry, tasks, batches, index, infos, x, kernel_slots, scales):
    number, height, breadth = geometry
    pixels = height * breadth
    channels = x.shape[1]
    width = channels // tasks
    windows = window_count(height, breadth)
    tall = shape((x.shape[0], width), F32)
    taps = shape((channels, 9 * width), BF)
    outs = [
        shape((8, width), F32), shape((8, width), F32), shape(x.shape, BF),
        shape(x.shape, BF), taps, taps,
        tall, tall, shape(x.shape, BF),
    ]
    return exchange_kernel(
        functools.partial(trunk_forward_body, geometry, tasks, batches),
        outs,
        "svvvv",
        (index, infos, x, kernel_slots, scales),
        [
            pltpu.VMEM(tall.shape, F32),
            pltpu.VMEM(tall.shape, F32),
            pltpu.VMEM(x.shape, BF),
            pltpu.VMEM(taps.shape, BF),
            pltpu.VMEM(taps.shape, BF),
            pltpu.VMEM(kernel_slots.shape, F32),
            pltpu.VMEM((channels, width), F32),
            pltpu.VMEM((pixels, 9 * width), F32),
            pltpu.VMEM((number * windows, width), BF),
            pltpu.VMEM((number * windows, channels), BF),
            pltpu.VMEM((x.shape[0], width), BF),
        ]
        + [pltpu.SemaphoreType.DMA((number, tasks))] * 4
        + total_scratch(2, batches)
        + [pltpu.SemaphoreType.DMA((6,))],
        1,
        60,
        flops=4 * x.size * taps.shape[1],
        places_out="vvvhhhhhh",
    )


def head_body(
    geometry, tasks, batches, summing,
    infos, features, weights, cotangent, scales, counts,
    task_out, upstream, norm_sums, *rest,
):
    grads_out, rest = rest[0], rest[1:]
    (
        grads, pre_one, pre_two, pre_three, hidden, gated, nine, work, lower, out, arrived,
        sends, receives, mine, slots, total_sends, total_receives, loaded,
    ) = rest[:18]
    number, height, breadth = geometry
    channels = features.shape[1]
    width = channels // tasks
    windows = task_out.shape[1]
    task = lax.axis_index("task")
    half = work.shape[2]
    _, col = places(height, breadth)
    widen = pool_choice(height, breadth, windows, False).astype(BF)
    narrow = pool_choice(height, breadth, windows, True).astype(BF)
    count = jnp.broadcast_to(counts[2:3, 0:1], (1, channels))
    cuts = (pl.ds(0, 2 * channels), pl.ds(2 * channels, 9 * channels))
    loads = [
        pltpu.make_async_copy(weights.at[cut, :], grads.at[cut, :], loaded.at[k])
        for k, cut in enumerate(cuts)
    ]
    for copy in loads:
        copy.start()
    first = grads.at[pl.ds(0, channels), :]
    second = grads.at[pl.ds(channels, channels), :]

    def kernel_rows(p):
        return pl.ds((2 + p) * channels, channels)

    def total(k, rows, meanwhile=None):
        return total_rows(
            k, "batch", batches, list(rows), mine, slots, total_sends, total_receives, meanwhile
        )

    if summing:
        near, near_sends, near_receives = rest[18:]
        place, core, chips = pair_place(batches)
        block = near.shape[1]

        def near_copy(chip):
            return remote(
                block_rows(grads, 2 * chip + 1 - core, block), near.at[chip],
                near_sends.at[chip], near_receives.at[chip], 2 * place + 1 - core, "batch",
            )

    def put_stats(pre, rows, value, valid, carry):
        pre[rows, :] = value
        kept = value * valid
        return carry[0] + col_sum(kept), carry[1] + col_sum(kept * value)

    nothing = zero_rows(2, channels)
    scale_one, scale_two, scale_three = (rows_of(scales, 2 * k, 2) for k in range(3))

    loads[0].wait()

    def first_step(i, rows, carry):
        valid = valid_of(infos, i, height, breadth)
        return put_stats(pre_one, rows, dot(features[rows, :], first[...]), valid, carry)

    sums = each_image(geometry, first_step, nothing)
    greet((("task", tasks), ("batch", batches)))
    totals_one = total(0, sums) + [count]

    def second_step(i, rows, carry):
        valid = valid_of(infos, i, height, breadth)
        _, _, scaled = norm_with(pre_one[rows, :], totals_one, scale_one)
        low = (silu(scaled) * valid).astype(BF)
        hidden[rows, :] = low
        return put_stats(pre_two, rows, dot(low, second[...]), valid, carry)

    sums = each_image(geometry, second_step, nothing)
    totals_two = total(1, sums) + [count]

    def third_step(i, rows, carry):
        valid = valid_of(infos, i, height, breadth)
        _, _, scaled = norm_with(pre_two[rows, :], totals_two, scale_two)
        low = (jax.nn.sigmoid(scaled) * features[rows, :].astype(F32)).astype(BF)
        gated[rows, :] = low
        parts = []
        for j in range(channels // half):
            cut = slice(j * half, (j + 1) * half)
            for p in range(9):
                work[p] = dot(low, grads[kernel_rows(p), cut])
            parts.append(gather_taps(lambda p: work[p], breadth, col))
        return put_stats(pre_three, rows, jnp.concatenate(parts, axis=1), valid, carry)

    loads[1].wait()
    sums = each_image(geometry, third_step, nothing)
    totals_three = total(2, sums) + [count]

    def out_step(i, rows, carry):
        valid = valid_of(infos, i, height, breadth)
        normal, _, scaled = norm_with(pre_three[rows, :], totals_three, scale_three)
        high, low = split(silu(scaled) * valid)
        mean = (dot(narrow, high) + dot(narrow, low)) * 0.25
        task_out[i] = mean.astype(BF)
        dy = silu_back(scaled) * dot(widen, cotangent[i]) * 0.25 * valid
        lower[rows, :] = dy
        return carry[0] + col_sum(dy), carry[1] + col_sum(dy * normal)

    sums = each_image(geometry, out_step, nothing)
    sums_three = total(3, sums)

    def third_back(i, rows, carry):
        valid = valid_of(infos, i, height, breadth)
        normal, inverse, _ = norm_with(pre_three[rows, :], totals_three, scale_three)
        dz = norm_back_with(lower[rows, :], normal, inverse, count, sums_three, scale_three, valid)
        for p, moved in enumerate(spread_taps(dz, breadth, col)):
            nine[p, rows, :] = moved.astype(BF)
        flow = None
        for p in range(9):
            piece = dot_nt(nine[p, rows, :], grads[kernel_rows(p), :])
            flow = piece if flow is None else flow + piece
        lower[rows, :] = flow
        normal, _, scaled = norm_with(pre_two[rows, :], totals_two, scale_two)
        gate = jax.nn.sigmoid(scaled)
        dy = flow * features[rows, :].astype(F32) * gate * (1.0 - gate) * valid
        pre_three[rows, :] = dy
        return carry[0] + col_sum(dy), carry[1] + col_sum(dy * normal)

    sums = each_image(geometry, third_back, nothing)

    def taps(begin, end):
        def tap(p, carry):
            rows = pl.ds(pl.multiple_of((2 + p) * channels, channels), channels)
            grads[rows, :] = dot_tn(gated[...], nine[p]).astype(BF)
            return carry

        lax.fori_loop(begin, end, tap, 0)

    sums_two = total(4, sums, lambda: taps(0, 3))

    def second_back(i, rows, carry):
        valid = valid_of(infos, i, height, breadth)
        normal, inverse, scaled = norm_with(pre_two[rows, :], totals_two, scale_two)
        dz = norm_back_with(
            pre_three[rows, :], normal, inverse, count, sums_two, scale_two, valid
        ).astype(BF)
        out[rows, :] = dz
        lower[rows, :] = lower[rows, :] * jax.nn.sigmoid(scaled)
        normal, _, scaled = norm_with(pre_one[rows, :], totals_one, scale_one)
        dy = silu_back(scaled) * dot_nt(dz, second[...]) * valid
        pre_three[rows, :] = dy
        return carry[0] + col_sum(dy), carry[1] + col_sum(dy * normal)

    sums = each_image(geometry, second_back, nothing)

    def weight_rows():
        grads[pl.ds(channels, channels), :] = dot_tn(hidden[...], out[...]).astype(BF)
        taps(3, 5)

    sums_one = total(5, sums, weight_rows)

    def flow_copy(i, rows, step, incoming=False):
        peer = lax.rem(task + (tasks - step if incoming else step), tasks)
        return remote(
            out.at[rows, columns_of(peer, width)], arrived.at[step - 1, rows, :],
            sends.at[i, step], receives.at[i, step], peer, "task",
        )

    def first_back(i, rows, carry):
        valid = valid_of(infos, i, height, breadth)
        normal, inverse, _ = norm_with(pre_one[rows, :], totals_one, scale_one)
        dz = norm_back_with(
            pre_three[rows, :], normal, inverse, count, sums_one, scale_one, valid
        ).astype(BF)
        hidden[rows, :] = dz
        flow = (lower[rows, :] + dot_nt(dz, first[...])) * valid
        out[rows, :] = flow.astype(BF)
        for step in range(1, tasks):
            flow_copy(i, rows, step).start()
        return carry

    each_image(geometry, first_back, 0)
    taps(5, 9)
    if summing:
        for chip in range(1, chips):
            near_copy(chip).start()
    grads[pl.ds(0, channels), :] = dot_tn(features[...], hidden[...]).astype(BF)
    if summing:
        near_copy(0).start()
        for chip in (*range(1, chips), 0):
            near_copy(chip).wait_recv()
            own = block_rows(grads, 2 * chip + core, block)[...].astype(F32)
            grads_out[chip] = (own + near[chip].astype(F32)).astype(BF)
    else:
        grads_out[...] = grads[...]
    put_sums(norm_sums, sums_one + sums_two + sums_three)

    def settle(i, rows, carry):
        for step in range(1, tasks):
            flow_copy(i, rows, step, True).wait_recv()
        flow = out[rows, columns_of(task, width)].astype(F32)
        for step in range(1, tasks):
            flow = flow + arrived[step - 1, rows, :].astype(F32)
        upstream[rows, :] = flow
        for step in range(1, tasks):
            flow_copy(i, rows, step).wait_send()
        return carry

    each_image(geometry, settle, 0)
    if summing:
        for chip in range(chips):
            near_copy(chip).wait_send()


def head(geometry, tasks, batches, infos, features, weights, cotangent, scales, counts):
    number, height, breadth = geometry
    pixels = height * breadth
    total, channels = features.shape
    width = channels // tasks
    block = weights.shape[0] // batches
    chips = batches // 2
    summing = block % 16 == 0
    outs = [
        shape((number, pixels // 4, channels), BF),
        shape((total, width), F32),
        shape((8, channels), F32),
        shape((chips, block, channels) if summing else weights.shape, BF),
    ]
    scratch = []
    if summing:
        scratch = [pltpu.VMEM((chips, block, channels), BF)]
        scratch += [pltpu.SemaphoreType.DMA((chips,))] * 2
    pooled, upstream, sums, grads = exchange_kernel(
        functools.partial(head_body, geometry, tasks, batches, summing),
        outs,
        "vvhvvv",
        (infos, features, weights, cotangent, scales, counts),
        [
            pltpu.VMEM(weights.shape, BF),
            pltpu.VMEM(features.shape, F32),
            pltpu.VMEM(features.shape, F32),
            pltpu.VMEM(features.shape, F32),
            pltpu.VMEM(features.shape, BF),
            pltpu.VMEM(features.shape, BF),
            pltpu.VMEM((9,) + features.shape, BF),
            pltpu.VMEM((9, pixels, min(channels, 256)), F32),
            pltpu.VMEM(features.shape, F32),
            pltpu.VMEM(features.shape, BF),
            pltpu.VMEM((tasks - 1, total, width), BF),
        ]
        + [pltpu.SemaphoreType.DMA((number, tasks))] * 2
        + total_scratch(6, batches)
        + [pltpu.SemaphoreType.DMA((2,))]
        + scratch,
        2,
        61,
        flops=6 * total * channels * weights.shape[0],
    )
    if summing:
        owned = lax.psum_scatter(
            grads.reshape(chips * block, channels), "batch", scatter_dimension=0,
            axis_index_groups=[list(range(core, batches, 2)) for core in range(2)], tiled=True,
        )
    else:
        owned = lax.psum_scatter(grads, "batch", scatter_dimension=0, tiled=True)
    return pooled, upstream, sums, owned


def trunk_backward_body(
    geometry, tasks, batches,
    infos, upstream, enc_totals, dec_totals, scales, *rest,
):
    kept, rest = rest[:6], rest[6:]
    (enc_grad, dec_grad, flow_out, norm_sums), rest = rest[:4], rest[4:]
    (x, enc_taps, dec_taps, enc_pre, dec_pre, spread), rest = rest[:6], rest[6:]
    (
        nine, change, packed, arrived, pooled, sends, receives,
        mine, slots, total_sends, total_receives, loaded,
    ) = rest
    targets = (x, enc_taps, dec_taps, enc_pre, dec_pre, spread)
    loads = [pltpu.make_async_copy(a, b, loaded.at[k]) for k, (a, b) in enumerate(zip(kept, targets))]
    for k in (4, 2, 5, 3, 1, 0):
        loads[k].start()
    number, height, breadth = geometry
    channels = x.shape[1]
    width = enc_pre.shape[1]
    windows = window_count(height, breadth)
    task = lax.axis_index("task")
    _, col = places(height, breadth)
    widen = pool_choice(height, breadth, windows, False).astype(BF)
    narrow = pool_choice(height, breadth, windows, True)
    nothing = zero_rows(2, width)

    def total(k, rows):
        return total_rows(
            k, "batch", batches, list(rows), mine, slots, total_sends, total_receives
        )

    def change_of(pre, totals, scale, flow):
        def image(i, rows, carry):
            valid = valid_of(infos, i, height, breadth)
            normal, _, scaled = norm_with(pre[rows, :], totals, scale)
            dy = silu_back(scaled) * flow(i, rows) * valid
            change[rows, :] = dy
            return carry[0] + col_sum(dy), carry[1] + col_sum(dy * normal)

        return each_image(geometry, image, nothing)

    def back(pre, totals, scale, sums, taps, put):
        def image(i, rows, carry):
            valid = valid_of(infos, i, height, breadth)
            normal, inverse, _ = norm_with(pre[rows, :], totals, scale)
            dz = norm_back_with(change[rows, :], normal, inverse, totals[2], sums, scale, valid)
            for p, moved in enumerate(spread_taps(dz, breadth, col)):
                nine[rows, p * width : (p + 1) * width] = moved.astype(BF)
            put(i, rows, dot_nt(nine[rows, :], taps[...]) * valid)
            return carry

        each_image(geometry, image, 0)

    totals = rows_of(dec_totals, 0, 3)
    scale = rows_of(scales, 2, 2)
    loads[4].wait()
    sums = change_of(dec_pre, totals, scale, lambda i, rows: upstream[rows, :])
    greet((("task", tasks), ("batch", batches)))
    dec_sums = total(0, sums)

    def copy_of(i, step, incoming=False):
        rows = window_rows(i, windows)
        peer = lax.rem(task + (tasks - step if incoming else step), tasks)
        return remote(
            packed.at[rows, columns_of(peer, width)], arrived.at[step - 1, rows, :],
            sends.at[i, step], receives.at[i, step], peer, "task",
        )

    def put_packed(i, rows, flow):
        chosen = chosen_cells(narrow, infos, i)
        packed[window_rows(i, windows), :] = dot(chosen, flow.astype(BF)).astype(BF)
        for step in range(1, tasks):
            copy_of(i, step).start()

    loads[2].wait()
    back(dec_pre, totals, scale, dec_sums, dec_taps, put_packed)
    loads[5].wait()
    dec_grad[...] = dot_tn(spread[...], nine[...])

    def collect(i, carry):
        for step in range(1, tasks):
            copy_of(i, step, True).wait_recv()
        rows = window_rows(i, windows)
        flow = packed[rows, columns_of(task, width)].astype(F32)
        for step in range(1, tasks):
            flow = flow + arrived[step - 1, rows, :].astype(F32)
        pooled[rows, :] = flow
        for step in range(1, tasks):
            copy_of(i, step).wait_send()
        return carry

    lax.fori_loop(0, number, collect, 0)

    def widened(i, rows):
        high, low = split(pooled[window_rows(i, windows), :])
        return (dot(widen, high) + dot(widen, low)) * 0.25

    totals = rows_of(enc_totals, 0, 3)
    scale = rows_of(scales, 0, 2)
    loads[3].wait()
    sums = change_of(enc_pre, totals, scale, widened)
    enc_sums = total(1, sums)

    def put_flow(i, rows, flow):
        flow_out[rows, :] = flow.astype(BF)

    loads[1].wait()
    back(enc_pre, totals, scale, enc_sums, enc_taps, put_flow)
    loads[0].wait()
    enc_grad[...] = dot_tn(x[...], nine[...])
    put_sums(norm_sums, enc_sums + dec_sums)


def trunk_backward(
    geometry, tasks, batches, infos, upstream, enc_totals, dec_totals, scales, kept
):
    number, height, breadth = geometry
    x, enc_taps, dec_taps = kept[:3]
    total, channels = x.shape
    width = channels // tasks
    windows = window_count(height, breadth)
    outs = [
        shape(enc_taps.shape, F32),
        shape(dec_taps.shape, F32),
        shape(x.shape, BF),
        shape((8, width), F32),
    ]
    return exchange_kernel(
        functools.partial(trunk_backward_body, geometry, tasks, batches),
        outs,
        "vvvvvhhhhhh",
        (infos, upstream, enc_totals, dec_totals, scales, *kept),
        [pltpu.VMEM(a.shape, a.dtype) for a in kept]
        + [
            pltpu.VMEM((total, 9 * width), BF),
            pltpu.VMEM((total, width), F32),
            pltpu.VMEM((number * windows, channels), BF),
            pltpu.VMEM((tasks - 1, number * windows, width), BF),
            pltpu.VMEM((number * windows, width), F32),
        ]
        + [pltpu.SemaphoreType.DMA((number, tasks))] * 2
        + total_scratch(2, batches)
        + [pltpu.SemaphoreType.DMA((6,))],
        3,
        60,
        flops=8 * x.size * enc_taps.shape[1],
    )


def to_slots_body(index, enc, dec, slots, wide):
    count = slots.shape[0]
    channels = enc.shape[0]
    width = slots.shape[1]
    step = 1024
    group = 32
    for p in range(18):
        source = enc if p < 9 else dec
        q = p % 9

        def place(i, carry):
            base = pl.multiple_of(i * group, group)
            values = source[pl.ds(base, group), q * width : (q + 1) * width]
            for u in range(group):
                wide[pl.ds(index[p * channels + base + u], 1), :] = values[u : u + 1, :]
            return carry

        lax.fori_loop(0, channels // group, place, 0)

    def narrow(i, carry):
        rows = pl.ds(pl.multiple_of(i * step, step), step)
        slots[rows, :] = wide[rows, :].astype(BF)
        return carry

    lax.fori_loop(0, count // step, narrow, 0)


def to_slots(index, enc, dec):
    width = enc.shape[1] // 9
    dims = (index.shape[0], width)
    return run(
        to_slots_body, [shape(dims, BF)], "svv", (index, enc, dec), [pltpu.VMEM(dims, F32)], vmem=60
    )[0]


def adam(gradient, moment_one, moment_two):
    new_one = BETA_ONE * moment_one + (1.0 - BETA_ONE) * gradient
    new_two = BETA_TWO * moment_two + (1.0 - BETA_TWO) * gradient * gradient
    direction = (
        new_one / (1.0 - BETA_ONE**STEP) / (jnp.sqrt(new_two / (1.0 - BETA_TWO**STEP)) + ADAM_EPS)
    )
    return new_one, new_two, direction


def pair_place(batches):
    me = lax.axis_index("batch")
    place = lax.div(me, 2)
    return place, me - 2 * place, batches // 2


def greet_pairs(tasks, batches):
    place, core, chips = pair_place(batches)
    task = lax.axis_index("task")
    barrier = pltpu.get_barrier_semaphore()

    def signal(device):
        pl.semaphore_signal(barrier, inc=1, device_id=device, device_id_type=MESH)

    for step in range(1, tasks):
        signal({"task": lax.rem(task + step, tasks)})
    signal({"batch": 2 * place + 1 - core})
    for step in range(1, chips):
        signal({"batch": 2 * lax.rem(place + step, chips) + core})
    pl.semaphore_wait(barrier, tasks - 1 + chips)


def block_rows(ref, index, count):
    return ref.at[pl.ds(pl.multiple_of(index * count, 8), count), :]


SMALL = 128 * 128


def far_first(chips):
    return sorted(range(chips), key=lambda step: -min(step, chips - step))


def pair_sum(batches, rows_of_block, own_block, near, paired, far, sems):
    place, core, chips = pair_place(batches)
    count = near.shape[1]
    near_send, near_receive, far_send, far_receive = sems
    other = 2 * place + 1 - core
    ring = chips == 4 and count % 32 == 0 and near.shape[2] * count > SMALL
    half = count // 2
    halves = (pl.ds(0, half), pl.ds(half, half))

    def near_copy(step):
        chip = lax.rem(place + step, chips)
        return remote(rows_of_block(2 * chip + 1 - core), near.at[step],
                      near_send.at[step], near_receive.at[step], other, "batch")

    def far_copy(step, incoming=False):
        chip = lax.rem(place + (chips - step if incoming else step), chips)
        return remote(paired.at[step], far.at[step], far_send.at[step], far_receive.at[step],
                      2 * chip + core, "batch")

    def ring_copy(which, way):
        chip = lax.rem(place + (1 if way == 0 else chips - 1), chips)
        if which == 0:
            source, target = paired.at[2, halves[way], :], far.at[2 + way, halves[0], :]
        else:
            cut = halves[way] if which == 2 else halves[1 - way]
            source, target = paired.at[1 if way == 0 else 3, cut, :], far.at[way, cut, :]
        k = 2 * which + way
        return remote(source, target, far_send.at[k], far_receive.at[k], 2 * chip + core, "batch")

    def start():
        for step in far_first(chips):
            near_copy(step).start()

    def middle():
        for step in far_first(chips):
            near_copy(step).wait_recv()
            if step:
                paired[step] = (own_block(step) + near[step].astype(F32)).astype(paired.dtype)
                if not ring:
                    far_copy(step).start()
                elif step == 2:
                    ring_copy(0, 0).start()
                    ring_copy(0, 1).start()
                else:
                    ring_copy(1, 0 if step == 1 else 1).start()

    def relay():
        if not ring:
            return
        for way in range(2):
            ring_copy(0, way).wait_recv()
            step = 1 if way == 0 else 3
            total = paired[step, halves[way], :].astype(F32) + far[2 + way, halves[0], :].astype(F32)
            paired[step, halves[way], :] = total.astype(paired.dtype)
            ring_copy(2, way).start()

    def end():
        total = own_block(0) + near[0].astype(F32)
        if ring:
            for way in range(2):
                ring_copy(1, way).wait_recv()
                ring_copy(2, way).wait_recv()
                total = total + far[way].astype(F32)
            for k in range(3):
                for way in range(2):
                    ring_copy(k, way).wait_send()
        else:
            for step in range(1, chips):
                far_copy(step, True).wait_recv()
                total = total + far[step].astype(F32)
            for step in range(1, chips):
                far_copy(step).wait_send()
        for step in range(chips):
            near_copy(step).wait_send()
        return total

    return start, middle, relay, end


def blocks_in(source, batches, count, piece=0, pieces=1):
    place, core, chips = pair_place(batches)

    def rows(index):
        start = (index * pieces + piece) * count
        return source.at[pl.ds(pl.multiple_of(start, 8), count), :]

    def own(step):
        chip = lax.rem(place + step, chips)
        return rows(2 * chip + core)[...].astype(F32)

    return rows, own


def pair_scratch(batches, rows, width, kind):
    chips = batches // 2
    return [pltpu.VMEM((chips, rows // batches, width), kind)] * 3 + [
        pltpu.SemaphoreType.DMA((max(chips, 6),))
    ] * 4


def chip_spread(batches, block, sends, receives):
    place, core, chips = pair_place(batches)
    count, width = block(place).shape
    ring = chips == 4 and count % 32 == 0 and width * count > SMALL
    half = count // 2

    def copy(step, incoming=False):
        peer = lax.rem(place + (chips - step if incoming else step), chips)
        ref = block(peer if incoming else place)
        return remote(ref, ref, sends.at[step], receives.at[step], 2 * peer + core, "batch")

    def pass_on(way, incoming=False):
        step = 1 if way == 0 else chips - 1
        peer = lax.rem(place + (chips - step if incoming else step), chips)
        home = lax.rem(place + (2 if incoming else chips - step), chips)
        ref = block(home).at[pl.ds(way * half, half), :]
        k = 2 if way == 0 else 0
        return remote(ref, ref, sends.at[k], receives.at[k], 2 * peer + core, "batch")

    steps = (1, chips - 1) if ring else tuple(range(1, chips))

    def start():
        for step in steps:
            copy(step).start()

    def relay():
        if ring:
            for way, step in enumerate(steps):
                copy(step, True).wait_recv()
                pass_on(way).start()

    def settle():
        if ring:
            for way in range(2):
                pass_on(way, True).wait_recv()
        else:
            for step in steps:
                copy(step, True).wait_recv()

    def drain():
        for step in steps:
            copy(step).wait_send()
        if ring:
            for way in range(2):
                pass_on(way).wait_send()

    return start, relay, settle, drain


def arrive_body(
    tasks, batches, geometry,
    image_raw, info, index, weight, head_weight,
    slots, x, infos, owners, head_low,
    image, head_raw, head_loaded, raw, raw_loaded, x_send, x_receive, info_send, info_receive,
    chip_send, chip_receive, pair_send, pair_receive, own,
):
    task = lax.axis_index("task")
    place, core, chips = pair_place(batches)
    count, width = raw.shape
    load = pltpu.make_async_copy(weight.at[:, columns_of(task, width)], raw, raw_loaded)
    load.start()
    head_load = pltpu.make_async_copy(head_weight, head_raw, head_loaded)
    head_load.start()
    number, height, breadth = geometry
    pixels = height * breadth
    for n in range(number):
        valid = valid_rows(info[8 * n + 1 : 8 * n + 2, 0:1], height, breadth)
        rows = slice(n * pixels, (n + 1) * pixels)
        image[rows, :] = (image_raw[rows, :].astype(F32) * valid).astype(BF)
    greet_pairs(tasks, batches)

    def task_copy(source, target, sends, receives, step, incoming=False):
        peer = lax.rem(task + (tasks - step if incoming else step), tasks)
        home = peer if incoming else task
        return remote(source, block_rows(target, home, source.shape[0]), sends.at[step],
                      receives.at[step], peer, "task")

    def moves(step, incoming=False):
        return (
            task_copy(info, infos, info_send, info_receive, step, incoming),
            task_copy(image, x, x_send, x_receive, step, incoming),
        )

    def block(chip):
        return block_rows(slots, 2 * chip + core, count)

    def pair_copy(hop, incoming=False):
        chip = lax.rem(place + chips - hop, chips)
        ref = block_rows(slots, 2 * chip + (1 - core if incoming else core), count)
        return remote(ref, ref, pair_send.at[hop], pair_receive.at[hop], 2 * place + 1 - core, "batch")

    start, relay, settle, drain = chip_spread(batches, block, chip_send, chip_receive)
    ring = chips == 4 and count % 32 == 0 and width * count > SMALL
    load.wait()
    block(place)[...] = raw[...].astype(BF)
    start()
    pair_copy(0).start()
    for step in range(1, tasks):
        for copy in moves(step):
            copy.start()
    locals_ = [
        pltpu.make_async_copy(image, block_rows(x, task, image.shape[0]), own.at[0]),
        pltpu.make_async_copy(info, block_rows(infos, task, info.shape[0]), own.at[1]),
    ]
    for copy in locals_:
        copy.start()
    mine = lax.broadcasted_iota(jnp.int32, (count, 1), 0) + lax.axis_index("batch") * count
    found = jnp.zeros((count, 128), F32)
    for k in range(index.shape[0] // 2, index.shape[0]):
        found = jnp.where(index[k : k + 1, :] == mine, 1.0, found)
    found = jnp.max(found, axis=1, keepdims=True)
    owners[:, 0:1] = 1.0 - found
    owners[:, 1:2] = found
    head_load.wait()
    head_low[...] = head_raw[...].astype(BF)
    relay()
    if ring:
        pair_copy(1).start()
        pair_copy(3).start()
        settle()
        pair_copy(2).start()
    else:
        settle()
        for hop in range(1, chips):
            pair_copy(hop).start()
    for copy in locals_:
        copy.wait()
    for step in range(1, tasks):
        for copy in moves(step, True):
            copy.wait_recv()
    for hop in range(chips):
        pair_copy(hop, True).wait_recv()
    for step in range(1, tasks):
        for copy in moves(step):
            copy.wait_send()
    for hop in range(chips):
        pair_copy(hop).wait_send()
    drain()


def arrive(tasks, batches, geometry, image, info, index, weight, head_weight):
    count, channels = weight.shape
    width = channels // tasks
    chips = batches // 2
    return exchange_kernel(
        functools.partial(arrive_body, tasks, batches, geometry),
        [
            shape((count * batches, width), BF),
            shape((image.shape[0] * tasks, channels), BF),
            shape((info.shape[0] * tasks, info.shape[1]), F32),
            shape((count, 2), F32),
            shape(head_weight.shape, BF),
        ],
        "vvvhh",
        (image, info, index.reshape(-1, 128), weight, head_weight),
        [
            pltpu.VMEM(image.shape, BF),
            pltpu.VMEM(head_weight.shape, F32),
            pltpu.SemaphoreType.DMA,
            pltpu.VMEM((count, width), F32),
            pltpu.SemaphoreType.DMA,
        ]
        + [pltpu.SemaphoreType.DMA((tasks,))] * 4
        + [pltpu.SemaphoreType.DMA((max(chips, 4),))] * 4
        + [pltpu.SemaphoreType.DMA((2,))],
        4,
        60,
        flops=20000 * MIB,
    )


def soap_rows(cuts, grad, owners, state, low, first, begin=0, end=None):
    total = grad.shape[0]

    def chunk(i, carry):
        rows = pl.ds(pl.multiple_of(i * (total // cuts), 8), total // cuts)
        values = grad[rows, :].astype(F32)
        marks = owners(i * (total // cuts), total // cuts)
        count = len(marks)
        rotated = None
        for m in range(count):
            part = dot((values * marks[m]).astype(BF), low[first + m])
            rotated = part if rotated is None else rotated + part
        new_one, new_two, direction = adam(rotated, state[1, rows, :], state[2, rows, :])
        state[1, rows, :] = new_one
        state[2, rows, :] = new_two
        stepped = None
        for m in range(count):
            part = dot_nt((direction * marks[m]).astype(BF), low[first + m])
            stepped = part if stepped is None else stepped + part
        old = state[0, rows, :]
        state[0, rows, :] = old - LEARN_MATRIX * (stepped + DECAY_MATRIX * old)
        return carry

    lax.fori_loop(begin, cuts if end is None else end, chunk, 0)


def factor_rows(values, identity, turn):
    size, width = values.shape
    sub = lax.broadcasted_iota(jnp.int32, (size, width), 0)
    rolled = pltpu.roll(values, turn, 1)
    columns = [jnp.broadcast_to(rolled[:, j : j + 1], (size, width)) for j in range(size)]
    scale = jnp.zeros((size, width), F32)
    for j in range(size):
        root = lax.rsqrt(columns[j][j : j + 1, :])
        scale = jnp.where(sub == j, root, scale)
        lower = jnp.where(sub > j, columns[j] * root, 0.0)
        values = values - lower * (values[j : j + 1, :] * root)
        identity = identity - lower * (identity[j : j + 1, :] * root)
        for i in range(j + 1, size):
            columns[i] = columns[i] - lower * (columns[i][j : j + 1, :] * root)
    return values * scale, identity * scale


GROUP = 16
PANEL = 128


def renew_panel(k, product, made, tables, inverses):
    count, size = product.shape[0], product.shape[1]
    here = slice(k * PANEL, (k + 1) * PANEL)
    row = lax.broadcasted_iota(jnp.int32, (PANEL, PANEL), 0)
    col = lax.broadcasted_iota(jnp.int32, (PANEL, PANEL), 1)
    unit = jnp.where(row == col, 1.0, 0.0).astype(F32)
    for n in range(count):
        tables[n][:, :PANEL] = dot3(dot_tn, product[n, :, here], product[n, :, here])
        tables[n][:, PANEL:] = unit

    def group(q, carry):
        rows = pl.ds(pl.multiple_of(q * GROUP, GROUP), GROUP)
        turn = lax.rem(PANEL - q * GROUP, PANEL)
        done = [
            factor_rows(tables[n][rows, :PANEL], tables[n][rows, PANEL:], turn)
            for n in range(count)
        ]
        for n in range(count):
            upper, inverse = done[n]
            inverses[n][rows, :] = inverse
            both = jnp.concatenate([upper, inverse], axis=1)
            tables[n][...] = tables[n][...] - dot3(dot_tn, upper, both)
        return carry

    lax.fori_loop(0, PANEL // GROUP, group, 0)
    for n in range(count):
        turned = dot3(dot_nt, product[n, :, here], inverses[n][...])
        made[n, :, here] = turned
        if k < size // PANEL - 1:
            rest = slice((k + 1) * PANEL, size)
            product[n, :, rest] = product[n, :, rest] - dot3(
                dot, turned, dot3(dot_tn, turned, product[n, :, rest])
            )


def tail_body(
    tasks, batches, cuts, pieces,
    slots, flow, sums, owners, head_grad,
    weight, one, two, head_weight, head_one, head_two, basis, head_basis,
    input_grad, norm_sums, state_new, head_state_new, grams, head_grams,
    grad, part, state, head_state, mine, head_mine, bases, low,
    flow_in, flow_send, flow_receive, send, receive, sum_send, sum_receive,
    *rest,
):
    row_scratch = [rest[7 * k : 7 * k + 7] for k in range(pieces)]
    gram_scratch, head_scratch, rest = rest[7 * pieces :][:7], rest[7 * pieces + 7 :][:7], rest[7 * pieces + 14 :]
    chip_send, chip_receive, task_send, task_receive, pair_send, pair_receive, load, save = rest
    task = lax.axis_index("task")
    place, core, chips = pair_place(batches)
    width = part.shape[1]
    channels = grad.shape[1]
    pixels = input_grad.shape[0]
    trunk_total = basis.shape[0]
    head_total = head_basis.shape[0]
    count, head_count = mine.shape[0] // batches, head_mine.shape[0] // batches

    def trunk_marks(start, size):
        rows = pl.ds(pl.multiple_of(start, 8), size)
        return [owners[rows, m : m + 1] for m in range(trunk_total)]

    def head_marks(start, size):
        index = lax.broadcasted_iota(jnp.int32, (size, 1), 0) + start
        index = index + lax.axis_index("batch") * head_grad.shape[0]
        owner = jnp.minimum(lax.div(index, channels), head_total - 1)
        return [jnp.where(owner == m, 1.0, 0.0).astype(F32) for m in range(head_total)]

    def put_grams(target, rows, columns, marks):
        for m, mark in enumerate(marks):
            held = (rows[...].astype(F32) * mark).astype(BF)
            target[m * channels : (m + 1) * channels, :] = dot_tn(held, columns[...]).astype(
                target.dtype
            )

    def peer_of(step, incoming):
        return lax.rem(task + (tasks - step if incoming else step), tasks)

    def flow_copy(step, incoming=False):
        peer = peer_of(step, incoming)
        return remote(block_rows(flow, peer, pixels), flow_in.at[step - 1], flow_send.at[step],
                      flow_receive.at[step], peer, "task")

    def sum_copy(step, incoming=False):
        peer = peer_of(step, incoming)
        home = peer if incoming else task
        return remote(sums, norm_sums.at[:, columns_of(home, width)], sum_send.at[step],
                      sum_receive.at[step], peer, "task")

    def part_copy(k, step, incoming=False):
        peer = peer_of(step, incoming)
        home = peer if incoming else task
        return remote(part.at[part_rows(k), :], grad.at[part_rows(k), columns_of(home, width)],
                      send.at[k, step], receive.at[k, step], peer, "task")

    def trunk_block(chip, home, which):
        rows = pl.ds(pl.multiple_of((2 * chip + which) * count, 8), count)
        return grams.at[rows, columns_of(home, width)]

    def head_block(chip, which):
        return block_rows(head_grams, 2 * chip + which, head_count)

    def task_copy(step, hop, incoming=False):
        peer = peer_of(step, incoming)
        chip = lax.rem(place + chips - hop, chips)
        block = trunk_block(chip, peer if incoming else task, core)
        return remote(block, block, task_send.at[step, hop], task_receive.at[step, hop], peer, "task")

    def pair_copy(kind, hop, incoming=False):
        chip = lax.rem(place + chips - hop, chips)
        which = 1 - core if incoming else core
        home = lax.rem(task + tasks - kind, tasks)
        block = head_block(chip, which) if kind == tasks else trunk_block(chip, home, which)
        return remote(block, block, pair_send.at[kind, hop], pair_receive.at[kind, hop],
                      2 * place + 1 - core, "batch")

    def sum_of(source, scratch, piece=0, total=1):
        near, paired, far, *sems = scratch
        return pair_sum(
            batches, *blocks_in(source, batches, near.shape[1], piece, total), near, paired, far, sems
        )

    def part_rows(k):
        size = part.shape[0] // pieces
        return pl.ds(k * size, size)

    moves = [
        (basis, bases.at[pl.ds(0, trunk_total)]),
        (head_basis, bases.at[pl.ds(trunk_total, head_total)]),
        (head_weight, head_state.at[0]),
        (head_one, head_state.at[1]),
        (head_two, head_state.at[2]),
        (weight, state.at[0]),
        (one, state.at[1]),
        (two, state.at[2]),
    ]
    loads = [pltpu.make_async_copy(a, b, load.at[k]) for k, (a, b) in enumerate(moves)]
    for copy in loads:
        copy.start()
    saves = [
        pltpu.make_async_copy(state, state_new, save.at[0]),
        pltpu.make_async_copy(head_state, head_state_new, save.at[1]),
    ]

    greet_pairs(tasks, batches)
    row_sums = [sum_of(slots, row_scratch[k], k, pieces) for k in range(pieces)]
    for stages in row_sums:
        stages[0]()
    for step in range(1, tasks):
        sum_copy(step).start()
        flow_copy(step).start()
    norm_sums[:, columns_of(task, width)] = sums[...]
    row_sums[0][1]()
    put_grams(head_mine, head_grad, head_grad, head_marks(0, head_grad.shape[0]))
    head_start, head_middle, head_relay, head_end = sum_of(head_mine, head_scratch)
    row_sums[0][2]()
    for stages in row_sums[1:]:
        stages[1]()
    head_start()
    for stages in row_sums[1:]:
        stages[2]()
    head_middle()
    for copy in loads[:5]:
        copy.wait()
    for m in range(trunk_total + head_total):
        low[m] = bases[m].astype(BF)
    for k, stages in enumerate(row_sums):
        total = stages[3]().astype(BF)
        part[part_rows(k), :] = total
        for step in range(1, tasks):
            part_copy(k, step).start()
        grad[part_rows(k), columns_of(task, width)] = total
    head_relay()

    soap_rows(cuts, head_grad, head_marks, head_state, low, trunk_total)
    saves[1].start()
    total = block_rows(flow, task, pixels)[...].astype(F32)
    for step in range(1, tasks):
        flow_copy(step, True).wait_recv()
        total = total + flow_in[step - 1].astype(F32)
    input_grad[...] = total
    head_block(place, core)[...] = head_end().astype(head_grams.dtype)
    trunk_spread = chip_spread(
        batches, lambda chip: trunk_block(chip, task, core), chip_send.at[0], chip_receive.at[0]
    )
    head_spread = chip_spread(
        batches, lambda chip: head_block(chip, core), chip_send.at[1], chip_receive.at[1]
    )
    head_spread[0]()
    pair_copy(tasks, 0).start()
    for k in range(pieces):
        for step in range(1, tasks):
            part_copy(k, step, True).wait_recv()

    put_grams(mine, grad, part, trunk_marks(0, grad.shape[0]))
    start, middle, relay, end = sum_of(mine, gram_scratch)
    start()
    middle()
    head_spread[1]()
    for copy in loads[5:]:
        copy.wait()
    relay()
    soap_rows(cuts, grad, trunk_marks, state, low, 0, 0, cuts // 2)
    trunk_block(place, task, core)[...] = end().astype(grams.dtype)
    trunk_spread[0]()
    for step in range(1, tasks):
        task_copy(step, 0).start()
    pair_copy(0, 0).start()
    soap_rows(cuts, grad, trunk_marks, state, low, 0, cuts // 2, cuts)
    saves[0].start()
    trunk_spread[1]()
    trunk_spread[2]()
    for hop in range(1, chips):
        for step in range(1, tasks):
            task_copy(step, hop).start()
        pair_copy(0, hop).start()
    head_spread[2]()
    for hop in range(1, chips):
        pair_copy(tasks, hop).start()
    for hop in range(chips):
        for step in range(1, tasks):
            task_copy(step, hop, True).wait_recv()
            pair_copy(step, hop).start()
    for hop in range(chips):
        for kind in range(tasks + 1):
            pair_copy(kind, hop, True).wait_recv()
    for step in range(1, tasks):
        sum_copy(step, True).wait_recv()

    for copy in saves:
        copy.wait()
    for step in range(1, tasks):
        sum_copy(step).wait_send()
        for k in range(pieces):
            part_copy(k, step).wait_send()
        flow_copy(step).wait_send()
    for hop in range(chips):
        for kind in range(tasks + 1):
            pair_copy(kind, hop).wait_send()
        for step in range(1, tasks):
            task_copy(step, hop).wait_send()
    trunk_spread[3]()
    head_spread[3]()


def renew_body(
    state, head_state, grams, head_grams, stat, head_stat, basis, head_basis,
    weight_new, one_new, two_new, head_weight_new, head_one_new, head_two_new,
    stat_new, head_stat_new, basis_new, head_basis_new,
    stats, product, made, low_grams, low_head_grams, held, head_held, load, save, *work,
):
    trunk_total, head_total = stat.shape[0], head_stat.shape[0]
    channels = stat.shape[1]
    count = trunk_total + head_total
    tables, inverses = work[:count], work[count:]
    loads = []

    def bring(source, target):
        copy = pltpu.make_async_copy(source, target, load.at[len(loads)])
        copy.start()
        loads.append(copy)

    for m in range(count):
        first = m < trunk_total
        place = m if first else m - trunk_total
        rows = pl.ds(place * channels, channels)
        here, there = (grams, low_grams) if first else (head_grams, low_head_grams)
        bring(here.at[rows, :], there.at[rows, :])
        bring((stat if first else head_stat).at[place], stats.at[m])
        bring((basis if first else head_basis).at[place], made.at[m])
    bring(state, held)
    bring(head_state, head_held)
    sources = [held.at[k] for k in range(3)] + [head_held.at[k] for k in range(3)]
    targets = [weight_new, one_new, two_new, head_weight_new, head_one_new, head_two_new]
    saves = [pltpu.make_async_copy(a, b, save.at[k]) for k, (a, b) in enumerate(zip(sources, targets))]
    for m in range(count):
        first = m < trunk_total
        place = m if first else m - trunk_total
        for copy in loads[3 * m : 3 * m + 3]:
            copy.wait()
        low = low_grams if first else low_head_grams
        gram = low[place * channels : (place + 1) * channels, :].astype(F32)
        stats[m] = STAT_DECAY * stats[m] + (1.0 - STAT_DECAY) * gram
        product[m] = dot3(dot, stats[m], made[m])
    groups = ((0, trunk_total, stat_new, basis_new), (trunk_total, head_total, head_stat_new, head_basis_new))
    for begin, size, out, _ in groups:
        copy = pltpu.make_async_copy(stats.at[pl.ds(begin, size)], out, save.at[len(saves)])
        copy.start()
        saves.append(copy)
    for copy in loads[3 * count :]:
        copy.wait()
    for copy in saves[:6]:
        copy.start()
    for k in range(channels // PANEL):
        renew_panel(k, product, made, tables, inverses)
        cut = pl.ds(k * PANEL, PANEL)
        for begin, size, _, out in groups:
            copy = pltpu.make_async_copy(
                made.at[pl.ds(begin, size), :, cut], out.at[:, :, cut], save.at[len(saves)]
            )
            copy.start()
            saves.append(copy)
    for copy in saves:
        copy.wait()


def finish(tasks, batches, local_grads, rows, matrices):
    slots, flow, sums, owners, head_grad = local_grads
    stat, head_stat, basis, head_basis = matrices
    total, channels = rows[0].shape
    width = channels // tasks
    trunk_total, head_total = basis.shape[0], head_basis.shape[0]
    gram_rows, head_rows = trunk_total * channels, head_total * channels
    chips = batches // 2
    kind = BF if gram_rows % (16 * batches) == 0 else F32
    head_kind = BF if head_rows % (16 * batches) == 0 else F32
    cuts = 4 if total % 64 == 0 and head_grad.shape[0] % 64 == 0 else 1
    pieces = 2 if total % 64 == 0 else 1
    square = (trunk_total + head_total, channels, channels)
    pixels = flow.shape[0] // tasks
    input_grad, norm_sums, *made = exchange_kernel(
        functools.partial(tail_body, tasks, batches, cuts, pieces),
        [
            shape((pixels, channels), F32),
            shape((8, channels), F32),
            shape((3, total, channels), F32),
            shape((3,) + head_grad.shape, F32),
            shape((gram_rows, channels), kind),
            shape((head_rows, channels), head_kind),
        ],
        "vvvvvhhhhhhhh",
        (*local_grads, *rows, basis, head_basis),
        [
            pltpu.VMEM((total, channels), BF),
            pltpu.VMEM((total, width), BF),
            pltpu.VMEM((3, total, channels), F32),
            pltpu.VMEM((3,) + head_grad.shape, F32),
            pltpu.VMEM((gram_rows, width), kind),
            pltpu.VMEM((head_rows, channels), head_kind),
            pltpu.VMEM(square, F32),
            pltpu.VMEM(square, BF),
            pltpu.VMEM((tasks - 1, pixels, channels), BF),
        ]
        + [pltpu.SemaphoreType.DMA((tasks,))] * 2
        + [pltpu.SemaphoreType.DMA((pieces, tasks))] * 2
        + [pltpu.SemaphoreType.DMA((tasks,))] * 2
        + pair_scratch(batches, slots.shape[0] // pieces, width, BF) * pieces
        + pair_scratch(batches, gram_rows, width, kind)
        + pair_scratch(batches, head_rows, channels, head_kind)
        + [pltpu.SemaphoreType.DMA((2, max(chips, 4)))] * 2
        + [pltpu.SemaphoreType.DMA((tasks, chips))] * 2
        + [pltpu.SemaphoreType.DMA((tasks + 1, chips))] * 2
        + [pltpu.SemaphoreType.DMA((8,)), pltpu.SemaphoreType.DMA((2,))],
        5,
        60,
        flops=50000 * MIB,
        places_out="vvhhvv",
    )
    outs = [shape(a.shape, F32) for a in (*rows, *matrices)]
    hbm = pl.BlockSpec(memory_space=pltpu.HBM)
    count = trunk_total + head_total
    results = pl.pallas_call(
        renew_body,
        out_shape=tuple(outs),
        in_specs=[hbm] * 8,
        out_specs=tuple(hbm for _ in outs),
        scratch_shapes=[pltpu.VMEM(square, F32)] * 3
        + [pltpu.VMEM(made[2].shape, kind), pltpu.VMEM(made[3].shape, head_kind)]
        + [pltpu.VMEM(made[0].shape, F32), pltpu.VMEM(made[1].shape, F32)]
        + [pltpu.SemaphoreType.DMA((3 * count + 2,))]
        + [pltpu.SemaphoreType.DMA((8 + 2 * (channels // PANEL),))]
        + [pltpu.VMEM((PANEL, 2 * PANEL), F32)] * count
        + [pltpu.VMEM((PANEL, PANEL), F32)] * count,
        compiler_params=pltpu.CompilerParams(vmem_limit_bytes=60 * MIB),
        cost_estimate=pl.CostEstimate(
            flops=60000 * MIB, bytes_accessed=64 * MIB, transcendentals=0
        ),
    )(*made, *matrices)
    return input_grad, norm_sums, results


def local(
    tasks,
    batches,
    images,
    image_small,
    pool_index,
    row_slot,
    trunk_weight,
    trunk_mean_grad,
    trunk_mean_square,
    trunk_statistic,
    trunk_basis,
    head_weight,
    head_mean_grad,
    head_mean_square,
    head_statistic,
    head_basis,
    trunk_gain,
    trunk_offset,
    trunk_norm_mean_grad,
    trunk_norm_mean_square,
    head_gain,
    head_offset,
    head_norm_mean_grad,
    head_norm_mean_square,
    cotangent,
):
    number, height, breadth, channels = images.shape
    pixels = height * breadth
    shown = tasks * number
    geometry = (shown, height, breadth)
    task = lax.axis_index("task")
    width = channels // tasks

    def quarter(values):
        return lax.dynamic_slice_in_dim(values, task * width, width, values.ndim - 1)

    def inside(flags):
        row_limit = jnp.where(flags > 0, height // 2, height)[:, None, None]
        col_limit = jnp.where(flags > 0, breadth // 2, breadth)[:, None, None]
        return (jnp.arange(height, dtype=jnp.int32)[None, :, None] < row_limit) & (
            jnp.arange(breadth, dtype=jnp.int32)[None, None, :] < col_limit
        )

    cell = 2 * jnp.arange(2, dtype=jnp.int32)[:, None, None] + jnp.arange(2, dtype=jnp.int32)
    cells = pool_index.reshape(number, height // 2, 1, breadth // 2, 1)
    valid = inside(image_small)
    chosen = ((cells == cell).reshape(number, height, breadth) & valid).reshape(number, pixels)
    info = jnp.zeros((8 * number, channels), F32)
    info = info.at[::8, :pixels].set(chosen.astype(F32))
    info = info.at[1::8, 0].set(image_small.astype(F32))
    slots, x, infos, trunk_owners, head_low = arrive(
        tasks, batches, (number, height, breadth), images.reshape(number * pixels, channels),
        info, row_slot, trunk_weight, head_weight[0],
    )
    head_rows = lax.all_gather(head_low, "batch", axis=0, tiled=True)

    scales = quarter(jnp.stack([trunk_gain, trunk_offset], axis=1)).reshape(4, width)
    enc_totals, dec_totals, features, *kept = trunk_forward(
        geometry, tasks, batches, row_slot, infos, x, slots, scales
    )
    head_scales = jnp.stack([head_gain[0], head_offset[0]], axis=1).reshape(6, channels)
    pooled, upstream, head_sums, head_owned = head(
        geometry, tasks, batches, infos, features, head_rows,
        cotangent.reshape(shown, pixels // 4, channels), head_scales, enc_totals,
    )
    task_features = pooled.reshape(cotangent.shape)
    enc_grad, dec_grad, flow, trunk_sums = trunk_backward(
        geometry, tasks, batches, infos, upstream, enc_totals, dec_totals, scales, kept
    )
    input_grad, norm_sums, results = finish(
        tasks, batches,
        (to_slots(row_slot, enc_grad, dec_grad), flow, trunk_sums, trunk_owners, head_owned),
        (trunk_weight, trunk_mean_grad, trunk_mean_square,
         head_weight[0], head_mean_grad[0], head_mean_square[0]),
        (trunk_statistic, head_statistic[0], trunk_basis, head_basis[0]),
    )
    input_grad = input_grad.reshape(images.shape)
    (
        trunk_weight_new, trunk_one_new, trunk_two_new,
        head_weight_new, head_one_new, head_two_new,
        trunk_stat_new, head_stat_new, trunk_basis_new, head_basis_new,
    ) = results

    trunk_norm = jnp.stack([trunk_gain, trunk_offset], axis=1)
    trunk_norm_grad = norm_sums[:4].reshape(2, 2, channels)[:, ::-1]
    trunk_norm_one, trunk_norm_two, trunk_direction = adam(
        trunk_norm_grad, trunk_norm_mean_grad, trunk_norm_mean_square
    )
    head_norm = jnp.stack([head_gain, head_offset], axis=2)
    head_norm_grad = head_sums[:6].reshape(1, 3, 2, channels)[:, :, ::-1]
    head_norm_one, head_norm_two, head_direction = adam(
        head_norm_grad, head_norm_mean_grad, head_norm_mean_square
    )
    return (
        task_features,
        input_grad,
        trunk_weight_new,
        trunk_one_new,
        trunk_two_new,
        trunk_stat_new,
        trunk_basis_new,
        head_weight_new[None],
        head_one_new[None],
        head_two_new[None],
        head_stat_new[None],
        head_basis_new[None],
        trunk_norm - LEARN_NORM * trunk_direction,
        trunk_norm_one,
        trunk_norm_two,
        head_norm - LEARN_NORM * head_direction,
        head_norm_one,
        head_norm_two,
    )


def solution(mesh):
    placed = (
        P(("task", "batch"), None, None, None),
        P(("task", "batch")),
        P(("task", "batch"), None, None),
        P(),
        P("batch", None),
        P("batch", None),
        P("batch", None),
        P(),
        P(),
        P("task", "batch", None),
        P("task", "batch", None),
        P("task", "batch", None),
        P("task", None, None, None),
        P("task", None, None, None),
        P(),
        P(),
        P(),
        P(),
        P("task", None, None),
        P("task", None, None),
        P("task", None, None, None),
        P("task", None, None, None),
        P("task", None, "batch", None, None, None),
    )
    return jax.shard_map(
        functools.partial(local, mesh.shape["task"], mesh.shape["batch"]),
        mesh=mesh,
        in_specs=placed,
        out_specs=(
            P("task", None, "batch", None, None, None),
            P(("task", "batch"), None, None, None),
            P("batch", None),
            P("batch", None),
            P("batch", None),
            P(),
            P(),
            P("task", "batch", None),
            P("task", "batch", None),
            P("task", "batch", None),
            P("task", None, None, None),
            P("task", None, None, None),
            P(),
            P(),
            P(),
            P("task", None, None, None),
            P("task", None, None, None),
            P("task", None, None, None),
        ),
        check_vma=False,
    )
```

```python
import functools

import jax
import jax.numpy as jnp
from jax import lax
from jax.experimental import pallas as pl
from jax.experimental.pallas import tpu as pltpu
from jax.sharding import PartitionSpec as P

STEP = 10


EPS = 1e-05
ADAM_EPS = 1e-08
BETA_ONE = 0.95
BETA_TWO = 0.95
STAT_DECAY = 0.95
LEARN_MATRIX = 0.02
LEARN_NORM = 0.5
DECAY_MATRIX = 0.01
BF = jnp.bfloat16
F32 = jnp.float32
MESH = pl.DeviceIdType.MESH
MIB = 1 << 20

VMEM_SPEC = pl.BlockSpec(memory_space=pltpu.VMEM)
SMEM_SPEC = pl.BlockSpec(memory_space=pltpu.SMEM)


def run(body, outs, specs, args, scratch=(), vmem=40, flops=0):
    size = sum(o.size * o.dtype.itemsize for o in outs) + sum(a.size * a.dtype.itemsize for a in args)
    return pl.pallas_call(
        body,
        out_shape=tuple(outs),
        in_specs=[SMEM_SPEC if s == "s" else VMEM_SPEC for s in specs],
        out_specs=tuple(VMEM_SPEC for _ in outs),
        scratch_shapes=list(scratch),
        compiler_params=pltpu.CompilerParams(vmem_limit_bytes=vmem * MIB),
        cost_estimate=pl.CostEstimate(flops=flops, bytes_accessed=size, transcendentals=0),
    )(*args)


def shape(dims, kind):
    return jax.ShapeDtypeStruct(tuple(dims), kind)


def dot(a, b):
    return jnp.dot(a, b, preferred_element_type=F32)


def dot_nt(a, b):
    return lax.dot_general(a, b, (((1,), (1,)), ((), ())), preferred_element_type=F32)


def dot_tn(a, b):
    return lax.dot_general(a, b, (((0,), (0,)), ((), ())), preferred_element_type=F32)


def split(a):
    high = a.astype(BF)
    return high, (a - high.astype(F32)).astype(BF)


def dot3(kind, a, b):
    dims = {dot: (1, 0), dot_nt: (1, 1), dot_tn: (0, 0)}[kind]
    a_high, a_low = split(a)
    b_high, b_low = split(b)
    return kind(
        jnp.concatenate([a_high, a_high, a_low], axis=dims[0]),
        jnp.concatenate([b_high, b_low, b_high], axis=dims[1]),
    )


def places(height, breadth):
    index = lax.broadcasted_iota(jnp.int32, (height * breadth, 1), 0)
    row = lax.div(index, breadth)
    return row, index - row * breadth


def valid_rows(kind, height, breadth):
    row, col = places(height, breadth)
    shrunk = kind > 0
    row_limit = jnp.where(shrunk, height // 2, height)
    col_limit = jnp.where(shrunk, breadth // 2, breadth)
    return jnp.where((row < row_limit) & (col < col_limit), 1.0, 0.0).astype(F32)


def move(values, rows):
    gap = jnp.zeros((abs(rows),) + values.shape[1:], values.dtype)
    if rows > 0:
        return jnp.concatenate([gap, values[:-rows]], axis=0)
    return jnp.concatenate([values[-rows:], gap], axis=0)


def from_left(values, col):
    return jnp.where(col > 0, pltpu.roll(values, 1, 0), 0.0)


def from_right(values, col, breadth):
    return jnp.where(col < breadth - 1, pltpu.roll(values, values.shape[0] - 1, 0), 0.0)


def gather_taps(tap, breadth, col):
    lines = [move(tap(b), breadth) + tap(3 + b) + move(tap(6 + b), -breadth) for b in range(3)]
    return lines[1] + from_left(lines[0], col) + from_right(lines[2], col, breadth)


def spread_taps(values, breadth, col):
    lines = [from_right(values, col, breadth), values, from_left(values, col)]
    return [
        move(lines[b], breadth * (a - 1)) if a != 1 else lines[b] for a in range(3) for b in range(3)
    ]


def window_sum(values, row, col, breadth):
    count = values.shape[0]
    pair = values + jnp.where(
        col % 2 == 0, pltpu.roll(values, count - 1, 0), pltpu.roll(values, 1, 0)
    )
    return pair + jnp.where(row % 2 == 0, move(pair, -breadth), move(pair, breadth))


def silu_back(scaled):
    sig = jax.nn.sigmoid(scaled)
    return sig * (1.0 + scaled * (1.0 - sig))


def col_sum(values):
    return jnp.sum(values, axis=0, keepdims=True)


def put_sums(ref, rows):
    width = ref.shape[1]
    rows = list(rows) + [jnp.zeros((1, width), F32)] * (8 - len(rows))
    ref[...] = jnp.concatenate(rows, axis=0)


def each_image(geometry, body, start):
    number, height, breadth = geometry
    pixels = height * breadth

    def step(image, carry):
        return body(image, pl.ds(pl.multiple_of(image * pixels, 16), pixels), carry)

    return lax.fori_loop(0, number, step, start)


def zero_rows(count, width):
    return (jnp.zeros((1, width), F32),) * count


def greet(axes):
    barrier = pltpu.get_barrier_semaphore()
    for axis, size in axes:
        me = lax.axis_index(axis)
        for step in range(1, size):
            pl.semaphore_signal(
                barrier, inc=1, device_id={axis: lax.rem(me + step, size)}, device_id_type=MESH
            )
    pl.semaphore_wait(barrier, sum(size - 1 for _, size in axes))


def remote(source, target, sends, receives, peer, axis):
    return pltpu.make_async_remote_copy(
        src_ref=source,
        dst_ref=target,
        send_sem=sends,
        recv_sem=receives,
        device_id={axis: peer},
        device_id_type=MESH,
    )


def pack(rows):
    parts = [row[:, i : i + 128] for row in rows for i in range(0, row.shape[1], 128)]
    parts += [jnp.zeros((1, 128), F32)] * (8 - len(parts))
    return jnp.concatenate(parts, axis=0)


def unpack(tile, count, width):
    per = width // 128
    return [
        jnp.concatenate([tile[k * per + i : k * per + i + 1, :] for i in range(per)], axis=1)
        for k in range(count)
    ]


def total_rows(k, axis, size, rows, mine, slots, sends, receives, meanwhile=None):
    me = lax.axis_index(axis)
    tile = pack(rows)
    mine[k] = tile
    slots[k, me] = tile
    for step in range(1, size):
        peer = lax.rem(me + step, size)
        remote(mine.at[k], slots.at[k, me], sends.at[k, step], receives.at[k, me], peer, axis).start()
    if meanwhile:
        meanwhile()
    for step in range(1, size):
        peer = lax.rem(me + size - step, size)
        remote(
            mine.at[k], slots.at[k, peer], sends.at[k, step], receives.at[k, peer], peer, axis
        ).wait_recv()
    total = slots[k, 0]
    for peer in range(1, size):
        total = total + slots[k, peer]
    for step in range(1, size):
        peer = lax.rem(me + step, size)
        remote(
            mine.at[k], slots.at[k, me], sends.at[k, step], receives.at[k, me], peer, axis
        ).wait_send()
    return unpack(total, len(rows), rows[0].shape[1])


def total_scratch(count, size):
    return [
        pltpu.VMEM((count, 8, 128), F32),
        pltpu.VMEM((count, size, 8, 128), F32),
        pltpu.SemaphoreType.DMA((count, size)),
        pltpu.SemaphoreType.DMA((count, size)),
    ]


def columns_of(place, width):
    return pl.ds(pl.multiple_of(place * width, 128), width)


SPECS = {"s": SMEM_SPEC, "v": VMEM_SPEC, "h": pl.BlockSpec(memory_space=pltpu.HBM)}


def exchange_kernel(body, outs, specs, args, scratch, identity, vmem, flops=0, places_out=None):
    size = sum(o.size * o.dtype.itemsize for o in outs) + sum(a.size * a.dtype.itemsize for a in args)
    return pl.pallas_call(
        body,
        out_shape=tuple(outs),
        in_specs=[SPECS[s] for s in specs],
        out_specs=tuple(SPECS[s] for s in places_out or "v" * len(outs)),
        scratch_shapes=list(scratch),
        compiler_params=pltpu.CompilerParams(
            vmem_limit_bytes=vmem * MIB, collective_id=identity, has_side_effects=True
        ),
        cost_estimate=pl.CostEstimate(flops=flops, bytes_accessed=size, transcendentals=0),
    )(*args)


def info_rows(infos, i):
    return infos[pl.ds(pl.multiple_of(i * 8, 8), 8), :]


def valid_of(infos, i, height, breadth):
    return valid_rows(info_rows(infos, i)[1:2, 0:1], height, breadth)


def chosen_cells(narrow, infos, i):
    return (narrow * info_rows(infos, i)[0:1, : narrow.shape[1]]).astype(BF)


def norm_with(values, totals, scale):
    total, squares, count = totals
    center = total / count
    inverse = lax.rsqrt(squares / count - center * center + EPS)
    normal = (values - center) * inverse
    return normal, inverse, normal * scale[0] + scale[1]


def norm_back_with(upstream, normal, inverse, count, sums, scale, valid):
    return scale[0] * inverse * (upstream - sums[0] / count - normal * (sums[1] / count)) * valid


def silu(values):
    return values * jax.nn.sigmoid(values)


def window_count(height, breadth):
    return -(-(height * breadth // 4) // 16) * 16


def pool_choice(height, breadth, windows, flipped):
    pixels = height * breadth
    dims = (windows, pixels) if flipped else (pixels, windows)
    pixel = lax.broadcasted_iota(jnp.int32, dims, 1 if flipped else 0)
    window = lax.broadcasted_iota(jnp.int32, dims, 0 if flipped else 1)
    row = lax.div(pixel, breadth)
    col = pixel - row * breadth
    home = lax.div(row, 2) * (breadth // 2) + lax.div(col, 2)
    return jnp.where(home == window, 1.0, 0.0).astype(F32)


def rows_of(ref, first, count):
    return [ref[first + k : first + k + 1, :] for k in range(count)]


def window_rows(i, windows):
    return pl.ds(pl.multiple_of(i * windows, 16), windows)


def trunk_forward_body(
    geometry, tasks, batches,
    index, infos, x, kernel_slots, scales,
    enc_totals, dec_totals, features, *rest,
):
    kept, (enc_pre, dec_pre, spread), rest = rest[:6], rest[6:9], rest[9:]
    (
        enc_taps, dec_taps, wide, tap,
        work, pooled, pooled_all, part, pool_sends, pool_receives, sends, receives,
    mine, slots, total_sends, total_receives, saved,
    ) = rest
    number, height, breadth = geometry
    width = enc_pre.shape[1]
    windows = window_count(height, breadth)
    task = lax.axis_index("task")
    _, col = places(height, breadth)
    choice = pool_choice(height, breadth, windows, True)
    narrow = choice.astype(BF)

    sources = (x, enc_taps, dec_taps, enc_pre, dec_pre, spread)
    saves = [pltpu.make_async_copy(a, b, saved.at[k]) for k, (a, b) in enumerate(zip(sources, kept))]
    saves[0].start()
    channels = x.shape[1]

    def widen(i, carry):
        rows = pl.ds(pl.multiple_of(i * channels, 16), channels)
        wide[rows, :] = kernel_slots[rows, :].astype(F32)
        return carry

    def fetch(taps, first, begin, end):
        group = 32
        for p in range(begin, end):

            def some(i, carry):
                base = i * group
                for u in range(group):
                    slot = index[(first + p) * channels + base + u]
                    tap[pl.ds(base + u, 1), :] = wide[pl.ds(slot, 1), :]
                return carry

            lax.fori_loop(0, channels // group, some, 0)
            taps[:, p * width : (p + 1) * width] = tap[...].astype(BF)

    lax.fori_loop(0, wide.shape[0] // channels, widen, 0)
    fetch(enc_taps, 0, 0, 9)
    saves[1].start()

    def conv(x, taps, pre):
        def image(i, rows, carry):
            valid = valid_of(infos, i, height, breadth)
            work[...] = dot(x[rows, :], taps[...])
            out = gather_taps(lambda p: work[:, p * width : (p + 1) * width], breadth, col)
            pre[rows, :] = out
            kept = out * valid
            return (
                carry[0] + col_sum(kept),
                carry[1] + col_sum(kept * out),
                carry[2] + jnp.broadcast_to(col_sum(valid), (1, width)),
            )

        return each_image(geometry, image, zero_rows(3, width))

    def total(k, rows, meanwhile=None):
        return total_rows(
            k, "batch", batches, list(rows), mine, slots, total_sends, total_receives, meanwhile
        )

    sums = conv(x, enc_taps, enc_pre)
    saves[3].start()
    greet((("task", tasks), ("batch", batches)))
    totals = total(0, sums, lambda: fetch(dec_taps, 9, 0, 4))
    put_sums(enc_totals, totals)
    scale = rows_of(scales, 0, 2)

    def peer_of(step, incoming):
        return lax.rem(task + (tasks - step if incoming else step), tasks)

    def pool_copy(i, step, incoming=False):
        rows = window_rows(i, windows)
        peer = peer_of(step, incoming)
        target = pooled_all.at[rows, columns_of(peer if incoming else task, width)]
        return remote(
            pooled.at[rows, :], target, pool_sends.at[i, step], pool_receives.at[i, step], peer, "task"
        )

    def pool(i, rows, carry):
        valid = valid_of(infos, i, height, breadth)
        _, _, scaled = norm_with(enc_pre[rows, :], totals, scale)
        high, low = split(silu(scaled) * valid)
        mean = ((dot(narrow, high) + dot(narrow, low)) * 0.25).astype(BF)
        here = window_rows(i, windows)
        pooled[here, :] = mean
        pooled_all[here, columns_of(task, width)] = mean
        for step in range(1, tasks):
            pool_copy(i, step).start()
        return carry

    each_image(geometry, pool, 0)
    fetch(dec_taps, 9, 4, 9)
    saves[2].start()

    def unpool(i, rows, carry):
        for step in range(1, tasks):
            pool_copy(i, step, True).wait_recv()
        wide = dot_tn(chosen_cells(choice, infos, i), pooled_all[window_rows(i, windows), :])
        spread[rows, :] = wide.astype(BF)
        return carry

    each_image(geometry, unpool, 0)
    saves[5].start()
    sums = conv(spread, dec_taps, dec_pre)
    saves[4].start()
    totals = total(1, sums)
    put_sums(dec_totals, totals)
    scale = rows_of(scales, 2, 2)

    def feature_copy(i, rows, step, incoming=False):
        peer = peer_of(step, incoming)
        target = features.at[rows, columns_of(peer if incoming else task, width)]
        return remote(
            part.at[rows, :], target, sends.at[i, step], receives.at[i, step], peer, "task"
        )

    def finish(i, rows, carry):
        valid = valid_of(infos, i, height, breadth)
        _, _, scaled = norm_with(dec_pre[rows, :], totals, scale)
        low = (silu(scaled) * valid).astype(BF)
        part[rows, :] = low
        features[rows, columns_of(task, width)] = low
        for step in range(1, tasks):
            feature_copy(i, rows, step).start()
        return carry

    each_image(geometry, finish, 0)

    def settle(i, rows, carry):
        for step in range(1, tasks):
            feature_copy(i, rows, step, True).wait_recv()
            feature_copy(i, rows, step).wait_send()
            pool_copy(i, step).wait_send()
        return carry

    each_image(geometry, settle, 0)
    for copy in saves:
        copy.wait()


def trunk_forward(geometry, tasks, batches, index, infos, x, kernel_slots, scales):
    number, height, breadth = geometry
    pixels = height * breadth
    channels = x.shape[1]
    width = channels // tasks
    windows = window_count(height, breadth)
    tall = shape((x.shape[0], width), F32)
    taps = shape((channels, 9 * width), BF)
    outs = [
        shape((8, width), F32), shape((8, width), F32), shape(x.shape, BF),
        shape(x.shape, BF), taps, taps,
        tall, tall, shape(x.shape, BF),
    ]
    return exchange_kernel(
        functools.partial(trunk_forward_body, geometry, tasks, batches),
        outs,
        "svvvv",
        (index, infos, x, kernel_slots, scales),
        [
            pltpu.VMEM(tall.shape, F32),
            pltpu.VMEM(tall.shape, F32),
            pltpu.VMEM(x.shape, BF),
            pltpu.VMEM(taps.shape, BF),
            pltpu.VMEM(taps.shape, BF),
            pltpu.VMEM(kernel_slots.shape, F32),
            pltpu.VMEM((channels, width), F32),
            pltpu.VMEM((pixels, 9 * width), F32),
            pltpu.VMEM((number * windows, width), BF),
            pltpu.VMEM((number * windows, channels), BF),
            pltpu.VMEM((x.shape[0], width), BF),
        ]
        + [pltpu.SemaphoreType.DMA((number, tasks))] * 4
        + total_scratch(2, batches)
        + [pltpu.SemaphoreType.DMA((6,))],
        1,
        60,
        flops=4 * x.size * taps.shape[1],
        places_out="vvvhhhhhh",
    )


def head_body(
    geometry, tasks, batches, summing,
    infos, features, weights, cotangent, scales, counts,
    task_out, upstream, norm_sums, *rest,
):
    grads_out, rest = rest[0], rest[1:]
    (
        grads, pre_one, pre_two, pre_three, hidden, gated, nine, work, lower, out, arrived,
        sends, receives, mine, slots, total_sends, total_receives, loaded,
    ) = rest[:18]
    number, height, breadth = geometry
    channels = features.shape[1]
    width = channels // tasks
    windows = task_out.shape[1]
    task = lax.axis_index("task")
    half = work.shape[2]
    _, col = places(height, breadth)
    widen = pool_choice(height, breadth, windows, False).astype(BF)
    narrow = pool_choice(height, breadth, windows, True).astype(BF)
    count = jnp.broadcast_to(counts[2:3, 0:1], (1, channels))
    cuts = (pl.ds(0, 2 * channels), pl.ds(2 * channels, 9 * channels))
    loads = [
        pltpu.make_async_copy(weights.at[cut, :], grads.at[cut, :], loaded.at[k])
        for k, cut in enumerate(cuts)
    ]
    for copy in loads:
        copy.start()
    first = grads.at[pl.ds(0, channels), :]
    second = grads.at[pl.ds(channels, channels), :]

    def kernel_rows(p):
        return pl.ds((2 + p) * channels, channels)

    def total(k, rows, meanwhile=None):
        return total_rows(
            k, "batch", batches, list(rows), mine, slots, total_sends, total_receives, meanwhile
        )

    if summing:
        near, near_sends, near_receives = rest[18:]
        place, core, chips = pair_place(batches)
        block = near.shape[1]

        def near_copy(chip):
            return remote(
                block_rows(grads, 2 * chip + 1 - core, block), near.at[chip],
                near_sends.at[chip], near_receives.at[chip], 2 * place + 1 - core, "batch",
            )

    def put_stats(pre, rows, value, valid, carry):
        pre[rows, :] = value
        kept = value * valid
        return carry[0] + col_sum(kept), carry[1] + col_sum(kept * value)

    nothing = zero_rows(2, channels)
    scale_one, scale_two, scale_three = (rows_of(scales, 2 * k, 2) for k in range(3))

    loads[0].wait()

    def first_step(i, rows, carry):
        valid = valid_of(infos, i, height, breadth)
        return put_stats(pre_one, rows, dot(features[rows, :], first[...]), valid, carry)

    sums = each_image(geometry, first_step, nothing)
    greet((("task", tasks), ("batch", batches)))
    totals_one = total(0, sums) + [count]

    def second_step(i, rows, carry):
        valid = valid_of(infos, i, height, breadth)
        _, _, scaled = norm_with(pre_one[rows, :], totals_one, scale_one)
        low = (silu(scaled) * valid).astype(BF)
        hidden[rows, :] = low
        return put_stats(pre_two, rows, dot(low, second[...]), valid, carry)

    sums = each_image(geometry, second_step, nothing)
    totals_two = total(1, sums) + [count]

    def third_step(i, rows, carry):
        valid = valid_of(infos, i, height, breadth)
        _, _, scaled = norm_with(pre_two[rows, :], totals_two, scale_two)
        low = (jax.nn.sigmoid(scaled) * features[rows, :].astype(F32)).astype(BF)
        gated[rows, :] = low
        parts = []
        for j in range(channels // half):
            cut = slice(j * half, (j + 1) * half)
            for p in range(9):
                work[p] = dot(low, grads[kernel_rows(p), cut])
            parts.append(gather_taps(lambda p: work[p], breadth, col))
        return put_stats(pre_three, rows, jnp.concatenate(parts, axis=1), valid, carry)

    loads[1].wait()
    sums = each_image(geometry, third_step, nothing)
    totals_three = total(2, sums) + [count]

    def out_step(i, rows, carry):
        valid = valid_of(infos, i, height, breadth)
        normal, _, scaled = norm_with(pre_three[rows, :], totals_three, scale_three)
        high, low = split(silu(scaled) * valid)
        mean = (dot(narrow, high) + dot(narrow, low)) * 0.25
        task_out[i] = mean.astype(BF)
        dy = silu_back(scaled) * dot(widen, cotangent[i]) * 0.25 * valid
        lower[rows, :] = dy
        return carry[0] + col_sum(dy), carry[1] + col_sum(dy * normal)

    sums = each_image(geometry, out_step, nothing)
    sums_three = total(3, sums)

    def third_back(i, rows, carry):
        valid = valid_of(infos, i, height, breadth)
        normal, inverse, _ = norm_with(pre_three[rows, :], totals_three, scale_three)
        dz = norm_back_with(lower[rows, :], normal, inverse, count, sums_three, scale_three, valid)
        for p, moved in enumerate(spread_taps(dz, breadth, col)):
            nine[p, rows, :] = moved.astype(BF)
        flow = None
        for p in range(9):
            piece = dot_nt(nine[p, rows, :], grads[kernel_rows(p), :])
            flow = piece if flow is None else flow + piece
        lower[rows, :] = flow
        normal, _, scaled = norm_with(pre_two[rows, :], totals_two, scale_two)
        gate = jax.nn.sigmoid(scaled)
        dy = flow * features[rows, :].astype(F32) * gate * (1.0 - gate) * valid
        pre_three[rows, :] = dy
        return carry[0] + col_sum(dy), carry[1] + col_sum(dy * normal)

    sums = each_image(geometry, third_back, nothing)

    def taps(begin, end):
        def tap(p, carry):
            rows = pl.ds(pl.multiple_of((2 + p) * channels, channels), channels)
            grads[rows, :] = dot_tn(gated[...], nine[p]).astype(BF)
            return carry

        lax.fori_loop(begin, end, tap, 0)

    sums_two = total(4, sums, lambda: taps(0, 3))

    def second_back(i, rows, carry):
        valid = valid_of(infos, i, height, breadth)
        normal, inverse, scaled = norm_with(pre_two[rows, :], totals_two, scale_two)
        dz = norm_back_with(
            pre_three[rows, :], normal, inverse, count, sums_two, scale_two, valid
        ).astype(BF)
        out[rows, :] = dz
        lower[rows, :] = lower[rows, :] * jax.nn.sigmoid(scaled)
        normal, _, scaled = norm_with(pre_one[rows, :], totals_one, scale_one)
        dy = silu_back(scaled) * dot_nt(dz, second[...]) * valid
        pre_three[rows, :] = dy
        return carry[0] + col_sum(dy), carry[1] + col_sum(dy * normal)

    sums = each_image(geometry, second_back, nothing)

    def weight_rows():
        grads[pl.ds(channels, channels), :] = dot_tn(hidden[...], out[...]).astype(BF)
        taps(3, 5)

    sums_one = total(5, sums, weight_rows)

    def flow_copy(i, rows, step, incoming=False):
        peer = lax.rem(task + (tasks - step if incoming else step), tasks)
        return remote(
            out.at[rows, columns_of(peer, width)], arrived.at[step - 1, rows, :],
            sends.at[i, step], receives.at[i, step], peer, "task",
        )

    def first_back(i, rows, carry):
        valid = valid_of(infos, i, height, breadth)
        normal, inverse, _ = norm_with(pre_one[rows, :], totals_one, scale_one)
        dz = norm_back_with(
            pre_three[rows, :], normal, inverse, count, sums_one, scale_one, valid
        ).astype(BF)
        hidden[rows, :] = dz
        flow = (lower[rows, :] + dot_nt(dz, first[...])) * valid
        out[rows, :] = flow.astype(BF)
        for step in range(1, tasks):
            flow_copy(i, rows, step).start()
        return carry

    each_image(geometry, first_back, 0)
    taps(5, 9)
    if summing:
        for chip in range(1, chips):
            near_copy(chip).start()
    grads[pl.ds(0, channels), :] = dot_tn(features[...], hidden[...]).astype(BF)
    if summing:
        near_copy(0).start()
        for chip in (*range(1, chips), 0):
            near_copy(chip).wait_recv()
            own = block_rows(grads, 2 * chip + core, block)[...].astype(F32)
            grads_out[chip] = (own + near[chip].astype(F32)).astype(BF)
    else:
        grads_out[...] = grads[...]
    put_sums(norm_sums, sums_one + sums_two + sums_three)

    def settle(i, rows, carry):
        for step in range(1, tasks):
            flow_copy(i, rows, step, True).wait_recv()
        flow = out[rows, columns_of(task, width)].astype(F32)
        for step in range(1, tasks):
            flow = flow + arrived[step - 1, rows, :].astype(F32)
        upstream[rows, :] = flow
        for step in range(1, tasks):
            flow_copy(i, rows, step).wait_send()
        return carry

    each_image(geometry, settle, 0)
    if summing:
        for chip in range(chips):
            near_copy(chip).wait_send()


def head(geometry, tasks, batches, infos, features, weights, cotangent, scales, counts):
    number, height, breadth = geometry
    pixels = height * breadth
    total, channels = features.shape
    width = channels // tasks
    block = weights.shape[0] // batches
    chips = batches // 2
    summing = block % 16 == 0
    outs = [
        shape((number, pixels // 4, channels), BF),
        shape((total, width), F32),
        shape((8, channels), F32),
        shape((chips, block, channels) if summing else weights.shape, BF),
    ]
    scratch = []
    if summing:
        scratch = [pltpu.VMEM((chips, block, channels), BF)]
        scratch += [pltpu.SemaphoreType.DMA((chips,))] * 2
    pooled, upstream, sums, grads = exchange_kernel(
        functools.partial(head_body, geometry, tasks, batches, summing),
        outs,
        "vvhvvv",
        (infos, features, weights, cotangent, scales, counts),
        [
            pltpu.VMEM(weights.shape, BF),
            pltpu.VMEM(features.shape, F32),
            pltpu.VMEM(features.shape, F32),
            pltpu.VMEM(features.shape, F32),
            pltpu.VMEM(features.shape, BF),
            pltpu.VMEM(features.shape, BF),
            pltpu.VMEM((9,) + features.shape, BF),
            pltpu.VMEM((9, pixels, min(channels, 256)), F32),
            pltpu.VMEM(features.shape, F32),
            pltpu.VMEM(features.shape, BF),
            pltpu.VMEM((tasks - 1, total, width), BF),
        ]
        + [pltpu.SemaphoreType.DMA((number, tasks))] * 2
        + total_scratch(6, batches)
        + [pltpu.SemaphoreType.DMA((2,))]
        + scratch,
        2,
        61,
        flops=6 * total * channels * weights.shape[0],
    )
    if summing:
        owned = lax.psum_scatter(
            grads.reshape(chips * block, channels), "batch", scatter_dimension=0,
            axis_index_groups=[list(range(core, batches, 2)) for core in range(2)], tiled=True,
        )
    else:
        owned = lax.psum_scatter(grads, "batch", scatter_dimension=0, tiled=True)
    return pooled, upstream, sums, owned


def trunk_backward_body(
    geometry, tasks, batches,
    infos, upstream, enc_totals, dec_totals, scales, *rest,
):
    kept, rest = rest[:6], rest[6:]
    (enc_grad, dec_grad, flow_out, norm_sums), rest = rest[:4], rest[4:]
    (x, enc_taps, dec_taps, enc_pre, dec_pre, spread), rest = rest[:6], rest[6:]
    (
        nine, change, packed, arrived, pooled, sends, receives,
        mine, slots, total_sends, total_receives, loaded,
    ) = rest
    targets = (x, enc_taps, dec_taps, enc_pre, dec_pre, spread)
    loads = [pltpu.make_async_copy(a, b, loaded.at[k]) for k, (a, b) in enumerate(zip(kept, targets))]
    for k in (4, 2, 5, 3, 1, 0):
        loads[k].start()
    number, height, breadth = geometry
    channels = x.shape[1]
    width = enc_pre.shape[1]
    windows = window_count(height, breadth)
    task = lax.axis_index("task")
    _, col = places(height, breadth)
    widen = pool_choice(height, breadth, windows, False).astype(BF)
    narrow = pool_choice(height, breadth, windows, True)
    nothing = zero_rows(2, width)

    def total(k, rows):
        return total_rows(
            k, "batch", batches, list(rows), mine, slots, total_sends, total_receives
        )

    def change_of(pre, totals, scale, flow):
        def image(i, rows, carry):
            valid = valid_of(infos, i, height, breadth)
            normal, _, scaled = norm_with(pre[rows, :], totals, scale)
            dy = silu_back(scaled) * flow(i, rows) * valid
            change[rows, :] = dy
            return carry[0] + col_sum(dy), carry[1] + col_sum(dy * normal)

        return each_image(geometry, image, nothing)

    def back(pre, totals, scale, sums, taps, put):
        def image(i, rows, carry):
            valid = valid_of(infos, i, height, breadth)
            normal, inverse, _ = norm_with(pre[rows, :], totals, scale)
            dz = norm_back_with(change[rows, :], normal, inverse, totals[2], sums, scale, valid)
            for p, moved in enumerate(spread_taps(dz, breadth, col)):
                nine[rows, p * width : (p + 1) * width] = moved.astype(BF)
            put(i, rows, dot_nt(nine[rows, :], taps[...]) * valid)
            return carry

        each_image(geometry, image, 0)

    totals = rows_of(dec_totals, 0, 3)
    scale = rows_of(scales, 2, 2)
    loads[4].wait()
    sums = change_of(dec_pre, totals, scale, lambda i, rows: upstream[rows, :])
    greet((("task", tasks), ("batch", batches)))
    dec_sums = total(0, sums)

    def copy_of(i, step, incoming=False):
        rows = window_rows(i, windows)
        peer = lax.rem(task + (tasks - step if incoming else step), tasks)
        return remote(
            packed.at[rows, columns_of(peer, width)], arrived.at[step - 1, rows, :],
            sends.at[i, step], receives.at[i, step], peer, "task",
        )

    def put_packed(i, rows, flow):
        chosen = chosen_cells(narrow, infos, i)
        packed[window_rows(i, windows), :] = dot(chosen, flow.astype(BF)).astype(BF)
        for step in range(1, tasks):
            copy_of(i, step).start()

    loads[2].wait()
    back(dec_pre, totals, scale, dec_sums, dec_taps, put_packed)
    loads[5].wait()
    dec_grad[...] = dot_tn(spread[...], nine[...])

    def collect(i, carry):
        for step in range(1, tasks):
            copy_of(i, step, True).wait_recv()
        rows = window_rows(i, windows)
        flow = packed[rows, columns_of(task, width)].astype(F32)
        for step in range(1, tasks):
            flow = flow + arrived[step - 1, rows, :].astype(F32)
        pooled[rows, :] = flow
        for step in range(1, tasks):
            copy_of(i, step).wait_send()
        return carry

    lax.fori_loop(0, number, collect, 0)

    def widened(i, rows):
        high, low = split(pooled[window_rows(i, windows), :])
        return (dot(widen, high) + dot(widen, low)) * 0.25

    totals = rows_of(enc_totals, 0, 3)
    scale = rows_of(scales, 0, 2)
    loads[3].wait()
    sums = change_of(enc_pre, totals, scale, widened)
    enc_sums = total(1, sums)

    def put_flow(i, rows, flow):
        flow_out[rows, :] = flow.astype(BF)

    loads[1].wait()
    back(enc_pre, totals, scale, enc_sums, enc_taps, put_flow)
    loads[0].wait()
    enc_grad[...] = dot_tn(x[...], nine[...])
    put_sums(norm_sums, enc_sums + dec_sums)


def trunk_backward(
    geometry, tasks, batches, infos, upstream, enc_totals, dec_totals, scales, kept
):
    number, height, breadth = geometry
    x, enc_taps, dec_taps = kept[:3]
    total, channels = x.shape
    width = channels // tasks
    windows = window_count(height, breadth)
    outs = [
        shape(enc_taps.shape, F32),
        shape(dec_taps.shape, F32),
        shape(x.shape, BF),
        shape((8, width), F32),
    ]
    return exchange_kernel(
        functools.partial(trunk_backward_body, geometry, tasks, batches),
        outs,
        "vvvvvhhhhhh",
        (infos, upstream, enc_totals, dec_totals, scales, *kept),
        [pltpu.VMEM(a.shape, a.dtype) for a in kept]
        + [
            pltpu.VMEM((total, 9 * width), BF),
            pltpu.VMEM((total, width), F32),
            pltpu.VMEM((number * windows, channels), BF),
            pltpu.VMEM((tasks - 1, number * windows, width), BF),
            pltpu.VMEM((number * windows, width), F32),
        ]
        + [pltpu.SemaphoreType.DMA((number, tasks))] * 2
        + total_scratch(2, batches)
        + [pltpu.SemaphoreType.DMA((6,))],
        3,
        60,
        flops=8 * x.size * enc_taps.shape[1],
    )


def to_slots_body(index, enc, dec, slots, wide):
    count = slots.shape[0]
    channels = enc.shape[0]
    width = slots.shape[1]
    step = 1024
    group = 32
    for p in range(18):
        source = enc if p < 9 else dec
        q = p % 9

        def place(i, carry):
            base = pl.multiple_of(i * group, group)
            values = source[pl.ds(base, group), q * width : (q + 1) * width]
            for u in range(group):
                wide[pl.ds(index[p * channels + base + u], 1), :] = values[u : u + 1, :]
            return carry

        lax.fori_loop(0, channels // group, place, 0)

    def narrow(i, carry):
        rows = pl.ds(pl.multiple_of(i * step, step), step)
        slots[rows, :] = wide[rows, :].astype(BF)
        return carry

    lax.fori_loop(0, count // step, narrow, 0)


def to_slots(index, enc, dec):
    width = enc.shape[1] // 9
    dims = (index.shape[0], width)
    return run(
        to_slots_body, [shape(dims, BF)], "svv", (index, enc, dec), [pltpu.VMEM(dims, F32)], vmem=60
    )[0]


def adam(gradient, moment_one, moment_two):
    new_one = BETA_ONE * moment_one + (1.0 - BETA_ONE) * gradient
    new_two = BETA_TWO * moment_two + (1.0 - BETA_TWO) * gradient * gradient
    direction = (
        new_one / (1.0 - BETA_ONE**STEP) / (jnp.sqrt(new_two / (1.0 - BETA_TWO**STEP)) + ADAM_EPS)
    )
    return new_one, new_two, direction


def pair_place(batches):
    me = lax.axis_index("batch")
    place = lax.div(me, 2)
    return place, me - 2 * place, batches // 2


def greet_pairs(tasks, batches):
    place, core, chips = pair_place(batches)
    task = lax.axis_index("task")
    barrier = pltpu.get_barrier_semaphore()

    def signal(device):
        pl.semaphore_signal(barrier, inc=1, device_id=device, device_id_type=MESH)

    for step in range(1, tasks):
        signal({"task": lax.rem(task + step, tasks)})
    signal({"batch": 2 * place + 1 - core})
    for step in range(1, chips):
        signal({"batch": 2 * lax.rem(place + step, chips) + core})
    pl.semaphore_wait(barrier, tasks - 1 + chips)


def block_rows(ref, index, count):
    return ref.at[pl.ds(pl.multiple_of(index * count, 8), count), :]


SMALL = 128 * 128


def far_first(chips):
    return sorted(range(chips), key=lambda step: -min(step, chips - step))


def pair_sum(batches, rows_of_block, own_block, near, paired, far, sems):
    place, core, chips = pair_place(batches)
    count = near.shape[1]
    near_send, near_receive, far_send, far_receive = sems
    other = 2 * place + 1 - core
    ring = chips == 4 and count % 32 == 0 and near.shape[2] * count > SMALL
    half = count // 2
    halves = (pl.ds(0, half), pl.ds(half, half))

    def near_copy(step):
        chip = lax.rem(place + step, chips)
        return remote(rows_of_block(2 * chip + 1 - core), near.at[step],
                      near_send.at[step], near_receive.at[step], other, "batch")

    def far_copy(step, incoming=False):
        chip = lax.rem(place + (chips - step if incoming else step), chips)
        return remote(paired.at[step], far.at[step], far_send.at[step], far_receive.at[step],
                      2 * chip + core, "batch")

    def ring_copy(which, way):
        chip = lax.rem(place + (1 if way == 0 else chips - 1), chips)
        if which == 0:
            source, target = paired.at[2, halves[way], :], far.at[2 + way, halves[0], :]
        else:
            cut = halves[way] if which == 2 else halves[1 - way]
            source, target = paired.at[1 if way == 0 else 3, cut, :], far.at[way, cut, :]
        k = 2 * which + way
        return remote(source, target, far_send.at[k], far_receive.at[k], 2 * chip + core, "batch")

    def start():
        for step in far_first(chips):
            near_copy(step).start()

    def middle():
        for step in far_first(chips):
            near_copy(step).wait_recv()
            if step:
                paired[step] = (own_block(step) + near[step].astype(F32)).astype(paired.dtype)
                if not ring:
                    far_copy(step).start()
                elif step == 2:
                    ring_copy(0, 0).start()
                    ring_copy(0, 1).start()
                else:
                    ring_copy(1, 0 if step == 1 else 1).start()

    def relay():
        if not ring:
            return
        for way in range(2):
            ring_copy(0, way).wait_recv()
            step = 1 if way == 0 else 3
            total = paired[step, halves[way], :].astype(F32) + far[2 + way, halves[0], :].astype(F32)
            paired[step, halves[way], :] = total.astype(paired.dtype)
            ring_copy(2, way).start()

    def end():
        total = own_block(0) + near[0].astype(F32)
        if ring:
            for way in range(2):
                ring_copy(1, way).wait_recv()
                ring_copy(2, way).wait_recv()
                total = total + far[way].astype(F32)
            for k in range(3):
                for way in range(2):
                    ring_copy(k, way).wait_send()
        else:
            for step in range(1, chips):
                far_copy(step, True).wait_recv()
                total = total + far[step].astype(F32)
            for step in range(1, chips):
                far_copy(step).wait_send()
        for step in range(chips):
            near_copy(step).wait_send()
        return total

    return start, middle, relay, end


def blocks_in(source, batches, count, piece=0, pieces=1):
    place, core, chips = pair_place(batches)

    def rows(index):
        start = (index * pieces + piece) * count
        return source.at[pl.ds(pl.multiple_of(start, 8), count), :]

    def own(step):
        chip = lax.rem(place + step, chips)
        return rows(2 * chip + core)[...].astype(F32)

    return rows, own


def pair_scratch(batches, rows, width, kind):
    chips = batches // 2
    return [pltpu.VMEM((chips, rows // batches, width), kind)] * 3 + [
        pltpu.SemaphoreType.DMA((max(chips, 6),))
    ] * 4


def chip_spread(batches, block, sends, receives):
    place, core, chips = pair_place(batches)
    count, width = block(place).shape
    ring = chips == 4 and count % 32 == 0 and width * count > SMALL
    half = count // 2

    def copy(step, incoming=False):
        peer = lax.rem(place + (chips - step if incoming else step), chips)
        ref = block(peer if incoming else place)
        return remote(ref, ref, sends.at[step], receives.at[step], 2 * peer + core, "batch")

    def pass_on(way, incoming=False):
        step = 1 if way == 0 else chips - 1
        peer = lax.rem(place + (chips - step if incoming else step), chips)
        home = lax.rem(place + (2 if incoming else chips - step), chips)
        ref = block(home).at[pl.ds(way * half, half), :]
        k = 2 if way == 0 else 0
        return remote(ref, ref, sends.at[k], receives.at[k], 2 * peer + core, "batch")

    steps = (1, chips - 1) if ring else tuple(range(1, chips))

    def start():
        for step in steps:
            copy(step).start()

    def relay():
        if ring:
            for way, step in enumerate(steps):
                copy(step, True).wait_recv()
                pass_on(way).start()

    def settle():
        if ring:
            for way in range(2):
                pass_on(way, True).wait_recv()
        else:
            for step in steps:
                copy(step, True).wait_recv()

    def drain():
        for step in steps:
            copy(step).wait_send()
        if ring:
            for way in range(2):
                pass_on(way).wait_send()

    return start, relay, settle, drain


def arrive_body(
    tasks, batches, geometry,
    image_raw, info, index, weight, head_weight,
    slots, x, infos, owners, head_low,
    image, head_raw, head_loaded, raw, raw_loaded, x_send, x_receive, info_send, info_receive,
    chip_send, chip_receive, pair_send, pair_receive, own,
):
    task = lax.axis_index("task")
    place, core, chips = pair_place(batches)
    count, width = raw.shape
    load = pltpu.make_async_copy(weight.at[:, columns_of(task, width)], raw, raw_loaded)
    load.start()
    head_load = pltpu.make_async_copy(head_weight, head_raw, head_loaded)
    head_load.start()
    number, height, breadth = geometry
    pixels = height * breadth
    for n in range(number):
        valid = valid_rows(info[8 * n + 1 : 8 * n + 2, 0:1], height, breadth)
        rows = slice(n * pixels, (n + 1) * pixels)
        image[rows, :] = (image_raw[rows, :].astype(F32) * valid).astype(BF)
    greet_pairs(tasks, batches)

    def task_copy(source, target, sends, receives, step, incoming=False):
        peer = lax.rem(task + (tasks - step if incoming else step), tasks)
        home = peer if incoming else task
        return remote(source, block_rows(target, home, source.shape[0]), sends.at[step],
                      receives.at[step], peer, "task")

    def moves(step, incoming=False):
        return (
            task_copy(info, infos, info_send, info_receive, step, incoming),
            task_copy(image, x, x_send, x_receive, step, incoming),
        )

    def block(chip):
        return block_rows(slots, 2 * chip + core, count)

    def pair_copy(hop, incoming=False):
        chip = lax.rem(place + chips - hop, chips)
        ref = block_rows(slots, 2 * chip + (1 - core if incoming else core), count)
        return remote(ref, ref, pair_send.at[hop], pair_receive.at[hop], 2 * place + 1 - core, "batch")

    start, relay, settle, drain = chip_spread(batches, block, chip_send, chip_receive)
    ring = chips == 4 and count % 32 == 0 and width * count > SMALL
    load.wait()
    block(place)[...] = raw[...].astype(BF)
    start()
    pair_copy(0).start()
    for step in range(1, tasks):
        for copy in moves(step):
            copy.start()
    locals_ = [
        pltpu.make_async_copy(image, block_rows(x, task, image.shape[0]), own.at[0]),
        pltpu.make_async_copy(info, block_rows(infos, task, info.shape[0]), own.at[1]),
    ]
    for copy in locals_:
        copy.start()
    mine = lax.broadcasted_iota(jnp.int32, (count, 1), 0) + lax.axis_index("batch") * count
    found = jnp.zeros((count, 128), F32)
    for k in range(index.shape[0] // 2, index.shape[0]):
        found = jnp.where(index[k : k + 1, :] == mine, 1.0, found)
    found = jnp.max(found, axis=1, keepdims=True)
    owners[:, 0:1] = 1.0 - found
    owners[:, 1:2] = found
    head_load.wait()
    head_low[...] = head_raw[...].astype(BF)
    relay()
    if ring:
        pair_copy(1).start()
        pair_copy(3).start()
        settle()
        pair_copy(2).start()
    else:
        settle()
        for hop in range(1, chips):
            pair_copy(hop).start()
    for copy in locals_:
        copy.wait()
    for step in range(1, tasks):
        for copy in moves(step, True):
            copy.wait_recv()
    for hop in range(chips):
        pair_copy(hop, True).wait_recv()
    for step in range(1, tasks):
        for copy in moves(step):
            copy.wait_send()
    for hop in range(chips):
        pair_copy(hop).wait_send()
    drain()


def arrive(tasks, batches, geometry, image, info, index, weight, head_weight):
    count, channels = weight.shape
    width = channels // tasks
    chips = batches // 2
    return exchange_kernel(
        functools.partial(arrive_body, tasks, batches, geometry),
        [
            shape((count * batches, width), BF),
            shape((image.shape[0] * tasks, channels), BF),
            shape((info.shape[0] * tasks, info.shape[1]), F32),
            shape((count, 2), F32),
            shape(head_weight.shape, BF),
        ],
        "vvvhh",
        (image, info, index.reshape(-1, 128), weight, head_weight),
        [
            pltpu.VMEM(image.shape, BF),
            pltpu.VMEM(head_weight.shape, F32),
            pltpu.SemaphoreType.DMA,
            pltpu.VMEM((count, width), F32),
            pltpu.SemaphoreType.DMA,
        ]
        + [pltpu.SemaphoreType.DMA((tasks,))] * 4
        + [pltpu.SemaphoreType.DMA((max(chips, 4),))] * 4
        + [pltpu.SemaphoreType.DMA((2,))],
        4,
        60,
        flops=20000 * MIB,
    )


def soap_rows(cuts, grad, owners, state, low, first, begin=0, end=None):
    total = grad.shape[0]

    def chunk(i, carry):
        rows = pl.ds(pl.multiple_of(i * (total // cuts), 8), total // cuts)
        values = grad[rows, :].astype(F32)
        marks = owners(i * (total // cuts), total // cuts)
        count = len(marks)
        rotated = None
        for m in range(count):
            part = dot((values * marks[m]).astype(BF), low[first + m])
            rotated = part if rotated is None else rotated + part
        new_one, new_two, direction = adam(rotated, state[1, rows, :], state[2, rows, :])
        state[1, rows, :] = new_one
        state[2, rows, :] = new_two
        stepped = None
        for m in range(count):
            part = dot_nt((direction * marks[m]).astype(BF), low[first + m])
            stepped = part if stepped is None else stepped + part
        old = state[0, rows, :]
        state[0, rows, :] = old - LEARN_MATRIX * (stepped + DECAY_MATRIX * old)
        return carry

    lax.fori_loop(begin, cuts if end is None else end, chunk, 0)


def factor_rows(values, identity, turn):
    size, width = values.shape
    sub = lax.broadcasted_iota(jnp.int32, (size, width), 0)
    rolled = pltpu.roll(values, turn, 1)
    columns = [jnp.broadcast_to(rolled[:, j : j + 1], (size, width)) for j in range(size)]
    scale = jnp.zeros((size, width), F32)
    for j in range(size):
        root = lax.rsqrt(columns[j][j : j + 1, :])
        scale = jnp.where(sub == j, root, scale)
        lower = jnp.where(sub > j, columns[j] * root, 0.0)
        values = values - lower * (values[j : j + 1, :] * root)
        identity = identity - lower * (identity[j : j + 1, :] * root)
        for i in range(j + 1, size):
            columns[i] = columns[i] - lower * (columns[i][j : j + 1, :] * root)
    return values * scale, identity * scale


GROUP = 16
PANEL = 128


def upper_blocks(size):
    return [(a, b) for a in range(0, size, PANEL) for b in range(a, size, PANEL)]


def renew_panel(k, product, made, tables, inverses):
    count, size = product.shape[0], product.shape[1]
    here = slice(k * PANEL, (k + 1) * PANEL)
    row = lax.broadcasted_iota(jnp.int32, (PANEL, PANEL), 0)
    col = lax.broadcasted_iota(jnp.int32, (PANEL, PANEL), 1)
    unit = jnp.where(row == col, 1.0, 0.0).astype(F32)
    for n in range(count):
        tables[n][:, :PANEL] = dot3(dot_tn, product[n, :, here], product[n, :, here])
        tables[n][:, PANEL:] = unit

    def group(q, carry):
        rows = pl.ds(pl.multiple_of(q * GROUP, GROUP), GROUP)
        turn = lax.rem(PANEL - q * GROUP, PANEL)
        done = [
            factor_rows(tables[n][rows, :PANEL], tables[n][rows, PANEL:], turn)
            for n in range(count)
        ]
        for n in range(count):
            upper, inverse = done[n]
            inverses[n][rows, :] = inverse
            both = jnp.concatenate([upper, inverse], axis=1)
            tables[n][...] = tables[n][...] - dot3(dot_tn, upper, both)
        return carry

    lax.fori_loop(0, PANEL // GROUP, group, 0)
    for n in range(count):
        turned = dot3(dot_nt, product[n, :, here], inverses[n][...])
        made[n, :, here] = turned
        if k < size // PANEL - 1:
            rest = slice((k + 1) * PANEL, size)
            product[n, :, rest] = product[n, :, rest] - dot3(
                dot, turned, dot3(dot_tn, turned, product[n, :, rest])
            )


def tail_body(
    tasks, batches, cuts, pieces,
    slots, flow, sums, owners, head_grad,
    weight, one, two, head_weight, head_one, head_two, basis, head_basis,
    input_grad, norm_sums, state_new, head_state_new, grams, head_grams,
    grad, part, state, head_state, mine, head_mine, bases, low,
    flow_in, flow_send, flow_receive, send, receive, sum_send, sum_receive,
    *rest,
):
    row_scratch = [rest[7 * k : 7 * k + 7] for k in range(pieces)]
    gram_scratch, head_scratch, rest = rest[7 * pieces :][:7], rest[7 * pieces + 7 :][:7], rest[7 * pieces + 14 :]
    chip_send, chip_receive, task_send, task_receive, pair_send, pair_receive, load, save = rest
    task = lax.axis_index("task")
    place, core, chips = pair_place(batches)
    width = part.shape[1]
    channels = grad.shape[1]
    pixels = input_grad.shape[0]
    trunk_total = basis.shape[0]
    head_total = head_basis.shape[0]
    count, head_count = mine.shape[0] // batches, head_mine.shape[0] // batches

    def trunk_marks(start, size):
        rows = pl.ds(pl.multiple_of(start, 8), size)
        return [owners[rows, m : m + 1] for m in range(trunk_total)]

    def head_marks(start, size):
        index = lax.broadcasted_iota(jnp.int32, (size, 1), 0) + start
        index = index + lax.axis_index("batch") * head_grad.shape[0]
        owner = jnp.minimum(lax.div(index, channels), head_total - 1)
        return [jnp.where(owner == m, 1.0, 0.0).astype(F32) for m in range(head_total)]

    def put_grams(target, rows, columns, marks):
        for m, mark in enumerate(marks):
            held = (rows[...].astype(F32) * mark).astype(BF)
            target[m * channels : (m + 1) * channels, :] = dot_tn(held, columns[...]).astype(
                target.dtype
            )

    def put_packed_grams(target, rows, marks):
        n = 0
        for mark in marks:
            held = (rows[...].astype(F32) * mark).astype(BF)
            for a, b in upper_blocks(channels):
                block = dot_tn(held[:, a : a + PANEL], rows[:, b : b + PANEL])
                target[n : n + PANEL, :] = block.astype(target.dtype)
                n += PANEL
        if n < target.shape[0]:
            target[n:, :] = jnp.zeros((target.shape[0] - n, PANEL), target.dtype)

    def peer_of(step, incoming):
        return lax.rem(task + (tasks - step if incoming else step), tasks)

    def flow_copy(step, incoming=False):
        peer = peer_of(step, incoming)
        return remote(block_rows(flow, peer, pixels), flow_in.at[step - 1], flow_send.at[step],
                      flow_receive.at[step], peer, "task")

    def sum_copy(step, incoming=False):
        peer = peer_of(step, incoming)
        home = peer if incoming else task
        return remote(sums, norm_sums.at[:, columns_of(home, width)], sum_send.at[step],
                      sum_receive.at[step], peer, "task")

    def part_copy(k, step, incoming=False):
        peer = peer_of(step, incoming)
        home = peer if incoming else task
        return remote(part.at[part_rows(k), :], grad.at[part_rows(k), columns_of(home, width)],
                      send.at[k, step], receive.at[k, step], peer, "task")

    def trunk_block(chip, home, which):
        rows = pl.ds(pl.multiple_of((2 * chip + which) * count, 8), count)
        return grams.at[rows, columns_of(home, width)]

    def head_block(chip, which):
        return block_rows(head_grams, 2 * chip + which, head_count)

    def task_copy(step, hop, incoming=False):
        peer = peer_of(step, incoming)
        chip = lax.rem(place + chips - hop, chips)
        block = trunk_block(chip, peer if incoming else task, core)
        return remote(block, block, task_send.at[step, hop], task_receive.at[step, hop], peer, "task")

    def pair_copy(kind, hop, incoming=False):
        chip = lax.rem(place + chips - hop, chips)
        which = 1 - core if incoming else core
        home = lax.rem(task + tasks - kind, tasks)
        block = head_block(chip, which) if kind == tasks else trunk_block(chip, home, which)
        return remote(block, block, pair_send.at[kind, hop], pair_receive.at[kind, hop],
                      2 * place + 1 - core, "batch")

    def sum_of(source, scratch, piece=0, total=1):
        near, paired, far, *sems = scratch
        return pair_sum(
            batches, *blocks_in(source, batches, near.shape[1], piece, total), near, paired, far, sems
        )

    def part_rows(k):
        size = part.shape[0] // pieces
        return pl.ds(k * size, size)

    moves = [
        (basis, bases.at[pl.ds(0, trunk_total)]),
        (head_basis, bases.at[pl.ds(trunk_total, head_total)]),
        (head_weight, head_state.at[0]),
        (head_one, head_state.at[1]),
        (head_two, head_state.at[2]),
        (weight, state.at[0]),
        (one, state.at[1]),
        (two, state.at[2]),
    ]
    loads = [pltpu.make_async_copy(a, b, load.at[k]) for k, (a, b) in enumerate(moves)]
    for copy in loads:
        copy.start()
    saves = [
        pltpu.make_async_copy(state, state_new, save.at[0]),
        pltpu.make_async_copy(head_state, head_state_new, save.at[1]),
    ]

    greet_pairs(tasks, batches)
    row_sums = [sum_of(slots, row_scratch[k], k, pieces) for k in range(pieces)]
    for stages in row_sums:
        stages[0]()
    for step in range(1, tasks):
        sum_copy(step).start()
        flow_copy(step).start()
    norm_sums[:, columns_of(task, width)] = sums[...]
    row_sums[0][1]()
    put_packed_grams(head_mine, head_grad, head_marks(0, head_grad.shape[0]))
    head_start, head_middle, head_relay, head_end = sum_of(head_mine, head_scratch)
    row_sums[0][2]()
    for stages in row_sums[1:]:
        stages[1]()
    head_start()
    for stages in row_sums[1:]:
        stages[2]()
    head_middle()
    for copy in loads[:5]:
        copy.wait()
    for m in range(trunk_total + head_total):
        low[m] = bases[m].astype(BF)
    for k, stages in enumerate(row_sums):
        total = stages[3]().astype(BF)
        part[part_rows(k), :] = total
        for step in range(1, tasks):
            part_copy(k, step).start()
        grad[part_rows(k), columns_of(task, width)] = total
    head_relay()

    soap_rows(cuts, head_grad, head_marks, head_state, low, trunk_total)
    saves[1].start()
    total = block_rows(flow, task, pixels)[...].astype(F32)
    for step in range(1, tasks):
        flow_copy(step, True).wait_recv()
        total = total + flow_in[step - 1].astype(F32)
    input_grad[...] = total
    head_block(place, core)[...] = head_end().astype(head_grams.dtype)
    trunk_spread = chip_spread(
        batches, lambda chip: trunk_block(chip, task, core), chip_send.at[0], chip_receive.at[0]
    )
    head_spread = chip_spread(
        batches, lambda chip: head_block(chip, core), chip_send.at[1], chip_receive.at[1]
    )
    head_spread[0]()
    pair_copy(tasks, 0).start()
    for k in range(pieces):
        for step in range(1, tasks):
            part_copy(k, step, True).wait_recv()

    put_grams(mine, grad, part, trunk_marks(0, grad.shape[0]))
    start, middle, relay, end = sum_of(mine, gram_scratch)
    start()
    middle()
    head_spread[1]()
    for copy in loads[5:]:
        copy.wait()
    relay()
    soap_rows(cuts, grad, trunk_marks, state, low, 0, 0, cuts // 2)
    trunk_block(place, task, core)[...] = end().astype(grams.dtype)
    trunk_spread[0]()
    for step in range(1, tasks):
        task_copy(step, 0).start()
    pair_copy(0, 0).start()
    soap_rows(cuts, grad, trunk_marks, state, low, 0, cuts // 2, cuts)
    saves[0].start()
    trunk_spread[1]()
    trunk_spread[2]()
    for hop in range(1, chips):
        for step in range(1, tasks):
            task_copy(step, hop).start()
        pair_copy(0, hop).start()
    head_spread[2]()
    for hop in range(1, chips):
        pair_copy(tasks, hop).start()
    for hop in range(chips):
        for step in range(1, tasks):
            task_copy(step, hop, True).wait_recv()
            pair_copy(step, hop).start()
    for hop in range(chips):
        for kind in range(tasks + 1):
            pair_copy(kind, hop, True).wait_recv()
    for step in range(1, tasks):
        sum_copy(step, True).wait_recv()

    for copy in saves:
        copy.wait()
    for step in range(1, tasks):
        sum_copy(step).wait_send()
        for k in range(pieces):
            part_copy(k, step).wait_send()
        flow_copy(step).wait_send()
    for hop in range(chips):
        for kind in range(tasks + 1):
            pair_copy(kind, hop).wait_send()
        for step in range(1, tasks):
            task_copy(step, hop).wait_send()
    trunk_spread[3]()
    head_spread[3]()


def renew_body(
    core, state, head_state, grams, head_grams, stat, head_stat, basis, head_basis,
    weight_new, one_new, two_new, head_weight_new, head_one_new, head_two_new,
    stat_new, head_stat_new, low_made,
    stats, product, made, low_grams, low_head_grams, held, head_held, load, save, *work,
):
    trunk_total, head_total = stat.shape[0], head_stat.shape[0]
    channels = stat.shape[1]
    count = trunk_total + head_total
    shared = product.shape[0]
    tables, inverses = work[:shared], work[shared:]
    loads = []
    blocks = upper_blocks(channels)
    packed = len(blocks) * PANEL

    def gram_rows(m, start):
        if m < trunk_total:
            first = m * channels + start
            return low_grams[first : first + PANEL, :].astype(F32)
        parts = []
        for b in range(0, channels, PANEL):
            n = blocks.index((min(start, b), max(start, b)))
            first = (m - trunk_total) * packed + n * PANEL
            block = low_head_grams[first : first + PANEL, :].astype(F32)
            parts.append(block if b >= start else block.T)
        return jnp.concatenate(parts, axis=1)

    def bring(source, target):
        copy = pltpu.make_async_copy(source, target, load.at[len(loads)])
        loads.append(copy)
        return copy

    for m in range(count):
        first = m < trunk_total
        place = m if first else m - trunk_total
        size = channels if first else packed
        rows = pl.ds(place * size, size)
        here, there = (grams, low_grams) if first else (head_grams, low_head_grams)
        bring(here.at[rows, :], there.at[rows, :]).start()
        bring((stat if first else head_stat).at[place], stats.at[m]).start()

    for n in range(shared):
        both = [
            basis.at[n] if n < trunk_total else head_basis.at[n - trunk_total],
            head_basis.at[n],
        ]
        copy = bring(both[1], made.at[n])
        for which, source in enumerate(both):

            @pl.when(core[0] == which)
            def _():
                pltpu.make_async_copy(source, made.at[n], load.at[2 * count + n]).start()

    bring(state, held).start()
    bring(head_state, head_held).start()
    sources = [held.at[k] for k in range(3)] + [head_held.at[k] for k in range(3)]
    targets = [weight_new, one_new, two_new, head_weight_new, head_one_new, head_two_new]
    saves = [pltpu.make_async_copy(a, b, save.at[k]) for k, (a, b) in enumerate(zip(sources, targets))]
    for m in range(count):
        for copy in loads[2 * m : 2 * m + 2]:
            copy.wait()
        for start in range(0, channels, PANEL):
            rows = slice(start, start + PANEL)
            stats[m, rows, :] = STAT_DECAY * stats[m, rows, :] + (1.0 - STAT_DECAY) * gram_rows(m, start)
    for begin, size, out in ((0, trunk_total, stat_new), (trunk_total, head_total, head_stat_new)):
        copy = pltpu.make_async_copy(stats.at[pl.ds(begin, size)], out, save.at[len(saves)])
        copy.start()
        saves.append(copy)
    for n in range(shared):
        loads[2 * count + n].wait()
        product[n] = dot3(dot, stats[trunk_total * core[0] + n], made[n])
    for k in range(channels // PANEL):
        renew_panel(k, product, made, tables, inverses)
        if k == 0:
            for copy in loads[2 * count + shared :]:
                copy.wait()
            for copy in saves[:6]:
                copy.start()
        cut = slice(k * PANEL, (k + 1) * PANEL)
        low_made[:, :, cut] = made[:, :, cut].astype(BF)
    for copy in saves:
        copy.wait()


def swap_body(batches, x, out, sends, receives):
    place, core, _ = pair_place(batches)
    other = 2 * place + 1 - core
    barrier = pltpu.get_barrier_semaphore()
    pl.semaphore_signal(barrier, inc=1, device_id={"batch": other}, device_id_type=MESH)
    pl.semaphore_wait(barrier, 1)
    copy = remote(x, out, sends, receives, other, "batch")
    copy.start()
    copy.wait()


def finish(tasks, batches, local_grads, rows, matrices):
    slots, flow, sums, owners, head_grad = local_grads
    stat, head_stat, basis, head_basis = matrices
    total, channels = rows[0].shape
    width = channels // tasks
    trunk_total, head_total = basis.shape[0], head_basis.shape[0]
    gram_rows = trunk_total * channels
    packed = len(upper_blocks(channels)) * PANEL
    head_rows = -(-head_total * packed // (16 * batches)) * 16 * batches
    chips = batches // 2
    kind = BF if gram_rows % (16 * batches) == 0 else F32
    cuts = 4 if total % 64 == 0 and head_grad.shape[0] % 64 == 0 else 1
    pieces = 2 if total % 64 == 0 else 1
    square = (trunk_total + head_total, channels, channels)
    pixels = flow.shape[0] // tasks
    input_grad, norm_sums, *made = exchange_kernel(
        functools.partial(tail_body, tasks, batches, cuts, pieces),
        [
            shape((pixels, channels), F32),
            shape((8, channels), F32),
            shape((3, total, channels), F32),
            shape((3,) + head_grad.shape, F32),
            shape((gram_rows, channels), kind),
            shape((head_rows, PANEL), BF),
        ],
        "vvvvvhhhhhhhh",
        (*local_grads, *rows, basis, head_basis),
        [
            pltpu.VMEM((total, channels), BF),
            pltpu.VMEM((total, width), BF),
            pltpu.VMEM((3, total, channels), F32),
            pltpu.VMEM((3,) + head_grad.shape, F32),
            pltpu.VMEM((gram_rows, width), kind),
            pltpu.VMEM((head_rows, PANEL), BF),
            pltpu.VMEM(square, F32),
            pltpu.VMEM(square, BF),
            pltpu.VMEM((tasks - 1, pixels, channels), BF),
        ]
        + [pltpu.SemaphoreType.DMA((tasks,))] * 2
        + [pltpu.SemaphoreType.DMA((pieces, tasks))] * 2
        + [pltpu.SemaphoreType.DMA((tasks,))] * 2
        + pair_scratch(batches, slots.shape[0] // pieces, width, BF) * pieces
        + pair_scratch(batches, gram_rows, width, kind)
        + pair_scratch(batches, head_rows, PANEL, BF)
        + [pltpu.SemaphoreType.DMA((2, max(chips, 4)))] * 2
        + [pltpu.SemaphoreType.DMA((tasks, chips))] * 2
        + [pltpu.SemaphoreType.DMA((tasks + 1, chips))] * 2
        + [pltpu.SemaphoreType.DMA((8,)), pltpu.SemaphoreType.DMA((2,))],
        5,
        60,
        flops=50000 * MIB,
        places_out="vvhhvv",
    )
    outs = [shape(a.shape, F32) for a in (*rows, *matrices)]
    hbm = pl.BlockSpec(memory_space=pltpu.HBM)
    count = trunk_total + head_total
    shared = max(trunk_total, head_total)
    core = lax.rem(lax.axis_index("batch"), 2)
    own = (shared, channels, channels)
    *results, made_low = pl.pallas_call(
        renew_body,
        out_shape=(*outs[:8], shape(own, BF)),
        in_specs=[SMEM_SPEC] + [hbm] * 8,
        out_specs=(*(hbm for _ in outs[:8]), VMEM_SPEC),
        scratch_shapes=[pltpu.VMEM(square, F32)]
        + [pltpu.VMEM(own, F32)] * 2
        + [pltpu.VMEM(made[2].shape, kind), pltpu.VMEM(made[3].shape, BF)]
        + [pltpu.VMEM(made[0].shape, F32), pltpu.VMEM(made[1].shape, F32)]
        + [pltpu.SemaphoreType.DMA((2 * count + shared + 2,))]
        + [pltpu.SemaphoreType.DMA((8,))]
        + [pltpu.VMEM((PANEL, 2 * PANEL), F32)] * shared
        + [pltpu.VMEM((PANEL, PANEL), F32)] * shared,
        compiler_params=pltpu.CompilerParams(vmem_limit_bytes=60 * MIB),
        cost_estimate=pl.CostEstimate(
            flops=50000 * MIB, bytes_accessed=64 * MIB, transcendentals=0
        ),
    )(core.reshape(1), *made, *matrices)
    theirs = exchange_kernel(
        functools.partial(swap_body, batches),
        [shape(own, BF)],
        "v",
        (made_low,),
        [pltpu.SemaphoreType.DMA] * 2,
        6,
        60,
        flops=5000 * MIB,
    )[0]
    results += [
        jnp.where(core == which, made_low[:total], theirs[:total]).astype(F32)
        for which, total in enumerate((trunk_total, head_total))
    ]
    return input_grad, norm_sums, results


def local(
    tasks,
    batches,
    images,
    image_small,
    pool_index,
    row_slot,
    trunk_weight,
    trunk_mean_grad,
    trunk_mean_square,
    trunk_statistic,
    trunk_basis,
    head_weight,
    head_mean_grad,
    head_mean_square,
    head_statistic,
    head_basis,
    trunk_gain,
    trunk_offset,
    trunk_norm_mean_grad,
    trunk_norm_mean_square,
    head_gain,
    head_offset,
    head_norm_mean_grad,
    head_norm_mean_square,
    cotangent,
):
    number, height, breadth, channels = images.shape
    pixels = height * breadth
    shown = tasks * number
    geometry = (shown, height, breadth)
    task = lax.axis_index("task")
    width = channels // tasks

    def quarter(values):
        return lax.dynamic_slice_in_dim(values, task * width, width, values.ndim - 1)

    def inside(flags):
        row_limit = jnp.where(flags > 0, height // 2, height)[:, None, None]
        col_limit = jnp.where(flags > 0, breadth // 2, breadth)[:, None, None]
        return (jnp.arange(height, dtype=jnp.int32)[None, :, None] < row_limit) & (
            jnp.arange(breadth, dtype=jnp.int32)[None, None, :] < col_limit
        )

    cell = 2 * jnp.arange(2, dtype=jnp.int32)[:, None, None] + jnp.arange(2, dtype=jnp.int32)
    cells = pool_index.reshape(number, height // 2, 1, breadth // 2, 1)
    valid = inside(image_small)
    chosen = ((cells == cell).reshape(number, height, breadth) & valid).reshape(number, pixels)
    info = jnp.zeros((8 * number, channels), F32)
    info = info.at[::8, :pixels].set(chosen.astype(F32))
    info = info.at[1::8, 0].set(image_small.astype(F32))
    slots, x, infos, trunk_owners, head_low = arrive(
        tasks, batches, (number, height, breadth), images.reshape(number * pixels, channels),
        info, row_slot, trunk_weight, head_weight[0],
    )
    head_rows = lax.all_gather(head_low, "batch", axis=0, tiled=True)

    scales = quarter(jnp.stack([trunk_gain, trunk_offset], axis=1)).reshape(4, width)
    enc_totals, dec_totals, features, *kept = trunk_forward(
        geometry, tasks, batches, row_slot, infos, x, slots, scales
    )
    head_scales = jnp.stack([head_gain[0], head_offset[0]], axis=1).reshape(6, channels)
    pooled, upstream, head_sums, head_owned = head(
        geometry, tasks, batches, infos, features, head_rows,
        cotangent.reshape(shown, pixels // 4, channels), head_scales, enc_totals,
    )
    task_features = pooled.reshape(cotangent.shape)
    enc_grad, dec_grad, flow, trunk_sums = trunk_backward(
        geometry, tasks, batches, infos, upstream, enc_totals, dec_totals, scales, kept
    )
    input_grad, norm_sums, results = finish(
        tasks, batches,
        (to_slots(row_slot, enc_grad, dec_grad), flow, trunk_sums, trunk_owners, head_owned),
        (trunk_weight, trunk_mean_grad, trunk_mean_square,
         head_weight[0], head_mean_grad[0], head_mean_square[0]),
        (trunk_statistic, head_statistic[0], trunk_basis, head_basis[0]),
    )
    input_grad = input_grad.reshape(images.shape)
    (
        trunk_weight_new, trunk_one_new, trunk_two_new,
        head_weight_new, head_one_new, head_two_new,
        trunk_stat_new, head_stat_new, trunk_basis_new, head_basis_new,
    ) = results

    trunk_norm = jnp.stack([trunk_gain, trunk_offset], axis=1)
    trunk_norm_grad = norm_sums[:4].reshape(2, 2, channels)[:, ::-1]
    trunk_norm_one, trunk_norm_two, trunk_direction = adam(
        trunk_norm_grad, trunk_norm_mean_grad, trunk_norm_mean_square
    )
    head_norm = jnp.stack([head_gain, head_offset], axis=2)
    head_norm_grad = head_sums[:6].reshape(1, 3, 2, channels)[:, :, ::-1]
    head_norm_one, head_norm_two, head_direction = adam(
        head_norm_grad, head_norm_mean_grad, head_norm_mean_square
    )
    return (
        task_features,
        input_grad,
        trunk_weight_new,
        trunk_one_new,
        trunk_two_new,
        trunk_stat_new,
        trunk_basis_new,
        head_weight_new[None],
        head_one_new[None],
        head_two_new[None],
        head_stat_new[None],
        head_basis_new[None],
        trunk_norm - LEARN_NORM * trunk_direction,
        trunk_norm_one,
        trunk_norm_two,
        head_norm - LEARN_NORM * head_direction,
        head_norm_one,
        head_norm_two,
    )


def solution(mesh):
    placed = (
        P(("task", "batch"), None, None, None),
        P(("task", "batch")),
        P(("task", "batch"), None, None),
        P(),
        P("batch", None),
        P("batch", None),
        P("batch", None),
        P(),
        P(),
        P("task", "batch", None),
        P("task", "batch", None),
        P("task", "batch", None),
        P("task", None, None, None),
        P("task", None, None, None),
        P(),
        P(),
        P(),
        P(),
        P("task", None, None),
        P("task", None, None),
        P("task", None, None, None),
        P("task", None, None, None),
        P("task", None, "batch", None, None, None),
    )
    return jax.shard_map(
        functools.partial(local, mesh.shape["task"], mesh.shape["batch"]),
        mesh=mesh,
        in_specs=placed,
        out_specs=(
            P("task", None, "batch", None, None, None),
            P(("task", "batch"), None, None, None),
            P("batch", None),
            P("batch", None),
            P("batch", None),
            P(),
            P(),
            P("task", "batch", None),
            P("task", "batch", None),
            P("task", "batch", None),
            P("task", None, None, None),
            P("task", None, None, None),
            P(),
            P(),
            P(),
            P("task", None, None, None),
            P("task", None, None, None),
            P("task", None, None, None),
        ),
        check_vma=False,
    )
```

```python
import functools

import jax
import jax.numpy as jnp
from jax import lax
from jax.experimental import pallas as pl
from jax.experimental.pallas import tpu as pltpu
from jax.sharding import PartitionSpec as P

STEP = 10


EPS = 1e-05
ADAM_EPS = 1e-08
BETA_ONE = 0.95
BETA_TWO = 0.95
STAT_DECAY = 0.95
LEARN_MATRIX = 0.02
LEARN_NORM = 0.5
DECAY_MATRIX = 0.01
BF = jnp.bfloat16
F32 = jnp.float32
MESH = pl.DeviceIdType.MESH
MIB = 1 << 20

VMEM_SPEC = pl.BlockSpec(memory_space=pltpu.VMEM)
SMEM_SPEC = pl.BlockSpec(memory_space=pltpu.SMEM)


def run(body, outs, specs, args, scratch=(), vmem=40, flops=0):
    size = sum(o.size * o.dtype.itemsize for o in outs) + sum(a.size * a.dtype.itemsize for a in args)
    return pl.pallas_call(
        body,
        out_shape=tuple(outs),
        in_specs=[SMEM_SPEC if s == "s" else VMEM_SPEC for s in specs],
        out_specs=tuple(VMEM_SPEC for _ in outs),
        scratch_shapes=list(scratch),
        compiler_params=pltpu.CompilerParams(vmem_limit_bytes=vmem * MIB),
        cost_estimate=pl.CostEstimate(flops=flops, bytes_accessed=size, transcendentals=0),
    )(*args)


def shape(dims, kind):
    return jax.ShapeDtypeStruct(tuple(dims), kind)


def dot(a, b):
    return jnp.dot(a, b, preferred_element_type=F32)


def dot_nt(a, b):
    return lax.dot_general(a, b, (((1,), (1,)), ((), ())), preferred_element_type=F32)


def dot_tn(a, b):
    return lax.dot_general(a, b, (((0,), (0,)), ((), ())), preferred_element_type=F32)


def split(a):
    high = a.astype(BF)
    return high, (a - high.astype(F32)).astype(BF)


def dot3(kind, a, b):
    dims = {dot: (1, 0), dot_nt: (1, 1), dot_tn: (0, 0)}[kind]
    a_high, a_low = split(a)
    b_high, b_low = split(b)
    return kind(
        jnp.concatenate([a_high, a_high, a_low], axis=dims[0]),
        jnp.concatenate([b_high, b_low, b_high], axis=dims[1]),
    )


def places(height, breadth):
    index = lax.broadcasted_iota(jnp.int32, (height * breadth, 1), 0)
    row = lax.div(index, breadth)
    return row, index - row * breadth


def valid_rows(kind, height, breadth):
    row, col = places(height, breadth)
    shrunk = kind > 0
    row_limit = jnp.where(shrunk, height // 2, height)
    col_limit = jnp.where(shrunk, breadth // 2, breadth)
    return jnp.where((row < row_limit) & (col < col_limit), 1.0, 0.0).astype(F32)


def move(values, rows):
    gap = jnp.zeros((abs(rows),) + values.shape[1:], values.dtype)
    if rows > 0:
        return jnp.concatenate([gap, values[:-rows]], axis=0)
    return jnp.concatenate([values[-rows:], gap], axis=0)


def from_left(values, col):
    return jnp.where(col > 0, pltpu.roll(values, 1, 0), 0.0)


def from_right(values, col, breadth):
    return jnp.where(col < breadth - 1, pltpu.roll(values, values.shape[0] - 1, 0), 0.0)


def gather_taps(tap, breadth, col):
    lines = [move(tap(b), breadth) + tap(3 + b) + move(tap(6 + b), -breadth) for b in range(3)]
    return lines[1] + from_left(lines[0], col) + from_right(lines[2], col, breadth)


def spread_taps(values, breadth, col):
    lines = [from_right(values, col, breadth), values, from_left(values, col)]
    return [
        move(lines[b], breadth * (a - 1)) if a != 1 else lines[b] for a in range(3) for b in range(3)
    ]


def window_sum(values, row, col, breadth):
    count = values.shape[0]
    pair = values + jnp.where(
        col % 2 == 0, pltpu.roll(values, count - 1, 0), pltpu.roll(values, 1, 0)
    )
    return pair + jnp.where(row % 2 == 0, move(pair, -breadth), move(pair, breadth))


def silu_back(scaled):
    sig = jax.nn.sigmoid(scaled)
    return sig * (1.0 + scaled * (1.0 - sig))


def col_sum(values):
    return jnp.sum(values, axis=0, keepdims=True)


def put_sums(ref, rows):
    width = ref.shape[1]
    rows = list(rows) + [jnp.zeros((1, width), F32)] * (8 - len(rows))
    ref[...] = jnp.concatenate(rows, axis=0)


def each_image(geometry, body, start):
    number, height, breadth = geometry
    pixels = height * breadth

    def step(image, carry):
        return body(image, pl.ds(pl.multiple_of(image * pixels, 16), pixels), carry)

    return lax.fori_loop(0, number, step, start)


def zero_rows(count, width):
    return (jnp.zeros((1, width), F32),) * count


def greet(axes):
    barrier = pltpu.get_barrier_semaphore()
    for axis, size in axes:
        me = lax.axis_index(axis)
        for step in range(1, size):
            pl.semaphore_signal(
                barrier, inc=1, device_id={axis: lax.rem(me + step, size)}, device_id_type=MESH
            )
    pl.semaphore_wait(barrier, sum(size - 1 for _, size in axes))


def remote(source, target, sends, receives, peer, axis):
    return pltpu.make_async_remote_copy(
        src_ref=source,
        dst_ref=target,
        send_sem=sends,
        recv_sem=receives,
        device_id={axis: peer},
        device_id_type=MESH,
    )


def pack(rows):
    parts = [row[:, i : i + 128] for row in rows for i in range(0, row.shape[1], 128)]
    parts += [jnp.zeros((1, 128), F32)] * (8 - len(parts))
    return jnp.concatenate(parts, axis=0)


def unpack(tile, count, width):
    per = width // 128
    return [
        jnp.concatenate([tile[k * per + i : k * per + i + 1, :] for i in range(per)], axis=1)
        for k in range(count)
    ]


def total_rows(k, axis, size, rows, mine, slots, sends, receives, meanwhile=None):
    me = lax.axis_index(axis)
    tile = pack(rows)
    mine[k] = tile
    slots[k, me] = tile
    for step in range(1, size):
        peer = lax.rem(me + step, size)
        remote(mine.at[k], slots.at[k, me], sends.at[k, step], receives.at[k, me], peer, axis).start()
    if meanwhile:
        meanwhile()
    for step in range(1, size):
        peer = lax.rem(me + size - step, size)
        remote(
            mine.at[k], slots.at[k, peer], sends.at[k, step], receives.at[k, peer], peer, axis
        ).wait_recv()
    total = slots[k, 0]
    for peer in range(1, size):
        total = total + slots[k, peer]
    for step in range(1, size):
        peer = lax.rem(me + step, size)
        remote(
            mine.at[k], slots.at[k, me], sends.at[k, step], receives.at[k, me], peer, axis
        ).wait_send()
    return unpack(total, len(rows), rows[0].shape[1])


def total_scratch(count, size):
    return [
        pltpu.VMEM((count, 8, 128), F32),
        pltpu.VMEM((count, size, 8, 128), F32),
        pltpu.SemaphoreType.DMA((count, size)),
        pltpu.SemaphoreType.DMA((count, size)),
    ]


def columns_of(place, width):
    return pl.ds(pl.multiple_of(place * width, 128), width)


SPECS = {"s": SMEM_SPEC, "v": VMEM_SPEC, "h": pl.BlockSpec(memory_space=pltpu.HBM)}


def exchange_kernel(body, outs, specs, args, scratch, identity, vmem, flops=0, places_out=None):
    size = sum(o.size * o.dtype.itemsize for o in outs) + sum(a.size * a.dtype.itemsize for a in args)
    return pl.pallas_call(
        body,
        out_shape=tuple(outs),
        in_specs=[SPECS[s] for s in specs],
        out_specs=tuple(SPECS[s] for s in places_out or "v" * len(outs)),
        scratch_shapes=list(scratch),
        compiler_params=pltpu.CompilerParams(
            vmem_limit_bytes=vmem * MIB, collective_id=identity, has_side_effects=True
        ),
        cost_estimate=pl.CostEstimate(flops=flops, bytes_accessed=size, transcendentals=0),
    )(*args)


def info_rows(infos, i):
    return infos[pl.ds(pl.multiple_of(i * 8, 8), 8), :]


def valid_of(infos, i, height, breadth):
    return valid_rows(info_rows(infos, i)[1:2, 0:1], height, breadth)


def chosen_cells(narrow, infos, i):
    return (narrow * info_rows(infos, i)[0:1, : narrow.shape[1]]).astype(BF)


def norm_with(values, totals, scale):
    total, squares, count = totals
    center = total / count
    inverse = lax.rsqrt(squares / count - center * center + EPS)
    normal = (values - center) * inverse
    return normal, inverse, normal * scale[0] + scale[1]


def norm_back_with(upstream, normal, inverse, count, sums, scale, valid):
    return scale[0] * inverse * (upstream - sums[0] / count - normal * (sums[1] / count)) * valid


def silu(values):
    return values * jax.nn.sigmoid(values)


def window_count(height, breadth):
    return -(-(height * breadth // 4) // 16) * 16


def pool_choice(height, breadth, windows, flipped):
    pixels = height * breadth
    dims = (windows, pixels) if flipped else (pixels, windows)
    pixel = lax.broadcasted_iota(jnp.int32, dims, 1 if flipped else 0)
    window = lax.broadcasted_iota(jnp.int32, dims, 0 if flipped else 1)
    row = lax.div(pixel, breadth)
    col = pixel - row * breadth
    home = lax.div(row, 2) * (breadth // 2) + lax.div(col, 2)
    return jnp.where(home == window, 1.0, 0.0).astype(F32)


def rows_of(ref, first, count):
    return [ref[first + k : first + k + 1, :] for k in range(count)]


def window_rows(i, windows):
    return pl.ds(pl.multiple_of(i * windows, 16), windows)


def trunk_forward_body(
    geometry, tasks, batches,
    index, infos, x_far, kernel_slots, scales,
    enc_totals, dec_totals, features, *rest,
):
    kept, (enc_pre, dec_pre, spread), rest = rest[:5], rest[5:8], rest[8:]
    (
        x, x_loaded, enc_taps, dec_taps, wide, tap,
        work, pooled, pooled_all, part, pool_sends, pool_receives, sends, receives,
    mine, slots, total_sends, total_receives, saved,
    ) = rest
    number, height, breadth = geometry
    width = enc_pre.shape[1]
    windows = window_count(height, breadth)
    task = lax.axis_index("task")
    _, col = places(height, breadth)
    choice = pool_choice(height, breadth, windows, True)
    narrow = choice.astype(BF)

    x_load = pltpu.make_async_copy(x_far, x, x_loaded)
    x_load.start()
    sources = (enc_taps, dec_taps, enc_pre, dec_pre, spread)
    saves = [pltpu.make_async_copy(a, b, saved.at[k]) for k, (a, b) in enumerate(zip(sources, kept))]
    channels = x.shape[1]

    def widen(i, carry):
        rows = pl.ds(pl.multiple_of(i * channels, 16), channels)
        wide[rows, :] = kernel_slots[rows, :].astype(F32)
        return carry

    def fetch(taps, first, begin, end):
        group = 32
        for p in range(begin, end):

            def some(i, carry):
                base = i * group
                for u in range(group):
                    slot = index[(first + p) * channels + base + u]
                    tap[pl.ds(base + u, 1), :] = wide[pl.ds(slot, 1), :]
                return carry

            lax.fori_loop(0, channels // group, some, 0)
            taps[:, p * width : (p + 1) * width] = tap[...].astype(BF)

    lax.fori_loop(0, wide.shape[0] // channels, widen, 0)
    fetch(enc_taps, 0, 0, 9)
    saves[0].start()
    x_load.wait()

    def conv(x, taps, pre):
        def image(i, rows, carry):
            valid = valid_of(infos, i, height, breadth)
            work[...] = dot(x[rows, :], taps[...])
            out = gather_taps(lambda p: work[:, p * width : (p + 1) * width], breadth, col)
            pre[rows, :] = out
            kept = out * valid
            return (
                carry[0] + col_sum(kept),
                carry[1] + col_sum(kept * out),
                carry[2] + jnp.broadcast_to(col_sum(valid), (1, width)),
            )

        return each_image(geometry, image, zero_rows(3, width))

    def total(k, rows, meanwhile=None):
        return total_rows(
            k, "batch", batches, list(rows), mine, slots, total_sends, total_receives, meanwhile
        )

    sums = conv(x, enc_taps, enc_pre)
    saves[2].start()
    greet((("task", tasks), ("batch", batches)))
    totals = total(0, sums, lambda: fetch(dec_taps, 9, 0, 4))
    put_sums(enc_totals, totals)
    scale = rows_of(scales, 0, 2)

    def peer_of(step, incoming):
        return lax.rem(task + (tasks - step if incoming else step), tasks)

    def pool_copy(i, step, incoming=False):
        rows = window_rows(i, windows)
        peer = peer_of(step, incoming)
        target = pooled_all.at[rows, columns_of(peer if incoming else task, width)]
        return remote(
            pooled.at[rows, :], target, pool_sends.at[i, step], pool_receives.at[i, step], peer, "task"
        )

    def pool(i, rows, carry):
        valid = valid_of(infos, i, height, breadth)
        _, _, scaled = norm_with(enc_pre[rows, :], totals, scale)
        high, low = split(silu(scaled) * valid)
        mean = ((dot(narrow, high) + dot(narrow, low)) * 0.25).astype(BF)
        here = window_rows(i, windows)
        pooled[here, :] = mean
        pooled_all[here, columns_of(task, width)] = mean
        for step in range(1, tasks):
            pool_copy(i, step).start()
        return carry

    each_image(geometry, pool, 0)
    fetch(dec_taps, 9, 4, 9)
    saves[1].start()

    def unpool(i, rows, carry):
        for step in range(1, tasks):
            pool_copy(i, step, True).wait_recv()
        wide = dot_tn(chosen_cells(choice, infos, i), pooled_all[window_rows(i, windows), :])
        spread[rows, :] = wide.astype(BF)
        return carry

    each_image(geometry, unpool, 0)
    saves[4].start()
    sums = conv(spread, dec_taps, dec_pre)
    saves[3].start()
    totals = total(1, sums)
    put_sums(dec_totals, totals)
    scale = rows_of(scales, 2, 2)

    def feature_copy(i, rows, step, incoming=False):
        peer = peer_of(step, incoming)
        target = features.at[rows, columns_of(peer if incoming else task, width)]
        return remote(
            part.at[rows, :], target, sends.at[i, step], receives.at[i, step], peer, "task"
        )

    def finish(i, rows, carry):
        valid = valid_of(infos, i, height, breadth)
        _, _, scaled = norm_with(dec_pre[rows, :], totals, scale)
        low = (silu(scaled) * valid).astype(BF)
        part[rows, :] = low
        features[rows, columns_of(task, width)] = low
        for step in range(1, tasks):
            feature_copy(i, rows, step).start()
        return carry

    each_image(geometry, finish, 0)

    def settle(i, rows, carry):
        for step in range(1, tasks):
            feature_copy(i, rows, step, True).wait_recv()
            feature_copy(i, rows, step).wait_send()
            pool_copy(i, step).wait_send()
        return carry

    each_image(geometry, settle, 0)
    for copy in saves:
        copy.wait()


def trunk_forward(geometry, tasks, batches, index, infos, x, kernel_slots, scales):
    number, height, breadth = geometry
    pixels = height * breadth
    channels = x.shape[1]
    width = channels // tasks
    windows = window_count(height, breadth)
    tall = shape((x.shape[0], width), F32)
    taps = shape((channels, 9 * width), BF)
    outs = [
        shape((8, width), F32), shape((8, width), F32), shape(x.shape, BF),
        taps, taps,
        tall, tall, shape(x.shape, BF),
    ]
    return exchange_kernel(
        functools.partial(trunk_forward_body, geometry, tasks, batches),
        outs,
        "svhvv",
        (index, infos, x, kernel_slots, scales),
        [
            pltpu.VMEM(tall.shape, F32),
            pltpu.VMEM(tall.shape, F32),
            pltpu.VMEM(x.shape, BF),
            pltpu.VMEM(x.shape, BF),
            pltpu.SemaphoreType.DMA,
            pltpu.VMEM(taps.shape, BF),
            pltpu.VMEM(taps.shape, BF),
            pltpu.VMEM(kernel_slots.shape, F32),
            pltpu.VMEM((channels, width), F32),
            pltpu.VMEM((pixels, 9 * width), F32),
            pltpu.VMEM((number * windows, width), BF),
            pltpu.VMEM((number * windows, channels), BF),
            pltpu.VMEM((x.shape[0], width), BF),
        ]
        + [pltpu.SemaphoreType.DMA((number, tasks))] * 4
        + total_scratch(2, batches)
        + [pltpu.SemaphoreType.DMA((5,))],
        1,
        60,
        flops=4 * x.size * taps.shape[1],
        places_out="vvvhhhhh",
    )


def head_body(
    geometry, tasks, batches, summing,
    infos, features, weights, cotangent, scales, counts,
    task_out, upstream, norm_sums, *rest,
):
    grads_out, rest = rest[0], rest[1:]
    (
        grads, pre_one, pre_two, pre_three, hidden, gated, nine, work, lower, out, arrived,
        sends, receives, mine, slots, total_sends, total_receives, loaded,
    ) = rest[:18]
    number, height, breadth = geometry
    channels = features.shape[1]
    width = channels // tasks
    windows = task_out.shape[1]
    task = lax.axis_index("task")
    half = work.shape[2]
    _, col = places(height, breadth)
    widen = pool_choice(height, breadth, windows, False).astype(BF)
    narrow = pool_choice(height, breadth, windows, True).astype(BF)
    count = jnp.broadcast_to(counts[2:3, 0:1], (1, channels))
    cuts = (pl.ds(0, 2 * channels), pl.ds(2 * channels, 9 * channels))
    loads = [
        pltpu.make_async_copy(weights.at[cut, :], grads.at[cut, :], loaded.at[k])
        for k, cut in enumerate(cuts)
    ]
    for copy in loads:
        copy.start()
    first = grads.at[pl.ds(0, channels), :]
    second = grads.at[pl.ds(channels, channels), :]

    def kernel_rows(p):
        return pl.ds((2 + p) * channels, channels)

    def total(k, rows, meanwhile=None):
        return total_rows(
            k, "batch", batches, list(rows), mine, slots, total_sends, total_receives, meanwhile
        )

    if summing:
        near, near_sends, near_receives, summed, saved = rest[18:]
        place, core, chips = pair_place(batches)
        block = near.shape[1]

        def near_copy(chip):
            return remote(
                block_rows(grads, 2 * chip + 1 - core, block), near.at[chip],
                near_sends.at[chip], near_receives.at[chip], 2 * place + 1 - core, "batch",
            )

    def put_stats(pre, rows, value, valid, carry):
        pre[rows, :] = value
        kept = value * valid
        return carry[0] + col_sum(kept), carry[1] + col_sum(kept * value)

    nothing = zero_rows(2, channels)
    scale_one, scale_two, scale_three = (rows_of(scales, 2 * k, 2) for k in range(3))

    loads[0].wait()

    def first_step(i, rows, carry):
        valid = valid_of(infos, i, height, breadth)
        return put_stats(pre_one, rows, dot(features[rows, :], first[...]), valid, carry)

    sums = each_image(geometry, first_step, nothing)
    greet((("task", tasks), ("batch", batches)))
    totals_one = total(0, sums) + [count]

    def second_step(i, rows, carry):
        valid = valid_of(infos, i, height, breadth)
        _, _, scaled = norm_with(pre_one[rows, :], totals_one, scale_one)
        low = (silu(scaled) * valid).astype(BF)
        hidden[rows, :] = low
        return put_stats(pre_two, rows, dot(low, second[...]), valid, carry)

    sums = each_image(geometry, second_step, nothing)
    totals_two = total(1, sums) + [count]

    def third_step(i, rows, carry):
        valid = valid_of(infos, i, height, breadth)
        _, _, scaled = norm_with(pre_two[rows, :], totals_two, scale_two)
        low = (jax.nn.sigmoid(scaled) * features[rows, :].astype(F32)).astype(BF)
        gated[rows, :] = low
        parts = []
        for j in range(channels // half):
            cut = slice(j * half, (j + 1) * half)
            for p in range(9):
                work[p] = dot(low, grads[kernel_rows(p), cut])
            parts.append(gather_taps(lambda p: work[p], breadth, col))
        return put_stats(pre_three, rows, jnp.concatenate(parts, axis=1), valid, carry)

    loads[1].wait()
    sums = each_image(geometry, third_step, nothing)
    totals_three = total(2, sums) + [count]

    def out_step(i, rows, carry):
        valid = valid_of(infos, i, height, breadth)
        normal, _, scaled = norm_with(pre_three[rows, :], totals_three, scale_three)
        high, low = split(silu(scaled) * valid)
        mean = (dot(narrow, high) + dot(narrow, low)) * 0.25
        task_out[i] = mean.astype(BF)
        dy = silu_back(scaled) * dot(widen, cotangent[i]) * 0.25 * valid
        lower[rows, :] = dy
        return carry[0] + col_sum(dy), carry[1] + col_sum(dy * normal)

    sums = each_image(geometry, out_step, nothing)
    sums_three = total(3, sums)

    def third_back(i, rows, carry):
        valid = valid_of(infos, i, height, breadth)
        normal, inverse, _ = norm_with(pre_three[rows, :], totals_three, scale_three)
        dz = norm_back_with(lower[rows, :], normal, inverse, count, sums_three, scale_three, valid)
        for p, moved in enumerate(spread_taps(dz, breadth, col)):
            nine[p, rows, :] = moved.astype(BF)
        flow = None
        for p in range(9):
            piece = dot_nt(nine[p, rows, :], grads[kernel_rows(p), :])
            flow = piece if flow is None else flow + piece
        lower[rows, :] = flow
        normal, _, scaled = norm_with(pre_two[rows, :], totals_two, scale_two)
        gate = jax.nn.sigmoid(scaled)
        dy = flow * features[rows, :].astype(F32) * gate * (1.0 - gate) * valid
        pre_three[rows, :] = dy
        return carry[0] + col_sum(dy), carry[1] + col_sum(dy * normal)

    sums = each_image(geometry, third_back, nothing)

    def taps(begin, end):
        def tap(p, carry):
            rows = pl.ds(pl.multiple_of((2 + p) * channels, channels), channels)
            grads[rows, :] = dot_tn(gated[...], nine[p]).astype(BF)
            return carry

        lax.fori_loop(begin, end, tap, 0)

    sums_two = total(4, sums, lambda: taps(0, 3))

    def second_back(i, rows, carry):
        valid = valid_of(infos, i, height, breadth)
        normal, inverse, scaled = norm_with(pre_two[rows, :], totals_two, scale_two)
        dz = norm_back_with(
            pre_three[rows, :], normal, inverse, count, sums_two, scale_two, valid
        ).astype(BF)
        out[rows, :] = dz
        lower[rows, :] = lower[rows, :] * jax.nn.sigmoid(scaled)
        normal, _, scaled = norm_with(pre_one[rows, :], totals_one, scale_one)
        dy = silu_back(scaled) * dot_nt(dz, second[...]) * valid
        pre_three[rows, :] = dy
        return carry[0] + col_sum(dy), carry[1] + col_sum(dy * normal)

    sums = each_image(geometry, second_back, nothing)

    def weight_rows():
        grads[pl.ds(channels, channels), :] = dot_tn(hidden[...], out[...]).astype(BF)
        taps(3, 5)

    sums_one = total(5, sums, weight_rows)

    def flow_copy(i, rows, step, incoming=False):
        peer = lax.rem(task + (tasks - step if incoming else step), tasks)
        return remote(
            out.at[rows, columns_of(peer, width)], arrived.at[step - 1, rows, :],
            sends.at[i, step], receives.at[i, step], peer, "task",
        )

    def first_back(i, rows, carry):
        valid = valid_of(infos, i, height, breadth)
        normal, inverse, _ = norm_with(pre_one[rows, :], totals_one, scale_one)
        dz = norm_back_with(
            pre_three[rows, :], normal, inverse, count, sums_one, scale_one, valid
        ).astype(BF)
        hidden[rows, :] = dz
        flow = (lower[rows, :] + dot_nt(dz, first[...])) * valid
        out[rows, :] = flow.astype(BF)
        for step in range(1, tasks):
            flow_copy(i, rows, step).start()
        return carry

    each_image(geometry, first_back, 0)
    taps(5, 9)
    if summing:
        for chip in range(1, chips):
            near_copy(chip).start()
    grads[pl.ds(0, channels), :] = dot_tn(features[...], hidden[...]).astype(BF)
    if summing:
        near_copy(0).start()
        for chip in (*range(1, chips), 0):
            near_copy(chip).wait_recv()
            own = block_rows(grads, 2 * chip + core, block)[...].astype(F32)
            summed[chip] = (own + near[chip].astype(F32)).astype(BF)
            pltpu.make_async_copy(summed.at[chip], grads_out.at[chip], saved.at[chip]).start()
    else:
        grads_out[...] = grads[...]
    put_sums(norm_sums, sums_one + sums_two + sums_three)

    def settle(i, rows, carry):
        for step in range(1, tasks):
            flow_copy(i, rows, step, True).wait_recv()
        flow = out[rows, columns_of(task, width)].astype(F32)
        for step in range(1, tasks):
            flow = flow + arrived[step - 1, rows, :].astype(F32)
        upstream[rows, :] = flow
        for step in range(1, tasks):
            flow_copy(i, rows, step).wait_send()
        return carry

    each_image(geometry, settle, 0)
    if summing:
        for chip in range(chips):
            near_copy(chip).wait_send()
            pltpu.make_async_copy(summed.at[chip], grads_out.at[chip], saved.at[chip]).wait()


def head(geometry, tasks, batches, infos, features, weights, cotangent, scales, counts):
    number, height, breadth = geometry
    pixels = height * breadth
    total, channels = features.shape
    width = channels // tasks
    block = weights.shape[0] // batches
    chips = batches // 2
    summing = block % 16 == 0
    outs = [
        shape((number, pixels // 4, channels), BF),
        shape((total, width), F32),
        shape((8, channels), F32),
        shape((chips, block, channels) if summing else weights.shape, BF),
    ]
    scratch = []
    if summing:
        scratch = [pltpu.VMEM((chips, block, channels), BF)]
        scratch += [pltpu.SemaphoreType.DMA((chips,))] * 2
        scratch += [pltpu.VMEM((chips, block, channels), BF), pltpu.SemaphoreType.DMA((chips,))]
    pooled, upstream, sums, grads = exchange_kernel(
        functools.partial(head_body, geometry, tasks, batches, summing),
        outs,
        "vvhvvv",
        (infos, features, weights, cotangent, scales, counts),
        [
            pltpu.VMEM(weights.shape, BF),
            pltpu.VMEM(features.shape, F32),
            pltpu.VMEM(features.shape, F32),
            pltpu.VMEM(features.shape, F32),
            pltpu.VMEM(features.shape, BF),
            pltpu.VMEM(features.shape, BF),
            pltpu.VMEM((9,) + features.shape, BF),
            pltpu.VMEM((9, pixels, min(channels, 256)), F32),
            pltpu.VMEM(features.shape, F32),
            pltpu.VMEM(features.shape, BF),
            pltpu.VMEM((tasks - 1, total, width), BF),
        ]
        + [pltpu.SemaphoreType.DMA((number, tasks))] * 2
        + total_scratch(6, batches)
        + [pltpu.SemaphoreType.DMA((2,))]
        + scratch,
        2,
        61,
        flops=6 * total * channels * weights.shape[0],
        places_out="vvvh" if summing else "vvvv",
    )
    if summing:
        owned = lax.psum_scatter(
            grads.reshape(chips * block, channels), "batch", scatter_dimension=0,
            axis_index_groups=[list(range(core, batches, 2)) for core in range(2)], tiled=True,
        )
    else:
        owned = lax.psum_scatter(grads, "batch", scatter_dimension=0, tiled=True)
    return pooled, upstream, sums, owned


def trunk_backward_body(
    geometry, tasks, batches,
    infos, upstream, enc_totals, dec_totals, scales, *rest,
):
    kept, rest = rest[:6], rest[6:]
    outs, norm_sums, rest = rest[:3], rest[3], rest[4:]
    (x, enc_taps, dec_taps, enc_pre, dec_pre, spread), rest = rest[:6], rest[6:]
    (
        nine, change, packed, arrived, pooled, sends, receives,
        mine, slots, total_sends, total_receives, loaded,
        enc_grad, dec_grad, flow_out, saved,
    ) = rest
    saves = [
        pltpu.make_async_copy(a, b, saved.at[k])
        for k, (a, b) in enumerate(zip((enc_grad, dec_grad, flow_out), outs))
    ]
    targets = (x, enc_taps, dec_taps, enc_pre, dec_pre, spread)
    loads = [pltpu.make_async_copy(a, b, loaded.at[k]) for k, (a, b) in enumerate(zip(kept, targets))]
    for k in (4, 2, 5, 3, 1, 0):
        loads[k].start()
    number, height, breadth = geometry
    channels = x.shape[1]
    width = enc_pre.shape[1]
    windows = window_count(height, breadth)
    task = lax.axis_index("task")
    _, col = places(height, breadth)
    widen = pool_choice(height, breadth, windows, False).astype(BF)
    narrow = pool_choice(height, breadth, windows, True)
    nothing = zero_rows(2, width)

    def total(k, rows):
        return total_rows(
            k, "batch", batches, list(rows), mine, slots, total_sends, total_receives
        )

    def change_of(pre, totals, scale, flow):
        def image(i, rows, carry):
            valid = valid_of(infos, i, height, breadth)
            normal, _, scaled = norm_with(pre[rows, :], totals, scale)
            dy = silu_back(scaled) * flow(i, rows) * valid
            change[rows, :] = dy
            return carry[0] + col_sum(dy), carry[1] + col_sum(dy * normal)

        return each_image(geometry, image, nothing)

    def back(pre, totals, scale, sums, taps, put):
        def image(i, rows, carry):
            valid = valid_of(infos, i, height, breadth)
            normal, inverse, _ = norm_with(pre[rows, :], totals, scale)
            dz = norm_back_with(change[rows, :], normal, inverse, totals[2], sums, scale, valid)
            for p, moved in enumerate(spread_taps(dz, breadth, col)):
                nine[rows, p * width : (p + 1) * width] = moved.astype(BF)
            put(i, rows, dot_nt(nine[rows, :], taps[...]) * valid)
            return carry

        each_image(geometry, image, 0)

    totals = rows_of(dec_totals, 0, 3)
    scale = rows_of(scales, 2, 2)
    loads[4].wait()
    sums = change_of(dec_pre, totals, scale, lambda i, rows: upstream[rows, :])
    greet((("task", tasks), ("batch", batches)))
    dec_sums = total(0, sums)

    def copy_of(i, step, incoming=False):
        rows = window_rows(i, windows)
        peer = lax.rem(task + (tasks - step if incoming else step), tasks)
        return remote(
            packed.at[rows, columns_of(peer, width)], arrived.at[step - 1, rows, :],
            sends.at[i, step], receives.at[i, step], peer, "task",
        )

    def put_packed(i, rows, flow):
        chosen = chosen_cells(narrow, infos, i)
        packed[window_rows(i, windows), :] = dot(chosen, flow.astype(BF)).astype(BF)
        for step in range(1, tasks):
            copy_of(i, step).start()

    loads[2].wait()
    back(dec_pre, totals, scale, dec_sums, dec_taps, put_packed)
    loads[5].wait()
    dec_grad[...] = dot_tn(spread[...], nine[...])
    saves[1].start()

    def collect(i, carry):
        for step in range(1, tasks):
            copy_of(i, step, True).wait_recv()
        rows = window_rows(i, windows)
        flow = packed[rows, columns_of(task, width)].astype(F32)
        for step in range(1, tasks):
            flow = flow + arrived[step - 1, rows, :].astype(F32)
        pooled[rows, :] = flow
        for step in range(1, tasks):
            copy_of(i, step).wait_send()
        return carry

    lax.fori_loop(0, number, collect, 0)

    def widened(i, rows):
        high, low = split(pooled[window_rows(i, windows), :])
        return (dot(widen, high) + dot(widen, low)) * 0.25

    totals = rows_of(enc_totals, 0, 3)
    scale = rows_of(scales, 0, 2)
    loads[3].wait()
    sums = change_of(enc_pre, totals, scale, widened)
    enc_sums = total(1, sums)

    def put_flow(i, rows, flow):
        flow_out[rows, :] = flow.astype(BF)

    loads[1].wait()
    back(enc_pre, totals, scale, enc_sums, enc_taps, put_flow)
    loads[0].wait()
    saves[2].start()
    enc_grad[...] = dot_tn(x[...], nine[...])
    saves[0].start()
    put_sums(norm_sums, enc_sums + dec_sums)
    for copy in saves:
        copy.wait()


def trunk_backward(
    geometry, tasks, batches, infos, upstream, enc_totals, dec_totals, scales, kept
):
    number, height, breadth = geometry
    x, enc_taps, dec_taps = kept[:3]
    total, channels = x.shape
    width = channels // tasks
    windows = window_count(height, breadth)
    outs = [
        shape(enc_taps.shape, F32),
        shape(dec_taps.shape, F32),
        shape(x.shape, BF),
        shape((8, width), F32),
    ]
    return exchange_kernel(
        functools.partial(trunk_backward_body, geometry, tasks, batches),
        outs,
        "vvvvvhhhhhh",
        (infos, upstream, enc_totals, dec_totals, scales, *kept),
        [pltpu.VMEM(a.shape, a.dtype) for a in kept]
        + [
            pltpu.VMEM((total, 9 * width), BF),
            pltpu.VMEM((total, width), F32),
            pltpu.VMEM((number * windows, channels), BF),
            pltpu.VMEM((tasks - 1, number * windows, width), BF),
            pltpu.VMEM((number * windows, width), F32),
        ]
        + [pltpu.SemaphoreType.DMA((number, tasks))] * 2
        + total_scratch(2, batches)
        + [pltpu.SemaphoreType.DMA((6,))]
        + [pltpu.VMEM(a.shape, a.dtype) for a in outs[:3]]
        + [pltpu.SemaphoreType.DMA((3,))],
        3,
        60,
        flops=8 * x.size * enc_taps.shape[1],
        places_out="hhhv",
    )


def to_slots_body(index, enc_far, dec_far, slots, enc, dec, wide, low, load, save):
    count = wide.shape[0]
    channels = enc.shape[0]
    width = wide.shape[1]
    step = 1024
    group = 32
    loads = [
        pltpu.make_async_copy(a, b, load.at[k])
        for k, (a, b) in enumerate(((dec_far, dec), (enc_far, enc)))
    ]
    for copy in loads:
        copy.start()
    for kernel, copy in ((1, loads[0]), (0, loads[1])):
        copy.wait()
        source = dec if kernel else enc
        for q in range(9):

            def place(i, carry):
                base = pl.multiple_of(i * group, group)
                first = (9 * kernel + q) * channels + base
                values = source[pl.ds(base, group), q * width : (q + 1) * width]
                for u in range(group):
                    wide[pl.ds(index[first + u], 1), :] = values[u : u + 1, :]
                return carry

            lax.fori_loop(0, channels // group, place, 0)

    def out(i):
        rows = pl.ds(pl.multiple_of(i * step, step), step)
        return pltpu.make_async_copy(low.at[rows, :], slots.at[rows, :], save.at[i])

    def narrow(i, carry):
        rows = pl.ds(pl.multiple_of(i * step, step), step)
        low[rows, :] = wide[rows, :].astype(BF)
        out(i).start()
        return carry

    def end(i, carry):
        out(i).wait()
        return carry

    lax.fori_loop(0, count // step, narrow, 0)
    lax.fori_loop(0, count // step, end, 0)


def to_slots(index, enc, dec):
    width = enc.shape[1] // 9
    dims = (index.shape[0], width)
    far = pl.BlockSpec(memory_space=pltpu.HBM)
    return pl.pallas_call(
        to_slots_body,
        out_shape=shape(dims, BF),
        in_specs=[SMEM_SPEC, far, far],
        out_specs=far,
        scratch_shapes=[
            pltpu.VMEM(enc.shape, F32),
            pltpu.VMEM(dec.shape, F32),
            pltpu.VMEM(dims, F32),
            pltpu.VMEM(dims, BF),
            pltpu.SemaphoreType.DMA((2,)),
            pltpu.SemaphoreType.DMA((dims[0] // 1024,)),
        ],
        compiler_params=pltpu.CompilerParams(vmem_limit_bytes=60 * MIB),
        cost_estimate=pl.CostEstimate(flops=10000 * MIB, bytes_accessed=8 * MIB, transcendentals=0),
    )(index, enc, dec)


def adam(gradient, moment_one, moment_two):
    new_one = BETA_ONE * moment_one + (1.0 - BETA_ONE) * gradient
    new_two = BETA_TWO * moment_two + (1.0 - BETA_TWO) * gradient * gradient
    direction = (
        new_one / (1.0 - BETA_ONE**STEP) / (jnp.sqrt(new_two / (1.0 - BETA_TWO**STEP)) + ADAM_EPS)
    )
    return new_one, new_two, direction


def pair_place(batches):
    me = lax.axis_index("batch")
    place = lax.div(me, 2)
    return place, me - 2 * place, batches // 2


def greet_pairs(tasks, batches):
    place, core, chips = pair_place(batches)
    task = lax.axis_index("task")
    barrier = pltpu.get_barrier_semaphore()

    def signal(device):
        pl.semaphore_signal(barrier, inc=1, device_id=device, device_id_type=MESH)

    for step in range(1, tasks):
        signal({"task": lax.rem(task + step, tasks)})
    signal({"batch": 2 * place + 1 - core})
    for step in range(1, chips):
        signal({"batch": 2 * lax.rem(place + step, chips) + core})
    pl.semaphore_wait(barrier, tasks - 1 + chips)


def block_rows(ref, index, count):
    return ref.at[pl.ds(pl.multiple_of(index * count, 8), count), :]


SMALL = 128 * 128


def far_first(chips):
    return sorted(range(chips), key=lambda step: -min(step, chips - step))


def pair_sum(batches, rows_of_block, own_block, near, paired, far, sems):
    place, core, chips = pair_place(batches)
    count = near.shape[1]
    near_send, near_receive, far_send, far_receive = sems
    other = 2 * place + 1 - core
    ring = chips == 4 and count % 32 == 0 and near.shape[2] * count > SMALL
    half = count // 2
    halves = (pl.ds(0, half), pl.ds(half, half))

    def near_copy(step):
        chip = lax.rem(place + step, chips)
        return remote(rows_of_block(2 * chip + 1 - core), near.at[step],
                      near_send.at[step], near_receive.at[step], other, "batch")

    def far_copy(step, incoming=False):
        chip = lax.rem(place + (chips - step if incoming else step), chips)
        return remote(paired.at[step], far.at[step], far_send.at[step], far_receive.at[step],
                      2 * chip + core, "batch")

    def ring_copy(which, way):
        chip = lax.rem(place + (1 if way == 0 else chips - 1), chips)
        if which == 0:
            source, target = paired.at[2, halves[way], :], far.at[2 + way, halves[0], :]
        else:
            cut = halves[way] if which == 2 else halves[1 - way]
            source, target = paired.at[1 if way == 0 else 3, cut, :], far.at[way, cut, :]
        k = 2 * which + way
        return remote(source, target, far_send.at[k], far_receive.at[k], 2 * chip + core, "batch")

    def start():
        for step in far_first(chips):
            near_copy(step).start()

    def middle():
        for step in far_first(chips):
            near_copy(step).wait_recv()
            if step:
                paired[step] = (own_block(step) + near[step].astype(F32)).astype(paired.dtype)
                if not ring:
                    far_copy(step).start()
                elif step == 2:
                    ring_copy(0, 0).start()
                    ring_copy(0, 1).start()
                else:
                    ring_copy(1, 0 if step == 1 else 1).start()

    def relay():
        if not ring:
            return
        for way in range(2):
            ring_copy(0, way).wait_recv()
            step = 1 if way == 0 else 3
            total = paired[step, halves[way], :].astype(F32) + far[2 + way, halves[0], :].astype(F32)
            paired[step, halves[way], :] = total.astype(paired.dtype)
            ring_copy(2, way).start()

    def end():
        total = own_block(0) + near[0].astype(F32)
        if ring:
            for way in range(2):
                ring_copy(1, way).wait_recv()
                ring_copy(2, way).wait_recv()
                total = total + far[way].astype(F32)
            for k in range(3):
                for way in range(2):
                    ring_copy(k, way).wait_send()
        else:
            for step in range(1, chips):
                far_copy(step, True).wait_recv()
                total = total + far[step].astype(F32)
            for step in range(1, chips):
                far_copy(step).wait_send()
        for step in range(chips):
            near_copy(step).wait_send()
        return total

    return start, middle, relay, end


def blocks_in(source, batches, count, piece=0, pieces=1):
    place, core, chips = pair_place(batches)

    def rows(index):
        start = (index * pieces + piece) * count
        return source.at[pl.ds(pl.multiple_of(start, 8), count), :]

    def own(step):
        chip = lax.rem(place + step, chips)
        return rows(2 * chip + core)[...].astype(F32)

    return rows, own


def pair_scratch(batches, rows, width, kind):
    chips = batches // 2
    return [pltpu.VMEM((chips, rows // batches, width), kind)] * 3 + [
        pltpu.SemaphoreType.DMA((max(chips, 6),))
    ] * 4


def chip_spread(batches, block, sends, receives):
    place, core, chips = pair_place(batches)
    count, width = block(place).shape
    ring = chips == 4 and count % 32 == 0 and width * count > SMALL
    half = count // 2

    def copy(step, incoming=False):
        peer = lax.rem(place + (chips - step if incoming else step), chips)
        ref = block(peer if incoming else place)
        return remote(ref, ref, sends.at[step], receives.at[step], 2 * peer + core, "batch")

    def pass_on(way, incoming=False):
        step = 1 if way == 0 else chips - 1
        peer = lax.rem(place + (chips - step if incoming else step), chips)
        home = lax.rem(place + (2 if incoming else chips - step), chips)
        ref = block(home).at[pl.ds(way * half, half), :]
        k = 2 if way == 0 else 0
        return remote(ref, ref, sends.at[k], receives.at[k], 2 * peer + core, "batch")

    steps = (1, chips - 1) if ring else tuple(range(1, chips))

    def start():
        for step in steps:
            copy(step).start()

    def relay():
        if ring:
            for way, step in enumerate(steps):
                copy(step, True).wait_recv()
                pass_on(way).start()

    def settle():
        if ring:
            for way in range(2):
                pass_on(way, True).wait_recv()
        else:
            for step in steps:
                copy(step, True).wait_recv()

    def drain():
        for step in steps:
            copy(step).wait_send()
        if ring:
            for way in range(2):
                pass_on(way).wait_send()

    return start, relay, settle, drain


def arrive_body(
    tasks, batches, geometry,
    image_raw, info, index, weight, head_weight,
    slots, x, infos, owners, head_low,
    image, head_raw, head_loaded, raw, raw_loaded, x_send, x_receive, info_send, info_receive,
    chip_send, chip_receive, pair_send, pair_receive, own,
):
    task = lax.axis_index("task")
    place, core, chips = pair_place(batches)
    count, width = raw.shape
    load = pltpu.make_async_copy(weight.at[:, columns_of(task, width)], raw, raw_loaded)
    load.start()
    head_load = pltpu.make_async_copy(head_weight, head_raw, head_loaded)
    head_load.start()
    number, height, breadth = geometry
    pixels = height * breadth
    for n in range(number):
        valid = valid_rows(info[8 * n + 1 : 8 * n + 2, 0:1], height, breadth)
        rows = slice(n * pixels, (n + 1) * pixels)
        image[rows, :] = (image_raw[rows, :].astype(F32) * valid).astype(BF)
    greet_pairs(tasks, batches)

    def task_copy(source, target, sends, receives, step, incoming=False):
        peer = lax.rem(task + (tasks - step if incoming else step), tasks)
        home = peer if incoming else task
        return remote(source, block_rows(target, home, source.shape[0]), sends.at[step],
                      receives.at[step], peer, "task")

    def moves(step, incoming=False):
        return (
            task_copy(info, infos, info_send, info_receive, step, incoming),
            task_copy(image, x, x_send, x_receive, step, incoming),
        )

    def block(chip):
        return block_rows(slots, 2 * chip + core, count)

    def pair_copy(hop, incoming=False):
        chip = lax.rem(place + chips - hop, chips)
        ref = block_rows(slots, 2 * chip + (1 - core if incoming else core), count)
        return remote(ref, ref, pair_send.at[hop], pair_receive.at[hop], 2 * place + 1 - core, "batch")

    start, relay, settle, drain = chip_spread(batches, block, chip_send, chip_receive)
    ring = chips == 4 and count % 32 == 0 and width * count > SMALL
    load.wait()
    block(place)[...] = raw[...].astype(BF)
    start()
    pair_copy(0).start()
    for step in range(1, tasks):
        for copy in moves(step):
            copy.start()
    locals_ = [
        pltpu.make_async_copy(image, block_rows(x, task, image.shape[0]), own.at[0]),
        pltpu.make_async_copy(info, block_rows(infos, task, info.shape[0]), own.at[1]),
    ]
    for copy in locals_:
        copy.start()
    mine = lax.broadcasted_iota(jnp.int32, (count, 1), 0) + lax.axis_index("batch") * count
    found = jnp.zeros((count, 128), F32)
    for k in range(index.shape[0] // 2, index.shape[0]):
        found = jnp.where(index[k : k + 1, :] == mine, 1.0, found)
    found = jnp.max(found, axis=1, keepdims=True)
    owners[:, 0:1] = 1.0 - found
    owners[:, 1:2] = found
    head_load.wait()
    head_low[...] = head_raw[...].astype(BF)
    relay()
    if ring:
        pair_copy(1).start()
        pair_copy(3).start()
        settle()
        pair_copy(2).start()
    else:
        settle()
        for hop in range(1, chips):
            pair_copy(hop).start()
    for copy in locals_:
        copy.wait()
    for step in range(1, tasks):
        for copy in moves(step, True):
            copy.wait_recv()
    for hop in range(chips):
        pair_copy(hop, True).wait_recv()
    for step in range(1, tasks):
        for copy in moves(step):
            copy.wait_send()
    for hop in range(chips):
        pair_copy(hop).wait_send()
    drain()


def arrive(tasks, batches, geometry, image, info, index, weight, head_weight):
    count, channels = weight.shape
    width = channels // tasks
    chips = batches // 2
    return exchange_kernel(
        functools.partial(arrive_body, tasks, batches, geometry),
        [
            shape((count * batches, width), BF),
            shape((image.shape[0] * tasks, channels), BF),
            shape((info.shape[0] * tasks, info.shape[1]), F32),
            shape((count, 2), F32),
            shape(head_weight.shape, BF),
        ],
        "vvvhh",
        (image, info, index.reshape(-1, 128), weight, head_weight),
        [
            pltpu.VMEM(image.shape, BF),
            pltpu.VMEM(head_weight.shape, F32),
            pltpu.SemaphoreType.DMA,
            pltpu.VMEM((count, width), F32),
            pltpu.SemaphoreType.DMA,
        ]
        + [pltpu.SemaphoreType.DMA((tasks,))] * 4
        + [pltpu.SemaphoreType.DMA((max(chips, 4),))] * 4
        + [pltpu.SemaphoreType.DMA((2,))],
        4,
        60,
        flops=20000 * MIB,
    )


def soap_rows(cuts, grad, owners, state, low, first, begin=0, end=None):
    total = grad.shape[0]

    def chunk(i, carry):
        rows = pl.ds(pl.multiple_of(i * (total // cuts), 8), total // cuts)
        values = grad[rows, :].astype(F32)
        marks = owners(i * (total // cuts), total // cuts)
        count = len(marks)
        rotated = None
        for m in range(count):
            part = dot((values * marks[m]).astype(BF), low[first + m])
            rotated = part if rotated is None else rotated + part
        new_one, new_two, direction = adam(rotated, state[1, rows, :], state[2, rows, :])
        state[1, rows, :] = new_one
        state[2, rows, :] = new_two
        stepped = None
        for m in range(count):
            part = dot_nt((direction * marks[m]).astype(BF), low[first + m])
            stepped = part if stepped is None else stepped + part
        old = state[0, rows, :]
        state[0, rows, :] = old - LEARN_MATRIX * (stepped + DECAY_MATRIX * old)
        return carry

    lax.fori_loop(begin, cuts if end is None else end, chunk, 0)


def factor_rows(values, identity, turn):
    size, width = values.shape
    sub = lax.broadcasted_iota(jnp.int32, (size, width), 0)
    rolled = pltpu.roll(values, turn, 1)
    columns = [jnp.broadcast_to(rolled[:, j : j + 1], (size, width)) for j in range(size)]
    scale = jnp.zeros((size, width), F32)
    for j in range(size):
        root = lax.rsqrt(columns[j][j : j + 1, :])
        scale = jnp.where(sub == j, root, scale)
        lower = jnp.where(sub > j, columns[j] * root, 0.0)
        values = values - lower * (values[j : j + 1, :] * root)
        identity = identity - lower * (identity[j : j + 1, :] * root)
        for i in range(j + 1, size):
            columns[i] = columns[i] - lower * (columns[i][j : j + 1, :] * root)
    return values * scale, identity * scale


GROUP = 16
PANEL = 128


def upper_blocks(size):
    return [(a, b) for a in range(0, size, PANEL) for b in range(a, size, PANEL)]


def renew_panel(k, product, made, tables, inverses):
    count, size = product.shape[0], product.shape[1]
    here = slice(k * PANEL, (k + 1) * PANEL)
    row = lax.broadcasted_iota(jnp.int32, (PANEL, PANEL), 0)
    col = lax.broadcasted_iota(jnp.int32, (PANEL, PANEL), 1)
    unit = jnp.where(row == col, 1.0, 0.0).astype(F32)
    for n in range(count):
        tables[n][:, :PANEL] = dot3(dot_tn, product[n, :, here], product[n, :, here])
        tables[n][:, PANEL:] = unit

    def group(q, carry):
        rows = pl.ds(pl.multiple_of(q * GROUP, GROUP), GROUP)
        turn = lax.rem(PANEL - q * GROUP, PANEL)
        done = [
            factor_rows(tables[n][rows, :PANEL], tables[n][rows, PANEL:], turn)
            for n in range(count)
        ]
        for n in range(count):
            upper, inverse = done[n]
            inverses[n][rows, :] = inverse
            both = jnp.concatenate([upper, inverse], axis=1)
            tables[n][...] = tables[n][...] - dot3(dot_tn, upper, both)
        return carry

    lax.fori_loop(0, PANEL // GROUP, group, 0)
    for n in range(count):
        turned = dot3(dot_nt, product[n, :, here], inverses[n][...])
        made[n, :, here] = turned
        if k < size // PANEL - 1:
            rest = slice((k + 1) * PANEL, size)
            product[n, :, rest] = product[n, :, rest] - dot3(
                dot, turned, dot3(dot_tn, turned, product[n, :, rest])
            )


def tail_body(
    tasks, batches, cuts, pieces,
    slots, flow, sums, owners, head_far,
    weight, one, two, head_weight, head_one, head_two, basis, head_basis,
    input_grad, norm_sums, state_new, head_state_new, grams, head_grams,
    grad, part, state, head_state, mine, head_mine, bases, low, head_grad, flow_own,
    flow_in, flow_send, flow_receive, send, receive, sum_send, sum_receive,
    *rest,
):
    row_scratch = [rest[7 * k : 7 * k + 7] for k in range(pieces)]
    gram_scratch, head_scratch, rest = rest[7 * pieces :][:7], rest[7 * pieces + 7 :][:7], rest[7 * pieces + 14 :]
    chip_send, chip_receive, task_send, task_receive, pair_send, pair_receive, load, save = rest
    task = lax.axis_index("task")
    place, core, chips = pair_place(batches)
    width = part.shape[1]
    channels = grad.shape[1]
    pixels = input_grad.shape[0]
    trunk_total = basis.shape[0]
    head_total = head_basis.shape[0]
    count, head_count = mine.shape[0] // batches, head_mine.shape[0] // batches

    def trunk_marks(start, size):
        rows = pl.ds(pl.multiple_of(start, 8), size)
        return [owners[rows, m : m + 1] for m in range(trunk_total)]

    def head_marks(start, size):
        index = lax.broadcasted_iota(jnp.int32, (size, 1), 0) + start
        index = index + lax.axis_index("batch") * head_grad.shape[0]
        owner = jnp.minimum(lax.div(index, channels), head_total - 1)
        return [jnp.where(owner == m, 1.0, 0.0).astype(F32) for m in range(head_total)]

    def put_grams(target, rows, columns, marks):
        for m, mark in enumerate(marks):
            held = (rows[...].astype(F32) * mark).astype(BF)
            target[m * channels : (m + 1) * channels, :] = dot_tn(held, columns[...]).astype(
                target.dtype
            )

    def put_packed_grams(target, rows, marks):
        n = 0
        for mark in marks:
            held = (rows[...].astype(F32) * mark).astype(BF)
            for a, b in upper_blocks(channels):
                block = dot_tn(held[:, a : a + PANEL], rows[:, b : b + PANEL])
                target[n : n + PANEL, :] = block.astype(target.dtype)
                n += PANEL
        if n < target.shape[0]:
            target[n:, :] = jnp.zeros((target.shape[0] - n, PANEL), target.dtype)

    def peer_of(step, incoming):
        return lax.rem(task + (tasks - step if incoming else step), tasks)

    def flow_copy(step, incoming=False):
        peer = peer_of(step, incoming)
        return remote(block_rows(flow, peer, pixels), flow_in.at[step - 1], flow_send.at[step],
                      flow_receive.at[step], peer, "task")

    def sum_copy(step, incoming=False):
        peer = peer_of(step, incoming)
        home = peer if incoming else task
        return remote(sums, norm_sums.at[:, columns_of(home, width)], sum_send.at[step],
                      sum_receive.at[step], peer, "task")

    def part_copy(k, step, incoming=False):
        peer = peer_of(step, incoming)
        home = peer if incoming else task
        return remote(part.at[part_rows(k), :], grad.at[part_rows(k), columns_of(home, width)],
                      send.at[k, step], receive.at[k, step], peer, "task")

    def trunk_block(chip, home, which):
        rows = pl.ds(pl.multiple_of((2 * chip + which) * count, 8), count)
        return grams.at[rows, columns_of(home, width)]

    def head_block(chip, which):
        return block_rows(head_grams, 2 * chip + which, head_count)

    def task_copy(step, hop, incoming=False):
        peer = peer_of(step, incoming)
        chip = lax.rem(place + chips - hop, chips)
        block = trunk_block(chip, peer if incoming else task, core)
        return remote(block, block, task_send.at[step, hop], task_receive.at[step, hop], peer, "task")

    def pair_copy(kind, hop, incoming=False):
        chip = lax.rem(place + chips - hop, chips)
        which = 1 - core if incoming else core
        home = lax.rem(task + tasks - kind, tasks)
        block = head_block(chip, which) if kind == tasks else trunk_block(chip, home, which)
        return remote(block, block, pair_send.at[kind, hop], pair_receive.at[kind, hop],
                      2 * place + 1 - core, "batch")

    def sum_of(source, scratch, piece=0, total=1):
        near, paired, far, *sems = scratch
        return pair_sum(
            batches, *blocks_in(source, batches, near.shape[1], piece, total), near, paired, far, sems
        )

    def part_rows(k):
        size = part.shape[0] // pieces
        return pl.ds(k * size, size)

    moves = [
        (basis, bases.at[pl.ds(0, trunk_total)]),
        (head_basis, bases.at[pl.ds(trunk_total, head_total)]),
        (head_weight, head_state.at[0]),
        (head_one, head_state.at[1]),
        (head_two, head_state.at[2]),
        (weight, state.at[0]),
        (one, state.at[1]),
        (two, state.at[2]),
        (head_far, head_grad),
        (block_rows(flow, task, pixels), flow_own),
    ]
    loads = [pltpu.make_async_copy(a, b, load.at[k]) for k, (a, b) in enumerate(moves)]
    loads[8].start()
    for copy in (*loads[:8], loads[9]):
        copy.start()
    saves = [
        pltpu.make_async_copy(state, state_new, save.at[0]),
        pltpu.make_async_copy(head_state, head_state_new, save.at[1]),
    ]

    greet_pairs(tasks, batches)
    row_sums = [sum_of(slots, row_scratch[k], k, pieces) for k in range(pieces)]
    for stages in row_sums:
        stages[0]()
    for step in range(1, tasks):
        sum_copy(step).start()
        flow_copy(step).start()
    norm_sums[:, columns_of(task, width)] = sums[...]
    row_sums[0][1]()
    loads[8].wait()
    put_packed_grams(head_mine, head_grad, head_marks(0, head_grad.shape[0]))
    head_start, head_middle, head_relay, head_end = sum_of(head_mine, head_scratch)
    row_sums[0][2]()
    for stages in row_sums[1:]:
        stages[1]()
    head_start()
    for stages in row_sums[1:]:
        stages[2]()
    head_middle()
    for copy in loads[:5]:
        copy.wait()
    for m in range(trunk_total + head_total):
        low[m] = bases[m].astype(BF)
    for k, stages in enumerate(row_sums):
        total = stages[3]().astype(BF)
        part[part_rows(k), :] = total
        for step in range(1, tasks):
            part_copy(k, step).start()
        grad[part_rows(k), columns_of(task, width)] = total
    head_relay()

    soap_rows(cuts, head_grad, head_marks, head_state, low, trunk_total)
    saves[1].start()
    loads[9].wait()
    total = flow_own[...].astype(F32)
    for step in range(1, tasks):
        flow_copy(step, True).wait_recv()
        total = total + flow_in[step - 1].astype(F32)
    input_grad[...] = total
    head_block(place, core)[...] = head_end().astype(head_grams.dtype)
    trunk_spread = chip_spread(
        batches, lambda chip: trunk_block(chip, task, core), chip_send.at[0], chip_receive.at[0]
    )
    head_spread = chip_spread(
        batches, lambda chip: head_block(chip, core), chip_send.at[1], chip_receive.at[1]
    )
    head_spread[0]()
    pair_copy(tasks, 0).start()
    for k in range(pieces):
        for step in range(1, tasks):
            part_copy(k, step, True).wait_recv()

    put_grams(mine, grad, part, trunk_marks(0, grad.shape[0]))
    start, middle, relay, end = sum_of(mine, gram_scratch)
    start()
    middle()
    head_spread[1]()
    for copy in loads[5:8]:
        copy.wait()
    relay()
    soap_rows(cuts, grad, trunk_marks, state, low, 0, 0, cuts // 2)
    trunk_block(place, task, core)[...] = end().astype(grams.dtype)
    trunk_spread[0]()
    for step in range(1, tasks):
        task_copy(step, 0).start()
    pair_copy(0, 0).start()
    soap_rows(cuts, grad, trunk_marks, state, low, 0, cuts // 2, cuts)
    saves[0].start()
    trunk_spread[1]()
    trunk_spread[2]()
    for hop in range(1, chips):
        for step in range(1, tasks):
            task_copy(step, hop).start()
        pair_copy(0, hop).start()
    head_spread[2]()
    for hop in range(1, chips):
        pair_copy(tasks, hop).start()
    for hop in range(chips):
        for step in range(1, tasks):
            task_copy(step, hop, True).wait_recv()
            pair_copy(step, hop).start()
    for hop in range(chips):
        for kind in range(tasks + 1):
            pair_copy(kind, hop, True).wait_recv()
    for step in range(1, tasks):
        sum_copy(step, True).wait_recv()

    for copy in saves:
        copy.wait()
    for step in range(1, tasks):
        sum_copy(step).wait_send()
        for k in range(pieces):
            part_copy(k, step).wait_send()
        flow_copy(step).wait_send()
    for hop in range(chips):
        for kind in range(tasks + 1):
            pair_copy(kind, hop).wait_send()
        for step in range(1, tasks):
            task_copy(step, hop).wait_send()
    trunk_spread[3]()
    head_spread[3]()


def renew_body(
    core, state, head_state, grams, head_grams, stat, head_stat, basis, head_basis,
    weight_new, one_new, two_new, head_weight_new, head_one_new, head_two_new,
    stat_new, head_stat_new, low_made,
    stats, product, made, low_grams, low_head_grams, held, head_held, load, save, *work,
):
    trunk_total, head_total = stat.shape[0], head_stat.shape[0]
    channels = stat.shape[1]
    count = trunk_total + head_total
    shared = product.shape[0]
    tables, inverses = work[:shared], work[shared:]
    loads = []
    blocks = upper_blocks(channels)
    packed = len(blocks) * PANEL

    def gram_rows(m, start):
        if m < trunk_total:
            first = m * channels + start
            return low_grams[first : first + PANEL, :].astype(F32)
        parts = []
        for b in range(0, channels, PANEL):
            n = blocks.index((min(start, b), max(start, b)))
            first = (m - trunk_total) * packed + n * PANEL
            block = low_head_grams[first : first + PANEL, :].astype(F32)
            parts.append(block if b >= start else block.T)
        return jnp.concatenate(parts, axis=1)

    def bring(source, target):
        copy = pltpu.make_async_copy(source, target, load.at[len(loads)])
        loads.append(copy)
        return copy

    for m in range(count):
        first = m < trunk_total
        place = m if first else m - trunk_total
        size = channels if first else packed
        rows = pl.ds(place * size, size)
        here, there = (grams, low_grams) if first else (head_grams, low_head_grams)
        bring(here.at[rows, :], there.at[rows, :]).start()
        bring((stat if first else head_stat).at[place], stats.at[m]).start()

    for n in range(shared):
        both = [
            basis.at[n] if n < trunk_total else head_basis.at[n - trunk_total],
            head_basis.at[n],
        ]
        copy = bring(both[1], made.at[n])
        for which, source in enumerate(both):

            @pl.when(core[0] == which)
            def _():
                pltpu.make_async_copy(source, made.at[n], load.at[2 * count + n]).start()

    bring(state, held).start()
    bring(head_state, head_held).start()
    sources = [held.at[k] for k in range(3)] + [head_held.at[k] for k in range(3)]
    targets = [weight_new, one_new, two_new, head_weight_new, head_one_new, head_two_new]
    saves = [pltpu.make_async_copy(a, b, save.at[k]) for k, (a, b) in enumerate(zip(sources, targets))]
    for m in range(count):
        for copy in loads[2 * m : 2 * m + 2]:
            copy.wait()
        for start in range(0, channels, PANEL):
            rows = slice(start, start + PANEL)
            stats[m, rows, :] = STAT_DECAY * stats[m, rows, :] + (1.0 - STAT_DECAY) * gram_rows(m, start)
    for begin, size, out in ((0, trunk_total, stat_new), (trunk_total, head_total, head_stat_new)):
        copy = pltpu.make_async_copy(stats.at[pl.ds(begin, size)], out, save.at[len(saves)])
        copy.start()
        saves.append(copy)
    for n in range(shared):
        loads[2 * count + n].wait()
        product[n] = dot3(dot, stats[trunk_total * core[0] + n], made[n])
    for k in range(channels // PANEL):
        renew_panel(k, product, made, tables, inverses)
        if k == 0:
            for copy in loads[2 * count + shared :]:
                copy.wait()
            for copy in saves[:6]:
                copy.start()
        cut = slice(k * PANEL, (k + 1) * PANEL)
        low_made[:, :, cut] = made[:, :, cut].astype(BF)
    for copy in saves:
        copy.wait()


def swap_body(batches, x, out, sends, receives):
    place, core, _ = pair_place(batches)
    other = 2 * place + 1 - core
    barrier = pltpu.get_barrier_semaphore()
    pl.semaphore_signal(barrier, inc=1, device_id={"batch": other}, device_id_type=MESH)
    pl.semaphore_wait(barrier, 1)
    copy = remote(x, out, sends, receives, other, "batch")
    copy.start()
    copy.wait()


def finish(tasks, batches, local_grads, rows, matrices):
    slots, flow, sums, owners, head_grad = local_grads
    stat, head_stat, basis, head_basis = matrices
    total, channels = rows[0].shape
    width = channels // tasks
    trunk_total, head_total = basis.shape[0], head_basis.shape[0]
    gram_rows = trunk_total * channels
    packed = len(upper_blocks(channels)) * PANEL
    head_rows = -(-head_total * packed // (16 * batches)) * 16 * batches
    chips = batches // 2
    kind = BF if gram_rows % (16 * batches) == 0 else F32
    cuts = 4 if total % 64 == 0 and head_grad.shape[0] % 64 == 0 else 1
    pieces = 2 if total % 64 == 0 else 1
    square = (trunk_total + head_total, channels, channels)
    pixels = flow.shape[0] // tasks
    input_grad, norm_sums, *made = exchange_kernel(
        functools.partial(tail_body, tasks, batches, cuts, pieces),
        [
            shape((pixels, channels), F32),
            shape((8, channels), F32),
            shape((3, total, channels), F32),
            shape((3,) + head_grad.shape, F32),
            shape((gram_rows, channels), kind),
            shape((head_rows, PANEL), BF),
        ],
        "vhvvhhhhhhhhh",
        (*local_grads, *rows, basis, head_basis),
        [
            pltpu.VMEM((total, channels), BF),
            pltpu.VMEM((total, width), BF),
            pltpu.VMEM((3, total, channels), F32),
            pltpu.VMEM((3,) + head_grad.shape, F32),
            pltpu.VMEM((gram_rows, width), kind),
            pltpu.VMEM((head_rows, PANEL), BF),
            pltpu.VMEM(square, F32),
            pltpu.VMEM(square, BF),
            pltpu.VMEM(head_grad.shape, BF),
            pltpu.VMEM((pixels, channels), BF),
            pltpu.VMEM((tasks - 1, pixels, channels), BF),
        ]
        + [pltpu.SemaphoreType.DMA((tasks,))] * 2
        + [pltpu.SemaphoreType.DMA((pieces, tasks))] * 2
        + [pltpu.SemaphoreType.DMA((tasks,))] * 2
        + pair_scratch(batches, slots.shape[0] // pieces, width, BF) * pieces
        + pair_scratch(batches, gram_rows, width, kind)
        + pair_scratch(batches, head_rows, PANEL, BF)
        + [pltpu.SemaphoreType.DMA((2, max(chips, 4)))] * 2
        + [pltpu.SemaphoreType.DMA((tasks, chips))] * 2
        + [pltpu.SemaphoreType.DMA((tasks + 1, chips))] * 2
        + [pltpu.SemaphoreType.DMA((10,)), pltpu.SemaphoreType.DMA((2,))],
        5,
        60,
        flops=50000 * MIB,
        places_out="vvhhvv",
    )
    outs = [shape(a.shape, F32) for a in (*rows, *matrices)]
    hbm = pl.BlockSpec(memory_space=pltpu.HBM)
    count = trunk_total + head_total
    shared = max(trunk_total, head_total)
    core = lax.rem(lax.axis_index("batch"), 2)
    own = (shared, channels, channels)
    *results, made_low = pl.pallas_call(
        renew_body,
        out_shape=(*outs[:8], shape(own, BF)),
        in_specs=[SMEM_SPEC] + [hbm] * 8,
        out_specs=(*(hbm for _ in outs[:8]), VMEM_SPEC),
        scratch_shapes=[pltpu.VMEM(square, F32)]
        + [pltpu.VMEM(own, F32)] * 2
        + [pltpu.VMEM(made[2].shape, kind), pltpu.VMEM(made[3].shape, BF)]
        + [pltpu.VMEM(made[0].shape, F32), pltpu.VMEM(made[1].shape, F32)]
        + [pltpu.SemaphoreType.DMA((2 * count + shared + 2,))]
        + [pltpu.SemaphoreType.DMA((8,))]
        + [pltpu.VMEM((PANEL, 2 * PANEL), F32)] * shared
        + [pltpu.VMEM((PANEL, PANEL), F32)] * shared,
        compiler_params=pltpu.CompilerParams(vmem_limit_bytes=60 * MIB),
        cost_estimate=pl.CostEstimate(
            flops=50000 * MIB, bytes_accessed=64 * MIB, transcendentals=0
        ),
    )(core.reshape(1), *made, *matrices)
    theirs = exchange_kernel(
        functools.partial(swap_body, batches),
        [shape(own, BF)],
        "v",
        (made_low,),
        [pltpu.SemaphoreType.DMA] * 2,
        6,
        60,
        flops=5000 * MIB,
    )[0]
    results += [
        jnp.where(core == which, made_low[:total], theirs[:total]).astype(F32)
        for which, total in enumerate((trunk_total, head_total))
    ]
    return input_grad, norm_sums, results


def local(
    tasks,
    batches,
    images,
    image_small,
    pool_index,
    row_slot,
    trunk_weight,
    trunk_mean_grad,
    trunk_mean_square,
    trunk_statistic,
    trunk_basis,
    head_weight,
    head_mean_grad,
    head_mean_square,
    head_statistic,
    head_basis,
    trunk_gain,
    trunk_offset,
    trunk_norm_mean_grad,
    trunk_norm_mean_square,
    head_gain,
    head_offset,
    head_norm_mean_grad,
    head_norm_mean_square,
    cotangent,
):
    number, height, breadth, channels = images.shape
    pixels = height * breadth
    shown = tasks * number
    geometry = (shown, height, breadth)
    task = lax.axis_index("task")
    width = channels // tasks

    def quarter(values):
        return lax.dynamic_slice_in_dim(values, task * width, width, values.ndim - 1)

    def inside(flags):
        row_limit = jnp.where(flags > 0, height // 2, height)[:, None, None]
        col_limit = jnp.where(flags > 0, breadth // 2, breadth)[:, None, None]
        return (jnp.arange(height, dtype=jnp.int32)[None, :, None] < row_limit) & (
            jnp.arange(breadth, dtype=jnp.int32)[None, None, :] < col_limit
        )

    cell = 2 * jnp.arange(2, dtype=jnp.int32)[:, None, None] + jnp.arange(2, dtype=jnp.int32)
    cells = pool_index.reshape(number, height // 2, 1, breadth // 2, 1)
    valid = inside(image_small)
    chosen = ((cells == cell).reshape(number, height, breadth) & valid).reshape(number, pixels)
    info = jnp.zeros((8 * number, channels), F32)
    info = info.at[::8, :pixels].set(chosen.astype(F32))
    info = info.at[1::8, 0].set(image_small.astype(F32))
    slots, x, infos, trunk_owners, head_low = arrive(
        tasks, batches, (number, height, breadth), images.reshape(number * pixels, channels),
        info, row_slot, trunk_weight, head_weight[0],
    )
    head_rows = lax.all_gather(head_low, "batch", axis=0, tiled=True)

    scales = quarter(jnp.stack([trunk_gain, trunk_offset], axis=1)).reshape(4, width)
    enc_totals, dec_totals, features, *kept = trunk_forward(
        geometry, tasks, batches, row_slot, infos, x, slots, scales
    )
    head_scales = jnp.stack([head_gain[0], head_offset[0]], axis=1).reshape(6, channels)
    pooled, upstream, head_sums, head_owned = head(
        geometry, tasks, batches, infos, features, head_rows,
        cotangent.reshape(shown, pixels // 4, channels), head_scales, enc_totals,
    )
    task_features = pooled.reshape(cotangent.shape)
    enc_grad, dec_grad, flow, trunk_sums = trunk_backward(
        geometry, tasks, batches, infos, upstream, enc_totals, dec_totals, scales, (x, *kept)
    )
    input_grad, norm_sums, results = finish(
        tasks, batches,
        (to_slots(row_slot, enc_grad, dec_grad), flow, trunk_sums, trunk_owners, head_owned),
        (trunk_weight, trunk_mean_grad, trunk_mean_square,
         head_weight[0], head_mean_grad[0], head_mean_square[0]),
        (trunk_statistic, head_statistic[0], trunk_basis, head_basis[0]),
    )
    input_grad = input_grad.reshape(images.shape)
    (
        trunk_weight_new, trunk_one_new, trunk_two_new,
        head_weight_new, head_one_new, head_two_new,
        trunk_stat_new, head_stat_new, trunk_basis_new, head_basis_new,
    ) = results

    trunk_norm = jnp.stack([trunk_gain, trunk_offset], axis=1)
    trunk_norm_grad = norm_sums[:4].reshape(2, 2, channels)[:, ::-1]
    trunk_norm_one, trunk_norm_two, trunk_direction = adam(
        trunk_norm_grad, trunk_norm_mean_grad, trunk_norm_mean_square
    )
    head_norm = jnp.stack([head_gain, head_offset], axis=2)
    head_norm_grad = head_sums[:6].reshape(1, 3, 2, channels)[:, :, ::-1]
    head_norm_one, head_norm_two, head_direction = adam(
        head_norm_grad, head_norm_mean_grad, head_norm_mean_square
    )
    return (
        task_features,
        input_grad,
        trunk_weight_new,
        trunk_one_new,
        trunk_two_new,
        trunk_stat_new,
        trunk_basis_new,
        head_weight_new[None],
        head_one_new[None],
        head_two_new[None],
        head_stat_new[None],
        head_basis_new[None],
        trunk_norm - LEARN_NORM * trunk_direction,
        trunk_norm_one,
        trunk_norm_two,
        head_norm - LEARN_NORM * head_direction,
        head_norm_one,
        head_norm_two,
    )


def solution(mesh):
    placed = (
        P(("task", "batch"), None, None, None),
        P(("task", "batch")),
        P(("task", "batch"), None, None),
        P(),
        P("batch", None),
        P("batch", None),
        P("batch", None),
        P(),
        P(),
        P("task", "batch", None),
        P("task", "batch", None),
        P("task", "batch", None),
        P("task", None, None, None),
        P("task", None, None, None),
        P(),
        P(),
        P(),
        P(),
        P("task", None, None),
        P("task", None, None),
        P("task", None, None, None),
        P("task", None, None, None),
        P("task", None, "batch", None, None, None),
    )
    return jax.shard_map(
        functools.partial(local, mesh.shape["task"], mesh.shape["batch"]),
        mesh=mesh,
        in_specs=placed,
        out_specs=(
            P("task", None, "batch", None, None, None),
            P(("task", "batch"), None, None, None),
            P("batch", None),
            P("batch", None),
            P("batch", None),
            P(),
            P(),
            P("task", "batch", None),
            P("task", "batch", None),
            P("task", "batch", None),
            P("task", None, None, None),
            P("task", None, None, None),
            P(),
            P(),
            P(),
            P("task", None, None, None),
            P("task", None, None, None),
            P("task", None, None, None),
        ),
        check_vma=False,
    )
```

```python
import functools

import jax
import jax.numpy as jnp
from jax import lax
from jax.experimental import pallas as pl
from jax.experimental.pallas import tpu as pltpu
from jax.sharding import PartitionSpec as P

STEP = 10


EPS = 1e-05
ADAM_EPS = 1e-08
BETA_ONE = 0.95
BETA_TWO = 0.95
STAT_DECAY = 0.95
LEARN_MATRIX = 0.02
LEARN_NORM = 0.5
DECAY_MATRIX = 0.01
BF = jnp.bfloat16
F32 = jnp.float32
MESH = pl.DeviceIdType.MESH
MIB = 1 << 20

VMEM_SPEC = pl.BlockSpec(memory_space=pltpu.VMEM)
SMEM_SPEC = pl.BlockSpec(memory_space=pltpu.SMEM)


def run(body, outs, specs, args, scratch=(), vmem=40, flops=0):
    size = sum(o.size * o.dtype.itemsize for o in outs) + sum(a.size * a.dtype.itemsize for a in args)
    return pl.pallas_call(
        body,
        out_shape=tuple(outs),
        in_specs=[SMEM_SPEC if s == "s" else VMEM_SPEC for s in specs],
        out_specs=tuple(VMEM_SPEC for _ in outs),
        scratch_shapes=list(scratch),
        compiler_params=pltpu.CompilerParams(vmem_limit_bytes=vmem * MIB),
        cost_estimate=pl.CostEstimate(flops=flops, bytes_accessed=size, transcendentals=0),
    )(*args)


def shape(dims, kind):
    return jax.ShapeDtypeStruct(tuple(dims), kind)


def dot(a, b):
    return jnp.dot(a, b, preferred_element_type=F32)


def dot_nt(a, b):
    return lax.dot_general(a, b, (((1,), (1,)), ((), ())), preferred_element_type=F32)


def dot_tn(a, b):
    return lax.dot_general(a, b, (((0,), (0,)), ((), ())), preferred_element_type=F32)


def split(a):
    high = a.astype(BF)
    return high, (a - high.astype(F32)).astype(BF)


def dot3(kind, a, b):
    dims = {dot: (1, 0), dot_nt: (1, 1), dot_tn: (0, 0)}[kind]
    a_high, a_low = split(a)
    b_high, b_low = split(b)
    return kind(
        jnp.concatenate([a_high, a_high, a_low], axis=dims[0]),
        jnp.concatenate([b_high, b_low, b_high], axis=dims[1]),
    )


def places(height, breadth):
    index = lax.broadcasted_iota(jnp.int32, (height * breadth, 1), 0)
    row = lax.div(index, breadth)
    return row, index - row * breadth


def valid_rows(kind, height, breadth, spot):
    row, col = spot
    shrunk = kind > 0
    row_limit = jnp.where(shrunk, height // 2, height)
    col_limit = jnp.where(shrunk, breadth // 2, breadth)
    return jnp.where((row < row_limit) & (col < col_limit), 1.0, 0.0).astype(F32)


def move(values, rows):
    gap = jnp.zeros((abs(rows),) + values.shape[1:], values.dtype)
    if rows > 0:
        return jnp.concatenate([gap, values[:-rows]], axis=0)
    return jnp.concatenate([values[-rows:], gap], axis=0)


def from_left(values, col):
    return jnp.where(col > 0, pltpu.roll(values, 1, 0), 0.0)


def from_right(values, col, breadth):
    return jnp.where(col < breadth - 1, pltpu.roll(values, values.shape[0] - 1, 0), 0.0)


def gather_taps(tap, breadth, col):
    lines = [move(tap(b), breadth) + tap(3 + b) + move(tap(6 + b), -breadth) for b in range(3)]
    return lines[1] + from_left(lines[0], col) + from_right(lines[2], col, breadth)


def spread_taps(values, breadth, col):
    lines = [from_right(values, col, breadth), values, from_left(values, col)]
    return [
        move(lines[b], breadth * (a - 1)) if a != 1 else lines[b] for a in range(3) for b in range(3)
    ]


def window_sum(values, row, col, breadth):
    count = values.shape[0]
    pair = values + jnp.where(
        col % 2 == 0, pltpu.roll(values, count - 1, 0), pltpu.roll(values, 1, 0)
    )
    return pair + jnp.where(row % 2 == 0, move(pair, -breadth), move(pair, breadth))


def sigmoid(values):
    return 0.5 * jnp.tanh(0.5 * values) + 0.5


def silu_back(scaled):
    sig = sigmoid(scaled)
    return sig * (1.0 + scaled * (1.0 - sig))


def col_sum(values):
    return jnp.sum(values, axis=0, keepdims=True)


def put_sums(ref, rows):
    width = ref.shape[1]
    rows = list(rows) + [jnp.zeros((1, width), F32)] * (8 - len(rows))
    ref[...] = jnp.concatenate(rows, axis=0)


def each_image(geometry, body, start):
    number, height, breadth = geometry
    pixels = height * breadth

    def step(image, carry):
        return body(image, pl.ds(pl.multiple_of(image * pixels, 16), pixels), carry)

    return lax.fori_loop(0, number, step, start)


def zero_rows(count, width):
    return (jnp.zeros((1, width), F32),) * count


def greet(axes):
    barrier = pltpu.get_barrier_semaphore()
    for axis, size in axes:
        me = lax.axis_index(axis)
        for step in range(1, size):
            pl.semaphore_signal(
                barrier, inc=1, device_id={axis: lax.rem(me + step, size)}, device_id_type=MESH
            )
    pl.semaphore_wait(barrier, sum(size - 1 for _, size in axes))


def remote(source, target, sends, receives, peer, axis):
    return pltpu.make_async_remote_copy(
        src_ref=source,
        dst_ref=target,
        send_sem=sends,
        recv_sem=receives,
        device_id={axis: peer},
        device_id_type=MESH,
    )


def pack(rows):
    parts = [row[:, i : i + 128] for row in rows for i in range(0, row.shape[1], 128)]
    parts += [jnp.zeros((1, 128), F32)] * (8 - len(parts))
    return jnp.concatenate(parts, axis=0)


def unpack(tile, count, width):
    per = width // 128
    return [
        jnp.concatenate([tile[k * per + i : k * per + i + 1, :] for i in range(per)], axis=1)
        for k in range(count)
    ]


def total_rows(k, axis, size, rows, mine, slots, sends, receives, meanwhile=None):
    me = lax.axis_index(axis)
    tile = pack(rows)
    mine[k] = tile
    slots[k, me] = tile
    for step in range(1, size):
        peer = lax.rem(me + step, size)
        remote(mine.at[k], slots.at[k, me], sends.at[k, step], receives.at[k, me], peer, axis).start()
    if meanwhile:
        meanwhile()
    for step in range(1, size):
        peer = lax.rem(me + size - step, size)
        remote(
            mine.at[k], slots.at[k, peer], sends.at[k, step], receives.at[k, peer], peer, axis
        ).wait_recv()
    total = slots[k, 0]
    for peer in range(1, size):
        total = total + slots[k, peer]
    for step in range(1, size):
        peer = lax.rem(me + step, size)
        remote(
            mine.at[k], slots.at[k, me], sends.at[k, step], receives.at[k, me], peer, axis
        ).wait_send()
    return unpack(total, len(rows), rows[0].shape[1])


def total_scratch(count, size):
    return [
        pltpu.VMEM((count, 8, 128), F32),
        pltpu.VMEM((count, size, 8, 128), F32),
        pltpu.SemaphoreType.DMA((count, size)),
        pltpu.SemaphoreType.DMA((count, size)),
    ]


def columns_of(place, width):
    return pl.ds(pl.multiple_of(place * width, 128), width)


SPECS = {"s": SMEM_SPEC, "v": VMEM_SPEC, "h": pl.BlockSpec(memory_space=pltpu.HBM)}


def exchange_kernel(body, outs, specs, args, scratch, identity, vmem, flops=0, places_out=None):
    size = sum(o.size * o.dtype.itemsize for o in outs) + sum(a.size * a.dtype.itemsize for a in args)
    return pl.pallas_call(
        body,
        out_shape=tuple(outs),
        in_specs=[SPECS[s] for s in specs],
        out_specs=tuple(SPECS[s] for s in places_out or "v" * len(outs)),
        scratch_shapes=list(scratch),
        compiler_params=pltpu.CompilerParams(
            vmem_limit_bytes=vmem * MIB, collective_id=identity, has_side_effects=True
        ),
        cost_estimate=pl.CostEstimate(flops=flops, bytes_accessed=size, transcendentals=0),
    )(*args)


def info_rows(infos, i):
    return infos[pl.ds(pl.multiple_of(i * 8, 8), 8), :]


def valid_of(infos, i, height, breadth, spot):
    return valid_rows(info_rows(infos, i)[1:2, 0:1], height, breadth, spot)


def chosen_cells(narrow, infos, i):
    return (narrow * info_rows(infos, i)[0:1, : narrow.shape[1]]).astype(BF)


def norm_moments(totals):
    total, squares, count = totals
    center = total / count
    return center, lax.rsqrt(squares / count - center * center + EPS)


def norm_line(totals, scale):
    center, inverse = norm_moments(totals)
    slope = inverse * scale[0]
    return slope, scale[1] - center * slope


def norm_sums(totals, sums):
    center, inverse = norm_moments(totals)
    return [sums[0], inverse * (sums[1] - center * sums[0])]


def norm_back_line(totals, sums, scale):
    center, inverse = norm_moments(totals)
    count = totals[2]
    slope = inverse * scale[0]
    lean = -slope * inverse * (sums[1] / count)
    return slope, lean, -slope * (sums[0] / count) - lean * center


def on_line(values, line):
    return values * line[0] + line[1]


def back_on_line(upstream, values, line, valid):
    return (upstream * line[0] + values * line[1] + line[2]) * valid


def silu(values):
    return values * sigmoid(values)


def window_count(height, breadth):
    return -(-(height * breadth // 4) // 16) * 16


def pool_choice(height, breadth, windows, flipped):
    pixels = height * breadth
    dims = (windows, pixels) if flipped else (pixels, windows)
    pixel = lax.broadcasted_iota(jnp.int32, dims, 1 if flipped else 0)
    window = lax.broadcasted_iota(jnp.int32, dims, 0 if flipped else 1)
    row = lax.div(pixel, breadth)
    col = pixel - row * breadth
    home = lax.div(row, 2) * (breadth // 2) + lax.div(col, 2)
    return jnp.where(home == window, 1.0, 0.0).astype(F32)


def rows_of(ref, first, count):
    return [ref[first + k : first + k + 1, :] for k in range(count)]


def window_rows(i, windows):
    return pl.ds(pl.multiple_of(i * windows, 16), windows)


def trunk_forward_body(
    geometry, tasks, batches,
    index, infos, x_far, kernel_slots, scales,
    enc_totals, dec_totals, features, *rest,
):
    kept, (enc_pre, dec_pre, spread), rest = rest[:5], rest[5:8], rest[8:]
    (
        x, x_loaded, enc_taps, dec_taps, wide, tap,
        work, pooled, pooled_all, part, pool_sends, pool_receives, sends, receives,
    mine, slots, total_sends, total_receives, saved,
    ) = rest
    number, height, breadth = geometry
    width = enc_pre.shape[1]
    windows = window_count(height, breadth)
    task = lax.axis_index("task")
    spot = places(height, breadth)
    _, col = spot
    choice = pool_choice(height, breadth, windows, True)
    narrow = choice.astype(BF)

    x_load = pltpu.make_async_copy(x_far, x, x_loaded)
    x_load.start()
    sources = (enc_taps, dec_taps, enc_pre, dec_pre, spread)
    saves = [pltpu.make_async_copy(a, b, saved.at[k]) for k, (a, b) in enumerate(zip(sources, kept))]
    channels = x.shape[1]

    def widen(i, carry):
        rows = pl.ds(pl.multiple_of(i * channels, 16), channels)
        wide[rows, :] = kernel_slots[rows, :].astype(F32)
        return carry

    def fetch(taps, first, begin, end):
        group = 32
        for p in range(begin, end):

            def some(i, carry):
                base = i * group
                for u in range(group):
                    slot = index[(first + p) * channels + base + u]
                    tap[pl.ds(base + u, 1), :] = wide[pl.ds(slot, 1), :]
                return carry

            lax.fori_loop(0, channels // group, some, 0)
            taps[:, p * width : (p + 1) * width] = tap[...].astype(BF)

    lax.fori_loop(0, wide.shape[0] // channels, widen, 0)
    fetch(enc_taps, 0, 0, 9)
    saves[0].start()
    x_load.wait()

    def conv(x, taps, pre):
        def image(i, rows, carry):
            valid = valid_of(infos, i, height, breadth, spot)
            work[...] = dot(x[rows, :], taps[...])
            out = gather_taps(lambda p: work[:, p * width : (p + 1) * width], breadth, col)
            pre[rows, :] = out
            kept = out * valid
            return (
                carry[0] + col_sum(kept),
                carry[1] + col_sum(kept * out),
                carry[2] + jnp.broadcast_to(col_sum(valid), (1, width)),
            )

        return each_image(geometry, image, zero_rows(3, width))

    def total(k, rows, meanwhile=None):
        return total_rows(
            k, "batch", batches, list(rows), mine, slots, total_sends, total_receives, meanwhile
        )

    sums = conv(x, enc_taps, enc_pre)
    saves[2].start()
    greet((("task", tasks), ("batch", batches)))
    totals = total(0, sums, lambda: fetch(dec_taps, 9, 0, 4))
    put_sums(enc_totals, totals)
    scale = rows_of(scales, 0, 2)

    def peer_of(step, incoming):
        return lax.rem(task + (tasks - step if incoming else step), tasks)

    def pool_copy(i, step, incoming=False):
        rows = window_rows(i, windows)
        peer = peer_of(step, incoming)
        target = pooled_all.at[rows, columns_of(peer if incoming else task, width)]
        return remote(
            pooled.at[rows, :], target, pool_sends.at[i, step], pool_receives.at[i, step], peer, "task"
        )

    line = norm_line(totals, scale)

    def pool(i, rows, carry):
        valid = valid_of(infos, i, height, breadth, spot)
        scaled = on_line(enc_pre[rows, :], line)
        high, low = split(silu(scaled) * valid)
        mean = ((dot(narrow, high) + dot(narrow, low)) * 0.25).astype(BF)
        here = window_rows(i, windows)
        pooled[here, :] = mean
        pooled_all[here, columns_of(task, width)] = mean
        for step in range(1, tasks):
            pool_copy(i, step).start()
        return carry

    each_image(geometry, pool, 0)
    fetch(dec_taps, 9, 4, 9)
    saves[1].start()

    def unpool(i, rows, carry):
        for step in range(1, tasks):
            pool_copy(i, step, True).wait_recv()
        wide = dot_tn(chosen_cells(choice, infos, i), pooled_all[window_rows(i, windows), :])
        spread[rows, :] = wide.astype(BF)
        return carry

    each_image(geometry, unpool, 0)
    saves[4].start()
    sums = conv(spread, dec_taps, dec_pre)
    saves[3].start()
    totals = total(1, sums)
    put_sums(dec_totals, totals)
    scale = rows_of(scales, 2, 2)

    def feature_copy(i, rows, step, incoming=False):
        peer = peer_of(step, incoming)
        target = features.at[rows, columns_of(peer if incoming else task, width)]
        return remote(
            part.at[rows, :], target, sends.at[i, step], receives.at[i, step], peer, "task"
        )

    last_line = norm_line(totals, scale)

    def finish(i, rows, carry):
        valid = valid_of(infos, i, height, breadth, spot)
        scaled = on_line(dec_pre[rows, :], last_line)
        low = (silu(scaled) * valid).astype(BF)
        part[rows, :] = low
        features[rows, columns_of(task, width)] = low
        for step in range(1, tasks):
            feature_copy(i, rows, step).start()
        return carry

    each_image(geometry, finish, 0)

    def settle(i, rows, carry):
        for step in range(1, tasks):
            feature_copy(i, rows, step, True).wait_recv()
            feature_copy(i, rows, step).wait_send()
            pool_copy(i, step).wait_send()
        return carry

    each_image(geometry, settle, 0)
    for copy in saves:
        copy.wait()


def trunk_forward(geometry, tasks, batches, index, infos, x, kernel_slots, scales):
    number, height, breadth = geometry
    pixels = height * breadth
    channels = x.shape[1]
    width = channels // tasks
    windows = window_count(height, breadth)
    tall = shape((x.shape[0], width), F32)
    taps = shape((channels, 9 * width), BF)
    outs = [
        shape((8, width), F32), shape((8, width), F32), shape(x.shape, BF),
        taps, taps,
        tall, tall, shape(x.shape, BF),
    ]
    return exchange_kernel(
        functools.partial(trunk_forward_body, geometry, tasks, batches),
        outs,
        "svhvv",
        (index, infos, x, kernel_slots, scales),
        [
            pltpu.VMEM(tall.shape, F32),
            pltpu.VMEM(tall.shape, F32),
            pltpu.VMEM(x.shape, BF),
            pltpu.VMEM(x.shape, BF),
            pltpu.SemaphoreType.DMA,
            pltpu.VMEM(taps.shape, BF),
            pltpu.VMEM(taps.shape, BF),
            pltpu.VMEM(kernel_slots.shape, F32),
            pltpu.VMEM((channels, width), F32),
            pltpu.VMEM((pixels, 9 * width), F32),
            pltpu.VMEM((number * windows, width), BF),
            pltpu.VMEM((number * windows, channels), BF),
            pltpu.VMEM((x.shape[0], width), BF),
        ]
        + [pltpu.SemaphoreType.DMA((number, tasks))] * 4
        + total_scratch(2, batches)
        + [pltpu.SemaphoreType.DMA((5,))],
        1,
        60,
        flops=4 * x.size * taps.shape[1],
        places_out="vvvhhhhh",
    )


def head_body(
    geometry, tasks, batches, summing,
    infos, features, weights, cotangent, scales, counts,
    task_out, upstream, sums_out, *rest,
):
    grads_out, rest = rest[0], rest[1:]
    (
        grads, pre_one, pre_two, pre_three, hidden, gated, nine, work, lower, out, arrived,
        sends, receives, mine, slots, total_sends, total_receives, loaded,
    ) = rest[:18]
    number, height, breadth = geometry
    channels = features.shape[1]
    width = channels // tasks
    windows = task_out.shape[1]
    task = lax.axis_index("task")
    half = work.shape[2]
    spot = places(height, breadth)
    _, col = spot
    widen = pool_choice(height, breadth, windows, False).astype(BF)
    narrow = pool_choice(height, breadth, windows, True).astype(BF)
    count = jnp.broadcast_to(counts[2:3, 0:1], (1, channels))
    cuts = (pl.ds(0, 2 * channels), pl.ds(2 * channels, 9 * channels))
    loads = [
        pltpu.make_async_copy(weights.at[cut, :], grads.at[cut, :], loaded.at[k])
        for k, cut in enumerate(cuts)
    ]
    for copy in loads:
        copy.start()
    first = grads.at[pl.ds(0, channels), :]
    second = grads.at[pl.ds(channels, channels), :]

    def kernel_rows(p):
        return pl.ds((2 + p) * channels, channels)

    def total(k, rows, meanwhile=None):
        return total_rows(
            k, "batch", batches, list(rows), mine, slots, total_sends, total_receives, meanwhile
        )

    if summing:
        near, near_sends, near_receives, summed, saved = rest[18:]
        place, core, chips = pair_place(batches)
        block = near.shape[1]

        def near_copy(chip):
            return remote(
                block_rows(grads, 2 * chip + 1 - core, block), near.at[chip],
                near_sends.at[chip], near_receives.at[chip], 2 * place + 1 - core, "batch",
            )

    def put_stats(pre, rows, value, valid, carry):
        pre[rows, :] = value
        kept = value * valid
        return carry[0] + col_sum(kept), carry[1] + col_sum(kept * value)

    nothing = zero_rows(2, channels)
    scale_one, scale_two, scale_three = (rows_of(scales, 2 * k, 2) for k in range(3))

    loads[0].wait()

    def first_step(i, rows, carry):
        valid = valid_of(infos, i, height, breadth, spot)
        return put_stats(pre_one, rows, dot(features[rows, :], first[...]), valid, carry)

    sums = each_image(geometry, first_step, nothing)
    greet((("task", tasks), ("batch", batches)))
    totals_one = total(0, sums) + [count]

    line_one = norm_line(totals_one, scale_one)

    def second_step(i, rows, carry):
        valid = valid_of(infos, i, height, breadth, spot)
        scaled = on_line(pre_one[rows, :], line_one)
        low = (silu(scaled) * valid).astype(BF)
        hidden[rows, :] = low
        return put_stats(pre_two, rows, dot(low, second[...]), valid, carry)

    sums = each_image(geometry, second_step, nothing)
    totals_two = total(1, sums) + [count]

    line_two = norm_line(totals_two, scale_two)

    def third_step(i, rows, carry):
        valid = valid_of(infos, i, height, breadth, spot)
        scaled = on_line(pre_two[rows, :], line_two)
        low = (sigmoid(scaled) * features[rows, :].astype(F32)).astype(BF)
        gated[rows, :] = low
        parts = []
        for j in range(channels // half):
            cut = slice(j * half, (j + 1) * half)
            for p in range(9):
                work[p] = dot(low, grads[kernel_rows(p), cut])
            parts.append(gather_taps(lambda p: work[p], breadth, col))
        return put_stats(pre_three, rows, jnp.concatenate(parts, axis=1), valid, carry)

    loads[1].wait()
    sums = each_image(geometry, third_step, nothing)
    totals_three = total(2, sums) + [count]

    line_three = norm_line(totals_three, scale_three)

    def out_step(i, rows, carry):
        valid = valid_of(infos, i, height, breadth, spot)
        values = pre_three[rows, :]
        scaled = on_line(values, line_three)
        high, low = split(silu(scaled) * valid)
        mean = (dot(narrow, high) + dot(narrow, low)) * 0.25
        task_out[i] = mean.astype(BF)
        dy = silu_back(scaled) * dot(widen, cotangent[i]) * 0.25 * valid
        lower[rows, :] = dy
        return carry[0] + col_sum(dy), carry[1] + col_sum(dy * values)

    sums = each_image(geometry, out_step, nothing)
    sums_three = total(3, norm_sums(totals_three, sums))
    back_three = norm_back_line(totals_three, sums_three, scale_three)

    def third_back(i, rows, carry):
        valid = valid_of(infos, i, height, breadth, spot)
        dz = back_on_line(lower[rows, :], pre_three[rows, :], back_three, valid)
        for p, moved in enumerate(spread_taps(dz, breadth, col)):
            nine[p, rows, :] = moved.astype(BF)
        flow = None
        for p in range(9):
            piece = dot_nt(nine[p, rows, :], grads[kernel_rows(p), :])
            flow = piece if flow is None else flow + piece
        values = pre_two[rows, :]
        gate = sigmoid(on_line(values, line_two))
        flow = flow * gate
        lower[rows, :] = flow
        dy = flow * features[rows, :].astype(F32) * (1.0 - gate)
        pre_three[rows, :] = dy
        return carry[0] + col_sum(dy), carry[1] + col_sum(dy * values)

    sums = each_image(geometry, third_back, nothing)

    def taps(begin, end):
        def tap(p, carry):
            rows = pl.ds(pl.multiple_of((2 + p) * channels, channels), channels)
            grads[rows, :] = dot_tn(gated[...], nine[p]).astype(BF)
            return carry

        lax.fori_loop(begin, end, tap, 0)

    sums_two = total(4, norm_sums(totals_two, sums), lambda: taps(0, 2))
    back_two = norm_back_line(totals_two, sums_two, scale_two)

    def second_back(i, rows, carry):
        valid = valid_of(infos, i, height, breadth, spot)
        dz = back_on_line(pre_three[rows, :], pre_two[rows, :], back_two, valid).astype(BF)
        out[rows, :] = dz
        values = pre_one[rows, :]
        dy = silu_back(on_line(values, line_one)) * dot_nt(dz, second[...])
        pre_three[rows, :] = dy
        return carry[0] + col_sum(dy), carry[1] + col_sum(dy * values)

    sums = each_image(geometry, second_back, nothing)

    def weight_rows():
        grads[pl.ds(channels, channels), :] = dot_tn(hidden[...], out[...]).astype(BF)
        taps(2, 3)

    sums_one = total(5, norm_sums(totals_one, sums), weight_rows)
    back_one = norm_back_line(totals_one, sums_one, scale_one)

    def flow_copy(i, rows, step, incoming=False):
        peer = lax.rem(task + (tasks - step if incoming else step), tasks)
        return remote(
            out.at[rows, columns_of(peer, width)], arrived.at[step - 1, rows, :],
            sends.at[i, step], receives.at[i, step], peer, "task",
        )

    def first_back(i, rows, carry):
        valid = valid_of(infos, i, height, breadth, spot)
        dz = back_on_line(pre_three[rows, :], pre_one[rows, :], back_one, valid).astype(BF)
        hidden[rows, :] = dz
        flow = (lower[rows, :] + dot_nt(dz, first[...])) * valid
        out[rows, :] = flow.astype(BF)
        for step in range(1, tasks):
            flow_copy(i, rows, step).start()
        return carry

    each_image(geometry, first_back, 0)
    taps(3, 9)
    if summing:
        for chip in range(1, chips):
            near_copy(chip).start()
    grads[pl.ds(0, channels), :] = dot_tn(features[...], hidden[...]).astype(BF)
    if summing:
        near_copy(0).start()
        for chip in (*range(1, chips), 0):
            near_copy(chip).wait_recv()
            own = block_rows(grads, 2 * chip + core, block)[...].astype(F32)
            summed[chip] = (own + near[chip].astype(F32)).astype(BF)
            pltpu.make_async_copy(summed.at[chip], grads_out.at[chip], saved.at[chip]).start()
    else:
        grads_out[...] = grads[...]
    put_sums(sums_out, sums_one + sums_two + sums_three)

    def settle(i, rows, carry):
        for step in range(1, tasks):
            flow_copy(i, rows, step, True).wait_recv()
        flow = out[rows, columns_of(task, width)].astype(F32)
        for step in range(1, tasks):
            flow = flow + arrived[step - 1, rows, :].astype(F32)
        upstream[rows, :] = flow
        for step in range(1, tasks):
            flow_copy(i, rows, step).wait_send()
        return carry

    each_image(geometry, settle, 0)
    if summing:
        for chip in range(chips):
            near_copy(chip).wait_send()
            pltpu.make_async_copy(summed.at[chip], grads_out.at[chip], saved.at[chip]).wait()


def head(geometry, tasks, batches, infos, features, weights, cotangent, scales, counts):
    number, height, breadth = geometry
    pixels = height * breadth
    total, channels = features.shape
    width = channels // tasks
    block = weights.shape[0] // batches
    chips = batches // 2
    summing = block % 16 == 0
    outs = [
        shape((number, pixels // 4, channels), BF),
        shape((total, width), F32),
        shape((8, channels), F32),
        shape((chips, block, channels) if summing else weights.shape, BF),
    ]
    scratch = []
    if summing:
        scratch = [pltpu.VMEM((chips, block, channels), BF)]
        scratch += [pltpu.SemaphoreType.DMA((chips,))] * 2
        scratch += [pltpu.VMEM((chips, block, channels), BF), pltpu.SemaphoreType.DMA((chips,))]
    pooled, upstream, sums, grads = exchange_kernel(
        functools.partial(head_body, geometry, tasks, batches, summing),
        outs,
        "vvhvvv",
        (infos, features, weights, cotangent, scales, counts),
        [
            pltpu.VMEM(weights.shape, BF),
            pltpu.VMEM(features.shape, F32),
            pltpu.VMEM(features.shape, F32),
            pltpu.VMEM(features.shape, F32),
            pltpu.VMEM(features.shape, BF),
            pltpu.VMEM(features.shape, BF),
            pltpu.VMEM((9,) + features.shape, BF),
            pltpu.VMEM((9, pixels, min(channels, 256)), F32),
            pltpu.VMEM(features.shape, F32),
            pltpu.VMEM(features.shape, BF),
            pltpu.VMEM((tasks - 1, total, width), BF),
        ]
        + [pltpu.SemaphoreType.DMA((number, tasks))] * 2
        + total_scratch(6, batches)
        + [pltpu.SemaphoreType.DMA((2,))]
        + scratch,
        2,
        61,
        flops=6 * total * channels * weights.shape[0],
        places_out="vvvh" if summing else "vvvv",
    )
    if summing:
        owned = lax.psum_scatter(
            grads.reshape(chips * block, channels), "batch", scatter_dimension=0,
            axis_index_groups=[list(range(core, batches, 2)) for core in range(2)], tiled=True,
        )
    else:
        owned = lax.psum_scatter(grads, "batch", scatter_dimension=0, tiled=True)
    return pooled, upstream, sums, owned


def trunk_backward_body(
    geometry, tasks, batches,
    infos, upstream, enc_totals, dec_totals, scales, *rest,
):
    kept, rest = rest[:6], rest[6:]
    outs, sums_out, rest = rest[:3], rest[3], rest[4:]
    (x, enc_taps, dec_taps, enc_pre, dec_pre, spread), rest = rest[:6], rest[6:]
    (
        nine, change, packed, arrived, pooled, sends, receives,
        mine, slots, total_sends, total_receives, loaded,
        enc_grad, dec_grad, flow_out, saved,
    ) = rest
    saves = [
        pltpu.make_async_copy(a, b, saved.at[k])
        for k, (a, b) in enumerate(zip((enc_grad, dec_grad, flow_out), outs))
    ]
    targets = (x, enc_taps, dec_taps, enc_pre, dec_pre, spread)
    loads = [pltpu.make_async_copy(a, b, loaded.at[k]) for k, (a, b) in enumerate(zip(kept, targets))]
    for k in (4, 2, 5, 3, 1, 0):
        loads[k].start()
    number, height, breadth = geometry
    channels = x.shape[1]
    width = enc_pre.shape[1]
    windows = window_count(height, breadth)
    task = lax.axis_index("task")
    spot = places(height, breadth)
    _, col = spot
    widen = pool_choice(height, breadth, windows, False).astype(BF)
    narrow = pool_choice(height, breadth, windows, True)
    nothing = zero_rows(2, width)

    def total(k, rows):
        return total_rows(
            k, "batch", batches, list(rows), mine, slots, total_sends, total_receives
        )

    def change_of(pre, totals, scale, flow):
        line = norm_line(totals, scale)

        def image(i, rows, carry):
            valid = valid_of(infos, i, height, breadth, spot)
            values = pre[rows, :]
            dy = silu_back(on_line(values, line)) * flow(i, rows) * valid
            change[rows, :] = dy
            return carry[0] + col_sum(dy), carry[1] + col_sum(dy * values)

        return norm_sums(totals, each_image(geometry, image, nothing))

    def back(pre, totals, scale, sums, taps, put):
        line = norm_back_line(totals, sums, scale)

        def image(i, rows, carry):
            valid = valid_of(infos, i, height, breadth, spot)
            dz = back_on_line(change[rows, :], pre[rows, :], line, valid)
            for p, moved in enumerate(spread_taps(dz, breadth, col)):
                nine[rows, p * width : (p + 1) * width] = moved.astype(BF)
            put(i, rows, dot_nt(nine[rows, :], taps[...]) * valid)
            return carry

        each_image(geometry, image, 0)

    totals = rows_of(dec_totals, 0, 3)
    scale = rows_of(scales, 2, 2)
    loads[4].wait()
    sums = change_of(dec_pre, totals, scale, lambda i, rows: upstream[rows, :])
    greet((("task", tasks), ("batch", batches)))
    dec_sums = total(0, sums)

    def copy_of(i, step, incoming=False):
        rows = window_rows(i, windows)
        peer = lax.rem(task + (tasks - step if incoming else step), tasks)
        return remote(
            packed.at[rows, columns_of(peer, width)], arrived.at[step - 1, rows, :],
            sends.at[i, step], receives.at[i, step], peer, "task",
        )

    def put_packed(i, rows, flow):
        chosen = chosen_cells(narrow, infos, i)
        packed[window_rows(i, windows), :] = dot(chosen, flow.astype(BF)).astype(BF)
        for step in range(1, tasks):
            copy_of(i, step).start()

    loads[2].wait()
    back(dec_pre, totals, scale, dec_sums, dec_taps, put_packed)
    loads[5].wait()
    dec_grad[...] = dot_tn(spread[...], nine[...])
    saves[1].start()

    def collect(i, carry):
        for step in range(1, tasks):
            copy_of(i, step, True).wait_recv()
        rows = window_rows(i, windows)
        flow = packed[rows, columns_of(task, width)].astype(F32)
        for step in range(1, tasks):
            flow = flow + arrived[step - 1, rows, :].astype(F32)
        pooled[rows, :] = flow
        for step in range(1, tasks):
            copy_of(i, step).wait_send()
        return carry

    lax.fori_loop(0, number, collect, 0)

    def widened(i, rows):
        high, low = split(pooled[window_rows(i, windows), :])
        return (dot(widen, high) + dot(widen, low)) * 0.25

    totals = rows_of(enc_totals, 0, 3)
    scale = rows_of(scales, 0, 2)
    loads[3].wait()
    sums = change_of(enc_pre, totals, scale, widened)
    enc_sums = total(1, sums)

    def put_flow(i, rows, flow):
        flow_out[rows, :] = flow.astype(BF)

    loads[1].wait()
    back(enc_pre, totals, scale, enc_sums, enc_taps, put_flow)
    loads[0].wait()
    saves[2].start()
    enc_grad[...] = dot_tn(x[...], nine[...])
    saves[0].start()
    put_sums(sums_out, enc_sums + dec_sums)
    for copy in saves:
        copy.wait()


def trunk_backward(
    geometry, tasks, batches, infos, upstream, enc_totals, dec_totals, scales, kept
):
    number, height, breadth = geometry
    x, enc_taps, dec_taps = kept[:3]
    total, channels = x.shape
    width = channels // tasks
    windows = window_count(height, breadth)
    outs = [
        shape(enc_taps.shape, F32),
        shape(dec_taps.shape, F32),
        shape(x.shape, BF),
        shape((8, width), F32),
    ]
    return exchange_kernel(
        functools.partial(trunk_backward_body, geometry, tasks, batches),
        outs,
        "vvvvvhhhhhh",
        (infos, upstream, enc_totals, dec_totals, scales, *kept),
        [pltpu.VMEM(a.shape, a.dtype) for a in kept]
        + [
            pltpu.VMEM((total, 9 * width), BF),
            pltpu.VMEM((total, width), F32),
            pltpu.VMEM((number * windows, channels), BF),
            pltpu.VMEM((tasks - 1, number * windows, width), BF),
            pltpu.VMEM((number * windows, width), F32),
        ]
        + [pltpu.SemaphoreType.DMA((number, tasks))] * 2
        + total_scratch(2, batches)
        + [pltpu.SemaphoreType.DMA((6,))]
        + [pltpu.VMEM(a.shape, a.dtype) for a in outs[:3]]
        + [pltpu.SemaphoreType.DMA((3,))],
        3,
        60,
        flops=8 * x.size * enc_taps.shape[1],
        places_out="hhhv",
    )


def to_slots_body(index, enc_far, dec_far, slots, enc, dec, wide, low, load, save):
    count = wide.shape[0]
    channels = enc.shape[0]
    width = wide.shape[1]
    step = 1024
    group = 32
    loads = [
        pltpu.make_async_copy(a, b, load.at[k])
        for k, (a, b) in enumerate(((dec_far, dec), (enc_far, enc)))
    ]
    for copy in loads:
        copy.start()
    for kernel, copy in ((1, loads[0]), (0, loads[1])):
        copy.wait()
        source = dec if kernel else enc
        for q in range(9):

            def place(i, carry):
                base = pl.multiple_of(i * group, group)
                first = (9 * kernel + q) * channels + base
                values = source[pl.ds(base, group), q * width : (q + 1) * width]
                for u in range(group):
                    wide[pl.ds(index[first + u], 1), :] = values[u : u + 1, :]
                return carry

            lax.fori_loop(0, channels // group, place, 0)

    def out(i):
        rows = pl.ds(pl.multiple_of(i * step, step), step)
        return pltpu.make_async_copy(low.at[rows, :], slots.at[rows, :], save.at[i])

    def narrow(i, carry):
        rows = pl.ds(pl.multiple_of(i * step, step), step)
        low[rows, :] = wide[rows, :].astype(BF)
        out(i).start()
        return carry

    def end(i, carry):
        out(i).wait()
        return carry

    lax.fori_loop(0, count // step, narrow, 0)
    lax.fori_loop(0, count // step, end, 0)


def to_slots(index, enc, dec):
    width = enc.shape[1] // 9
    dims = (index.shape[0], width)
    far = pl.BlockSpec(memory_space=pltpu.HBM)
    return pl.pallas_call(
        to_slots_body,
        out_shape=shape(dims, BF),
        in_specs=[SMEM_SPEC, far, far],
        out_specs=far,
        scratch_shapes=[
            pltpu.VMEM(enc.shape, F32),
            pltpu.VMEM(dec.shape, F32),
            pltpu.VMEM(dims, F32),
            pltpu.VMEM(dims, BF),
            pltpu.SemaphoreType.DMA((2,)),
            pltpu.SemaphoreType.DMA((dims[0] // 1024,)),
        ],
        compiler_params=pltpu.CompilerParams(vmem_limit_bytes=60 * MIB),
        cost_estimate=pl.CostEstimate(flops=10000 * MIB, bytes_accessed=8 * MIB, transcendentals=0),
    )(index, enc, dec)


def adam(gradient, moment_one, moment_two):
    new_one = BETA_ONE * moment_one + (1.0 - BETA_ONE) * gradient
    new_two = BETA_TWO * moment_two + (1.0 - BETA_TWO) * gradient * gradient
    direction = (
        new_one / (1.0 - BETA_ONE**STEP) / (jnp.sqrt(new_two / (1.0 - BETA_TWO**STEP)) + ADAM_EPS)
    )
    return new_one, new_two, direction


def pair_place(batches):
    me = lax.axis_index("batch")
    place = lax.div(me, 2)
    return place, me - 2 * place, batches // 2


def greet_pairs(tasks, batches):
    place, core, chips = pair_place(batches)
    task = lax.axis_index("task")
    barrier = pltpu.get_barrier_semaphore()

    def signal(device):
        pl.semaphore_signal(barrier, inc=1, device_id=device, device_id_type=MESH)

    for step in range(1, tasks):
        signal({"task": lax.rem(task + step, tasks)})
    signal({"batch": 2 * place + 1 - core})
    for step in range(1, chips):
        signal({"batch": 2 * lax.rem(place + step, chips) + core})
    pl.semaphore_wait(barrier, tasks - 1 + chips)


def block_rows(ref, index, count):
    return ref.at[pl.ds(pl.multiple_of(index * count, 8), count), :]


SMALL = 128 * 128


def far_first(chips):
    return sorted(range(chips), key=lambda step: -min(step, chips - step))


def pair_sum(batches, rows_of_block, own_block, near, paired, far, sems):
    place, core, chips = pair_place(batches)
    count = near.shape[1]
    near_send, near_receive, far_send, far_receive = sems
    other = 2 * place + 1 - core
    ring = chips == 4 and count % 32 == 0 and near.shape[2] * count > SMALL
    half = count // 2
    halves = (pl.ds(0, half), pl.ds(half, half))

    def near_copy(step):
        chip = lax.rem(place + step, chips)
        return remote(rows_of_block(2 * chip + 1 - core), near.at[step],
                      near_send.at[step], near_receive.at[step], other, "batch")

    def far_copy(step, incoming=False):
        chip = lax.rem(place + (chips - step if incoming else step), chips)
        return remote(paired.at[step], far.at[step], far_send.at[step], far_receive.at[step],
                      2 * chip + core, "batch")

    def ring_copy(which, way):
        chip = lax.rem(place + (1 if way == 0 else chips - 1), chips)
        if which == 0:
            source, target = paired.at[2, halves[way], :], far.at[2 + way, halves[0], :]
        else:
            cut = halves[way] if which == 2 else halves[1 - way]
            source, target = paired.at[1 if way == 0 else 3, cut, :], far.at[way, cut, :]
        k = 2 * which + way
        return remote(source, target, far_send.at[k], far_receive.at[k], 2 * chip + core, "batch")

    def start():
        for step in far_first(chips):
            near_copy(step).start()

    def middle():
        for step in far_first(chips):
            near_copy(step).wait_recv()
            if step:
                paired[step] = (own_block(step) + near[step].astype(F32)).astype(paired.dtype)
                if not ring:
                    far_copy(step).start()
                elif step == 2:
                    ring_copy(0, 0).start()
                    ring_copy(0, 1).start()
                else:
                    ring_copy(1, 0 if step == 1 else 1).start()

    def relay():
        if not ring:
            return
        for way in range(2):
            ring_copy(0, way).wait_recv()
            step = 1 if way == 0 else 3
            total = paired[step, halves[way], :].astype(F32) + far[2 + way, halves[0], :].astype(F32)
            paired[step, halves[way], :] = total.astype(paired.dtype)
            ring_copy(2, way).start()

    def end():
        total = own_block(0) + near[0].astype(F32)
        if ring:
            for way in range(2):
                ring_copy(1, way).wait_recv()
                ring_copy(2, way).wait_recv()
                total = total + far[way].astype(F32)
            for k in range(3):
                for way in range(2):
                    ring_copy(k, way).wait_send()
        else:
            for step in range(1, chips):
                far_copy(step, True).wait_recv()
                total = total + far[step].astype(F32)
            for step in range(1, chips):
                far_copy(step).wait_send()
        for step in range(chips):
            near_copy(step).wait_send()
        return total

    return start, middle, relay, end


def blocks_in(source, batches, count, piece=0, pieces=1):
    place, core, chips = pair_place(batches)

    def rows(index):
        start = (index * pieces + piece) * count
        return source.at[pl.ds(pl.multiple_of(start, 8), count), :]

    def own(step):
        chip = lax.rem(place + step, chips)
        return rows(2 * chip + core)[...].astype(F32)

    return rows, own


def pair_scratch(batches, rows, width, kind):
    chips = batches // 2
    return [pltpu.VMEM((chips, rows // batches, width), kind)] * 3 + [
        pltpu.SemaphoreType.DMA((max(chips, 6),))
    ] * 4


def chip_spread(batches, block, sends, receives):
    place, core, chips = pair_place(batches)
    count, width = block(place).shape
    ring = chips == 4 and count % 32 == 0 and width * count > SMALL
    half = count // 2

    def copy(step, incoming=False):
        peer = lax.rem(place + (chips - step if incoming else step), chips)
        ref = block(peer if incoming else place)
        return remote(ref, ref, sends.at[step], receives.at[step], 2 * peer + core, "batch")

    def pass_on(way, incoming=False):
        step = 1 if way == 0 else chips - 1
        peer = lax.rem(place + (chips - step if incoming else step), chips)
        home = lax.rem(place + (2 if incoming else chips - step), chips)
        ref = block(home).at[pl.ds(way * half, half), :]
        k = 2 if way == 0 else 0
        return remote(ref, ref, sends.at[k], receives.at[k], 2 * peer + core, "batch")

    steps = (1, chips - 1) if ring else tuple(range(1, chips))

    def start():
        for step in steps:
            copy(step).start()

    def relay():
        if ring:
            for way, step in enumerate(steps):
                copy(step, True).wait_recv()
                pass_on(way).start()

    def settle():
        if ring:
            for way in range(2):
                pass_on(way, True).wait_recv()
        else:
            for step in steps:
                copy(step, True).wait_recv()

    def drain():
        for step in steps:
            copy(step).wait_send()
        if ring:
            for way in range(2):
                pass_on(way).wait_send()

    return start, relay, settle, drain


def arrive_body(
    tasks, batches, geometry,
    image_raw, info, index, weight, head_weight,
    slots, x, infos, owners, head_low,
    image, head_raw, head_loaded, raw, raw_loaded, x_send, x_receive, info_send, info_receive,
    chip_send, chip_receive, pair_send, pair_receive, own,
):
    task = lax.axis_index("task")
    place, core, chips = pair_place(batches)
    count, width = raw.shape
    load = pltpu.make_async_copy(weight.at[:, columns_of(task, width)], raw, raw_loaded)
    load.start()
    head_load = pltpu.make_async_copy(head_weight, head_raw, head_loaded)
    head_load.start()
    number, height, breadth = geometry
    pixels = height * breadth
    for n in range(number):
        valid = valid_rows(
            info[8 * n + 1 : 8 * n + 2, 0:1], height, breadth, places(height, breadth)
        )
        rows = slice(n * pixels, (n + 1) * pixels)
        image[rows, :] = (image_raw[rows, :].astype(F32) * valid).astype(BF)
    greet_pairs(tasks, batches)

    def task_copy(source, target, sends, receives, step, incoming=False):
        peer = lax.rem(task + (tasks - step if incoming else step), tasks)
        home = peer if incoming else task
        return remote(source, block_rows(target, home, source.shape[0]), sends.at[step],
                      receives.at[step], peer, "task")

    def moves(step, incoming=False):
        return (
            task_copy(info, infos, info_send, info_receive, step, incoming),
            task_copy(image, x, x_send, x_receive, step, incoming),
        )

    def block(chip):
        return block_rows(slots, 2 * chip + core, count)

    def pair_copy(hop, incoming=False):
        chip = lax.rem(place + chips - hop, chips)
        ref = block_rows(slots, 2 * chip + (1 - core if incoming else core), count)
        return remote(ref, ref, pair_send.at[hop], pair_receive.at[hop], 2 * place + 1 - core, "batch")

    start, relay, settle, drain = chip_spread(batches, block, chip_send, chip_receive)
    ring = chips == 4 and count % 32 == 0 and width * count > SMALL
    load.wait()
    block(place)[...] = raw[...].astype(BF)
    start()
    pair_copy(0).start()
    for step in range(1, tasks):
        for copy in moves(step):
            copy.start()
    locals_ = [
        pltpu.make_async_copy(image, block_rows(x, task, image.shape[0]), own.at[0]),
        pltpu.make_async_copy(info, block_rows(infos, task, info.shape[0]), own.at[1]),
    ]
    for copy in locals_:
        copy.start()
    mine = lax.broadcasted_iota(jnp.int32, (count, 1), 0) + lax.axis_index("batch") * count
    found = jnp.zeros((count, 128), F32)
    for k in range(index.shape[0] // 2, index.shape[0]):
        found = jnp.where(index[k : k + 1, :] == mine, 1.0, found)
    found = jnp.max(found, axis=1, keepdims=True)
    owners[:, 0:1] = 1.0 - found
    owners[:, 1:2] = found
    head_load.wait()
    head_low[...] = head_raw[...].astype(BF)
    relay()
    if ring:
        pair_copy(1).start()
        pair_copy(3).start()
        settle()
        pair_copy(2).start()
    else:
        settle()
        for hop in range(1, chips):
            pair_copy(hop).start()
    for copy in locals_:
        copy.wait()
    for step in range(1, tasks):
        for copy in moves(step, True):
            copy.wait_recv()
    for hop in range(chips):
        pair_copy(hop, True).wait_recv()
    for step in range(1, tasks):
        for copy in moves(step):
            copy.wait_send()
    for hop in range(chips):
        pair_copy(hop).wait_send()
    drain()


def arrive(tasks, batches, geometry, image, info, index, weight, head_weight):
    count, channels = weight.shape
    width = channels // tasks
    chips = batches // 2
    return exchange_kernel(
        functools.partial(arrive_body, tasks, batches, geometry),
        [
            shape((count * batches, width), BF),
            shape((image.shape[0] * tasks, channels), BF),
            shape((info.shape[0] * tasks, info.shape[1]), F32),
            shape((count, 2), F32),
            shape(head_weight.shape, BF),
        ],
        "vvvhh",
        (image, info, index.reshape(-1, 128), weight, head_weight),
        [
            pltpu.VMEM(image.shape, BF),
            pltpu.VMEM(head_weight.shape, F32),
            pltpu.SemaphoreType.DMA,
            pltpu.VMEM((count, width), F32),
            pltpu.SemaphoreType.DMA,
        ]
        + [pltpu.SemaphoreType.DMA((tasks,))] * 4
        + [pltpu.SemaphoreType.DMA((max(chips, 4),))] * 4
        + [pltpu.SemaphoreType.DMA((2,))],
        4,
        60,
        flops=20000 * MIB,
    )


def soap_rows(cuts, grad, owners, state, low, first, begin=0, end=None):
    total = grad.shape[0]

    def chunk(i, carry):
        rows = pl.ds(pl.multiple_of(i * (total // cuts), 8), total // cuts)
        values = grad[rows, :].astype(F32)
        marks = owners(i * (total // cuts), total // cuts)
        count = len(marks)
        rotated = None
        for m in range(count):
            part = dot((values * marks[m]).astype(BF), low[first + m])
            rotated = part if rotated is None else rotated + part
        new_one, new_two, direction = adam(rotated, state[1, rows, :], state[2, rows, :])
        state[1, rows, :] = new_one
        state[2, rows, :] = new_two
        stepped = None
        for m in range(count):
            part = dot_nt((direction * marks[m]).astype(BF), low[first + m])
            stepped = part if stepped is None else stepped + part
        old = state[0, rows, :]
        state[0, rows, :] = old - LEARN_MATRIX * (stepped + DECAY_MATRIX * old)
        return carry

    lax.fori_loop(begin, cuts if end is None else end, chunk, 0)


def factor_rows(values, identity, turn):
    size, width = values.shape
    sub = lax.broadcasted_iota(jnp.int32, (size, width), 0)
    rolled = pltpu.roll(values, turn, 1)
    columns = [jnp.broadcast_to(rolled[:, j : j + 1], (size, width)) for j in range(size)]
    scale = jnp.zeros((size, width), F32)
    for j in range(size):
        root = lax.rsqrt(columns[j][j : j + 1, :])
        scale = jnp.where(sub == j, root, scale)
        lower = jnp.where(sub > j, columns[j] * root, 0.0)
        values = values - lower * (values[j : j + 1, :] * root)
        identity = identity - lower * (identity[j : j + 1, :] * root)
        for i in range(j + 1, size):
            columns[i] = columns[i] - lower * (columns[i][j : j + 1, :] * root)
    return values * scale, identity * scale


GROUP = 16
PANEL = 128


def upper_blocks(size):
    return [(a, b) for a in range(0, size, PANEL) for b in range(a, size, PANEL)]


def renew_panel(k, product, made, tables, inverses):
    count, size = product.shape[0], product.shape[1]
    here = slice(k * PANEL, (k + 1) * PANEL)
    row = lax.broadcasted_iota(jnp.int32, (PANEL, PANEL), 0)
    col = lax.broadcasted_iota(jnp.int32, (PANEL, PANEL), 1)
    unit = jnp.where(row == col, 1.0, 0.0).astype(F32)
    for n in range(count):
        tables[n][:, :PANEL] = dot3(dot_tn, product[n, :, here], product[n, :, here])
        tables[n][:, PANEL:] = unit

    for first in range(0, PANEL, GROUP):
        rows, rest = slice(first, first + GROUP), slice(first + GROUP, PANEL)
        done = [
            factor_rows(tables[n][rows, :PANEL], tables[n][rows, PANEL:], (PANEL - first) % PANEL)
            for n in range(count)
        ]
        for n in range(count):
            upper, inverse = done[n]
            inverses[n][rows, :] = inverse
            if first + GROUP < PANEL:
                both = jnp.concatenate([upper, inverse], axis=1)
                tables[n][rest, :] = tables[n][rest, :] - dot3(dot_tn, upper[:, rest], both)
    for n in range(count):
        turned = dot3(dot_nt, product[n, :, here], inverses[n][...])
        made[n, :, here] = turned
        if k < size // PANEL - 1:
            rest = slice((k + 1) * PANEL, size)
            product[n, :, rest] = product[n, :, rest] - dot3(
                dot, turned, dot3(dot_tn, turned, product[n, :, rest])
            )


def tail_body(
    tasks, batches, cuts, pieces,
    slots, flow, sums, owners, head_far,
    weight, one, two, head_weight, head_one, head_two, basis, head_basis,
    input_grad, norm_sums, state_new, head_state_new, grams, head_grams,
    grad, part, state, head_state, mine, head_mine, bases, low, head_grad, flow_own,
    flow_in, flow_send, flow_receive, send, receive, sum_send, sum_receive,
    *rest,
):
    row_scratch = [rest[7 * k : 7 * k + 7] for k in range(pieces)]
    gram_scratch, head_scratch, rest = rest[7 * pieces :][:7], rest[7 * pieces + 7 :][:7], rest[7 * pieces + 14 :]
    chip_send, chip_receive, task_send, task_receive, pair_send, pair_receive, load, save = rest
    task = lax.axis_index("task")
    place, core, chips = pair_place(batches)
    width = part.shape[1]
    channels = grad.shape[1]
    pixels = input_grad.shape[0]
    trunk_total = basis.shape[0]
    head_total = head_basis.shape[0]
    count, head_count = mine.shape[0] // batches, head_mine.shape[0] // batches

    def trunk_marks(start, size):
        rows = pl.ds(pl.multiple_of(start, 8), size)
        return [owners[rows, m : m + 1] for m in range(trunk_total)]

    def head_marks(start, size):
        index = lax.broadcasted_iota(jnp.int32, (size, 1), 0) + start
        index = index + lax.axis_index("batch") * head_grad.shape[0]
        owner = jnp.minimum(lax.div(index, channels), head_total - 1)
        return [jnp.where(owner == m, 1.0, 0.0).astype(F32) for m in range(head_total)]

    def put_grams(target, rows, columns, marks):
        for m, mark in enumerate(marks):
            held = (rows[...].astype(F32) * mark).astype(BF)
            target[m * channels : (m + 1) * channels, :] = dot_tn(held, columns[...]).astype(
                target.dtype
            )

    def put_packed_grams(target, rows, marks):
        n = 0
        for mark in marks:
            held = (rows[...].astype(F32) * mark).astype(BF)
            for a, b in upper_blocks(channels):
                block = dot_tn(held[:, a : a + PANEL], rows[:, b : b + PANEL])
                target[n : n + PANEL, :] = block.astype(target.dtype)
                n += PANEL
        if n < target.shape[0]:
            target[n:, :] = jnp.zeros((target.shape[0] - n, PANEL), target.dtype)

    def peer_of(step, incoming):
        return lax.rem(task + (tasks - step if incoming else step), tasks)

    def flow_copy(step, incoming=False):
        peer = peer_of(step, incoming)
        return remote(block_rows(flow, peer, pixels), flow_in.at[step - 1], flow_send.at[step],
                      flow_receive.at[step], peer, "task")

    def sum_copy(step, incoming=False):
        peer = peer_of(step, incoming)
        home = peer if incoming else task
        return remote(sums, norm_sums.at[:, columns_of(home, width)], sum_send.at[step],
                      sum_receive.at[step], peer, "task")

    def part_copy(k, step, incoming=False):
        peer = peer_of(step, incoming)
        home = peer if incoming else task
        return remote(part.at[part_rows(k), :], grad.at[part_rows(k), columns_of(home, width)],
                      send.at[k, step], receive.at[k, step], peer, "task")

    def trunk_block(chip, home, which):
        rows = pl.ds(pl.multiple_of((2 * chip + which) * count, 8), count)
        return grams.at[rows, columns_of(home, width)]

    def head_block(chip, which):
        return block_rows(head_grams, 2 * chip + which, head_count)

    def task_copy(step, hop, incoming=False):
        peer = peer_of(step, incoming)
        chip = lax.rem(place + chips - hop, chips)
        block = trunk_block(chip, peer if incoming else task, core)
        return remote(block, block, task_send.at[step, hop], task_receive.at[step, hop], peer, "task")

    def pair_copy(kind, hop, incoming=False):
        chip = lax.rem(place + chips - hop, chips)
        which = 1 - core if incoming else core
        home = lax.rem(task + tasks - kind, tasks)
        block = head_block(chip, which) if kind == tasks else trunk_block(chip, home, which)
        return remote(block, block, pair_send.at[kind, hop], pair_receive.at[kind, hop],
                      2 * place + 1 - core, "batch")

    def sum_of(source, scratch, piece=0, total=1):
        near, paired, far, *sems = scratch
        return pair_sum(
            batches, *blocks_in(source, batches, near.shape[1], piece, total), near, paired, far, sems
        )

    def part_rows(k):
        size = part.shape[0] // pieces
        return pl.ds(k * size, size)

    moves = [
        (basis, bases.at[pl.ds(0, trunk_total)]),
        (head_basis, bases.at[pl.ds(trunk_total, head_total)]),
        (head_weight, head_state.at[0]),
        (head_one, head_state.at[1]),
        (head_two, head_state.at[2]),
        (weight, state.at[0]),
        (one, state.at[1]),
        (two, state.at[2]),
        (head_far, head_grad),
        (block_rows(flow, task, pixels), flow_own),
    ]
    loads = [pltpu.make_async_copy(a, b, load.at[k]) for k, (a, b) in enumerate(moves)]
    loads[8].start()
    for copy in (*loads[:8], loads[9]):
        copy.start()
    saves = [
        pltpu.make_async_copy(state, state_new, save.at[0]),
        pltpu.make_async_copy(head_state, head_state_new, save.at[1]),
    ]

    greet_pairs(tasks, batches)
    row_sums = [sum_of(slots, row_scratch[k], k, pieces) for k in range(pieces)]
    for stages in row_sums:
        stages[0]()
    for step in range(1, tasks):
        sum_copy(step).start()
        flow_copy(step).start()
    norm_sums[:, columns_of(task, width)] = sums[...]
    row_sums[0][1]()
    loads[8].wait()
    put_packed_grams(head_mine, head_grad, head_marks(0, head_grad.shape[0]))
    head_start, head_middle, head_relay, head_end = sum_of(head_mine, head_scratch)
    row_sums[0][2]()
    for stages in row_sums[1:]:
        stages[1]()
    head_start()
    for stages in row_sums[1:]:
        stages[2]()
    head_middle()
    for copy in loads[:5]:
        copy.wait()
    for m in range(trunk_total + head_total):
        low[m] = bases[m].astype(BF)
    for k, stages in enumerate(row_sums):
        total = stages[3]().astype(BF)
        part[part_rows(k), :] = total
        for step in range(1, tasks):
            part_copy(k, step).start()
        grad[part_rows(k), columns_of(task, width)] = total
    head_relay()

    soap_rows(cuts, head_grad, head_marks, head_state, low, trunk_total)
    saves[1].start()
    loads[9].wait()
    total = flow_own[...].astype(F32)
    for step in range(1, tasks):
        flow_copy(step, True).wait_recv()
        total = total + flow_in[step - 1].astype(F32)
    input_grad[...] = total
    head_block(place, core)[...] = head_end().astype(head_grams.dtype)
    trunk_spread = chip_spread(
        batches, lambda chip: trunk_block(chip, task, core), chip_send.at[0], chip_receive.at[0]
    )
    head_spread = chip_spread(
        batches, lambda chip: head_block(chip, core), chip_send.at[1], chip_receive.at[1]
    )
    head_spread[0]()
    pair_copy(tasks, 0).start()
    for k in range(pieces):
        for step in range(1, tasks):
            part_copy(k, step, True).wait_recv()

    put_grams(mine, grad, part, trunk_marks(0, grad.shape[0]))
    start, middle, relay, end = sum_of(mine, gram_scratch)
    start()
    middle()
    head_spread[1]()
    for copy in loads[5:8]:
        copy.wait()
    relay()
    soap_rows(cuts, grad, trunk_marks, state, low, 0, 0, cuts // 2)
    trunk_block(place, task, core)[...] = end().astype(grams.dtype)
    trunk_spread[0]()
    for step in range(1, tasks):
        task_copy(step, 0).start()
    pair_copy(0, 0).start()
    soap_rows(cuts, grad, trunk_marks, state, low, 0, cuts // 2, cuts)
    saves[0].start()
    trunk_spread[1]()
    trunk_spread[2]()
    for hop in range(1, chips):
        for step in range(1, tasks):
            task_copy(step, hop).start()
        pair_copy(0, hop).start()
    head_spread[2]()
    for hop in range(1, chips):
        pair_copy(tasks, hop).start()
    for hop in range(chips):
        for step in range(1, tasks):
            task_copy(step, hop, True).wait_recv()
            pair_copy(step, hop).start()
    for hop in range(chips):
        for kind in range(tasks + 1):
            pair_copy(kind, hop, True).wait_recv()
    for step in range(1, tasks):
        sum_copy(step, True).wait_recv()

    for copy in saves:
        copy.wait()
    for step in range(1, tasks):
        sum_copy(step).wait_send()
        for k in range(pieces):
            part_copy(k, step).wait_send()
        flow_copy(step).wait_send()
    for hop in range(chips):
        for kind in range(tasks + 1):
            pair_copy(kind, hop).wait_send()
        for step in range(1, tasks):
            task_copy(step, hop).wait_send()
    trunk_spread[3]()
    head_spread[3]()


def renew_body(
    core, state, head_state, grams, head_grams, stat, head_stat, basis, head_basis,
    weight_new, one_new, two_new, head_weight_new, head_one_new, head_two_new,
    stat_new, head_stat_new, low_made,
    stats, product, made, low_grams, low_head_grams, held, head_held, load, save, *work,
):
    trunk_total, head_total = stat.shape[0], head_stat.shape[0]
    channels = stat.shape[1]
    count = trunk_total + head_total
    shared = product.shape[0]
    tables, inverses = work[:shared], work[shared:]
    loads = []
    blocks = upper_blocks(channels)
    packed = len(blocks) * PANEL

    def gram_rows(m, start):
        if m < trunk_total:
            first = m * channels + start
            return low_grams[first : first + PANEL, :].astype(F32)
        parts = []
        for b in range(0, channels, PANEL):
            n = blocks.index((min(start, b), max(start, b)))
            first = (m - trunk_total) * packed + n * PANEL
            block = low_head_grams[first : first + PANEL, :].astype(F32)
            parts.append(block if b >= start else block.T)
        return jnp.concatenate(parts, axis=1)

    def bring(source, target):
        copy = pltpu.make_async_copy(source, target, load.at[len(loads)])
        loads.append(copy)
        return copy

    for m in range(count):
        first = m < trunk_total
        place = m if first else m - trunk_total
        size = channels if first else packed
        rows = pl.ds(place * size, size)
        here, there = (grams, low_grams) if first else (head_grams, low_head_grams)
        bring(here.at[rows, :], there.at[rows, :]).start()
        bring((stat if first else head_stat).at[place], stats.at[m]).start()

    for n in range(shared):
        both = [
            basis.at[n] if n < trunk_total else head_basis.at[n - trunk_total],
            head_basis.at[n],
        ]
        copy = bring(both[1], made.at[n])
        for which, source in enumerate(both):

            @pl.when(core[0] == which)
            def _():
                pltpu.make_async_copy(source, made.at[n], load.at[2 * count + n]).start()

    bring(state, held).start()
    bring(head_state, head_held).start()
    sources = [held.at[k] for k in range(3)] + [head_held.at[k] for k in range(3)]
    targets = [weight_new, one_new, two_new, head_weight_new, head_one_new, head_two_new]
    saves = [pltpu.make_async_copy(a, b, save.at[k]) for k, (a, b) in enumerate(zip(sources, targets))]
    for m in range(count):
        for copy in loads[2 * m : 2 * m + 2]:
            copy.wait()
        for start in range(0, channels, PANEL):
            rows = slice(start, start + PANEL)
            stats[m, rows, :] = STAT_DECAY * stats[m, rows, :] + (1.0 - STAT_DECAY) * gram_rows(m, start)
    for begin, size, out in ((0, trunk_total, stat_new), (trunk_total, head_total, head_stat_new)):
        copy = pltpu.make_async_copy(stats.at[pl.ds(begin, size)], out, save.at[len(saves)])
        copy.start()
        saves.append(copy)
    for n in range(shared):
        loads[2 * count + n].wait()
        product[n] = dot3(dot, stats[trunk_total * core[0] + n], made[n])
    for k in range(channels // PANEL):
        renew_panel(k, product, made, tables, inverses)
        if k == 0:
            for copy in loads[2 * count + shared :]:
                copy.wait()
            for copy in saves[:6]:
                copy.start()
        cut = slice(k * PANEL, (k + 1) * PANEL)
        low_made[:, :, cut] = made[:, :, cut].astype(BF)
    for copy in saves:
        copy.wait()


def swap_body(batches, x, out, sends, receives):
    place, core, _ = pair_place(batches)
    other = 2 * place + 1 - core
    barrier = pltpu.get_barrier_semaphore()
    pl.semaphore_signal(barrier, inc=1, device_id={"batch": other}, device_id_type=MESH)
    pl.semaphore_wait(barrier, 1)
    copy = remote(x, out, sends, receives, other, "batch")
    copy.start()
    copy.wait()


def finish(tasks, batches, local_grads, rows, matrices):
    slots, flow, sums, owners, head_grad = local_grads
    stat, head_stat, basis, head_basis = matrices
    total, channels = rows[0].shape
    width = channels // tasks
    trunk_total, head_total = basis.shape[0], head_basis.shape[0]
    gram_rows = trunk_total * channels
    packed = len(upper_blocks(channels)) * PANEL
    head_rows = -(-head_total * packed // (16 * batches)) * 16 * batches
    chips = batches // 2
    kind = BF if gram_rows % (16 * batches) == 0 else F32
    cuts = 4 if total % 64 == 0 and head_grad.shape[0] % 64 == 0 else 1
    pieces = 2 if total % 64 == 0 else 1
    square = (trunk_total + head_total, channels, channels)
    pixels = flow.shape[0] // tasks
    input_grad, norm_sums, *made = exchange_kernel(
        functools.partial(tail_body, tasks, batches, cuts, pieces),
        [
            shape((pixels, channels), F32),
            shape((8, channels), F32),
            shape((3, total, channels), F32),
            shape((3,) + head_grad.shape, F32),
            shape((gram_rows, channels), kind),
            shape((head_rows, PANEL), BF),
        ],
        "vhvvhhhhhhhhh",
        (*local_grads, *rows, basis, head_basis),
        [
            pltpu.VMEM((total, channels), BF),
            pltpu.VMEM((total, width), BF),
            pltpu.VMEM((3, total, channels), F32),
            pltpu.VMEM((3,) + head_grad.shape, F32),
            pltpu.VMEM((gram_rows, width), kind),
            pltpu.VMEM((head_rows, PANEL), BF),
            pltpu.VMEM(square, F32),
            pltpu.VMEM(square, BF),
            pltpu.VMEM(head_grad.shape, BF),
            pltpu.VMEM((pixels, channels), BF),
            pltpu.VMEM((tasks - 1, pixels, channels), BF),
        ]
        + [pltpu.SemaphoreType.DMA((tasks,))] * 2
        + [pltpu.SemaphoreType.DMA((pieces, tasks))] * 2
        + [pltpu.SemaphoreType.DMA((tasks,))] * 2
        + pair_scratch(batches, slots.shape[0] // pieces, width, BF) * pieces
        + pair_scratch(batches, gram_rows, width, kind)
        + pair_scratch(batches, head_rows, PANEL, BF)
        + [pltpu.SemaphoreType.DMA((2, max(chips, 4)))] * 2
        + [pltpu.SemaphoreType.DMA((tasks, chips))] * 2
        + [pltpu.SemaphoreType.DMA((tasks + 1, chips))] * 2
        + [pltpu.SemaphoreType.DMA((10,)), pltpu.SemaphoreType.DMA((2,))],
        5,
        60,
        flops=50000 * MIB,
        places_out="vvhhvv",
    )
    outs = [shape(a.shape, F32) for a in (*rows, *matrices)]
    hbm = pl.BlockSpec(memory_space=pltpu.HBM)
    count = trunk_total + head_total
    shared = max(trunk_total, head_total)
    core = lax.rem(lax.axis_index("batch"), 2)
    own = (shared, channels, channels)
    *results, made_low = pl.pallas_call(
        renew_body,
        out_shape=(*outs[:8], shape(own, BF)),
        in_specs=[SMEM_SPEC] + [hbm] * 8,
        out_specs=(*(hbm for _ in outs[:8]), VMEM_SPEC),
        scratch_shapes=[pltpu.VMEM(square, F32)]
        + [pltpu.VMEM(own, F32)] * 2
        + [pltpu.VMEM(made[2].shape, kind), pltpu.VMEM(made[3].shape, BF)]
        + [pltpu.VMEM(made[0].shape, F32), pltpu.VMEM(made[1].shape, F32)]
        + [pltpu.SemaphoreType.DMA((2 * count + shared + 2,))]
        + [pltpu.SemaphoreType.DMA((8,))]
        + [pltpu.VMEM((PANEL, 2 * PANEL), F32)] * shared
        + [pltpu.VMEM((PANEL, PANEL), F32)] * shared,
        compiler_params=pltpu.CompilerParams(vmem_limit_bytes=60 * MIB),
        cost_estimate=pl.CostEstimate(
            flops=50000 * MIB, bytes_accessed=64 * MIB, transcendentals=0
        ),
    )(core.reshape(1), *made, *matrices)
    theirs = exchange_kernel(
        functools.partial(swap_body, batches),
        [shape(own, BF)],
        "v",
        (made_low,),
        [pltpu.SemaphoreType.DMA] * 2,
        6,
        60,
        flops=5000 * MIB,
    )[0]
    results += [
        jnp.where(core == which, made_low[:total], theirs[:total]).astype(F32)
        for which, total in enumerate((trunk_total, head_total))
    ]
    return input_grad, norm_sums, results


def local(
    tasks,
    batches,
    images,
    image_small,
    pool_index,
    row_slot,
    trunk_weight,
    trunk_mean_grad,
    trunk_mean_square,
    trunk_statistic,
    trunk_basis,
    head_weight,
    head_mean_grad,
    head_mean_square,
    head_statistic,
    head_basis,
    trunk_gain,
    trunk_offset,
    trunk_norm_mean_grad,
    trunk_norm_mean_square,
    head_gain,
    head_offset,
    head_norm_mean_grad,
    head_norm_mean_square,
    cotangent,
):
    number, height, breadth, channels = images.shape
    pixels = height * breadth
    shown = tasks * number
    geometry = (shown, height, breadth)
    task = lax.axis_index("task")
    width = channels // tasks

    def quarter(values):
        return lax.dynamic_slice_in_dim(values, task * width, width, values.ndim - 1)

    def inside(flags):
        row_limit = jnp.where(flags > 0, height // 2, height)[:, None, None]
        col_limit = jnp.where(flags > 0, breadth // 2, breadth)[:, None, None]
        return (jnp.arange(height, dtype=jnp.int32)[None, :, None] < row_limit) & (
            jnp.arange(breadth, dtype=jnp.int32)[None, None, :] < col_limit
        )

    cell = 2 * jnp.arange(2, dtype=jnp.int32)[:, None, None] + jnp.arange(2, dtype=jnp.int32)
    cells = pool_index.reshape(number, height // 2, 1, breadth // 2, 1)
    valid = inside(image_small)
    chosen = ((cells == cell).reshape(number, height, breadth) & valid).reshape(number, pixels)
    info = jnp.zeros((8 * number, channels), F32)
    info = info.at[::8, :pixels].set(chosen.astype(F32))
    info = info.at[1::8, 0].set(image_small.astype(F32))
    slots, x, infos, trunk_owners, head_low = arrive(
        tasks, batches, (number, height, breadth), images.reshape(number * pixels, channels),
        info, row_slot, trunk_weight, head_weight[0],
    )
    head_rows = lax.all_gather(head_low, "batch", axis=0, tiled=True)

    scales = quarter(jnp.stack([trunk_gain, trunk_offset], axis=1)).reshape(4, width)
    enc_totals, dec_totals, features, *kept = trunk_forward(
        geometry, tasks, batches, row_slot, infos, x, slots, scales
    )
    head_scales = jnp.stack([head_gain[0], head_offset[0]], axis=1).reshape(6, channels)
    pooled, upstream, head_sums, head_owned = head(
        geometry, tasks, batches, infos, features, head_rows,
        cotangent.reshape(shown, pixels // 4, channels), head_scales, enc_totals,
    )
    task_features = pooled.reshape(cotangent.shape)
    enc_grad, dec_grad, flow, trunk_sums = trunk_backward(
        geometry, tasks, batches, infos, upstream, enc_totals, dec_totals, scales, (x, *kept)
    )
    input_grad, norm_sums, results = finish(
        tasks, batches,
        (to_slots(row_slot, enc_grad, dec_grad), flow, trunk_sums, trunk_owners, head_owned),
        (trunk_weight, trunk_mean_grad, trunk_mean_square,
         head_weight[0], head_mean_grad[0], head_mean_square[0]),
        (trunk_statistic, head_statistic[0], trunk_basis, head_basis[0]),
    )
    input_grad = input_grad.reshape(images.shape)
    (
        trunk_weight_new, trunk_one_new, trunk_two_new,
        head_weight_new, head_one_new, head_two_new,
        trunk_stat_new, head_stat_new, trunk_basis_new, head_basis_new,
    ) = results

    trunk_norm = jnp.stack([trunk_gain, trunk_offset], axis=1)
    trunk_norm_grad = norm_sums[:4].reshape(2, 2, channels)[:, ::-1]
    trunk_norm_one, trunk_norm_two, trunk_direction = adam(
        trunk_norm_grad, trunk_norm_mean_grad, trunk_norm_mean_square
    )
    head_norm = jnp.stack([head_gain, head_offset], axis=2)
    head_norm_grad = head_sums[:6].reshape(1, 3, 2, channels)[:, :, ::-1]
    head_norm_one, head_norm_two, head_direction = adam(
        head_norm_grad, head_norm_mean_grad, head_norm_mean_square
    )
    return (
        task_features,
        input_grad,
        trunk_weight_new,
        trunk_one_new,
        trunk_two_new,
        trunk_stat_new,
        trunk_basis_new,
        head_weight_new[None],
        head_one_new[None],
        head_two_new[None],
        head_stat_new[None],
        head_basis_new[None],
        trunk_norm - LEARN_NORM * trunk_direction,
        trunk_norm_one,
        trunk_norm_two,
        head_norm - LEARN_NORM * head_direction,
        head_norm_one,
        head_norm_two,
    )


def solution(mesh):
    placed = (
        P(("task", "batch"), None, None, None),
        P(("task", "batch")),
        P(("task", "batch"), None, None),
        P(),
        P("batch", None),
        P("batch", None),
        P("batch", None),
        P(),
        P(),
        P("task", "batch", None),
        P("task", "batch", None),
        P("task", "batch", None),
        P("task", None, None, None),
        P("task", None, None, None),
        P(),
        P(),
        P(),
        P(),
        P("task", None, None),
        P("task", None, None),
        P("task", None, None, None),
        P("task", None, None, None),
        P("task", None, "batch", None, None, None),
    )
    return jax.shard_map(
        functools.partial(local, mesh.shape["task"], mesh.shape["batch"]),
        mesh=mesh,
        in_specs=placed,
        out_specs=(
            P("task", None, "batch", None, None, None),
            P(("task", "batch"), None, None, None),
            P("batch", None),
            P("batch", None),
            P("batch", None),
            P(),
            P(),
            P("task", "batch", None),
            P("task", "batch", None),
            P("task", "batch", None),
            P("task", None, None, None),
            P("task", None, None, None),
            P(),
            P(),
            P(),
            P("task", None, None, None),
            P("task", None, None, None),
            P("task", None, None, None),
        ),
        check_vma=False,
    )
```

```python
import functools

import jax
import jax.numpy as jnp
from jax import lax
from jax.experimental import pallas as pl
from jax.experimental.pallas import tpu as pltpu
from jax.sharding import PartitionSpec as P

STEP = 10


EPS = 1e-05
ADAM_EPS = 1e-08
BETA_ONE = 0.95
BETA_TWO = 0.95
STAT_DECAY = 0.95
LEARN_MATRIX = 0.02
LEARN_NORM = 0.5
DECAY_MATRIX = 0.01
BF = jnp.bfloat16
F32 = jnp.float32
MESH = pl.DeviceIdType.MESH
MIB = 1 << 20

VMEM_SPEC = pl.BlockSpec(memory_space=pltpu.VMEM)
SMEM_SPEC = pl.BlockSpec(memory_space=pltpu.SMEM)


def run(body, outs, specs, args, scratch=(), vmem=40, flops=0):
    size = sum(o.size * o.dtype.itemsize for o in outs) + sum(a.size * a.dtype.itemsize for a in args)
    return pl.pallas_call(
        body,
        out_shape=tuple(outs),
        in_specs=[SMEM_SPEC if s == "s" else VMEM_SPEC for s in specs],
        out_specs=tuple(VMEM_SPEC for _ in outs),
        scratch_shapes=list(scratch),
        compiler_params=pltpu.CompilerParams(vmem_limit_bytes=vmem * MIB),
        cost_estimate=pl.CostEstimate(flops=flops, bytes_accessed=size, transcendentals=0),
    )(*args)


def shape(dims, kind):
    return jax.ShapeDtypeStruct(tuple(dims), kind)


def dot(a, b):
    return jnp.dot(a, b, preferred_element_type=F32)


def dot_nt(a, b):
    return lax.dot_general(a, b, (((1,), (1,)), ((), ())), preferred_element_type=F32)


def dot_tn(a, b):
    return lax.dot_general(a, b, (((0,), (0,)), ((), ())), preferred_element_type=F32)


def split(a):
    high = a.astype(BF)
    return high, (a - high.astype(F32)).astype(BF)


def dot3(kind, a, b):
    dims = {dot: (1, 0), dot_nt: (1, 1), dot_tn: (0, 0)}[kind]
    a_high, a_low = split(a)
    b_high, b_low = split(b)
    return kind(
        jnp.concatenate([a_high, a_high, a_low], axis=dims[0]),
        jnp.concatenate([b_high, b_low, b_high], axis=dims[1]),
    )


def places(height, breadth):
    index = lax.broadcasted_iota(jnp.int32, (height * breadth, 1), 0)
    row = lax.div(index, breadth)
    return row, index - row * breadth


def valid_rows(kind, height, breadth, spot):
    row, col = spot
    shrunk = kind > 0
    row_limit = jnp.where(shrunk, height // 2, height)
    col_limit = jnp.where(shrunk, breadth // 2, breadth)
    return jnp.where((row < row_limit) & (col < col_limit), 1.0, 0.0).astype(F32)


def move(values, rows):
    gap = jnp.zeros((abs(rows),) + values.shape[1:], values.dtype)
    if rows > 0:
        return jnp.concatenate([gap, values[:-rows]], axis=0)
    return jnp.concatenate([values[-rows:], gap], axis=0)


def from_left(values, col):
    return jnp.where(col > 0, pltpu.roll(values, 1, 0), 0.0)


def from_right(values, col, breadth):
    return jnp.where(col < breadth - 1, pltpu.roll(values, values.shape[0] - 1, 0), 0.0)


def gather_taps(tap, breadth, col):
    lines = [move(tap(b), breadth) + tap(3 + b) + move(tap(6 + b), -breadth) for b in range(3)]
    return lines[1] + from_left(lines[0], col) + from_right(lines[2], col, breadth)


def spread_taps(values, breadth, col):
    lines = [from_right(values, col, breadth), values, from_left(values, col)]
    return [
        move(lines[b], breadth * (a - 1)) if a != 1 else lines[b] for a in range(3) for b in range(3)
    ]


def window_sum(values, row, col, breadth):
    count = values.shape[0]
    pair = values + jnp.where(
        col % 2 == 0, pltpu.roll(values, count - 1, 0), pltpu.roll(values, 1, 0)
    )
    return pair + jnp.where(row % 2 == 0, move(pair, -breadth), move(pair, breadth))


def sigmoid(values):
    return 0.5 * jnp.tanh(0.5 * values) + 0.5


def silu_back(scaled):
    sig = sigmoid(scaled)
    return sig * (1.0 + scaled * (1.0 - sig))


def col_sum(values):
    return jnp.sum(values, axis=0, keepdims=True)


def put_sums(ref, rows):
    width = ref.shape[1]
    rows = list(rows) + [jnp.zeros((1, width), F32)] * (8 - len(rows))
    ref[...] = jnp.concatenate(rows, axis=0)


def each_image(geometry, body, start):
    number, height, breadth = geometry
    pixels = height * breadth

    def step(image, carry):
        return body(image, pl.ds(pl.multiple_of(image * pixels, 16), pixels), carry)

    return lax.fori_loop(0, number, step, start)


def zero_rows(count, width):
    return (jnp.zeros((1, width), F32),) * count


def greet(axes):
    barrier = pltpu.get_barrier_semaphore()
    for axis, size in axes:
        me = lax.axis_index(axis)
        for step in range(1, size):
            pl.semaphore_signal(
                barrier, inc=1, device_id={axis: lax.rem(me + step, size)}, device_id_type=MESH
            )
    pl.semaphore_wait(barrier, sum(size - 1 for _, size in axes))


def remote(source, target, sends, receives, peer, axis):
    return pltpu.make_async_remote_copy(
        src_ref=source,
        dst_ref=target,
        send_sem=sends,
        recv_sem=receives,
        device_id={axis: peer},
        device_id_type=MESH,
    )


def pack(rows):
    parts = [row[:, i : i + 128] for row in rows for i in range(0, row.shape[1], 128)]
    parts += [jnp.zeros((1, 128), F32)] * (8 - len(parts))
    return jnp.concatenate(parts, axis=0)


def unpack(tile, count, width):
    per = width // 128
    return [
        jnp.concatenate([tile[k * per + i : k * per + i + 1, :] for i in range(per)], axis=1)
        for k in range(count)
    ]


def total_rows(k, axis, size, rows, mine, slots, sends, receives, meanwhile=None):
    me = lax.axis_index(axis)
    tile = pack(rows)
    mine[k] = tile
    slots[k, me] = tile
    for step in range(1, size):
        peer = lax.rem(me + step, size)
        remote(mine.at[k], slots.at[k, me], sends.at[k, step], receives.at[k, me], peer, axis).start()
    if meanwhile:
        meanwhile()
    for step in range(1, size):
        peer = lax.rem(me + size - step, size)
        remote(
            mine.at[k], slots.at[k, peer], sends.at[k, step], receives.at[k, peer], peer, axis
        ).wait_recv()
    total = slots[k, 0]
    for peer in range(1, size):
        total = total + slots[k, peer]
    for step in range(1, size):
        peer = lax.rem(me + step, size)
        remote(
            mine.at[k], slots.at[k, me], sends.at[k, step], receives.at[k, me], peer, axis
        ).wait_send()
    return unpack(total, len(rows), rows[0].shape[1])


def total_scratch(count, size):
    return [
        pltpu.VMEM((count, 8, 128), F32),
        pltpu.VMEM((count, size, 8, 128), F32),
        pltpu.SemaphoreType.DMA((count, size)),
        pltpu.SemaphoreType.DMA((count, size)),
    ]


def columns_of(place, width):
    return pl.ds(pl.multiple_of(place * width, 128), width)


SPECS = {"s": SMEM_SPEC, "v": VMEM_SPEC, "h": pl.BlockSpec(memory_space=pltpu.HBM)}


def exchange_kernel(body, outs, specs, args, scratch, identity, vmem, flops=0, places_out=None):
    size = sum(o.size * o.dtype.itemsize for o in outs) + sum(a.size * a.dtype.itemsize for a in args)
    return pl.pallas_call(
        body,
        out_shape=tuple(outs),
        in_specs=[SPECS[s] for s in specs],
        out_specs=tuple(SPECS[s] for s in places_out or "v" * len(outs)),
        scratch_shapes=list(scratch),
        compiler_params=pltpu.CompilerParams(
            vmem_limit_bytes=vmem * MIB, collective_id=identity, has_side_effects=True
        ),
        cost_estimate=pl.CostEstimate(flops=flops, bytes_accessed=size, transcendentals=0),
    )(*args)


def info_rows(infos, i):
    return infos[pl.ds(pl.multiple_of(i * 8, 8), 8), :]


def valid_of(infos, i, height, breadth, spot):
    return valid_rows(info_rows(infos, i)[1:2, 0:1], height, breadth, spot)


def chosen_cells(narrow, infos, i):
    return (narrow * info_rows(infos, i)[0:1, : narrow.shape[1]]).astype(BF)


def norm_moments(totals):
    total, squares, count = totals
    center = total / count
    return center, lax.rsqrt(squares / count - center * center + EPS)


def norm_line(totals, scale):
    center, inverse = norm_moments(totals)
    slope = inverse * scale[0]
    return slope, scale[1] - center * slope


def norm_sums(totals, sums):
    center, inverse = norm_moments(totals)
    return [sums[0], inverse * (sums[1] - center * sums[0])]


def norm_back_line(totals, sums, scale):
    center, inverse = norm_moments(totals)
    count = totals[2]
    slope = inverse * scale[0]
    lean = -slope * inverse * (sums[1] / count)
    return slope, lean, -slope * (sums[0] / count) - lean * center


def on_line(values, line):
    return values * line[0] + line[1]


def back_on_line(upstream, values, line, valid):
    return (upstream * line[0] + values * line[1] + line[2]) * valid


def silu(values):
    return values * sigmoid(values)


def window_count(height, breadth):
    return -(-(height * breadth // 4) // 16) * 16


def pool_choice(height, breadth, windows, flipped):
    pixels = height * breadth
    dims = (windows, pixels) if flipped else (pixels, windows)
    pixel = lax.broadcasted_iota(jnp.int32, dims, 1 if flipped else 0)
    window = lax.broadcasted_iota(jnp.int32, dims, 0 if flipped else 1)
    row = lax.div(pixel, breadth)
    col = pixel - row * breadth
    home = lax.div(row, 2) * (breadth // 2) + lax.div(col, 2)
    return jnp.where(home == window, 1.0, 0.0).astype(F32)


def rows_of(ref, first, count):
    return [ref[first + k : first + k + 1, :] for k in range(count)]


def window_rows(i, windows):
    return pl.ds(pl.multiple_of(i * windows, 16), windows)


def trunk_forward_body(
    geometry, tasks, batches,
    index, infos, x_far, kernel_slots, scales,
    enc_totals, dec_totals, features, *rest,
):
    kept, (enc_pre, dec_pre, spread), rest = rest[:5], rest[5:8], rest[8:]
    (
        x, x_loaded, enc_taps, dec_taps, wide, tap,
        work, pooled, pooled_all, part, pool_sends, pool_receives, sends, receives,
    mine, slots, total_sends, total_receives, saved,
    ) = rest
    number, height, breadth = geometry
    width = enc_pre.shape[1]
    windows = window_count(height, breadth)
    task = lax.axis_index("task")
    spot = places(height, breadth)
    _, col = spot
    choice = pool_choice(height, breadth, windows, True)
    narrow = choice.astype(BF)

    x_load = pltpu.make_async_copy(x_far, x, x_loaded)
    x_load.start()
    sources = (enc_taps, dec_taps, enc_pre, dec_pre, spread)
    saves = [pltpu.make_async_copy(a, b, saved.at[k]) for k, (a, b) in enumerate(zip(sources, kept))]
    channels = x.shape[1]

    def widen(i, carry):
        rows = pl.ds(pl.multiple_of(i * channels, 16), channels)
        wide[rows, :] = kernel_slots[rows, :].astype(F32)
        return carry

    def fetch(taps, first, begin, end):
        group = 32
        for p in range(begin, end):

            def some(i, carry):
                base = i * group
                for u in range(group):
                    slot = index[(first + p) * channels + base + u]
                    tap[pl.ds(base + u, 1), :] = wide[pl.ds(slot, 1), :]
                return carry

            lax.fori_loop(0, channels // group, some, 0)
            taps[:, p * width : (p + 1) * width] = tap[...].astype(BF)

    lax.fori_loop(0, wide.shape[0] // channels, widen, 0)
    fetch(enc_taps, 0, 0, 9)
    saves[0].start()
    x_load.wait()

    def conv(x, taps, pre):
        def image(i, rows, carry):
            valid = valid_of(infos, i, height, breadth, spot)
            work[...] = dot(x[rows, :], taps[...])
            out = gather_taps(lambda p: work[:, p * width : (p + 1) * width], breadth, col)
            pre[rows, :] = out
            kept = out * valid
            return (
                carry[0] + col_sum(kept),
                carry[1] + col_sum(kept * out),
                carry[2] + jnp.broadcast_to(col_sum(valid), (1, width)),
            )

        return each_image(geometry, image, zero_rows(3, width))

    def total(k, rows, meanwhile=None):
        return total_rows(
            k, "batch", batches, list(rows), mine, slots, total_sends, total_receives, meanwhile
        )

    sums = conv(x, enc_taps, enc_pre)
    saves[2].start()
    greet((("task", tasks), ("batch", batches)))
    totals = total(0, sums, lambda: fetch(dec_taps, 9, 0, 4))
    put_sums(enc_totals, totals)
    scale = rows_of(scales, 0, 2)

    def peer_of(step, incoming):
        return lax.rem(task + (tasks - step if incoming else step), tasks)

    def pool_copy(i, step, incoming=False):
        rows = window_rows(i, windows)
        peer = peer_of(step, incoming)
        target = pooled_all.at[rows, columns_of(peer if incoming else task, width)]
        return remote(
            pooled.at[rows, :], target, pool_sends.at[i, step], pool_receives.at[i, step], peer, "task"
        )

    line = norm_line(totals, scale)

    def pool(i, rows, carry):
        valid = valid_of(infos, i, height, breadth, spot)
        scaled = on_line(enc_pre[rows, :], line)
        high, low = split(silu(scaled) * valid)
        mean = ((dot(narrow, high) + dot(narrow, low)) * 0.25).astype(BF)
        here = window_rows(i, windows)
        pooled[here, :] = mean
        pooled_all[here, columns_of(task, width)] = mean
        for step in range(1, tasks):
            pool_copy(i, step).start()
        return carry

    each_image(geometry, pool, 0)
    fetch(dec_taps, 9, 4, 9)
    saves[1].start()

    def unpool(i, rows, carry):
        for step in range(1, tasks):
            pool_copy(i, step, True).wait_recv()
        wide = dot_tn(chosen_cells(choice, infos, i), pooled_all[window_rows(i, windows), :])
        spread[rows, :] = wide.astype(BF)
        return carry

    each_image(geometry, unpool, 0)
    saves[4].start()
    sums = conv(spread, dec_taps, dec_pre)
    saves[3].start()
    totals = total(1, sums)
    put_sums(dec_totals, totals)
    scale = rows_of(scales, 2, 2)

    def feature_copy(i, rows, step, incoming=False):
        peer = peer_of(step, incoming)
        target = features.at[rows, columns_of(peer if incoming else task, width)]
        return remote(
            part.at[rows, :], target, sends.at[i, step], receives.at[i, step], peer, "task"
        )

    last_line = norm_line(totals, scale)

    def finish(i, rows, carry):
        valid = valid_of(infos, i, height, breadth, spot)
        scaled = on_line(dec_pre[rows, :], last_line)
        low = (silu(scaled) * valid).astype(BF)
        part[rows, :] = low
        features[rows, columns_of(task, width)] = low
        for step in range(1, tasks):
            feature_copy(i, rows, step).start()
        return carry

    each_image(geometry, finish, 0)

    def settle(i, rows, carry):
        for step in range(1, tasks):
            feature_copy(i, rows, step, True).wait_recv()
            feature_copy(i, rows, step).wait_send()
            pool_copy(i, step).wait_send()
        return carry

    each_image(geometry, settle, 0)
    for copy in saves:
        copy.wait()


def trunk_forward(geometry, tasks, batches, index, infos, x, kernel_slots, scales):
    number, height, breadth = geometry
    pixels = height * breadth
    channels = x.shape[1]
    width = channels // tasks
    windows = window_count(height, breadth)
    tall = shape((x.shape[0], width), F32)
    taps = shape((channels, 9 * width), BF)
    outs = [
        shape((8, width), F32), shape((8, width), F32), shape(x.shape, BF),
        taps, taps,
        tall, tall, shape(x.shape, BF),
    ]
    return exchange_kernel(
        functools.partial(trunk_forward_body, geometry, tasks, batches),
        outs,
        "svhvv",
        (index, infos, x, kernel_slots, scales),
        [
            pltpu.VMEM(tall.shape, F32),
            pltpu.VMEM(tall.shape, F32),
            pltpu.VMEM(x.shape, BF),
            pltpu.VMEM(x.shape, BF),
            pltpu.SemaphoreType.DMA,
            pltpu.VMEM(taps.shape, BF),
            pltpu.VMEM(taps.shape, BF),
            pltpu.VMEM(kernel_slots.shape, F32),
            pltpu.VMEM((channels, width), F32),
            pltpu.VMEM((pixels, 9 * width), F32),
            pltpu.VMEM((number * windows, width), BF),
            pltpu.VMEM((number * windows, channels), BF),
            pltpu.VMEM((x.shape[0], width), BF),
        ]
        + [pltpu.SemaphoreType.DMA((number, tasks))] * 4
        + total_scratch(2, batches)
        + [pltpu.SemaphoreType.DMA((5,))],
        1,
        60,
        flops=4 * x.size * taps.shape[1],
        places_out="vvvhhhhh",
    )


def head_body(
    geometry, tasks, batches, summing,
    infos, features, weights, cotangent, scales, counts,
    task_out, upstream, sums_out, *rest,
):
    grads_out, rest = rest[0], rest[1:]
    (
        grads, pre_one, pre_two, pre_three, hidden, gated, nine, work, lower, out, arrived,
        sends, receives, mine, slots, total_sends, total_receives, loaded,
    ) = rest[:18]
    number, height, breadth = geometry
    channels = features.shape[1]
    width = channels // tasks
    windows = task_out.shape[1]
    task = lax.axis_index("task")
    half = work.shape[2]
    spot = places(height, breadth)
    _, col = spot
    widen = pool_choice(height, breadth, windows, False).astype(BF)
    narrow = pool_choice(height, breadth, windows, True).astype(BF)
    count = jnp.broadcast_to(counts[2:3, 0:1], (1, channels))
    cuts = (pl.ds(0, 2 * channels), pl.ds(2 * channels, 9 * channels))
    loads = [
        pltpu.make_async_copy(weights.at[cut, :], grads.at[cut, :], loaded.at[k])
        for k, cut in enumerate(cuts)
    ]
    for copy in loads:
        copy.start()
    first = grads.at[pl.ds(0, channels), :]
    second = grads.at[pl.ds(channels, channels), :]

    def kernel_rows(p):
        return pl.ds((2 + p) * channels, channels)

    def total(k, rows, meanwhile=None):
        return total_rows(
            k, "batch", batches, list(rows), mine, slots, total_sends, total_receives, meanwhile
        )

    if summing:
        near, near_sends, near_receives, summed, saved = rest[18:]
        place, core, chips = pair_place(batches)
        block = near.shape[1]

        def near_copy(chip):
            return remote(
                block_rows(grads, 2 * chip + 1 - core, block), near.at[chip],
                near_sends.at[chip], near_receives.at[chip], 2 * place + 1 - core, "batch",
            )

    def put_stats(pre, rows, value, valid, carry):
        pre[rows, :] = value
        kept = value * valid
        return carry[0] + col_sum(kept), carry[1] + col_sum(kept * value)

    nothing = zero_rows(2, channels)
    scale_one, scale_two, scale_three = (rows_of(scales, 2 * k, 2) for k in range(3))

    loads[0].wait()

    def first_step(i, rows, carry):
        valid = valid_of(infos, i, height, breadth, spot)
        return put_stats(pre_one, rows, dot(features[rows, :], first[...]), valid, carry)

    sums = each_image(geometry, first_step, nothing)
    greet((("task", tasks), ("batch", batches)))
    totals_one = total(0, sums) + [count]

    line_one = norm_line(totals_one, scale_one)

    def second_step(i, rows, carry):
        valid = valid_of(infos, i, height, breadth, spot)
        scaled = on_line(pre_one[rows, :], line_one)
        low = (silu(scaled) * valid).astype(BF)
        hidden[rows, :] = low
        return put_stats(pre_two, rows, dot(low, second[...]), valid, carry)

    sums = each_image(geometry, second_step, nothing)
    totals_two = total(1, sums) + [count]

    line_two = norm_line(totals_two, scale_two)

    def third_step(i, rows, carry):
        valid = valid_of(infos, i, height, breadth, spot)
        scaled = on_line(pre_two[rows, :], line_two)
        low = (sigmoid(scaled) * features[rows, :].astype(F32)).astype(BF)
        gated[rows, :] = low
        parts = []
        for j in range(channels // half):
            cut = slice(j * half, (j + 1) * half)
            for p in range(9):
                work[p] = dot(low, grads[kernel_rows(p), cut])
            parts.append(gather_taps(lambda p: work[p], breadth, col))
        return put_stats(pre_three, rows, jnp.concatenate(parts, axis=1), valid, carry)

    loads[1].wait()
    sums = each_image(geometry, third_step, nothing)
    totals_three = total(2, sums) + [count]

    line_three = norm_line(totals_three, scale_three)

    def out_step(i, rows, carry):
        valid = valid_of(infos, i, height, breadth, spot)
        values = pre_three[rows, :]
        scaled = on_line(values, line_three)
        high, low = split(silu(scaled) * valid)
        mean = (dot(narrow, high) + dot(narrow, low)) * 0.25
        task_out[i] = mean.astype(BF)
        dy = silu_back(scaled) * dot(widen, cotangent[i]) * 0.25 * valid
        lower[rows, :] = dy
        return carry[0] + col_sum(dy), carry[1] + col_sum(dy * values)

    sums = each_image(geometry, out_step, nothing)
    sums_three = total(3, norm_sums(totals_three, sums))
    back_three = norm_back_line(totals_three, sums_three, scale_three)

    def third_back(i, rows, carry):
        valid = valid_of(infos, i, height, breadth, spot)
        dz = back_on_line(lower[rows, :], pre_three[rows, :], back_three, valid)
        for p, moved in enumerate(spread_taps(dz, breadth, col)):
            nine[p, rows, :] = moved.astype(BF)
        flow = None
        for p in range(9):
            piece = dot_nt(nine[p, rows, :], grads[kernel_rows(p), :])
            flow = piece if flow is None else flow + piece
        values = pre_two[rows, :]
        gate = sigmoid(on_line(values, line_two))
        flow = flow * gate
        lower[rows, :] = flow
        dy = flow * features[rows, :].astype(F32) * (1.0 - gate)
        pre_three[rows, :] = dy
        return carry[0] + col_sum(dy), carry[1] + col_sum(dy * values)

    sums = each_image(geometry, third_back, nothing)

    def taps(begin, end):
        def tap(p, carry):
            rows = pl.ds(pl.multiple_of((2 + p) * channels, channels), channels)
            grads[rows, :] = dot_tn(gated[...], nine[p]).astype(BF)
            return carry

        lax.fori_loop(begin, end, tap, 0)

    sums_two = total(4, norm_sums(totals_two, sums), lambda: taps(0, 2))
    back_two = norm_back_line(totals_two, sums_two, scale_two)

    def second_back(i, rows, carry):
        valid = valid_of(infos, i, height, breadth, spot)
        dz = back_on_line(pre_three[rows, :], pre_two[rows, :], back_two, valid).astype(BF)
        out[rows, :] = dz
        values = pre_one[rows, :]
        dy = silu_back(on_line(values, line_one)) * dot_nt(dz, second[...])
        pre_three[rows, :] = dy
        return carry[0] + col_sum(dy), carry[1] + col_sum(dy * values)

    sums = each_image(geometry, second_back, nothing)

    def weight_rows():
        grads[pl.ds(channels, channels), :] = dot_tn(hidden[...], out[...]).astype(BF)
        taps(2, 3)

    sums_one = total(5, norm_sums(totals_one, sums), weight_rows)
    back_one = norm_back_line(totals_one, sums_one, scale_one)

    def flow_copy(i, rows, step, incoming=False):
        peer = lax.rem(task + (tasks - step if incoming else step), tasks)
        return remote(
            out.at[rows, columns_of(peer, width)], arrived.at[step - 1, rows, :],
            sends.at[i, step], receives.at[i, step], peer, "task",
        )

    def first_back(i, rows, carry):
        valid = valid_of(infos, i, height, breadth, spot)
        dz = back_on_line(pre_three[rows, :], pre_one[rows, :], back_one, valid).astype(BF)
        hidden[rows, :] = dz
        flow = (lower[rows, :] + dot_nt(dz, first[...])) * valid
        out[rows, :] = flow.astype(BF)
        for step in range(1, tasks):
            flow_copy(i, rows, step).start()
        return carry

    each_image(geometry, first_back, 0)
    taps(3, 9)
    if summing:
        for chip in range(1, chips):
            near_copy(chip).start()
    grads[pl.ds(0, channels), :] = dot_tn(features[...], hidden[...]).astype(BF)
    if summing:
        near_copy(0).start()
        for chip in (*range(1, chips), 0):
            near_copy(chip).wait_recv()
            own = block_rows(grads, 2 * chip + core, block)[...].astype(F32)
            summed[chip] = (own + near[chip].astype(F32)).astype(BF)
            pltpu.make_async_copy(summed.at[chip], grads_out.at[chip], saved.at[chip]).start()
    else:
        grads_out[...] = grads[...]
    put_sums(sums_out, sums_one + sums_two + sums_three)

    def settle(i, rows, carry):
        for step in range(1, tasks):
            flow_copy(i, rows, step, True).wait_recv()
        flow = out[rows, columns_of(task, width)].astype(F32)
        for step in range(1, tasks):
            flow = flow + arrived[step - 1, rows, :].astype(F32)
        upstream[rows, :] = flow
        for step in range(1, tasks):
            flow_copy(i, rows, step).wait_send()
        return carry

    each_image(geometry, settle, 0)
    if summing:
        for chip in range(chips):
            near_copy(chip).wait_send()
            pltpu.make_async_copy(summed.at[chip], grads_out.at[chip], saved.at[chip]).wait()


def head(geometry, tasks, batches, infos, features, weights, cotangent, scales, counts):
    number, height, breadth = geometry
    pixels = height * breadth
    total, channels = features.shape
    width = channels // tasks
    block = weights.shape[0] // batches
    chips = batches // 2
    summing = block % 16 == 0
    outs = [
        shape((number, pixels // 4, channels), BF),
        shape((total, width), F32),
        shape((8, channels), F32),
        shape((chips, block, channels) if summing else weights.shape, BF),
    ]
    scratch = []
    if summing:
        scratch = [pltpu.VMEM((chips, block, channels), BF)]
        scratch += [pltpu.SemaphoreType.DMA((chips,))] * 2
        scratch += [pltpu.VMEM((chips, block, channels), BF), pltpu.SemaphoreType.DMA((chips,))]
    pooled, upstream, sums, grads = exchange_kernel(
        functools.partial(head_body, geometry, tasks, batches, summing),
        outs,
        "vvhvvv",
        (infos, features, weights, cotangent, scales, counts),
        [
            pltpu.VMEM(weights.shape, BF),
            pltpu.VMEM(features.shape, F32),
            pltpu.VMEM(features.shape, F32),
            pltpu.VMEM(features.shape, F32),
            pltpu.VMEM(features.shape, BF),
            pltpu.VMEM(features.shape, BF),
            pltpu.VMEM((9,) + features.shape, BF),
            pltpu.VMEM((9, pixels, min(channels, 256)), F32),
            pltpu.VMEM(features.shape, F32),
            pltpu.VMEM(features.shape, BF),
            pltpu.VMEM((tasks - 1, total, width), BF),
        ]
        + [pltpu.SemaphoreType.DMA((number, tasks))] * 2
        + total_scratch(6, batches)
        + [pltpu.SemaphoreType.DMA((2,))]
        + scratch,
        2,
        61,
        flops=6 * total * channels * weights.shape[0],
        places_out="vvvh" if summing else "vvvv",
    )
    if summing:
        owned = lax.psum_scatter(
            grads.reshape(chips * block, channels), "batch", scatter_dimension=0,
            axis_index_groups=[list(range(core, batches, 2)) for core in range(2)], tiled=True,
        )
    else:
        owned = lax.psum_scatter(grads, "batch", scatter_dimension=0, tiled=True)
    return pooled, upstream, sums, owned


def trunk_backward_body(
    geometry, tasks, batches,
    infos, upstream, enc_totals, dec_totals, scales, *rest,
):
    kept, rest = rest[:6], rest[6:]
    outs, sums_out, rest = rest[:3], rest[3], rest[4:]
    (x, enc_taps, dec_taps, enc_pre, dec_pre, spread), rest = rest[:6], rest[6:]
    (
        nine, change, packed, arrived, pooled, sends, receives,
        mine, slots, total_sends, total_receives, loaded,
        enc_grad, dec_grad, flow_out, saved, sums_own, sum_sends, sum_receives,
    ) = rest
    saves = [
        pltpu.make_async_copy(a, b, saved.at[k])
        for k, (a, b) in enumerate(zip((enc_grad, dec_grad, flow_out), outs))
    ]
    targets = (x, enc_taps, dec_taps, enc_pre, dec_pre, spread)
    loads = [pltpu.make_async_copy(a, b, loaded.at[k]) for k, (a, b) in enumerate(zip(kept, targets))]
    for k in (4, 2, 5, 3, 1, 0):
        loads[k].start()
    number, height, breadth = geometry
    channels = x.shape[1]
    width = enc_pre.shape[1]
    windows = window_count(height, breadth)
    task = lax.axis_index("task")
    spot = places(height, breadth)
    _, col = spot
    widen = pool_choice(height, breadth, windows, False).astype(BF)
    narrow = pool_choice(height, breadth, windows, True)
    nothing = zero_rows(2, width)

    def total(k, rows):
        return total_rows(
            k, "batch", batches, list(rows), mine, slots, total_sends, total_receives
        )

    def change_of(pre, totals, scale, flow):
        line = norm_line(totals, scale)

        def image(i, rows, carry):
            valid = valid_of(infos, i, height, breadth, spot)
            values = pre[rows, :]
            dy = silu_back(on_line(values, line)) * flow(i, rows) * valid
            change[rows, :] = dy
            return carry[0] + col_sum(dy), carry[1] + col_sum(dy * values)

        return norm_sums(totals, each_image(geometry, image, nothing))

    def back(pre, totals, scale, sums, taps, put):
        line = norm_back_line(totals, sums, scale)

        def image(i, rows, carry):
            valid = valid_of(infos, i, height, breadth, spot)
            dz = back_on_line(change[rows, :], pre[rows, :], line, valid)
            for p, moved in enumerate(spread_taps(dz, breadth, col)):
                nine[rows, p * width : (p + 1) * width] = moved.astype(BF)
            put(i, rows, dot_nt(nine[rows, :], taps[...]) * valid)
            return carry

        each_image(geometry, image, 0)

    totals = rows_of(dec_totals, 0, 3)
    scale = rows_of(scales, 2, 2)
    loads[4].wait()
    sums = change_of(dec_pre, totals, scale, lambda i, rows: upstream[rows, :])
    greet((("task", tasks), ("batch", batches)))
    dec_sums = total(0, sums)

    def copy_of(i, step, incoming=False):
        rows = window_rows(i, windows)
        peer = lax.rem(task + (tasks - step if incoming else step), tasks)
        return remote(
            packed.at[rows, columns_of(peer, width)], arrived.at[step - 1, rows, :],
            sends.at[i, step], receives.at[i, step], peer, "task",
        )

    def put_packed(i, rows, flow):
        chosen = chosen_cells(narrow, infos, i)
        packed[window_rows(i, windows), :] = dot(chosen, flow.astype(BF)).astype(BF)
        for step in range(1, tasks):
            copy_of(i, step).start()

    loads[2].wait()
    back(dec_pre, totals, scale, dec_sums, dec_taps, put_packed)
    loads[5].wait()
    dec_grad[...] = dot_tn(spread[...], nine[...])
    saves[1].start()

    def collect(i, carry):
        for step in range(1, tasks):
            copy_of(i, step, True).wait_recv()
        rows = window_rows(i, windows)
        flow = packed[rows, columns_of(task, width)].astype(F32)
        for step in range(1, tasks):
            flow = flow + arrived[step - 1, rows, :].astype(F32)
        pooled[rows, :] = flow
        for step in range(1, tasks):
            copy_of(i, step).wait_send()
        return carry

    lax.fori_loop(0, number, collect, 0)

    def widened(i, rows):
        high, low = split(pooled[window_rows(i, windows), :])
        return (dot(widen, high) + dot(widen, low)) * 0.25

    totals = rows_of(enc_totals, 0, 3)
    scale = rows_of(scales, 0, 2)
    loads[3].wait()
    sums = change_of(enc_pre, totals, scale, widened)
    enc_sums = total(1, sums)
    put_sums(sums_own, enc_sums + dec_sums)

    def sum_copy(step, incoming=False):
        peer = lax.rem(task + (tasks - step if incoming else step), tasks)
        home = peer if incoming else task
        return remote(sums_own, sums_out.at[:, columns_of(home, width)], sum_sends.at[step],
                      sum_receives.at[step], peer, "task")

    for step in range(1, tasks):
        sum_copy(step).start()
    sums_out[:, columns_of(task, width)] = sums_own[...]

    def put_flow(i, rows, flow):
        flow_out[rows, :] = flow.astype(BF)

    loads[1].wait()
    back(enc_pre, totals, scale, enc_sums, enc_taps, put_flow)
    loads[0].wait()
    saves[2].start()
    enc_grad[...] = dot_tn(x[...], nine[...])
    saves[0].start()
    for copy in saves:
        copy.wait()
    for step in range(1, tasks):
        sum_copy(step, True).wait_recv()
        sum_copy(step).wait_send()


def trunk_backward(
    geometry, tasks, batches, infos, upstream, enc_totals, dec_totals, scales, kept
):
    number, height, breadth = geometry
    x, enc_taps, dec_taps = kept[:3]
    total, channels = x.shape
    width = channels // tasks
    windows = window_count(height, breadth)
    outs = [
        shape(enc_taps.shape, F32),
        shape(dec_taps.shape, F32),
        shape(x.shape, BF),
        shape((8, channels), F32),
    ]
    return exchange_kernel(
        functools.partial(trunk_backward_body, geometry, tasks, batches),
        outs,
        "vvvvvhhhhhh",
        (infos, upstream, enc_totals, dec_totals, scales, *kept),
        [pltpu.VMEM(a.shape, a.dtype) for a in kept]
        + [
            pltpu.VMEM((total, 9 * width), BF),
            pltpu.VMEM((total, width), F32),
            pltpu.VMEM((number * windows, channels), BF),
            pltpu.VMEM((tasks - 1, number * windows, width), BF),
            pltpu.VMEM((number * windows, width), F32),
        ]
        + [pltpu.SemaphoreType.DMA((number, tasks))] * 2
        + total_scratch(2, batches)
        + [pltpu.SemaphoreType.DMA((6,))]
        + [pltpu.VMEM(a.shape, a.dtype) for a in outs[:3]]
        + [pltpu.SemaphoreType.DMA((3,)), pltpu.VMEM((8, width), F32)]
        + [pltpu.SemaphoreType.DMA((tasks,))] * 2,
        3,
        60,
        flops=8 * x.size * enc_taps.shape[1],
        places_out="hhhv",
    )


def to_slots_body(index, enc_far, dec_far, slots, enc, dec, wide, low, load, save):
    count = wide.shape[0]
    channels = enc.shape[0]
    width = wide.shape[1]
    step = 1024
    group = 32
    loads = [
        pltpu.make_async_copy(a, b, load.at[k])
        for k, (a, b) in enumerate(((dec_far, dec), (enc_far, enc)))
    ]
    for copy in loads:
        copy.start()
    for kernel, copy in ((1, loads[0]), (0, loads[1])):
        copy.wait()
        source = dec if kernel else enc
        for q in range(9):

            def place(i, carry):
                base = pl.multiple_of(i * group, group)
                first = (9 * kernel + q) * channels + base
                values = source[pl.ds(base, group), q * width : (q + 1) * width]
                for u in range(group):
                    wide[pl.ds(index[first + u], 1), :] = values[u : u + 1, :]
                return carry

            lax.fori_loop(0, channels // group, place, 0)

    def out(i):
        rows = pl.ds(pl.multiple_of(i * step, step), step)
        return pltpu.make_async_copy(low.at[rows, :], slots.at[rows, :], save.at[i])

    def narrow(i, carry):
        rows = pl.ds(pl.multiple_of(i * step, step), step)
        low[rows, :] = wide[rows, :].astype(BF)
        out(i).start()
        return carry

    def end(i, carry):
        out(i).wait()
        return carry

    lax.fori_loop(0, count // step, narrow, 0)
    lax.fori_loop(0, count // step, end, 0)


def to_slots(index, enc, dec):
    width = enc.shape[1] // 9
    dims = (index.shape[0], width)
    far = pl.BlockSpec(memory_space=pltpu.HBM)
    return pl.pallas_call(
        to_slots_body,
        out_shape=shape(dims, BF),
        in_specs=[SMEM_SPEC, far, far],
        out_specs=far,
        scratch_shapes=[
            pltpu.VMEM(enc.shape, F32),
            pltpu.VMEM(dec.shape, F32),
            pltpu.VMEM(dims, F32),
            pltpu.VMEM(dims, BF),
            pltpu.SemaphoreType.DMA((2,)),
            pltpu.SemaphoreType.DMA((dims[0] // 1024,)),
        ],
        compiler_params=pltpu.CompilerParams(vmem_limit_bytes=60 * MIB),
        cost_estimate=pl.CostEstimate(flops=10000 * MIB, bytes_accessed=8 * MIB, transcendentals=0),
    )(index, enc, dec)


def adam(gradient, moment_one, moment_two):
    new_one = BETA_ONE * moment_one + (1.0 - BETA_ONE) * gradient
    new_two = BETA_TWO * moment_two + (1.0 - BETA_TWO) * gradient * gradient
    direction = (
        new_one / (1.0 - BETA_ONE**STEP) / (jnp.sqrt(new_two / (1.0 - BETA_TWO**STEP)) + ADAM_EPS)
    )
    return new_one, new_two, direction


def pair_place(batches):
    me = lax.axis_index("batch")
    place = lax.div(me, 2)
    return place, me - 2 * place, batches // 2


def greet_pairs(tasks, batches):
    place, core, chips = pair_place(batches)
    task = lax.axis_index("task")
    barrier = pltpu.get_barrier_semaphore()

    def signal(device):
        pl.semaphore_signal(barrier, inc=1, device_id=device, device_id_type=MESH)

    for step in range(1, tasks):
        signal({"task": lax.rem(task + step, tasks)})
    signal({"batch": 2 * place + 1 - core})
    for step in range(1, chips):
        signal({"batch": 2 * lax.rem(place + step, chips) + core})
    pl.semaphore_wait(barrier, tasks - 1 + chips)


def block_rows(ref, index, count):
    return ref.at[pl.ds(pl.multiple_of(index * count, 8), count), :]


SMALL = 128 * 128


def far_first(chips):
    return sorted(range(chips), key=lambda step: -min(step, chips - step))


def pair_sum(batches, rows_of_block, own_block, near, paired, far, sems):
    place, core, chips = pair_place(batches)
    count = near.shape[1]
    near_send, near_receive, far_send, far_receive = sems
    other = 2 * place + 1 - core
    ring = chips == 4 and count % 32 == 0 and near.shape[2] * count > SMALL
    half = count // 2
    halves = (pl.ds(0, half), pl.ds(half, half))

    def near_copy(step):
        chip = lax.rem(place + step, chips)
        return remote(rows_of_block(2 * chip + 1 - core), near.at[step],
                      near_send.at[step], near_receive.at[step], other, "batch")

    def far_copy(step, incoming=False):
        chip = lax.rem(place + (chips - step if incoming else step), chips)
        return remote(paired.at[step], far.at[step], far_send.at[step], far_receive.at[step],
                      2 * chip + core, "batch")

    def ring_copy(which, way):
        chip = lax.rem(place + (1 if way == 0 else chips - 1), chips)
        if which == 0:
            source, target = paired.at[2, halves[way], :], far.at[2 + way, halves[0], :]
        else:
            cut = halves[way] if which == 2 else halves[1 - way]
            source, target = paired.at[1 if way == 0 else 3, cut, :], far.at[way, cut, :]
        k = 2 * which + way
        return remote(source, target, far_send.at[k], far_receive.at[k], 2 * chip + core, "batch")

    def start():
        for step in far_first(chips):
            near_copy(step).start()

    def middle():
        for step in far_first(chips):
            near_copy(step).wait_recv()
            if step:
                paired[step] = (own_block(step) + near[step].astype(F32)).astype(paired.dtype)
                if not ring:
                    far_copy(step).start()
                elif step == 2:
                    ring_copy(0, 0).start()
                    ring_copy(0, 1).start()
                else:
                    ring_copy(1, 0 if step == 1 else 1).start()

    def relay():
        if not ring:
            return
        for way in range(2):
            ring_copy(0, way).wait_recv()
            step = 1 if way == 0 else 3
            total = paired[step, halves[way], :].astype(F32) + far[2 + way, halves[0], :].astype(F32)
            paired[step, halves[way], :] = total.astype(paired.dtype)
            ring_copy(2, way).start()

    def end():
        total = own_block(0) + near[0].astype(F32)
        if ring:
            for way in range(2):
                ring_copy(1, way).wait_recv()
                ring_copy(2, way).wait_recv()
                total = total + far[way].astype(F32)
            for k in range(3):
                for way in range(2):
                    ring_copy(k, way).wait_send()
        else:
            for step in range(1, chips):
                far_copy(step, True).wait_recv()
                total = total + far[step].astype(F32)
            for step in range(1, chips):
                far_copy(step).wait_send()
        for step in range(chips):
            near_copy(step).wait_send()
        return total

    return start, middle, relay, end


def blocks_in(source, batches, count, piece=0, pieces=1):
    place, core, chips = pair_place(batches)

    def rows(index):
        start = (index * pieces + piece) * count
        return source.at[pl.ds(pl.multiple_of(start, 8), count), :]

    def own(step):
        chip = lax.rem(place + step, chips)
        return rows(2 * chip + core)[...].astype(F32)

    return rows, own


def pair_scratch(batches, rows, width, kind):
    chips = batches // 2
    return [pltpu.VMEM((chips, rows // batches, width), kind)] * 3 + [
        pltpu.SemaphoreType.DMA((max(chips, 6),))
    ] * 4


def chip_spread(batches, block, sends, receives):
    place, core, chips = pair_place(batches)
    count, width = block(place).shape
    ring = chips == 4 and count % 32 == 0 and width * count > SMALL
    half = count // 2

    def copy(step, incoming=False):
        peer = lax.rem(place + (chips - step if incoming else step), chips)
        ref = block(peer if incoming else place)
        return remote(ref, ref, sends.at[step], receives.at[step], 2 * peer + core, "batch")

    def pass_on(way, incoming=False):
        step = 1 if way == 0 else chips - 1
        peer = lax.rem(place + (chips - step if incoming else step), chips)
        home = lax.rem(place + (2 if incoming else chips - step), chips)
        ref = block(home).at[pl.ds(way * half, half), :]
        k = 2 if way == 0 else 0
        return remote(ref, ref, sends.at[k], receives.at[k], 2 * peer + core, "batch")

    steps = (1, chips - 1) if ring else tuple(range(1, chips))

    def start():
        for step in steps:
            copy(step).start()

    def relay():
        if ring:
            for way, step in enumerate(steps):
                copy(step, True).wait_recv()
                pass_on(way).start()

    def settle():
        if ring:
            for way in range(2):
                pass_on(way, True).wait_recv()
        else:
            for step in steps:
                copy(step, True).wait_recv()

    def drain():
        for step in steps:
            copy(step).wait_send()
        if ring:
            for way in range(2):
                pass_on(way).wait_send()

    return start, relay, settle, drain


def arrive_body(
    tasks, batches, geometry,
    image_raw, info, index, weight, head_weight,
    slots, x, infos, owners, head_low,
    image, head_raw, head_loaded, raw, raw_loaded, x_send, x_receive, info_send, info_receive,
    chip_send, chip_receive, pair_send, pair_receive, own,
):
    task = lax.axis_index("task")
    place, core, chips = pair_place(batches)
    count, width = raw.shape
    load = pltpu.make_async_copy(weight.at[:, columns_of(task, width)], raw, raw_loaded)
    load.start()
    head_load = pltpu.make_async_copy(head_weight, head_raw, head_loaded)
    head_load.start()
    number, height, breadth = geometry
    pixels = height * breadth
    for n in range(number):
        valid = valid_rows(
            info[8 * n + 1 : 8 * n + 2, 0:1], height, breadth, places(height, breadth)
        )
        rows = slice(n * pixels, (n + 1) * pixels)
        image[rows, :] = (image_raw[rows, :].astype(F32) * valid).astype(BF)
    greet_pairs(tasks, batches)

    def task_copy(source, target, sends, receives, step, incoming=False):
        peer = lax.rem(task + (tasks - step if incoming else step), tasks)
        home = peer if incoming else task
        return remote(source, block_rows(target, home, source.shape[0]), sends.at[step],
                      receives.at[step], peer, "task")

    def moves(step, incoming=False):
        return (
            task_copy(info, infos, info_send, info_receive, step, incoming),
            task_copy(image, x, x_send, x_receive, step, incoming),
        )

    def block(chip):
        return block_rows(slots, 2 * chip + core, count)

    def pair_copy(hop, incoming=False):
        chip = lax.rem(place + chips - hop, chips)
        ref = block_rows(slots, 2 * chip + (1 - core if incoming else core), count)
        return remote(ref, ref, pair_send.at[hop], pair_receive.at[hop], 2 * place + 1 - core, "batch")

    start, relay, settle, drain = chip_spread(batches, block, chip_send, chip_receive)
    ring = chips == 4 and count % 32 == 0 and width * count > SMALL
    load.wait()
    block(place)[...] = raw[...].astype(BF)
    start()
    pair_copy(0).start()
    for step in range(1, tasks):
        for copy in moves(step):
            copy.start()
    locals_ = [
        pltpu.make_async_copy(image, block_rows(x, task, image.shape[0]), own.at[0]),
        pltpu.make_async_copy(info, block_rows(infos, task, info.shape[0]), own.at[1]),
    ]
    for copy in locals_:
        copy.start()
    mine = lax.broadcasted_iota(jnp.int32, (count, 1), 0) + lax.axis_index("batch") * count
    found = jnp.zeros((count, 128), F32)
    for k in range(index.shape[0] // 2, index.shape[0]):
        found = jnp.where(index[k : k + 1, :] == mine, 1.0, found)
    found = jnp.max(found, axis=1, keepdims=True)
    owners[:, 0:1] = 1.0 - found
    owners[:, 1:2] = found
    head_load.wait()
    head_low[...] = head_raw[...].astype(BF)
    relay()
    if ring:
        pair_copy(1).start()
        pair_copy(3).start()
        settle()
        pair_copy(2).start()
    else:
        settle()
        for hop in range(1, chips):
            pair_copy(hop).start()
    for copy in locals_:
        copy.wait()
    for step in range(1, tasks):
        for copy in moves(step, True):
            copy.wait_recv()
    for hop in range(chips):
        pair_copy(hop, True).wait_recv()
    for step in range(1, tasks):
        for copy in moves(step):
            copy.wait_send()
    for hop in range(chips):
        pair_copy(hop).wait_send()
    drain()


def arrive(tasks, batches, geometry, image, info, index, weight, head_weight):
    count, channels = weight.shape
    width = channels // tasks
    chips = batches // 2
    return exchange_kernel(
        functools.partial(arrive_body, tasks, batches, geometry),
        [
            shape((count * batches, width), BF),
            shape((image.shape[0] * tasks, channels), BF),
            shape((info.shape[0] * tasks, info.shape[1]), F32),
            shape((count, 2), F32),
            shape(head_weight.shape, BF),
        ],
        "vvvhh",
        (image, info, index.reshape(-1, 128), weight, head_weight),
        [
            pltpu.VMEM(image.shape, BF),
            pltpu.VMEM(head_weight.shape, F32),
            pltpu.SemaphoreType.DMA,
            pltpu.VMEM((count, width), F32),
            pltpu.SemaphoreType.DMA,
        ]
        + [pltpu.SemaphoreType.DMA((tasks,))] * 4
        + [pltpu.SemaphoreType.DMA((max(chips, 4),))] * 4
        + [pltpu.SemaphoreType.DMA((2,))],
        4,
        60,
        flops=20000 * MIB,
    )


def soap_rows(cuts, grad, owners, state, low, first, begin=0, end=None):
    total = grad.shape[0]

    def chunk(i, carry):
        rows = pl.ds(pl.multiple_of(i * (total // cuts), 8), total // cuts)
        values = grad[rows, :].astype(F32)
        marks = owners(i * (total // cuts), total // cuts)
        count = len(marks)
        rotated = None
        for m in range(count):
            part = dot((values * marks[m]).astype(BF), low[first + m])
            rotated = part if rotated is None else rotated + part
        new_one, new_two, direction = adam(rotated, state[1, rows, :], state[2, rows, :])
        state[1, rows, :] = new_one
        state[2, rows, :] = new_two
        stepped = None
        for m in range(count):
            part = dot_nt((direction * marks[m]).astype(BF), low[first + m])
            stepped = part if stepped is None else stepped + part
        old = state[0, rows, :]
        state[0, rows, :] = old - LEARN_MATRIX * (stepped + DECAY_MATRIX * old)
        return carry

    lax.fori_loop(begin, cuts if end is None else end, chunk, 0)


def factor_rows(values, identity, turn):
    size, width = values.shape
    sub = lax.broadcasted_iota(jnp.int32, (size, width), 0)
    rolled = pltpu.roll(values, turn, 1)
    columns = [jnp.broadcast_to(rolled[:, j : j + 1], (size, width)) for j in range(size)]
    scale = jnp.zeros((size, width), F32)
    for j in range(size):
        root = lax.rsqrt(columns[j][j : j + 1, :])
        scale = jnp.where(sub == j, root, scale)
        lower = jnp.where(sub > j, columns[j] * root, 0.0)
        values = values - lower * (values[j : j + 1, :] * root)
        identity = identity - lower * (identity[j : j + 1, :] * root)
        for i in range(j + 1, size):
            columns[i] = columns[i] - lower * (columns[i][j : j + 1, :] * root)
    return values * scale, identity * scale


GROUP = 16
PANEL = 128


def upper_blocks(size):
    return [(a, b) for a in range(0, size, PANEL) for b in range(a, size, PANEL)]


def renew_panel(k, product, made, tables, inverses):
    count, size = product.shape[0], product.shape[1]
    here = slice(k * PANEL, (k + 1) * PANEL)
    row = lax.broadcasted_iota(jnp.int32, (PANEL, PANEL), 0)
    col = lax.broadcasted_iota(jnp.int32, (PANEL, PANEL), 1)
    unit = jnp.where(row == col, 1.0, 0.0).astype(F32)
    for n in range(count):
        tables[n][:, :PANEL] = dot3(dot_tn, product[n, :, here], product[n, :, here])
        tables[n][:, PANEL:] = unit

    for first in range(0, PANEL, GROUP):
        rows, rest = slice(first, first + GROUP), slice(first + GROUP, PANEL)
        done = [
            factor_rows(tables[n][rows, :PANEL], tables[n][rows, PANEL:], (PANEL - first) % PANEL)
            for n in range(count)
        ]
        for n in range(count):
            upper, inverse = done[n]
            inverses[n][rows, :] = inverse
            if first + GROUP < PANEL:
                both = jnp.concatenate([upper, inverse], axis=1)
                tables[n][rest, :] = tables[n][rest, :] - dot3(dot_tn, upper[:, rest], both)
    for n in range(count):
        turned = dot3(dot_nt, product[n, :, here], inverses[n][...])
        made[n, :, here] = turned
        if k < size // PANEL - 1:
            rest = slice((k + 1) * PANEL, size)
            product[n, :, rest] = product[n, :, rest] - dot3(
                dot, turned, dot3(dot_tn, turned, product[n, :, rest])
            )


def tail_body(
    tasks, batches, cuts, pieces,
    slots, flow, owners, head_far,
    weight, one, two, head_weight, head_one, head_two, basis, head_basis,
    input_grad, state_new, head_state_new, grams, head_grams,
    grad, part, state, head_state, mine, head_mine, bases, low, head_grad, flow_own,
    flow_in, flow_send, flow_receive, send, receive,
    *rest,
):
    row_scratch = [rest[7 * k : 7 * k + 7] for k in range(pieces)]
    gram_scratch, head_scratch, rest = rest[7 * pieces :][:7], rest[7 * pieces + 7 :][:7], rest[7 * pieces + 14 :]
    chip_send, chip_receive, task_send, task_receive, pair_send, pair_receive, load, save = rest
    task = lax.axis_index("task")
    place, core, chips = pair_place(batches)
    width = part.shape[1]
    channels = grad.shape[1]
    pixels = input_grad.shape[0]
    trunk_total = basis.shape[0]
    head_total = head_basis.shape[0]
    count, head_count = mine.shape[0] // batches, head_mine.shape[0] // batches

    def trunk_marks(start, size):
        rows = pl.ds(pl.multiple_of(start, 8), size)
        return [owners[rows, m : m + 1] for m in range(trunk_total)]

    def head_marks(start, size):
        index = lax.broadcasted_iota(jnp.int32, (size, 1), 0) + start
        index = index + lax.axis_index("batch") * head_grad.shape[0]
        owner = jnp.minimum(lax.div(index, channels), head_total - 1)
        return [jnp.where(owner == m, 1.0, 0.0).astype(F32) for m in range(head_total)]

    def put_grams(target, rows, columns, marks):
        for m, mark in enumerate(marks):
            held = (rows[...].astype(F32) * mark).astype(BF)
            target[m * channels : (m + 1) * channels, :] = dot_tn(held, columns[...]).astype(
                target.dtype
            )

    def put_packed_grams(target, rows, marks):
        n = 0
        for mark in marks:
            held = (rows[...].astype(F32) * mark).astype(BF)
            for a, b in upper_blocks(channels):
                block = dot_tn(held[:, a : a + PANEL], rows[:, b : b + PANEL])
                target[n : n + PANEL, :] = block.astype(target.dtype)
                n += PANEL
        if n < target.shape[0]:
            target[n:, :] = jnp.zeros((target.shape[0] - n, PANEL), target.dtype)

    def peer_of(step, incoming):
        return lax.rem(task + (tasks - step if incoming else step), tasks)

    def flow_copy(step, incoming=False):
        peer = peer_of(step, incoming)
        return remote(block_rows(flow, peer, pixels), flow_in.at[step - 1], flow_send.at[step],
                      flow_receive.at[step], peer, "task")

    def part_copy(k, step, incoming=False):
        peer = peer_of(step, incoming)
        home = peer if incoming else task
        return remote(part.at[part_rows(k), :], grad.at[part_rows(k), columns_of(home, width)],
                      send.at[k, step], receive.at[k, step], peer, "task")

    def trunk_block(chip, home, which):
        rows = pl.ds(pl.multiple_of((2 * chip + which) * count, 8), count)
        return grams.at[rows, columns_of(home, width)]

    def head_block(chip, which):
        return block_rows(head_grams, 2 * chip + which, head_count)

    def task_copy(step, hop, incoming=False):
        peer = peer_of(step, incoming)
        chip = lax.rem(place + chips - hop, chips)
        block = trunk_block(chip, peer if incoming else task, core)
        return remote(block, block, task_send.at[step, hop], task_receive.at[step, hop], peer, "task")

    def pair_copy(kind, hop, incoming=False):
        chip = lax.rem(place + chips - hop, chips)
        which = 1 - core if incoming else core
        home = lax.rem(task + tasks - kind, tasks)
        block = head_block(chip, which) if kind == tasks else trunk_block(chip, home, which)
        return remote(block, block, pair_send.at[kind, hop], pair_receive.at[kind, hop],
                      2 * place + 1 - core, "batch")

    def sum_of(source, scratch, piece=0, total=1):
        near, paired, far, *sems = scratch
        return pair_sum(
            batches, *blocks_in(source, batches, near.shape[1], piece, total), near, paired, far, sems
        )

    def part_rows(k):
        size = part.shape[0] // pieces
        return pl.ds(k * size, size)

    moves = [
        (basis, bases.at[pl.ds(0, trunk_total)]),
        (head_basis, bases.at[pl.ds(trunk_total, head_total)]),
        (head_weight, head_state.at[0]),
        (head_one, head_state.at[1]),
        (head_two, head_state.at[2]),
        (weight, state.at[0]),
        (one, state.at[1]),
        (two, state.at[2]),
        (head_far, head_grad),
        (block_rows(flow, task, pixels), flow_own),
    ]
    loads = [pltpu.make_async_copy(a, b, load.at[k]) for k, (a, b) in enumerate(moves)]
    loads[8].start()
    for copy in (*loads[:8], loads[9]):
        copy.start()
    saves = [
        pltpu.make_async_copy(state, state_new, save.at[0]),
        pltpu.make_async_copy(head_state, head_state_new, save.at[1]),
    ]

    greet_pairs(tasks, batches)
    row_sums = [sum_of(slots, row_scratch[k], k, pieces) for k in range(pieces)]
    for stages in row_sums:
        stages[0]()
    for step in range(1, tasks):
        flow_copy(step).start()
    row_sums[0][1]()
    loads[8].wait()
    put_packed_grams(head_mine, head_grad, head_marks(0, head_grad.shape[0]))
    head_start, head_middle, head_relay, head_end = sum_of(head_mine, head_scratch)
    row_sums[0][2]()
    for stages in row_sums[1:]:
        stages[1]()
    head_start()
    for stages in row_sums[1:]:
        stages[2]()
    head_middle()
    for copy in loads[:5]:
        copy.wait()
    for m in range(trunk_total + head_total):
        low[m] = bases[m].astype(BF)
    for k, stages in enumerate(row_sums):
        total = stages[3]().astype(BF)
        part[part_rows(k), :] = total
        for step in range(1, tasks):
            part_copy(k, step).start()
        grad[part_rows(k), columns_of(task, width)] = total
    head_relay()

    soap_rows(cuts, head_grad, head_marks, head_state, low, trunk_total)
    saves[1].start()
    loads[9].wait()
    total = flow_own[...].astype(F32)
    for step in range(1, tasks):
        flow_copy(step, True).wait_recv()
        total = total + flow_in[step - 1].astype(F32)
    input_grad[...] = total
    head_block(place, core)[...] = head_end().astype(head_grams.dtype)
    trunk_spread = chip_spread(
        batches, lambda chip: trunk_block(chip, task, core), chip_send.at[0], chip_receive.at[0]
    )
    head_spread = chip_spread(
        batches, lambda chip: head_block(chip, core), chip_send.at[1], chip_receive.at[1]
    )
    head_spread[0]()
    pair_copy(tasks, 0).start()
    for k in range(pieces):
        for step in range(1, tasks):
            part_copy(k, step, True).wait_recv()

    put_grams(mine, grad, part, trunk_marks(0, grad.shape[0]))
    start, middle, relay, end = sum_of(mine, gram_scratch)
    start()
    middle()
    head_spread[1]()
    for copy in loads[5:8]:
        copy.wait()
    relay()
    soap_rows(cuts, grad, trunk_marks, state, low, 0, 0, cuts // 2)
    trunk_block(place, task, core)[...] = end().astype(grams.dtype)
    trunk_spread[0]()
    for step in range(1, tasks):
        task_copy(step, 0).start()
    pair_copy(0, 0).start()
    soap_rows(cuts, grad, trunk_marks, state, low, 0, cuts // 2, cuts)
    saves[0].start()
    trunk_spread[1]()
    trunk_spread[2]()
    for hop in range(1, chips):
        for step in range(1, tasks):
            task_copy(step, hop).start()
        pair_copy(0, hop).start()
    head_spread[2]()
    for hop in range(1, chips):
        pair_copy(tasks, hop).start()
    for hop in range(chips):
        for step in range(1, tasks):
            task_copy(step, hop, True).wait_recv()
            pair_copy(step, hop).start()
    for hop in range(chips):
        for kind in range(tasks + 1):
            pair_copy(kind, hop, True).wait_recv()
    for copy in saves:
        copy.wait()
    for step in range(1, tasks):
        for k in range(pieces):
            part_copy(k, step).wait_send()
        flow_copy(step).wait_send()
    for hop in range(chips):
        for kind in range(tasks + 1):
            pair_copy(kind, hop).wait_send()
        for step in range(1, tasks):
            task_copy(step, hop).wait_send()
    trunk_spread[3]()
    head_spread[3]()


def renew_body(
    core, state, head_state, grams, head_grams, stat, head_stat, basis, head_basis,
    weight_new, one_new, two_new, head_weight_new, head_one_new, head_two_new,
    stat_new, head_stat_new, low_made,
    stats, product, made, low_grams, low_head_grams, held, head_held, load, save, *work,
):
    trunk_total, head_total = stat.shape[0], head_stat.shape[0]
    channels = stat.shape[1]
    count = trunk_total + head_total
    shared = product.shape[0]
    tables, inverses = work[:shared], work[shared:]
    loads = []
    blocks = upper_blocks(channels)
    packed = len(blocks) * PANEL

    def gram_rows(m, start):
        if m < trunk_total:
            first = m * channels + start
            return low_grams[first : first + PANEL, :].astype(F32)
        parts = []
        for b in range(0, channels, PANEL):
            n = blocks.index((min(start, b), max(start, b)))
            first = (m - trunk_total) * packed + n * PANEL
            block = low_head_grams[first : first + PANEL, :].astype(F32)
            parts.append(block if b >= start else block.T)
        return jnp.concatenate(parts, axis=1)

    def bring(source, target):
        copy = pltpu.make_async_copy(source, target, load.at[len(loads)])
        loads.append(copy)
        return copy

    for m in range(count):
        first = m < trunk_total
        place = m if first else m - trunk_total
        size = channels if first else packed
        rows = pl.ds(place * size, size)
        here, there = (grams, low_grams) if first else (head_grams, low_head_grams)
        bring(here.at[rows, :], there.at[rows, :]).start()
        bring((stat if first else head_stat).at[place], stats.at[m]).start()

    for n in range(shared):
        both = [
            basis.at[n] if n < trunk_total else head_basis.at[n - trunk_total],
            head_basis.at[n],
        ]
        copy = bring(both[1], made.at[n])
        for which, source in enumerate(both):

            @pl.when(core[0] == which)
            def _():
                pltpu.make_async_copy(source, made.at[n], load.at[2 * count + n]).start()

    bring(state, held).start()
    bring(head_state, head_held).start()
    sources = [held.at[k] for k in range(3)] + [head_held.at[k] for k in range(3)]
    targets = [weight_new, one_new, two_new, head_weight_new, head_one_new, head_two_new]
    saves = [pltpu.make_async_copy(a, b, save.at[k]) for k, (a, b) in enumerate(zip(sources, targets))]
    for m in range(count):
        for copy in loads[2 * m : 2 * m + 2]:
            copy.wait()
        for start in range(0, channels, PANEL):
            rows = slice(start, start + PANEL)
            stats[m, rows, :] = STAT_DECAY * stats[m, rows, :] + (1.0 - STAT_DECAY) * gram_rows(m, start)
    for begin, size, out in ((0, trunk_total, stat_new), (trunk_total, head_total, head_stat_new)):
        copy = pltpu.make_async_copy(stats.at[pl.ds(begin, size)], out, save.at[len(saves)])
        copy.start()
        saves.append(copy)
    for n in range(shared):
        loads[2 * count + n].wait()
        product[n] = dot3(dot, stats[trunk_total * core[0] + n], made[n])
    for k in range(channels // PANEL):
        renew_panel(k, product, made, tables, inverses)
        if k == 0:
            for copy in loads[2 * count + shared :]:
                copy.wait()
            for copy in saves[:6]:
                copy.start()
        cut = slice(k * PANEL, (k + 1) * PANEL)
        low_made[:, :, cut] = made[:, :, cut].astype(BF)
    for copy in saves:
        copy.wait()


def swap_body(batches, x, out, sends, receives):
    place, core, _ = pair_place(batches)
    other = 2 * place + 1 - core
    barrier = pltpu.get_barrier_semaphore()
    pl.semaphore_signal(barrier, inc=1, device_id={"batch": other}, device_id_type=MESH)
    pl.semaphore_wait(barrier, 1)
    copy = remote(x, out, sends, receives, other, "batch")
    copy.start()
    copy.wait()


def finish(tasks, batches, local_grads, rows, matrices):
    slots, flow, owners, head_grad = local_grads
    stat, head_stat, basis, head_basis = matrices
    total, channels = rows[0].shape
    width = channels // tasks
    trunk_total, head_total = basis.shape[0], head_basis.shape[0]
    gram_rows = trunk_total * channels
    packed = len(upper_blocks(channels)) * PANEL
    head_rows = -(-head_total * packed // (16 * batches)) * 16 * batches
    chips = batches // 2
    kind = BF if gram_rows % (16 * batches) == 0 else F32
    cuts = 4 if total % 64 == 0 and head_grad.shape[0] % 64 == 0 else 1
    pieces = 2 if total % 64 == 0 else 1
    square = (trunk_total + head_total, channels, channels)
    pixels = flow.shape[0] // tasks
    input_grad, *made = exchange_kernel(
        functools.partial(tail_body, tasks, batches, cuts, pieces),
        [
            shape((pixels, channels), F32),
            shape((3, total, channels), F32),
            shape((3,) + head_grad.shape, F32),
            shape((gram_rows, channels), kind),
            shape((head_rows, PANEL), BF),
        ],
        "vhvhhhhhhhhh",
        (*local_grads, *rows, basis, head_basis),
        [
            pltpu.VMEM((total, channels), BF),
            pltpu.VMEM((total, width), BF),
            pltpu.VMEM((3, total, channels), F32),
            pltpu.VMEM((3,) + head_grad.shape, F32),
            pltpu.VMEM((gram_rows, width), kind),
            pltpu.VMEM((head_rows, PANEL), BF),
            pltpu.VMEM(square, F32),
            pltpu.VMEM(square, BF),
            pltpu.VMEM(head_grad.shape, BF),
            pltpu.VMEM((pixels, channels), BF),
            pltpu.VMEM((tasks - 1, pixels, channels), BF),
        ]
        + [pltpu.SemaphoreType.DMA((tasks,))] * 2
        + [pltpu.SemaphoreType.DMA((pieces, tasks))] * 2
        + pair_scratch(batches, slots.shape[0] // pieces, width, BF) * pieces
        + pair_scratch(batches, gram_rows, width, kind)
        + pair_scratch(batches, head_rows, PANEL, BF)
        + [pltpu.SemaphoreType.DMA((2, max(chips, 4)))] * 2
        + [pltpu.SemaphoreType.DMA((tasks, chips))] * 2
        + [pltpu.SemaphoreType.DMA((tasks + 1, chips))] * 2
        + [pltpu.SemaphoreType.DMA((10,)), pltpu.SemaphoreType.DMA((2,))],
        5,
        60,
        flops=50000 * MIB,
        places_out="vhhvv",
    )
    outs = [shape(a.shape, F32) for a in (*rows, *matrices)]
    hbm = pl.BlockSpec(memory_space=pltpu.HBM)
    count = trunk_total + head_total
    shared = max(trunk_total, head_total)
    core = lax.rem(lax.axis_index("batch"), 2)
    own = (shared, channels, channels)
    *results, made_low = pl.pallas_call(
        renew_body,
        out_shape=(*outs[:8], shape(own, BF)),
        in_specs=[SMEM_SPEC] + [hbm] * 8,
        out_specs=(*(hbm for _ in outs[:8]), VMEM_SPEC),
        scratch_shapes=[pltpu.VMEM(square, F32)]
        + [pltpu.VMEM(own, F32)] * 2
        + [pltpu.VMEM(made[2].shape, kind), pltpu.VMEM(made[3].shape, BF)]
        + [pltpu.VMEM(made[0].shape, F32), pltpu.VMEM(made[1].shape, F32)]
        + [pltpu.SemaphoreType.DMA((2 * count + shared + 2,))]
        + [pltpu.SemaphoreType.DMA((8,))]
        + [pltpu.VMEM((PANEL, 2 * PANEL), F32)] * shared
        + [pltpu.VMEM((PANEL, PANEL), F32)] * shared,
        compiler_params=pltpu.CompilerParams(vmem_limit_bytes=60 * MIB),
        cost_estimate=pl.CostEstimate(
            flops=50000 * MIB, bytes_accessed=64 * MIB, transcendentals=0
        ),
    )(core.reshape(1), *made, *matrices)
    theirs = exchange_kernel(
        functools.partial(swap_body, batches),
        [shape(own, BF)],
        "v",
        (made_low,),
        [pltpu.SemaphoreType.DMA] * 2,
        6,
        60,
        flops=5000 * MIB,
    )[0]
    results += [
        jnp.where(core == which, made_low[:total], theirs[:total]).astype(F32)
        for which, total in enumerate((trunk_total, head_total))
    ]
    return input_grad, results


def local(
    tasks,
    batches,
    images,
    image_small,
    pool_index,
    row_slot,
    trunk_weight,
    trunk_mean_grad,
    trunk_mean_square,
    trunk_statistic,
    trunk_basis,
    head_weight,
    head_mean_grad,
    head_mean_square,
    head_statistic,
    head_basis,
    trunk_gain,
    trunk_offset,
    trunk_norm_mean_grad,
    trunk_norm_mean_square,
    head_gain,
    head_offset,
    head_norm_mean_grad,
    head_norm_mean_square,
    cotangent,
):
    number, height, breadth, channels = images.shape
    pixels = height * breadth
    shown = tasks * number
    geometry = (shown, height, breadth)
    task = lax.axis_index("task")
    width = channels // tasks

    def quarter(values):
        return lax.dynamic_slice_in_dim(values, task * width, width, values.ndim - 1)

    def inside(flags):
        row_limit = jnp.where(flags > 0, height // 2, height)[:, None, None]
        col_limit = jnp.where(flags > 0, breadth // 2, breadth)[:, None, None]
        return (jnp.arange(height, dtype=jnp.int32)[None, :, None] < row_limit) & (
            jnp.arange(breadth, dtype=jnp.int32)[None, None, :] < col_limit
        )

    cell = 2 * jnp.arange(2, dtype=jnp.int32)[:, None, None] + jnp.arange(2, dtype=jnp.int32)
    cells = pool_index.reshape(number, height // 2, 1, breadth // 2, 1)
    valid = inside(image_small)
    chosen = ((cells == cell).reshape(number, height, breadth) & valid).reshape(number, pixels)
    info = jnp.zeros((8 * number, channels), F32)
    info = info.at[::8, :pixels].set(chosen.astype(F32))
    info = info.at[1::8, 0].set(image_small.astype(F32))
    slots, x, infos, trunk_owners, head_low = arrive(
        tasks, batches, (number, height, breadth), images.reshape(number * pixels, channels),
        info, row_slot, trunk_weight, head_weight[0],
    )
    head_rows = lax.all_gather(head_low, "batch", axis=0, tiled=True)

    scales = quarter(jnp.stack([trunk_gain, trunk_offset], axis=1)).reshape(4, width)
    enc_totals, dec_totals, features, *kept = trunk_forward(
        geometry, tasks, batches, row_slot, infos, x, slots, scales
    )
    head_scales = jnp.stack([head_gain[0], head_offset[0]], axis=1).reshape(6, channels)
    pooled, upstream, head_sums, head_owned = head(
        geometry, tasks, batches, infos, features, head_rows,
        cotangent.reshape(shown, pixels // 4, channels), head_scales, enc_totals,
    )
    task_features = pooled.reshape(cotangent.shape)
    enc_grad, dec_grad, flow, norm_totals = trunk_backward(
        geometry, tasks, batches, infos, upstream, enc_totals, dec_totals, scales, (x, *kept)
    )
    input_grad, results = finish(
        tasks, batches,
        (to_slots(row_slot, enc_grad, dec_grad), flow, trunk_owners, head_owned),
        (trunk_weight, trunk_mean_grad, trunk_mean_square,
         head_weight[0], head_mean_grad[0], head_mean_square[0]),
        (trunk_statistic, head_statistic[0], trunk_basis, head_basis[0]),
    )
    input_grad = input_grad.reshape(images.shape)
    (
        trunk_weight_new, trunk_one_new, trunk_two_new,
        head_weight_new, head_one_new, head_two_new,
        trunk_stat_new, head_stat_new, trunk_basis_new, head_basis_new,
    ) = results

    trunk_norm = jnp.stack([trunk_gain, trunk_offset], axis=1)
    trunk_norm_grad = norm_totals[:4].reshape(2, 2, channels)[:, ::-1]
    trunk_norm_one, trunk_norm_two, trunk_direction = adam(
        trunk_norm_grad, trunk_norm_mean_grad, trunk_norm_mean_square
    )
    head_norm = jnp.stack([head_gain, head_offset], axis=2)
    head_norm_grad = head_sums[:6].reshape(1, 3, 2, channels)[:, :, ::-1]
    head_norm_one, head_norm_two, head_direction = adam(
        head_norm_grad, head_norm_mean_grad, head_norm_mean_square
    )
    return (
        task_features,
        input_grad,
        trunk_weight_new,
        trunk_one_new,
        trunk_two_new,
        trunk_stat_new,
        trunk_basis_new,
        head_weight_new[None],
        head_one_new[None],
        head_two_new[None],
        head_stat_new[None],
        head_basis_new[None],
        trunk_norm - LEARN_NORM * trunk_direction,
        trunk_norm_one,
        trunk_norm_two,
        head_norm - LEARN_NORM * head_direction,
        head_norm_one,
        head_norm_two,
    )


def solution(mesh):
    placed = (
        P(("task", "batch"), None, None, None),
        P(("task", "batch")),
        P(("task", "batch"), None, None),
        P(),
        P("batch", None),
        P("batch", None),
        P("batch", None),
        P(),
        P(),
        P("task", "batch", None),
        P("task", "batch", None),
        P("task", "batch", None),
        P("task", None, None, None),
        P("task", None, None, None),
        P(),
        P(),
        P(),
        P(),
        P("task", None, None),
        P("task", None, None),
        P("task", None, None, None),
        P("task", None, None, None),
        P("task", None, "batch", None, None, None),
    )
    return jax.shard_map(
        functools.partial(local, mesh.shape["task"], mesh.shape["batch"]),
        mesh=mesh,
        in_specs=placed,
        out_specs=(
            P("task", None, "batch", None, None, None),
            P(("task", "batch"), None, None, None),
            P("batch", None),
            P("batch", None),
            P("batch", None),
            P(),
            P(),
            P("task", "batch", None),
            P("task", "batch", None),
            P("task", "batch", None),
            P("task", None, None, None),
            P("task", None, None, None),
            P(),
            P(),
            P(),
            P("task", None, None, None),
            P("task", None, None, None),
            P("task", None, None, None),
        ),
        check_vma=False,
    )
```

```python
import functools

import jax
import jax.numpy as jnp
from jax import lax
from jax.experimental import pallas as pl
from jax.experimental.pallas import tpu as pltpu
from jax.sharding import PartitionSpec as P

STEP = 10


EPS = 1e-05
ADAM_EPS = 1e-08
BETA_ONE = 0.95
BETA_TWO = 0.95
STAT_DECAY = 0.95
LEARN_MATRIX = 0.02
LEARN_NORM = 0.5
DECAY_MATRIX = 0.01
BF = jnp.bfloat16
F32 = jnp.float32
MESH = pl.DeviceIdType.MESH
MIB = 1 << 20

VMEM_SPEC = pl.BlockSpec(memory_space=pltpu.VMEM)
SMEM_SPEC = pl.BlockSpec(memory_space=pltpu.SMEM)


def run(body, outs, specs, args, scratch=(), vmem=40, flops=0):
    size = sum(o.size * o.dtype.itemsize for o in outs) + sum(a.size * a.dtype.itemsize for a in args)
    return pl.pallas_call(
        body,
        out_shape=tuple(outs),
        in_specs=[SMEM_SPEC if s == "s" else VMEM_SPEC for s in specs],
        out_specs=tuple(VMEM_SPEC for _ in outs),
        scratch_shapes=list(scratch),
        compiler_params=pltpu.CompilerParams(vmem_limit_bytes=vmem * MIB),
        cost_estimate=pl.CostEstimate(flops=flops, bytes_accessed=size, transcendentals=0),
    )(*args)


def shape(dims, kind):
    return jax.ShapeDtypeStruct(tuple(dims), kind)


def dot(a, b):
    return jnp.dot(a, b, preferred_element_type=F32)


def dot_nt(a, b):
    return lax.dot_general(a, b, (((1,), (1,)), ((), ())), preferred_element_type=F32)


def dot_tn(a, b):
    return lax.dot_general(a, b, (((0,), (0,)), ((), ())), preferred_element_type=F32)


def split(a):
    high = a.astype(BF)
    return high, (a - high.astype(F32)).astype(BF)


def dot3(kind, a, b):
    dims = {dot: (1, 0), dot_nt: (1, 1), dot_tn: (0, 0)}[kind]
    a_high, a_low = split(a)
    b_high, b_low = split(b)
    return kind(
        jnp.concatenate([a_high, a_high, a_low], axis=dims[0]),
        jnp.concatenate([b_high, b_low, b_high], axis=dims[1]),
    )


def places(height, breadth):
    index = lax.broadcasted_iota(jnp.int32, (height * breadth, 1), 0)
    row = lax.div(index, breadth)
    return row, index - row * breadth


def valid_rows(kind, height, breadth, spot):
    row, col = spot
    shrunk = kind > 0
    row_limit = jnp.where(shrunk, height // 2, height)
    col_limit = jnp.where(shrunk, breadth // 2, breadth)
    return jnp.where((row < row_limit) & (col < col_limit), 1.0, 0.0).astype(F32)


def move(values, rows):
    gap = jnp.zeros((abs(rows),) + values.shape[1:], values.dtype)
    if rows > 0:
        return jnp.concatenate([gap, values[:-rows]], axis=0)
    return jnp.concatenate([values[-rows:], gap], axis=0)


def from_left(values, col):
    return jnp.where(col > 0, pltpu.roll(values, 1, 0), 0.0)


def from_right(values, col, breadth):
    return jnp.where(col < breadth - 1, pltpu.roll(values, values.shape[0] - 1, 0), 0.0)


def gather_taps(tap, breadth, col):
    lines = [move(tap(b), breadth) + tap(3 + b) + move(tap(6 + b), -breadth) for b in range(3)]
    return lines[1] + from_left(lines[0], col) + from_right(lines[2], col, breadth)


def spread_taps(values, breadth, col):
    lines = [from_right(values, col, breadth), values, from_left(values, col)]
    return [
        move(lines[b], breadth * (a - 1)) if a != 1 else lines[b] for a in range(3) for b in range(3)
    ]


def window_sum(values, row, col, breadth):
    count = values.shape[0]
    pair = values + jnp.where(
        col % 2 == 0, pltpu.roll(values, count - 1, 0), pltpu.roll(values, 1, 0)
    )
    return pair + jnp.where(row % 2 == 0, move(pair, -breadth), move(pair, breadth))


def sigmoid(values):
    return 0.5 * jnp.tanh(0.5 * values) + 0.5


def silu_back(scaled):
    sig = sigmoid(scaled)
    return sig * (1.0 + scaled * (1.0 - sig))


def col_sum(values):
    return jnp.sum(values, axis=0, keepdims=True)


def put_sums(ref, rows):
    width = ref.shape[1]
    rows = list(rows) + [jnp.zeros((1, width), F32)] * (8 - len(rows))
    ref[...] = jnp.concatenate(rows, axis=0)


def each_image(geometry, body, start):
    number, height, breadth = geometry
    pixels = height * breadth

    def step(image, carry):
        return body(image, pl.ds(pl.multiple_of(image * pixels, 16), pixels), carry)

    return lax.fori_loop(0, number, step, start)


def zero_rows(count, width):
    return (jnp.zeros((1, width), F32),) * count


def greet(axes):
    barrier = pltpu.get_barrier_semaphore()
    for axis, size in axes:
        me = lax.axis_index(axis)
        for step in range(1, size):
            pl.semaphore_signal(
                barrier, inc=1, device_id={axis: lax.rem(me + step, size)}, device_id_type=MESH
            )
    pl.semaphore_wait(barrier, sum(size - 1 for _, size in axes))


def remote(source, target, sends, receives, peer, axis):
    return pltpu.make_async_remote_copy(
        src_ref=source,
        dst_ref=target,
        send_sem=sends,
        recv_sem=receives,
        device_id={axis: peer},
        device_id_type=MESH,
    )


def pack(rows):
    parts = [row[:, i : i + 128] for row in rows for i in range(0, row.shape[1], 128)]
    parts += [jnp.zeros((1, 128), F32)] * (8 - len(parts))
    return jnp.concatenate(parts, axis=0)


def unpack(tile, count, width):
    per = width // 128
    return [
        jnp.concatenate([tile[k * per + i : k * per + i + 1, :] for i in range(per)], axis=1)
        for k in range(count)
    ]


def total_rows(k, axis, size, rows, mine, slots, sends, receives, meanwhile=None):
    me = lax.axis_index(axis)
    tile = pack(rows)
    mine[k] = tile
    slots[k, me] = tile
    for step in range(1, size):
        peer = lax.rem(me + step, size)
        remote(mine.at[k], slots.at[k, me], sends.at[k, step], receives.at[k, me], peer, axis).start()
    if meanwhile:
        meanwhile()
    for step in range(1, size):
        peer = lax.rem(me + size - step, size)
        remote(
            mine.at[k], slots.at[k, peer], sends.at[k, step], receives.at[k, peer], peer, axis
        ).wait_recv()
    total = slots[k, 0]
    for peer in range(1, size):
        total = total + slots[k, peer]
    for step in range(1, size):
        peer = lax.rem(me + step, size)
        remote(
            mine.at[k], slots.at[k, me], sends.at[k, step], receives.at[k, me], peer, axis
        ).wait_send()
    return unpack(total, len(rows), rows[0].shape[1])


def total_scratch(count, size):
    return [
        pltpu.VMEM((count, 8, 128), F32),
        pltpu.VMEM((count, size, 8, 128), F32),
        pltpu.SemaphoreType.DMA((count, size)),
        pltpu.SemaphoreType.DMA((count, size)),
    ]


def columns_of(place, width):
    return pl.ds(pl.multiple_of(place * width, 128), width)


SPECS = {"s": SMEM_SPEC, "v": VMEM_SPEC, "h": pl.BlockSpec(memory_space=pltpu.HBM)}


def exchange_kernel(body, outs, specs, args, scratch, identity, vmem, flops=0, places_out=None):
    size = sum(o.size * o.dtype.itemsize for o in outs) + sum(a.size * a.dtype.itemsize for a in args)
    return pl.pallas_call(
        body,
        out_shape=tuple(outs),
        in_specs=[SPECS[s] for s in specs],
        out_specs=tuple(SPECS[s] for s in places_out or "v" * len(outs)),
        scratch_shapes=list(scratch),
        compiler_params=pltpu.CompilerParams(
            vmem_limit_bytes=vmem * MIB, collective_id=identity, has_side_effects=True
        ),
        cost_estimate=pl.CostEstimate(flops=flops, bytes_accessed=size, transcendentals=0),
    )(*args)


def info_rows(infos, i):
    return infos[pl.ds(pl.multiple_of(i * 8, 8), 8), :]


def valid_of(infos, i, height, breadth, spot):
    return valid_rows(info_rows(infos, i)[1:2, 0:1], height, breadth, spot)


def chosen_cells(narrow, infos, i):
    return (narrow * info_rows(infos, i)[0:1, : narrow.shape[1]]).astype(BF)


def norm_moments(totals):
    total, squares, count = totals
    center = total / count
    return center, lax.rsqrt(squares / count - center * center + EPS)


def norm_line(totals, scale):
    center, inverse = norm_moments(totals)
    slope = inverse * scale[0]
    return slope, scale[1] - center * slope


def norm_sums(totals, sums):
    center, inverse = norm_moments(totals)
    return [sums[0], inverse * (sums[1] - center * sums[0])]


def norm_back_line(totals, sums, scale):
    center, inverse = norm_moments(totals)
    count = totals[2]
    slope = inverse * scale[0]
    lean = -slope * inverse * (sums[1] / count)
    return slope, lean, -slope * (sums[0] / count) - lean * center


def on_line(values, line):
    return values * line[0] + line[1]


def back_on_line(upstream, values, line, valid):
    return (upstream * line[0] + values * line[1] + line[2]) * valid


def silu(values):
    return values * sigmoid(values)


def window_count(height, breadth):
    return -(-(height * breadth // 4) // 16) * 16


def pool_choice(height, breadth, windows, flipped):
    pixels = height * breadth
    dims = (windows, pixels) if flipped else (pixels, windows)
    pixel = lax.broadcasted_iota(jnp.int32, dims, 1 if flipped else 0)
    window = lax.broadcasted_iota(jnp.int32, dims, 0 if flipped else 1)
    row = lax.div(pixel, breadth)
    col = pixel - row * breadth
    home = lax.div(row, 2) * (breadth // 2) + lax.div(col, 2)
    return jnp.where(home == window, 1.0, 0.0).astype(F32)


def rows_of(ref, first, count):
    return [ref[first + k : first + k + 1, :] for k in range(count)]


def window_rows(i, windows):
    return pl.ds(pl.multiple_of(i * windows, 16), windows)


def trunk_forward_body(
    geometry, tasks, batches,
    index, infos, x_far, kernel_slots, scales,
    enc_totals, dec_totals, features, *rest,
):
    kept, (enc_pre, dec_pre, spread), rest = rest[:5], rest[5:8], rest[8:]
    (
        x, x_loaded, enc_taps, dec_taps, wide, tap,
        work, pooled, pooled_all, part, pool_sends, pool_receives, sends, receives,
    mine, slots, total_sends, total_receives, saved,
    ) = rest
    number, height, breadth = geometry
    width = enc_pre.shape[1]
    windows = window_count(height, breadth)
    task = lax.axis_index("task")
    spot = places(height, breadth)
    _, col = spot
    choice = pool_choice(height, breadth, windows, True)
    narrow = choice.astype(BF)

    x_load = pltpu.make_async_copy(x_far, x, x_loaded)
    x_load.start()
    sources = (enc_taps, dec_taps, enc_pre, dec_pre, spread)
    saves = [pltpu.make_async_copy(a, b, saved.at[k]) for k, (a, b) in enumerate(zip(sources, kept))]
    channels = x.shape[1]

    def widen(i, carry):
        rows = pl.ds(pl.multiple_of(i * channels, 16), channels)
        wide[rows, :] = kernel_slots[rows, :].astype(F32)
        return carry

    def fetch(taps, first, begin, end):
        group = 32
        for p in range(begin, end):

            def some(i, carry):
                base = i * group
                for u in range(group):
                    slot = index[(first + p) * channels + base + u]
                    tap[pl.ds(base + u, 1), :] = wide[pl.ds(slot, 1), :]
                return carry

            lax.fori_loop(0, channels // group, some, 0)
            taps[:, p * width : (p + 1) * width] = tap[...].astype(BF)

    lax.fori_loop(0, wide.shape[0] // channels, widen, 0)
    fetch(enc_taps, 0, 0, 9)
    saves[0].start()
    x_load.wait()

    def conv(x, taps, pre):
        def image(i, rows, carry):
            valid = valid_of(infos, i, height, breadth, spot)
            work[...] = dot(x[rows, :], taps[...])
            out = gather_taps(lambda p: work[:, p * width : (p + 1) * width], breadth, col)
            pre[rows, :] = out
            kept = out * valid
            return (
                carry[0] + col_sum(kept),
                carry[1] + col_sum(kept * out),
                carry[2] + jnp.broadcast_to(col_sum(valid), (1, width)),
            )

        return each_image(geometry, image, zero_rows(3, width))

    def total(k, rows, meanwhile=None):
        return total_rows(
            k, "batch", batches, list(rows), mine, slots, total_sends, total_receives, meanwhile
        )

    sums = conv(x, enc_taps, enc_pre)
    saves[2].start()
    greet((("task", tasks), ("batch", batches)))
    totals = total(0, sums, lambda: fetch(dec_taps, 9, 0, 4))
    put_sums(enc_totals, totals)
    scale = rows_of(scales, 0, 2)

    def peer_of(step, incoming):
        return lax.rem(task + (tasks - step if incoming else step), tasks)

    def pool_copy(i, step, incoming=False):
        rows = window_rows(i, windows)
        peer = peer_of(step, incoming)
        target = pooled_all.at[rows, columns_of(peer if incoming else task, width)]
        return remote(
            pooled.at[rows, :], target, pool_sends.at[i, step], pool_receives.at[i, step], peer, "task"
        )

    line = norm_line(totals, scale)

    def pool(i, rows, carry):
        valid = valid_of(infos, i, height, breadth, spot)
        scaled = on_line(enc_pre[rows, :], line)
        high, low = split(silu(scaled) * valid)
        mean = ((dot(narrow, high) + dot(narrow, low)) * 0.25).astype(BF)
        here = window_rows(i, windows)
        pooled[here, :] = mean
        pooled_all[here, columns_of(task, width)] = mean
        for step in range(1, tasks):
            pool_copy(i, step).start()
        return carry

    each_image(geometry, pool, 0)
    fetch(dec_taps, 9, 4, 9)
    saves[1].start()

    def unpool(i, rows, carry):
        for step in range(1, tasks):
            pool_copy(i, step, True).wait_recv()
        wide = dot_tn(chosen_cells(choice, infos, i), pooled_all[window_rows(i, windows), :])
        spread[rows, :] = wide.astype(BF)
        return carry

    each_image(geometry, unpool, 0)
    saves[4].start()
    sums = conv(spread, dec_taps, dec_pre)
    saves[3].start()
    totals = total(1, sums)
    put_sums(dec_totals, totals)
    scale = rows_of(scales, 2, 2)

    def feature_copy(i, rows, step, incoming=False):
        peer = peer_of(step, incoming)
        target = features.at[rows, columns_of(peer if incoming else task, width)]
        return remote(
            part.at[rows, :], target, sends.at[i, step], receives.at[i, step], peer, "task"
        )

    last_line = norm_line(totals, scale)

    def finish(i, rows, carry):
        valid = valid_of(infos, i, height, breadth, spot)
        scaled = on_line(dec_pre[rows, :], last_line)
        low = (silu(scaled) * valid).astype(BF)
        part[rows, :] = low
        features[rows, columns_of(task, width)] = low
        for step in range(1, tasks):
            feature_copy(i, rows, step).start()
        return carry

    each_image(geometry, finish, 0)

    def settle(i, rows, carry):
        for step in range(1, tasks):
            feature_copy(i, rows, step, True).wait_recv()
            feature_copy(i, rows, step).wait_send()
            pool_copy(i, step).wait_send()
        return carry

    each_image(geometry, settle, 0)
    for copy in saves:
        copy.wait()


def trunk_forward(geometry, tasks, batches, index, infos, x, kernel_slots, scales):
    number, height, breadth = geometry
    pixels = height * breadth
    channels = x.shape[1]
    width = channels // tasks
    windows = window_count(height, breadth)
    tall = shape((x.shape[0], width), F32)
    taps = shape((channels, 9 * width), BF)
    outs = [
        shape((8, width), F32), shape((8, width), F32), shape(x.shape, BF),
        taps, taps,
        tall, tall, shape(x.shape, BF),
    ]
    return exchange_kernel(
        functools.partial(trunk_forward_body, geometry, tasks, batches),
        outs,
        "svhvv",
        (index, infos, x, kernel_slots, scales),
        [
            pltpu.VMEM(tall.shape, F32),
            pltpu.VMEM(tall.shape, F32),
            pltpu.VMEM(x.shape, BF),
            pltpu.VMEM(x.shape, BF),
            pltpu.SemaphoreType.DMA,
            pltpu.VMEM(taps.shape, BF),
            pltpu.VMEM(taps.shape, BF),
            pltpu.VMEM(kernel_slots.shape, F32),
            pltpu.VMEM((channels, width), F32),
            pltpu.VMEM((pixels, 9 * width), F32),
            pltpu.VMEM((number * windows, width), BF),
            pltpu.VMEM((number * windows, channels), BF),
            pltpu.VMEM((x.shape[0], width), BF),
        ]
        + [pltpu.SemaphoreType.DMA((number, tasks))] * 4
        + total_scratch(2, batches)
        + [pltpu.SemaphoreType.DMA((5,))],
        1,
        60,
        flops=4 * x.size * taps.shape[1],
        places_out="vvvhhhhh",
    )


def head_body(
    geometry, tasks, batches, summing,
    infos, features, weights, cotangent, scales, counts,
    task_out, upstream, sums_out, *rest,
):
    grads_out, rest = rest[0], rest[1:]
    (
        grads, pre_one, pre_two, pre_three, hidden, gated, nine, work, lower, out, arrived,
        sends, receives, mine, slots, total_sends, total_receives, loaded,
    ) = rest[:18]
    number, height, breadth = geometry
    channels = features.shape[1]
    width = channels // tasks
    windows = task_out.shape[1]
    task = lax.axis_index("task")
    half = work.shape[2]
    spot = places(height, breadth)
    _, col = spot
    widen = pool_choice(height, breadth, windows, False).astype(BF)
    narrow = pool_choice(height, breadth, windows, True).astype(BF)
    count = jnp.broadcast_to(counts[2:3, 0:1], (1, channels))
    cuts = (pl.ds(0, 2 * channels), pl.ds(2 * channels, 9 * channels))
    loads = [
        pltpu.make_async_copy(weights.at[cut, :], grads.at[cut, :], loaded.at[k])
        for k, cut in enumerate(cuts)
    ]
    for copy in loads:
        copy.start()
    first = grads.at[pl.ds(0, channels), :]
    second = grads.at[pl.ds(channels, channels), :]

    def kernel_rows(p):
        return pl.ds((2 + p) * channels, channels)

    def total(k, rows, meanwhile=None):
        return total_rows(
            k, "batch", batches, list(rows), mine, slots, total_sends, total_receives, meanwhile
        )

    if summing:
        near, near_sends, near_receives, summed, saved = rest[18:]
        place, core, chips = pair_place(batches)
        block = near.shape[1]

        def near_copy(chip):
            return remote(
                block_rows(grads, 2 * chip + 1 - core, block), near.at[chip],
                near_sends.at[chip], near_receives.at[chip], 2 * place + 1 - core, "batch",
            )

    def put_stats(pre, rows, value, valid, carry):
        pre[rows, :] = value
        kept = value * valid
        return carry[0] + col_sum(kept), carry[1] + col_sum(kept * value)

    nothing = zero_rows(2, channels)
    scale_one, scale_two, scale_three = (rows_of(scales, 2 * k, 2) for k in range(3))

    loads[0].wait()

    def first_step(i, rows, carry):
        valid = valid_of(infos, i, height, breadth, spot)
        return put_stats(pre_one, rows, dot(features[rows, :], first[...]), valid, carry)

    sums = each_image(geometry, first_step, nothing)
    greet((("task", tasks), ("batch", batches)))
    totals_one = total(0, sums) + [count]

    line_one = norm_line(totals_one, scale_one)

    def second_step(i, rows, carry):
        valid = valid_of(infos, i, height, breadth, spot)
        scaled = on_line(pre_one[rows, :], line_one)
        low = (silu(scaled) * valid).astype(BF)
        hidden[rows, :] = low
        return put_stats(pre_two, rows, dot(low, second[...]), valid, carry)

    sums = each_image(geometry, second_step, nothing)
    totals_two = total(1, sums) + [count]

    line_two = norm_line(totals_two, scale_two)

    def third_step(i, rows, carry):
        valid = valid_of(infos, i, height, breadth, spot)
        scaled = on_line(pre_two[rows, :], line_two)
        low = (sigmoid(scaled) * features[rows, :].astype(F32)).astype(BF)
        gated[rows, :] = low
        parts = []
        for j in range(channels // half):
            cut = slice(j * half, (j + 1) * half)
            for p in range(9):
                work[p] = dot(low, grads[kernel_rows(p), cut])
            parts.append(gather_taps(lambda p: work[p], breadth, col))
        return put_stats(pre_three, rows, jnp.concatenate(parts, axis=1), valid, carry)

    loads[1].wait()
    sums = each_image(geometry, third_step, nothing)
    totals_three = total(2, sums) + [count]

    line_three = norm_line(totals_three, scale_three)

    def out_step(i, rows, carry):
        valid = valid_of(infos, i, height, breadth, spot)
        values = pre_three[rows, :]
        scaled = on_line(values, line_three)
        high, low = split(silu(scaled) * valid)
        mean = (dot(narrow, high) + dot(narrow, low)) * 0.25
        task_out[i] = mean.astype(BF)
        dy = silu_back(scaled) * dot(widen, cotangent[i]) * 0.25 * valid
        lower[rows, :] = dy
        return carry[0] + col_sum(dy), carry[1] + col_sum(dy * values)

    sums = each_image(geometry, out_step, nothing)
    sums_three = total(3, norm_sums(totals_three, sums))
    back_three = norm_back_line(totals_three, sums_three, scale_three)

    def third_back(i, rows, carry):
        valid = valid_of(infos, i, height, breadth, spot)
        dz = back_on_line(lower[rows, :], pre_three[rows, :], back_three, valid)
        for p, moved in enumerate(spread_taps(dz, breadth, col)):
            nine[p, rows, :] = moved.astype(BF)
        flow = None
        for p in range(9):
            piece = dot_nt(nine[p, rows, :], grads[kernel_rows(p), :])
            flow = piece if flow is None else flow + piece
        values = pre_two[rows, :]
        gate = sigmoid(on_line(values, line_two))
        flow = flow * gate
        lower[rows, :] = flow
        dy = flow * features[rows, :].astype(F32) * (1.0 - gate)
        pre_three[rows, :] = dy
        return carry[0] + col_sum(dy), carry[1] + col_sum(dy * values)

    sums = each_image(geometry, third_back, nothing)

    def taps(begin, end):
        def tap(p, carry):
            rows = pl.ds(pl.multiple_of((2 + p) * channels, channels), channels)
            grads[rows, :] = dot_tn(gated[...], nine[p]).astype(BF)
            return carry

        lax.fori_loop(begin, end, tap, 0)

    sums_two = total(4, norm_sums(totals_two, sums), lambda: taps(0, 2))
    back_two = norm_back_line(totals_two, sums_two, scale_two)

    def second_back(i, rows, carry):
        valid = valid_of(infos, i, height, breadth, spot)
        dz = back_on_line(pre_three[rows, :], pre_two[rows, :], back_two, valid).astype(BF)
        out[rows, :] = dz
        values = pre_one[rows, :]
        dy = silu_back(on_line(values, line_one)) * dot_nt(dz, second[...])
        pre_three[rows, :] = dy
        return carry[0] + col_sum(dy), carry[1] + col_sum(dy * values)

    sums = each_image(geometry, second_back, nothing)

    def weight_rows():
        grads[pl.ds(channels, channels), :] = dot_tn(hidden[...], out[...]).astype(BF)
        taps(2, 3)

    sums_one = total(5, norm_sums(totals_one, sums), weight_rows)
    back_one = norm_back_line(totals_one, sums_one, scale_one)

    def flow_copy(i, rows, step, incoming=False):
        peer = lax.rem(task + (tasks - step if incoming else step), tasks)
        return remote(
            out.at[rows, columns_of(peer, width)], arrived.at[step - 1, rows, :],
            sends.at[i, step], receives.at[i, step], peer, "task",
        )

    def first_back(i, rows, carry):
        valid = valid_of(infos, i, height, breadth, spot)
        dz = back_on_line(pre_three[rows, :], pre_one[rows, :], back_one, valid).astype(BF)
        hidden[rows, :] = dz
        flow = (lower[rows, :] + dot_nt(dz, first[...])) * valid
        out[rows, :] = flow.astype(BF)
        for step in range(1, tasks):
            flow_copy(i, rows, step).start()
        return carry

    each_image(geometry, first_back, 0)
    taps(3, 9)
    if summing:
        for chip in range(1, chips):
            near_copy(chip).start()
    grads[pl.ds(0, channels), :] = dot_tn(features[...], hidden[...]).astype(BF)
    if summing:
        near_copy(0).start()
        for chip in (*range(1, chips), 0):
            near_copy(chip).wait_recv()
            own = block_rows(grads, 2 * chip + core, block)[...].astype(F32)
            summed[chip] = (own + near[chip].astype(F32)).astype(BF)
            pltpu.make_async_copy(summed.at[chip], grads_out.at[chip], saved.at[chip]).start()
    else:
        grads_out[...] = grads[...]
    put_sums(sums_out, sums_one + sums_two + sums_three)

    def settle(i, rows, carry):
        for step in range(1, tasks):
            flow_copy(i, rows, step, True).wait_recv()
        flow = out[rows, columns_of(task, width)].astype(F32)
        for step in range(1, tasks):
            flow = flow + arrived[step - 1, rows, :].astype(F32)
        upstream[rows, :] = flow
        for step in range(1, tasks):
            flow_copy(i, rows, step).wait_send()
        return carry

    each_image(geometry, settle, 0)
    if summing:
        for chip in range(chips):
            near_copy(chip).wait_send()
            pltpu.make_async_copy(summed.at[chip], grads_out.at[chip], saved.at[chip]).wait()


def head(geometry, tasks, batches, infos, features, weights, cotangent, scales, counts):
    number, height, breadth = geometry
    pixels = height * breadth
    total, channels = features.shape
    width = channels // tasks
    block = weights.shape[0] // batches
    chips = batches // 2
    summing = block % 16 == 0
    outs = [
        shape((number, pixels // 4, channels), BF),
        shape((total, width), F32),
        shape((8, channels), F32),
        shape((chips, block, channels) if summing else weights.shape, BF),
    ]
    scratch = []
    if summing:
        scratch = [pltpu.VMEM((chips, block, channels), BF)]
        scratch += [pltpu.SemaphoreType.DMA((chips,))] * 2
        scratch += [pltpu.VMEM((chips, block, channels), BF), pltpu.SemaphoreType.DMA((chips,))]
    pooled, upstream, sums, grads = exchange_kernel(
        functools.partial(head_body, geometry, tasks, batches, summing),
        outs,
        "vvhvvv",
        (infos, features, weights, cotangent, scales, counts),
        [
            pltpu.VMEM(weights.shape, BF),
            pltpu.VMEM(features.shape, F32),
            pltpu.VMEM(features.shape, F32),
            pltpu.VMEM(features.shape, F32),
            pltpu.VMEM(features.shape, BF),
            pltpu.VMEM(features.shape, BF),
            pltpu.VMEM((9,) + features.shape, BF),
            pltpu.VMEM((9, pixels, min(channels, 256)), F32),
            pltpu.VMEM(features.shape, F32),
            pltpu.VMEM(features.shape, BF),
            pltpu.VMEM((tasks - 1, total, width), BF),
        ]
        + [pltpu.SemaphoreType.DMA((number, tasks))] * 2
        + total_scratch(6, batches)
        + [pltpu.SemaphoreType.DMA((2,))]
        + scratch,
        2,
        61,
        flops=6 * total * channels * weights.shape[0],
        places_out="vvvh" if summing else "vvvv",
    )
    if summing:
        groups = [list(range(core, batches, 2)) for core in range(2)]
        half = channels // 2
        owned = jnp.concatenate(
            [
                lax.psum_scatter(
                    grads.reshape(chips * block, channels)[:, cut : cut + half], "batch",
                    scatter_dimension=0, axis_index_groups=groups, tiled=True,
                )
                for cut in (0, half)
            ],
            axis=1,
        )
    else:
        owned = lax.psum_scatter(grads, "batch", scatter_dimension=0, tiled=True)
    return pooled, upstream, sums, owned


def trunk_backward_body(
    geometry, tasks, batches,
    infos, upstream, enc_totals, dec_totals, scales, *rest,
):
    kept, rest = rest[:6], rest[6:]
    outs, sums_out, rest = rest[:3], rest[3], rest[4:]
    (x, enc_taps, dec_taps, enc_pre, dec_pre, spread), rest = rest[:6], rest[6:]
    (
        nine, change, packed, arrived, pooled, sends, receives,
        mine, slots, total_sends, total_receives, loaded,
        enc_grad, dec_grad, flow_out, saved, sums_own, sum_sends, sum_receives,
    ) = rest
    saves = [
        pltpu.make_async_copy(a, b, saved.at[k])
        for k, (a, b) in enumerate(zip((enc_grad, dec_grad, flow_out), outs))
    ]
    targets = (x, enc_taps, dec_taps, enc_pre, dec_pre, spread)
    loads = [pltpu.make_async_copy(a, b, loaded.at[k]) for k, (a, b) in enumerate(zip(kept, targets))]
    for k in (4, 2, 5, 3, 1, 0):
        loads[k].start()
    number, height, breadth = geometry
    channels = x.shape[1]
    width = enc_pre.shape[1]
    windows = window_count(height, breadth)
    task = lax.axis_index("task")
    spot = places(height, breadth)
    _, col = spot
    widen = pool_choice(height, breadth, windows, False).astype(BF)
    narrow = pool_choice(height, breadth, windows, True)
    nothing = zero_rows(2, width)

    def total(k, rows):
        return total_rows(
            k, "batch", batches, list(rows), mine, slots, total_sends, total_receives
        )

    def change_of(pre, totals, scale, flow):
        line = norm_line(totals, scale)

        def image(i, rows, carry):
            valid = valid_of(infos, i, height, breadth, spot)
            values = pre[rows, :]
            dy = silu_back(on_line(values, line)) * flow(i, rows) * valid
            change[rows, :] = dy
            return carry[0] + col_sum(dy), carry[1] + col_sum(dy * values)

        return norm_sums(totals, each_image(geometry, image, nothing))

    def back(pre, totals, scale, sums, taps, put):
        line = norm_back_line(totals, sums, scale)

        def image(i, rows, carry):
            valid = valid_of(infos, i, height, breadth, spot)
            dz = back_on_line(change[rows, :], pre[rows, :], line, valid)
            for p, moved in enumerate(spread_taps(dz, breadth, col)):
                nine[rows, p * width : (p + 1) * width] = moved.astype(BF)
            put(i, rows, dot_nt(nine[rows, :], taps[...]) * valid)
            return carry

        each_image(geometry, image, 0)

    totals = rows_of(dec_totals, 0, 3)
    scale = rows_of(scales, 2, 2)
    loads[4].wait()
    sums = change_of(dec_pre, totals, scale, lambda i, rows: upstream[rows, :])
    greet((("task", tasks), ("batch", batches)))
    dec_sums = total(0, sums)

    def copy_of(i, step, incoming=False):
        rows = window_rows(i, windows)
        peer = lax.rem(task + (tasks - step if incoming else step), tasks)
        return remote(
            packed.at[rows, columns_of(peer, width)], arrived.at[step - 1, rows, :],
            sends.at[i, step], receives.at[i, step], peer, "task",
        )

    def put_packed(i, rows, flow):
        chosen = chosen_cells(narrow, infos, i)
        packed[window_rows(i, windows), :] = dot(chosen, flow.astype(BF)).astype(BF)
        for step in range(1, tasks):
            copy_of(i, step).start()

    loads[2].wait()
    back(dec_pre, totals, scale, dec_sums, dec_taps, put_packed)
    loads[5].wait()
    dec_grad[...] = dot_tn(spread[...], nine[...])
    saves[1].start()

    def collect(i, carry):
        for step in range(1, tasks):
            copy_of(i, step, True).wait_recv()
        rows = window_rows(i, windows)
        flow = packed[rows, columns_of(task, width)].astype(F32)
        for step in range(1, tasks):
            flow = flow + arrived[step - 1, rows, :].astype(F32)
        pooled[rows, :] = flow
        for step in range(1, tasks):
            copy_of(i, step).wait_send()
        return carry

    lax.fori_loop(0, number, collect, 0)

    def widened(i, rows):
        high, low = split(pooled[window_rows(i, windows), :])
        return (dot(widen, high) + dot(widen, low)) * 0.25

    totals = rows_of(enc_totals, 0, 3)
    scale = rows_of(scales, 0, 2)
    loads[3].wait()
    sums = change_of(enc_pre, totals, scale, widened)
    enc_sums = total(1, sums)
    put_sums(sums_own, enc_sums + dec_sums)

    def sum_copy(step, incoming=False):
        peer = lax.rem(task + (tasks - step if incoming else step), tasks)
        home = peer if incoming else task
        return remote(sums_own, sums_out.at[:, columns_of(home, width)], sum_sends.at[step],
                      sum_receives.at[step], peer, "task")

    for step in range(1, tasks):
        sum_copy(step).start()
    sums_out[:, columns_of(task, width)] = sums_own[...]

    def put_flow(i, rows, flow):
        flow_out[rows, :] = flow.astype(BF)

    loads[1].wait()
    back(enc_pre, totals, scale, enc_sums, enc_taps, put_flow)
    loads[0].wait()
    saves[2].start()
    enc_grad[...] = dot_tn(x[...], nine[...])
    saves[0].start()
    for copy in saves:
        copy.wait()
    for step in range(1, tasks):
        sum_copy(step, True).wait_recv()
        sum_copy(step).wait_send()


def trunk_backward(
    geometry, tasks, batches, infos, upstream, enc_totals, dec_totals, scales, kept
):
    number, height, breadth = geometry
    x, enc_taps, dec_taps = kept[:3]
    total, channels = x.shape
    width = channels // tasks
    windows = window_count(height, breadth)
    outs = [
        shape(enc_taps.shape, F32),
        shape(dec_taps.shape, F32),
        shape(x.shape, BF),
        shape((8, channels), F32),
    ]
    return exchange_kernel(
        functools.partial(trunk_backward_body, geometry, tasks, batches),
        outs,
        "vvvvvhhhhhh",
        (infos, upstream, enc_totals, dec_totals, scales, *kept),
        [pltpu.VMEM(a.shape, a.dtype) for a in kept]
        + [
            pltpu.VMEM((total, 9 * width), BF),
            pltpu.VMEM((total, width), F32),
            pltpu.VMEM((number * windows, channels), BF),
            pltpu.VMEM((tasks - 1, number * windows, width), BF),
            pltpu.VMEM((number * windows, width), F32),
        ]
        + [pltpu.SemaphoreType.DMA((number, tasks))] * 2
        + total_scratch(2, batches)
        + [pltpu.SemaphoreType.DMA((6,))]
        + [pltpu.VMEM(a.shape, a.dtype) for a in outs[:3]]
        + [pltpu.SemaphoreType.DMA((3,)), pltpu.VMEM((8, width), F32)]
        + [pltpu.SemaphoreType.DMA((tasks,))] * 2,
        3,
        60,
        flops=8 * x.size * enc_taps.shape[1],
        places_out="hhhv",
    )


def to_slots_body(index, enc_far, dec_far, slots, enc, dec, wide, low, load, save):
    count = wide.shape[0]
    channels = enc.shape[0]
    width = wide.shape[1]
    step = 1024
    group = 32
    loads = [
        pltpu.make_async_copy(a, b, load.at[k])
        for k, (a, b) in enumerate(((dec_far, dec), (enc_far, enc)))
    ]
    for copy in loads:
        copy.start()
    for kernel, copy in ((1, loads[0]), (0, loads[1])):
        copy.wait()
        source = dec if kernel else enc
        for q in range(9):

            def place(i, carry):
                base = pl.multiple_of(i * group, group)
                first = (9 * kernel + q) * channels + base
                values = source[pl.ds(base, group), q * width : (q + 1) * width]
                for u in range(group):
                    wide[pl.ds(index[first + u], 1), :] = values[u : u + 1, :]
                return carry

            lax.fori_loop(0, channels // group, place, 0)

    def out(i):
        rows = pl.ds(pl.multiple_of(i * step, step), step)
        return pltpu.make_async_copy(low.at[rows, :], slots.at[rows, :], save.at[i])

    def narrow(i, carry):
        rows = pl.ds(pl.multiple_of(i * step, step), step)
        low[rows, :] = wide[rows, :].astype(BF)
        out(i).start()
        return carry

    def end(i, carry):
        out(i).wait()
        return carry

    lax.fori_loop(0, count // step, narrow, 0)
    lax.fori_loop(0, count // step, end, 0)


def to_slots(index, enc, dec):
    width = enc.shape[1] // 9
    dims = (index.shape[0], width)
    far = pl.BlockSpec(memory_space=pltpu.HBM)
    return pl.pallas_call(
        to_slots_body,
        out_shape=shape(dims, BF),
        in_specs=[SMEM_SPEC, far, far],
        out_specs=far,
        scratch_shapes=[
            pltpu.VMEM(enc.shape, F32),
            pltpu.VMEM(dec.shape, F32),
            pltpu.VMEM(dims, F32),
            pltpu.VMEM(dims, BF),
            pltpu.SemaphoreType.DMA((2,)),
            pltpu.SemaphoreType.DMA((dims[0] // 1024,)),
        ],
        compiler_params=pltpu.CompilerParams(vmem_limit_bytes=60 * MIB),
        cost_estimate=pl.CostEstimate(flops=10000 * MIB, bytes_accessed=8 * MIB, transcendentals=0),
    )(index, enc, dec)


def adam(gradient, moment_one, moment_two):
    new_one = BETA_ONE * moment_one + (1.0 - BETA_ONE) * gradient
    new_two = BETA_TWO * moment_two + (1.0 - BETA_TWO) * gradient * gradient
    direction = (
        new_one / (1.0 - BETA_ONE**STEP) / (jnp.sqrt(new_two / (1.0 - BETA_TWO**STEP)) + ADAM_EPS)
    )
    return new_one, new_two, direction


def pair_place(batches):
    me = lax.axis_index("batch")
    place = lax.div(me, 2)
    return place, me - 2 * place, batches // 2


def greet_pairs(tasks, batches):
    place, core, chips = pair_place(batches)
    task = lax.axis_index("task")
    barrier = pltpu.get_barrier_semaphore()

    def signal(device):
        pl.semaphore_signal(barrier, inc=1, device_id=device, device_id_type=MESH)

    for step in range(1, tasks):
        signal({"task": lax.rem(task + step, tasks)})
    signal({"batch": 2 * place + 1 - core})
    for step in range(1, chips):
        signal({"batch": 2 * lax.rem(place + step, chips) + core})
    pl.semaphore_wait(barrier, tasks - 1 + chips)


def block_rows(ref, index, count):
    return ref.at[pl.ds(pl.multiple_of(index * count, 8), count), :]


SMALL = 128 * 128


def far_first(chips):
    return sorted(range(chips), key=lambda step: -min(step, chips - step))


def pair_sum(batches, rows_of_block, own_block, near, paired, far, sems):
    place, core, chips = pair_place(batches)
    count = near.shape[1]
    near_send, near_receive, far_send, far_receive = sems
    other = 2 * place + 1 - core
    ring = chips == 4 and count % 32 == 0 and near.shape[2] * count > SMALL
    half = count // 2
    halves = (pl.ds(0, half), pl.ds(half, half))

    def near_copy(step):
        chip = lax.rem(place + step, chips)
        return remote(rows_of_block(2 * chip + 1 - core), near.at[step],
                      near_send.at[step], near_receive.at[step], other, "batch")

    def far_copy(step, incoming=False):
        chip = lax.rem(place + (chips - step if incoming else step), chips)
        return remote(paired.at[step], far.at[step], far_send.at[step], far_receive.at[step],
                      2 * chip + core, "batch")

    def ring_copy(which, way):
        chip = lax.rem(place + (1 if way == 0 else chips - 1), chips)
        if which == 0:
            source, target = paired.at[2, halves[way], :], far.at[2 + way, halves[0], :]
        else:
            cut = halves[way] if which == 2 else halves[1 - way]
            source, target = paired.at[1 if way == 0 else 3, cut, :], far.at[way, cut, :]
        k = 2 * which + way
        return remote(source, target, far_send.at[k], far_receive.at[k], 2 * chip + core, "batch")

    def start():
        for step in far_first(chips):
            near_copy(step).start()

    def middle():
        for step in far_first(chips):
            near_copy(step).wait_recv()
            if step:
                paired[step] = (own_block(step) + near[step].astype(F32)).astype(paired.dtype)
                if not ring:
                    far_copy(step).start()
                elif step == 2:
                    ring_copy(0, 0).start()
                    ring_copy(0, 1).start()
                else:
                    ring_copy(1, 0 if step == 1 else 1).start()

    def relay():
        if not ring:
            return
        for way in range(2):
            ring_copy(0, way).wait_recv()
            step = 1 if way == 0 else 3
            total = paired[step, halves[way], :].astype(F32) + far[2 + way, halves[0], :].astype(F32)
            paired[step, halves[way], :] = total.astype(paired.dtype)
            ring_copy(2, way).start()

    def end():
        total = own_block(0) + near[0].astype(F32)
        if ring:
            for way in range(2):
                ring_copy(1, way).wait_recv()
                ring_copy(2, way).wait_recv()
                total = total + far[way].astype(F32)
            for k in range(3):
                for way in range(2):
                    ring_copy(k, way).wait_send()
        else:
            for step in range(1, chips):
                far_copy(step, True).wait_recv()
                total = total + far[step].astype(F32)
            for step in range(1, chips):
                far_copy(step).wait_send()
        for step in range(chips):
            near_copy(step).wait_send()
        return total

    return start, middle, relay, end


def blocks_in(source, batches, count, piece=0, pieces=1):
    place, core, chips = pair_place(batches)

    def rows(index):
        start = (index * pieces + piece) * count
        return source.at[pl.ds(pl.multiple_of(start, 8), count), :]

    def own(step):
        chip = lax.rem(place + step, chips)
        return rows(2 * chip + core)[...].astype(F32)

    return rows, own


def pair_scratch(batches, rows, width, kind):
    chips = batches // 2
    return [pltpu.VMEM((chips, rows // batches, width), kind)] * 3 + [
        pltpu.SemaphoreType.DMA((max(chips, 6),))
    ] * 4


def chip_spread(batches, block, sends, receives):
    place, core, chips = pair_place(batches)
    count, width = block(place).shape
    ring = chips == 4 and count % 32 == 0 and width * count > SMALL
    half = count // 2

    def copy(step, incoming=False):
        peer = lax.rem(place + (chips - step if incoming else step), chips)
        ref = block(peer if incoming else place)
        return remote(ref, ref, sends.at[step], receives.at[step], 2 * peer + core, "batch")

    def pass_on(way, incoming=False):
        step = 1 if way == 0 else chips - 1
        peer = lax.rem(place + (chips - step if incoming else step), chips)
        home = lax.rem(place + (2 if incoming else chips - step), chips)
        ref = block(home).at[pl.ds(way * half, half), :]
        k = 2 if way == 0 else 0
        return remote(ref, ref, sends.at[k], receives.at[k], 2 * peer + core, "batch")

    steps = (1, chips - 1) if ring else tuple(range(1, chips))

    def start():
        for step in steps:
            copy(step).start()

    def relay():
        if ring:
            for way, step in enumerate(steps):
                copy(step, True).wait_recv()
                pass_on(way).start()

    def settle():
        if ring:
            for way in range(2):
                pass_on(way, True).wait_recv()
        else:
            for step in steps:
                copy(step, True).wait_recv()

    def drain():
        for step in steps:
            copy(step).wait_send()
        if ring:
            for way in range(2):
                pass_on(way).wait_send()

    return start, relay, settle, drain


def arrive_body(
    tasks, batches, geometry,
    image_raw, info, index, weight, head_weight,
    slots, x, infos, owners, head_low,
    image, head_raw, head_loaded, raw, raw_loaded, x_send, x_receive, info_send, info_receive,
    chip_send, chip_receive, pair_send, pair_receive, own,
):
    task = lax.axis_index("task")
    place, core, chips = pair_place(batches)
    count, width = raw.shape
    load = pltpu.make_async_copy(weight.at[:, columns_of(task, width)], raw, raw_loaded)
    load.start()
    head_load = pltpu.make_async_copy(head_weight, head_raw, head_loaded)
    head_load.start()
    number, height, breadth = geometry
    pixels = height * breadth
    for n in range(number):
        valid = valid_rows(
            info[8 * n + 1 : 8 * n + 2, 0:1], height, breadth, places(height, breadth)
        )
        rows = slice(n * pixels, (n + 1) * pixels)
        image[rows, :] = (image_raw[rows, :].astype(F32) * valid).astype(BF)
    greet_pairs(tasks, batches)

    def task_copy(source, target, sends, receives, step, incoming=False):
        peer = lax.rem(task + (tasks - step if incoming else step), tasks)
        home = peer if incoming else task
        return remote(source, block_rows(target, home, source.shape[0]), sends.at[step],
                      receives.at[step], peer, "task")

    def moves(step, incoming=False):
        return (
            task_copy(info, infos, info_send, info_receive, step, incoming),
            task_copy(image, x, x_send, x_receive, step, incoming),
        )

    def block(chip):
        return block_rows(slots, 2 * chip + core, count)

    def pair_copy(hop, incoming=False):
        chip = lax.rem(place + chips - hop, chips)
        ref = block_rows(slots, 2 * chip + (1 - core if incoming else core), count)
        return remote(ref, ref, pair_send.at[hop], pair_receive.at[hop], 2 * place + 1 - core, "batch")

    start, relay, settle, drain = chip_spread(batches, block, chip_send, chip_receive)
    ring = chips == 4 and count % 32 == 0 and width * count > SMALL
    load.wait()
    block(place)[...] = raw[...].astype(BF)
    start()
    pair_copy(0).start()
    for step in range(1, tasks):
        for copy in moves(step):
            copy.start()
    locals_ = [
        pltpu.make_async_copy(image, block_rows(x, task, image.shape[0]), own.at[0]),
        pltpu.make_async_copy(info, block_rows(infos, task, info.shape[0]), own.at[1]),
    ]
    for copy in locals_:
        copy.start()
    mine = lax.broadcasted_iota(jnp.int32, (count, 1), 0) + lax.axis_index("batch") * count
    found = jnp.zeros((count, 128), F32)
    for k in range(index.shape[0] // 2, index.shape[0]):
        found = jnp.where(index[k : k + 1, :] == mine, 1.0, found)
    found = jnp.max(found, axis=1, keepdims=True)
    owners[:, 0:1] = 1.0 - found
    owners[:, 1:2] = found
    head_load.wait()
    head_low[...] = head_raw[...].astype(BF)
    relay()
    if ring:
        pair_copy(1).start()
        pair_copy(3).start()
        settle()
        pair_copy(2).start()
    else:
        settle()
        for hop in range(1, chips):
            pair_copy(hop).start()
    for copy in locals_:
        copy.wait()
    for step in range(1, tasks):
        for copy in moves(step, True):
            copy.wait_recv()
    for hop in range(chips):
        pair_copy(hop, True).wait_recv()
    for step in range(1, tasks):
        for copy in moves(step):
            copy.wait_send()
    for hop in range(chips):
        pair_copy(hop).wait_send()
    drain()


def arrive(tasks, batches, geometry, image, info, index, weight, head_weight):
    count, channels = weight.shape
    width = channels // tasks
    chips = batches // 2
    return exchange_kernel(
        functools.partial(arrive_body, tasks, batches, geometry),
        [
            shape((count * batches, width), BF),
            shape((image.shape[0] * tasks, channels), BF),
            shape((info.shape[0] * tasks, info.shape[1]), F32),
            shape((count, 2), F32),
            shape(head_weight.shape, BF),
        ],
        "vvvhh",
        (image, info, index.reshape(-1, 128), weight, head_weight),
        [
            pltpu.VMEM(image.shape, BF),
            pltpu.VMEM(head_weight.shape, F32),
            pltpu.SemaphoreType.DMA,
            pltpu.VMEM((count, width), F32),
            pltpu.SemaphoreType.DMA,
        ]
        + [pltpu.SemaphoreType.DMA((tasks,))] * 4
        + [pltpu.SemaphoreType.DMA((max(chips, 4),))] * 4
        + [pltpu.SemaphoreType.DMA((2,))],
        4,
        60,
        flops=20000 * MIB,
    )


def soap_rows(cuts, grad, owners, state, low, first, begin=0, end=None):
    total = grad.shape[0]

    def chunk(i, carry):
        rows = pl.ds(pl.multiple_of(i * (total // cuts), 8), total // cuts)
        values = grad[rows, :].astype(F32)
        marks = owners(i * (total // cuts), total // cuts)
        count = len(marks)
        rotated = None
        for m in range(count):
            part = dot((values * marks[m]).astype(BF), low[first + m])
            rotated = part if rotated is None else rotated + part
        new_one, new_two, direction = adam(rotated, state[1, rows, :], state[2, rows, :])
        state[1, rows, :] = new_one
        state[2, rows, :] = new_two
        stepped = None
        for m in range(count):
            part = dot_nt((direction * marks[m]).astype(BF), low[first + m])
            stepped = part if stepped is None else stepped + part
        old = state[0, rows, :]
        state[0, rows, :] = old - LEARN_MATRIX * (stepped + DECAY_MATRIX * old)
        return carry

    lax.fori_loop(begin, cuts if end is None else end, chunk, 0)


def factor_rows(values, identity, turn):
    size, width = values.shape
    sub = lax.broadcasted_iota(jnp.int32, (size, width), 0)
    rolled = pltpu.roll(values, turn, 1)
    columns = [jnp.broadcast_to(rolled[:, j : j + 1], (size, width)) for j in range(size)]
    scale = jnp.zeros((size, width), F32)
    for j in range(size):
        root = lax.rsqrt(columns[j][j : j + 1, :])
        scale = jnp.where(sub == j, root, scale)
        lower = jnp.where(sub > j, columns[j] * root, 0.0)
        values = values - lower * (values[j : j + 1, :] * root)
        identity = identity - lower * (identity[j : j + 1, :] * root)
        for i in range(j + 1, size):
            columns[i] = columns[i] - lower * (columns[i][j : j + 1, :] * root)
    return values * scale, identity * scale


GROUP = 16
PANEL = 128


def upper_blocks(size):
    return [(a, b) for a in range(0, size, PANEL) for b in range(a, size, PANEL)]


def renew_panel(k, product, made, tables, inverses):
    count, size = product.shape[0], product.shape[1]
    here = slice(k * PANEL, (k + 1) * PANEL)
    row = lax.broadcasted_iota(jnp.int32, (PANEL, PANEL), 0)
    col = lax.broadcasted_iota(jnp.int32, (PANEL, PANEL), 1)
    unit = jnp.where(row == col, 1.0, 0.0).astype(F32)
    for n in range(count):
        tables[n][:, :PANEL] = dot3(dot_tn, product[n, :, here], product[n, :, here])
        tables[n][:, PANEL:] = unit

    for first in range(0, PANEL, GROUP):
        rows, rest = slice(first, first + GROUP), slice(first + GROUP, PANEL)
        done = [
            factor_rows(tables[n][rows, :PANEL], tables[n][rows, PANEL:], (PANEL - first) % PANEL)
            for n in range(count)
        ]
        for n in range(count):
            upper, inverse = done[n]
            inverses[n][rows, :] = inverse
            if first + GROUP < PANEL:
                both = jnp.concatenate([upper, inverse], axis=1)
                tables[n][rest, :] = tables[n][rest, :] - dot3(dot_tn, upper[:, rest], both)
    for n in range(count):
        turned = dot3(dot_nt, product[n, :, here], inverses[n][...])
        made[n, :, here] = turned
        if k < size // PANEL - 1:
            rest = slice((k + 1) * PANEL, size)
            product[n, :, rest] = product[n, :, rest] - dot3(
                dot, turned, dot3(dot_tn, turned, product[n, :, rest])
            )


def tail_body(
    tasks, batches, cuts, pieces,
    slots, flow, owners, head_far,
    weight, one, two, head_weight, head_one, head_two, basis, head_basis,
    input_grad, state_new, head_state_new, grams, head_grams,
    grad, part, state, head_state, mine, head_mine, bases, low, head_grad, flow_own,
    flow_in, flow_send, flow_receive, send, receive,
    *rest,
):
    row_scratch = [rest[7 * k : 7 * k + 7] for k in range(pieces)]
    gram_scratch, head_scratch, rest = rest[7 * pieces :][:7], rest[7 * pieces + 7 :][:7], rest[7 * pieces + 14 :]
    chip_send, chip_receive, task_send, task_receive, pair_send, pair_receive, load, save = rest
    task = lax.axis_index("task")
    place, core, chips = pair_place(batches)
    width = part.shape[1]
    channels = grad.shape[1]
    pixels = input_grad.shape[0]
    trunk_total = basis.shape[0]
    head_total = head_basis.shape[0]
    count, head_count = mine.shape[0] // batches, head_mine.shape[0] // batches

    def trunk_marks(start, size):
        rows = pl.ds(pl.multiple_of(start, 8), size)
        return [owners[rows, m : m + 1] for m in range(trunk_total)]

    def head_marks(start, size):
        index = lax.broadcasted_iota(jnp.int32, (size, 1), 0) + start
        index = index + lax.axis_index("batch") * head_grad.shape[0]
        owner = jnp.minimum(lax.div(index, channels), head_total - 1)
        return [jnp.where(owner == m, 1.0, 0.0).astype(F32) for m in range(head_total)]

    def put_grams(target, rows, columns, marks):
        for m, mark in enumerate(marks):
            held = (rows[...].astype(F32) * mark).astype(BF)
            target[m * channels : (m + 1) * channels, :] = dot_tn(held, columns[...]).astype(
                target.dtype
            )

    def put_packed_grams(target, rows, marks):
        n = 0
        for mark in marks:
            held = (rows[...].astype(F32) * mark).astype(BF)
            for a, b in upper_blocks(channels):
                block = dot_tn(held[:, a : a + PANEL], rows[:, b : b + PANEL])
                target[n : n + PANEL, :] = block.astype(target.dtype)
                n += PANEL
        if n < target.shape[0]:
            target[n:, :] = jnp.zeros((target.shape[0] - n, PANEL), target.dtype)

    def peer_of(step, incoming):
        return lax.rem(task + (tasks - step if incoming else step), tasks)

    def flow_copy(step, incoming=False):
        peer = peer_of(step, incoming)
        return remote(block_rows(flow, peer, pixels), flow_in.at[step - 1], flow_send.at[step],
                      flow_receive.at[step], peer, "task")

    def part_copy(k, step, incoming=False):
        peer = peer_of(step, incoming)
        home = peer if incoming else task
        return remote(part.at[part_rows(k), :], grad.at[part_rows(k), columns_of(home, width)],
                      send.at[k, step], receive.at[k, step], peer, "task")

    def trunk_block(chip, home, which):
        rows = pl.ds(pl.multiple_of((2 * chip + which) * count, 8), count)
        return grams.at[rows, columns_of(home, width)]

    def head_block(chip, which):
        return block_rows(head_grams, 2 * chip + which, head_count)

    def task_copy(step, hop, incoming=False):
        peer = peer_of(step, incoming)
        chip = lax.rem(place + chips - hop, chips)
        block = trunk_block(chip, peer if incoming else task, core)
        return remote(block, block, task_send.at[step, hop], task_receive.at[step, hop], peer, "task")

    def pair_copy(kind, hop, incoming=False):
        chip = lax.rem(place + chips - hop, chips)
        which = 1 - core if incoming else core
        home = lax.rem(task + tasks - kind, tasks)
        block = head_block(chip, which) if kind == tasks else trunk_block(chip, home, which)
        return remote(block, block, pair_send.at[kind, hop], pair_receive.at[kind, hop],
                      2 * place + 1 - core, "batch")

    def sum_of(source, scratch, piece=0, total=1):
        near, paired, far, *sems = scratch
        return pair_sum(
            batches, *blocks_in(source, batches, near.shape[1], piece, total), near, paired, far, sems
        )

    def part_rows(k):
        size = part.shape[0] // pieces
        return pl.ds(k * size, size)

    moves = [
        (basis, bases.at[pl.ds(0, trunk_total)]),
        (head_basis, bases.at[pl.ds(trunk_total, head_total)]),
        (head_weight, head_state.at[0]),
        (head_one, head_state.at[1]),
        (head_two, head_state.at[2]),
        (weight, state.at[0]),
        (one, state.at[1]),
        (two, state.at[2]),
        (head_far, head_grad),
        (block_rows(flow, task, pixels), flow_own),
    ]
    loads = [pltpu.make_async_copy(a, b, load.at[k]) for k, (a, b) in enumerate(moves)]
    loads[8].start()
    for copy in (*loads[:8], loads[9]):
        copy.start()
    saves = [
        pltpu.make_async_copy(state, state_new, save.at[0]),
        pltpu.make_async_copy(head_state, head_state_new, save.at[1]),
    ]

    greet_pairs(tasks, batches)
    row_sums = [sum_of(slots, row_scratch[k], k, pieces) for k in range(pieces)]
    for stages in row_sums:
        stages[0]()
    for step in range(1, tasks):
        flow_copy(step).start()
    row_sums[0][1]()
    loads[8].wait()
    put_packed_grams(head_mine, head_grad, head_marks(0, head_grad.shape[0]))
    head_start, head_middle, head_relay, head_end = sum_of(head_mine, head_scratch)
    row_sums[0][2]()
    for stages in row_sums[1:]:
        stages[1]()
    head_start()
    for stages in row_sums[1:]:
        stages[2]()
    head_middle()
    for copy in loads[:5]:
        copy.wait()
    for m in range(trunk_total + head_total):
        low[m] = bases[m].astype(BF)
    for k, stages in enumerate(row_sums):
        total = stages[3]().astype(BF)
        part[part_rows(k), :] = total
        for step in range(1, tasks):
            part_copy(k, step).start()
        grad[part_rows(k), columns_of(task, width)] = total
    head_relay()

    soap_rows(cuts, head_grad, head_marks, head_state, low, trunk_total)
    saves[1].start()
    loads[9].wait()
    total = flow_own[...].astype(F32)
    for step in range(1, tasks):
        flow_copy(step, True).wait_recv()
        total = total + flow_in[step - 1].astype(F32)
    input_grad[...] = total
    head_block(place, core)[...] = head_end().astype(head_grams.dtype)
    trunk_spread = chip_spread(
        batches, lambda chip: trunk_block(chip, task, core), chip_send.at[0], chip_receive.at[0]
    )
    head_spread = chip_spread(
        batches, lambda chip: head_block(chip, core), chip_send.at[1], chip_receive.at[1]
    )
    head_spread[0]()
    pair_copy(tasks, 0).start()
    for k in range(pieces):
        for step in range(1, tasks):
            part_copy(k, step, True).wait_recv()

    put_grams(mine, grad, part, trunk_marks(0, grad.shape[0]))
    start, middle, relay, end = sum_of(mine, gram_scratch)
    start()
    middle()
    head_spread[1]()
    for copy in loads[5:8]:
        copy.wait()
    relay()
    soap_rows(cuts, grad, trunk_marks, state, low, 0, 0, cuts // 2)
    trunk_block(place, task, core)[...] = end().astype(grams.dtype)
    trunk_spread[0]()
    for step in range(1, tasks):
        task_copy(step, 0).start()
    pair_copy(0, 0).start()
    soap_rows(cuts, grad, trunk_marks, state, low, 0, cuts // 2, cuts)
    saves[0].start()
    trunk_spread[1]()
    trunk_spread[2]()
    for hop in range(1, chips):
        for step in range(1, tasks):
            task_copy(step, hop).start()
        pair_copy(0, hop).start()
    head_spread[2]()
    for hop in range(1, chips):
        pair_copy(tasks, hop).start()
    for hop in range(chips):
        for step in range(1, tasks):
            task_copy(step, hop, True).wait_recv()
            pair_copy(step, hop).start()
    for hop in range(chips):
        for kind in range(tasks + 1):
            pair_copy(kind, hop, True).wait_recv()
    for copy in saves:
        copy.wait()
    for step in range(1, tasks):
        for k in range(pieces):
            part_copy(k, step).wait_send()
        flow_copy(step).wait_send()
    for hop in range(chips):
        for kind in range(tasks + 1):
            pair_copy(kind, hop).wait_send()
        for step in range(1, tasks):
            task_copy(step, hop).wait_send()
    trunk_spread[3]()
    head_spread[3]()


def renew_body(
    core, state, head_state, grams, head_grams, stat, head_stat, basis, head_basis,
    weight_new, one_new, two_new, head_weight_new, head_one_new, head_two_new,
    stat_new, head_stat_new, low_made,
    stats, product, made, low_grams, low_head_grams, held, head_held, load, save, *work,
):
    trunk_total, head_total = stat.shape[0], head_stat.shape[0]
    channels = stat.shape[1]
    count = trunk_total + head_total
    shared = product.shape[0]
    tables, inverses = work[:shared], work[shared:]
    loads = []
    blocks = upper_blocks(channels)
    packed = len(blocks) * PANEL

    def gram_rows(m, start):
        if m < trunk_total:
            first = m * channels + start
            return low_grams[first : first + PANEL, :].astype(F32)
        parts = []
        for b in range(0, channels, PANEL):
            n = blocks.index((min(start, b), max(start, b)))
            first = (m - trunk_total) * packed + n * PANEL
            block = low_head_grams[first : first + PANEL, :].astype(F32)
            parts.append(block if b >= start else block.T)
        return jnp.concatenate(parts, axis=1)

    def bring(source, target):
        copy = pltpu.make_async_copy(source, target, load.at[len(loads)])
        loads.append(copy)
        return copy

    for m in range(count):
        first = m < trunk_total
        place = m if first else m - trunk_total
        size = channels if first else packed
        rows = pl.ds(place * size, size)
        here, there = (grams, low_grams) if first else (head_grams, low_head_grams)
        bring(here.at[rows, :], there.at[rows, :]).start()
        bring((stat if first else head_stat).at[place], stats.at[m]).start()

    for n in range(shared):
        both = [
            basis.at[n] if n < trunk_total else head_basis.at[n - trunk_total],
            head_basis.at[n],
        ]
        copy = bring(both[1], made.at[n])
        for which, source in enumerate(both):

            @pl.when(core[0] == which)
            def _():
                pltpu.make_async_copy(source, made.at[n], load.at[2 * count + n]).start()

    bring(state, held).start()
    bring(head_state, head_held).start()
    sources = [held.at[k] for k in range(3)] + [head_held.at[k] for k in range(3)]
    targets = [weight_new, one_new, two_new, head_weight_new, head_one_new, head_two_new]
    saves = [pltpu.make_async_copy(a, b, save.at[k]) for k, (a, b) in enumerate(zip(sources, targets))]
    for m in range(count):
        for copy in loads[2 * m : 2 * m + 2]:
            copy.wait()
        for start in range(0, channels, PANEL):
            rows = slice(start, start + PANEL)
            stats[m, rows, :] = STAT_DECAY * stats[m, rows, :] + (1.0 - STAT_DECAY) * gram_rows(m, start)
    for begin, size, out in ((0, trunk_total, stat_new), (trunk_total, head_total, head_stat_new)):
        copy = pltpu.make_async_copy(stats.at[pl.ds(begin, size)], out, save.at[len(saves)])
        copy.start()
        saves.append(copy)
    for n in range(shared):
        loads[2 * count + n].wait()
        product[n] = dot3(dot, stats[trunk_total * core[0] + n], made[n])
    for k in range(channels // PANEL):
        renew_panel(k, product, made, tables, inverses)
        if k == 0:
            for copy in loads[2 * count + shared :]:
                copy.wait()
            for copy in saves[:6]:
                copy.start()
        cut = slice(k * PANEL, (k + 1) * PANEL)
        low_made[:, :, cut] = made[:, :, cut].astype(BF)
    for copy in saves:
        copy.wait()


def swap_body(batches, x, out, sends, receives):
    place, core, _ = pair_place(batches)
    other = 2 * place + 1 - core
    barrier = pltpu.get_barrier_semaphore()
    pl.semaphore_signal(barrier, inc=1, device_id={"batch": other}, device_id_type=MESH)
    pl.semaphore_wait(barrier, 1)
    copy = remote(x, out, sends, receives, other, "batch")
    copy.start()
    copy.wait()


def finish(tasks, batches, local_grads, rows, matrices):
    slots, flow, owners, head_grad = local_grads
    stat, head_stat, basis, head_basis = matrices
    total, channels = rows[0].shape
    width = channels // tasks
    trunk_total, head_total = basis.shape[0], head_basis.shape[0]
    gram_rows = trunk_total * channels
    packed = len(upper_blocks(channels)) * PANEL
    head_rows = -(-head_total * packed // (16 * batches)) * 16 * batches
    chips = batches // 2
    kind = BF if gram_rows % (16 * batches) == 0 else F32
    cuts = 4 if total % 64 == 0 and head_grad.shape[0] % 64 == 0 else 1
    pieces = 2 if total % 64 == 0 else 1
    square = (trunk_total + head_total, channels, channels)
    pixels = flow.shape[0] // tasks
    input_grad, *made = exchange_kernel(
        functools.partial(tail_body, tasks, batches, cuts, pieces),
        [
            shape((pixels, channels), F32),
            shape((3, total, channels), F32),
            shape((3,) + head_grad.shape, F32),
            shape((gram_rows, channels), kind),
            shape((head_rows, PANEL), BF),
        ],
        "vhvhhhhhhhhh",
        (*local_grads, *rows, basis, head_basis),
        [
            pltpu.VMEM((total, channels), BF),
            pltpu.VMEM((total, width), BF),
            pltpu.VMEM((3, total, channels), F32),
            pltpu.VMEM((3,) + head_grad.shape, F32),
            pltpu.VMEM((gram_rows, width), kind),
            pltpu.VMEM((head_rows, PANEL), BF),
            pltpu.VMEM(square, F32),
            pltpu.VMEM(square, BF),
            pltpu.VMEM(head_grad.shape, BF),
            pltpu.VMEM((pixels, channels), BF),
            pltpu.VMEM((tasks - 1, pixels, channels), BF),
        ]
        + [pltpu.SemaphoreType.DMA((tasks,))] * 2
        + [pltpu.SemaphoreType.DMA((pieces, tasks))] * 2
        + pair_scratch(batches, slots.shape[0] // pieces, width, BF) * pieces
        + pair_scratch(batches, gram_rows, width, kind)
        + pair_scratch(batches, head_rows, PANEL, BF)
        + [pltpu.SemaphoreType.DMA((2, max(chips, 4)))] * 2
        + [pltpu.SemaphoreType.DMA((tasks, chips))] * 2
        + [pltpu.SemaphoreType.DMA((tasks + 1, chips))] * 2
        + [pltpu.SemaphoreType.DMA((10,)), pltpu.SemaphoreType.DMA((2,))],
        5,
        60,
        flops=50000 * MIB,
        places_out="vhhvv",
    )
    outs = [shape(a.shape, F32) for a in (*rows, *matrices)]
    hbm = pl.BlockSpec(memory_space=pltpu.HBM)
    count = trunk_total + head_total
    shared = max(trunk_total, head_total)
    core = lax.rem(lax.axis_index("batch"), 2)
    own = (shared, channels, channels)
    *results, made_low = pl.pallas_call(
        renew_body,
        out_shape=(*outs[:8], shape(own, BF)),
        in_specs=[SMEM_SPEC] + [hbm] * 8,
        out_specs=(*(hbm for _ in outs[:8]), VMEM_SPEC),
        scratch_shapes=[pltpu.VMEM(square, F32)]
        + [pltpu.VMEM(own, F32)] * 2
        + [pltpu.VMEM(made[2].shape, kind), pltpu.VMEM(made[3].shape, BF)]
        + [pltpu.VMEM(made[0].shape, F32), pltpu.VMEM(made[1].shape, F32)]
        + [pltpu.SemaphoreType.DMA((2 * count + shared + 2,))]
        + [pltpu.SemaphoreType.DMA((8,))]
        + [pltpu.VMEM((PANEL, 2 * PANEL), F32)] * shared
        + [pltpu.VMEM((PANEL, PANEL), F32)] * shared,
        compiler_params=pltpu.CompilerParams(vmem_limit_bytes=60 * MIB),
        cost_estimate=pl.CostEstimate(
            flops=50000 * MIB, bytes_accessed=64 * MIB, transcendentals=0
        ),
    )(core.reshape(1), *made, *matrices)
    theirs = exchange_kernel(
        functools.partial(swap_body, batches),
        [shape(own, BF)],
        "v",
        (made_low,),
        [pltpu.SemaphoreType.DMA] * 2,
        6,
        60,
        flops=5000 * MIB,
    )[0]
    results += [
        jnp.where(core == which, made_low[:total], theirs[:total]).astype(F32)
        for which, total in enumerate((trunk_total, head_total))
    ]
    return input_grad, results


def local(
    tasks,
    batches,
    images,
    image_small,
    pool_index,
    row_slot,
    trunk_weight,
    trunk_mean_grad,
    trunk_mean_square,
    trunk_statistic,
    trunk_basis,
    head_weight,
    head_mean_grad,
    head_mean_square,
    head_statistic,
    head_basis,
    trunk_gain,
    trunk_offset,
    trunk_norm_mean_grad,
    trunk_norm_mean_square,
    head_gain,
    head_offset,
    head_norm_mean_grad,
    head_norm_mean_square,
    cotangent,
):
    number, height, breadth, channels = images.shape
    pixels = height * breadth
    shown = tasks * number
    geometry = (shown, height, breadth)
    task = lax.axis_index("task")
    width = channels // tasks

    def quarter(values):
        return lax.dynamic_slice_in_dim(values, task * width, width, values.ndim - 1)

    def inside(flags):
        row_limit = jnp.where(flags > 0, height // 2, height)[:, None, None]
        col_limit = jnp.where(flags > 0, breadth // 2, breadth)[:, None, None]
        return (jnp.arange(height, dtype=jnp.int32)[None, :, None] < row_limit) & (
            jnp.arange(breadth, dtype=jnp.int32)[None, None, :] < col_limit
        )

    cell = 2 * jnp.arange(2, dtype=jnp.int32)[:, None, None] + jnp.arange(2, dtype=jnp.int32)
    cells = pool_index.reshape(number, height // 2, 1, breadth // 2, 1)
    valid = inside(image_small)
    chosen = ((cells == cell).reshape(number, height, breadth) & valid).reshape(number, pixels)
    info = jnp.zeros((8 * number, channels), F32)
    info = info.at[::8, :pixels].set(chosen.astype(F32))
    info = info.at[1::8, 0].set(image_small.astype(F32))
    slots, x, infos, trunk_owners, head_low = arrive(
        tasks, batches, (number, height, breadth), images.reshape(number * pixels, channels),
        info, row_slot, trunk_weight, head_weight[0],
    )
    head_rows = lax.all_gather(head_low, "batch", axis=0, tiled=True)

    scales = quarter(jnp.stack([trunk_gain, trunk_offset], axis=1)).reshape(4, width)
    enc_totals, dec_totals, features, *kept = trunk_forward(
        geometry, tasks, batches, row_slot, infos, x, slots, scales
    )
    head_scales = jnp.stack([head_gain[0], head_offset[0]], axis=1).reshape(6, channels)
    pooled, upstream, head_sums, head_owned = head(
        geometry, tasks, batches, infos, features, head_rows,
        cotangent.reshape(shown, pixels // 4, channels), head_scales, enc_totals,
    )
    task_features = pooled.reshape(cotangent.shape)
    enc_grad, dec_grad, flow, norm_totals = trunk_backward(
        geometry, tasks, batches, infos, upstream, enc_totals, dec_totals, scales, (x, *kept)
    )
    input_grad, results = finish(
        tasks, batches,
        (to_slots(row_slot, enc_grad, dec_grad), flow, trunk_owners, head_owned),
        (trunk_weight, trunk_mean_grad, trunk_mean_square,
         head_weight[0], head_mean_grad[0], head_mean_square[0]),
        (trunk_statistic, head_statistic[0], trunk_basis, head_basis[0]),
    )
    input_grad = input_grad.reshape(images.shape)
    (
        trunk_weight_new, trunk_one_new, trunk_two_new,
        head_weight_new, head_one_new, head_two_new,
        trunk_stat_new, head_stat_new, trunk_basis_new, head_basis_new,
    ) = results

    trunk_norm = jnp.stack([trunk_gain, trunk_offset], axis=1)
    trunk_norm_grad = norm_totals[:4].reshape(2, 2, channels)[:, ::-1]
    trunk_norm_one, trunk_norm_two, trunk_direction = adam(
        trunk_norm_grad, trunk_norm_mean_grad, trunk_norm_mean_square
    )
    head_norm = jnp.stack([head_gain, head_offset], axis=2)
    head_norm_grad = head_sums[:6].reshape(1, 3, 2, channels)[:, :, ::-1]
    head_norm_one, head_norm_two, head_direction = adam(
        head_norm_grad, head_norm_mean_grad, head_norm_mean_square
    )
    return (
        task_features,
        input_grad,
        trunk_weight_new,
        trunk_one_new,
        trunk_two_new,
        trunk_stat_new,
        trunk_basis_new,
        head_weight_new[None],
        head_one_new[None],
        head_two_new[None],
        head_stat_new[None],
        head_basis_new[None],
        trunk_norm - LEARN_NORM * trunk_direction,
        trunk_norm_one,
        trunk_norm_two,
        head_norm - LEARN_NORM * head_direction,
        head_norm_one,
        head_norm_two,
    )


def solution(mesh):
    placed = (
        P(("task", "batch"), None, None, None),
        P(("task", "batch")),
        P(("task", "batch"), None, None),
        P(),
        P("batch", None),
        P("batch", None),
        P("batch", None),
        P(),
        P(),
        P("task", "batch", None),
        P("task", "batch", None),
        P("task", "batch", None),
        P("task", None, None, None),
        P("task", None, None, None),
        P(),
        P(),
        P(),
        P(),
        P("task", None, None),
        P("task", None, None),
        P("task", None, None, None),
        P("task", None, None, None),
        P("task", None, "batch", None, None, None),
    )
    return jax.shard_map(
        functools.partial(local, mesh.shape["task"], mesh.shape["batch"]),
        mesh=mesh,
        in_specs=placed,
        out_specs=(
            P("task", None, "batch", None, None, None),
            P(("task", "batch"), None, None, None),
            P("batch", None),
            P("batch", None),
            P("batch", None),
            P(),
            P(),
            P("task", "batch", None),
            P("task", "batch", None),
            P("task", "batch", None),
            P("task", None, None, None),
            P("task", None, None, None),
            P(),
            P(),
            P(),
            P("task", None, None, None),
            P("task", None, None, None),
            P("task", None, None, None),
        ),
        check_vma=False,
    )
```
